32 devices in a mesh: seq: 4 (over x, core), shard: 8 (over z, y).
Axes of the slice: x: 2, y: 2, z: 4, core: 2. Of those that a mesh axis runs over, the one named last changes fastest.
Arguments:
- hidden_in: bfloat16 [8, 1024, 2048], P('shard', 'seq'), may hold values from -6 to 6
- segment_ids: int32 [8, 1024], P('shard'), may hold values from 0 to 2, as said below
- norm_attn_gain: float32 [2048], replicated, may hold values from 0.25 to 1.75
- w_query: bfloat16 [2048, 2048], P('shard'), may hold values from -0.125 to 0.125
- w_key: bfloat16 [2048, 1024], P('shard'), may hold values from -0.125 to 0.125
- w_value: bfloat16 [2048, 1024], P('shard'), may hold values from -0.125 to 0.125
- query_gain: float32 [128], replicated, may hold values from 0.25 to 1.75
- key_gain: float32 [128], replicated, may hold values from 0.25 to 1.75
- w_out: bfloat16 [2048, 2048], P('shard'), may hold values from -1 to 1
- norm_mlp_gain: float32 [2048], replicated, may hold values from 0.25 to 1.75
- w_gate: bfloat16 [2048, 6144], P('shard'), may hold values from -0.125 to 0.125
- w_up: bfloat16 [2048, 6144], P('shard'), may hold values from -0.125 to 0.125
- w_down: bfloat16 [6144, 2048], P('shard'), may hold values from -0.078125 to 0.078125
- out_cotangent: bfloat16 [8, 1024, 2048], P('shard', 'seq'), may hold values from -6 to 6
Outputs:
- hidden_out: bfloat16 [8, 1024, 2048], P('shard', 'seq')
- grad_in: float32 [8, 1024, 2048], P('shard', 'seq')
- grad_norm_attn: float32 [2048], replicated
- grad_query: float32 [2048, 2048], P(('seq', 'shard'))
- grad_key: float32 [2048, 1024], P(('seq', 'shard'))
- grad_value: float32 [2048, 1024], P(('seq', 'shard'))
- grad_query_gain: float32 [128], replicated
- grad_key_gain: float32 [128], replicated
- grad_out: float32 [2048, 2048], P(('seq', 'shard'))
- grad_norm_mlp: float32 [2048], replicated
- grad_gate: float32 [2048, 6144], P(('seq', 'shard'))
- grad_up: float32 [2048, 6144], P(('seq', 'shard'))
- grad_down: float32 [6144, 2048], P(None, ('seq', 'shard'))
The draws below stay inside these ranges and needn't reach their ends.
Inputs may be any that keep to these rules, and one draw needn't show every extreme that they name: `segment_ids`: segment numbers never fall along a sequence; a document is a run of equal numbers.
All inputs are finite; a program needn't handle non-finite values.
Results may differ from the reference program's by a relative error of at most 0.015.
Values may be sent and summed in bfloat16 or wider, within the bound.
A program may use at most 640 MiB of HBM per device.

```python
import jax
import jax.numpy as jnp
from jax import lax

HIDDEN_SIZE = 2048
Q_HEADS = 16
KV_HEADS = 8
HEAD_DIM = 128
FF_WIDTH = 6144
PIECE_LEN = 256
Q_WIDTH = 2048
KV_WIDTH = 1024
LENGTH = 1024
SEQUENCES = 8


def draw_segment_ids(key, part):
    key = jax.random.fold_in(key, 7)
    head_key, tail_key = jax.random.split(key)
    opening = jax.random.randint(head_key, (SEQUENCES, 1), 1, PIECE_LEN // 2 + 1)
    closing = LENGTH - jax.random.randint(tail_key, (SEQUENCES, 1), 1, PIECE_LEN // 2 + 1)
    places = jnp.arange(LENGTH, dtype=jnp.int32)[None, :]
    return (places >= opening).astype(jnp.int32) + (places >= closing).astype(jnp.int32)


def steps_of(rng, extent, pieces, low, high):
    level = 1.0
    for dim, blocks in pieces:
        steps = jax.random.uniform(jax.random.fold_in(jax.random.fold_in(rng, 6), dim), (blocks,), jnp.float32, low / len(pieces), high / len(pieces))
        level = level * jnp.repeat(jnp.exp(steps), extent[dim] // blocks).reshape((-1,) + (1,) * (len(extent) - 1 - dim))
    return level


def bell_draw(own_key, dims, width, bound, cuts=(), kind=jnp.bfloat16):
    drawn = width * jax.random.normal(own_key, dims, jnp.float32)
    if cuts:
        drawn = drawn * steps_of(own_key, dims, cuts, -0.22, 0.18)
    return jnp.clip(drawn, -bound, bound).astype(kind)


def setup_inputs(seed: int = 0) -> dict:
    key_list = jax.random.split(jax.random.key(seed), 15)
    return {
        "hidden_in": bell_draw(key_list[0], (SEQUENCES, LENGTH, HIDDEN_SIZE), 1.0, 6.0, ((0, 8), (1, 4))),
        "segment_ids": draw_segment_ids(jax.random.fold_in(key_list[14], 71), 0),
        "norm_attn_gain": jnp.clip(1.0 + 0.15 * jax.random.normal(key_list[2], (HIDDEN_SIZE,), jnp.float32), 0.25, 1.75),
        "w_query": bell_draw(key_list[3], (HIDDEN_SIZE, Q_WIDTH), HIDDEN_SIZE ** -0.5, 0.125, ((0, 8),)),
        "w_key": bell_draw(key_list[4], (HIDDEN_SIZE, KV_WIDTH), HIDDEN_SIZE ** -0.5, 0.125, ((0, 8),)),
        "w_value": bell_draw(key_list[5], (HIDDEN_SIZE, KV_WIDTH), HIDDEN_SIZE ** -0.5, 0.125, ((0, 8),)),
        "query_gain": jnp.clip(1.0 + 0.15 * jax.random.normal(key_list[6], (HEAD_DIM,), jnp.float32), 0.25, 1.75),
        "key_gain": jnp.clip(1.0 + 0.15 * jax.random.normal(key_list[7], (HEAD_DIM,), jnp.float32), 0.25, 1.75),
        "w_out": bell_draw(key_list[8], (Q_WIDTH, HIDDEN_SIZE), (HEAD_DIM // 4) ** -0.5, 1.0, ((0, 8),)),
        "norm_mlp_gain": jnp.clip(1.0 + 0.15 * jax.random.normal(key_list[9], (HIDDEN_SIZE,), jnp.float32), 0.25, 1.75),
        "w_gate": bell_draw(key_list[10], (HIDDEN_SIZE, FF_WIDTH), HIDDEN_SIZE ** -0.5, 0.125, ((0, 8),)),
        "w_up": bell_draw(key_list[11], (HIDDEN_SIZE, FF_WIDTH), HIDDEN_SIZE ** -0.5, 0.125, ((0, 8),)),
        "w_down": bell_draw(key_list[12], (FF_WIDTH, HIDDEN_SIZE), FF_WIDTH ** -0.5, 0.078125, ((0, 8),)),
        "out_cotangent": bell_draw(key_list[13], (SEQUENCES, LENGTH, HIDDEN_SIZE), 1.0, 6.0, ((0, 8), (1, 4))),
    }


EPSILON = 1e-06
ROPE_BASE = 1000000.0
NEGATIVE = -1e+30
HIGHEST = lax.Precision.HIGHEST

@jax.custom_vjp
def low(v):
    return lax.optimization_barrier(v.astype(jnp.bfloat16)).astype(jnp.float32)

@jax.custom_vjp
def low_back(v):
    return v

def low_keep(v):
    return (low(v), None)

def low_pass(kept, grad):
    return (grad,)

def back_keep(v):
    return (v, None)

def back_low(kept, grad):
    return (low(grad),)
low.defvjp(low_keep, low_pass)
low_back.defvjp(back_keep, back_low)

def product(left, right):
    return jnp.dot(left, right, precision=HIGHEST, preferred_element_type=jnp.float32)

def normalize(values, gain):
    return values * lax.rsqrt(lax.optimization_barrier(jnp.mean(values * values, axis=-1, keepdims=True)) + EPSILON) * gain

def rotate(values):
    middle = values.shape[-1] // 2
    return jnp.concatenate([-values[..., middle:], values[..., :middle]], axis=-1)

def positions_of(segment):
    places = jnp.arange(segment.shape[0], dtype=jnp.int32)
    fresh = jnp.concatenate([jnp.ones((1,), jnp.bool_), segment[1:] != segment[:-1]])
    return places - lax.cummax(jnp.where(fresh, places, 0), axis=0)

def rotary_tables(positions):
    inverse = ROPE_BASE ** (-(jnp.arange(HEAD_DIM // 2, dtype=jnp.float32) * 2.0) / HEAD_DIM)
    angles = positions.astype(jnp.float32)[:, None] * inverse[None, :]
    angles = jnp.concatenate([angles, angles], axis=-1)
    return (jnp.cos(angles)[:, None, :], jnp.sin(angles)[:, None, :])

def decoder_layer(hidden, segment, norm_attn_gain, w_query, w_key, w_value, query_gain, key_gain, w_out, norm_mlp_gain, w_gate, w_up, w_down):
    amount = hidden.shape[0]
    places = jnp.arange(amount, dtype=jnp.int32)
    cosine, sine = rotary_tables(positions_of(segment))
    attn_in = low(normalize(hidden, norm_attn_gain))
    queries = low_back(product(attn_in, w_query)).reshape(amount, Q_HEADS, HEAD_DIM)
    keys = low_back(product(attn_in, w_key)).reshape(amount, KV_HEADS, HEAD_DIM)
    values = low_back(low(product(attn_in, w_value))).reshape(amount, KV_HEADS, HEAD_DIM)
    queries = normalize(queries, query_gain)
    queries = low_back(low(queries * cosine + rotate(queries) * sine))
    keys = normalize(keys, key_gain)
    keys = low_back(low(keys * cosine + rotate(keys) * sine))
    group_size = Q_HEADS // KV_HEADS
    keys_all = jnp.repeat(keys, group_size, axis=1)
    values_all = jnp.repeat(values, group_size, axis=1)
    block_rows = min(512, amount)
    blocks = amount // block_rows

    def attend(inputs):
        q_block, offset = inputs
        here_places = offset + jnp.arange(block_rows, dtype=jnp.int32)
        near_segments = lax.dynamic_slice_in_dim(segment, offset, block_rows)
        allowed = (near_segments[:, None] == segment[None, :]) & (places[None, :] <= here_places[:, None])
        scores = low_back(jnp.einsum('qhd,khd->hqk', q_block, keys_all, precision=HIGHEST) * HEAD_DIM ** (-0.5))
        scores = jnp.where(allowed[None], scores, NEGATIVE)
        scores = scores - lax.optimization_barrier(jnp.max(scores, axis=-1, keepdims=True))
        weights = jnp.exp(scores)
        weights = weights / lax.optimization_barrier(jnp.sum(weights, axis=-1, keepdims=True))
        return jnp.einsum('hqk,khd->qhd', low(weights), values_all, precision=HIGHEST)
    starts = jnp.arange(blocks, dtype=jnp.int32) * block_rows
    mixed = lax.map(jax.checkpoint(attend), (queries.reshape(blocks, block_rows, Q_HEADS, HEAD_DIM), starts))
    mixed = low_back(low(mixed.reshape(amount, Q_HEADS * HEAD_DIM)))
    middle = hidden + low_back(product(mixed, w_out))
    mlp_in = low(normalize(middle, norm_mlp_gain))
    gate_proj = low_back(product(mlp_in, w_gate))
    up_proj = low_back(product(mlp_in, w_up))
    return middle + product(low(jax.nn.silu(gate_proj) * up_proj), w_down)

def reference(hidden_in, segment_ids, norm_attn_gain, w_query, w_key, w_value, query_gain, key_gain, w_out, norm_mlp_gain, w_gate, w_up, w_down, out_cotangent):
    params = tuple((argument.astype(jnp.float32) for argument in (norm_attn_gain, w_query, w_key, w_value, query_gain, key_gain, w_out, norm_mlp_gain, w_gate, w_up, w_down)))

    def one_sequence(totals, inputs):
        hidden, segment, cotangent = inputs

        def forward(hidden_now, *weights):
            return decoder_layer(hidden_now, segment, *weights)
        outputs, pull = jax.vjp(forward, hidden, *params)
        grads = pull(cotangent)
        summed = tuple((running + fresh for running, fresh in zip(totals, grads[1:])))
        return (summed, (outputs.astype(jnp.bfloat16), grads[0]))
    starting = tuple((jnp.zeros_like(argument) for argument in params))
    totals, (hidden_out, grad_in) = lax.scan(one_sequence, starting, (hidden_in.astype(jnp.float32), segment_ids, out_cotangent.astype(jnp.float32)))
    return (hidden_out, grad_in, totals[0], totals[1], totals[2], totals[3], totals[4], totals[5], totals[6], totals[7], totals[8], totals[9], totals[10])
```

```python
import jax
import jax.numpy as jnp
from jax import lax
from jax.sharding import PartitionSpec as P

Q_HEADS = 16
KV_HEADS = 8
HEAD_DIM = 128
EPSILON = 1e-06
ROPE_BASE = 1000000.0
NEGATIVE = -1e30
BF = jnp.bfloat16
F32 = jnp.float32


def normalize(values):
    scales = lax.rsqrt(jnp.mean(values * values, axis=-1, keepdims=True) + EPSILON)
    return (values * scales, scales)


def norm_back(upper, normed, scales):
    return scales * (upper - normed * jnp.mean(upper * normed, axis=-1, keepdims=True))


def rotate(values):
    middle = values.shape[-1] // 2
    return jnp.concatenate([-values[..., middle:], values[..., :middle]], axis=-1)


def rotate_back(values):
    middle = values.shape[-1] // 2
    return jnp.concatenate([values[..., middle:], -values[..., :middle]], axis=-1)


def positions_of(segment):
    places = jnp.arange(segment.shape[0], dtype=jnp.int32)
    fresh = jnp.concatenate([jnp.ones((1,), jnp.bool_), segment[1:] != segment[:-1]])
    return places - lax.cummax(jnp.where(fresh, places, 0), axis=0)


def rotary_tables(positions):
    inverse = ROPE_BASE ** (-(jnp.arange(HEAD_DIM // 2, dtype=F32) * 2.0) / HEAD_DIM)
    angles = positions.astype(F32)[:, None] * inverse[None, :]
    angles = jnp.concatenate([angles, angles], axis=-1)
    return (jnp.cos(angles)[:, None, :], jnp.sin(angles)[:, None, :])


def dot(left, right):
    return jnp.dot(left, right, preferred_element_type=F32)


def contract_rows(left, right):
    return lax.dot_general(left, right, (((0,), (0,)), ((), ())), preferred_element_type=F32)


def contract_cols(left, right):
    return lax.dot_general(left, right, (((1,), (1,)), ((), ())), preferred_element_type=F32)


def head_back(rotated_grad, cosine, sine, head_hat, head_scale, gain):
    gained_grad = rotated_grad * cosine + rotate_back(rotated_grad * sine)
    gain_grad = jnp.sum(gained_grad * head_hat, axis=(0, 1))
    return (norm_back(gained_grad * gain, head_hat, head_scale), gain_grad)


def other_core(value):
    return lax.ppermute(value, "seq", [(i, i ^ 1) for i in range(4)])


def other_chip(value):
    return lax.ppermute(value, "seq", [(i, i ^ 2) for i in range(4)])


def gather_tokens(own):
    chip, core = lax.axis_index("seq") // 2, lax.axis_index("seq") % 2
    far = other_chip(own)
    pair = jnp.where(chip == 0, jnp.stack([own, far]), jnp.stack([far, own]))
    mate = other_core(pair)
    first = jnp.where(core == 0, pair, mate)
    second = jnp.where(core == 0, mate, pair)
    return jnp.stack([first, second], axis=1).reshape(4 * own.shape[0], own.shape[1])


def scatter_tokens(part):
    chip, core = lax.axis_index("seq") // 2, lax.axis_index("seq") % 2
    rows = part.shape[0] // 4
    blocks = part.reshape(2, 2, rows, part.shape[1])
    give = lax.dynamic_index_in_dim(blocks, 1 - core, 1, keepdims=False).astype(BF)
    keep = lax.dynamic_index_in_dim(blocks, core, 1, keepdims=False)
    pair = keep + other_core(give).astype(F32)
    give = lax.dynamic_index_in_dim(pair, 1 - chip, 0, keepdims=False).astype(BF)
    keep = lax.dynamic_index_in_dim(pair, chip, 0, keepdims=False)
    return keep + other_chip(give).astype(F32)


def outer_shift(value, amount):
    size = lax.axis_size("shard")
    outer = size // 2
    return lax.ppermute(
        value, "shard", [(i, (i // 2 + amount) % outer * 2 + i % 2) for i in range(size)]
    )


def inner_swap(value):
    return lax.ppermute(value, "shard", [(i, i ^ 1) for i in range(lax.axis_size("shard"))])


def gather_rows(own):
    size = lax.axis_size("shard")
    outer = size // 2
    place, half = lax.axis_index("shard") // 2, lax.axis_index("shard") % 2
    whole = jnp.zeros((size,) + own.shape, own.dtype)
    for amount in range(outer):
        block = outer_shift(own, amount) if amount else own
        twin = inner_swap(block)
        source = (place - amount + outer) % outer
        whole = lax.dynamic_update_slice(whole, block[None], (source * 2 + half, 0, 0))
        whole = lax.dynamic_update_slice(whole, twin[None], (source * 2 + 1 - half, 0, 0))
    return whole.reshape(size * own.shape[0], own.shape[1])


def gather_out(own):
    size = lax.axis_size("shard")
    seq = lax.axis_index("seq")
    rows = own.shape[0]
    if size != 8:
        whole = lax.all_gather(own, "shard", axis=0, tiled=True)
        return lax.dynamic_slice_in_dim(whole, seq * (size // 4) * rows, size // 4 * rows, 0)
    place, half = lax.axis_index("shard") // 2, lax.axis_index("shard") % 2
    block = jnp.where(place == seq, own, jnp.zeros_like(own))
    for amount in range(1, 4):
        pairs = [
            (s * 8 + s * 2 + i, s * 8 + (s + amount) % 4 * 2 + i) for s in range(4) for i in range(2)
        ]
        block = block + lax.ppermute(own, ("seq", "shard"), pairs)
    twin = inner_swap(block)
    first = jnp.where(half == 0, block, twin)
    second = jnp.where(half == 0, twin, block)
    return jnp.concatenate([first, second], axis=0)


def split_columns(left):
    size = lax.axis_size("shard")
    outer = size // 2
    tokens, width = left.shape
    rows = width // (4 * size)
    blocks = left.reshape(tokens, 4, outer, 2, rows).transpose(3, 0, 2, 1, 4)
    blocks = blocks.reshape(2, tokens, width // 2)
    half = lax.axis_index("shard") % 2
    return (
        lax.dynamic_index_in_dim(blocks, half, 0, keepdims=False),
        lax.dynamic_index_in_dim(blocks, 1 - half, 0, keepdims=False),
    )


def sum_terms(mine, theirs, right):
    outer = lax.axis_size("shard") // 2
    place = lax.axis_index("shard") // 2
    arrived = inner_swap(contract_rows(theirs, right).astype(BF))
    total = contract_rows(mine, right) + arrived.astype(F32)
    blocks = total.reshape(outer, total.shape[0] // outer, total.shape[1])
    result = lax.dynamic_index_in_dim(blocks, place, 0, keepdims=False)
    sent = blocks.astype(BF)
    for amount in range(1, outer):
        block = lax.dynamic_index_in_dim(sent, (place + amount) % outer, 0, keepdims=False)
        result = result + outer_shift(block, amount).astype(F32)
    return result


def own_rows(summed):
    blocks = summed.astype(BF).reshape(4, summed.shape[0] // 4, summed.shape[1])
    return lax.all_to_all(blocks, "seq", split_axis=0, concat_axis=0, tiled=True).astype(F32)


def local(
    hidden_in,
    segment_ids,
    norm_attn_gain,
    w_query,
    w_key,
    w_value,
    query_gain,
    key_gain,
    w_out,
    norm_mlp_gain,
    w_gate,
    w_up,
    w_down,
    out_cotangent,
):
    size = lax.axis_size("shard")
    seq = lax.axis_index("seq")
    _, piece_len, width = hidden_in.shape
    length = piece_len * 4
    heads = Q_HEADS // 4
    kv_heads = KV_HEADS // 4
    group = Q_HEADS // KV_HEADS
    scale = HEAD_DIM ** (-0.5)
    ff_part = w_down.shape[0] // 4
    ff_width = w_gate.shape[1]
    q_part = heads * HEAD_DIM
    kv_part = kv_heads * HEAD_DIM

    def columns(weight, count):
        return lax.dynamic_slice_in_dim(weight, seq * count, count, 1)

    def units(weight):
        blocks = weight.reshape(weight.shape[0], size, 4, ff_part)
        return lax.dynamic_index_in_dim(blocks, seq, 2, keepdims=False).reshape(
            weight.shape[0], size * ff_part
        )

    qkv_full = gather_rows(
        jnp.concatenate(
            [columns(w_query, q_part), columns(w_key, kv_part), columns(w_value, kv_part)], axis=1
        )
    )
    hidden = hidden_in[0].astype(F32)
    normed_one, scale_one = normalize(hidden)
    attn_in = gather_tokens((normed_one * norm_attn_gain).astype(BF))
    out_full = gather_out(w_out)
    gate_full = gather_rows(units(w_gate))
    up_full = gather_rows(units(w_up))
    down_full = gather_rows(lax.dynamic_slice_in_dim(w_down, seq * ff_part, ff_part, 0))
    upstream = gather_tokens(out_cotangent[0])

    segment = segment_ids[0]
    cosine, sine = rotary_tables(positions_of(segment))
    qkv = dot(attn_in, qkv_full)
    query_proj = qkv[:, :q_part].reshape(length, heads, HEAD_DIM)
    key_proj = qkv[:, q_part : q_part + kv_part].reshape(length, kv_heads, HEAD_DIM)
    values = qkv[:, q_part + kv_part :].astype(BF).reshape(length, kv_heads, HEAD_DIM)
    query_hat, query_scale = normalize(query_proj)
    query_gained = query_hat * query_gain
    queries = (query_gained * cosine + rotate(query_gained) * sine).astype(BF)
    key_hat, key_scale = normalize(key_proj)
    key_gained = key_hat * key_gain
    keys = (key_gained * cosine + rotate(key_gained) * sine).astype(BF)

    block_rows = min(512, length)
    places = jnp.arange(length, dtype=jnp.int32)

    def block_scores(q_block, offset):
        end = offset + block_rows
        here_places = offset + jnp.arange(block_rows, dtype=jnp.int32)
        near_segments = segment[offset:end]
        allowed = (near_segments[:, None] == segment[None, :end]) & (
            places[None, :end] <= here_places[:, None]
        )
        scores = (
            jnp.einsum("qkgd,tkd->kgqt", q_block, keys[:end], preferred_element_type=F32) * scale
        )
        return jnp.where(allowed, scores, NEGATIVE)

    outputs = []
    totals = []
    for offset in range(0, length, block_rows):
        end = offset + block_rows
        q_block = queries[offset:end].reshape(block_rows, kv_heads, group, HEAD_DIM)
        scores = block_scores(q_block, offset)
        highest = jnp.max(scores, axis=-1, keepdims=True)
        raised = jnp.exp(scores - highest)
        row_sums = jnp.sum(raised, axis=-1, keepdims=True)
        weights = (raised / row_sums).astype(BF)
        totals.append(highest + jnp.log(row_sums))
        mixed = jnp.einsum("kgqt,tkd->qkgd", weights, values[:end], preferred_element_type=F32)
        outputs.append(mixed.astype(BF).reshape(block_rows, q_part))
    attended = jnp.concatenate(outputs, axis=0)

    middle = hidden + scatter_tokens(dot(attended, out_full))
    normed_two, scale_two = normalize(middle)
    mlp_in = gather_tokens((normed_two * norm_mlp_gain).astype(BF))
    gate_proj = dot(mlp_in, gate_full)
    up_proj = dot(mlp_in, up_full)
    sigmoid_gate = jax.nn.sigmoid(gate_proj)
    silu_gate = gate_proj * sigmoid_gate
    activated = (silu_gate * up_proj).astype(BF)
    mlp_out = scatter_tokens(dot(activated, down_full))
    hidden_out = (middle + mlp_out).astype(BF)

    down_terms = sum_terms(*split_columns(upstream), activated)
    act_grad = contract_cols(upstream, down_full)
    gate_grad = (
        act_grad * up_proj * sigmoid_gate * (1.0 + gate_proj * (1.0 - sigmoid_gate))
    ).astype(BF)
    up_grad = (act_grad * silu_gate).astype(BF)
    mlp_mine, mlp_theirs = split_columns(mlp_in)
    gate_terms = sum_terms(mlp_mine, mlp_theirs, gate_grad)
    up_terms = sum_terms(mlp_mine, mlp_theirs, up_grad)
    update = scatter_tokens(contract_cols(gate_grad, gate_full) + contract_cols(up_grad, up_full))
    mlp_gain_grad = jnp.sum(update * normed_two, axis=0)
    middle_grad = out_cotangent[0].astype(F32) + norm_back(
        update * norm_mlp_gain, normed_two, scale_two
    )
    attn_grad = gather_tokens(middle_grad.astype(BF))
    mixed_grad = contract_cols(attn_grad, out_full).astype(BF)

    key_total = jnp.zeros((length, kv_heads, HEAD_DIM), F32)
    value_total = jnp.zeros((length, kv_heads, HEAD_DIM), F32)
    query_parts = []
    for block_index, offset in enumerate(range(0, length, block_rows)):
        end = offset + block_rows
        q_block = queries[offset:end].reshape(block_rows, kv_heads, group, HEAD_DIM)
        out_grad = mixed_grad[offset:end].reshape(block_rows, kv_heads, group, HEAD_DIM)
        scores = block_scores(q_block, offset)
        weights = jnp.exp(scores - totals[block_index])
        weight_grad = jnp.einsum(
            "qkgd,tkd->kgqt", out_grad, values[:end], preferred_element_type=F32
        )
        inner_sum = jnp.sum(weights * weight_grad, axis=-1, keepdims=True)
        score_grad = (weights * (weight_grad - inner_sum)).astype(BF)
        query_part = (
            jnp.einsum("kgqt,tkd->qkgd", score_grad, keys[:end], preferred_element_type=F32) * scale
        )
        query_parts.append(query_part.astype(BF).reshape(block_rows, heads, HEAD_DIM))
        key_part = (
            jnp.einsum("kgqt,qkgd->tkd", score_grad, q_block, preferred_element_type=F32) * scale
        )
        value_part = jnp.einsum(
            "kgqt,qkgd->tkd", weights.astype(BF), out_grad, preferred_element_type=F32
        )
        key_total = key_total.at[:end].add(key_part)
        value_total = value_total.at[:end].add(value_part)
    query_rot_grad = jnp.concatenate(query_parts, axis=0).astype(F32)
    key_rot_grad = key_total.astype(BF).astype(F32)
    value_grad = value_total.astype(BF).reshape(length, kv_part)
    query_proj_grad, query_gain_grad = head_back(
        query_rot_grad, cosine, sine, query_hat, query_scale, query_gain
    )
    key_proj_grad, key_gain_grad = head_back(
        key_rot_grad, cosine, sine, key_hat, key_scale, key_gain
    )
    proj_grads = jnp.concatenate(
        [
            query_proj_grad.reshape(length, q_part).astype(BF),
            key_proj_grad.reshape(length, kv_part).astype(BF),
            value_grad,
        ],
        axis=1,
    )
    out_rows = Q_HEADS * HEAD_DIM // (4 * size)
    out_left = attended.reshape(length, size // 2, 2, out_rows).transpose(2, 0, 1, 3)
    out_left = out_left.reshape(2, length, q_part // 2)
    half = lax.axis_index("shard") % 2
    grad_out = sum_terms(
        lax.dynamic_index_in_dim(out_left, half, 0, keepdims=False),
        lax.dynamic_index_in_dim(out_left, 1 - half, 0, keepdims=False),
        attn_grad,
    )
    qkv_terms = sum_terms(*split_columns(attn_in), proj_grads)
    attn_in_grad = scatter_tokens(contract_cols(proj_grads, qkv_full))
    attn_gain_grad = jnp.sum(attn_in_grad * normed_one, axis=0)
    grad_in = middle_grad + norm_back(attn_in_grad * norm_attn_gain, normed_one, scale_one)
    gain_totals = lax.psum(
        (attn_gain_grad, query_gain_grad, key_gain_grad, mlp_gain_grad), ("seq", "shard")
    )

    def units_back(blocks):
        rows = blocks.shape[1]
        return blocks.reshape(4, rows, size, ff_part).transpose(1, 2, 0, 3).reshape(rows, ff_width)

    def side_by_side(blocks):
        return blocks.transpose(1, 0, 2).reshape(blocks.shape[1], 4 * blocks.shape[2])

    qkv_own = own_rows(qkv_terms)
    return (
        hidden_out[None],
        grad_in[None],
        gain_totals[0],
        side_by_side(qkv_own[:, :, :q_part]),
        side_by_side(qkv_own[:, :, q_part : q_part + kv_part]),
        side_by_side(qkv_own[:, :, q_part + kv_part :]),
        gain_totals[1],
        gain_totals[2],
        grad_out,
        gain_totals[3],
        units_back(own_rows(gate_terms)),
        units_back(own_rows(up_terms)),
        units_back(own_rows(down_terms)).T,
    )


def solution(mesh):
    return jax.shard_map(
        local,
        mesh=mesh,
        in_specs=(
            P("shard", "seq", None),
            P("shard", None),
            P(),
            P("shard", None),
            P("shard", None),
            P("shard", None),
            P(),
            P(),
            P("shard", None),
            P(),
            P("shard", None),
            P("shard", None),
            P("shard", None),
            P("shard", "seq", None),
        ),
        out_specs=(
            P("shard", "seq", None),
            P("shard", "seq", None),
            P(),
            P(("seq", "shard"), None),
            P(("seq", "shard"), None),
            P(("seq", "shard"), None),
            P(),
            P(),
            P(("seq", "shard"), None),
            P(),
            P(("seq", "shard"), None),
            P(("seq", "shard"), None),
            P(None, ("seq", "shard")),
        ),
        check_vma=False,
    )
```

```python
import functools

import jax
import jax.numpy as jnp
from jax import lax
from jax.experimental import pallas as pl
from jax.experimental.pallas import tpu as pltpu
from jax.sharding import PartitionSpec as P

Q_HEADS = 16
KV_HEADS = 8
HEAD_DIM = 128
EPSILON = 1e-06
ROPE_BASE = 1000000.0
NEGATIVE = -1e30
BF = jnp.bfloat16
F32 = jnp.float32
MESH = pl.DeviceIdType.MESH
ANY = pl.BlockSpec(memory_space=pl.ANY)
VMEM = pl.BlockSpec(memory_space=pltpu.VMEM)
VMEM_BYTES = 60 * 1024 * 1024


def normalize(values):
    scales = lax.rsqrt(jnp.mean(values * values, axis=-1, keepdims=True) + EPSILON)
    return (values * scales, scales)


def norm_back(upper, normed, scales):
    return scales * (upper - normed * jnp.mean(upper * normed, axis=-1, keepdims=True))


def rotate(values):
    middle = values.shape[-1] // 2
    return jnp.concatenate([-values[..., middle:], values[..., :middle]], axis=-1)


def rotate_back(values):
    middle = values.shape[-1] // 2
    return jnp.concatenate([values[..., middle:], -values[..., :middle]], axis=-1)


def positions_of(segment):
    places = jnp.arange(segment.shape[0], dtype=jnp.int32)
    fresh = jnp.concatenate([jnp.ones((1,), jnp.bool_), segment[1:] != segment[:-1]])
    return places - lax.cummax(jnp.where(fresh, places, 0), axis=0)


def rotary_tables(positions):
    inverse = ROPE_BASE ** (-(jnp.arange(HEAD_DIM // 2, dtype=F32) * 2.0) / HEAD_DIM)
    angles = positions.astype(F32)[:, None] * inverse[None, :]
    angles = jnp.concatenate([angles, angles], axis=-1)
    return (jnp.cos(angles)[:, None, :], jnp.sin(angles)[:, None, :])


def dot(left, right):
    return jnp.dot(left, right, preferred_element_type=F32)


def contract_rows(left, right):
    return lax.dot_general(left, right, (((0,), (0,)), ((), ())), preferred_element_type=F32)


def contract_cols(left, right):
    return lax.dot_general(left, right, (((1,), (1,)), ((), ())), preferred_element_type=F32)


def head_back(rotated_grad, cosine, sine, head_hat, head_scale, gain):
    gained_grad = rotated_grad * cosine + rotate_back(rotated_grad * sine)
    gain_grad = jnp.sum(gained_grad * head_hat, axis=(0, 1))
    return (norm_back(gained_grad * gain, head_hat, head_scale), gain_grad)


class Place:
    def __init__(self, size):
        self.size = size
        self.outer = size // 2
        self.quarter = size // 4
        self.seq = lax.axis_index("seq")
        self.shard = lax.axis_index("shard")
        self.chip = self.seq // 2
        self.core = lax.rem(self.seq, 2)
        self.place = self.shard // 2
        self.half = lax.rem(self.shard, 2)
        self.far_seq = lax.rem(self.seq + 2, 4)
        self.mate_seq = self.chip * 2 + 1 - self.core
        self.far = {"seq": self.far_seq}
        self.mate = {"seq": self.mate_seq}
        self.twin_shard = self.place * 2 + 1 - self.half
        self.twin = {"shard": self.twin_shard}

    def ahead(self, amount):
        return lax.rem(self.place + amount, self.outer)

    def behind(self, amount):
        return lax.rem(self.place + self.outer - amount, self.outer)

    def outer_peer(self, place):
        return {"shard": place * 2 + self.half}

    def greet(self):
        barrier = pltpu.get_barrier_semaphore()
        peers = [self.far, self.mate, self.twin]
        peers += [self.outer_peer(self.ahead(k)) for k in range(1, self.outer)]
        for peer in peers:
            pl.semaphore_signal(barrier, inc=1, device_id=peer, device_id_type=MESH)
        pl.semaphore_wait(barrier, len(peers))


def remote(source, target, send, receive, peer):
    return pltpu.make_async_remote_copy(
        src_ref=source,
        dst_ref=target,
        send_sem=send,
        recv_sem=receive,
        device_id=peer,
        device_id_type=MESH,
    )


class RowGather:
    def __init__(self, here, own, whole, slot, sems):
        self.here, self.own, self.whole, self.slot = here, own, whole, slot
        self.zs, self.zr, self.ys, self.yr, self.local = sems

    def keep(self):
        return pltpu.make_async_copy(
            self.own, self.slot(self.whole, self.here.shard), self.local
        )

    def along(self, amount):
        here = self.here
        return remote(
            self.own,
            self.slot(self.whole, here.shard),
            self.zs.at[amount - 1],
            self.zr.at[amount - 1],
            here.outer_peer(here.ahead(amount)),
        )

    def across(self, amount):
        here = self.here
        block = self.slot(self.whole, here.behind(amount) * 2 + here.half)
        return remote(
            block if amount else self.own, block, self.ys.at[amount], self.yr.at[amount], here.twin
        )

    def send(self):
        self.keep().start()
        for amount in range(1, self.here.outer):
            self.along(amount).start()

    def forward(self):
        self.across(0).start()
        for amount in range(1, self.here.outer):
            self.along(amount).wait_recv()
            self.across(amount).start()

    def arrive(self):
        self.keep().wait()
        for amount in range(self.here.outer):
            self.across(amount).wait_recv()

    def finish(self):
        for amount in range(1, self.here.outer):
            self.along(amount).wait_send()
        for amount in range(self.here.outer):
            self.across(amount).wait_send()


class HeadGather:
    def __init__(self, here, own, whole, sems):
        self.here, self.own, self.whole = here, own, whole
        self.zs, self.zr, self.ys, self.yr, self.local = sems
        self.count = here.quarter // 2
        self.first = here.seq * self.count
        self.mine = here.place - self.first
        self.inside = (self.mine >= 0) & (self.mine < self.count)

    def slot(self, index):
        return self.whole.at[index * 2 + self.here.half]

    def keep(self):
        return pltpu.make_async_copy(self.own, self.slot(self.mine), self.local)

    def along(self, amount):
        here = self.here
        return remote(
            self.own,
            self.slot(self.mine),
            self.zs.at[amount - 1],
            self.zr.at[self.mine],
            here.outer_peer(here.ahead(amount)),
        )

    def arrival(self, index):
        block = self.slot(index)
        return remote(block, block, self.zs.at[0], self.zr.at[index], self.here.twin)

    def across(self, index):
        block = self.slot(index)
        return remote(block, block, self.ys.at[index], self.yr.at[index], self.here.twin)

    def send(self):
        @pl.when(self.inside)
        def _():
            self.keep().start()
            for amount in range(1, self.here.outer):
                self.along(amount).start()

    def forward(self):
        @pl.when(self.inside)
        def _():
            self.keep().wait()

        for index in range(self.count):

            @pl.when(self.mine != index)
            def _():
                self.arrival(index).wait_recv()

            self.across(index).start()

    def arrive(self):
        for index in range(self.count):
            self.across(index).wait_recv()

    def finish(self):
        @pl.when(self.inside)
        def _():
            for amount in range(1, self.here.outer):
                self.along(amount).wait_send()

        for index in range(self.count):
            self.across(index).wait_send()


class TokenGather:
    def __init__(self, here, own, whole, sems):
        self.here, self.own, self.whole = here, own, whole
        self.send_sems, self.recv_sems, self.local = sems
        self.rows = whole.shape[0] // 4

    def slot(self, seq):
        return self.whole.at[pl.ds(pl.multiple_of(seq * self.rows, self.rows), self.rows), :]

    def keep(self):
        return pltpu.make_async_copy(self.own, self.slot(self.here.seq), self.local)

    def copy(self, index):
        here = self.here
        slot = self.slot(here.far_seq if index == 2 else here.seq)
        return remote(
            slot if index == 2 else self.own,
            slot,
            self.send_sems.at[index],
            self.recv_sems.at[index],
            here.far if index == 0 else here.mate,
        )

    def send(self):
        self.copy(0).start()
        self.copy(1).start()
        self.keep().start()

    def forward(self):
        self.copy(0).wait_recv()
        self.copy(2).start()

    def arrive(self):
        self.copy(1).wait_recv()
        self.copy(2).wait_recv()
        self.keep().wait()

    def finish(self):
        for index in range(3):
            self.copy(index).wait_send()


def scatter_sum(here, piece, base, give, got, pair, far_got, sems, width, step):
    send_sems, recv_sems = sems
    other = 1 - here.chip
    to_mate = [
        remote(
            give.at[chip], got.at[chip], send_sems.at[index], recv_sems.at[index], here.mate
        )
        for index, chip in enumerate((other, here.chip))
    ]
    to_far = remote(pair, far_got, send_sems.at[2], recv_sems.at[2], here.far)

    def columns(body):
        @pl.loop(0, width // step)
        def _(index):
            body(pl.ds(pl.multiple_of(index * step, step), step))

    for index, chip in enumerate((other, here.chip)):
        seq = chip * 2 + 1 - here.core

        def fill(column, chip=chip, seq=seq):
            give[chip, :, column] = piece(seq, column).astype(BF)

        columns(fill)
        to_mate[index].start()

    to_mate[0].wait_recv()

    def fill_pair(column):
        term = piece(here.far_seq, column) + got[other, :, column].astype(F32)
        pair[:, column] = term.astype(BF)

    columns(fill_pair)
    to_far.start()
    to_mate[1].wait_recv()

    def fill_base(column):
        base[:, column] += piece(here.seq, column) + got[here.chip, :, column].astype(F32)

    columns(fill_base)
    to_far.wait_recv()

    def fill_far(column):
        base[:, column] += far_got[:, column].astype(F32)

    columns(fill_far)
    for copy in (*to_mate, to_far):
        copy.wait_send()


def forward_kernel(
    size,
    hidden_ref,
    dy_own,
    qkv_own,
    out_own,
    first_own,
    second_own,
    down_own,
    attn_gain_ref,
    mlp_gain_ref,
    query_gain_ref,
    key_gain_ref,
    cos_ref,
    sin_ref,
    seg_col_ref,
    seg_row_ref,
    qkv_full,
    out_full,
    first_full,
    second_full,
    down_full,
    n1_full,
    dy_full,
    n2_full,
    gate_out,
    up_out,
    act_out,
    proj_ref,
    heads_ref,
    mixed_ref,
    lse_ref,
    middle_ref,
    lhs,
    qkv_w,
    out_w,
    own_rows,
    give,
    got,
    pair,
    far_got,
    zs,
    zr,
    ys,
    yr,
    row_local,
    ts,
    tr,
    token_local,
    load_sem,
    ss,
    sr,
):
    here = Place(size)
    quarter = here.quarter

    def mixed_slot(whole, shard):
        return whole.at[:, lax.rem(shard, quarter), :, shard // quarter]

    def plain_slot(whole, shard):
        return whole.at[shard]

    def sems(index):
        return (zs.at[index], zr.at[index], ys.at[index], yr.at[index], row_local.at[index])

    qkv = RowGather(here, qkv_own, qkv_full, mixed_slot, sems(0))
    out = HeadGather(here, out_own, out_full, sems(1))
    first = RowGather(here, first_own, first_full, mixed_slot, sems(2))
    second = RowGather(here, second_own, second_full, mixed_slot, sems(3))
    down = RowGather(here, down_own, down_full, plain_slot, sems(4))
    n1 = TokenGather(here, own_rows.at[0], n1_full, (ts.at[0], tr.at[0], token_local.at[0]))
    n2 = TokenGather(here, own_rows.at[1], n2_full, (ts.at[1], tr.at[1], token_local.at[1]))
    dy = TokenGather(here, dy_own, dy_full, (ts.at[2], tr.at[2], token_local.at[2]))

    length, width = lhs.shape
    rows = length // 4
    units = gate_out.shape[1]
    heads = lse_ref.shape[0]
    kv_heads = heads // 2

    here.greet()
    qkv.send()
    out.send()

    def norm_rows(source, gain_ref, target):
        @pl.loop(0, rows // 32)
        def _(index):
            part = pl.ds(pl.multiple_of(index * 32, 32), 32)
            values = source[part, :].astype(F32)
            scales = lax.rsqrt(jnp.mean(values * values, axis=-1, keepdims=True) + EPSILON)
            target[part, :] = (values * scales * gain_ref[...]).astype(BF)

    norm_rows(hidden_ref, attn_gain_ref, own_rows.at[0])
    n1.send()
    first.send()
    qkv.forward()
    n1.forward()
    n1.arrive()
    load_lhs = pltpu.make_async_copy(n1_full, lhs, load_sem.at[0])
    load_lhs.start()
    dy.send()
    qkv.arrive()
    load_qkv = pltpu.make_async_copy(qkv_full, qkv_w, load_sem.at[1])
    load_qkv.start()
    load_lhs.wait()
    load_qkv.wait()

    def project(tile):
        weight = qkv_w[:, :, :, :, :, tile * 256 : tile * 256 + 256].reshape(width, 256)
        gain_ref = query_gain_ref if tile < heads // 2 else key_gain_ref

        @pl.loop(0, 4)
        def _(index):
            part = pl.ds(pl.multiple_of(index * rows, rows), rows)
            both = dot(lhs[part, :], weight)
            for side in range(2):
                head = tile * 2 + side
                proj = both[:, side * HEAD_DIM : (side + 1) * HEAD_DIM]
                if head >= heads + kv_heads:
                    heads_ref[head, part, :] = proj.astype(BF)
                    continue
                proj_ref[head, part, :] = proj
                scales = lax.rsqrt(jnp.mean(proj * proj, axis=-1, keepdims=True) + EPSILON)
                gained = proj * scales * gain_ref[...]
                turned = pltpu.roll(gained, HEAD_DIM // 2, 1)
                heads_ref[head, part, :] = (
                    gained * cos_ref[part, :] + turned * sin_ref[part, :]
                ).astype(BF)

    for tile in range((heads + 2 * kv_heads) // 2):
        project(tile)
    out.forward()
    second.send()

    def attend(head):
        pair_head = head // 2
        for block in range(4):
            end = (block + 1) * rows
            part = pl.ds(block * rows, rows)
            scores = contract_cols(
                heads_ref[head, part, :], heads_ref[heads + pair_head, 0:end, :]
            ) * (HEAD_DIM ** (-0.5))
            row_place = lax.broadcasted_iota(jnp.int32, (rows, end), 0) + block * rows
            col_place = lax.broadcasted_iota(jnp.int32, (rows, end), 1)
            allowed = (seg_col_ref[part, :] == seg_row_ref[:, 0:end]) & (col_place <= row_place)
            scores = jnp.where(allowed, scores, NEGATIVE)
            highest = jnp.max(scores, axis=-1, keepdims=True)
            raised = jnp.exp(scores - highest)
            sums = jnp.sum(raised, axis=-1, keepdims=True)
            weights = (raised * (1.0 / sums)).astype(BF)
            mixed = dot(weights, heads_ref[heads + kv_heads + pair_head, 0:end, :])
            lane = pl.ds(pl.multiple_of(head * HEAD_DIM, HEAD_DIM), HEAD_DIM)
            mixed_ref[part, lane] = mixed.astype(BF)
            lse_ref[head, part, :] = highest + jnp.log(sums)

    pl.loop(0, heads // 2)(attend)
    dy.forward()
    first.forward()
    down.send()
    pl.loop(heads // 2, heads)(attend)

    out.arrive()
    load_out = pltpu.make_async_copy(out_full, out_w, load_sem.at[2])
    load_out.start()
    load_out.wait()

    def out_piece(seq, column):
        part = pl.ds(pl.multiple_of(seq * rows, rows), rows)
        weight = out_w[:, :, column]
        return dot(mixed_ref[part, :], weight.reshape(-1, weight.shape[-1]))

    middle_ref[...] = hidden_ref[...].astype(F32)
    scatter_sum(here, out_piece, middle_ref, give, got, pair, far_got, (ss, sr), width, 512)
    norm_rows(middle_ref, mlp_gain_ref, own_rows.at[1])
    n2.send()
    second.forward()
    n2.forward()
    n2.arrive()
    load_lhs = pltpu.make_async_copy(n2_full, lhs, load_sem.at[3])
    load_lhs.start()
    first.arrive()
    load_lhs.wait()

    def feed(gather, chunk):
        tiles = units // 2 // 256
        block = gather.whole.shape[:-1] + (256,)

        def body(gate_w, up_w, gate_ref, up_ref, act_ref):
            gate_tile = gate_w[...].reshape(width, 256)
            up_tile = up_w[...].reshape(width, 256)

            @pl.loop(0, 4)
            def _(index):
                part = pl.ds(pl.multiple_of(index * rows, rows), rows)
                gate = dot(lhs[part, :], gate_tile)
                up = dot(lhs[part, :], up_tile)
                gate_ref[part, :] = gate
                up_ref[part, :] = up
                act_ref[part, :] = (gate * jax.nn.sigmoid(gate) * up).astype(BF)

        spot = pl.BlockSpec((length, 256), lambda t: (0, t + chunk * tiles))
        pltpu.emit_pipeline(
            body,
            grid=(tiles,),
            in_specs=[
                pl.BlockSpec(block, lambda t: (0, 0, 0, 0, 0, t)),
                pl.BlockSpec(block, lambda t: (0, 0, 0, 0, 0, t + tiles)),
            ],
            out_specs=[spot, spot, spot],
        )(gather.whole, gather.whole, gate_out, up_out, act_out)

    feed(first, 0)
    down.forward()
    second.arrive()
    feed(second, 1)
    dy.arrive()
    down.arrive()
    for gather in (qkv, out, first, second, down, n1, n2, dy):
        gather.finish()


def forward(
    hidden, upstream, qkv_own, out_own, first_own, second_own, down_own, gains, tables, segment
):
    size = lax.axis_size("shard")
    quarter, outer = size // 4, size // 2
    piece, width = hidden.shape
    length = piece * 4
    heads = Q_HEADS // 4
    kv_heads = KV_HEADS // 4
    units = size * down_own.shape[0]

    def whole(own):
        return jax.ShapeDtypeStruct((2, quarter, 2, 4) + own.shape[2:], BF)

    def shape(*dims, kind=BF):
        return jax.ShapeDtypeStruct(dims, kind)

    results = [
        whole(qkv_own),
        shape(quarter, *out_own.shape),
        whole(first_own),
        whole(second_own),
        shape(size, *down_own.shape),
        shape(length, width),
        shape(length, width),
        shape(length, width),
        shape(length, units, kind=F32),
        shape(length, units, kind=F32),
        shape(length, units),
        shape(heads + kv_heads, length, HEAD_DIM, kind=F32),
        shape(heads + 2 * kv_heads, length, HEAD_DIM),
        shape(length, heads * HEAD_DIM),
        shape(heads, length, 1, kind=F32),
        shape(piece, width, kind=F32),
    ]
    dma = pltpu.SemaphoreType.DMA
    return pl.pallas_call(
        functools.partial(forward_kernel, size),
        out_shape=results,
        in_specs=[VMEM] + [ANY] * 6 + [VMEM] * 8,
        out_specs=[ANY] * 11 + [VMEM] * 5,
        scratch_shapes=[
            pltpu.VMEM((length, width), BF),
            pltpu.VMEM(whole(qkv_own).shape, BF),
            pltpu.VMEM((quarter,) + out_own.shape, BF),
            pltpu.VMEM((2, piece, width), BF),
            pltpu.VMEM((2, piece, width), BF),
            pltpu.VMEM((2, piece, width), BF),
            pltpu.VMEM((piece, width), BF),
            pltpu.VMEM((piece, width), BF),
            dma((5, outer)),
            dma((5, outer)),
            dma((5, outer)),
            dma((5, outer)),
            dma((5,)),
            dma((3, 3)),
            dma((3, 3)),
            dma((3,)),
            dma((4,)),
            dma((3,)),
            dma((3,)),
        ],
        compiler_params=pltpu.CompilerParams(
            collective_id=0, has_side_effects=True, vmem_limit_bytes=VMEM_BYTES
        ),
        name="forward_gather",
    )(
        hidden,
        upstream,
        qkv_own,
        out_own,
        first_own,
        second_own,
        down_own,
        *gains,
        *tables,
        segment.reshape(length, 1),
        segment.reshape(1, length),
    )


def mix(value):
    outer = lax.axis_size("shard") // 2
    lead = value.shape[:-1]
    blocks = value.reshape(lead + (4, outer, 2, value.shape[-1] // (8 * outer)))
    at = len(lead)
    blocks = blocks.transpose(tuple(range(at)) + (at + 2, at + 1, at, at + 3))
    return blocks.reshape(value.shape)


def unmix(value):
    outer = lax.axis_size("shard") // 2
    lead = value.shape[:-1]
    blocks = value.reshape(lead + (2, outer, 4, value.shape[-1] // (8 * outer)))
    at = len(lead)
    blocks = blocks.transpose(tuple(range(at)) + (at + 2, at + 1, at, at + 3))
    return blocks.reshape(value.shape)


def mix_rows(own):
    rows, width = own.shape
    return own.reshape(2, 2, rows // 4, width).transpose(1, 0, 2, 3)


def other_core(value):
    return lax.ppermute(value, "seq", [(i, i ^ 1) for i in range(4)])


def other_chip(value):
    return lax.ppermute(value, "seq", [(i, i ^ 2) for i in range(4)])


def gather_tokens(own):
    chip, core = lax.axis_index("seq") // 2, lax.axis_index("seq") % 2
    far = other_chip(own)
    pair = jnp.where(chip == 0, jnp.stack([own, far]), jnp.stack([far, own]))
    mate = other_core(pair)
    first = jnp.where(core == 0, pair, mate)
    second = jnp.where(core == 0, mate, pair)
    return jnp.stack([first, second], axis=1).reshape(4 * own.shape[0], own.shape[1])


def scatter_tokens(part):
    chip, core = lax.axis_index("seq") // 2, lax.axis_index("seq") % 2
    rows = part.shape[0] // 4
    blocks = part.reshape(2, 2, rows, part.shape[1])
    give = lax.dynamic_index_in_dim(blocks, 1 - core, 1, keepdims=False).astype(BF)
    keep = lax.dynamic_index_in_dim(blocks, core, 1, keepdims=False)
    pair = keep + other_core(give).astype(F32)
    give = lax.dynamic_index_in_dim(pair, 1 - chip, 0, keepdims=False).astype(BF)
    keep = lax.dynamic_index_in_dim(pair, chip, 0, keepdims=False)
    return keep + other_chip(give).astype(F32)


def outer_shift(value, amount):
    size = lax.axis_size("shard")
    outer = size // 2
    return lax.ppermute(
        value, "shard", [(i, (i // 2 + amount) % outer * 2 + i % 2) for i in range(size)]
    )


def inner_swap(value):
    return lax.ppermute(value, "shard", [(i, i ^ 1) for i in range(lax.axis_size("shard"))])


def split_columns(left):
    half = lax.axis_index("shard") % 2
    count = left.shape[1] // 2
    return (
        lax.dynamic_slice_in_dim(left, half * count, count, 1),
        lax.dynamic_slice_in_dim(left, (1 - half) * count, count, 1),
    )


def sum_terms(mine, theirs, right):
    outer = lax.axis_size("shard") // 2
    place = lax.axis_index("shard") // 2
    arrived = inner_swap(contract_rows(theirs, right).astype(BF))
    total = contract_rows(mine, right) + arrived.astype(F32)
    blocks = total.reshape(outer, total.shape[0] // outer, total.shape[1])
    result = lax.dynamic_index_in_dim(blocks, place, 0, keepdims=False)
    sent = blocks.astype(BF)
    for amount in range(1, outer):
        block = lax.dynamic_index_in_dim(sent, (place + amount) % outer, 0, keepdims=False)
        result = result + outer_shift(block, amount).astype(F32)
    return result


def own_rows(summed):
    blocks = summed.astype(BF).reshape(4, summed.shape[0] // 4, summed.shape[1])
    return lax.all_to_all(blocks, "seq", split_axis=0, concat_axis=0, tiled=True).astype(F32)


def local(
    hidden_in,
    segment_ids,
    norm_attn_gain,
    w_query,
    w_key,
    w_value,
    query_gain,
    key_gain,
    w_out,
    norm_mlp_gain,
    w_gate,
    w_up,
    w_down,
    out_cotangent,
):
    size = lax.axis_size("shard")
    seq = lax.axis_index("seq")
    _, piece_len, width = hidden_in.shape
    length = piece_len * 4
    heads = Q_HEADS // 4
    kv_heads = KV_HEADS // 4
    group = Q_HEADS // KV_HEADS
    scale = HEAD_DIM ** (-0.5)
    ff_part = w_down.shape[0] // 4
    q_part = heads * HEAD_DIM
    kv_part = kv_heads * HEAD_DIM
    units = size * ff_part
    chunk = units // 2

    def columns(weight, count):
        return lax.dynamic_slice_in_dim(weight, seq * count, count, 1)

    def own_units(weight):
        blocks = weight.reshape(weight.shape[0], size, 4, ff_part)
        return lax.dynamic_index_in_dim(blocks, seq, 2, keepdims=False).reshape(
            weight.shape[0], units
        )

    qkv_own = mix_rows(
        jnp.concatenate(
            [columns(w_query, q_part), columns(w_key, kv_part), columns(w_value, kv_part)], axis=1
        )
    )
    gate_own, up_own = own_units(w_gate), own_units(w_up)
    first_own, second_own = (
        mix_rows(jnp.concatenate([gate_own[:, at : at + chunk], up_own[:, at : at + chunk]], axis=1))
        for at in (0, chunk)
    )
    down_own = mix(lax.dynamic_slice_in_dim(w_down, seq * ff_part, ff_part, 0))
    hidden_own = mix(hidden_in[0])
    upstream_own = mix(out_cotangent[0])
    attn_gain, mlp_gain = mix(norm_attn_gain), mix(norm_mlp_gain)
    segment = segment_ids[0]
    places = jnp.arange(length, dtype=jnp.int32)
    starts = jnp.sum((segment[None, :] < segment[:, None]).astype(jnp.int32), axis=1)
    cosine, sine = rotary_tables(places - starts)
    signs = jnp.where(jnp.arange(HEAD_DIM) < HEAD_DIM // 2, -1.0, 1.0).astype(F32)
    (
        qkv_full,
        out_full,
        first_full,
        second_full,
        down_full,
        attn_in,
        upstream,
        mlp_in,
        gate_proj,
        up_proj,
        activated,
        projections,
        heads_all,
        attended,
        log_totals,
        middle,
    ) = forward(
        hidden_own,
        upstream_own,
        qkv_own,
        mix(w_out),
        first_own,
        second_own,
        down_own,
        (attn_gain[None], mlp_gain[None], query_gain[None], key_gain[None]),
        (cosine[:, 0], sine[:, 0] * signs),
        segment,
    )
    qkv_full = qkv_full.reshape(width, -1)
    out_full = out_full.reshape(-1, width)
    first_full = first_full.reshape(width, -1)
    second_full = second_full.reshape(width, -1)
    down_full = down_full.reshape(-1, width)

    hidden = hidden_own.astype(F32)
    normed_one, scale_one = normalize(hidden)
    normed_two, scale_two = normalize(middle)
    mlp_out = scatter_tokens(dot(activated, down_full))
    hidden_out = (middle + mlp_out).astype(BF)

    down_terms = sum_terms(*split_columns(upstream), activated)
    mlp_mine, mlp_theirs = split_columns(mlp_in)
    pair_terms = []
    update = 0.0
    for at, weight in ((0, first_full), (chunk, second_full)):
        gate, up = gate_proj[:, at : at + chunk], up_proj[:, at : at + chunk]
        sigmoid_gate = jax.nn.sigmoid(gate)
        act_grad = contract_cols(upstream, down_full[at : at + chunk])
        gate_grad = (act_grad * up * sigmoid_gate * (1.0 + gate * (1.0 - sigmoid_gate))).astype(BF)
        up_grad = (act_grad * gate * sigmoid_gate).astype(BF)
        both = jnp.concatenate([gate_grad, up_grad], axis=1)
        pair_terms.append(sum_terms(mlp_mine, mlp_theirs, both))
        update = update + contract_cols(both, weight)
    update = scatter_tokens(update)
    mlp_gain_grad = jnp.sum(update * normed_two, axis=0)
    middle_grad = upstream_own.astype(F32) + norm_back(update * mlp_gain, normed_two, scale_two)
    attn_grad = gather_tokens(middle_grad.astype(BF))
    mixed_grad = contract_cols(attn_grad, out_full).astype(BF)

    queries, keys, values = (
        heads_all[:heads].reshape(kv_heads, group, length, HEAD_DIM),
        heads_all[heads : heads + kv_heads],
        heads_all[heads + kv_heads :],
    )
    out_grad_all = mixed_grad.reshape(length, kv_heads, group, HEAD_DIM).transpose(1, 2, 0, 3)
    totals = log_totals.reshape(kv_heads, group, length, 1)
    block_rows = min(512, length)
    key_total = jnp.zeros((kv_heads, length, HEAD_DIM), F32)
    value_total = jnp.zeros((kv_heads, length, HEAD_DIM), F32)
    query_parts = []
    for offset in range(0, length, block_rows):
        end = offset + block_rows
        q_block = queries[:, :, offset:end]
        out_grad = out_grad_all[:, :, offset:end]
        allowed = (segment[offset:end, None] == segment[None, :end]) & (
            places[None, :end] <= places[offset:end, None]
        )
        scores = (
            jnp.einsum("kgqd,ktd->kgqt", q_block, keys[:, :end], preferred_element_type=F32) * scale
        )
        weights = jnp.exp(jnp.where(allowed, scores, NEGATIVE) - totals[:, :, offset:end])
        weight_grad = jnp.einsum(
            "kgqd,ktd->kgqt", out_grad, values[:, :end], preferred_element_type=F32
        )
        inner_sum = jnp.sum(weights * weight_grad, axis=-1, keepdims=True)
        score_grad = (weights * (weight_grad - inner_sum)).astype(BF)
        query_part = (
            jnp.einsum("kgqt,ktd->kgqd", score_grad, keys[:, :end], preferred_element_type=F32)
            * scale
        )
        query_parts.append(query_part.astype(BF))
        key_part = (
            jnp.einsum("kgqt,kgqd->ktd", score_grad, q_block, preferred_element_type=F32) * scale
        )
        value_part = jnp.einsum(
            "kgqt,kgqd->ktd", weights.astype(BF), out_grad, preferred_element_type=F32
        )
        key_total = key_total.at[:, :end].add(key_part)
        value_total = value_total.at[:, :end].add(value_part)
    query_rot_grad = jnp.concatenate(query_parts, axis=2).reshape(heads, length, HEAD_DIM)
    rot_grad = jnp.concatenate([query_rot_grad, key_total.astype(BF)], axis=0).astype(F32)
    value_grad = value_total.astype(BF)
    head_hat, head_scale = normalize(projections)
    gained_grad = rot_grad * cosine[:, 0] + rotate_back(rot_grad * sine[:, 0])
    gain_grads = jnp.sum(gained_grad * head_hat, axis=1)
    query_gain_grad = jnp.sum(gain_grads[:heads], axis=0)
    key_gain_grad = jnp.sum(gain_grads[heads:], axis=0)
    gains = jnp.concatenate(
        [jnp.broadcast_to(query_gain, (heads, 1, HEAD_DIM)), jnp.broadcast_to(key_gain, (kv_heads, 1, HEAD_DIM))]
    )
    proj_grads = norm_back(gained_grad * gains, head_hat, head_scale).astype(BF)
    proj_grads = jnp.concatenate([proj_grads, value_grad], axis=0)
    proj_grads = proj_grads.transpose(1, 0, 2).reshape(length, q_part + 2 * kv_part)
    out_rows = q_part // size
    out_left = attended.reshape(length, size // 2, 2, out_rows).transpose(2, 0, 1, 3)
    out_left = out_left.reshape(2, length, q_part // 2)
    half = lax.axis_index("shard") % 2
    grad_out = unmix(
        sum_terms(
            lax.dynamic_index_in_dim(out_left, half, 0, keepdims=False),
            lax.dynamic_index_in_dim(out_left, 1 - half, 0, keepdims=False),
            attn_grad,
        )
    )
    qkv_terms = sum_terms(*split_columns(attn_in), proj_grads)
    attn_in_grad = scatter_tokens(contract_cols(proj_grads, qkv_full))
    attn_gain_grad = jnp.sum(attn_in_grad * normed_one, axis=0)
    grad_in = middle_grad + norm_back(attn_in_grad * attn_gain, normed_one, scale_one)
    gain_totals = lax.psum(
        (attn_gain_grad, query_gain_grad, key_gain_grad, mlp_gain_grad), ("seq", "shard")
    )

    def units_back(blocks):
        rows = blocks[0].shape[1]
        count = blocks[0].shape[2] // ff_part
        blocks = [
            block.reshape(4, rows, count, ff_part).transpose(1, 2, 0, 3) for block in blocks
        ]
        return jnp.concatenate(blocks, axis=1).reshape(rows, 4 * units)

    def side_by_side(blocks):
        return blocks.transpose(1, 0, 2).reshape(blocks.shape[1], 4 * blocks.shape[2])

    qkv_rows = own_rows(qkv_terms)
    pair_rows = [own_rows(terms) for terms in pair_terms]
    return (
        unmix(hidden_out)[None],
        unmix(grad_in)[None],
        unmix(gain_totals[0]),
        side_by_side(qkv_rows[:, :, :q_part]),
        side_by_side(qkv_rows[:, :, q_part : q_part + kv_part]),
        side_by_side(qkv_rows[:, :, q_part + kv_part :]),
        gain_totals[1],
        gain_totals[2],
        grad_out,
        unmix(gain_totals[3]),
        units_back([pair[:, :, :chunk] for pair in pair_rows]),
        units_back([pair[:, :, chunk:] for pair in pair_rows]),
        units_back([own_rows(down_terms)]).T,
    )


def solution(mesh):
    return jax.shard_map(
        local,
        mesh=mesh,
        in_specs=(
            P("shard", "seq", None),
            P("shard", None),
            P(),
            P("shard", None),
            P("shard", None),
            P("shard", None),
            P(),
            P(),
            P("shard", None),
            P(),
            P("shard", None),
            P("shard", None),
            P("shard", None),
            P("shard", "seq", None),
        ),
        out_specs=(
            P("shard", "seq", None),
            P("shard", "seq", None),
            P(),
            P(("seq", "shard"), None),
            P(("seq", "shard"), None),
            P(("seq", "shard"), None),
            P(),
            P(),
            P(("seq", "shard"), None),
            P(),
            P(("seq", "shard"), None),
            P(("seq", "shard"), None),
            P(None, ("seq", "shard")),
        ),
        check_vma=False,
    )
```

```python
import functools

import jax
import jax.numpy as jnp
from jax import lax
from jax.experimental import pallas as pl
from jax.experimental.pallas import tpu as pltpu
from jax.sharding import PartitionSpec as P

Q_HEADS = 16
KV_HEADS = 8
HEAD_DIM = 128
EPSILON = 1e-06
ROPE_BASE = 1000000.0
NEGATIVE = -1e30
BF = jnp.bfloat16
F32 = jnp.float32
MESH = pl.DeviceIdType.MESH
ANY = pl.BlockSpec(memory_space=pl.ANY)
VMEM = pl.BlockSpec(memory_space=pltpu.VMEM)
VMEM_BYTES = 60 * 1024 * 1024


def normalize(values):
    scales = lax.rsqrt(jnp.mean(values * values, axis=-1, keepdims=True) + EPSILON)
    return (values * scales, scales)


def norm_back(upper, normed, scales):
    return scales * (upper - normed * jnp.mean(upper * normed, axis=-1, keepdims=True))


def rotate(values):
    middle = values.shape[-1] // 2
    return jnp.concatenate([-values[..., middle:], values[..., :middle]], axis=-1)


def rotate_back(values):
    middle = values.shape[-1] // 2
    return jnp.concatenate([values[..., middle:], -values[..., :middle]], axis=-1)


def positions_of(segment):
    places = jnp.arange(segment.shape[0], dtype=jnp.int32)
    fresh = jnp.concatenate([jnp.ones((1,), jnp.bool_), segment[1:] != segment[:-1]])
    return places - lax.cummax(jnp.where(fresh, places, 0), axis=0)


def rotary_tables(positions):
    inverse = ROPE_BASE ** (-(jnp.arange(HEAD_DIM // 2, dtype=F32) * 2.0) / HEAD_DIM)
    angles = positions.astype(F32)[:, None] * inverse[None, :]
    angles = jnp.concatenate([angles, angles], axis=-1)
    return (jnp.cos(angles)[:, None, :], jnp.sin(angles)[:, None, :])


def dot(left, right):
    return jnp.dot(left, right, preferred_element_type=F32)


def contract_rows(left, right):
    return lax.dot_general(left, right, (((0,), (0,)), ((), ())), preferred_element_type=F32)


def contract_cols(left, right):
    return lax.dot_general(left, right, (((1,), (1,)), ((), ())), preferred_element_type=F32)


def head_back(rotated_grad, cosine, sine, head_hat, head_scale, gain):
    gained_grad = rotated_grad * cosine + rotate_back(rotated_grad * sine)
    gain_grad = jnp.sum(gained_grad * head_hat, axis=(0, 1))
    return (norm_back(gained_grad * gain, head_hat, head_scale), gain_grad)


class Place:
    def __init__(self, size):
        self.size = size
        self.outer = size // 2
        self.quarter = size // 4
        self.seq = lax.axis_index("seq")
        self.shard = lax.axis_index("shard")
        self.chip = self.seq // 2
        self.core = lax.rem(self.seq, 2)
        self.place = self.shard // 2
        self.half = lax.rem(self.shard, 2)
        self.far_seq = lax.rem(self.seq + 2, 4)
        self.mate_seq = self.chip * 2 + 1 - self.core
        self.far = {"seq": self.far_seq}
        self.mate = {"seq": self.mate_seq}
        self.twin_shard = self.place * 2 + 1 - self.half
        self.twin = {"shard": self.twin_shard}

    def outer_peer(self, place):
        return {"shard": place * 2 + self.half}

    def greet(self):
        barrier = pltpu.get_barrier_semaphore()
        last = self.outer - 1

        def signal(peer):
            pl.semaphore_signal(barrier, inc=1, device_id=peer, device_id_type=MESH)

        for peer in (self.far, self.mate, self.twin):
            signal(peer)

        @pl.when(self.place < last)
        def _():
            signal(self.outer_peer(self.place + 1))

        @pl.when(self.place > 0)
        def _():
            signal(self.outer_peer(self.place - 1))

        inner = ((self.place > 0) & (self.place < last)).astype(jnp.int32)
        pl.semaphore_wait(barrier, 4 + inner)


def remote(source, target, send, receive, peer):
    return pltpu.make_async_remote_copy(
        src_ref=source,
        dst_ref=target,
        send_sem=send,
        recv_sem=receive,
        device_id=peer,
        device_id_type=MESH,
    )


class RowGather:
    def __init__(self, here, own, whole, sems):
        self.here, self.own, self.whole = here, own, whole
        self.us, self.ur, self.ds, self.dr, self.ys, self.yr, self.local = sems
        self.last = here.outer - 1

    def slot(self, place):
        return self.whole.at[place * 2 + self.here.half]

    def keep(self):
        return pltpu.make_async_copy(self.own, self.slot(self.here.place), self.local)

    def up(self, distance):
        here = self.here
        slot = self.slot(here.place - distance)
        source = slot if distance else self.own
        peer = here.outer_peer(here.place + 1)
        return remote(source, slot, self.us.at[distance], self.ur.at[distance], peer)

    def down(self, distance):
        here = self.here
        slot = self.slot(here.place + distance)
        source = slot if distance else self.own
        peer = here.outer_peer(here.place - 1)
        return remote(source, slot, self.ds.at[distance], self.dr.at[distance], peer)

    def across(self, place, own=False):
        slot = self.slot(place)
        source = self.own if own else slot
        return remote(source, slot, self.ys.at[place], self.yr.at[place], self.here.twin)

    def send(self):
        here = self.here

        @pl.when(here.place < self.last)
        def _():
            self.up(0).start()

        @pl.when(here.place > 0)
        def _():
            self.down(0).start()

        self.across(here.place, own=True).start()
        self.keep().start()

    def step(self, distance):
        here = self.here
        below = here.place - 1 - distance
        above = here.place + 1 + distance

        @pl.when(below >= 0)
        def _():
            slot = self.slot(below)
            remote(
                slot, slot, self.us.at[0], self.ur.at[distance], self.here.twin
            ).wait_recv()

            @pl.when(here.place < self.last)
            def _():
                self.up(distance + 1).start()

            self.across(below).start()

        @pl.when(above <= self.last)
        def _():
            slot = self.slot(above)
            remote(
                slot, slot, self.ds.at[0], self.dr.at[distance], self.here.twin
            ).wait_recv()

            @pl.when(here.place > 0)
            def _():
                self.down(distance + 1).start()

            self.across(above).start()

    def arrive(self):
        self.keep().wait()
        for place in range(self.here.outer):
            slot = self.whole.at[place * 2 + 1 - self.here.half]
            remote(
                slot, slot, self.ys.at[place], self.yr.at[place], self.here.twin
            ).wait_recv()

    def finish(self):
        here = self.here
        for distance in range(self.last):

            @pl.when((here.place - distance >= 0) & (here.place < self.last))
            def _():
                self.up(distance).wait_send()

            @pl.when((here.place + distance <= self.last) & (here.place > 0))
            def _():
                self.down(distance).wait_send()

        for place in range(here.outer):
            self.across(place).wait_send()


class HeadGather:
    def __init__(self, here, own, whole, sems):
        self.here, self.own, self.whole = here, own, whole
        self.us, self.zr, self.ds, _, self.ys, self.yr, self.local = sems
        self.last = here.outer - 1
        self.count = here.quarter // 2
        self.first = here.seq * self.count
        self.mine = here.place - self.first
        self.inside = (self.mine >= 0) & (self.mine < self.count)

    def slot(self, index):
        return self.whole.at[index * 2 + self.here.half]

    def keep(self):
        return pltpu.make_async_copy(self.own, self.slot(self.mine), self.local)

    def up(self, index, own=False):
        slot = self.slot(index)
        peer = self.here.outer_peer(self.here.place + 1)
        return remote(self.own if own else slot, slot, self.us.at[index], self.zr.at[index], peer)

    def down(self, index, own=False):
        slot = self.slot(index)
        peer = self.here.outer_peer(self.here.place - 1)
        return remote(self.own if own else slot, slot, self.ds.at[index], self.zr.at[index], peer)

    def across(self, index):
        slot = self.slot(index)
        return remote(slot, slot, self.ys.at[index], self.yr.at[index], self.here.twin)

    def send(self):
        @pl.when(self.inside)
        def _():
            self.keep().start()

            @pl.when(self.here.place < self.last)
            def _():
                self.up(self.mine, own=True).start()

            @pl.when(self.here.place > 0)
            def _():
                self.down(self.mine, own=True).start()

    def step(self):
        here = self.here

        @pl.when(self.inside)
        def _():
            self.keep().wait()

        for index in range(self.count):
            slot = self.slot(index)
            arrival = remote(slot, slot, self.us.at[0], self.zr.at[index], here.twin)

            @pl.when(self.mine > index)
            def _():
                arrival.wait_recv()

                @pl.when(here.place < self.last)
                def _():
                    self.up(index).start()

            @pl.when(self.mine < index)
            def _():
                arrival.wait_recv()

                @pl.when(here.place > 0)
                def _():
                    self.down(index).start()

            self.across(index).start()

    def arrive(self):
        for index in range(self.count):
            slot = self.whole.at[index * 2 + 1 - self.here.half]
            remote(
                slot, slot, self.ys.at[index], self.yr.at[index], self.here.twin
            ).wait_recv()

    def finish(self):
        here = self.here
        for index in range(self.count):

            @pl.when((self.mine >= index) & (here.place < self.last))
            def _():
                self.up(index).wait_send()

            @pl.when((self.mine <= index) & (here.place > 0))
            def _():
                self.down(index).wait_send()

            self.across(index).wait_send()


class TokenGather:
    def __init__(self, here, own, whole, sems):
        self.here, self.own, self.whole = here, own, whole
        self.send_sems, self.recv_sems, self.local = sems
        self.rows = whole.shape[0] // 4

    def slot(self, seq):
        return self.whole.at[pl.ds(pl.multiple_of(seq * self.rows, self.rows), self.rows), :]

    def keep(self):
        return pltpu.make_async_copy(self.own, self.slot(self.here.seq), self.local)

    def copy(self, index):
        here = self.here
        slot = self.slot(here.far_seq if index == 2 else here.seq)
        return remote(
            slot if index == 2 else self.own,
            slot,
            self.send_sems.at[index],
            self.recv_sems.at[index],
            here.far if index == 0 else here.mate,
        )

    def send(self):
        self.copy(0).start()
        self.copy(1).start()
        self.keep().start()

    def forward(self):
        self.copy(0).wait_recv()
        self.copy(2).start()

    def arrive(self):
        self.copy(1).wait_recv()
        self.copy(2).wait_recv()
        self.keep().wait()

    def finish(self):
        for index in range(3):
            self.copy(index).wait_send()


def scatter_sum(here, piece, base, give, got, pair, far_got, sems, width, step):
    send_sems, recv_sems = sems
    other = 1 - here.chip
    to_mate = [
        remote(
            give.at[chip], got.at[chip], send_sems.at[index], recv_sems.at[index], here.mate
        )
        for index, chip in enumerate((other, here.chip))
    ]
    to_far = remote(pair, far_got, send_sems.at[2], recv_sems.at[2], here.far)

    def columns(body):
        @pl.loop(0, width // step)
        def _(index):
            body(pl.ds(pl.multiple_of(index * step, step), step))

    for index, chip in enumerate((other, here.chip)):
        seq = chip * 2 + 1 - here.core

        def fill(column, chip=chip, seq=seq):
            give[chip, :, column] = piece(seq, column).astype(BF)

        columns(fill)
        to_mate[index].start()

    to_mate[0].wait_recv()

    def fill_pair(column):
        term = piece(here.far_seq, column) + got[other, :, column].astype(F32)
        pair[:, column] = term.astype(BF)

    columns(fill_pair)
    to_far.start()
    to_mate[1].wait_recv()

    def fill_base(column):
        base[:, column] += piece(here.seq, column) + got[here.chip, :, column].astype(F32)

    columns(fill_base)
    to_far.wait_recv()

    def fill_far(column):
        base[:, column] += far_got[:, column].astype(F32)

    columns(fill_far)
    for copy in (*to_mate, to_far):
        copy.wait_send()


def forward_kernel(
    size,
    hidden_ref,
    dy_own,
    w_query,
    w_key,
    w_value,
    w_out,
    w_gate,
    w_up,
    w_down,
    attn_gain_ref,
    mlp_gain_ref,
    query_gain_ref,
    key_gain_ref,
    cos_ref,
    sin_ref,
    seg_col_ref,
    seg_row_ref,
    qkv_full,
    out_full,
    first_full,
    second_full,
    down_full,
    n1_full,
    dy_full,
    n2_full,
    gate_out,
    up_out,
    act_out,
    proj_ref,
    heads_ref,
    mixed_ref,
    lse_ref,
    middle_ref,
    lhs,
    qkv_w,
    out_w,
    qkv_own,
    gate_all,
    up_all,
    first_own,
    second_own,
    own_rows,
    give,
    got,
    pair,
    far_got,
    us,
    ur,
    ds,
    dr,
    ys,
    yr,
    row_local,
    ts,
    tr,
    token_local,
    load_sem,
    ss,
    sr,
):
    here = Place(size)
    length, width = lhs.shape
    rows = length // 4
    units = gate_out.shape[1]
    chunk = units // 2
    heads = lse_ref.shape[0]
    kv_heads = heads // 2
    ff_part = units // size

    def sems(index):
        return tuple(kind.at[index] for kind in (us, ur, ds, dr, ys, yr, row_local))

    down_rows = pl.ds(pl.multiple_of(here.seq * ff_part, ff_part), ff_part)
    qkv = RowGather(here, qkv_own, qkv_full, sems(0))
    out = HeadGather(here, w_out, out_full, sems(1))
    first = RowGather(here, first_own, first_full, sems(2))
    second = RowGather(here, second_own, second_full, sems(3))
    down = RowGather(here, w_down.at[down_rows, :], down_full, sems(4))
    n1 = TokenGather(here, own_rows.at[0], n1_full, (ts.at[0], tr.at[0], token_local.at[0]))
    n2 = TokenGather(here, own_rows.at[1], n2_full, (ts.at[1], tr.at[1], token_local.at[1]))
    dy = TokenGather(here, dy_own, dy_full, (ts.at[2], tr.at[2], token_local.at[2]))

    loads = []
    at = 0
    for index, (weight, count) in enumerate(((w_query, heads), (w_key, kv_heads), (w_value, kv_heads))):
        count = count * HEAD_DIM
        source = weight.at[:, pl.ds(pl.multiple_of(here.seq * count, count), count)]
        loads.append(
            pltpu.make_async_copy(source, qkv_own.at[:, at : at + count], load_sem.at[index])
        )
        at += count
    loads.append(pltpu.make_async_copy(w_gate, gate_all, load_sem.at[3]))
    loads.append(pltpu.make_async_copy(w_up, up_all, load_sem.at[4]))
    for load in loads:
        load.start()
    here.greet()
    for load in loads[:3]:
        load.wait()
    qkv.send()
    out.send()

    def norm_rows(source, gain_ref, target):
        @pl.loop(0, rows // 32)
        def _(index):
            part = pl.ds(pl.multiple_of(index * 32, 32), 32)
            values = source[part, :].astype(F32)
            scales = lax.rsqrt(jnp.mean(values * values, axis=-1, keepdims=True) + EPSILON)
            target[part, :] = (values * scales * gain_ref[...]).astype(BF)

    norm_rows(hidden_ref, attn_gain_ref, own_rows.at[0])
    n1.send()
    for load in loads[3:]:
        load.wait()

    for seq in range(4):

        @pl.when(here.seq == seq)
        def _():
            @pl.loop(0, first_own.shape[0] // 16)
            def _(index):
                part = pl.ds(pl.multiple_of(index * 16, 16), 16)
                for target, begin in ((first_own, 0), (second_own, size // 2)):
                    for source, at in ((gate_all, 0), (up_all, chunk)):
                        pieces = [
                            source[part, (block * 4 + seq) * ff_part : (block * 4 + seq + 1) * ff_part]
                            for block in range(begin, begin + size // 2)
                        ]
                        target[part, at : at + chunk] = jnp.concatenate(pieces, axis=1)

    first.send()
    last = here.outer - 1
    for distance in range(last):
        qkv.step(distance)
    n1.forward()
    second.send()
    n1.arrive()
    load_lhs = pltpu.make_async_copy(n1_full, lhs, load_sem.at[0])
    load_lhs.start()
    dy.send()
    out.step()
    qkv.arrive()
    load_qkv = pltpu.make_async_copy(qkv_full, qkv_w, load_sem.at[1])
    load_qkv.start()
    load_lhs.wait()
    load_qkv.wait()

    def project(tile):
        weight = qkv_w[:, :, tile * 256 : tile * 256 + 256].reshape(width, 256)
        gain_ref = query_gain_ref if tile < heads // 2 else key_gain_ref

        @pl.loop(0, 4)
        def _(index):
            part = pl.ds(pl.multiple_of(index * rows, rows), rows)
            both = dot(lhs[part, :], weight)
            for side in range(2):
                head = tile * 2 + side
                proj = both[:, side * HEAD_DIM : (side + 1) * HEAD_DIM]
                if head >= heads + kv_heads:
                    heads_ref[head, part, :] = proj.astype(BF)
                    continue
                proj_ref[head, part, :] = proj
                scales = lax.rsqrt(jnp.mean(proj * proj, axis=-1, keepdims=True) + EPSILON)
                gained = proj * scales * gain_ref[...]
                turned = pltpu.roll(gained, HEAD_DIM // 2, 1)
                heads_ref[head, part, :] = (
                    gained * cos_ref[part, :] + turned * sin_ref[part, :]
                ).astype(BF)

    def attend(head):
        pair_head = head // 2
        for block in range(4):
            end = (block + 1) * rows
            part = pl.ds(block * rows, rows)
            scores = contract_cols(
                heads_ref[head, part, :], heads_ref[heads + pair_head, 0:end, :]
            ) * (HEAD_DIM ** (-0.5))
            row_place = lax.broadcasted_iota(jnp.int32, (rows, end), 0) + block * rows
            col_place = lax.broadcasted_iota(jnp.int32, (rows, end), 1)
            allowed = (seg_col_ref[part, :] == seg_row_ref[:, 0:end]) & (col_place <= row_place)
            scores = jnp.where(allowed, scores, NEGATIVE)
            highest = jnp.max(scores, axis=-1, keepdims=True)
            raised = jnp.exp(scores - highest)
            sums = jnp.sum(raised, axis=-1, keepdims=True)
            weights = (raised * (1.0 / sums)).astype(BF)
            mixed = dot(weights, heads_ref[heads + kv_heads + pair_head, 0:end, :])
            mixed_ref[part, head * HEAD_DIM : (head + 1) * HEAD_DIM] = mixed.astype(BF)
            lse_ref[head, part, :] = highest + jnp.log(sums)

    for tile in range((heads + 2 * kv_heads) // 2):
        project(tile)
    pending = [(first, distance) for distance in range(last)]
    pending += [(second, distance) for distance in range(last)]
    pending += [(down, distance) for distance in range(last)]

    def pump(share):
        for _ in range(max(1, last * share // 3)):
            if pending:
                gather, distance = pending.pop(0)
                gather.step(distance)

    pump(1)
    attend(0)
    pump(1)
    down.send()
    attend(1)
    pump(1)
    attend(2)
    dy.forward()
    pump(1)
    attend(3)
    pump(1)

    out.arrive()
    load_out = pltpu.make_async_copy(out_full, out_w, load_sem.at[2])
    load_out.start()
    load_out.wait()

    def out_piece(seq, column):
        part = pl.ds(pl.multiple_of(seq * rows, rows), rows)
        weight = out_w[:, :, column]
        return dot(mixed_ref[part, :], weight.reshape(-1, weight.shape[-1]))

    middle_ref[...] = hidden_ref[...].astype(F32)
    scatter_sum(here, out_piece, middle_ref, give, got, pair, far_got, (ss, sr), width, 512)
    norm_rows(middle_ref, mlp_gain_ref, own_rows.at[1])
    n2.send()
    pump(1)
    n2.forward()
    pump(1)
    n2.arrive()
    load_lhs = pltpu.make_async_copy(n2_full, lhs, load_sem.at[3])
    load_lhs.start()
    first.arrive()
    load_lhs.wait()

    def feed(gather, part_index):
        tiles = chunk // 256
        block = gather.whole.shape[:-1] + (256,)

        def body(gate_w, up_w, gate_ref, up_ref, act_ref):
            gate_tile = gate_w[...].reshape(width, 256)
            up_tile = up_w[...].reshape(width, 256)

            @pl.loop(0, 4)
            def _(index):
                part = pl.ds(pl.multiple_of(index * rows, rows), rows)
                gate = dot(lhs[part, :], gate_tile)
                up = dot(lhs[part, :], up_tile)
                gate_ref[part, :] = gate
                up_ref[part, :] = up
                act_ref[part, :] = (gate * jax.nn.sigmoid(gate) * up).astype(BF)

        spot = pl.BlockSpec((length, 256), lambda t: (0, t + part_index * tiles))
        pltpu.emit_pipeline(
            body,
            grid=(tiles,),
            in_specs=[
                pl.BlockSpec(block, lambda t: (0, 0, t)),
                pl.BlockSpec(block, lambda t: (0, 0, t + tiles)),
            ],
            out_specs=[spot, spot, spot],
        )(gather.whole, gather.whole, gate_out, up_out, act_out)

    feed(first, 0)
    while pending:
        pump(1)
    second.arrive()
    feed(second, 1)
    dy.arrive()
    down.arrive()
    for gather in (qkv, out, first, second, down, n1, n2, dy):
        gather.finish()


def forward(hidden, upstream, weights, gains, tables, segment):
    size = lax.axis_size("shard")
    quarter, outer = size // 4, size // 2
    piece, width = hidden.shape
    length = piece * 4
    heads = Q_HEADS // 4
    kv_heads = KV_HEADS // 4
    w_query, _, _, w_out, w_gate, _, w_down = weights
    own = w_query.shape[0]
    qkv_width = (heads + 2 * kv_heads) * HEAD_DIM
    units = w_down.shape[0] // 4 * size

    def shape(*dims, kind=BF):
        return jax.ShapeDtypeStruct(dims, kind)

    results = [
        shape(size, own, qkv_width),
        shape(quarter, *w_out.shape),
        shape(size, own, units),
        shape(size, own, units),
        shape(size, w_down.shape[0] // 4, width),
        shape(length, width),
        shape(length, width),
        shape(length, width),
        shape(length, units, kind=F32),
        shape(length, units, kind=F32),
        shape(length, units),
        shape(heads + kv_heads, length, HEAD_DIM, kind=F32),
        shape(heads + 2 * kv_heads, length, HEAD_DIM),
        shape(length, heads * HEAD_DIM),
        shape(heads, length, 1, kind=F32),
        shape(piece, width, kind=F32),
    ]
    dma = pltpu.SemaphoreType.DMA
    return pl.pallas_call(
        functools.partial(forward_kernel, size),
        out_shape=results,
        in_specs=[VMEM] + [ANY] * 8 + [VMEM] * 8,
        out_specs=[ANY] * 11 + [VMEM] * 5,
        scratch_shapes=[
            pltpu.VMEM((length, width), BF),
            pltpu.VMEM((size, own, qkv_width), BF),
            pltpu.VMEM((quarter,) + w_out.shape, BF),
            pltpu.VMEM((own, qkv_width), BF),
            pltpu.VMEM(w_gate.shape, BF),
            pltpu.VMEM(w_gate.shape, BF),
            pltpu.VMEM((own, units), BF),
            pltpu.VMEM((own, units), BF),
            pltpu.VMEM((2, piece, width), BF),
            pltpu.VMEM((2, piece, width), BF),
            pltpu.VMEM((2, piece, width), BF),
            pltpu.VMEM((piece, width), BF),
            pltpu.VMEM((piece, width), BF),
            dma((5, outer)),
            dma((5, outer)),
            dma((5, outer)),
            dma((5, outer)),
            dma((5, outer)),
            dma((5, outer)),
            dma((5,)),
            dma((3, 3)),
            dma((3, 3)),
            dma((3,)),
            dma((5,)),
            dma((3,)),
            dma((3,)),
        ],
        compiler_params=pltpu.CompilerParams(
            collective_id=0, has_side_effects=True, vmem_limit_bytes=VMEM_BYTES
        ),
        name="forward_gather",
    )(
        hidden,
        upstream,
        *weights,
        *gains,
        *tables,
        segment.reshape(length, 1),
        segment.reshape(1, length),
    )


def other_core(value):
    return lax.ppermute(value, "seq", [(i, i ^ 1) for i in range(4)])


def other_chip(value):
    return lax.ppermute(value, "seq", [(i, i ^ 2) for i in range(4)])


def gather_tokens(own):
    chip, core = lax.axis_index("seq") // 2, lax.axis_index("seq") % 2
    far = other_chip(own)
    pair = jnp.where(chip == 0, jnp.stack([own, far]), jnp.stack([far, own]))
    mate = other_core(pair)
    first = jnp.where(core == 0, pair, mate)
    second = jnp.where(core == 0, mate, pair)
    return jnp.stack([first, second], axis=1).reshape(4 * own.shape[0], own.shape[1])


def scatter_tokens(part):
    chip, core = lax.axis_index("seq") // 2, lax.axis_index("seq") % 2
    rows = part.shape[0] // 4
    blocks = part.reshape(2, 2, rows, part.shape[1])
    give = lax.dynamic_index_in_dim(blocks, 1 - core, 1, keepdims=False).astype(BF)
    keep = lax.dynamic_index_in_dim(blocks, core, 1, keepdims=False)
    pair = keep + other_core(give).astype(F32)
    give = lax.dynamic_index_in_dim(pair, 1 - chip, 0, keepdims=False).astype(BF)
    keep = lax.dynamic_index_in_dim(pair, chip, 0, keepdims=False)
    return keep + other_chip(give).astype(F32)


def outer_shift(value, amount):
    size = lax.axis_size("shard")
    outer = size // 2
    return lax.ppermute(
        value, "shard", [(i, (i // 2 + amount) % outer * 2 + i % 2) for i in range(size)]
    )


def inner_swap(value):
    return lax.ppermute(value, "shard", [(i, i ^ 1) for i in range(lax.axis_size("shard"))])


def sum_terms(left, right, groups):
    outer = lax.axis_size("shard") // 2
    place, half = lax.axis_index("shard") // 2, lax.axis_index("shard") % 2
    terms = contract_rows(left, right)
    rows = terms.shape[0] // (groups * outer * 2)
    terms = terms.reshape(groups, outer, 2, rows, terms.shape[1])
    theirs = lax.dynamic_index_in_dim(terms, 1 - half, 2, keepdims=False).astype(BF)
    total = lax.dynamic_index_in_dim(terms, half, 2, keepdims=False) + inner_swap(theirs).astype(F32)
    result = lax.dynamic_index_in_dim(total, place, 1, keepdims=False)
    sent = total.astype(BF)
    for amount in range(1, outer):
        block = lax.dynamic_index_in_dim(sent, (place + amount) % outer, 1, keepdims=False)
        result = result + outer_shift(block, amount).astype(F32)
    return result


def own_rows(summed):
    blocks = summed.astype(BF)
    return lax.all_to_all(blocks, "seq", split_axis=0, concat_axis=0, tiled=True).astype(F32)


def local(
    hidden_in,
    segment_ids,
    norm_attn_gain,
    w_query,
    w_key,
    w_value,
    query_gain,
    key_gain,
    w_out,
    norm_mlp_gain,
    w_gate,
    w_up,
    w_down,
    out_cotangent,
):
    size = lax.axis_size("shard")
    seq = lax.axis_index("seq")
    _, piece_len, width = hidden_in.shape
    length = piece_len * 4
    heads = Q_HEADS // 4
    kv_heads = KV_HEADS // 4
    group = Q_HEADS // KV_HEADS
    scale = HEAD_DIM ** (-0.5)
    ff_part = w_down.shape[0] // 4
    q_part = heads * HEAD_DIM
    kv_part = kv_heads * HEAD_DIM
    units = size * ff_part
    chunk = units // 2

    segment = segment_ids[0]
    places = jnp.arange(length, dtype=jnp.int32)
    starts = jnp.sum((segment[None, :] < segment[:, None]).astype(jnp.int32), axis=1)
    cosine, sine = rotary_tables(places - starts)
    signs = jnp.where(jnp.arange(HEAD_DIM) < HEAD_DIM // 2, -1.0, 1.0).astype(F32)
    (
        qkv_full,
        out_full,
        first_full,
        second_full,
        down_full,
        attn_in,
        upstream,
        mlp_in,
        gate_proj,
        up_proj,
        activated,
        projections,
        heads_all,
        attended,
        log_totals,
        middle,
    ) = forward(
        hidden_in[0],
        out_cotangent[0],
        (w_query, w_key, w_value, w_out, w_gate, w_up, w_down),
        (norm_attn_gain[None], norm_mlp_gain[None], query_gain[None], key_gain[None]),
        (cosine[:, 0], sine[:, 0] * signs),
        segment,
    )
    qkv_full = qkv_full.reshape(width, -1)
    out_full = out_full.reshape(-1, width)
    first_full = first_full.reshape(width, -1)
    second_full = second_full.reshape(width, -1)
    down_full = down_full.reshape(-1, width)

    hidden = hidden_in[0].astype(F32)
    normed_one, scale_one = normalize(hidden)
    normed_two, scale_two = normalize(middle)
    mlp_out = scatter_tokens(dot(activated, down_full))
    hidden_out = (middle + mlp_out).astype(BF)

    down_terms = sum_terms(upstream, activated, 4)
    pair_terms = []
    update = 0.0
    for at, weight in ((0, first_full), (chunk, second_full)):
        gate, up = gate_proj[:, at : at + chunk], up_proj[:, at : at + chunk]
        sigmoid_gate = jax.nn.sigmoid(gate)
        act_grad = contract_cols(upstream, down_full[at : at + chunk])
        gate_grad = (act_grad * up * sigmoid_gate * (1.0 + gate * (1.0 - sigmoid_gate))).astype(BF)
        up_grad = (act_grad * gate * sigmoid_gate).astype(BF)
        both = jnp.concatenate([gate_grad, up_grad], axis=1)
        pair_terms.append(sum_terms(mlp_in, both, 4))
        update = update + contract_cols(both, weight)
    update = scatter_tokens(update)
    mlp_gain_grad = jnp.sum(update * normed_two, axis=0)
    middle_grad = out_cotangent[0].astype(F32) + norm_back(update * norm_mlp_gain, normed_two, scale_two)
    attn_grad = gather_tokens(middle_grad.astype(BF))
    mixed_grad = contract_cols(attn_grad, out_full).astype(BF)

    queries, keys, values = (
        heads_all[:heads].reshape(kv_heads, group, length, HEAD_DIM),
        heads_all[heads : heads + kv_heads],
        heads_all[heads + kv_heads :],
    )
    out_grad_all = mixed_grad.reshape(length, kv_heads, group, HEAD_DIM).transpose(1, 2, 0, 3)
    totals = log_totals.reshape(kv_heads, group, length, 1)
    block_rows = min(512, length)
    key_total = jnp.zeros((kv_heads, length, HEAD_DIM), F32)
    value_total = jnp.zeros((kv_heads, length, HEAD_DIM), F32)
    query_parts = []
    for offset in range(0, length, block_rows):
        end = offset + block_rows
        q_block = queries[:, :, offset:end]
        out_grad = out_grad_all[:, :, offset:end]
        allowed = (segment[offset:end, None] == segment[None, :end]) & (
            places[None, :end] <= places[offset:end, None]
        )
        scores = (
            jnp.einsum("kgqd,ktd->kgqt", q_block, keys[:, :end], preferred_element_type=F32) * scale
        )
        weights = jnp.exp(jnp.where(allowed, scores, NEGATIVE) - totals[:, :, offset:end])
        weight_grad = jnp.einsum(
            "kgqd,ktd->kgqt", out_grad, values[:, :end], preferred_element_type=F32
        )
        inner_sum = jnp.sum(weights * weight_grad, axis=-1, keepdims=True)
        score_grad = (weights * (weight_grad - inner_sum)).astype(BF)
        query_part = (
            jnp.einsum("kgqt,ktd->kgqd", score_grad, keys[:, :end], preferred_element_type=F32)
            * scale
        )
        query_parts.append(query_part.astype(BF))
        key_part = (
            jnp.einsum("kgqt,kgqd->ktd", score_grad, q_block, preferred_element_type=F32) * scale
        )
        value_part = jnp.einsum(
            "kgqt,kgqd->ktd", weights.astype(BF), out_grad, preferred_element_type=F32
        )
        key_total = key_total.at[:, :end].add(key_part)
        value_total = value_total.at[:, :end].add(value_part)
    query_rot_grad = jnp.concatenate(query_parts, axis=2).reshape(heads, length, HEAD_DIM)
    rot_grad = jnp.concatenate([query_rot_grad, key_total.astype(BF)], axis=0).astype(F32)
    value_grad = value_total.astype(BF)
    head_hat, head_scale = normalize(projections)
    gained_grad = rot_grad * cosine[:, 0] + rotate_back(rot_grad * sine[:, 0])
    gain_grads = jnp.sum(gained_grad * head_hat, axis=1)
    query_gain_grad = jnp.sum(gain_grads[:heads], axis=0)
    key_gain_grad = jnp.sum(gain_grads[heads:], axis=0)
    gains = jnp.concatenate(
        [jnp.broadcast_to(query_gain, (heads, 1, HEAD_DIM)), jnp.broadcast_to(key_gain, (kv_heads, 1, HEAD_DIM))]
    )
    proj_grads = norm_back(gained_grad * gains, head_hat, head_scale).astype(BF)
    proj_grads = jnp.concatenate([proj_grads, value_grad], axis=0)
    proj_grads = proj_grads.transpose(1, 0, 2).reshape(length, q_part + 2 * kv_part)
    grad_out = sum_terms(attended, attn_grad, 1)[0]
    qkv_terms = sum_terms(attn_in, proj_grads, 4)
    attn_in_grad = scatter_tokens(contract_cols(proj_grads, qkv_full))
    attn_gain_grad = jnp.sum(attn_in_grad * normed_one, axis=0)
    grad_in = middle_grad + norm_back(attn_in_grad * norm_attn_gain, normed_one, scale_one)
    gain_totals = lax.psum(
        (attn_gain_grad, query_gain_grad, key_gain_grad, mlp_gain_grad), ("seq", "shard")
    )

    def units_back(blocks):
        rows = blocks[0].shape[1]
        count = blocks[0].shape[2] // ff_part
        blocks = [
            block.reshape(4, rows, count, ff_part).transpose(1, 2, 0, 3) for block in blocks
        ]
        return jnp.concatenate(blocks, axis=1).reshape(rows, 4 * units)

    def side_by_side(blocks):
        return blocks.transpose(1, 0, 2).reshape(blocks.shape[1], 4 * blocks.shape[2])

    qkv_rows = own_rows(qkv_terms)
    pair_rows = [own_rows(terms) for terms in pair_terms]
    return (
        hidden_out[None],
        grad_in[None],
        gain_totals[0],
        side_by_side(qkv_rows[:, :, :q_part]),
        side_by_side(qkv_rows[:, :, q_part : q_part + kv_part]),
        side_by_side(qkv_rows[:, :, q_part + kv_part :]),
        gain_totals[1],
        gain_totals[2],
        grad_out,
        gain_totals[3],
        units_back([pair[:, :, :chunk] for pair in pair_rows]),
        units_back([pair[:, :, chunk:] for pair in pair_rows]),
        units_back([own_rows(down_terms)]).T,
    )


def solution(mesh):
    return jax.shard_map(
        local,
        mesh=mesh,
        in_specs=(
            P("shard", "seq", None),
            P("shard", None),
            P(),
            P("shard", None),
            P("shard", None),
            P("shard", None),
            P(),
            P(),
            P("shard", None),
            P(),
            P("shard", None),
            P("shard", None),
            P("shard", None),
            P("shard", "seq", None),
        ),
        out_specs=(
            P("shard", "seq", None),
            P("shard", "seq", None),
            P(),
            P(("seq", "shard"), None),
            P(("seq", "shard"), None),
            P(("seq", "shard"), None),
            P(),
            P(),
            P(("seq", "shard"), None),
            P(),
            P(("seq", "shard"), None),
            P(("seq", "shard"), None),
            P(None, ("seq", "shard")),
        ),
        check_vma=False,
    )
```

```python
import functools

import jax
import jax.numpy as jnp
from jax import lax
from jax.experimental import pallas as pl
from jax.experimental.pallas import tpu as pltpu
from jax.sharding import PartitionSpec as P

Q_HEADS = 16
KV_HEADS = 8
HEAD_DIM = 128
EPSILON = 1e-06
ROPE_BASE = 1000000.0
NEGATIVE = -1e30
BF = jnp.bfloat16
F32 = jnp.float32
MESH = pl.DeviceIdType.MESH
ANY = pl.BlockSpec(memory_space=pl.ANY)
VMEM = pl.BlockSpec(memory_space=pltpu.VMEM)
VMEM_BYTES = 62 * 1024 * 1024


def rotary_tables(positions):
    inverse = ROPE_BASE ** (-(jnp.arange(HEAD_DIM // 2, dtype=F32) * 2.0) / HEAD_DIM)
    angles = positions.astype(F32)[:, None] * inverse[None, :]
    angles = jnp.concatenate([angles, angles], axis=-1)
    return (jnp.cos(angles), jnp.sin(angles))


def dot(left, right):
    return jnp.dot(left, right, preferred_element_type=F32)


def contract_rows(left, right):
    return lax.dot_general(left, right, (((0,), (0,)), ((), ())), preferred_element_type=F32)


def contract_cols(left, right):
    return lax.dot_general(left, right, (((1,), (1,)), ((), ())), preferred_element_type=F32)


class Place:
    def __init__(self, size):
        self.size = size
        self.outer = size // 2
        self.quarter = size // 4
        self.seq = lax.axis_index("seq")
        self.shard = lax.axis_index("shard")
        self.chip = self.seq // 2
        self.core = lax.rem(self.seq, 2)
        self.place = self.shard // 2
        self.half = lax.rem(self.shard, 2)
        self.far_seq = lax.rem(self.seq + 2, 4)
        self.mate_seq = self.chip * 2 + 1 - self.core
        self.far = {"seq": self.far_seq}
        self.mate = {"seq": self.mate_seq}
        self.twin_shard = self.place * 2 + 1 - self.half
        self.twin = {"shard": self.twin_shard}

    def outer_peer(self, place):
        return {"shard": place * 2 + self.half}

    def line_peers(self):
        peers = []
        step = 1
        while step < self.outer:
            sign = 1 - 2 * lax.rem(self.place // step, 2)
            peers.append(self.outer_peer(self.place + sign * step))
            step *= 2
        return peers

    def greet(self, wide=False):
        barrier = pltpu.get_barrier_semaphore()
        last = self.outer - 1

        def signal(peer):
            pl.semaphore_signal(barrier, inc=1, device_id=peer, device_id_type=MESH)

        peers = [self.far, self.mate, self.twin]
        if wide:
            peers += [{"seq": 3 - self.seq}] + self.line_peers()[1:]
        for peer in peers:
            signal(peer)

        @pl.when(self.place < last)
        def _():
            signal(self.outer_peer(self.place + 1))

        @pl.when(self.place > 0)
        def _():
            signal(self.outer_peer(self.place - 1))

        inner = ((self.place > 0) & (self.place < last)).astype(jnp.int32)
        pl.semaphore_wait(barrier, len(peers) + 1 + inner)


def remote(source, target, send, receive, peer):
    return pltpu.make_async_remote_copy(
        src_ref=source,
        dst_ref=target,
        send_sem=send,
        recv_sem=receive,
        device_id=peer,
        device_id_type=MESH,
    )


class RowGather:
    def __init__(self, here, own, whole, sems):
        self.here, self.own, self.whole = here, own, whole
        self.us, self.ur, self.ds, self.dr, self.ys, self.yr, self.local = sems
        self.last = here.outer - 1

    def slot(self, place):
        return self.whole.at[place * 2 + self.here.half]

    def keep(self):
        return pltpu.make_async_copy(self.own, self.slot(self.here.place), self.local)

    def up(self, distance):
        here = self.here
        slot = self.slot(here.place - distance)
        source = slot if distance else self.own
        peer = here.outer_peer(here.place + 1)
        return remote(source, slot, self.us.at[distance], self.ur.at[distance], peer)

    def down(self, distance):
        here = self.here
        slot = self.slot(here.place + distance)
        source = slot if distance else self.own
        peer = here.outer_peer(here.place - 1)
        return remote(source, slot, self.ds.at[distance], self.dr.at[distance], peer)

    def across(self, place, own=False):
        slot = self.slot(place)
        source = self.own if own else slot
        return remote(source, slot, self.ys.at[place], self.yr.at[place], self.here.twin)

    def send(self):
        here = self.here

        @pl.when(here.place < self.last)
        def _():
            self.up(0).start()

        @pl.when(here.place > 0)
        def _():
            self.down(0).start()

        self.across(here.place, own=True).start()
        self.keep().start()

    def step(self, distance):
        here = self.here
        below = here.place - 1 - distance
        above = here.place + 1 + distance

        @pl.when(below >= 0)
        def _():
            slot = self.slot(below)
            remote(
                slot, slot, self.us.at[0], self.ur.at[distance], self.here.twin
            ).wait_recv()

            @pl.when(here.place < self.last)
            def _():
                self.up(distance + 1).start()

            self.across(below).start()

        @pl.when(above <= self.last)
        def _():
            slot = self.slot(above)
            remote(
                slot, slot, self.ds.at[0], self.dr.at[distance], self.here.twin
            ).wait_recv()

            @pl.when(here.place > 0)
            def _():
                self.down(distance + 1).start()

            self.across(above).start()

    def arrive(self):
        self.keep().wait()
        for place in range(self.here.outer):
            slot = self.whole.at[place * 2 + 1 - self.here.half]
            remote(
                slot, slot, self.ys.at[place], self.yr.at[place], self.here.twin
            ).wait_recv()

    def finish(self):
        here = self.here
        for distance in range(self.last):

            @pl.when((here.place - distance >= 0) & (here.place < self.last))
            def _():
                self.up(distance).wait_send()

            @pl.when((here.place + distance <= self.last) & (here.place > 0))
            def _():
                self.down(distance).wait_send()

        for place in range(here.outer):
            self.across(place).wait_send()


class HeadGather:
    def __init__(self, here, own, whole, sems):
        self.here, self.own, self.whole = here, own, whole
        self.us, self.zr, self.ds, _, self.ys, self.yr, self.local = sems
        self.last = here.outer - 1
        self.count = here.quarter // 2
        self.first = here.seq * self.count
        self.mine = here.place - self.first
        self.inside = (self.mine >= 0) & (self.mine < self.count)

    def slot(self, index):
        return self.whole.at[index * 2 + self.here.half]

    def keep(self):
        return pltpu.make_async_copy(self.own, self.slot(self.mine), self.local)

    def up(self, index, own=False):
        slot = self.slot(index)
        peer = self.here.outer_peer(self.here.place + 1)
        return remote(self.own if own else slot, slot, self.us.at[index], self.zr.at[index], peer)

    def down(self, index, own=False):
        slot = self.slot(index)
        peer = self.here.outer_peer(self.here.place - 1)
        return remote(self.own if own else slot, slot, self.ds.at[index], self.zr.at[index], peer)

    def across(self, index):
        slot = self.slot(index)
        return remote(slot, slot, self.ys.at[index], self.yr.at[index], self.here.twin)

    def send(self):
        @pl.when(self.inside)
        def _():
            self.keep().start()

            @pl.when(self.here.place < self.last)
            def _():
                self.up(self.mine, own=True).start()

            @pl.when(self.here.place > 0)
            def _():
                self.down(self.mine, own=True).start()

    def step(self):
        here = self.here

        @pl.when(self.inside)
        def _():
            self.keep().wait()

        for index in range(self.count):
            slot = self.slot(index)
            arrival = remote(slot, slot, self.us.at[0], self.zr.at[index], here.twin)

            @pl.when(self.mine > index)
            def _():
                arrival.wait_recv()

                @pl.when(here.place < self.last)
                def _():
                    self.up(index).start()

            @pl.when(self.mine < index)
            def _():
                arrival.wait_recv()

                @pl.when(here.place > 0)
                def _():
                    self.down(index).start()

            self.across(index).start()

    def arrive(self):
        for index in range(self.count):
            slot = self.whole.at[index * 2 + 1 - self.here.half]
            remote(
                slot, slot, self.ys.at[index], self.yr.at[index], self.here.twin
            ).wait_recv()

    def finish(self):
        here = self.here
        for index in range(self.count):

            @pl.when((self.mine >= index) & (here.place < self.last))
            def _():
                self.up(index).wait_send()

            @pl.when((self.mine <= index) & (here.place > 0))
            def _():
                self.down(index).wait_send()

            self.across(index).wait_send()


class TokenGather:
    def __init__(self, here, own, whole, sems):
        self.here, self.own, self.whole = here, own, whole
        self.send_sems, self.recv_sems, self.local = sems
        self.rows = whole.shape[0] // 4

    def slot(self, seq):
        return self.whole.at[pl.ds(pl.multiple_of(seq * self.rows, self.rows), self.rows), :]

    def keep(self):
        return pltpu.make_async_copy(self.own, self.slot(self.here.seq), self.local)

    def copy(self, index):
        here = self.here
        slot = self.slot(here.far_seq if index == 2 else here.seq)
        return remote(
            slot if index == 2 else self.own,
            slot,
            self.send_sems.at[index],
            self.recv_sems.at[index],
            here.far if index == 0 else here.mate,
        )

    def send(self):
        self.copy(0).start()
        self.copy(1).start()
        self.keep().start()

    def forward(self):
        self.copy(0).wait_recv()
        self.copy(2).start()

    def mate_arrived(self):
        self.copy(1).wait_recv()

    def rest_arrived(self):
        self.copy(2).wait_recv()
        self.keep().wait()

    def arrive(self):
        self.mate_arrived()
        self.rest_arrived()

    def finish(self):
        for index in range(3):
            self.copy(index).wait_send()


def scatter_sum(here, piece, base, give, got, pair, far_got, sems, width, step):
    send_sems, recv_sems = sems
    other = 1 - here.chip
    to_mate = [
        remote(
            give.at[chip], got.at[chip], send_sems.at[index], recv_sems.at[index], here.mate
        )
        for index, chip in enumerate((other, here.chip))
    ]
    to_far = remote(pair, far_got, send_sems.at[2], recv_sems.at[2], here.far)

    def columns(body):
        @pl.loop(0, width // step)
        def _(index):
            body(pl.ds(pl.multiple_of(index * step, step), step))

    for index, chip in enumerate((other, here.chip)):
        seq = chip * 2 + 1 - here.core

        def fill(column, chip=chip, seq=seq):
            give[chip, :, column] = piece(seq, column).astype(BF)

        columns(fill)
        to_mate[index].start()

    to_mate[0].wait_recv()

    def fill_pair(column):
        term = piece(here.far_seq, column) + got[other, :, column].astype(F32)
        pair[:, column] = term.astype(BF)

    columns(fill_pair)
    to_far.start()
    to_mate[1].wait_recv()

    def fill_base(column):
        base[:, column] += piece(here.seq, column) + got[here.chip, :, column].astype(F32)

    columns(fill_base)
    to_far.wait_recv()

    def fill_far(column):
        base[:, column] += far_got[:, column].astype(F32)

    columns(fill_far)
    for copy in (*to_mate, to_far):
        copy.wait_send()


def forward_kernel(
    size,
    hidden_ref,
    dy_own,
    w_query,
    w_key,
    w_value,
    w_out,
    w_gate,
    w_up,
    w_down,
    attn_gain_ref,
    mlp_gain_ref,
    query_gain_ref,
    key_gain_ref,
    cos_ref,
    sin_ref,
    seg_col_ref,
    seg_row_ref,
    qkv_full,
    out_full,
    first_full,
    second_full,
    down_full,
    n1_full,
    dy_full,
    n2_full,
    gate_out,
    up_out,
    act_out,
    proj_ref,
    heads_ref,
    mixed_ref,
    lse_ref,
    middle_ref,
    lhs,
    qkv_w,
    out_w,
    qkv_own,
    gate_all,
    up_all,
    first_own,
    second_own,
    own_rows,
    give,
    got,
    pair,
    far_got,
    us,
    ur,
    ds,
    dr,
    ys,
    yr,
    row_local,
    ts,
    tr,
    token_local,
    load_sem,
    ss,
    sr,
):
    here = Place(size)
    length, width = lhs.shape
    lse_ref[...] = jnp.zeros_like(lse_ref)
    rows = length // 4
    units = gate_out.shape[1]
    chunk = units // 2
    heads = mixed_ref.shape[1] // HEAD_DIM
    kv_heads = heads // 2
    ff_part = units // size

    def sems(index):
        return tuple(kind.at[index] for kind in (us, ur, ds, dr, ys, yr, row_local))

    down_rows = pl.ds(pl.multiple_of(here.seq * ff_part, ff_part), ff_part)
    qkv = RowGather(here, qkv_own, qkv_full, sems(0))
    out = HeadGather(here, w_out, out_full, sems(1))
    first = RowGather(here, first_own, first_full, sems(2))
    second = RowGather(here, second_own, second_full, sems(3))
    down = RowGather(here, w_down.at[down_rows, :], down_full, sems(4))
    n1 = TokenGather(here, own_rows.at[0], n1_full, (ts.at[0], tr.at[0], token_local.at[0]))
    n2 = TokenGather(here, own_rows.at[1], n2_full, (ts.at[1], tr.at[1], token_local.at[1]))
    dy = TokenGather(here, dy_own, dy_full, (ts.at[2], tr.at[2], token_local.at[2]))

    loads = []
    at = 0
    for index, (weight, count) in enumerate(((w_query, heads), (w_key, kv_heads), (w_value, kv_heads))):
        count = count * HEAD_DIM
        source = weight.at[:, pl.ds(pl.multiple_of(here.seq * count, count), count)]
        loads.append(
            pltpu.make_async_copy(source, qkv_own.at[:, at : at + count], load_sem.at[index])
        )
        at += count
    loads.append(pltpu.make_async_copy(w_gate, gate_all, load_sem.at[3]))
    loads.append(pltpu.make_async_copy(w_up, up_all, load_sem.at[4]))
    for load in loads:
        load.start()
    here.greet()
    for load in loads[:3]:
        load.wait()
    qkv.send()
    out.send()

    def norm_rows(source, gain_ref, target):
        @pl.loop(0, rows // 32)
        def _(index):
            part = pl.ds(pl.multiple_of(index * 32, 32), 32)
            values = source[part, :].astype(F32)
            scales = lax.rsqrt(jnp.mean(values * values, axis=-1, keepdims=True) + EPSILON)
            target[part, :] = (values * scales * gain_ref[...]).astype(BF)

    norm_rows(hidden_ref, attn_gain_ref, own_rows.at[0])
    n1.send()
    for load in loads[3:]:
        load.wait()

    for seq in range(4):

        @pl.when(here.seq == seq)
        def _():
            @pl.loop(0, first_own.shape[0] // 16)
            def _(index):
                part = pl.ds(pl.multiple_of(index * 16, 16), 16)
                for target, begin in ((first_own, 0), (second_own, size // 2)):
                    for source, at in ((gate_all, 0), (up_all, chunk)):
                        pieces = [
                            source[part, (block * 4 + seq) * ff_part : (block * 4 + seq + 1) * ff_part]
                            for block in range(begin, begin + size // 2)
                        ]
                        target[part, at : at + chunk] = jnp.concatenate(pieces, axis=1)

    first.send()
    last = here.outer - 1
    for distance in range(last):
        qkv.step(distance)
    n1.forward()
    second.send()
    n1.arrive()
    load_lhs = pltpu.make_async_copy(n1_full, lhs, load_sem.at[0])
    load_lhs.start()
    dy.send()
    out.step()
    qkv.arrive()
    load_qkv = pltpu.make_async_copy(qkv_full, qkv_w, load_sem.at[1])
    load_qkv.start()
    load_lhs.wait()
    load_qkv.wait()

    def project(tile):
        weight = qkv_w[:, :, tile * 256 : tile * 256 + 256].reshape(width, 256)
        gain_ref = query_gain_ref if tile < heads // 2 else key_gain_ref

        @pl.loop(0, 4)
        def _(index):
            part = pl.ds(pl.multiple_of(index * rows, rows), rows)
            both = dot(lhs[part, :], weight)
            for side in range(2):
                head = tile * 2 + side
                proj = both[:, side * HEAD_DIM : (side + 1) * HEAD_DIM]
                if head >= heads + kv_heads:
                    heads_ref[head, part, :] = proj.astype(BF)
                    continue
                proj_ref[head, part, :] = proj
                scales = lax.rsqrt(jnp.mean(proj * proj, axis=-1, keepdims=True) + EPSILON)
                gained = proj * scales * gain_ref[...]
                turned = pltpu.roll(gained, HEAD_DIM // 2, 1)
                heads_ref[head, part, :] = (
                    gained * cos_ref[part, :] + turned * sin_ref[part, :]
                ).astype(BF)

    def attend(head):
        pair_head = head // 2
        for block in range(4):
            end = (block + 1) * rows
            part = pl.ds(block * rows, rows)
            scores = contract_cols(
                heads_ref[head, part, :], heads_ref[heads + pair_head, 0:end, :]
            ) * (HEAD_DIM ** (-0.5))
            row_place = lax.broadcasted_iota(jnp.int32, (rows, end), 0) + block * rows
            col_place = lax.broadcasted_iota(jnp.int32, (rows, end), 1)
            allowed = (seg_col_ref[part, :] == seg_row_ref[:, 0:end]) & (col_place <= row_place)
            scores = jnp.where(allowed, scores, NEGATIVE)
            highest = jnp.max(scores, axis=-1, keepdims=True)
            raised = jnp.exp(scores - highest)
            sums = jnp.sum(raised, axis=-1, keepdims=True)
            weights = (raised * (1.0 / sums)).astype(BF)
            mixed = dot(weights, heads_ref[heads + kv_heads + pair_head, 0:end, :])
            mixed_ref[part, head * HEAD_DIM : (head + 1) * HEAD_DIM] = mixed.astype(BF)
            lse_ref[part, head : head + 1] = highest + jnp.log(sums)

    for tile in range((heads + 2 * kv_heads) // 2):
        project(tile)
    pending = [(first, distance) for distance in range(last)]
    pending += [(second, distance) for distance in range(last)]
    pending += [(down, distance) for distance in range(last)]

    def pump(share):
        for _ in range(max(1, last * share // 3)):
            if pending:
                gather, distance = pending.pop(0)
                gather.step(distance)

    pump(1)
    attend(0)
    pump(1)
    down.send()
    attend(1)
    pump(1)
    attend(2)
    dy.forward()
    pump(1)
    attend(3)
    pump(1)

    out.arrive()
    load_out = pltpu.make_async_copy(out_full, out_w, load_sem.at[2])
    load_out.start()
    load_out.wait()

    def out_piece(seq, column):
        part = pl.ds(pl.multiple_of(seq * rows, rows), rows)
        weight = out_w[:, :, column]
        return dot(mixed_ref[part, :], weight.reshape(-1, weight.shape[-1]))

    middle_ref[...] = hidden_ref[...].astype(F32)
    scatter_sum(here, out_piece, middle_ref, give, got, pair, far_got, (ss, sr), width, 512)
    norm_rows(middle_ref, mlp_gain_ref, own_rows.at[1])
    n2.send()
    pump(1)
    n2.forward()
    pump(1)
    n2.arrive()
    load_lhs = pltpu.make_async_copy(n2_full, lhs, load_sem.at[3])
    load_lhs.start()
    first.arrive()
    load_lhs.wait()

    def feed(gather, part_index):
        tiles = chunk // 256
        block = gather.whole.shape[:-1] + (256,)

        def body(gate_w, up_w, gate_ref, up_ref, act_ref):
            gate_tile = gate_w[...].reshape(width, 256)
            up_tile = up_w[...].reshape(width, 256)

            @pl.loop(0, 4)
            def _(index):
                part = pl.ds(pl.multiple_of(index * rows, rows), rows)
                gate = dot(lhs[part, :], gate_tile)
                up = dot(lhs[part, :], up_tile)
                gate_ref[part, :] = gate
                up_ref[part, :] = up
                act_ref[part, :] = (gate * jax.nn.sigmoid(gate) * up).astype(BF)

        spot = pl.BlockSpec((length, 256), lambda t: (0, t + part_index * tiles))
        pltpu.emit_pipeline(
            body,
            grid=(tiles,),
            in_specs=[
                pl.BlockSpec(block, lambda t: (0, 0, t)),
                pl.BlockSpec(block, lambda t: (0, 0, t + tiles)),
            ],
            out_specs=[spot, spot, spot],
        )(gather.whole, gather.whole, gate_out, up_out, act_out)

    feed(first, 0)
    while pending:
        pump(1)
    second.arrive()
    feed(second, 1)
    dy.arrive()
    down.arrive()
    for gather in (qkv, out, first, second, down, n1, n2, dy):
        gather.finish()


def forward(hidden, upstream, weights, gains, tables, segment):
    size = lax.axis_size("shard")
    quarter, outer = size // 4, size // 2
    piece, width = hidden.shape
    length = piece * 4
    heads = Q_HEADS // 4
    kv_heads = KV_HEADS // 4
    w_query, _, _, w_out, w_gate, _, w_down = weights
    own = w_query.shape[0]
    qkv_width = (heads + 2 * kv_heads) * HEAD_DIM
    units = w_down.shape[0] // 4 * size

    def shape(*dims, kind=BF):
        return jax.ShapeDtypeStruct(dims, kind)

    results = [
        shape(size, own, qkv_width),
        shape(quarter, *w_out.shape),
        shape(size, own, units),
        shape(size, own, units),
        shape(size, w_down.shape[0] // 4, width),
        shape(length, width),
        shape(length, width),
        shape(length, width),
        shape(length, units, kind=F32),
        shape(length, units, kind=F32),
        shape(length, units),
        shape(heads + kv_heads, length, HEAD_DIM, kind=F32),
        shape(heads + 2 * kv_heads, length, HEAD_DIM),
        shape(length, heads * HEAD_DIM),
        shape(length, 128, kind=F32),
        shape(piece, width, kind=F32),
    ]
    dma = pltpu.SemaphoreType.DMA
    return pl.pallas_call(
        functools.partial(forward_kernel, size),
        out_shape=results,
        in_specs=[VMEM] + [ANY] * 8 + [VMEM] * 8,
        out_specs=[ANY] * 11 + [VMEM] * 5,
        scratch_shapes=[
            pltpu.VMEM((length, width), BF),
            pltpu.VMEM((size, own, qkv_width), BF),
            pltpu.VMEM((quarter,) + w_out.shape, BF),
            pltpu.VMEM((own, qkv_width), BF),
            pltpu.VMEM(w_gate.shape, BF),
            pltpu.VMEM(w_gate.shape, BF),
            pltpu.VMEM((own, units), BF),
            pltpu.VMEM((own, units), BF),
            pltpu.VMEM((2, piece, width), BF),
            pltpu.VMEM((2, piece, width), BF),
            pltpu.VMEM((2, piece, width), BF),
            pltpu.VMEM((piece, width), BF),
            pltpu.VMEM((piece, width), BF),
            dma((5, outer)),
            dma((5, outer)),
            dma((5, outer)),
            dma((5, outer)),
            dma((5, outer)),
            dma((5, outer)),
            dma((5,)),
            dma((3, 3)),
            dma((3, 3)),
            dma((3,)),
            dma((5,)),
            dma((3,)),
            dma((3,)),
        ],
        compiler_params=pltpu.CompilerParams(
            collective_id=0, has_side_effects=True, vmem_limit_bytes=VMEM_BYTES
        ),
        name="forward_gather",
    )(
        hidden,
        upstream,
        *weights,
        *gains,
        *tables,
        segment.reshape(length, 1),
        segment.reshape(1, length),
    )


def add_rows(target, sources, step=16):
    groups, rows, _ = target.shape

    @pl.loop(0, groups * (rows // step))
    def _(index):
        group = index // (rows // step)
        part = pl.ds(pl.multiple_of(lax.rem(index, rows // step) * step, step), step)
        total = sources[0][group, part, :].astype(F32)
        for source in sources[1:]:
            total = total + source[group, part, :].astype(F32)
        target[group, part, :] = total.astype(target.dtype)


class RowSum:
    def __init__(self, here, give, keep, near, rising, falling, stage, total, sems):
        self.here, self.give, self.keep = here, give, keep
        self.near, self.rising, self.falling = near, rising, falling
        self.stage, self.total = stage, total
        self.ys, self.yr, self.us, self.ur, self.ds, self.dr, self.load = sems
        self.last = here.outer - 1

    def across(self, place):
        return remote(
            self.give.at[place],
            self.near.at[place],
            self.ys.at[place],
            self.yr.at[place],
            self.here.twin,
        )

    def up(self, place):
        peer = self.here.outer_peer(self.here.place + 1)
        return remote(
            self.keep.at[place], self.rising.at[place], self.us.at[place], self.ur.at[place], peer
        )

    def down(self, place):
        peer = self.here.outer_peer(self.here.place - 1)
        return remote(
            self.keep.at[place], self.falling.at[place], self.ds.at[place], self.dr.at[place], peer
        )

    def arrived(self, slot, send, receive):
        remote(slot, slot, send, receive, self.here.twin).wait_recv()

    def compute(self, left, right, tiles, zones, ready=None):
        here = self.here
        own = self.give.shape[2]
        per = 128 // (2 * own)
        width = self.give.shape[3]
        step = 256
        for group in range(zones):
            spots = tiles(group)

            @pl.loop(0, width // step)
            def _(index):
                lane = pl.ds(pl.multiple_of(index * step, step), step)
                terms = dot(left(group), right[:, lane])
                for spot, (zone, seq_group) in enumerate(spots):
                    for sub in range(per):
                        at = spot * 128 + sub * 2 * own
                        even, odd = terms[at : at + own], terms[at + own : at + 2 * own]
                        place = zone * per + sub
                        mine = jnp.where(here.half == 0, even, odd).astype(BF)
                        theirs = jnp.where(here.half == 0, odd, even).astype(BF)
                        self.keep[place, seq_group, :, lane] = mine
                        self.give[place, seq_group, :, lane] = theirs

            for zone in sorted({zone for zone, _ in spots}):
                for sub in range(per):
                    self.across(zone * per + sub).start()

    def fold(self, distance):
        here = self.here
        above = here.place + distance
        below = here.place - distance

        def merge(place, line, receive, first):
            near = pltpu.make_async_copy(self.near.at[place], self.stage.at[0], self.load.at[0])
            self.arrived(self.near.at[place], self.ys.at[place], self.yr.at[place])
            near.start()

            @pl.when(first)
            def _():
                near.wait()
                add_rows(self.keep.at[place], [self.keep.at[place], self.stage.at[0]])

            @pl.when(jnp.logical_not(first))
            def _():
                self.arrived(line.at[place], self.us.at[0], receive.at[place])
                far = pltpu.make_async_copy(line.at[place], self.stage.at[1], self.load.at[1])
                far.start()
                near.wait()
                far.wait()
                add_rows(
                    self.keep.at[place], [self.keep.at[place], self.stage.at[0], self.stage.at[1]]
                )

        @pl.when(above <= self.last)
        def _():
            merge(above, self.rising, self.ur, here.place == 0)
            self.up(above).start()

        @pl.when(below >= 0)
        def _():
            merge(below, self.falling, self.dr, here.place == self.last)
            self.down(below).start()

    def finish(self):
        here = self.here
        place = here.place
        self.arrived(self.near.at[place], self.ys.at[place], self.yr.at[place])
        keep = self.keep.at[place]
        near = pltpu.make_async_copy(self.near.at[place], self.stage.at[0], self.load.at[0])
        low = pltpu.make_async_copy(self.rising.at[place], self.stage.at[1], self.load.at[1])
        high = pltpu.make_async_copy(self.falling.at[place], self.stage.at[1], self.load.at[1])
        near.start()

        @pl.when(place > 0)
        def _():
            self.arrived(self.rising.at[place], self.us.at[0], self.ur.at[place])
            low.start()
            low.wait()

        @pl.when(place == 0)
        def _():
            self.arrived(self.falling.at[place], self.ds.at[0], self.dr.at[place])
            high.start()
            high.wait()

        near.wait()

        @pl.when((place > 0) & (place < self.last))
        def _():
            add_rows(keep, [keep, self.stage.at[0], self.stage.at[1]])
            self.arrived(self.falling.at[place], self.ds.at[0], self.dr.at[place])
            high.start()
            high.wait()
            add_rows(self.total, [keep, self.stage.at[1]])

        @pl.when((place == 0) | (place == self.last))
        def _():
            add_rows(self.total, [keep, self.stage.at[0], self.stage.at[1]])

    def sent(self):
        for place in range(self.here.outer):
            self.across(place).wait_send()

    def settle(self):
        here = self.here
        for place in range(here.outer):

            @pl.when(place > here.place)
            def _():
                self.up(place).wait_send()

            @pl.when(place < here.place)
            def _():
                self.down(place).wait_send()


class RowSpread:
    def __init__(self, here, rows, whole, sems):
        self.here, self.rows, self.whole = here, rows, whole
        self.send_sems, self.recv_sems, self.local = sems

    def copy(self, amount):
        seq = lax.rem(self.here.seq + amount, 4)
        return remote(
            self.rows.at[seq],
            self.whole.at[self.here.seq],
            self.send_sems.at[amount - 1],
            self.recv_sems.at[amount - 1],
            {"seq": seq},
        )

    def keep(self):
        seq = self.here.seq
        return pltpu.make_async_copy(self.rows.at[seq], self.whole.at[seq], self.local)

    def send(self):
        for amount in (2, 3, 1):
            self.copy(amount).start()
        self.keep().start()

    def arrive(self):
        for amount in (1, 2, 3):
            self.copy(amount).wait_recv()
        self.keep().wait()

    def finish(self):
        for amount in (1, 2, 3):
            self.copy(amount).wait_send()


class TokenSum:
    def __init__(self, here, part, got, pair, far_got, base, sems):
        self.here, self.part, self.got, self.pair = here, part, got, pair
        self.far_got, self.base = far_got, base
        self.send_sems, self.recv_sems = sems
        self.rows = part.shape[0] // 4

    def piece(self, seq):
        return pl.ds(pl.multiple_of(seq * self.rows, self.rows), self.rows)

    def to_mate(self, index):
        here = self.here
        chip = here.chip if index else 1 - here.chip
        seq = chip * 2 + 1 - here.core
        return remote(
            self.part.at[self.piece(seq), :],
            self.got.at[index],
            self.send_sems.at[index],
            self.recv_sems.at[index],
            here.mate,
        )

    def to_far(self):
        return remote(
            self.pair, self.far_got, self.send_sems.at[2], self.recv_sems.at[2], self.here.far
        )

    def send(self):
        self.to_mate(0).start()
        self.to_mate(1).start()

    def loop(self, body):
        @pl.loop(0, self.rows // 32)
        def _(index):
            body(index * 32)

    def pass_on(self):
        self.to_mate(0).wait_recv()
        begin = self.here.far_seq * self.rows

        def body(at):
            part = pl.ds(pl.multiple_of(at, 32), 32)
            source = pl.ds(pl.multiple_of(begin + at, 32), 32)
            total = self.part[source, :].astype(F32) + self.got[0, part, :].astype(F32)
            self.pair[part, :] = total.astype(BF)

        self.loop(body)
        self.to_far().start()

    def add_near(self):
        self.to_mate(1).wait_recv()
        begin = self.here.seq * self.rows

        def body(at):
            part = pl.ds(pl.multiple_of(at, 32), 32)
            source = pl.ds(pl.multiple_of(begin + at, 32), 32)
            self.base[part, :] += self.part[source, :].astype(F32) + self.got[1, part, :].astype(F32)

        self.loop(body)
        self.to_mate(0).wait_send()
        self.to_mate(1).wait_send()

    def add_far(self):
        self.to_far().wait_recv()

        def body(at):
            part = pl.ds(pl.multiple_of(at, 32), 32)
            self.base[part, :] += self.far_got[part, :].astype(F32)

        self.loop(body)
        self.to_far().wait_send()


class GainSum:
    def __init__(self, here, parts, arrived, sems):
        self.here, self.parts, self.arrived = here, parts, arrived
        self.send_sems, self.recv_sems = sems
        self.peers = [here.mate, here.far, here.twin] + here.line_peers()

    def run(self):
        for index, peer in enumerate(self.peers):
            copy = remote(
                self.parts.at[index],
                self.arrived.at[index],
                self.send_sems.at[index],
                self.recv_sems.at[index],
                peer,
            )
            copy.start()
            copy.wait()
            self.parts[index + 1] = self.parts[index] + self.arrived[index]


def backward_kernel(
    size,
    n1_hbm,
    dy_hbm,
    n2_hbm,
    gate_hbm,
    up_hbm,
    act_hbm,
    proj_hbm,
    heads_ref,
    mixed_ref,
    lse_ref,
    middle_hbm,
    hidden_hbm,
    dy_own,
    qkv_full,
    out_full,
    first_full,
    second_full,
    down_full,
    attn_gain_ref,
    mlp_gain_ref,
    query_gain_ref,
    key_gain_ref,
    cos_ref,
    sin_ref,
    seg_col_ref,
    seg_row_ref,
    grad_in,
    gains_out,
    grad_out,
    hidden_out,
    down_rows,
    first_rows,
    second_rows,
    qkv_rows,
    pair_hbm,
    da_hbm,
    near_mlp,
    rising_mlp,
    falling_mlp,
    near_qkv,
    rising_qkv,
    falling_qkv,
    near_out,
    rising_out,
    falling_out,
    lhs,
    turned,
    first_r,
    second_r,
    give,
    keep,
    give_out,
    keep_out,
    stage,
    stage_out,
    total_out,
    dout_ref,
    da_own,
    got,
    far_got,
    pair,
    middle_grad,
    proj_buf,
    lse_t,
    dk_sum,
    dv_sum,
    gain_rows,
    gain_got,
    ys,
    yr,
    us,
    ur,
    ds,
    dr,
    fold_load,
    spread_s,
    spread_r,
    spread_l,
    sum_s,
    sum_r,
    ts,
    tr,
    token_local,
    gs,
    gr,
    load_sem,
):
    here = Place(size)
    length, width = lhs.shape
    rows = length // 4
    units = first_r.shape[1]
    chunk = units // 2
    ff_part = units // size
    heads = mixed_ref.shape[1] // HEAD_DIM
    kv_heads = heads // 2
    qkv_width = qkv_full.shape[2]
    last = here.outer - 1
    zones = width // 512
    scale = HEAD_DIM ** (-0.5)

    def load(source, target, index):
        copy = pltpu.make_async_copy(source, target, load_sem.at[index])
        copy.start()
        return copy

    def sems(index):
        return tuple(kind.at[index] for kind in (ys, yr, us, ur, ds, dr, fold_load))

    mlp = [
        RowSum(
            here,
            give.at[index % 2],
            keep.at[index],
            near_mlp.at[index],
            rising_mlp.at[index],
            falling_mlp.at[index],
            stage,
            keep.at[index, here.place],
            sems(index),
        )
        for index in range(3)
    ]
    down, first, second = mlp
    thin = slice(0, qkv_width)
    qkv = RowSum(
        here,
        give.at[1, :, :, :, thin],
        keep.at[0, :, :, :, thin],
        near_qkv,
        rising_qkv,
        falling_qkv,
        stage.at[:, :, :, thin],
        keep.at[0, here.place, :, :, thin],
        sems(3),
    )
    out = RowSum(
        here, give_out, keep_out, near_out, rising_out, falling_out, stage_out, total_out, sems(4)
    )

    def spread(index, job, whole):
        return RowSpread(
            here, job.total, whole, (spread_s.at[index], spread_r.at[index], spread_l.at[index])
        )

    spread_down = spread(0, down, down_rows)
    spread_first = spread(1, first, first_rows)
    spread_second = spread(2, second, second_rows)
    spread_qkv = spread(3, qkv, qkv_rows)

    def token_sum(index, base):
        return TokenSum(
            here, lhs, got, pair, far_got, base, (sum_s.at[index], sum_r.at[index])
        )

    sum_mlp = token_sum(0, middle_grad)
    sum_hidden = token_sum(1, grad_in)
    sum_attn = token_sum(2, grad_in)
    da = TokenGather(here, da_own, da_hbm, (ts, tr, token_local.at[0]))

    def model_tiles(group):
        return [(group, seq_group) for seq_group in range(4)]

    def model_left(group):
        return turned[group * 4 : group * 4 + 4].reshape(512, length)

    def turn_model():
        for seq_group in range(4):
            for zone in range(zones):
                at = (seq_group * zones + zone) * 128
                turned[zone * 4 + seq_group] = lhs[:, at : at + 128].T

    load_lhs = load(dy_hbm, lhs, 0)
    load_act = load(act_hbm, first_r, 1)
    load_middle = load(middle_hbm, grad_in, 2)
    load_dy = load(dy_own, da_own, 4)
    here.greet(wide=True)
    load_lhs.wait()
    turn_model()
    load_act.wait()
    down.compute(model_left, first_r, model_tiles, zones)

    wide = 384
    blocks = wide // ff_part

    def gate_body(weight, gate_tile, up_tile, gate_grad, up_grad):
        part = pl.ds(pl.multiple_of(pl.program_id(1) * rows, rows), rows)
        act_grad = contract_cols(lhs[part, :], weight[...].reshape(wide, width))
        gate = gate_tile[...]
        up = up_tile[...]
        sigmoid = jax.nn.sigmoid(gate)
        gate_grad[...] = (act_grad * up * sigmoid * (1.0 + gate * (1.0 - sigmoid))).astype(BF)
        up_grad[...] = (act_grad * (gate * sigmoid)).astype(BF)

    tiles = chunk // wide
    for index in range(2):

        def spot(base):
            return pl.BlockSpec((rows, wide), lambda t, r, base=base: (r, t + base))

        pltpu.emit_pipeline(
            gate_body,
            grid=(tiles, 4),
            in_specs=[
                pl.BlockSpec(
                    (blocks, ff_part, width), lambda t, r, index=index: (t + index * tiles, 0, 0)
                ),
                spot(index * tiles),
                spot(index * tiles),
            ],
            out_specs=[spot(0), spot(tiles)],
        )(down_full, gate_hbm, up_hbm, pair_hbm.at[index], pair_hbm.at[index])

    load_lhs = load(n2_hbm, lhs, 0)
    load_first = load(pair_hbm.at[0], first_r, 1)
    load_second = load(pair_hbm.at[1], second_r, 3)
    load_lhs.wait()
    turn_model()
    load_first.wait()
    first.compute(model_left, first_r, model_tiles, zones)
    load_second.wait()

    own = width // size
    slabs = 256 // own

    def dn2_body(first_w, second_w):
        lane = pl.ds(pl.multiple_of(pl.program_id(0) * 256, 256), 256)
        first_tile = first_w[...].reshape(256, units)
        second_tile = second_w[...].reshape(256, units)

        @pl.loop(0, 4)
        def _(index):
            part = pl.ds(pl.multiple_of(index * rows, rows), rows)
            total = contract_cols(first_r[part, :], first_tile)
            total = total + contract_cols(second_r[part, :], second_tile)
            lhs[part, lane] = total.astype(BF)

    slab = pl.BlockSpec((slabs, own, units), lambda t: (t, 0, 0))
    pltpu.emit_pipeline(dn2_body, grid=(width // 256,), in_specs=[slab, slab])(
        first_full, second_full
    )
    middle_grad[...] = jnp.zeros_like(middle_grad)
    load_act = load(act_hbm, first_r, 1)
    sum_mlp.send()
    sum_mlp.pass_on()
    sum_mlp.add_near()
    down.fold(last)
    sum_mlp.add_far()

    load_middle.wait()
    load_dy.wait()
    gain_rows[0] = jnp.zeros_like(gain_rows[0])
    narrow = 16

    @pl.loop(0, rows // narrow)
    def _(index):
        part = pl.ds(pl.multiple_of(index * narrow, narrow), narrow)
        values = grad_in[part, :]
        scales = lax.rsqrt(jnp.mean(values * values, axis=-1, keepdims=True) + EPSILON)
        normed = values * scales
        update = middle_grad[part, :]
        gain_rows[0, 1:2, :] += jnp.sum(update * normed, axis=0, keepdims=True)
        upper = update * mlp_gain_ref[...]
        inner = jnp.mean(upper * normed, axis=-1, keepdims=True)
        grad = da_own[part, :].astype(F32) + scales * (upper - normed * inner)
        middle_grad[part, :] = grad
        da_own[part, :] = grad.astype(BF)

    da.send()
    down.sent()
    second.compute(model_left, second_r, model_tiles, zones)

    def hidden_body(weight):
        lane = pl.ds(pl.multiple_of(pl.program_id(0) * 256, 256), 256)
        tile = weight[...].reshape(units, 256)

        @pl.loop(0, 4)
        def _(index):
            part = pl.ds(pl.multiple_of(index * rows, rows), rows)
            lhs[part, lane] = dot(first_r[part, :], tile).astype(BF)

    load_act.wait()
    pltpu.emit_pipeline(
        hidden_body,
        grid=(width // 256,),
        in_specs=[pl.BlockSpec((size, ff_part, 256), lambda t: (0, 0, t))],
    )(down_full)
    da.mate_arrived()
    sum_hidden.send()
    da.forward()
    sum_hidden.pass_on()
    sum_hidden.add_near()
    for distance in range(last - 1, 0, -1):
        down.fold(distance)
    da.rest_arrived()
    da.finish()
    load_lhs = load(da_hbm, lhs, 0)
    load_own = load(hidden_hbm, da_own, 2)
    load_lhs.wait()

    def dout_body(weight):
        lane = pl.ds(pl.multiple_of(pl.program_id(0) * 256, 256), 256)
        tile = weight[...].reshape(256, width)

        @pl.loop(0, 4)
        def _(index):
            part = pl.ds(pl.multiple_of(index * rows, rows), rows)
            dout_ref[part, lane] = contract_cols(lhs[part, :], tile).astype(BF)

    out_blocks, out_rows = out_full.shape[:2]
    pltpu.emit_pipeline(
        dout_body,
        grid=(out_blocks * out_rows // 256,),
        in_specs=[pl.BlockSpec((256 // out_rows, out_rows, width), lambda t: (t, 0, 0))],
    )(out_full)

    for head in range(heads):
        turned[head] = mixed_ref[:, head * HEAD_DIM : (head + 1) * HEAD_DIM].T
    out.compute(
        lambda group: turned[0:heads].reshape(heads * HEAD_DIM, length),
        lhs,
        lambda group: [(zone, 0) for zone in range(heads)],
        1,
    )
    load_lhs = load(n1_hbm, lhs, 0)
    down.finish()
    sum_hidden.add_far()

    @pl.loop(0, rows // 32)
    def _(index):
        part = pl.ds(pl.multiple_of(index * 32, 32), 32)
        pair[part, :] = grad_in[part, :].astype(BF)

    store_hidden = load(pair, hidden_out, 1)
    spread_down.send()

    lse_t[...] = lse_ref[...].T[0:8]
    pending = [(first, distance) for distance in range(last, 0, -1)]

    def pump():
        for _ in range(max(1, last // 3)):
            if pending:
                job, distance = pending.pop(0)
                job.fold(distance)

    def through_norm(grad, head, part, gain_ref, gain_row):
        proj = proj_buf[lax.rem(head, 2), part, :]
        scales = lax.rsqrt(jnp.mean(proj * proj, axis=-1, keepdims=True) + EPSILON)
        normed = proj * scales
        grad = grad.astype(F32)
        upper = grad * cos_ref[part, :] - pltpu.roll(grad, HEAD_DIM // 2, 1) * sin_ref[part, :]
        gain_rows[0, 2:3, gain_row * HEAD_DIM : (gain_row + 1) * HEAD_DIM] += jnp.sum(
            upper * normed, axis=0, keepdims=True
        )
        upper = upper * gain_ref[...]
        inner = jnp.mean(upper * normed, axis=-1, keepdims=True)
        result = (scales * (upper - normed * inner)).astype(BF)
        first_r[part, head * HEAD_DIM : (head + 1) * HEAD_DIM] = result

    for head in range(heads):
        pair_head = head // 2
        load_proj = load(proj_hbm.at[head], proj_buf.at[head % 2], 4)
        if head % 2 == 0:
            dk_sum[...] = jnp.zeros_like(dk_sum)
            dv_sum[...] = jnp.zeros_like(dv_sum)
        load_proj.wait()
        for block in range(4):
            end = (block + 1) * rows
            part = pl.ds(block * rows, rows)
            queries = heads_ref[head, part, :]
            keys = heads_ref[heads + pair_head, 0:end, :]
            values = heads_ref[heads + kv_heads + pair_head, 0:end, :]
            out_grad = dout_ref[part, head * HEAD_DIM : (head + 1) * HEAD_DIM]
            scores = contract_cols(keys, queries) * scale
            key_place = lax.broadcasted_iota(jnp.int32, (end, rows), 0)
            query_place = lax.broadcasted_iota(jnp.int32, (end, rows), 1) + block * rows
            allowed = (seg_col_ref[0:end, :] == seg_row_ref[:, part]) & (key_place <= query_place)
            weights = jnp.exp(
                jnp.where(allowed, scores, NEGATIVE) - lse_t[head : head + 1, part]
            )
            weight_grad = contract_cols(values, out_grad)
            inner = jnp.sum(weights * weight_grad, axis=0, keepdims=True)
            score_grad = (weights * (weight_grad - inner)).astype(BF)
            dk_sum[0:end, :] += dot(score_grad, queries) * scale
            dv_sum[0:end, :] += dot(weights.astype(BF), out_grad)
            query_grad = (contract_rows(score_grad, keys) * scale).astype(BF)
            through_norm(query_grad, head, part, query_gain_ref, 0)
        if head % 2:
            key = heads + pair_head
            value_at = (heads + kv_heads + pair_head) * HEAD_DIM
            load(proj_hbm.at[key], proj_buf.at[key % 2], 4).wait()

            @pl.loop(0, 4)
            def _(index):
                part = pl.ds(pl.multiple_of(index * rows, rows), rows)
                through_norm(dk_sum[part, :].astype(BF), key, part, key_gain_ref, 1)
                first_r[part, value_at : value_at + HEAD_DIM] = dv_sum[part, :].astype(BF)

        pump()

    load_lhs.wait()
    turn_model()
    down.settle()
    spread_down.finish()
    spread_down.arrive()
    first.sent()
    store_hidden.wait()
    proj_grads = first_r.at[:, 0:qkv_width]
    qkv.compute(model_left, proj_grads, model_tiles, zones)

    def dn1_body(weight):
        lane = pl.ds(pl.multiple_of(pl.program_id(0) * 256, 256), 256)
        tile = weight[...].reshape(256, qkv_width)

        @pl.loop(0, 4)
        def _(index):
            part = pl.ds(pl.multiple_of(index * rows, rows), rows)
            lhs[part, lane] = contract_cols(proj_grads[part, :], tile).astype(BF)

    pltpu.emit_pipeline(
        dn1_body,
        grid=(width // 256,),
        in_specs=[pl.BlockSpec((slabs, own, qkv_width), lambda t: (t, 0, 0))],
    )(qkv_full)
    grad_in[...] = jnp.zeros_like(grad_in)
    sum_attn.send()
    while pending:
        pump()
    sum_attn.pass_on()
    sum_attn.add_near()
    first.finish()
    spread_first.send()
    sum_attn.add_far()
    load_own.wait()

    @pl.loop(0, rows // narrow)
    def _(index):
        part = pl.ds(pl.multiple_of(index * narrow, narrow), narrow)
        values = da_own[part, :].astype(F32)
        scales = lax.rsqrt(jnp.mean(values * values, axis=-1, keepdims=True) + EPSILON)
        normed = values * scales
        update = grad_in[part, :]
        gain_rows[0, 0:1, :] += jnp.sum(update * normed, axis=0, keepdims=True)
        upper = update * attn_gain_ref[...]
        inner = jnp.mean(upper * normed, axis=-1, keepdims=True)
        grad_in[part, :] = middle_grad[part, :] + scales * (upper - normed * inner)

    for distance in range(last, 0, -1):
        second.fold(distance)
    GainSum(here, gain_rows, gain_got, (gs, gr)).run()
    gains_out[...] = gain_rows[gain_rows.shape[0] - 1]
    for distance in range(last, 0, -1):
        out.fold(distance)
    second.finish()
    spread_second.send()
    for distance in range(last, 0, -1):
        qkv.fold(distance)
    out.finish()
    grad_out[...] = total_out[0]
    qkv.finish()
    spread_qkv.send()
    for job in (spread_first, spread_second, spread_qkv):
        job.arrive()
        job.finish()
    for job in (second, out, qkv):
        job.sent()
    for job in (first, second, out, qkv):
        job.settle()


def backward(saved, weights, own, gains, tables, segment):
    size = lax.axis_size("shard")
    outer = size // 2
    (n1, dy, n2, gate, up, act, proj, heads_all, mixed, lse, middle) = saved
    length, width = n1.shape
    piece = length // 4
    units = act.shape[1]
    qkv_width = weights[0].shape[2]
    rows = width // (4 * size)
    q_width = mixed.shape[1]

    def shape(*dims, kind=BF):
        return jax.ShapeDtypeStruct(dims, kind)

    results = [
        shape(piece, width, kind=F32),
        shape(8, width, kind=F32),
        shape(rows, width, kind=F32),
        shape(piece, width),
        shape(4, rows, units),
        shape(4, rows, units),
        shape(4, rows, units),
        shape(4, rows, qkv_width),
        shape(2, length, units),
        shape(length, width),
    ]
    results += [shape(3, outer, 4, rows, units)] * 3
    results += [shape(outer, 4, rows, qkv_width)] * 3
    results += [shape(outer, 1, rows, width)] * 3
    dma = pltpu.SemaphoreType.DMA
    hops = 3 + outer.bit_length() - 1
    vmem = pltpu.VMEM
    return pl.pallas_call(
        functools.partial(backward_kernel, size),
        out_shape=results,
        in_specs=[ANY] * 7 + [VMEM] * 3 + [ANY] * 8 + [VMEM] * 8,
        out_specs=[VMEM] * 3 + [ANY] * (len(results) - 3),
        scratch_shapes=[
            vmem((length, width), BF),
            vmem((width // 128, 128, length), BF),
            vmem((length, units), BF),
            vmem((length, units), BF),
            vmem((2, outer, 4, rows, units), BF),
            vmem((3, outer, 4, rows, units), BF),
            vmem((outer, 1, rows, width), BF),
            vmem((outer, 1, rows, width), BF),
            vmem((2, 4, rows, units), BF),
            vmem((2, 1, rows, width), BF),
            vmem((1, rows, width), F32),
            vmem((length, q_width), BF),
            vmem((piece, width), BF),
            vmem((2, piece, width), BF),
            vmem((piece, width), BF),
            vmem((piece, width), BF),
            vmem((piece, width), F32),
            vmem((2, length, HEAD_DIM), F32),
            vmem((8, length), F32),
            vmem((length, HEAD_DIM), F32),
            vmem((length, HEAD_DIM), F32),
            vmem((hops + 1, 8, width), F32),
            vmem((hops, 8, width), F32),
            dma((5, outer)),
            dma((5, outer)),
            dma((5, outer)),
            dma((5, outer)),
            dma((5, outer)),
            dma((5, outer)),
            dma((5, 3)),
            dma((4, 3)),
            dma((4, 3)),
            dma((4,)),
            dma((3, 3)),
            dma((3, 3)),
            dma((3,)),
            dma((3,)),
            dma((1,)),
            dma((hops,)),
            dma((hops,)),
            dma((5,)),
        ],
        compiler_params=pltpu.CompilerParams(
            collective_id=1, has_side_effects=True, vmem_limit_bytes=VMEM_BYTES
        ),
        name="backward_sums",
    )(
        n1,
        dy,
        n2,
        gate,
        up,
        act,
        proj,
        heads_all,
        mixed,
        lse,
        middle,
        *own,
        *weights,
        *gains,
        *tables,
        segment.reshape(length, 1),
        segment.reshape(1, length),
    )


def local(
    hidden_in,
    segment_ids,
    norm_attn_gain,
    w_query,
    w_key,
    w_value,
    query_gain,
    key_gain,
    w_out,
    norm_mlp_gain,
    w_gate,
    w_up,
    w_down,
    out_cotangent,
):
    size = lax.axis_size("shard")
    length = hidden_in.shape[1] * 4
    q_part = Q_HEADS // 4 * HEAD_DIM
    kv_part = KV_HEADS // 4 * HEAD_DIM
    ff_part = w_down.shape[0] // 4
    units = size * ff_part
    chunk = units // 2
    segment = segment_ids[0]
    places = jnp.arange(length, dtype=jnp.int32)
    starts = jnp.sum((segment[None, :] < segment[:, None]).astype(jnp.int32), axis=1)
    cosine, sine = rotary_tables(places - starts)
    signs = jnp.where(jnp.arange(HEAD_DIM) < HEAD_DIM // 2, -1.0, 1.0).astype(F32)
    tables = (cosine, sine * signs)
    gains = (norm_attn_gain[None], norm_mlp_gain[None], query_gain[None], key_gain[None])
    results = forward(
        hidden_in[0],
        out_cotangent[0],
        (w_query, w_key, w_value, w_out, w_gate, w_up, w_down),
        gains,
        tables,
        segment,
    )
    grad_in, gain_totals, grad_out, hidden_out, down_rows, first_rows, second_rows, qkv_rows = (
        backward(
            results[5:],
            results[:5],
            (hidden_in[0], out_cotangent[0]),
            gains,
            tables,
            segment,
        )[:8]
    )

    def units_back(blocks):
        rows = blocks[0].shape[1]
        count = blocks[0].shape[2] // ff_part
        blocks = [
            block.reshape(4, rows, count, ff_part).transpose(1, 2, 0, 3) for block in blocks
        ]
        return jnp.concatenate(blocks, axis=1).reshape(rows, 4 * units).astype(F32)

    def side_by_side(blocks):
        return blocks.transpose(1, 0, 2).reshape(blocks.shape[1], 4 * blocks.shape[2]).astype(F32)

    return (
        hidden_out[None],
        grad_in[None],
        gain_totals[0],
        side_by_side(qkv_rows[:, :, :q_part]),
        side_by_side(qkv_rows[:, :, q_part : q_part + kv_part]),
        side_by_side(qkv_rows[:, :, q_part + kv_part :]),
        gain_totals[2, :HEAD_DIM],
        gain_totals[2, HEAD_DIM : 2 * HEAD_DIM],
        grad_out,
        gain_totals[1],
        units_back([pair[:, :, :chunk] for pair in (first_rows, second_rows)]),
        units_back([pair[:, :, chunk:] for pair in (first_rows, second_rows)]),
        units_back([down_rows]).T,
    )


def solution(mesh):
    return jax.shard_map(
        local,
        mesh=mesh,
        in_specs=(
            P("shard", "seq", None),
            P("shard", None),
            P(),
            P("shard", None),
            P("shard", None),
            P("shard", None),
            P(),
            P(),
            P("shard", None),
            P(),
            P("shard", None),
            P("shard", None),
            P("shard", None),
            P("shard", "seq", None),
        ),
        out_specs=(
            P("shard", "seq", None),
            P("shard", "seq", None),
            P(),
            P(("seq", "shard"), None),
            P(("seq", "shard"), None),
            P(("seq", "shard"), None),
            P(),
            P(),
            P(("seq", "shard"), None),
            P(),
            P(("seq", "shard"), None),
            P(("seq", "shard"), None),
            P(None, ("seq", "shard")),
        ),
        check_vma=False,
    )
```

```python
import functools

import jax
import jax.numpy as jnp
from jax import lax
from jax.experimental import pallas as pl
from jax.experimental.pallas import tpu as pltpu
from jax.sharding import PartitionSpec as P

Q_HEADS = 16
KV_HEADS = 8
HEAD_DIM = 128
EPSILON = 1e-06
ROPE_BASE = 1000000.0
NEGATIVE = -1e30
BF = jnp.bfloat16
F32 = jnp.float32
MESH = pl.DeviceIdType.MESH
ANY = pl.BlockSpec(memory_space=pl.ANY)
VMEM = pl.BlockSpec(memory_space=pltpu.VMEM)
VMEM_BYTES = 62 * 1024 * 1024


def rotary_tables(positions):
    inverse = ROPE_BASE ** (-(jnp.arange(HEAD_DIM // 2, dtype=F32) * 2.0) / HEAD_DIM)
    angles = positions.astype(F32)[:, None] * inverse[None, :]
    angles = jnp.concatenate([angles, angles], axis=-1)
    return (jnp.cos(angles), jnp.sin(angles))


def dot(left, right):
    return jnp.dot(left, right, preferred_element_type=F32)


def contract_rows(left, right):
    return lax.dot_general(left, right, (((0,), (0,)), ((), ())), preferred_element_type=F32)


def contract_cols(left, right):
    return lax.dot_general(left, right, (((1,), (1,)), ((), ())), preferred_element_type=F32)


class Place:
    def __init__(self, size):
        self.size = size
        self.outer = size // 2
        self.quarter = size // 4
        self.seq = lax.axis_index("seq")
        self.shard = lax.axis_index("shard")
        self.chip = self.seq // 2
        self.core = lax.rem(self.seq, 2)
        self.place = self.shard // 2
        self.half = lax.rem(self.shard, 2)
        self.far_seq = lax.rem(self.seq + 2, 4)
        self.mate_seq = self.chip * 2 + 1 - self.core
        self.far = {"seq": self.far_seq}
        self.mate = {"seq": self.mate_seq}
        self.twin_shard = self.place * 2 + 1 - self.half
        self.twin = {"shard": self.twin_shard}

    def outer_peer(self, place):
        return {"shard": place * 2 + self.half}

    def line_peers(self):
        peers = []
        step = 1
        while step < self.outer:
            sign = 1 - 2 * lax.rem(self.place // step, 2)
            peers.append(self.outer_peer(self.place + sign * step))
            step *= 2
        return peers

    def greet(self, wide=False):
        barrier = pltpu.get_barrier_semaphore()
        last = self.outer - 1

        def signal(peer):
            pl.semaphore_signal(barrier, inc=1, device_id=peer, device_id_type=MESH)

        peers = [self.far, self.mate, self.twin]
        if wide:
            peers += [{"seq": 3 - self.seq}] + self.line_peers()[1:]
        for peer in peers:
            signal(peer)

        @pl.when(self.place < last)
        def _():
            signal(self.outer_peer(self.place + 1))

        @pl.when(self.place > 0)
        def _():
            signal(self.outer_peer(self.place - 1))

        inner = ((self.place > 0) & (self.place < last)).astype(jnp.int32)
        pl.semaphore_wait(barrier, len(peers) + 1 + inner)


def remote(source, target, send, receive, peer):
    return pltpu.make_async_remote_copy(
        src_ref=source,
        dst_ref=target,
        send_sem=send,
        recv_sem=receive,
        device_id=peer,
        device_id_type=MESH,
    )


class RowGather:
    def __init__(self, here, own, whole, sems, spot=lambda shard: shard):
        self.here, self.own, self.whole, self.spot = here, own, whole, spot
        self.us, self.ur, self.ds, self.dr, self.ys, self.yr, self.local = sems
        self.last = here.outer - 1

    def slot(self, place):
        return self.whole.at[self.spot(place * 2 + self.here.half)]

    def keep(self):
        return pltpu.make_async_copy(self.own, self.slot(self.here.place), self.local)

    def up(self, distance):
        here = self.here
        slot = self.slot(here.place - distance)
        source = slot if distance else self.own
        peer = here.outer_peer(here.place + 1)
        return remote(source, slot, self.us.at[distance], self.ur.at[distance], peer)

    def down(self, distance):
        here = self.here
        slot = self.slot(here.place + distance)
        source = slot if distance else self.own
        peer = here.outer_peer(here.place - 1)
        return remote(source, slot, self.ds.at[distance], self.dr.at[distance], peer)

    def across(self, place, own=False):
        slot = self.slot(place)
        source = self.own if own else slot
        return remote(source, slot, self.ys.at[place], self.yr.at[place], self.here.twin)

    def send(self):
        here = self.here

        @pl.when(here.place < self.last)
        def _():
            self.up(0).start()

        @pl.when(here.place > 0)
        def _():
            self.down(0).start()

        self.across(here.place, own=True).start()
        self.keep().start()

    def step(self, distance):
        here = self.here
        below = here.place - 1 - distance
        above = here.place + 1 + distance

        @pl.when(below >= 0)
        def _():
            slot = self.slot(below)
            remote(
                slot, slot, self.us.at[0], self.ur.at[distance], self.here.twin
            ).wait_recv()

            @pl.when(here.place < self.last)
            def _():
                self.up(distance + 1).start()

            self.across(below).start()

        @pl.when(above <= self.last)
        def _():
            slot = self.slot(above)
            remote(
                slot, slot, self.ds.at[0], self.dr.at[distance], self.here.twin
            ).wait_recv()

            @pl.when(here.place > 0)
            def _():
                self.down(distance + 1).start()

            self.across(above).start()

    def arrive(self):
        self.keep().wait()
        for place in range(self.here.outer):
            slot = self.whole.at[self.spot(place * 2 + 1 - self.here.half)]
            remote(
                slot, slot, self.ys.at[place], self.yr.at[place], self.here.twin
            ).wait_recv()

    def finish(self):
        here = self.here
        for distance in range(self.last):

            @pl.when((here.place - distance >= 0) & (here.place < self.last))
            def _():
                self.up(distance).wait_send()

            @pl.when((here.place + distance <= self.last) & (here.place > 0))
            def _():
                self.down(distance).wait_send()

        for place in range(here.outer):
            self.across(place).wait_send()


class HeadGather:
    def __init__(self, here, own, whole, sems):
        self.here, self.own, self.whole = here, own, whole
        self.us, self.zr, self.ds, _, self.ys, self.yr, self.local = sems
        self.last = here.outer - 1
        self.count = here.quarter // 2
        self.first = here.seq * self.count
        self.mine = here.place - self.first
        self.inside = (self.mine >= 0) & (self.mine < self.count)

    def slot(self, index):
        return self.whole.at[index * 2 + self.here.half]

    def keep(self):
        return pltpu.make_async_copy(self.own, self.slot(self.mine), self.local)

    def up(self, index, own=False):
        slot = self.slot(index)
        peer = self.here.outer_peer(self.here.place + 1)
        return remote(self.own if own else slot, slot, self.us.at[index], self.zr.at[index], peer)

    def down(self, index, own=False):
        slot = self.slot(index)
        peer = self.here.outer_peer(self.here.place - 1)
        return remote(self.own if own else slot, slot, self.ds.at[index], self.zr.at[index], peer)

    def across(self, index):
        slot = self.slot(index)
        return remote(slot, slot, self.ys.at[index], self.yr.at[index], self.here.twin)

    def send(self):
        @pl.when(self.inside)
        def _():
            self.keep().start()

            @pl.when(self.here.place < self.last)
            def _():
                self.up(self.mine, own=True).start()

            @pl.when(self.here.place > 0)
            def _():
                self.down(self.mine, own=True).start()

    def step(self):
        here = self.here

        @pl.when(self.inside)
        def _():
            self.keep().wait()

        for index in range(self.count):
            slot = self.slot(index)
            arrival = remote(slot, slot, self.us.at[0], self.zr.at[index], here.twin)

            @pl.when(self.mine > index)
            def _():
                arrival.wait_recv()

                @pl.when(here.place < self.last)
                def _():
                    self.up(index).start()

            @pl.when(self.mine < index)
            def _():
                arrival.wait_recv()

                @pl.when(here.place > 0)
                def _():
                    self.down(index).start()

            self.across(index).start()

    def arrive(self):
        for index in range(self.count):
            slot = self.whole.at[index * 2 + 1 - self.here.half]
            remote(
                slot, slot, self.ys.at[index], self.yr.at[index], self.here.twin
            ).wait_recv()

    def finish(self):
        here = self.here
        for index in range(self.count):

            @pl.when((self.mine >= index) & (here.place < self.last))
            def _():
                self.up(index).wait_send()

            @pl.when((self.mine <= index) & (here.place > 0))
            def _():
                self.down(index).wait_send()

            self.across(index).wait_send()


class TokenGather:
    def __init__(self, here, own, whole, sems):
        self.here, self.own, self.whole = here, own, whole
        self.send_sems, self.recv_sems, self.local = sems
        self.rows = whole.shape[0] // 4

    def slot(self, seq):
        return self.whole.at[pl.ds(pl.multiple_of(seq * self.rows, self.rows), self.rows), :]

    def keep(self):
        return pltpu.make_async_copy(self.own, self.slot(self.here.seq), self.local)

    def copy(self, index):
        here = self.here
        slot = self.slot(here.far_seq if index == 2 else here.seq)
        return remote(
            slot if index == 2 else self.own,
            slot,
            self.send_sems.at[index],
            self.recv_sems.at[index],
            here.far if index == 0 else here.mate,
        )

    def send(self):
        self.copy(0).start()
        self.copy(1).start()
        self.keep().start()

    def forward(self):
        self.copy(0).wait_recv()
        self.copy(2).start()

    def mate_arrived(self):
        self.copy(1).wait_recv()

    def rest_arrived(self):
        self.copy(2).wait_recv()
        self.keep().wait()

    def arrive(self):
        self.mate_arrived()
        self.rest_arrived()

    def finish(self):
        for index in range(3):
            self.copy(index).wait_send()


def scatter_sum(here, piece, base, give, got, pair, far_got, sems, width, step):
    send_sems, recv_sems = sems
    other = 1 - here.chip
    to_mate = [
        remote(
            give.at[chip], got.at[chip], send_sems.at[index], recv_sems.at[index], here.mate
        )
        for index, chip in enumerate((other, here.chip))
    ]
    to_far = remote(pair, far_got, send_sems.at[2], recv_sems.at[2], here.far)

    def columns(body):
        @pl.loop(0, width // step)
        def _(index):
            body(pl.ds(pl.multiple_of(index * step, step), step))

    for index, chip in enumerate((other, here.chip)):
        seq = chip * 2 + 1 - here.core

        def fill(column, chip=chip, seq=seq):
            give[chip, :, column] = piece(seq, column).astype(BF)

        columns(fill)
        to_mate[index].start()

    to_mate[0].wait_recv()

    def fill_pair(column):
        term = piece(here.far_seq, column) + got[other, :, column].astype(F32)
        pair[:, column] = term.astype(BF)

    columns(fill_pair)
    to_far.start()
    to_mate[1].wait_recv()

    def fill_base(column):
        base[:, column] += piece(here.seq, column) + got[here.chip, :, column].astype(F32)

    columns(fill_base)
    to_far.wait_recv()

    def fill_far(column):
        base[:, column] += far_got[:, column].astype(F32)

    columns(fill_far)
    for copy in (*to_mate, to_far):
        copy.wait_send()


def forward_kernel(
    size,
    hidden_ref,
    dy_own,
    w_query,
    w_key,
    w_value,
    w_out,
    w_gate,
    w_up,
    w_down,
    attn_gain_ref,
    mlp_gain_ref,
    query_gain_ref,
    key_gain_ref,
    cos_ref,
    sin_ref,
    seg_col_ref,
    seg_row_ref,
    qkv_full,
    out_full,
    first_full,
    second_full,
    down_full,
    n1_full,
    dy_full,
    n2_full,
    n1_turned,
    dy_turned,
    n2_turned,
    act_out,
    pair_out,
    proj_ref,
    heads_ref,
    mixed_ref,
    lse_ref,
    middle_ref,
    lhs,
    dy_all,
    turned,
    qkv_w,
    out_w,
    qkv_own,
    gate_all,
    up_all,
    first_own,
    second_own,
    own_rows,
    give,
    got,
    pair,
    far_got,
    us,
    ur,
    ds,
    dr,
    ys,
    yr,
    row_local,
    ts,
    tr,
    token_local,
    load_sem,
    ss,
    sr,
):
    here = Place(size)
    length, width = lhs.shape
    lse_ref[...] = jnp.zeros_like(lse_ref)
    rows = length // 4
    units = act_out.shape[1]
    chunk = units // 2
    tail = 256
    heads = mixed_ref.shape[1] // HEAD_DIM
    kv_heads = heads // 2
    ff_part = units // size

    def sems(index):
        return tuple(kind.at[index] for kind in (us, ur, ds, dr, ys, yr, row_local))

    down_rows = pl.ds(pl.multiple_of(here.seq * ff_part, ff_part), ff_part)
    qkv = RowGather(here, qkv_own, qkv_full, sems(0))
    out = HeadGather(here, w_out, out_full, sems(1))
    down = RowGather(
        here,
        w_down.at[down_rows, :],
        down_full,
        sems(2),
        lambda shard: pl.ds(pl.multiple_of(shard * ff_part, ff_part), ff_part),
    )
    first = RowGather(here, first_own, first_full, sems(3))
    cut = 2 * (chunk - tail)
    second = RowGather(here, second_own.at[:, 0:cut], second_full.at[:, :, 0:cut], sems(4))
    third = RowGather(
        here, second_own.at[:, cut : 2 * chunk], second_full.at[:, :, cut : 2 * chunk], sems(5)
    )
    n1 = TokenGather(here, own_rows.at[0], n1_full, (ts.at[0], tr.at[0], token_local.at[0]))
    n2 = TokenGather(here, own_rows.at[1], n2_full, (ts.at[1], tr.at[1], token_local.at[1]))
    dy = TokenGather(here, dy_own, dy_full, (ts.at[2], tr.at[2], token_local.at[2]))

    loads = []
    at = 0
    for index, (weight, count) in enumerate(((w_query, heads), (w_key, kv_heads), (w_value, kv_heads))):
        count = count * HEAD_DIM
        source = weight.at[:, pl.ds(pl.multiple_of(here.seq * count, count), count)]
        loads.append(
            pltpu.make_async_copy(source, qkv_own.at[:, at : at + count], load_sem.at[index])
        )
        at += count
    loads.append(pltpu.make_async_copy(w_gate, gate_all, load_sem.at[3]))
    loads.append(pltpu.make_async_copy(w_up, up_all, load_sem.at[4]))
    for load in loads:
        load.start()
    here.greet()
    for load in loads[:3]:
        load.wait()
    qkv.send()
    out.send()

    def norm_rows(source, gain_ref, target):
        @pl.loop(0, rows // 32)
        def _(index):
            part = pl.ds(pl.multiple_of(index * 32, 32), 32)
            values = source[part, :].astype(F32)
            scales = lax.rsqrt(jnp.mean(values * values, axis=-1, keepdims=True) + EPSILON)
            target[part, :] = (values * scales * gain_ref[...]).astype(BF)

    norm_rows(hidden_ref, attn_gain_ref, own_rows.at[0])
    n1.send()
    down.send()
    for load in loads[3:]:
        load.wait()

    for seq in range(4):

        @pl.when(here.seq == seq)
        def _():
            @pl.loop(0, first_own.shape[0] // 16)
            def _(index):
                part = pl.ds(pl.multiple_of(index * 16, 16), 16)

                def gathered(source, begin):
                    pieces = [
                        source[part, (block * 4 + seq) * ff_part : (block * 4 + seq + 1) * ff_part]
                        for block in range(begin, begin + size // 2)
                    ]
                    return jnp.concatenate(pieces, axis=1)

                first_own[part, 0:chunk] = gathered(gate_all, 0)
                first_own[part, chunk : 2 * chunk] = gathered(up_all, 0)
                gate = gathered(gate_all, size // 2)
                up = gathered(up_all, size // 2)
                most = chunk - tail
                second_own[part, 0:most] = gate[:, 0:most]
                second_own[part, most : 2 * most] = up[:, 0:most]
                second_own[part, 2 * most : 2 * most + tail] = gate[:, most:]
                second_own[part, 2 * most + tail : 2 * chunk] = up[:, most:]

    last = here.outer - 1
    for distance in range(last):
        qkv.step(distance)
    n1.forward()
    first.send()
    n1.arrive()
    load_lhs = pltpu.make_async_copy(n1_full, lhs, load_sem.at[0])
    load_lhs.start()
    dy.send()
    out.step()
    qkv.arrive()
    load_qkv = pltpu.make_async_copy(qkv_full, qkv_w, load_sem.at[1])
    load_qkv.start()
    load_lhs.wait()
    load_qkv.wait()

    def project(tile):
        weight = qkv_w[:, :, tile * 256 : tile * 256 + 256].reshape(width, 256)
        gain_ref = query_gain_ref if tile < heads // 2 else key_gain_ref

        @pl.loop(0, 4)
        def _(index):
            part = pl.ds(pl.multiple_of(index * rows, rows), rows)
            both = dot(lhs[part, :], weight)
            for side in range(2):
                head = tile * 2 + side
                proj = both[:, side * HEAD_DIM : (side + 1) * HEAD_DIM]
                if head >= heads + kv_heads:
                    heads_ref[head, part, :] = proj.astype(BF)
                    continue
                proj_ref[head, part, :] = proj
                scales = lax.rsqrt(jnp.mean(proj * proj, axis=-1, keepdims=True) + EPSILON)
                gained = proj * scales * gain_ref[...]
                turned = pltpu.roll(gained, HEAD_DIM // 2, 1)
                heads_ref[head, part, :] = (
                    gained * cos_ref[part, :] + turned * sin_ref[part, :]
                ).astype(BF)

    def attend(head):
        pair_head = head // 2
        for block in range(4):
            end = (block + 1) * rows
            part = pl.ds(block * rows, rows)
            scores = contract_cols(
                heads_ref[head, part, :], heads_ref[heads + pair_head, 0:end, :]
            ) * (HEAD_DIM ** (-0.5))
            row_place = lax.broadcasted_iota(jnp.int32, (rows, end), 0) + block * rows
            col_place = lax.broadcasted_iota(jnp.int32, (rows, end), 1)
            allowed = (seg_col_ref[part, :] == seg_row_ref[:, 0:end]) & (col_place <= row_place)
            scores = jnp.where(allowed, scores, NEGATIVE)
            highest = jnp.max(scores, axis=-1, keepdims=True)
            raised = jnp.exp(scores - highest)
            sums = jnp.sum(raised, axis=-1, keepdims=True)
            weights = (raised * (1.0 / sums)).astype(BF)
            mixed = dot(weights, heads_ref[heads + kv_heads + pair_head, 0:end, :])
            mixed_ref[part, head * HEAD_DIM : (head + 1) * HEAD_DIM] = mixed.astype(BF)
            lse_ref[part, head : head + 1] = highest + jnp.log(sums)

    for tile in range((heads + 2 * kv_heads) // 2):
        project(tile)
    pending = [
        (gather, distance) for gather in (down, first, second, third) for distance in range(last)
    ]

    def pump():
        for _ in range(max(1, last // 3)):
            if pending:
                gather, distance = pending.pop(0)
                gather.step(distance)

    zones = width // 512

    def turn(source, target):
        for seq_group in range(4):
            for zone in range(zones):
                at = (seq_group * zones + zone) * 128
                turned[zone * 4 + seq_group] = source[:, at : at + 128].T
        copy = pltpu.make_async_copy(turned, target, load_sem.at[4])
        copy.start()
        return copy

    pump()
    store = turn(lhs, n1_turned)
    pump()
    second.send()
    attend(0)
    pump()
    attend(1)
    pump()
    third.send()
    attend(2)
    dy.forward()
    pump()
    attend(3)
    pump()
    dy.arrive()
    load_dy = pltpu.make_async_copy(dy_full, dy_all, load_sem.at[0])
    load_dy.start()

    out.arrive()
    load_out = pltpu.make_async_copy(out_full, out_w, load_sem.at[2])
    load_out.start()
    load_out.wait()

    def out_piece(seq, column):
        part = pl.ds(pl.multiple_of(seq * rows, rows), rows)
        weight = out_w[:, :, column]
        return dot(mixed_ref[part, :], weight.reshape(-1, weight.shape[-1]))

    middle_ref[...] = hidden_ref[...].astype(F32)
    scatter_sum(here, out_piece, middle_ref, give, got, pair, far_got, (ss, sr), width, 512)
    norm_rows(middle_ref, mlp_gain_ref, own_rows.at[1])
    n2.send()
    store.wait()
    load_dy.wait()
    store = turn(dy_all, dy_turned)
    pump()
    n2.forward()
    n2.arrive()
    load_lhs = pltpu.make_async_copy(n2_full, lhs, load_sem.at[3])
    load_lhs.start()
    pump()
    down.arrive()
    first.arrive()
    load_lhs.wait()

    def feed(gather, begin, count):
        tiles = count // 256
        spot = begin // 256

        def body(gate_w, up_w, down_w, act_ref, gate_grad, up_grad):
            gate_tile = gate_w[...].reshape(width, 256)
            up_tile = up_w[...].reshape(width, 256)
            down_tile = down_w[...]

            @pl.loop(0, 4)
            def _(index):
                part = pl.ds(pl.multiple_of(index * rows, rows), rows)
                gate = dot(lhs[part, :], gate_tile)
                up = dot(lhs[part, :], up_tile)
                act_grad = contract_cols(dy_all[part, :], down_tile)
                sigmoid = jax.nn.sigmoid(gate)
                silu = gate * sigmoid
                act_ref[part, :] = (silu * up).astype(BF)
                gate_grad[part, :] = (
                    act_grad * up * sigmoid * (1.0 + gate * (1.0 - sigmoid))
                ).astype(BF)
                up_grad[part, :] = (act_grad * silu).astype(BF)

        block = gather.whole.shape[:-1] + (256,)
        grads = pair_out.at[0 if begin < chunk else 1]
        first_spot = 0 if begin < chunk + 1 else 2 * (begin - chunk) // 256
        pltpu.emit_pipeline(
            body,
            grid=(tiles,),
            in_specs=[
                pl.BlockSpec(block, lambda t: (0, 0, t)),
                pl.BlockSpec(block, lambda t: (0, 0, t + tiles)),
                pl.BlockSpec((256, width), lambda t: (t + spot, 0)),
            ],
            out_specs=[
                pl.BlockSpec((length, 256), lambda t: (0, t + spot)),
                pl.BlockSpec((length, 256), lambda t: (0, t + first_spot)),
                pl.BlockSpec((length, 256), lambda t: (0, t + first_spot + tiles)),
            ],
        )(gather.whole, gather.whole, down_full, act_out, grads, grads)

    feed(first, 0, chunk)
    pump()
    pump()
    store.wait()
    store = turn(lhs, n2_turned)
    pump()
    second.arrive()
    feed(second, chunk, chunk - tail)
    while pending:
        pump()
    third.arrive()
    feed(third, 2 * chunk - tail, tail)
    store.wait()
    for gather in (qkv, out, first, second, third, down, n1, n2, dy):
        gather.finish()


def forward(hidden, upstream, weights, gains, tables, segment):
    size = lax.axis_size("shard")
    quarter, outer = size // 4, size // 2
    piece, width = hidden.shape
    length = piece * 4
    heads = Q_HEADS // 4
    kv_heads = KV_HEADS // 4
    w_query, _, _, w_out, w_gate, _, w_down = weights
    own = w_query.shape[0]
    qkv_width = (heads + 2 * kv_heads) * HEAD_DIM
    units = w_down.shape[0] // 4 * size

    def shape(*dims, kind=BF):
        return jax.ShapeDtypeStruct(dims, kind)

    results = [
        shape(size, own, qkv_width),
        shape(quarter, *w_out.shape),
        shape(size, own, units),
        shape(size, own, units),
        shape(units, width),
        shape(length, width),
        shape(length, width),
        shape(length, width),
        shape(width // 128, 128, length),
        shape(width // 128, 128, length),
        shape(width // 128, 128, length),
        shape(length, units),
        shape(2, length, units),
        shape(heads + kv_heads, length, HEAD_DIM, kind=F32),
        shape(heads + 2 * kv_heads, length, HEAD_DIM),
        shape(length, heads * HEAD_DIM),
        shape(length, 128, kind=F32),
        shape(piece, width, kind=F32),
    ]
    dma = pltpu.SemaphoreType.DMA
    return pl.pallas_call(
        functools.partial(forward_kernel, size),
        out_shape=results,
        in_specs=[VMEM] + [ANY] * 8 + [VMEM] * 8,
        out_specs=[ANY] * 13 + [VMEM] * 5,
        scratch_shapes=[
            pltpu.VMEM((length, width), BF),
            pltpu.VMEM((length, width), BF),
            pltpu.VMEM((width // 128, 128, length), BF),
            pltpu.VMEM((size, own, qkv_width), BF),
            pltpu.VMEM((quarter,) + w_out.shape, BF),
            pltpu.VMEM((own, qkv_width), BF),
            pltpu.VMEM(w_gate.shape, BF),
            pltpu.VMEM(w_gate.shape, BF),
            pltpu.VMEM((own, units), BF),
            pltpu.VMEM((own, units), BF),
            pltpu.VMEM((2, piece, width), BF),
            pltpu.VMEM((2, piece, width), BF),
            pltpu.VMEM((2, piece, width), BF),
            pltpu.VMEM((piece, width), BF),
            pltpu.VMEM((piece, width), BF),
            dma((6, outer)),
            dma((6, outer)),
            dma((6, outer)),
            dma((6, outer)),
            dma((6, outer)),
            dma((6, outer)),
            dma((6,)),
            dma((3, 3)),
            dma((3, 3)),
            dma((3,)),
            dma((5,)),
            dma((3,)),
            dma((3,)),
        ],
        compiler_params=pltpu.CompilerParams(
            collective_id=0, has_side_effects=True, vmem_limit_bytes=VMEM_BYTES
        ),
        name="forward_gather",
    )(
        hidden,
        upstream,
        *weights,
        *gains,
        *tables,
        segment.reshape(length, 1),
        segment.reshape(1, length),
    )


def add_rows(target, sources, step=16):
    groups, rows, _ = target.shape

    @pl.loop(0, groups * (rows // step))
    def _(index):
        group = index // (rows // step)
        part = pl.ds(pl.multiple_of(lax.rem(index, rows // step) * step, step), step)
        total = sources[0][group, part, :].astype(F32)
        for source in sources[1:]:
            total = total + source[group, part, :].astype(F32)
        target[group, part, :] = total.astype(target.dtype)


class RowSum:
    def __init__(self, here, give, keep, near, rising, falling, stage, total, sems):
        self.here, self.give, self.keep = here, give, keep
        self.near, self.rising, self.falling = near, rising, falling
        self.stage, self.total = stage, total
        self.ys, self.yr, self.us, self.ur, self.ds, self.dr, self.load = sems
        self.last = here.outer - 1

    def across(self, place):
        return remote(
            self.give.at[place],
            self.near.at[place],
            self.ys.at[place],
            self.yr.at[place],
            self.here.twin,
        )

    def up(self, place):
        peer = self.here.outer_peer(self.here.place + 1)
        return remote(
            self.keep.at[place], self.rising.at[place], self.us.at[place], self.ur.at[place], peer
        )

    def down(self, place):
        peer = self.here.outer_peer(self.here.place - 1)
        return remote(
            self.keep.at[place], self.falling.at[place], self.ds.at[place], self.dr.at[place], peer
        )

    def arrived(self, slot, send, receive):
        remote(slot, slot, send, receive, self.here.twin).wait_recv()

    def compute(self, left, right, tiles, zones, ready=None):
        here = self.here
        own = self.give.shape[2]
        per = 128 // (2 * own)
        width = self.give.shape[3]
        step = 256
        for group in range(zones):
            spots = tiles(group)

            @pl.loop(0, width // step)
            def _(index):
                lane = pl.ds(pl.multiple_of(index * step, step), step)
                terms = dot(left(group), right[:, lane])
                for spot, (zone, seq_group) in enumerate(spots):
                    for sub in range(per):
                        at = spot * 128 + sub * 2 * own
                        even, odd = terms[at : at + own], terms[at + own : at + 2 * own]
                        place = zone * per + sub
                        mine = jnp.where(here.half == 0, even, odd).astype(BF)
                        theirs = jnp.where(here.half == 0, odd, even).astype(BF)
                        self.keep[place, seq_group, :, lane] = mine
                        self.give[place, seq_group, :, lane] = theirs

            for zone in sorted({zone for zone, _ in spots}):
                for sub in range(per):
                    self.across(zone * per + sub).start()

    def fold(self, distance):
        here = self.here
        above = here.place + distance
        below = here.place - distance

        def merge(place, line, receive, first):
            near = pltpu.make_async_copy(self.near.at[place], self.stage.at[0], self.load.at[0])
            self.arrived(self.near.at[place], self.ys.at[place], self.yr.at[place])
            near.start()

            @pl.when(first)
            def _():
                near.wait()
                add_rows(self.keep.at[place], [self.keep.at[place], self.stage.at[0]])

            @pl.when(jnp.logical_not(first))
            def _():
                self.arrived(line.at[place], self.us.at[0], receive.at[place])
                far = pltpu.make_async_copy(line.at[place], self.stage.at[1], self.load.at[1])
                far.start()
                near.wait()
                far.wait()
                add_rows(
                    self.keep.at[place], [self.keep.at[place], self.stage.at[0], self.stage.at[1]]
                )

        @pl.when(above <= self.last)
        def _():
            merge(above, self.rising, self.ur, here.place == 0)
            self.up(above).start()

        @pl.when(below >= 0)
        def _():
            merge(below, self.falling, self.dr, here.place == self.last)
            self.down(below).start()

    def finish(self):
        here = self.here
        place = here.place
        self.arrived(self.near.at[place], self.ys.at[place], self.yr.at[place])
        keep = self.keep.at[place]
        near = pltpu.make_async_copy(self.near.at[place], self.stage.at[0], self.load.at[0])
        low = pltpu.make_async_copy(self.rising.at[place], self.stage.at[1], self.load.at[1])
        high = pltpu.make_async_copy(self.falling.at[place], self.stage.at[1], self.load.at[1])
        near.start()

        @pl.when(place > 0)
        def _():
            self.arrived(self.rising.at[place], self.us.at[0], self.ur.at[place])
            low.start()
            low.wait()

        @pl.when(place == 0)
        def _():
            self.arrived(self.falling.at[place], self.ds.at[0], self.dr.at[place])
            high.start()
            high.wait()

        near.wait()

        @pl.when((place > 0) & (place < self.last))
        def _():
            add_rows(keep, [keep, self.stage.at[0], self.stage.at[1]])
            self.arrived(self.falling.at[place], self.ds.at[0], self.dr.at[place])
            high.start()
            high.wait()
            add_rows(self.total, [keep, self.stage.at[1]])

        @pl.when((place == 0) | (place == self.last))
        def _():
            add_rows(self.total, [keep, self.stage.at[0], self.stage.at[1]])

    def sent(self):
        for place in range(self.here.outer):
            self.across(place).wait_send()

    def settle(self):
        here = self.here
        for place in range(here.outer):

            @pl.when(place > here.place)
            def _():
                self.up(place).wait_send()

            @pl.when(place < here.place)
            def _():
                self.down(place).wait_send()


class RowSpread:
    def __init__(self, here, rows, whole, sems):
        self.here, self.rows, self.whole = here, rows, whole
        self.send_sems, self.recv_sems, self.local = sems

    def copy(self, amount):
        seq = lax.rem(self.here.seq + amount, 4)
        return remote(
            self.rows.at[seq],
            self.whole.at[self.here.seq],
            self.send_sems.at[amount - 1],
            self.recv_sems.at[amount - 1],
            {"seq": seq},
        )

    def keep(self):
        seq = self.here.seq
        return pltpu.make_async_copy(self.rows.at[seq], self.whole.at[seq], self.local)

    def send(self):
        for amount in (2, 3, 1):
            self.copy(amount).start()
        self.keep().start()

    def arrive(self):
        for amount in (1, 2, 3):
            self.copy(amount).wait_recv()
        self.keep().wait()

    def finish(self):
        for amount in (1, 2, 3):
            self.copy(amount).wait_send()


class TokenSum:
    def __init__(self, here, part, got, pair, far_got, base, sems):
        self.here, self.part, self.got, self.pair = here, part, got, pair
        self.far_got, self.base = far_got, base
        self.send_sems, self.recv_sems = sems
        self.rows = part.shape[0] // 4

    def piece(self, seq):
        return pl.ds(pl.multiple_of(seq * self.rows, self.rows), self.rows)

    def to_mate(self, index):
        here = self.here
        chip = here.chip if index else 1 - here.chip
        seq = chip * 2 + 1 - here.core
        return remote(
            self.part.at[self.piece(seq), :],
            self.got.at[index],
            self.send_sems.at[index],
            self.recv_sems.at[index],
            here.mate,
        )

    def to_far(self):
        return remote(
            self.pair, self.far_got, self.send_sems.at[2], self.recv_sems.at[2], self.here.far
        )

    def send(self):
        self.to_mate(0).start()
        self.to_mate(1).start()

    def loop(self, body):
        @pl.loop(0, self.rows // 32)
        def _(index):
            body(index * 32)

    def pass_on(self):
        self.to_mate(0).wait_recv()
        begin = self.here.far_seq * self.rows

        def body(at):
            part = pl.ds(pl.multiple_of(at, 32), 32)
            source = pl.ds(pl.multiple_of(begin + at, 32), 32)
            total = self.part[source, :].astype(F32) + self.got[0, part, :].astype(F32)
            self.pair[part, :] = total.astype(BF)

        self.loop(body)
        self.to_far().start()

    def add_near(self):
        self.to_mate(1).wait_recv()
        begin = self.here.seq * self.rows

        def body(at):
            part = pl.ds(pl.multiple_of(at, 32), 32)
            source = pl.ds(pl.multiple_of(begin + at, 32), 32)
            self.base[part, :] += self.part[source, :].astype(F32) + self.got[1, part, :].astype(F32)

        self.loop(body)
        self.to_mate(0).wait_send()
        self.to_mate(1).wait_send()

    def add_far(self):
        self.to_far().wait_recv()

        def body(at):
            part = pl.ds(pl.multiple_of(at, 32), 32)
            self.base[part, :] += self.far_got[part, :].astype(F32)

        self.loop(body)
        self.to_far().wait_send()


class GainSum:
    def __init__(self, here, parts, arrived, sems):
        self.here, self.parts, self.arrived = here, parts, arrived
        self.send_sems, self.recv_sems = sems
        self.peers = [here.mate, here.far, here.twin] + here.line_peers()

    def copy(self, index):
        return remote(
            self.parts.at[index],
            self.arrived.at[index],
            self.send_sems.at[index],
            self.recv_sems.at[index],
            self.peers[index],
        )

    def start(self):
        self.copy(0).start()

    def hop(self, index):
        self.copy(index).wait()
        self.parts[index + 1] = self.parts[index] + self.arrived[index]
        if index + 1 < len(self.peers):
            self.copy(index + 1).start()


def backward_kernel(
    size,
    n1_hbm,
    dy_hbm,
    n2_hbm,
    act_hbm,
    pair_hbm,
    proj_hbm,
    heads_ref,
    mixed_ref,
    lse_ref,
    middle_hbm,
    hidden_hbm,
    dy_own,
    qkv_full,
    out_full,
    first_full,
    second_full,
    down_full,
    attn_gain_ref,
    mlp_gain_ref,
    query_gain_ref,
    key_gain_ref,
    cos_ref,
    sin_ref,
    seg_col_ref,
    seg_row_ref,
    grad_in,
    gains_out,
    grad_out,
    grad_query,
    grad_key,
    grad_value,
    hidden_out,
    grad_gate,
    grad_up,
    grad_down,
    down_rows,
    first_rows,
    second_rows,
    qkv_rows,
    da_hbm,
    near_mlp,
    rising_mlp,
    falling_mlp,
    near_qkv,
    rising_qkv,
    falling_qkv,
    near_out,
    rising_out,
    falling_out,
    lhs,
    turned,
    first_r,
    second_r,
    give,
    keep,
    give_out,
    keep_out,
    stage,
    stage_out,
    total_out,
    dout_ref,
    da_own,
    got,
    far_got,
    pair,
    middle_grad,
    proj_buf,
    lse_t,
    dk_sum,
    dv_sum,
    gain_rows,
    gain_got,
    wide_rows,
    ys,
    yr,
    us,
    ur,
    ds,
    dr,
    fold_load,
    spread_s,
    spread_r,
    spread_l,
    sum_s,
    sum_r,
    ts,
    tr,
    token_local,
    gs,
    gr,
    load_sem,
):
    here = Place(size)
    length, width = lhs.shape
    rows = length // 4
    units = first_r.shape[1]
    chunk = units // 2
    ff_part = units // size
    heads = mixed_ref.shape[1] // HEAD_DIM
    kv_heads = heads // 2
    qkv_width = qkv_full.shape[2]
    last = here.outer - 1
    zones = width // 512
    scale = HEAD_DIM ** (-0.5)

    def load(source, target, index):
        copy = pltpu.make_async_copy(source, target, load_sem.at[index])
        copy.start()
        return copy

    def sems(index):
        return tuple(kind.at[index] for kind in (ys, yr, us, ur, ds, dr, fold_load))

    mlp = [
        RowSum(
            here,
            give.at[index % 2],
            keep.at[index],
            near_mlp.at[index],
            rising_mlp.at[index],
            falling_mlp.at[index],
            stage,
            keep.at[index, here.place],
            sems(index),
        )
        for index in range(3)
    ]
    down, first, second = mlp
    thin = slice(0, qkv_width)
    qkv = RowSum(
        here,
        give.at[1, :, :, :, thin],
        keep.at[0, :, :, :, thin],
        near_qkv,
        rising_qkv,
        falling_qkv,
        stage.at[:, :, :, thin],
        keep.at[0, here.place, :, :, thin],
        sems(3),
    )
    out = RowSum(
        here, give_out, keep_out, near_out, rising_out, falling_out, stage_out, total_out, sems(4)
    )

    def spread(index, job, whole):
        return RowSpread(
            here, job.total, whole, (spread_s.at[index], spread_r.at[index], spread_l.at[index])
        )

    spread_down = spread(0, down, down_rows)
    spread_first = spread(1, first, first_rows)
    spread_second = spread(2, second, second_rows)
    spread_qkv = spread(3, qkv, qkv_rows)

    def token_sum(index, base):
        return TokenSum(
            here, lhs, got, pair, far_got, base, (sum_s.at[index], sum_r.at[index])
        )

    sum_mlp = token_sum(0, middle_grad)
    sum_hidden = token_sum(1, grad_in)
    sum_attn = token_sum(2, grad_in)
    da = TokenGather(here, da_own, da_hbm, (ts, tr, token_local.at[0]))

    def model_tiles(group):
        return [(group, seq_group) for seq_group in range(4)]

    def model_left(group):
        return turned[group * 4 : group * 4 + 4].reshape(512, length)

    load_turned = load(dy_hbm, turned, 0)
    load_act = load(act_hbm, first_r, 1)
    load_middle = load(middle_hbm, grad_in, 2)
    load_dy = load(dy_own, da_own, 4)
    load_second = load(pair_hbm.at[1], second_r, 3)
    here.greet(wide=True)
    load_turned.wait()
    load_act.wait()
    down.compute(model_left, first_r, model_tiles, zones)
    load_turned = load(n2_hbm, turned, 0)
    load_first = load(pair_hbm.at[0], first_r, 1)
    load_first.wait()
    load_second.wait()

    own = width // size
    slabs = 256 // own

    def dn2_body(first_w, second_w):
        lane = pl.ds(pl.multiple_of(pl.program_id(0) * 256, 256), 256)
        first_tile = first_w[...].reshape(256, units)
        second_tile = second_w[...].reshape(256, units)

        @pl.loop(0, 4)
        def _(index):
            part = pl.ds(pl.multiple_of(index * rows, rows), rows)
            total = contract_cols(first_r[part, :], first_tile)
            total = total + contract_cols(second_r[part, :], second_tile)
            lhs[part, lane] = total.astype(BF)

    slab = pl.BlockSpec((slabs, own, units), lambda t: (t, 0, 0))
    pltpu.emit_pipeline(dn2_body, grid=(width // 256,), in_specs=[slab, slab])(
        first_full, second_full
    )
    sum_mlp.send()
    middle_grad[...] = jnp.zeros_like(middle_grad)
    load_turned.wait()
    sum_mlp.pass_on()
    sum_mlp.add_near()
    first.compute(model_left, first_r, model_tiles, zones)
    load_act = load(act_hbm, first_r, 1)
    sum_mlp.add_far()

    load_middle.wait()
    load_dy.wait()
    gain_rows[0] = jnp.zeros_like(gain_rows[0])
    narrow = 16

    @pl.loop(0, rows // narrow)
    def _(index):
        part = pl.ds(pl.multiple_of(index * narrow, narrow), narrow)
        values = grad_in[part, :]
        scales = lax.rsqrt(jnp.mean(values * values, axis=-1, keepdims=True) + EPSILON)
        normed = values * scales
        update = middle_grad[part, :]
        gain_rows[0, 1:2, :] += jnp.sum(update * normed, axis=0, keepdims=True)
        upper = update * mlp_gain_ref[...]
        inner = jnp.mean(upper * normed, axis=-1, keepdims=True)
        grad = da_own[part, :].astype(F32) + scales * (upper - normed * inner)
        middle_grad[part, :] = grad
        da_own[part, :] = grad.astype(BF)

    da.send()
    down.sent()
    second.compute(model_left, second_r, model_tiles, zones)

    def hidden_body(weight):
        lane = pl.ds(pl.multiple_of(pl.program_id(0) * 256, 256), 256)
        tile = weight[...]

        @pl.loop(0, 4)
        def _(index):
            part = pl.ds(pl.multiple_of(index * rows, rows), rows)
            lhs[part, lane] = dot(first_r[part, :], tile).astype(BF)

    load_act.wait()
    pltpu.emit_pipeline(
        hidden_body,
        grid=(width // 256,),
        in_specs=[pl.BlockSpec((units, 256), lambda t: (0, t))],
    )(down_full)
    da.mate_arrived()
    sum_hidden.send()
    da.forward()
    sum_hidden.pass_on()
    sum_hidden.add_near()
    for distance in range(last, 0, -1):
        down.fold(distance)
    da.rest_arrived()
    da.finish()
    load_lhs = load(da_hbm, lhs, 0)
    load_own = load(hidden_hbm, da_own, 2)
    load_lhs.wait()

    def dout_body(weight):
        lane = pl.ds(pl.multiple_of(pl.program_id(0) * 256, 256), 256)
        tile = weight[...].reshape(256, width)

        @pl.loop(0, 4)
        def _(index):
            part = pl.ds(pl.multiple_of(index * rows, rows), rows)
            dout_ref[part, lane] = contract_cols(lhs[part, :], tile).astype(BF)

    out_blocks, out_rows = out_full.shape[:2]
    pltpu.emit_pipeline(
        dout_body,
        grid=(out_blocks * out_rows // 256,),
        in_specs=[pl.BlockSpec((256 // out_rows, out_rows, width), lambda t: (t, 0, 0))],
    )(out_full)

    for head in range(heads):
        turned[head] = mixed_ref[:, head * HEAD_DIM : (head + 1) * HEAD_DIM].T
    out.compute(
        lambda group: turned[0:heads].reshape(heads * HEAD_DIM, length),
        lhs,
        lambda group: [(zone, 0) for zone in range(heads)],
        1,
    )
    load_turned = load(n1_hbm, turned, 0)
    down.finish()
    sum_hidden.add_far()

    @pl.loop(0, rows // 32)
    def _(index):
        part = pl.ds(pl.multiple_of(index * 32, 32), 32)
        pair[part, :] = grad_in[part, :].astype(BF)

    store_hidden = load(pair, hidden_out, 1)
    spread_down.send()

    lse_t[...] = lse_ref[...].T[0:8]
    pending = [(first, distance) for distance in range(last, 0, -1)]

    def pump():
        for _ in range(max(1, last // 3)):
            if pending:
                job, distance = pending.pop(0)
                job.fold(distance)

    def through_norm(grad, head, part, gain_ref, gain_row):
        proj = proj_buf[lax.rem(head, 2), part, :]
        scales = lax.rsqrt(jnp.mean(proj * proj, axis=-1, keepdims=True) + EPSILON)
        normed = proj * scales
        grad = grad.astype(F32)
        upper = grad * cos_ref[part, :] - pltpu.roll(grad, HEAD_DIM // 2, 1) * sin_ref[part, :]
        gain_rows[0, 2:3, gain_row * HEAD_DIM : (gain_row + 1) * HEAD_DIM] += jnp.sum(
            upper * normed, axis=0, keepdims=True
        )
        upper = upper * gain_ref[...]
        inner = jnp.mean(upper * normed, axis=-1, keepdims=True)
        result = (scales * (upper - normed * inner)).astype(BF)
        first_r[part, head * HEAD_DIM : (head + 1) * HEAD_DIM] = result

    for head in range(heads):
        pair_head = head // 2
        load_proj = load(proj_hbm.at[head], proj_buf.at[head % 2], 4)
        if head % 2 == 0:
            dk_sum[...] = jnp.zeros_like(dk_sum)
            dv_sum[...] = jnp.zeros_like(dv_sum)
        load_proj.wait()
        for block in range(4):
            end = (block + 1) * rows
            part = pl.ds(block * rows, rows)
            queries = heads_ref[head, part, :]
            keys = heads_ref[heads + pair_head, 0:end, :]
            values = heads_ref[heads + kv_heads + pair_head, 0:end, :]
            out_grad = dout_ref[part, head * HEAD_DIM : (head + 1) * HEAD_DIM]
            scores = contract_cols(keys, queries) * scale
            key_place = lax.broadcasted_iota(jnp.int32, (end, rows), 0)
            query_place = lax.broadcasted_iota(jnp.int32, (end, rows), 1) + block * rows
            allowed = (seg_col_ref[0:end, :] == seg_row_ref[:, part]) & (key_place <= query_place)
            weights = jnp.exp(
                jnp.where(allowed, scores, NEGATIVE) - lse_t[head : head + 1, part]
            )
            weight_grad = contract_cols(values, out_grad)
            inner = jnp.sum(weights * weight_grad, axis=0, keepdims=True)
            score_grad = (weights * (weight_grad - inner)).astype(BF)
            dk_sum[0:end, :] += dot(score_grad, queries) * scale
            dv_sum[0:end, :] += dot(weights.astype(BF), out_grad)
            query_grad = (contract_rows(score_grad, keys) * scale).astype(BF)
            through_norm(query_grad, head, part, query_gain_ref, 0)
        if head % 2:
            key = heads + pair_head
            value_at = (heads + kv_heads + pair_head) * HEAD_DIM
            load(proj_hbm.at[key], proj_buf.at[key % 2], 4).wait()

            @pl.loop(0, 4)
            def _(index):
                part = pl.ds(pl.multiple_of(index * rows, rows), rows)
                through_norm(dk_sum[part, :].astype(BF), key, part, key_gain_ref, 1)
                first_r[part, value_at : value_at + HEAD_DIM] = dv_sum[part, :].astype(BF)

        pump()

    load_turned.wait()
    down.settle()
    spread_down.finish()
    spread_down.arrive()
    first.sent()
    store_hidden.wait()
    proj_grads = first_r.at[:, 0:qkv_width]
    qkv.compute(model_left, proj_grads, model_tiles, zones)

    def dn1_body(weight):
        lane = pl.ds(pl.multiple_of(pl.program_id(0) * 256, 256), 256)
        tile = weight[...].reshape(256, qkv_width)

        @pl.loop(0, 4)
        def _(index):
            part = pl.ds(pl.multiple_of(index * rows, rows), rows)
            lhs[part, lane] = contract_cols(proj_grads[part, :], tile).astype(BF)

    pltpu.emit_pipeline(
        dn1_body,
        grid=(width // 256,),
        in_specs=[pl.BlockSpec((slabs, own, qkv_width), lambda t: (t, 0, 0))],
    )(qkv_full)
    grad_in[...] = jnp.zeros_like(grad_in)
    sum_attn.send()
    while pending:
        pump()
    sum_attn.pass_on()
    sum_attn.add_near()
    first.finish()
    spread_first.send()
    sum_attn.add_far()
    load_own.wait()

    @pl.loop(0, rows // narrow)
    def _(index):
        part = pl.ds(pl.multiple_of(index * narrow, narrow), narrow)
        values = da_own[part, :].astype(F32)
        scales = lax.rsqrt(jnp.mean(values * values, axis=-1, keepdims=True) + EPSILON)
        normed = values * scales
        update = grad_in[part, :]
        gain_rows[0, 0:1, :] += jnp.sum(update * normed, axis=0, keepdims=True)
        upper = update * attn_gain_ref[...]
        inner = jnp.mean(upper * normed, axis=-1, keepdims=True)
        grad_in[part, :] = middle_grad[part, :] + scales * (upper - normed * inner)

    gain_sum = GainSum(here, gain_rows, gain_got, (gs, gr))
    gain_sum.start()
    hops = list(range(len(gain_sum.peers)))

    def next_hop():
        if hops:
            gain_sum.hop(hops.pop(0))

    for distance in range(last, 0, -1):
        second.fold(distance)
        next_hop()
    second.finish()
    spread_second.send()
    for distance in range(last, 0, -1):
        out.fold(distance)
        next_hop()
    while hops:
        next_hop()
    gains_out[...] = gain_rows[gain_rows.shape[0] - 1]

    def units_of(read, target):
        @pl.loop(0, wide_rows.shape[0] // 16)
        def _(index):
            part = pl.ds(pl.multiple_of(index * 16, 16), 16)
            values = [read(seq, part).astype(F32) for seq in range(4)]
            pieces = [
                values[seq][:, block * ff_part : (block + 1) * ff_part]
                for block in range(size)
                for seq in range(4)
            ]
            wide_rows[part, :] = jnp.concatenate(pieces, axis=1)

        load(wide_rows, target, 3).wait()

    load(down_rows, stage.at[0], 1).wait()
    units_of(lambda seq, part: stage[0, seq, part, :], grad_down)
    for distance in range(last, 0, -1):
        qkv.fold(distance)
    out.finish()
    grad_out[...] = total_out[0]
    spread_first.arrive()
    spread_second.arrive()
    load_first = load(first_rows, stage.at[0], 1)
    load(second_rows, stage.at[1], 2).wait()
    load_first.wait()
    most, tail = chunk - 256, 256

    def halves(side):
        def read(seq, part):
            return jnp.concatenate(
                [
                    stage[0, seq, part, side * chunk : (side + 1) * chunk],
                    stage[1, seq, part, side * most : (side + 1) * most],
                    stage[1, seq, part, 2 * most + side * tail : 2 * most + (side + 1) * tail],
                ],
                axis=1,
            )

        return read

    units_of(halves(0), grad_gate)
    units_of(halves(1), grad_up)
    qkv.finish()
    spread_qkv.send()
    spread_qkv.arrive()
    load(qkv_rows, stage.at[0, :, :, thin], 1).wait()
    q_part, kv_part = heads * HEAD_DIM, kv_heads * HEAD_DIM
    for seq in range(4):
        at = 0
        for target, count in ((grad_query, q_part), (grad_key, kv_part), (grad_value, kv_part)):
            target[:, seq * count : (seq + 1) * count] = stage[0, seq, :, at : at + count].astype(F32)
            at += count
    for job in (spread_first, spread_second, spread_qkv):
        job.finish()
    for job in (second, out, qkv):
        job.sent()
    for job in (first, second, out, qkv):
        job.settle()


def backward(saved, weights, own, gains, tables, segment):
    size = lax.axis_size("shard")
    outer = size // 2
    (n1, dy, n2, act, pairs, proj, heads_all, mixed, lse, middle) = saved
    length, width = heads_all.shape[1], middle.shape[1]
    piece = length // 4
    units = act.shape[1]
    qkv_width = weights[0].shape[2]
    rows = width // (4 * size)
    q_width = mixed.shape[1]

    def shape(*dims, kind=BF):
        return jax.ShapeDtypeStruct(dims, kind)

    results = [
        shape(piece, width, kind=F32),
        shape(8, width, kind=F32),
        shape(rows, width, kind=F32),
        shape(rows, 4 * q_width, kind=F32),
        shape(rows, 2 * q_width, kind=F32),
        shape(rows, 2 * q_width, kind=F32),
        shape(piece, width),
        shape(rows, 4 * units, kind=F32),
        shape(rows, 4 * units, kind=F32),
        shape(rows, 4 * units, kind=F32),
        shape(4, rows, units),
        shape(4, rows, units),
        shape(4, rows, units),
        shape(4, rows, qkv_width),
        shape(length, width),
    ]
    results += [shape(3, outer, 4, rows, units)] * 3
    results += [shape(outer, 4, rows, qkv_width)] * 3
    results += [shape(outer, 1, rows, width)] * 3
    dma = pltpu.SemaphoreType.DMA
    hops = 3 + outer.bit_length() - 1
    vmem = pltpu.VMEM
    return pl.pallas_call(
        functools.partial(backward_kernel, size),
        out_shape=results,
        in_specs=[ANY] * 6 + [VMEM] * 3 + [ANY] * 8 + [VMEM] * 8,
        out_specs=[VMEM] * 6 + [ANY] * (len(results) - 6),
        scratch_shapes=[
            vmem((length, width), BF),
            vmem((width // 128, 128, length), BF),
            vmem((length, units), BF),
            vmem((length, units), BF),
            vmem((2, outer, 4, rows, units), BF),
            vmem((3, outer, 4, rows, units), BF),
            vmem((outer, 1, rows, width), BF),
            vmem((outer, 1, rows, width), BF),
            vmem((2, 4, rows, units), BF),
            vmem((2, 1, rows, width), BF),
            vmem((1, rows, width), F32),
            vmem((length, q_width), BF),
            vmem((piece, width), BF),
            vmem((2, piece, width), BF),
            vmem((piece, width), BF),
            vmem((piece, width), BF),
            vmem((piece, width), F32),
            vmem((2, length, HEAD_DIM), F32),
            vmem((8, length), F32),
            vmem((length, HEAD_DIM), F32),
            vmem((length, HEAD_DIM), F32),
            vmem((hops + 1, 8, width), F32),
            vmem((hops, 8, width), F32),
            vmem((rows, 4 * units), F32),
            dma((5, outer)),
            dma((5, outer)),
            dma((5, outer)),
            dma((5, outer)),
            dma((5, outer)),
            dma((5, outer)),
            dma((5, 3)),
            dma((4, 3)),
            dma((4, 3)),
            dma((4,)),
            dma((3, 3)),
            dma((3, 3)),
            dma((3,)),
            dma((3,)),
            dma((1,)),
            dma((hops,)),
            dma((hops,)),
            dma((5,)),
        ],
        compiler_params=pltpu.CompilerParams(
            collective_id=1, has_side_effects=True, vmem_limit_bytes=VMEM_BYTES
        ),
        name="backward_sums",
    )(
        n1,
        dy,
        n2,
        act,
        pairs,
        proj,
        heads_all,
        mixed,
        lse,
        middle,
        *own,
        *weights,
        *gains,
        *tables,
        segment.reshape(length, 1),
        segment.reshape(1, length),
    )


def local(
    hidden_in,
    segment_ids,
    norm_attn_gain,
    w_query,
    w_key,
    w_value,
    query_gain,
    key_gain,
    w_out,
    norm_mlp_gain,
    w_gate,
    w_up,
    w_down,
    out_cotangent,
):
    length = hidden_in.shape[1] * 4
    segment = segment_ids[0]
    places = jnp.arange(length, dtype=jnp.int32)
    starts = jnp.sum((segment[None, :] < segment[:, None]).astype(jnp.int32), axis=1)
    cosine, sine = rotary_tables(places - starts)
    signs = jnp.where(jnp.arange(HEAD_DIM) < HEAD_DIM // 2, -1.0, 1.0).astype(F32)
    tables = (cosine, sine * signs)
    gains = (norm_attn_gain[None], norm_mlp_gain[None], query_gain[None], key_gain[None])
    results = forward(
        hidden_in[0],
        out_cotangent[0],
        (w_query, w_key, w_value, w_out, w_gate, w_up, w_down),
        gains,
        tables,
        segment,
    )
    (
        grad_in,
        gain_totals,
        grad_out,
        grad_query,
        grad_key,
        grad_value,
        hidden_out,
        grad_gate,
        grad_up,
        grad_down,
    ) = backward(
        results[8:],
        results[:5],
        (hidden_in[0], out_cotangent[0]),
        gains,
        tables,
        segment,
    )[:10]
    return (
        hidden_out[None],
        grad_in[None],
        gain_totals[0],
        grad_query,
        grad_key,
        grad_value,
        gain_totals[2, :HEAD_DIM],
        gain_totals[2, HEAD_DIM : 2 * HEAD_DIM],
        grad_out,
        gain_totals[1],
        grad_gate,
        grad_up,
        grad_down.T,
    )


def solution(mesh):
    return jax.shard_map(
        local,
        mesh=mesh,
        in_specs=(
            P("shard", "seq", None),
            P("shard", None),
            P(),
            P("shard", None),
            P("shard", None),
            P("shard", None),
            P(),
            P(),
            P("shard", None),
            P(),
            P("shard", None),
            P("shard", None),
            P("shard", None),
            P("shard", "seq", None),
        ),
        out_specs=(
            P("shard", "seq", None),
            P("shard", "seq", None),
            P(),
            P(("seq", "shard"), None),
            P(("seq", "shard"), None),
            P(("seq", "shard"), None),
            P(),
            P(),
            P(("seq", "shard"), None),
            P(),
            P(("seq", "shard"), None),
            P(("seq", "shard"), None),
            P(None, ("seq", "shard")),
        ),
        check_vma=False,
    )
```

```python
import functools

import jax
import jax.numpy as jnp
from jax import lax
from jax.experimental import pallas as pl
from jax.experimental.pallas import tpu as pltpu
from jax.sharding import PartitionSpec as P

Q_HEADS = 16
KV_HEADS = 8
HEAD_DIM = 128
EPSILON = 1e-06
ROPE_BASE = 1000000.0
NEGATIVE = -1e30
BF = jnp.bfloat16
F32 = jnp.float32
MESH = pl.DeviceIdType.MESH
ANY = pl.BlockSpec(memory_space=pl.ANY)
VMEM = pl.BlockSpec(memory_space=pltpu.VMEM)
VMEM_BYTES = 62 * 1024 * 1024


def rotary_tables(positions):
    inverse = ROPE_BASE ** (-(jnp.arange(HEAD_DIM // 2, dtype=F32) * 2.0) / HEAD_DIM)
    angles = positions.astype(F32)[:, None] * inverse[None, :]
    angles = jnp.concatenate([angles, angles], axis=-1)
    return (jnp.cos(angles), jnp.sin(angles))


def dot(left, right):
    return jnp.dot(left, right, preferred_element_type=F32)


def contract_rows(left, right):
    return lax.dot_general(left, right, (((0,), (0,)), ((), ())), preferred_element_type=F32)


def contract_cols(left, right):
    return lax.dot_general(left, right, (((1,), (1,)), ((), ())), preferred_element_type=F32)


class Place:
    def __init__(self, size):
        self.size = size
        self.outer = size // 2
        self.quarter = size // 4
        self.seq = lax.axis_index("seq")
        self.shard = lax.axis_index("shard")
        self.chip = self.seq // 2
        self.core = lax.rem(self.seq, 2)
        self.place = self.shard // 2
        self.half = lax.rem(self.shard, 2)
        self.far_seq = lax.rem(self.seq + 2, 4)
        self.mate_seq = self.chip * 2 + 1 - self.core
        self.far = {"seq": self.far_seq}
        self.mate = {"seq": self.mate_seq}
        self.twin_shard = self.place * 2 + 1 - self.half
        self.twin = {"shard": self.twin_shard}

    def outer_peer(self, place):
        return {"shard": place * 2 + self.half}

    def line_peers(self):
        peers = []
        step = 1
        while step < self.outer:
            sign = 1 - 2 * lax.rem(self.place // step, 2)
            peers.append(self.outer_peer(self.place + sign * step))
            step *= 2
        return peers

    def greet(self, wide=False):
        barrier = pltpu.get_barrier_semaphore()
        last = self.outer - 1

        def signal(peer):
            pl.semaphore_signal(barrier, inc=1, device_id=peer, device_id_type=MESH)

        peers = [self.far, self.mate, self.twin]
        if wide:
            peers += [{"seq": 3 - self.seq}] + self.line_peers()[1:]
        for peer in peers:
            signal(peer)

        @pl.when(self.place < last)
        def _():
            signal(self.outer_peer(self.place + 1))

        @pl.when(self.place > 0)
        def _():
            signal(self.outer_peer(self.place - 1))

        inner = ((self.place > 0) & (self.place < last)).astype(jnp.int32)
        pl.semaphore_wait(barrier, len(peers) + 1 + inner)


def remote(source, target, send, receive, peer):
    return pltpu.make_async_remote_copy(
        src_ref=source,
        dst_ref=target,
        send_sem=send,
        recv_sem=receive,
        device_id=peer,
        device_id_type=MESH,
    )


class RowGather:
    def __init__(self, here, own, whole, sems, spot=lambda shard: shard):
        self.here, self.own, self.whole, self.spot = here, own, whole, spot
        self.us, self.ur, self.ds, self.dr, self.ys, self.yr, self.local = sems
        self.last = here.outer - 1

    def slot(self, place):
        return self.whole.at[self.spot(place * 2 + self.here.half)]

    def keep(self):
        return pltpu.make_async_copy(self.own, self.slot(self.here.place), self.local)

    def up(self, distance):
        here = self.here
        slot = self.slot(here.place - distance)
        source = slot if distance else self.own
        peer = here.outer_peer(here.place + 1)
        return remote(source, slot, self.us.at[distance], self.ur.at[distance], peer)

    def down(self, distance):
        here = self.here
        slot = self.slot(here.place + distance)
        source = slot if distance else self.own
        peer = here.outer_peer(here.place - 1)
        return remote(source, slot, self.ds.at[distance], self.dr.at[distance], peer)

    def across(self, place, own=False):
        slot = self.slot(place)
        source = self.own if own else slot
        return remote(source, slot, self.ys.at[place], self.yr.at[place], self.here.twin)

    def send(self):
        here = self.here

        @pl.when(here.place < self.last)
        def _():
            self.up(0).start()

        @pl.when(here.place > 0)
        def _():
            self.down(0).start()

        self.across(here.place, own=True).start()
        self.keep().start()

    def step(self, distance):
        here = self.here
        below = here.place - 1 - distance
        above = here.place + 1 + distance

        @pl.when(below >= 0)
        def _():
            slot = self.slot(below)
            remote(
                slot, slot, self.us.at[0], self.ur.at[distance], self.here.twin
            ).wait_recv()

            @pl.when(here.place < self.last)
            def _():
                self.up(distance + 1).start()

            self.across(below).start()

        @pl.when(above <= self.last)
        def _():
            slot = self.slot(above)
            remote(
                slot, slot, self.ds.at[0], self.dr.at[distance], self.here.twin
            ).wait_recv()

            @pl.when(here.place > 0)
            def _():
                self.down(distance + 1).start()

            self.across(above).start()

    def arrive(self):
        self.keep().wait()
        for place in range(self.here.outer):
            slot = self.whole.at[self.spot(place * 2 + 1 - self.here.half)]
            remote(
                slot, slot, self.ys.at[place], self.yr.at[place], self.here.twin
            ).wait_recv()

    def finish(self):
        here = self.here
        for distance in range(self.last):

            @pl.when((here.place - distance >= 0) & (here.place < self.last))
            def _():
                self.up(distance).wait_send()

            @pl.when((here.place + distance <= self.last) & (here.place > 0))
            def _():
                self.down(distance).wait_send()

        for place in range(here.outer):
            self.across(place).wait_send()


class HeadGather:
    def __init__(self, here, own, whole, sems):
        self.here, self.own, self.whole = here, own, whole
        self.us, self.zr, self.ds, _, self.ys, self.yr, self.local = sems
        self.last = here.outer - 1
        self.count = here.quarter // 2
        self.first = here.seq * self.count
        self.mine = here.place - self.first
        self.inside = (self.mine >= 0) & (self.mine < self.count)

    def slot(self, index):
        return self.whole.at[index * 2 + self.here.half]

    def keep(self):
        return pltpu.make_async_copy(self.own, self.slot(self.mine), self.local)

    def up(self, index, own=False):
        slot = self.slot(index)
        peer = self.here.outer_peer(self.here.place + 1)
        return remote(self.own if own else slot, slot, self.us.at[index], self.zr.at[index], peer)

    def down(self, index, own=False):
        slot = self.slot(index)
        peer = self.here.outer_peer(self.here.place - 1)
        return remote(self.own if own else slot, slot, self.ds.at[index], self.zr.at[index], peer)

    def across(self, index):
        slot = self.slot(index)
        return remote(slot, slot, self.ys.at[index], self.yr.at[index], self.here.twin)

    def send(self):
        @pl.when(self.inside)
        def _():
            self.keep().start()

            @pl.when(self.here.place < self.last)
            def _():
                self.up(self.mine, own=True).start()

            @pl.when(self.here.place > 0)
            def _():
                self.down(self.mine, own=True).start()

    def step(self):
        here = self.here

        @pl.when(self.inside)
        def _():
            self.keep().wait()

        for index in range(self.count):
            slot = self.slot(index)
            arrival = remote(slot, slot, self.us.at[0], self.zr.at[index], here.twin)

            @pl.when(self.mine > index)
            def _():
                arrival.wait_recv()

                @pl.when(here.place < self.last)
                def _():
                    self.up(index).start()

            @pl.when(self.mine < index)
            def _():
                arrival.wait_recv()

                @pl.when(here.place > 0)
                def _():
                    self.down(index).start()

            self.across(index).start()

    def arrive(self):
        for index in range(self.count):
            slot = self.whole.at[index * 2 + 1 - self.here.half]
            remote(
                slot, slot, self.ys.at[index], self.yr.at[index], self.here.twin
            ).wait_recv()

    def finish(self):
        here = self.here
        for index in range(self.count):

            @pl.when((self.mine >= index) & (here.place < self.last))
            def _():
                self.up(index).wait_send()

            @pl.when((self.mine <= index) & (here.place > 0))
            def _():
                self.down(index).wait_send()

            self.across(index).wait_send()


class TokenGather:
    def __init__(self, here, own, whole, sems):
        self.here, self.own, self.whole = here, own, whole
        self.send_sems, self.recv_sems, self.local = sems
        self.rows = whole.shape[0] // 4

    def slot(self, seq):
        return self.whole.at[pl.ds(pl.multiple_of(seq * self.rows, self.rows), self.rows), :]

    def keep(self):
        return pltpu.make_async_copy(self.own, self.slot(self.here.seq), self.local)

    def copy(self, index):
        here = self.here
        slot = self.slot(here.far_seq if index == 2 else here.seq)
        return remote(
            slot if index == 2 else self.own,
            slot,
            self.send_sems.at[index],
            self.recv_sems.at[index],
            here.far if index == 0 else here.mate,
        )

    def send(self):
        self.copy(0).start()
        self.copy(1).start()
        self.keep().start()

    def forward(self):
        self.copy(0).wait_recv()
        self.copy(2).start()

    def mate_arrived(self):
        self.copy(1).wait_recv()

    def rest_arrived(self):
        self.copy(2).wait_recv()
        self.keep().wait()

    def arrive(self):
        self.mate_arrived()
        self.rest_arrived()

    def finish(self):
        for index in range(3):
            self.copy(index).wait_send()


def scatter_sum(here, piece, base, give, got, pair, far_got, sems, width, step):
    send_sems, recv_sems = sems
    other = 1 - here.chip
    to_mate = [
        remote(
            give.at[chip], got.at[chip], send_sems.at[index], recv_sems.at[index], here.mate
        )
        for index, chip in enumerate((other, here.chip))
    ]
    to_far = remote(pair, far_got, send_sems.at[2], recv_sems.at[2], here.far)

    def columns(body):
        @pl.loop(0, width // step)
        def _(index):
            body(pl.ds(pl.multiple_of(index * step, step), step))

    for index, chip in enumerate((other, here.chip)):
        seq = chip * 2 + 1 - here.core

        def fill(column, chip=chip, seq=seq):
            give[chip, :, column] = piece(seq, column).astype(BF)

        columns(fill)
        to_mate[index].start()

    to_mate[0].wait_recv()

    def fill_pair(column):
        term = piece(here.far_seq, column) + got[other, :, column].astype(F32)
        pair[:, column] = term.astype(BF)

    columns(fill_pair)
    to_far.start()
    to_mate[1].wait_recv()

    def fill_base(column):
        base[:, column] += piece(here.seq, column) + got[here.chip, :, column].astype(F32)

    columns(fill_base)
    to_far.wait_recv()

    def fill_far(column):
        base[:, column] += far_got[:, column].astype(F32)

    columns(fill_far)
    for copy in (*to_mate, to_far):
        copy.wait_send()


def forward_kernel(
    size,
    hidden_ref,
    dy_own,
    w_query,
    w_key,
    w_value,
    w_out,
    w_gate,
    w_up,
    w_down,
    attn_gain_ref,
    mlp_gain_ref,
    query_gain_ref,
    key_gain_ref,
    cos_ref,
    sin_ref,
    seg_col_ref,
    seg_row_ref,
    qkv_full,
    out_full,
    first_full,
    second_full,
    down_full,
    n1_full,
    dy_full,
    n2_full,
    n1_turned,
    dy_turned,
    n2_turned,
    act_out,
    first_pair,
    second_pair,
    proj_ref,
    heads_ref,
    mixed_ref,
    lse_ref,
    middle_ref,
    lhs,
    dy_all,
    turned,
    qkv_w,
    out_w,
    qkv_own,
    gate_all,
    up_all,
    first_own,
    second_own,
    own_rows,
    give,
    got,
    pair,
    far_got,
    us,
    ur,
    ds,
    dr,
    ys,
    yr,
    row_local,
    ts,
    tr,
    token_local,
    load_sem,
    ss,
    sr,
):
    here = Place(size)
    length, width = lhs.shape
    lse_ref[...] = jnp.zeros_like(lse_ref)
    rows = length // 4
    units = act_out.shape[1]
    chunk = units // 2
    tail = 256
    heads = mixed_ref.shape[1] // HEAD_DIM
    kv_heads = heads // 2
    ff_part = units // size

    def sems(index):
        return tuple(kind.at[index] for kind in (us, ur, ds, dr, ys, yr, row_local))

    down_rows = pl.ds(pl.multiple_of(here.seq * ff_part, ff_part), ff_part)
    qkv = RowGather(here, qkv_own, qkv_full, sems(0))
    out = HeadGather(here, w_out, out_full, sems(1))
    down = RowGather(
        here,
        w_down.at[down_rows, :],
        down_full,
        sems(2),
        lambda shard: pl.ds(pl.multiple_of(shard * ff_part, ff_part), ff_part),
    )
    first = RowGather(here, first_own, first_full, sems(3))
    cut = 2 * (chunk - tail)
    second = RowGather(here, second_own.at[:, 0:cut], second_full.at[:, :, 0:cut], sems(4))
    third = RowGather(
        here, second_own.at[:, cut : 2 * chunk], second_full.at[:, :, cut : 2 * chunk], sems(5)
    )
    n1 = TokenGather(here, own_rows.at[0], n1_full, (ts.at[0], tr.at[0], token_local.at[0]))
    n2 = TokenGather(here, own_rows.at[1], n2_full, (ts.at[1], tr.at[1], token_local.at[1]))
    dy = TokenGather(here, dy_own, dy_full, (ts.at[2], tr.at[2], token_local.at[2]))

    loads = []
    at = 0
    for index, (weight, count) in enumerate(((w_query, heads), (w_key, kv_heads), (w_value, kv_heads))):
        count = count * HEAD_DIM
        source = weight.at[:, pl.ds(pl.multiple_of(here.seq * count, count), count)]
        loads.append(
            pltpu.make_async_copy(source, qkv_own.at[:, at : at + count], load_sem.at[index])
        )
        at += count
    loads.append(pltpu.make_async_copy(w_gate, gate_all, load_sem.at[3]))
    loads.append(pltpu.make_async_copy(w_up, up_all, load_sem.at[4]))
    for load in loads:
        load.start()
    here.greet()
    for load in loads[:3]:
        load.wait()
    qkv.send()
    out.send()

    def norm_rows(source, gain_ref, target):
        @pl.loop(0, rows // 32)
        def _(index):
            part = pl.ds(pl.multiple_of(index * 32, 32), 32)
            values = source[part, :].astype(F32)
            scales = lax.rsqrt(jnp.mean(values * values, axis=-1, keepdims=True) + EPSILON)
            target[part, :] = (values * scales * gain_ref[...]).astype(BF)

    norm_rows(hidden_ref, attn_gain_ref, own_rows.at[0])
    n1.send()
    down.send()
    for load in loads[3:]:
        load.wait()

    for seq in range(4):

        @pl.when(here.seq == seq)
        def _():
            @pl.loop(0, first_own.shape[0] // 16)
            def _(index):
                part = pl.ds(pl.multiple_of(index * 16, 16), 16)

                def gathered(source, begin):
                    pieces = [
                        source[part, (block * 4 + seq) * ff_part : (block * 4 + seq + 1) * ff_part]
                        for block in range(begin, begin + size // 2)
                    ]
                    return jnp.concatenate(pieces, axis=1)

                first_own[part, 0:chunk] = gathered(gate_all, 0)
                first_own[part, chunk : 2 * chunk] = gathered(up_all, 0)
                gate = gathered(gate_all, size // 2)
                up = gathered(up_all, size // 2)
                most = chunk - tail
                second_own[part, 0:most] = gate[:, 0:most]
                second_own[part, most : 2 * most] = up[:, 0:most]
                second_own[part, 2 * most : 2 * most + tail] = gate[:, most:]
                second_own[part, 2 * most + tail : 2 * chunk] = up[:, most:]

    last = here.outer - 1
    for distance in range(last):
        qkv.step(distance)
    n1.forward()
    first.send()
    n1.arrive()
    load_lhs = pltpu.make_async_copy(n1_full, lhs, load_sem.at[0])
    load_lhs.start()
    dy.send()
    out.step()
    qkv.arrive()
    load_qkv = pltpu.make_async_copy(qkv_full, qkv_w, load_sem.at[1])
    load_qkv.start()
    load_lhs.wait()
    load_qkv.wait()

    def project(tile):
        weight = qkv_w[:, :, tile * 256 : tile * 256 + 256].reshape(width, 256)
        gain_ref = query_gain_ref if tile < heads // 2 else key_gain_ref

        @pl.loop(0, 4)
        def _(index):
            part = pl.ds(pl.multiple_of(index * rows, rows), rows)
            both = dot(lhs[part, :], weight)
            for side in range(2):
                head = tile * 2 + side
                proj = both[:, side * HEAD_DIM : (side + 1) * HEAD_DIM]
                if head >= heads + kv_heads:
                    heads_ref[head, part, :] = proj.astype(BF)
                    continue
                proj_ref[head, part, :] = proj
                scales = lax.rsqrt(jnp.mean(proj * proj, axis=-1, keepdims=True) + EPSILON)
                gained = proj * scales * gain_ref[...]
                turned = pltpu.roll(gained, HEAD_DIM // 2, 1)
                heads_ref[head, part, :] = (
                    gained * cos_ref[part, :] + turned * sin_ref[part, :]
                ).astype(BF)

    def attend(head):
        pair_head = head // 2
        for block in range(4):
            end = (block + 1) * rows
            part = pl.ds(block * rows, rows)
            scores = contract_cols(
                heads_ref[head, part, :], heads_ref[heads + pair_head, 0:end, :]
            ) * (HEAD_DIM ** (-0.5))
            row_place = lax.broadcasted_iota(jnp.int32, (rows, end), 0) + block * rows
            col_place = lax.broadcasted_iota(jnp.int32, (rows, end), 1)
            allowed = (seg_col_ref[part, :] == seg_row_ref[:, 0:end]) & (col_place <= row_place)
            scores = jnp.where(allowed, scores, NEGATIVE)
            highest = jnp.max(scores, axis=-1, keepdims=True)
            raised = jnp.exp(scores - highest)
            sums = jnp.sum(raised, axis=-1, keepdims=True)
            weights = (raised * (1.0 / sums)).astype(BF)
            mixed = dot(weights, heads_ref[heads + kv_heads + pair_head, 0:end, :])
            mixed_ref[part, head * HEAD_DIM : (head + 1) * HEAD_DIM] = mixed.astype(BF)
            lse_ref[part, head : head + 1] = highest + jnp.log(sums)

    for tile in range((heads + 2 * kv_heads) // 2):
        project(tile)
    pending = [
        (gather, distance) for gather in (down, first, second, third) for distance in range(last)
    ]

    def pump():
        for _ in range(max(1, last // 3)):
            if pending:
                gather, distance = pending.pop(0)
                gather.step(distance)

    zones = width // 512

    def turn(source, target):
        for seq_group in range(4):
            for zone in range(zones):
                at = (seq_group * zones + zone) * 128
                turned[zone * 4 + seq_group] = source[:, at : at + 128].T
        copy = pltpu.make_async_copy(turned, target, load_sem.at[4])
        copy.start()
        return copy

    pump()
    store = turn(lhs, n1_turned)
    pump()
    second.send()
    attend(0)
    pump()
    attend(1)
    pump()
    third.send()
    attend(2)
    dy.forward()
    pump()
    attend(3)
    pump()
    dy.arrive()
    load_dy = pltpu.make_async_copy(dy_full, dy_all, load_sem.at[0])
    load_dy.start()

    out.arrive()
    load_out = pltpu.make_async_copy(out_full, out_w, load_sem.at[2])
    load_out.start()
    load_out.wait()

    def out_piece(seq, column):
        part = pl.ds(pl.multiple_of(seq * rows, rows), rows)
        weight = out_w[:, :, column]
        return dot(mixed_ref[part, :], weight.reshape(-1, weight.shape[-1]))

    middle_ref[...] = hidden_ref[...].astype(F32)
    scatter_sum(here, out_piece, middle_ref, give, got, pair, far_got, (ss, sr), width, 512)
    norm_rows(middle_ref, mlp_gain_ref, own_rows.at[1])
    n2.send()
    store.wait()
    load_dy.wait()
    store = turn(dy_all, dy_turned)
    pump()
    n2.forward()
    n2.arrive()
    load_lhs = pltpu.make_async_copy(n2_full, lhs, load_sem.at[3])
    load_lhs.start()
    pump()
    down.arrive()
    first.arrive()
    load_lhs.wait()

    def feed(gather, begin, count):
        tiles = count // 256
        spot = begin // 256

        def body(gate_w, up_w, down_w, act_ref, gate_grad, up_grad):
            gate_tile = gate_w[...].reshape(width, 256)
            up_tile = up_w[...].reshape(width, 256)
            down_tile = down_w[...]

            @pl.loop(0, 4)
            def _(index):
                part = pl.ds(pl.multiple_of(index * rows, rows), rows)
                gate = dot(lhs[part, :], gate_tile)
                up = dot(lhs[part, :], up_tile)
                act_grad = contract_cols(dy_all[part, :], down_tile)
                sigmoid = jax.nn.sigmoid(gate)
                silu = gate * sigmoid
                act_ref[part, :] = (silu * up).astype(BF)
                gate_grad[part, :] = (
                    act_grad * up * sigmoid * (1.0 + gate * (1.0 - sigmoid))
                ).astype(BF)
                up_grad[part, :] = (act_grad * silu).astype(BF)

        block = gather.whole.shape[:-1] + (256,)
        grads = first_pair if begin < chunk else second_pair
        first_spot = 0 if begin < chunk + 1 else 2 * (begin - chunk) // 256
        pltpu.emit_pipeline(
            body,
            grid=(tiles,),
            in_specs=[
                pl.BlockSpec(block, lambda t: (0, 0, t)),
                pl.BlockSpec(block, lambda t: (0, 0, t + tiles)),
                pl.BlockSpec((256, width), lambda t: (t + spot, 0)),
            ],
            out_specs=[
                pl.BlockSpec((length, 256), lambda t: (0, t + spot)),
                pl.BlockSpec((length, 256), lambda t: (0, t + first_spot)),
                pl.BlockSpec((length, 256), lambda t: (0, t + first_spot + tiles)),
            ],
        )(gather.whole, gather.whole, down_full, act_out, grads, grads)

    feed(first, 0, chunk)
    pump()
    pump()
    store.wait()
    store = turn(lhs, n2_turned)
    pump()
    second.arrive()
    feed(second, chunk, chunk - tail)
    while pending:
        pump()
    third.arrive()
    feed(third, 2 * chunk - tail, tail)
    store.wait()
    for gather in (qkv, out, first, second, third, down, n1, n2, dy):
        gather.finish()


def forward(hidden, upstream, weights, gains, tables, segment):
    size = lax.axis_size("shard")
    quarter, outer = size // 4, size // 2
    piece, width = hidden.shape
    length = piece * 4
    heads = Q_HEADS // 4
    kv_heads = KV_HEADS // 4
    w_query, _, _, w_out, w_gate, _, w_down = weights
    own = w_query.shape[0]
    qkv_width = (heads + 2 * kv_heads) * HEAD_DIM
    units = w_down.shape[0] // 4 * size

    def shape(*dims, kind=BF):
        return jax.ShapeDtypeStruct(dims, kind)

    results = [
        shape(size, own, qkv_width),
        shape(quarter, *w_out.shape),
        shape(size, own, units),
        shape(size, own, units),
        shape(units, width),
        shape(length, width),
        shape(length, width),
        shape(length, width),
        shape(width // 128, 128, length),
        shape(width // 128, 128, length),
        shape(width // 128, 128, length),
        shape(length, units),
        shape(length, units),
        shape(length, units),
        shape(heads + kv_heads, length, HEAD_DIM, kind=F32),
        shape(heads + 2 * kv_heads, length, HEAD_DIM),
        shape(length, heads * HEAD_DIM),
        shape(length, 128, kind=F32),
        shape(piece, width, kind=F32),
    ]
    dma = pltpu.SemaphoreType.DMA
    return pl.pallas_call(
        functools.partial(forward_kernel, size),
        out_shape=results,
        in_specs=[VMEM] + [ANY] * 8 + [VMEM] * 8,
        out_specs=[ANY] * 14 + [VMEM] * 5,
        scratch_shapes=[
            pltpu.VMEM((length, width), BF),
            pltpu.VMEM((length, width), BF),
            pltpu.VMEM((width // 128, 128, length), BF),
            pltpu.VMEM((size, own, qkv_width), BF),
            pltpu.VMEM((quarter,) + w_out.shape, BF),
            pltpu.VMEM((own, qkv_width), BF),
            pltpu.VMEM(w_gate.shape, BF),
            pltpu.VMEM(w_gate.shape, BF),
            pltpu.VMEM((own, units), BF),
            pltpu.VMEM((own, units), BF),
            pltpu.VMEM((2, piece, width), BF),
            pltpu.VMEM((2, piece, width), BF),
            pltpu.VMEM((2, piece, width), BF),
            pltpu.VMEM((piece, width), BF),
            pltpu.VMEM((piece, width), BF),
            dma((6, outer)),
            dma((6, outer)),
            dma((6, outer)),
            dma((6, outer)),
            dma((6, outer)),
            dma((6, outer)),
            dma((6,)),
            dma((3, 3)),
            dma((3, 3)),
            dma((3,)),
            dma((5,)),
            dma((3,)),
            dma((3,)),
        ],
        compiler_params=pltpu.CompilerParams(
            collective_id=0, has_side_effects=True, vmem_limit_bytes=VMEM_BYTES
        ),
        name="forward_gather",
    )(
        hidden,
        upstream,
        *weights,
        *gains,
        *tables,
        segment.reshape(length, 1),
        segment.reshape(1, length),
    )


def add_rows(target, sources, step=16):
    groups, rows, _ = target.shape

    @pl.loop(0, groups * (rows // step))
    def _(index):
        group = index // (rows // step)
        part = pl.ds(pl.multiple_of(lax.rem(index, rows // step) * step, step), step)
        total = sources[0][group, part, :].astype(F32)
        for source in sources[1:]:
            total = total + source[group, part, :].astype(F32)
        target[group, part, :] = total.astype(target.dtype)


class RowSum:
    def __init__(self, here, give, keep, near, rising, falling, stage, total, sems):
        self.here, self.give, self.keep = here, give, keep
        self.near, self.rising, self.falling = near, rising, falling
        self.stage, self.total = stage, total
        self.ys, self.yr, self.us, self.ur, self.ds, self.dr, self.load = sems
        self.last = here.outer - 1

    def across(self, place):
        return remote(
            self.give.at[place],
            self.near.at[place],
            self.ys.at[place],
            self.yr.at[place],
            self.here.twin,
        )

    def up(self, place):
        peer = self.here.outer_peer(self.here.place + 1)
        return remote(
            self.keep.at[place], self.rising.at[place], self.us.at[place], self.ur.at[place], peer
        )

    def down(self, place):
        peer = self.here.outer_peer(self.here.place - 1)
        return remote(
            self.keep.at[place], self.falling.at[place], self.ds.at[place], self.dr.at[place], peer
        )

    def arrived(self, slot, send, receive):
        remote(slot, slot, send, receive, self.here.twin).wait_recv()

    def compute(self, left, right, tiles, zones, send=True):
        here = self.here
        own = self.give.shape[2]
        per = 128 // (2 * own)
        width = self.give.shape[3]
        step = 256
        for group in range(zones):
            spots = tiles(group)

            @pl.loop(0, width // step)
            def _(index):
                lane = pl.ds(pl.multiple_of(index * step, step), step)
                terms = dot(left(group), right(lane))
                for spot, (zone, seq_group) in enumerate(spots):
                    for sub in range(per):
                        at = spot * 128 + sub * 2 * own
                        even, odd = terms[at : at + own], terms[at + own : at + 2 * own]
                        place = zone * per + sub
                        mine = jnp.where(here.half == 0, even, odd).astype(BF)
                        theirs = jnp.where(here.half == 0, odd, even).astype(BF)
                        self.keep[place, seq_group, :, lane] = mine
                        self.give[place, seq_group, :, lane] = theirs

            for zone in sorted({zone for zone, _ in spots}) if send else ():
                for sub in range(per):
                    self.across(zone * per + sub).start()

    def fold(self, distance):
        here = self.here
        above = here.place + distance
        below = here.place - distance

        def merge(place, line, receive, first):
            near = pltpu.make_async_copy(self.near.at[place], self.stage.at[0], self.load.at[0])
            self.arrived(self.near.at[place], self.ys.at[place], self.yr.at[place])
            near.start()

            @pl.when(first)
            def _():
                near.wait()
                add_rows(self.keep.at[place], [self.keep.at[place], self.stage.at[0]])

            @pl.when(jnp.logical_not(first))
            def _():
                self.arrived(line.at[place], self.us.at[0], receive.at[place])
                far = pltpu.make_async_copy(line.at[place], self.stage.at[1], self.load.at[1])
                far.start()
                near.wait()
                far.wait()
                add_rows(
                    self.keep.at[place], [self.keep.at[place], self.stage.at[0], self.stage.at[1]]
                )

        @pl.when(above <= self.last)
        def _():
            merge(above, self.rising, self.ur, here.place == 0)
            self.up(above).start()

        @pl.when(below >= 0)
        def _():
            merge(below, self.falling, self.dr, here.place == self.last)
            self.down(below).start()

    def finish(self):
        here = self.here
        place = here.place
        self.arrived(self.near.at[place], self.ys.at[place], self.yr.at[place])
        keep = self.keep.at[place]
        near = pltpu.make_async_copy(self.near.at[place], self.stage.at[0], self.load.at[0])
        low = pltpu.make_async_copy(self.rising.at[place], self.stage.at[1], self.load.at[1])
        high = pltpu.make_async_copy(self.falling.at[place], self.stage.at[1], self.load.at[1])
        near.start()

        @pl.when(place > 0)
        def _():
            self.arrived(self.rising.at[place], self.us.at[0], self.ur.at[place])
            low.start()
            low.wait()

        @pl.when(place == 0)
        def _():
            self.arrived(self.falling.at[place], self.ds.at[0], self.dr.at[place])
            high.start()
            high.wait()

        near.wait()

        @pl.when((place > 0) & (place < self.last))
        def _():
            add_rows(keep, [keep, self.stage.at[0], self.stage.at[1]])
            self.arrived(self.falling.at[place], self.ds.at[0], self.dr.at[place])
            high.start()
            high.wait()
            add_rows(self.total, [keep, self.stage.at[1]])

        @pl.when((place == 0) | (place == self.last))
        def _():
            add_rows(self.total, [keep, self.stage.at[0], self.stage.at[1]])

    def sent(self):
        for place in range(self.here.outer):
            self.across(place).wait_send()

    def settle(self):
        here = self.here
        for place in range(here.outer):

            @pl.when(place > here.place)
            def _():
                self.up(place).wait_send()

            @pl.when(place < here.place)
            def _():
                self.down(place).wait_send()


class LineSum:
    def __init__(self, here, terms, rising, falling, stage, sems):
        self.here, self.terms, self.stage = here, terms, stage
        self.rising, self.falling = rising, falling
        self.us, self.ur, self.ds, self.dr, self.load = sems
        self.last = here.outer - 1

    def up(self, place):
        peer = self.here.outer_peer(self.here.place + 1)
        return remote(
            self.terms.at[place], self.rising.at[place], self.us.at[place], self.ur.at[place], peer
        )

    def down(self, place):
        peer = self.here.outer_peer(self.here.place - 1)
        return remote(
            self.terms.at[place], self.falling.at[place], self.ds.at[place], self.dr.at[place], peer
        )

    def merge(self, place, line, receive):
        slot = line.at[place]
        remote(slot, slot, self.us.at[0], receive.at[place], self.here.twin).wait_recv()
        copy = pltpu.make_async_copy(slot, self.stage.at[0], self.load.at[0])
        copy.start()
        copy.wait()
        add_rows(self.terms.at[place], [self.terms.at[place], self.stage.at[0]])

    def fold(self, distance):
        here = self.here
        above = here.place + distance
        below = here.place - distance

        @pl.when(above <= self.last)
        def _():
            @pl.when(here.place > 0)
            def _():
                self.merge(above, self.rising, self.ur)

            self.up(above).start()

        @pl.when(below >= 0)
        def _():
            @pl.when(here.place < self.last)
            def _():
                self.merge(below, self.falling, self.dr)

            self.down(below).start()

    def gather(self):
        place = self.here.place

        @pl.when(place > 0)
        def _():
            self.merge(place, self.rising, self.ur)

        @pl.when(place < self.last)
        def _():
            self.merge(place, self.falling, self.dr)

    def settle(self):
        here = self.here
        for place in range(here.outer):

            @pl.when(place > here.place)
            def _():
                self.up(place).wait_send()

            @pl.when(place < here.place)
            def _():
                self.down(place).wait_send()


class LineFirstSum(RowSum):
    def __init__(self, here, give, keep, near, lines, stage, total, sems, twin_sems):
        self.here, self.give, self.keep = here, give, keep
        self.near, self.stage, self.total = near, stage, total
        self.ys, self.yr, self.load = sems[0], sems[1], sems[6]
        self.lines = [
            LineSum(here, terms, rising, falling, stage, kinds[2:])
            for terms, (rising, falling), kinds in (
                (give, lines[0], twin_sems),
                (keep, lines[1], sems),
            )
        ]

    def fold(self, distance):
        for line in self.lines:
            line.fold(distance)

    def pass_on(self):
        self.lines[0].gather()
        self.across(self.here.place).start()
        self.lines[1].gather()

    def finish(self):
        place = self.here.place
        self.arrived(self.near.at[place], self.ys.at[place], self.yr.at[place])
        near = pltpu.make_async_copy(self.near.at[place], self.stage.at[0], self.load.at[0])
        near.start()
        near.wait()
        add_rows(self.total, [self.keep.at[place], self.stage.at[0]])

    def sent(self):
        self.across(self.here.place).wait_send()

    def settle(self):
        for line in self.lines:
            line.settle()


class RowSpread:
    def __init__(self, here, rows, whole, sems):
        self.here, self.rows, self.whole = here, rows, whole
        self.send_sems, self.recv_sems, self.local = sems

    def copy(self, amount):
        seq = lax.rem(self.here.seq + amount, 4)
        return remote(
            self.rows.at[seq],
            self.whole.at[self.here.seq],
            self.send_sems.at[amount - 1],
            self.recv_sems.at[amount - 1],
            {"seq": seq},
        )

    def keep(self):
        seq = self.here.seq
        return pltpu.make_async_copy(self.rows.at[seq], self.whole.at[seq], self.local)

    def send(self):
        for amount in (2, 3, 1):
            self.copy(amount).start()
        self.keep().start()

    def arrive(self):
        for amount in (1, 2, 3):
            self.copy(amount).wait_recv()
        self.keep().wait()

    def finish(self):
        for amount in (1, 2, 3):
            self.copy(amount).wait_send()


class TokenSum:
    def __init__(self, here, part, got, pair, far_got, base, sems):
        self.here, self.part, self.got, self.pair = here, part, got, pair
        self.far_got, self.base = far_got, base
        self.send_sems, self.recv_sems = sems
        self.rows = part.shape[0] // 4

    def piece(self, seq):
        return pl.ds(pl.multiple_of(seq * self.rows, self.rows), self.rows)

    def to_mate(self, index):
        here = self.here
        chip = here.chip if index else 1 - here.chip
        seq = chip * 2 + 1 - here.core
        return remote(
            self.part.at[self.piece(seq), :],
            self.got.at[index],
            self.send_sems.at[index],
            self.recv_sems.at[index],
            here.mate,
        )

    def to_far(self):
        return remote(
            self.pair, self.far_got, self.send_sems.at[2], self.recv_sems.at[2], self.here.far
        )

    def send(self):
        self.to_mate(0).start()
        self.to_mate(1).start()

    def loop(self, body):
        @pl.loop(0, self.rows // 32)
        def _(index):
            body(index * 32)

    def pass_on(self):
        self.to_mate(0).wait_recv()
        begin = self.here.far_seq * self.rows

        def body(at):
            part = pl.ds(pl.multiple_of(at, 32), 32)
            source = pl.ds(pl.multiple_of(begin + at, 32), 32)
            total = self.part[source, :].astype(F32) + self.got[0, part, :].astype(F32)
            self.pair[part, :] = total.astype(BF)

        self.loop(body)
        self.to_far().start()

    def add_near(self):
        self.to_mate(1).wait_recv()
        begin = self.here.seq * self.rows

        def body(at):
            part = pl.ds(pl.multiple_of(at, 32), 32)
            source = pl.ds(pl.multiple_of(begin + at, 32), 32)
            self.base[part, :] += self.part[source, :].astype(F32) + self.got[1, part, :].astype(F32)

        self.loop(body)
        self.to_mate(0).wait_send()
        self.to_mate(1).wait_send()

    def add_far(self):
        self.to_far().wait_recv()

        def body(at):
            part = pl.ds(pl.multiple_of(at, 32), 32)
            self.base[part, :] += self.far_got[part, :].astype(F32)

        self.loop(body)
        self.to_far().wait_send()


class GainSum:
    def __init__(self, here, parts, arrived, sems):
        self.here, self.parts, self.arrived = here, parts, arrived
        self.send_sems, self.recv_sems = sems
        self.peers = [here.mate, here.far, here.twin] + here.line_peers()

    def copy(self, index):
        return remote(
            self.parts.at[index],
            self.arrived.at[index],
            self.send_sems.at[index],
            self.recv_sems.at[index],
            self.peers[index],
        )

    def start(self):
        self.copy(0).start()

    def hop(self, index):
        self.copy(index).wait()
        self.parts[index + 1] = self.parts[index] + self.arrived[index]
        if index + 1 < len(self.peers):
            self.copy(index + 1).start()


PLAN = (
    (("down", 3),),
    (("down", 2),),
    (),
    (),
    (("down", 1),),
    (),
    (("first", 3), ("first", 2),),
    (),
    (("first", 1),),
    (),
    (("out", 3), ("out", 2),),
    (),
    (("second", 3), ("second", 2), ("first", "finish"),),
    (("down", "pass"),),
    (("out", 1), ("qkv", 3), ("qkv", 2), ("second", 1),),
    (("out", "pass"), ("qkv", 1),),
    (("second", "finish"), ("out", "finish"), ("down", "finish"), ("qkv", "finish"),),
)


def backward_kernel(
    size,
    n1_hbm,
    dy_hbm,
    n2_hbm,
    act_hbm,
    first_hbm,
    second_hbm,
    proj_hbm,
    heads_ref,
    mixed_ref,
    lse_ref,
    middle_hbm,
    hidden_hbm,
    dy_own,
    qkv_full,
    out_full,
    first_full,
    second_full,
    down_full,
    attn_gain_ref,
    mlp_gain_ref,
    query_gain_ref,
    key_gain_ref,
    cos_ref,
    sin_ref,
    seg_col_ref,
    seg_row_ref,
    grad_in,
    gains_out,
    grad_out,
    grad_query,
    grad_key,
    grad_value,
    hidden_out,
    grad_gate,
    grad_up,
    grad_down,
    down_rows,
    first_rows,
    second_rows,
    qkv_rows,
    da_hbm,
    near_mlp,
    rising_mlp,
    falling_mlp,
    rising_twin,
    falling_twin,
    near_qkv,
    rising_qkv,
    falling_qkv,
    near_out,
    rising_out,
    falling_out,
    rising_out_twin,
    falling_out_twin,
    lhs,
    turned,
    first_r,
    second_r,
    give,
    keep,
    give_out,
    keep_out,
    stage,
    stage_out,
    dout_ref,
    da_own,
    got,
    far_got,
    pair,
    middle_grad,
    proj_buf,
    lse_t,
    dk_sum,
    dv_sum,
    gain_rows,
    gain_got,
    wide_rows,
    ys,
    yr,
    us,
    ur,
    ds,
    dr,
    fold_load,
    spread_s,
    spread_r,
    spread_l,
    sum_s,
    sum_r,
    ts,
    tr,
    token_local,
    gs,
    gr,
    load_sem,
    credit,
):
    here = Place(size)
    length, width = lhs.shape
    rows = length // 4
    units = first_r.shape[1]
    chunk = units // 2
    ff_part = units // size
    heads = mixed_ref.shape[1] // HEAD_DIM
    kv_heads = heads // 2
    qkv_width = qkv_full.shape[2]
    last = here.outer - 1
    zones = width // 512
    scale = HEAD_DIM ** (-0.5)

    def load(source, target, index):
        copy = pltpu.make_async_copy(source, target, load_sem.at[index])
        copy.start()
        return copy

    def sems(index):
        return tuple(kind.at[index] for kind in (ys, yr, us, ur, ds, dr, fold_load))

    down = LineFirstSum(
        here,
        give.at[2],
        keep.at[0],
        near_mlp.at[0],
        ((rising_twin, falling_twin), (rising_mlp.at[0], falling_mlp.at[0])),
        stage,
        keep.at[0, here.place],
        sems(0),
        sems(5),
    )
    first, second = [
        RowSum(
            here,
            give.at[2 - index],
            keep.at[index],
            near_mlp.at[index],
            rising_mlp.at[index],
            falling_mlp.at[index],
            stage,
            keep.at[index, here.place],
            sems(index),
        )
        for index in (1, 2)
    ]
    thin = slice(0, qkv_width)
    qkv = RowSum(
        here,
        give.at[1, :, :, :, thin],
        second_r.at[:, :, :, thin],
        near_qkv,
        rising_qkv,
        falling_qkv,
        stage.at[:, :, :, thin],
        second_r.at[here.place, :, :, thin],
        sems(3),
    )
    out = LineFirstSum(
        here,
        give_out,
        keep_out,
        near_out,
        ((rising_out_twin, falling_out_twin), (rising_out, falling_out)),
        stage_out,
        grad_out,
        sems(4),
        sems(6),
    )

    def spread(index, job, whole):
        return RowSpread(
            here, job.total, whole, (spread_s.at[index], spread_r.at[index], spread_l.at[index])
        )

    spread_down = spread(0, down, down_rows)
    spread_first = spread(1, first, first_rows)
    spread_second = spread(2, second, second_rows)
    spread_qkv = spread(3, qkv, qkv_rows)

    def token_sum(index, base):
        return TokenSum(
            here, lhs, got, pair, far_got, base, (sum_s.at[index], sum_r.at[index])
        )

    sum_mlp = token_sum(0, middle_grad)
    sum_hidden = token_sum(1, grad_in)
    sum_attn = token_sum(2, grad_in)
    da = TokenGather(here, da_own, da_hbm, (ts, tr, token_local.at[0]))

    def model_tiles(group):
        return [(group, seq_group) for seq_group in range(4)]

    def first_columns(lane):
        return first_r[:, lane]

    def model_left(group):
        return turned[group * 4 : group * 4 + 4].reshape(512, length)

    jobs = {"down": down, "first": first, "second": second, "out": out, "qkv": qkv}
    spreads = {
        "down": spread_down,
        "first": spread_first,
        "second": spread_second,
        "qkv": spread_qkv,
    }

    ended = []

    def advance(steps):
        for name, step in steps:
            job = jobs[name]
            if step == "pass":
                job.pass_on()
            elif step == "finish":
                job.finish()
                if name in spreads:
                    spreads[name].send()
                    ended.append(name)
            else:
                for distance in range(last * step // 3, last * (step - 1) // 3, -1):
                    job.fold(distance)

    load_turned = load(dy_hbm, turned, 0)
    load_act = load(act_hbm, first_r, 1)
    load_middle = load(middle_hbm, grad_in, 2)
    load_dy = load(dy_own, da_own, 4)
    load_second = load(second_hbm, second_r, 3)
    here.greet(wide=True)
    load_turned.wait()
    load_act.wait()
    down.compute(model_left, first_columns, model_tiles, zones, send=False)
    advance(PLAN[0])
    load_turned = load(n2_hbm, turned, 0)
    load_first = load(first_hbm, first_r, 1)
    load_first.wait()
    load_second.wait()

    own = width // size
    slabs = 256 // own

    def dn2_body(first_w, second_w):
        lane = pl.ds(pl.multiple_of(pl.program_id(0) * 256, 256), 256)
        first_tile = first_w[...].reshape(256, units)
        second_tile = second_w[...].reshape(256, units)

        @pl.loop(0, 4)
        def _(index):
            part = pl.ds(pl.multiple_of(index * rows, rows), rows)
            total = contract_cols(first_r[part, :], first_tile)
            blocks = pl.ds(index * (here.outer // 4), here.outer // 4)
            second_rows = second_r[blocks].reshape(rows, units)
            total = total + contract_cols(second_rows, second_tile)
            lhs[part, lane] = total.astype(BF)

    slab = pl.BlockSpec((slabs, own, units), lambda t: (t, 0, 0))
    pltpu.emit_pipeline(dn2_body, grid=(width // 256,), in_specs=[slab, slab])(
        first_full, second_full
    )
    sum_mlp.send()
    middle_grad[...] = jnp.zeros_like(middle_grad)
    load_turned.wait()
    advance(PLAN[1])
    sum_mlp.pass_on()
    sum_mlp.add_near()
    first.compute(model_left, first_columns, model_tiles, zones)
    load_act = load(act_hbm, first_r, 1)
    advance(PLAN[2])
    sum_mlp.add_far()

    load_middle.wait()
    load_dy.wait()
    gain_rows[0] = jnp.zeros_like(gain_rows[0])
    narrow = 16

    @pl.loop(0, rows // narrow)
    def _(index):
        part = pl.ds(pl.multiple_of(index * narrow, narrow), narrow)
        values = grad_in[part, :]
        scales = lax.rsqrt(jnp.mean(values * values, axis=-1, keepdims=True) + EPSILON)
        normed = values * scales
        update = middle_grad[part, :]
        gain_rows[0, 1:2, :] += jnp.sum(update * normed, axis=0, keepdims=True)
        upper = update * mlp_gain_ref[...]
        inner = jnp.mean(upper * normed, axis=-1, keepdims=True)
        grad = da_own[part, :].astype(F32) + scales * (upper - normed * inner)
        middle_grad[part, :] = grad
        da_own[part, :] = grad.astype(BF)

    da.send()
    advance(PLAN[3])
    second.compute(
        model_left, lambda lane: second_r[:, :, :, lane].reshape(length, -1), model_tiles, zones
    )
    advance(PLAN[4])

    def hidden_body(weight):
        lane = pl.ds(pl.multiple_of(pl.program_id(0) * 256, 256), 256)
        tile = weight[...]

        @pl.loop(0, 4)
        def _(index):
            part = pl.ds(pl.multiple_of(index * rows, rows), rows)
            lhs[part, lane] = dot(first_r[part, :], tile).astype(BF)

    load_act.wait()
    pltpu.emit_pipeline(
        hidden_body,
        grid=(width // 256,),
        in_specs=[pl.BlockSpec((units, 256), lambda t: (0, t))],
    )(down_full)
    da.mate_arrived()
    sum_hidden.send()
    da.forward()
    advance(PLAN[5])
    sum_hidden.pass_on()
    sum_hidden.add_near()
    advance(PLAN[6])
    da.rest_arrived()
    da.finish()
    load_lhs = load(da_hbm, lhs, 0)
    load_own = load(hidden_hbm, da_own, 2)
    load_lhs.wait()

    def dout_body(weight):
        lane = pl.ds(pl.multiple_of(pl.program_id(0) * 256, 256), 256)
        tile = weight[...].reshape(256, width)

        @pl.loop(0, 4)
        def _(index):
            part = pl.ds(pl.multiple_of(index * rows, rows), rows)
            dout_ref[part, lane] = contract_cols(lhs[part, :], tile).astype(BF)

    out_blocks, out_rows = out_full.shape[:2]
    pltpu.emit_pipeline(
        dout_body,
        grid=(out_blocks * out_rows // 256,),
        in_specs=[pl.BlockSpec((256 // out_rows, out_rows, width), lambda t: (t, 0, 0))],
    )(out_full)

    for head in range(heads):
        turned[head] = mixed_ref[:, head * HEAD_DIM : (head + 1) * HEAD_DIM].T
    out.compute(
        lambda group: turned[0:heads].reshape(heads * HEAD_DIM, length),
        lambda lane: lhs[:, lane],
        lambda group: [(zone, 0) for zone in range(heads)],
        1,
        send=False,
    )
    load_turned = load(n1_hbm, turned, 0)
    sum_hidden.add_far()
    for index, peer in enumerate((here.mate, here.far)):
        pl.semaphore_signal(credit.at[index], inc=1, device_id=peer, device_id_type=MESH)

    @pl.loop(0, rows // 32)
    def _(index):
        part = pl.ds(pl.multiple_of(index * 32, 32), 32)
        pair[part, :] = grad_in[part, :].astype(BF)

    store_hidden = load(pair, hidden_out, 1)
    advance(PLAN[7])

    lse_t[...] = lse_ref[...].T[0:8]
    def through_norm(grad, head, part, gain_ref, gain_row):
        proj = proj_buf[part, :]
        scales = lax.rsqrt(jnp.mean(proj * proj, axis=-1, keepdims=True) + EPSILON)
        normed = proj * scales
        grad = grad.astype(F32)
        upper = grad * cos_ref[part, :] - pltpu.roll(grad, HEAD_DIM // 2, 1) * sin_ref[part, :]
        gain_rows[0, 2:3, gain_row * HEAD_DIM : (gain_row + 1) * HEAD_DIM] += jnp.sum(
            upper * normed, axis=0, keepdims=True
        )
        upper = upper * gain_ref[...]
        inner = jnp.mean(upper * normed, axis=-1, keepdims=True)
        result = (scales * (upper - normed * inner)).astype(BF)
        first_r[part, head * HEAD_DIM : (head + 1) * HEAD_DIM] = result

    for head in range(heads):
        pair_head = head // 2
        load_proj = load(proj_hbm.at[head], proj_buf, 4)
        if head % 2 == 0:
            dk_sum[...] = jnp.zeros_like(dk_sum)
            dv_sum[...] = jnp.zeros_like(dv_sum)
        load_proj.wait()
        for block in range(4):
            end = (block + 1) * rows
            part = pl.ds(block * rows, rows)
            queries = heads_ref[head, part, :]
            keys = heads_ref[heads + pair_head, 0:end, :]
            values = heads_ref[heads + kv_heads + pair_head, 0:end, :]
            out_grad = dout_ref[part, head * HEAD_DIM : (head + 1) * HEAD_DIM]
            scores = contract_cols(keys, queries) * scale
            key_place = lax.broadcasted_iota(jnp.int32, (end, rows), 0)
            query_place = lax.broadcasted_iota(jnp.int32, (end, rows), 1) + block * rows
            allowed = (seg_col_ref[0:end, :] == seg_row_ref[:, part]) & (key_place <= query_place)
            weights = jnp.exp(
                jnp.where(allowed, scores, NEGATIVE) - lse_t[head : head + 1, part]
            )
            weight_grad = contract_cols(values, out_grad)
            inner = jnp.sum(weights * weight_grad, axis=0, keepdims=True)
            score_grad = (weights * (weight_grad - inner)).astype(BF)
            dk_sum[0:end, :] += dot(score_grad, queries) * scale
            dv_sum[0:end, :] += dot(weights.astype(BF), out_grad)
            query_grad = (contract_rows(score_grad, keys) * scale).astype(BF)
            through_norm(query_grad, head, part, query_gain_ref, 0)
        if head % 2:
            key = heads + pair_head
            value_at = (heads + kv_heads + pair_head) * HEAD_DIM
            load(proj_hbm.at[key], proj_buf, 4).wait()

            @pl.loop(0, 4)
            def _(index):
                part = pl.ds(pl.multiple_of(index * rows, rows), rows)
                through_norm(dk_sum[part, :].astype(BF), key, part, key_gain_ref, 1)
                first_r[part, value_at : value_at + HEAD_DIM] = dv_sum[part, :].astype(BF)

        advance(PLAN[8 + head])

    load_turned.wait()
    first.sent()
    store_hidden.wait()
    proj_grads = first_r.at[:, 0:qkv_width]
    qkv.compute(model_left, first_columns, model_tiles, zones)
    advance(PLAN[12])

    def dn1_body(weight):
        lane = pl.ds(pl.multiple_of(pl.program_id(0) * 256, 256), 256)
        tile = weight[...].reshape(256, qkv_width)

        @pl.loop(0, 4)
        def _(index):
            part = pl.ds(pl.multiple_of(index * rows, rows), rows)
            lhs[part, lane] = contract_cols(proj_grads[part, :], tile).astype(BF)

    pltpu.emit_pipeline(
        dn1_body,
        grid=(width // 256,),
        in_specs=[pl.BlockSpec((slabs, own, qkv_width), lambda t: (t, 0, 0))],
    )(qkv_full)
    grad_in[...] = jnp.zeros_like(grad_in)
    pl.semaphore_wait(credit.at[0], 1)
    pl.semaphore_wait(credit.at[1], 1)
    sum_attn.send()
    advance(PLAN[13])
    sum_attn.pass_on()
    sum_attn.add_near()
    advance(PLAN[14])
    sum_attn.add_far()
    load_own.wait()

    @pl.loop(0, rows // narrow)
    def _(index):
        part = pl.ds(pl.multiple_of(index * narrow, narrow), narrow)
        values = da_own[part, :].astype(F32)
        scales = lax.rsqrt(jnp.mean(values * values, axis=-1, keepdims=True) + EPSILON)
        normed = values * scales
        update = grad_in[part, :]
        gain_rows[0, 0:1, :] += jnp.sum(update * normed, axis=0, keepdims=True)
        upper = update * attn_gain_ref[...]
        inner = jnp.mean(upper * normed, axis=-1, keepdims=True)
        grad_in[part, :] = middle_grad[part, :] + scales * (upper - normed * inner)

    gain_sum = GainSum(here, gain_rows, gain_got, (gs, gr))
    gain_sum.start()
    advance(PLAN[15])
    hops = list(range(len(gain_sum.peers)))
    slab = wide_rows.shape[0]

    def place_rows(read, target, lane):
        width_here = lane.stop - lane.start

        for index in range(target.shape[0] // slab):
            part = slice(index * slab, (index + 1) * slab)
            wide_rows[:, 0:width_here] = read(part)
            load(wide_rows.at[:, 0:width_here], target.at[part, lane], 3).wait()

    def place_units(read, target, begin, blocks):
        def ordered(part):
            values = [read(seq, part).astype(F32) for seq in range(4)]
            return jnp.concatenate(
                [
                    values[seq][:, block * ff_part : (block + 1) * ff_part]
                    for block in range(blocks)
                    for seq in range(4)
                ],
                axis=1,
            )

        lane = slice(begin * 4 * ff_part, (begin + blocks) * 4 * ff_part)
        place_rows(ordered, target, lane)

    most, tail = chunk - 256, 256

    def place(name):
        spreads[name].arrive()
        if name == "down":
            load(down_rows, stage.at[0], 1).wait()
            place_units(lambda seq, part: stage[0, seq, part, 0:chunk], grad_down, 0, size // 2)
            place_units(
                lambda seq, part: stage[0, seq, part, chunk:units], grad_down, size // 2, size // 2
            )
        elif name == "first":
            load(first_rows, stage.at[0], 1).wait()
            for side, target in enumerate((grad_gate, grad_up)):
                place_units(
                    lambda seq, part: stage[0, seq, part, side * chunk : (side + 1) * chunk],
                    target,
                    0,
                    size // 2,
                )
        elif name == "second":
            load(second_rows, stage.at[0], 1).wait()
            for side, target in enumerate((grad_gate, grad_up)):

                def read(seq, part):
                    at = 2 * most + side * tail
                    return jnp.concatenate(
                        [
                            stage[0, seq, part, side * most : (side + 1) * most],
                            stage[0, seq, part, at : at + tail],
                        ],
                        axis=1,
                    )

                place_units(read, target, size // 2, size // 2)
        else:
            load(qkv_rows, stage.at[0, :, :, thin], 1).wait()
            at = 0
            for target, count in (
                (grad_query, heads * HEAD_DIM),
                (grad_key, kv_heads * HEAD_DIM),
                (grad_value, kv_heads * HEAD_DIM),
            ):

                def side_by_side(part):
                    return jnp.concatenate(
                        [stage[0, seq, part, at : at + count].astype(F32) for seq in range(4)],
                        axis=1,
                    )

                place_rows(side_by_side, target, slice(0, 4 * count))
                at += count

    for index, (name, step) in enumerate(PLAN[16]):
        advance([(name, step)])
        if hops:
            gain_sum.hop(hops.pop(0))
        while ended and ended[0] not in [job for job, _ in PLAN[16][max(0, index - 1) : index + 1]]:
            place(ended.pop(0))
    for index in hops:
        gain_sum.hop(index)
    gains_out[...] = gain_rows[gain_rows.shape[0] - 1]
    for name in ended:
        place(name)
    for job in (down, second, out, qkv):
        job.sent()
    for job in jobs.values():
        job.settle()
    for job in spreads.values():
        job.finish()


def backward(saved, weights, own, gains, tables, segment):
    size = lax.axis_size("shard")
    outer = size // 2
    (n1, dy, n2, act, first, second, proj, heads_all, mixed, lse, middle) = saved
    length, width = heads_all.shape[1], middle.shape[1]
    piece = length // 4
    units = act.shape[1]
    qkv_width = weights[0].shape[2]
    rows = width // (4 * size)
    q_width = mixed.shape[1]

    def shape(*dims, kind=BF):
        return jax.ShapeDtypeStruct(dims, kind)

    results = [
        shape(piece, width, kind=F32),
        shape(8, width, kind=F32),
        shape(1, rows, width, kind=F32),
        shape(rows, 4 * q_width, kind=F32),
        shape(rows, 2 * q_width, kind=F32),
        shape(rows, 2 * q_width, kind=F32),
        shape(piece, width),
        shape(rows, 4 * units, kind=F32),
        shape(rows, 4 * units, kind=F32),
        shape(rows, 4 * units, kind=F32),
        shape(4, rows, units),
        shape(4, rows, units),
        shape(4, rows, units),
        shape(4, rows, qkv_width),
        shape(length, width),
    ]
    results += [shape(3, outer, 4, rows, units)] * 3
    results += [shape(outer, 4, rows, units)] * 2
    results += [shape(outer, 4, rows, qkv_width)] * 3
    results += [shape(outer, 1, rows, width)] * 5
    dma = pltpu.SemaphoreType.DMA
    hops = 3 + outer.bit_length() - 1
    vmem = pltpu.VMEM
    return pl.pallas_call(
        functools.partial(backward_kernel, size),
        out_shape=results,
        in_specs=[ANY] * 7 + [VMEM] * 3 + [ANY] * 8 + [VMEM] * 8,
        out_specs=[VMEM] * 3 + [ANY] * (len(results) - 3),
        scratch_shapes=[
            vmem((length, width), BF),
            vmem((width // 128, 128, length), BF),
            vmem((length, units), BF),
            vmem((outer, 4, rows, units), BF),
            vmem((3, outer, 4, rows, units), BF),
            vmem((3, outer, 4, rows, units), BF),
            vmem((outer, 1, rows, width), BF),
            vmem((outer, 1, rows, width), BF),
            vmem((2, 4, rows, units), BF),
            vmem((2, 1, rows, width), BF),
            vmem((length, q_width), BF),
            vmem((piece, width), BF),
            vmem((2, piece, width), BF),
            vmem((piece, width), BF),
            vmem((piece, width), BF),
            vmem((piece, width), F32),
            vmem((length, HEAD_DIM), F32),
            vmem((8, length), F32),
            vmem((length, HEAD_DIM), F32),
            vmem((length, HEAD_DIM), F32),
            vmem((hops + 1, 8, width), F32),
            vmem((hops, 8, width), F32),
            vmem((16, 2 * units), F32),
            dma((7, outer)),
            dma((7, outer)),
            dma((7, outer)),
            dma((7, outer)),
            dma((7, outer)),
            dma((7, outer)),
            dma((7, 3)),
            dma((4, 3)),
            dma((4, 3)),
            dma((4,)),
            dma((3, 3)),
            dma((3, 3)),
            dma((3,)),
            dma((3,)),
            dma((1,)),
            dma((hops,)),
            dma((hops,)),
            dma((5,)),
            pltpu.SemaphoreType.REGULAR((2,)),
        ],
        compiler_params=pltpu.CompilerParams(
            collective_id=1, has_side_effects=True, vmem_limit_bytes=VMEM_BYTES
        ),
        name="backward_sums",
    )(
        n1,
        dy,
        n2,
        act,
        first,
        second.reshape(outer, 4, rows, units),
        proj,
        heads_all,
        mixed,
        lse,
        middle,
        *own,
        *weights,
        *gains,
        *tables,
        segment.reshape(length, 1),
        segment.reshape(1, length),
    )


def local(
    hidden_in,
    segment_ids,
    norm_attn_gain,
    w_query,
    w_key,
    w_value,
    query_gain,
    key_gain,
    w_out,
    norm_mlp_gain,
    w_gate,
    w_up,
    w_down,
    out_cotangent,
):
    length = hidden_in.shape[1] * 4
    segment = segment_ids[0]
    places = jnp.arange(length, dtype=jnp.int32)
    starts = jnp.sum((segment[None, :] < segment[:, None]).astype(jnp.int32), axis=1)
    cosine, sine = rotary_tables(places - starts)
    signs = jnp.where(jnp.arange(HEAD_DIM) < HEAD_DIM // 2, -1.0, 1.0).astype(F32)
    tables = (cosine, sine * signs)
    gains = (norm_attn_gain[None], norm_mlp_gain[None], query_gain[None], key_gain[None])
    results = forward(
        hidden_in[0],
        out_cotangent[0],
        (w_query, w_key, w_value, w_out, w_gate, w_up, w_down),
        gains,
        tables,
        segment,
    )
    (
        grad_in,
        gain_totals,
        grad_out,
        grad_query,
        grad_key,
        grad_value,
        hidden_out,
        grad_gate,
        grad_up,
        grad_down,
    ) = backward(
        results[8:],
        results[:5],
        (hidden_in[0], out_cotangent[0]),
        gains,
        tables,
        segment,
    )[:10]
    return (
        hidden_out[None],
        grad_in[None],
        gain_totals[0],
        grad_query,
        grad_key,
        grad_value,
        gain_totals[2, :HEAD_DIM],
        gain_totals[2, HEAD_DIM : 2 * HEAD_DIM],
        grad_out[0],
        gain_totals[1],
        grad_gate,
        grad_up,
        grad_down.T,
    )


def solution(mesh):
    return jax.shard_map(
        local,
        mesh=mesh,
        in_specs=(
            P("shard", "seq", None),
            P("shard", None),
            P(),
            P("shard", None),
            P("shard", None),
            P("shard", None),
            P(),
            P(),
            P("shard", None),
            P(),
            P("shard", None),
            P("shard", None),
            P("shard", None),
            P("shard", "seq", None),
        ),
        out_specs=(
            P("shard", "seq", None),
            P("shard", "seq", None),
            P(),
            P(("seq", "shard"), None),
            P(("seq", "shard"), None),
            P(("seq", "shard"), None),
            P(),
            P(),
            P(("seq", "shard"), None),
            P(),
            P(("seq", "shard"), None),
            P(("seq", "shard"), None),
            P(None, ("seq", "shard")),
        ),
        check_vma=False,
    )
```

```python
import functools

import jax
import jax.numpy as jnp
from jax import lax
from jax.experimental import pallas as pl
from jax.experimental.pallas import tpu as pltpu
from jax.sharding import PartitionSpec as P

Q_HEADS = 16
KV_HEADS = 8
HEAD_DIM = 128
EPSILON = 1e-06
ROPE_BASE = 1000000.0
NEGATIVE = -1e30
BF = jnp.bfloat16
F32 = jnp.float32
MESH = pl.DeviceIdType.MESH
ANY = pl.BlockSpec(memory_space=pl.ANY)
VMEM = pl.BlockSpec(memory_space=pltpu.VMEM)
VMEM_BYTES = 62 * 1024 * 1024


def rotary_tables(positions):
    inverse = ROPE_BASE ** (-(jnp.arange(HEAD_DIM // 2, dtype=F32) * 2.0) / HEAD_DIM)
    angles = positions.astype(F32)[:, None] * inverse[None, :]
    angles = jnp.concatenate([angles, angles], axis=-1)
    return (jnp.cos(angles), jnp.sin(angles))


def dot(left, right):
    return jnp.dot(left, right, preferred_element_type=F32)


def contract_rows(left, right):
    return lax.dot_general(left, right, (((0,), (0,)), ((), ())), preferred_element_type=F32)


def contract_cols(left, right):
    return lax.dot_general(left, right, (((1,), (1,)), ((), ())), preferred_element_type=F32)


class Place:
    def __init__(self, size):
        self.size = size
        self.outer = size // 2
        self.quarter = size // 4
        self.seq = lax.axis_index("seq")
        self.shard = lax.axis_index("shard")
        self.chip = self.seq // 2
        self.core = lax.rem(self.seq, 2)
        self.place = self.shard // 2
        self.half = lax.rem(self.shard, 2)
        self.far_seq = lax.rem(self.seq + 2, 4)
        self.mate_seq = self.chip * 2 + 1 - self.core
        self.far = {"seq": self.far_seq}
        self.mate = {"seq": self.mate_seq}
        self.twin_shard = self.place * 2 + 1 - self.half
        self.twin = {"shard": self.twin_shard}

    def outer_peer(self, place):
        return {"shard": place * 2 + self.half}

    def line_peers(self):
        peers = []
        step = 1
        while step < self.outer:
            sign = 1 - 2 * lax.rem(self.place // step, 2)
            peers.append(self.outer_peer(self.place + sign * step))
            step *= 2
        return peers

    def greet(self, wide=False):
        barrier = pltpu.get_barrier_semaphore()
        last = self.outer - 1

        def signal(peer):
            pl.semaphore_signal(barrier, inc=1, device_id=peer, device_id_type=MESH)

        peers = [self.far, self.mate, self.twin]
        if wide:
            peers += [{"seq": 3 - self.seq}] + self.line_peers()[1:]
        for peer in peers:
            signal(peer)

        @pl.when(self.place < last)
        def _():
            signal(self.outer_peer(self.place + 1))

        @pl.when(self.place > 0)
        def _():
            signal(self.outer_peer(self.place - 1))

        inner = ((self.place > 0) & (self.place < last)).astype(jnp.int32)
        pl.semaphore_wait(barrier, len(peers) + 1 + inner)


def remote(source, target, send, receive, peer):
    return pltpu.make_async_remote_copy(
        src_ref=source,
        dst_ref=target,
        send_sem=send,
        recv_sem=receive,
        device_id=peer,
        device_id_type=MESH,
    )


class LineGather:
    def __init__(self, here, own, slot, sems):
        self.here, self.own, self.slot = here, own, slot
        self.us, self.ur, self.ds, self.dr = sems
        self.last = here.outer - 1

    def up(self, distance):
        here = self.here
        slot = self.slot(here.place - distance)
        source = slot if distance else self.own
        peer = here.outer_peer(here.place + 1)
        return remote(source, slot, self.us.at[distance], self.ur.at[distance], peer)

    def down(self, distance):
        here = self.here
        slot = self.slot(here.place + distance)
        source = slot if distance else self.own
        peer = here.outer_peer(here.place - 1)
        return remote(source, slot, self.ds.at[distance], self.dr.at[distance], peer)

    def send(self):
        here = self.here

        @pl.when(here.place < self.last)
        def _():
            self.up(0).start()

        @pl.when(here.place > 0)
        def _():
            self.down(0).start()

    def step(self, distance, arrived=lambda place: None):
        here = self.here
        below = here.place - 1 - distance
        above = here.place + 1 + distance

        @pl.when(below >= 0)
        def _():
            slot = self.slot(below)
            remote(slot, slot, self.us.at[0], self.ur.at[distance], here.twin).wait_recv()

            @pl.when(here.place < self.last)
            def _():
                self.up(distance + 1).start()

            arrived(below)

        @pl.when(above <= self.last)
        def _():
            slot = self.slot(above)
            remote(slot, slot, self.ds.at[0], self.dr.at[distance], here.twin).wait_recv()

            @pl.when(here.place > 0)
            def _():
                self.down(distance + 1).start()

            arrived(above)

    def finish(self):
        here = self.here
        for distance in range(self.last):

            @pl.when((here.place - distance >= 0) & (here.place < self.last))
            def _():
                self.up(distance).wait_send()

            @pl.when((here.place + distance <= self.last) & (here.place > 0))
            def _():
                self.down(distance).wait_send()


class RowGather:
    def __init__(self, here, own, whole, sems, spot=lambda shard: shard):
        self.here, self.own, self.whole, self.spot = here, own, whole, spot
        self.ys, self.yr, self.local = sems[4:]
        self.line = LineGather(here, own, self.mine, sems[:4])

    def mine(self, place):
        return self.whole.at[self.spot(place * 2 + self.here.half)]

    def theirs(self, place):
        return self.whole.at[self.spot(place * 2 + 1 - self.here.half)]

    def keep(self):
        return pltpu.make_async_copy(self.own, self.mine(self.here.place), self.local)

    def across(self, place, own=False):
        slot = self.mine(place)
        source = self.own if own else slot
        return remote(source, slot, self.ys.at[place], self.yr.at[place], self.here.twin)

    def arrived(self, place):
        slot = self.theirs(place)
        remote(slot, slot, self.ys.at[place], self.yr.at[place], self.here.twin).wait_recv()

    def send(self):
        self.line.send()
        self.across(self.here.place, own=True).start()
        self.keep().start()

    def step(self, distance):
        self.line.step(distance, lambda place: self.across(place).start())

    def arrive(self):
        self.keep().wait()
        for place in range(self.here.outer):
            self.arrived(place)

    def finish(self):
        self.line.finish()
        for place in range(self.here.outer):
            self.across(place).wait_send()


class TwinFirstGather(RowGather):
    def __init__(self, here, own, whole, sems, twin_sems):
        super().__init__(here, own, whole, sems)
        self.lines = [
            self.line,
            LineGather(here, self.theirs(here.place), self.theirs, twin_sems[:4]),
        ]

    def twin(self):
        self.arrived(self.here.place)
        self.lines[1].send()

    def step(self, distance):
        for line in self.lines:
            line.step(distance)

    def arrive(self):
        self.keep().wait()

    def finish(self):
        for line in self.lines:
            line.finish()
        self.across(self.here.place, own=True).wait_send()


class HeadGather:
    def __init__(self, here, own, whole, sems):
        self.here, self.own, self.whole = here, own, whole
        self.us, self.zr, self.ds, _, self.ys, self.yr, self.local = sems
        self.last = here.outer - 1
        self.count = here.quarter // 2
        self.first = here.seq * self.count
        self.mine = here.place - self.first
        self.inside = (self.mine >= 0) & (self.mine < self.count)

    def slot(self, index):
        return self.whole.at[index * 2 + self.here.half]

    def keep(self):
        return pltpu.make_async_copy(self.own, self.slot(self.mine), self.local)

    def up(self, index, own=False):
        slot = self.slot(index)
        peer = self.here.outer_peer(self.here.place + 1)
        return remote(self.own if own else slot, slot, self.us.at[index], self.zr.at[index], peer)

    def down(self, index, own=False):
        slot = self.slot(index)
        peer = self.here.outer_peer(self.here.place - 1)
        return remote(self.own if own else slot, slot, self.ds.at[index], self.zr.at[index], peer)

    def across(self, index):
        slot = self.slot(index)
        return remote(slot, slot, self.ys.at[index], self.yr.at[index], self.here.twin)

    def send(self):
        @pl.when(self.inside)
        def _():
            self.keep().start()

            @pl.when(self.here.place < self.last)
            def _():
                self.up(self.mine, own=True).start()

            @pl.when(self.here.place > 0)
            def _():
                self.down(self.mine, own=True).start()

    def step(self):
        here = self.here

        @pl.when(self.inside)
        def _():
            self.keep().wait()

        for index in range(self.count):
            slot = self.slot(index)
            arrival = remote(slot, slot, self.us.at[0], self.zr.at[index], here.twin)

            @pl.when(self.mine > index)
            def _():
                arrival.wait_recv()

                @pl.when(here.place < self.last)
                def _():
                    self.up(index).start()

            @pl.when(self.mine < index)
            def _():
                arrival.wait_recv()

                @pl.when(here.place > 0)
                def _():
                    self.down(index).start()

            self.across(index).start()

    def arrive(self):
        for index in range(self.count):
            slot = self.whole.at[index * 2 + 1 - self.here.half]
            remote(
                slot, slot, self.ys.at[index], self.yr.at[index], self.here.twin
            ).wait_recv()

    def finish(self):
        here = self.here
        for index in range(self.count):

            @pl.when((self.mine >= index) & (here.place < self.last))
            def _():
                self.up(index).wait_send()

            @pl.when((self.mine <= index) & (here.place > 0))
            def _():
                self.down(index).wait_send()

            self.across(index).wait_send()


class TokenGather:
    def __init__(self, here, own, whole, sems):
        self.here, self.own, self.whole = here, own, whole
        self.send_sems, self.recv_sems, self.local = sems
        self.rows = whole.shape[0] // 4

    def slot(self, seq):
        return self.whole.at[pl.ds(pl.multiple_of(seq * self.rows, self.rows), self.rows), :]

    def keep(self):
        return pltpu.make_async_copy(self.own, self.slot(self.here.seq), self.local)

    def copy(self, index):
        here = self.here
        slot = self.slot(here.far_seq if index == 2 else here.seq)
        return remote(
            slot if index == 2 else self.own,
            slot,
            self.send_sems.at[index],
            self.recv_sems.at[index],
            here.far if index == 0 else here.mate,
        )

    def send(self):
        self.copy(0).start()
        self.copy(1).start()
        self.keep().start()

    def forward(self):
        self.copy(0).wait_recv()
        self.copy(2).start()

    def mate_arrived(self):
        self.copy(1).wait_recv()

    def rest_arrived(self):
        self.copy(2).wait_recv()
        self.keep().wait()

    def arrive(self):
        self.mate_arrived()
        self.rest_arrived()

    def finish(self):
        for index in range(3):
            self.copy(index).wait_send()


class PieceSum:
    def __init__(self, here, piece, base, give, got, pair, far_got, sems, step):
        self.here, self.piece, self.base, self.step = here, piece, base, step
        self.give, self.got, self.pair, self.far_got = give, got, pair, far_got
        self.send_sems, self.recv_sems = sems

    def to_mate(self, index):
        return remote(
            self.give.at[index],
            self.got.at[index],
            self.send_sems.at[index],
            self.recv_sems.at[index],
            self.here.mate,
        )

    def to_far(self):
        return remote(
            self.pair, self.far_got, self.send_sems.at[2], self.recv_sems.at[2], self.here.far
        )

    def columns(self, body):
        step = self.step

        @pl.loop(0, self.pair.shape[1] // step)
        def _(index):
            body(pl.ds(pl.multiple_of(index * step, step), step))

    def send(self):
        here = self.here
        for index, chip in enumerate((1 - here.chip, here.chip)):
            seq = chip * 2 + 1 - here.core

            def fill(column, index=index, seq=seq):
                self.give[index, :, column] = self.piece(seq, column).astype(BF)

            self.columns(fill)
            self.to_mate(index).start()

    def pass_on(self):
        self.to_mate(0).wait_recv()

        def fill(column):
            term = self.piece(self.here.far_seq, column) + self.got[0, :, column].astype(F32)
            self.pair[:, column] = term.astype(BF)

        self.columns(fill)
        self.to_far().start()

    def add_near(self):
        self.to_mate(1).wait_recv()

        def fill(column):
            term = self.piece(self.here.seq, column) + self.got[1, :, column].astype(F32)
            self.base[:, column] += term

        self.columns(fill)

    def add_far(self):
        self.to_far().wait_recv()

        def fill(column):
            self.base[:, column] += self.far_got[:, column].astype(F32)

        self.columns(fill)
        for copy in (self.to_mate(0), self.to_mate(1), self.to_far()):
            copy.wait_send()


FORWARD_PLAN = (
    (("down", "send"),),
    (),
    (("out", "send"),),
    (("down", 0),),
    (("down", 1), ("down", 2),),
    (("out", 0),),
    (("third", "send"),),
    (),
    (("first", "send"),),
    (),
    (("second", "send"),),
    (),
    (),
    (("first", 0),),
    (),
    (("first", 1), ("first", 2),),
    (("second", "twin"),),
    (("third", 0), ("second", 0), ("third", 1),),
    (("second", 1),),
    (),
    (("third", 2), ("second", 2),),
    (),
)


def forward_kernel(
    size,
    hidden_ref,
    dy_own,
    w_query,
    w_key,
    w_value,
    w_out,
    w_gate,
    w_up,
    w_down,
    attn_gain_ref,
    mlp_gain_ref,
    query_gain_ref,
    key_gain_ref,
    cos_ref,
    sin_ref,
    start_ref,
    qkv_full,
    out_full,
    first_full,
    second_full,
    down_full,
    n1_full,
    dy_full,
    n2_full,
    n1_turned,
    dy_turned,
    n2_turned,
    act_out,
    first_pair,
    second_pair,
    proj_ref,
    heads_ref,
    mixed_ref,
    lse_ref,
    middle_ref,
    lhs,
    dy_all,
    turned,
    qkv_w,
    out_w,
    qkv_own,
    gate_all,
    up_all,
    first_own,
    second_own,
    own_rows,
    give,
    got,
    pair,
    far_got,
    us,
    ur,
    ds,
    dr,
    ys,
    yr,
    row_local,
    ts,
    tr,
    token_local,
    load_sem,
    ss,
    sr,
):
    here = Place(size)
    last = here.outer - 1
    length, width = lhs.shape
    lse_ref[...] = jnp.zeros_like(lse_ref)
    rows = length // 4
    units = act_out.shape[1]
    chunk = units // 2
    tail = 256
    heads = mixed_ref.shape[1] // HEAD_DIM
    kv_heads = heads // 2
    ff_part = units // size

    def sems(index):
        return tuple(kind.at[index] for kind in (us, ur, ds, dr, ys, yr, row_local))

    down_rows = pl.ds(pl.multiple_of(here.seq * ff_part, ff_part), ff_part)
    qkv = RowGather(here, qkv_own, qkv_full, sems(0))
    out = HeadGather(here, w_out, out_full, sems(1))
    down = RowGather(
        here,
        w_down.at[down_rows, :],
        down_full,
        sems(2),
        lambda shard: pl.ds(pl.multiple_of(shard * ff_part, ff_part), ff_part),
    )
    first = RowGather(here, first_own, first_full, sems(3))
    cut = 2 * (chunk - tail)
    second = TwinFirstGather(
        here, second_own.at[:, 0:cut], second_full.at[:, :, 0:cut], sems(4), sems(6)
    )
    third = RowGather(
        here, second_own.at[:, cut : 2 * chunk], second_full.at[:, :, cut : 2 * chunk], sems(5)
    )
    n1 = TokenGather(here, own_rows.at[0], n1_full, (ts.at[0], tr.at[0], token_local.at[0]))
    n2 = TokenGather(here, own_rows.at[1], n2_full, (ts.at[1], tr.at[1], token_local.at[1]))
    dy = TokenGather(here, dy_own, dy_full, (ts.at[2], tr.at[2], token_local.at[2]))

    loads = []
    at = 0
    for index, (weight, count) in enumerate(((w_query, heads), (w_key, kv_heads), (w_value, kv_heads))):
        count = count * HEAD_DIM
        source = weight.at[:, pl.ds(pl.multiple_of(here.seq * count, count), count)]
        loads.append(
            pltpu.make_async_copy(source, qkv_own.at[:, at : at + count], load_sem.at[index])
        )
        at += count
    loads.append(pltpu.make_async_copy(w_gate, gate_all, load_sem.at[3]))
    loads.append(pltpu.make_async_copy(w_up, up_all, load_sem.at[4]))
    for load in loads:
        load.start()
    here.greet()
    for load in loads[:3]:
        load.wait()
    qkv.send()

    def norm_rows(source, gain_ref, target):
        @pl.loop(0, rows // 32)
        def _(index):
            part = pl.ds(pl.multiple_of(index * 32, 32), 32)
            values = source[part, :].astype(F32)
            scales = lax.rsqrt(jnp.mean(values * values, axis=-1, keepdims=True) + EPSILON)
            target[part, :] = (values * scales * gain_ref[...]).astype(BF)

    gathers = {"out": out, "down": down, "first": first, "second": second, "third": third}

    def advance(steps):
        for name, step in steps:
            gather = gathers[name]
            if step == "send":
                gather.send()
            elif step == "twin":
                gather.twin()
            elif name == "out":
                gather.step()
            else:
                for distance in range(last * step // 3, last * (step + 1) // 3):
                    gather.step(distance)

    norm_rows(hidden_ref, attn_gain_ref, own_rows.at[0])
    n1.send()
    advance(FORWARD_PLAN[0])
    for load in loads[3:]:
        load.wait()

    for seq in range(4):

        @pl.when(here.seq == seq)
        def _():
            @pl.loop(0, first_own.shape[0] // 16)
            def _(index):
                part = pl.ds(pl.multiple_of(index * 16, 16), 16)

                def gathered(source, begin):
                    pieces = [
                        source[part, (block * 4 + seq) * ff_part : (block * 4 + seq + 1) * ff_part]
                        for block in range(begin, begin + size // 2)
                    ]
                    return jnp.concatenate(pieces, axis=1)

                first_own[part, 0:chunk] = gathered(gate_all, 0)
                first_own[part, chunk : 2 * chunk] = gathered(up_all, 0)
                gate = gathered(gate_all, size // 2)
                up = gathered(up_all, size // 2)
                most = chunk - tail
                second_own[part, 0:most] = gate[:, 0:most]
                second_own[part, most : 2 * most] = up[:, 0:most]
                second_own[part, 2 * most : 2 * most + tail] = gate[:, most:]
                second_own[part, 2 * most + tail : 2 * chunk] = up[:, most:]

    advance(FORWARD_PLAN[1])
    for third_part in range(3):
        for distance in range(last * third_part // 3, last * (third_part + 1) // 3):
            qkv.step(distance)
        advance(FORWARD_PLAN[2 + third_part])
    n1.forward()
    advance(FORWARD_PLAN[5])
    n1.arrive()
    load_lhs = pltpu.make_async_copy(n1_full, lhs, load_sem.at[0])
    load_lhs.start()
    dy.send()
    advance(FORWARD_PLAN[6])
    qkv.arrive()
    load_qkv = pltpu.make_async_copy(qkv_full, qkv_w, load_sem.at[1])
    load_qkv.start()
    advance(FORWARD_PLAN[7])
    load_lhs.wait()
    load_qkv.wait()

    def project(tile):
        weight = qkv_w[:, :, tile * 256 : tile * 256 + 256].reshape(width, 256)
        gain_ref = query_gain_ref if tile < heads // 2 else key_gain_ref

        @pl.loop(0, 4)
        def _(index):
            part = pl.ds(pl.multiple_of(index * rows, rows), rows)
            both = dot(lhs[part, :], weight)
            for side in range(2):
                head = tile * 2 + side
                proj = both[:, side * HEAD_DIM : (side + 1) * HEAD_DIM]
                if head >= heads + kv_heads:
                    heads_ref[head, part, :] = proj.astype(BF)
                    continue
                proj_ref[head, part, :] = proj
                scales = lax.rsqrt(jnp.mean(proj * proj, axis=-1, keepdims=True) + EPSILON)
                gained = proj * scales * gain_ref[...]
                turned = pltpu.roll(gained, HEAD_DIM // 2, 1)
                heads_ref[head, part, :] = (
                    gained * cos_ref[part, :] + turned * sin_ref[part, :]
                ).astype(BF)

    def attend(head):
        pair_head = head // 2
        for block in range(4):
            end = (block + 1) * rows
            part = pl.ds(block * rows, rows)
            scores = contract_cols(
                heads_ref[head, part, :], heads_ref[heads + pair_head, 0:end, :]
            )
            row_place = lax.broadcasted_iota(jnp.int32, (rows, end), 0) + block * rows
            col_place = lax.broadcasted_iota(jnp.int32, (rows, end), 1)
            allowed = (col_place >= start_ref[part, :]) & (col_place <= row_place)
            raised = jnp.where(allowed, jnp.exp(scores * (HEAD_DIM ** (-0.5))), 0.0)
            sums = jnp.sum(raised, axis=-1, keepdims=True)
            mixed = dot(raised.astype(BF), heads_ref[heads + kv_heads + pair_head, 0:end, :])
            mixed = mixed * (1.0 / sums)
            mixed_ref[part, head * HEAD_DIM : (head + 1) * HEAD_DIM] = mixed.astype(BF)
            lse_ref[part, head : head + 1] = jnp.log(sums)

    tiles = (heads + 2 * kv_heads) // 2
    for tile in range(tiles):
        if tile == tiles // 2:
            advance(FORWARD_PLAN[8])
        project(tile)
    advance(FORWARD_PLAN[9])

    zones = width // 512

    def turn(source, target):
        for seq_group in range(4):
            for zone in range(zones):
                at = (seq_group * zones + zone) * 128
                turned[zone * 4 + seq_group] = source[:, at : at + 128].T
        copy = pltpu.make_async_copy(turned, target, load_sem.at[4])
        copy.start()
        return copy

    for head in range(heads):
        attend(head)
        if head == 1:
            dy.forward()
        advance(FORWARD_PLAN[10 + head])
    dy.arrive()
    load_dy = pltpu.make_async_copy(dy_full, dy_all, load_sem.at[0])
    load_dy.start()

    out.arrive()
    load_out = pltpu.make_async_copy(out_full, out_w, load_sem.at[2])
    load_out.start()
    load_out.wait()

    def out_piece(seq, column):
        part = pl.ds(pl.multiple_of(seq * rows, rows), rows)
        weight = out_w[:, :, column]
        return dot(mixed_ref[part, :], weight.reshape(-1, weight.shape[-1]))

    middle_ref[...] = hidden_ref[...].astype(F32)
    token_sum = PieceSum(
        here, out_piece, middle_ref, give, got, pair, far_got, (ss, sr), 512
    )
    token_sum.send()
    advance(FORWARD_PLAN[14])
    token_sum.pass_on()
    token_sum.add_near()
    store = turn(lhs, n1_turned)
    advance(FORWARD_PLAN[15])
    token_sum.add_far()
    norm_rows(middle_ref, mlp_gain_ref, own_rows.at[1])
    n2.send()
    advance(FORWARD_PLAN[16])
    store.wait()
    load_dy.wait()
    store = turn(dy_all, dy_turned)
    advance(FORWARD_PLAN[17])
    n2.forward()
    advance(FORWARD_PLAN[18])
    n2.arrive()
    load_lhs = pltpu.make_async_copy(n2_full, lhs, load_sem.at[3])
    load_lhs.start()
    down.arrive()
    first.arrive()
    load_lhs.wait()

    def feed(gather, begin, count):
        tiles = count // 256
        spot = begin // 256

        def body(gate_w, up_w, down_w, act_ref, gate_grad, up_grad):
            gate_tile = gate_w[...].reshape(width, 256)
            up_tile = up_w[...].reshape(width, 256)
            down_tile = down_w[...]

            @pl.loop(0, 4)
            def _(index):
                part = pl.ds(pl.multiple_of(index * rows, rows), rows)
                gate = dot(lhs[part, :], gate_tile)
                up = dot(lhs[part, :], up_tile)
                act_grad = contract_cols(dy_all[part, :], down_tile)
                sigmoid = jax.nn.sigmoid(gate)
                silu = gate * sigmoid
                act_ref[part, :] = (silu * up).astype(BF)
                gate_grad[part, :] = (
                    act_grad * up * sigmoid * (1.0 + gate * (1.0 - sigmoid))
                ).astype(BF)
                up_grad[part, :] = (act_grad * silu).astype(BF)

        block = gather.whole.shape[:-1] + (256,)
        grads = first_pair if begin < chunk else second_pair
        first_spot = 0 if begin < chunk + 1 else 2 * (begin - chunk) // 256
        pltpu.emit_pipeline(
            body,
            grid=(tiles,),
            in_specs=[
                pl.BlockSpec(block, lambda t: (0, 0, t)),
                pl.BlockSpec(block, lambda t: (0, 0, t + tiles)),
                pl.BlockSpec((256, width), lambda t: (t + spot, 0)),
            ],
            out_specs=[
                pl.BlockSpec((length, 256), lambda t: (0, t + spot)),
                pl.BlockSpec((length, 256), lambda t: (0, t + first_spot)),
                pl.BlockSpec((length, 256), lambda t: (0, t + first_spot + tiles)),
            ],
        )(gather.whole, gather.whole, down_full, act_out, grads, grads)

    feed(first, 0, chunk)
    advance(FORWARD_PLAN[19])
    store.wait()
    store = turn(lhs, n2_turned)
    advance(FORWARD_PLAN[20])
    second.arrive()
    feed(second, chunk, chunk - tail)
    advance(FORWARD_PLAN[21])
    third.arrive()
    feed(third, 2 * chunk - tail, tail)
    store.wait()
    for gather in (qkv, out, first, second, third, down, n1, n2, dy):
        gather.finish()


def forward(hidden, upstream, weights, gains, tables, starts):
    size = lax.axis_size("shard")
    quarter, outer = size // 4, size // 2
    piece, width = hidden.shape
    length = piece * 4
    heads = Q_HEADS // 4
    kv_heads = KV_HEADS // 4
    w_query, _, _, w_out, w_gate, _, w_down = weights
    own = w_query.shape[0]
    qkv_width = (heads + 2 * kv_heads) * HEAD_DIM
    units = w_down.shape[0] // 4 * size

    def shape(*dims, kind=BF):
        return jax.ShapeDtypeStruct(dims, kind)

    results = [
        shape(size, own, qkv_width),
        shape(quarter, *w_out.shape),
        shape(size, own, units),
        shape(size, own, units),
        shape(units, width),
        shape(length, width),
        shape(length, width),
        shape(length, width),
        shape(width // 128, 128, length),
        shape(width // 128, 128, length),
        shape(width // 128, 128, length),
        shape(length, units),
        shape(length, units),
        shape(length, units),
        shape(heads + kv_heads, length, HEAD_DIM, kind=F32),
        shape(heads + 2 * kv_heads, length, HEAD_DIM),
        shape(length, heads * HEAD_DIM),
        shape(length, 128, kind=F32),
        shape(piece, width, kind=F32),
    ]
    dma = pltpu.SemaphoreType.DMA
    return pl.pallas_call(
        functools.partial(forward_kernel, size),
        out_shape=results,
        in_specs=[VMEM] + [ANY] * 8 + [VMEM] * 7,
        out_specs=[ANY] * 14 + [VMEM] * 5,
        scratch_shapes=[
            pltpu.VMEM((length, width), BF),
            pltpu.VMEM((length, width), BF),
            pltpu.VMEM((width // 128, 128, length), BF),
            pltpu.VMEM((size, own, qkv_width), BF),
            pltpu.VMEM((quarter,) + w_out.shape, BF),
            pltpu.VMEM((own, qkv_width), BF),
            pltpu.VMEM(w_gate.shape, BF),
            pltpu.VMEM(w_gate.shape, BF),
            pltpu.VMEM((own, units), BF),
            pltpu.VMEM((own, units), BF),
            pltpu.VMEM((2, piece, width), BF),
            pltpu.VMEM((2, piece, width), BF),
            pltpu.VMEM((2, piece, width), BF),
            pltpu.VMEM((piece, width), BF),
            pltpu.VMEM((piece, width), BF),
            dma((7, outer)),
            dma((7, outer)),
            dma((7, outer)),
            dma((7, outer)),
            dma((7, outer)),
            dma((7, outer)),
            dma((7,)),
            dma((3, 3)),
            dma((3, 3)),
            dma((3,)),
            dma((5,)),
            dma((3,)),
            dma((3,)),
        ],
        compiler_params=pltpu.CompilerParams(
            collective_id=0, has_side_effects=True, vmem_limit_bytes=VMEM_BYTES
        ),
        name="forward_gather",
    )(
        hidden,
        upstream,
        *weights,
        *gains,
        *tables,
        starts.reshape(length, 1),
    )


def add_rows(target, sources, step=16):
    groups, rows, _ = target.shape

    @pl.loop(0, groups * (rows // step))
    def _(index):
        group = index // (rows // step)
        part = pl.ds(pl.multiple_of(lax.rem(index, rows // step) * step, step), step)
        total = sources[0][group, part, :].astype(F32)
        for source in sources[1:]:
            total = total + source[group, part, :].astype(F32)
        target[group, part, :] = total.astype(target.dtype)


class RowSum:
    def __init__(self, here, give, keep, near, rising, falling, stage, total, sems):
        self.here, self.give, self.keep = here, give, keep
        self.near, self.rising, self.falling = near, rising, falling
        self.stage, self.total = stage, total
        self.ys, self.yr, self.us, self.ur, self.ds, self.dr, self.load = sems
        self.last = here.outer - 1

    def across(self, place):
        return remote(
            self.give.at[place],
            self.near.at[place],
            self.ys.at[place],
            self.yr.at[place],
            self.here.twin,
        )

    def up(self, place):
        peer = self.here.outer_peer(self.here.place + 1)
        return remote(
            self.keep.at[place], self.rising.at[place], self.us.at[place], self.ur.at[place], peer
        )

    def down(self, place):
        peer = self.here.outer_peer(self.here.place - 1)
        return remote(
            self.keep.at[place], self.falling.at[place], self.ds.at[place], self.dr.at[place], peer
        )

    def arrived(self, slot, send, receive):
        remote(slot, slot, send, receive, self.here.twin).wait_recv()

    def compute(self, left, right, tiles, zones, send=True):
        here = self.here
        own = self.give.shape[2]
        per = 128 // (2 * own)
        width = self.give.shape[3]
        step = 256
        for group in range(zones):
            spots = tiles(group)

            @pl.loop(0, width // step)
            def _(index):
                lane = pl.ds(pl.multiple_of(index * step, step), step)
                terms = dot(left(group), right(lane))
                for spot, (zone, seq_group) in enumerate(spots):
                    for sub in range(per):
                        at = spot * 128 + sub * 2 * own
                        even, odd = terms[at : at + own], terms[at + own : at + 2 * own]
                        place = zone * per + sub
                        mine = jnp.where(here.half == 0, even, odd).astype(BF)
                        theirs = jnp.where(here.half == 0, odd, even).astype(BF)
                        self.keep[place, seq_group, :, lane] = mine
                        self.give[place, seq_group, :, lane] = theirs

            for zone in sorted({zone for zone, _ in spots}) if send else ():
                for sub in range(per):
                    self.across(zone * per + sub).start()

    def fold(self, distance):
        here = self.here
        above = here.place + distance
        below = here.place - distance

        def merge(place, line, receive, first):
            near = pltpu.make_async_copy(self.near.at[place], self.stage.at[0], self.load.at[0])
            self.arrived(self.near.at[place], self.ys.at[place], self.yr.at[place])
            near.start()

            @pl.when(first)
            def _():
                near.wait()
                add_rows(self.keep.at[place], [self.keep.at[place], self.stage.at[0]])

            @pl.when(jnp.logical_not(first))
            def _():
                self.arrived(line.at[place], self.us.at[0], receive.at[place])
                far = pltpu.make_async_copy(line.at[place], self.stage.at[1], self.load.at[1])
                far.start()
                near.wait()
                far.wait()
                add_rows(
                    self.keep.at[place], [self.keep.at[place], self.stage.at[0], self.stage.at[1]]
                )

        @pl.when(above <= self.last)
        def _():
            merge(above, self.rising, self.ur, here.place == 0)
            self.up(above).start()

        @pl.when(below >= 0)
        def _():
            merge(below, self.falling, self.dr, here.place == self.last)
            self.down(below).start()

    def finish(self):
        here = self.here
        place = here.place
        self.arrived(self.near.at[place], self.ys.at[place], self.yr.at[place])
        keep = self.keep.at[place]
        near = pltpu.make_async_copy(self.near.at[place], self.stage.at[0], self.load.at[0])
        low = pltpu.make_async_copy(self.rising.at[place], self.stage.at[1], self.load.at[1])
        high = pltpu.make_async_copy(self.falling.at[place], self.stage.at[1], self.load.at[1])
        near.start()

        @pl.when(place > 0)
        def _():
            self.arrived(self.rising.at[place], self.us.at[0], self.ur.at[place])
            low.start()
            low.wait()

        @pl.when(place == 0)
        def _():
            self.arrived(self.falling.at[place], self.ds.at[0], self.dr.at[place])
            high.start()
            high.wait()

        near.wait()

        @pl.when((place > 0) & (place < self.last))
        def _():
            add_rows(keep, [keep, self.stage.at[0], self.stage.at[1]])
            self.arrived(self.falling.at[place], self.ds.at[0], self.dr.at[place])
            high.start()
            high.wait()
            add_rows(self.total, [keep, self.stage.at[1]])

        @pl.when((place == 0) | (place == self.last))
        def _():
            add_rows(self.total, [keep, self.stage.at[0], self.stage.at[1]])

    def sent(self):
        for place in range(self.here.outer):
            self.across(place).wait_send()

    def settle(self):
        here = self.here
        for place in range(here.outer):

            @pl.when(place > here.place)
            def _():
                self.up(place).wait_send()

            @pl.when(place < here.place)
            def _():
                self.down(place).wait_send()


class LineSum:
    def __init__(self, here, terms, rising, falling, stage, sems):
        self.here, self.terms, self.stage = here, terms, stage
        self.rising, self.falling = rising, falling
        self.us, self.ur, self.ds, self.dr, self.load = sems
        self.last = here.outer - 1

    def up(self, place):
        peer = self.here.outer_peer(self.here.place + 1)
        return remote(
            self.terms.at[place], self.rising.at[place], self.us.at[place], self.ur.at[place], peer
        )

    def down(self, place):
        peer = self.here.outer_peer(self.here.place - 1)
        return remote(
            self.terms.at[place], self.falling.at[place], self.ds.at[place], self.dr.at[place], peer
        )

    def merge(self, place, line, receive):
        slot = line.at[place]
        remote(slot, slot, self.us.at[0], receive.at[place], self.here.twin).wait_recv()
        copy = pltpu.make_async_copy(slot, self.stage.at[0], self.load.at[0])
        copy.start()
        copy.wait()
        add_rows(self.terms.at[place], [self.terms.at[place], self.stage.at[0]])

    def fold(self, distance):
        here = self.here
        above = here.place + distance
        below = here.place - distance

        @pl.when(above <= self.last)
        def _():
            @pl.when(here.place > 0)
            def _():
                self.merge(above, self.rising, self.ur)

            self.up(above).start()

        @pl.when(below >= 0)
        def _():
            @pl.when(here.place < self.last)
            def _():
                self.merge(below, self.falling, self.dr)

            self.down(below).start()

    def gather(self):
        place = self.here.place

        @pl.when(place > 0)
        def _():
            self.merge(place, self.rising, self.ur)

        @pl.when(place < self.last)
        def _():
            self.merge(place, self.falling, self.dr)

    def settle(self):
        here = self.here
        for place in range(here.outer):

            @pl.when(place > here.place)
            def _():
                self.up(place).wait_send()

            @pl.when(place < here.place)
            def _():
                self.down(place).wait_send()


class LineFirstSum(RowSum):
    def __init__(self, here, give, keep, near, lines, stage, total, sems, twin_sems):
        self.here, self.give, self.keep = here, give, keep
        self.near, self.stage, self.total = near, stage, total
        self.ys, self.yr, self.load = sems[0], sems[1], sems[6]
        self.lines = [
            LineSum(here, terms, rising, falling, stage, kinds[2:])
            for terms, (rising, falling), kinds in (
                (give, lines[0], twin_sems),
                (keep, lines[1], sems),
            )
        ]

    def fold(self, distance):
        for line in self.lines:
            line.fold(distance)

    def pass_on(self):
        self.lines[0].gather()
        self.across(self.here.place).start()
        self.lines[1].gather()

    def finish(self):
        place = self.here.place
        self.arrived(self.near.at[place], self.ys.at[place], self.yr.at[place])
        near = pltpu.make_async_copy(self.near.at[place], self.stage.at[0], self.load.at[0])
        near.start()
        near.wait()
        add_rows(self.total, [self.keep.at[place], self.stage.at[0]])

    def sent(self):
        self.across(self.here.place).wait_send()

    def settle(self):
        for line in self.lines:
            line.settle()


class RowSpread:
    def __init__(self, here, rows, whole, sems):
        self.here, self.rows, self.whole = here, rows, whole
        self.send_sems, self.recv_sems, self.local = sems

    def copy(self, amount):
        seq = lax.rem(self.here.seq + amount, 4)
        return remote(
            self.rows.at[seq],
            self.whole.at[self.here.seq],
            self.send_sems.at[amount - 1],
            self.recv_sems.at[amount - 1],
            {"seq": seq},
        )

    def keep(self):
        seq = self.here.seq
        return pltpu.make_async_copy(self.rows.at[seq], self.whole.at[seq], self.local)

    def send(self):
        for amount in (2, 3, 1):
            self.copy(amount).start()
        self.keep().start()

    def arrive(self):
        for amount in (1, 2, 3):
            self.copy(amount).wait_recv()
        self.keep().wait()

    def finish(self):
        for amount in (1, 2, 3):
            self.copy(amount).wait_send()


class TokenSum:
    def __init__(self, here, part, got, pair, far_got, base, sems):
        self.here, self.part, self.got, self.pair = here, part, got, pair
        self.far_got, self.base = far_got, base
        self.send_sems, self.recv_sems = sems
        self.rows = part.shape[0] // 4

    def piece(self, seq):
        return pl.ds(pl.multiple_of(seq * self.rows, self.rows), self.rows)

    def to_mate(self, index):
        here = self.here
        chip = here.chip if index else 1 - here.chip
        seq = chip * 2 + 1 - here.core
        return remote(
            self.part.at[self.piece(seq), :],
            self.got.at[index],
            self.send_sems.at[index],
            self.recv_sems.at[index],
            here.mate,
        )

    def to_far(self):
        return remote(
            self.pair, self.far_got, self.send_sems.at[2], self.recv_sems.at[2], self.here.far
        )

    def send(self):
        self.to_mate(0).start()
        self.to_mate(1).start()

    def loop(self, body):
        @pl.loop(0, self.rows // 32)
        def _(index):
            body(index * 32)

    def pass_on(self):
        self.to_mate(0).wait_recv()
        begin = self.here.far_seq * self.rows

        def body(at):
            part = pl.ds(pl.multiple_of(at, 32), 32)
            source = pl.ds(pl.multiple_of(begin + at, 32), 32)
            total = self.part[source, :].astype(F32) + self.got[0, part, :].astype(F32)
            self.pair[part, :] = total.astype(BF)

        self.loop(body)
        self.to_far().start()

    def add_near(self):
        self.to_mate(1).wait_recv()
        begin = self.here.seq * self.rows

        def body(at):
            part = pl.ds(pl.multiple_of(at, 32), 32)
            source = pl.ds(pl.multiple_of(begin + at, 32), 32)
            self.base[part, :] += self.part[source, :].astype(F32) + self.got[1, part, :].astype(F32)

        self.loop(body)
        self.to_mate(0).wait_send()
        self.to_mate(1).wait_send()

    def add_far(self):
        self.to_far().wait_recv()

        def body(at):
            part = pl.ds(pl.multiple_of(at, 32), 32)
            self.base[part, :] += self.far_got[part, :].astype(F32)

        self.loop(body)
        self.to_far().wait_send()


class GainSum:
    def __init__(self, here, parts, arrived, sems):
        self.here, self.parts, self.arrived = here, parts, arrived
        self.send_sems, self.recv_sems = sems
        self.peers = [here.mate, here.far, here.twin] + here.line_peers()

    def copy(self, index):
        return remote(
            self.parts.at[index],
            self.arrived.at[index],
            self.send_sems.at[index],
            self.recv_sems.at[index],
            self.peers[index],
        )

    def start(self):
        self.copy(0).start()

    def hop(self, index):
        self.copy(index).wait()
        self.parts[index + 1] = self.parts[index] + self.arrived[index]
        if index + 1 < len(self.peers):
            self.copy(index + 1).start()


PLAN = (
    (("down", 3),),
    (("down", 2),),
    (),
    (),
    (("down", 1),),
    (),
    (("first", 3), ("first", 2),),
    (),
    (("first", 1),),
    (),
    (("out", 3), ("out", 2),),
    (),
    (("second", 3), ("second", 2), ("first", "finish"),),
    (("down", "pass"),),
    (("out", 1), ("qkv", 3), ("qkv", 2), ("second", 1),),
    (("out", "pass"), ("qkv", 1),),
    (("second", "finish"), ("out", "finish"), ("down", "finish"), ("qkv", "finish"),),
)


def backward_kernel(
    size,
    n1_hbm,
    dy_hbm,
    n2_hbm,
    act_hbm,
    first_hbm,
    second_hbm,
    proj_hbm,
    heads_ref,
    mixed_ref,
    lse_ref,
    middle_hbm,
    hidden_hbm,
    dy_own,
    qkv_full,
    out_full,
    first_full,
    second_full,
    down_full,
    attn_gain_ref,
    mlp_gain_ref,
    query_gain_ref,
    key_gain_ref,
    cos_ref,
    sin_ref,
    start_ref,
    grad_in,
    gains_out,
    grad_out,
    grad_query,
    grad_key,
    grad_value,
    hidden_out,
    grad_gate,
    grad_up,
    grad_down,
    down_rows,
    first_rows,
    second_rows,
    qkv_rows,
    da_hbm,
    near_mlp,
    rising_mlp,
    falling_mlp,
    rising_twin,
    falling_twin,
    near_qkv,
    rising_qkv,
    falling_qkv,
    near_out,
    rising_out,
    falling_out,
    rising_out_twin,
    falling_out_twin,
    lhs,
    turned,
    first_r,
    second_r,
    give,
    keep,
    give_out,
    keep_out,
    stage,
    stage_out,
    dout_ref,
    da_own,
    got,
    far_got,
    pair,
    middle_grad,
    proj_buf,
    lse_t,
    delta,
    delta_t,
    dk_sum,
    dv_sum,
    gain_rows,
    gain_got,
    wide_rows,
    ys,
    yr,
    us,
    ur,
    ds,
    dr,
    fold_load,
    spread_s,
    spread_r,
    spread_l,
    sum_s,
    sum_r,
    ts,
    tr,
    token_local,
    gs,
    gr,
    load_sem,
    credit,
):
    here = Place(size)
    length, width = lhs.shape
    rows = length // 4
    units = first_r.shape[1]
    chunk = units // 2
    ff_part = units // size
    heads = mixed_ref.shape[1] // HEAD_DIM
    kv_heads = heads // 2
    qkv_width = qkv_full.shape[2]
    last = here.outer - 1
    zones = width // 512
    scale = HEAD_DIM ** (-0.5)

    def load(source, target, index):
        copy = pltpu.make_async_copy(source, target, load_sem.at[index])
        copy.start()
        return copy

    def sems(index):
        return tuple(kind.at[index] for kind in (ys, yr, us, ur, ds, dr, fold_load))

    down = LineFirstSum(
        here,
        give.at[2],
        keep.at[0],
        near_mlp.at[0],
        ((rising_twin, falling_twin), (rising_mlp.at[0], falling_mlp.at[0])),
        stage,
        keep.at[0, here.place],
        sems(0),
        sems(5),
    )
    first, second = [
        RowSum(
            here,
            give.at[2 - index],
            keep.at[index],
            near_mlp.at[index],
            rising_mlp.at[index],
            falling_mlp.at[index],
            stage,
            keep.at[index, here.place],
            sems(index),
        )
        for index in (1, 2)
    ]
    thin = slice(0, qkv_width)
    qkv = RowSum(
        here,
        give.at[1, :, :, :, thin],
        second_r.at[:, :, :, thin],
        near_qkv,
        rising_qkv,
        falling_qkv,
        stage.at[:, :, :, thin],
        second_r.at[here.place, :, :, thin],
        sems(3),
    )
    out = LineFirstSum(
        here,
        give_out,
        keep_out,
        near_out,
        ((rising_out_twin, falling_out_twin), (rising_out, falling_out)),
        stage_out,
        grad_out,
        sems(4),
        sems(6),
    )

    def spread(index, job, whole):
        return RowSpread(
            here, job.total, whole, (spread_s.at[index], spread_r.at[index], spread_l.at[index])
        )

    spread_down = spread(0, down, down_rows)
    spread_first = spread(1, first, first_rows)
    spread_second = spread(2, second, second_rows)
    spread_qkv = spread(3, qkv, qkv_rows)

    def token_sum(index, base):
        return TokenSum(
            here, lhs, got, pair, far_got, base, (sum_s.at[index], sum_r.at[index])
        )

    sum_mlp = token_sum(0, middle_grad)
    sum_hidden = token_sum(1, grad_in)
    sum_attn = token_sum(2, grad_in)
    da = TokenGather(here, da_own, da_hbm, (ts, tr, token_local.at[0]))

    def model_tiles(group):
        return [(group, seq_group) for seq_group in range(4)]

    def first_columns(lane):
        return first_r[:, lane]

    def model_left(group):
        return turned[group * 4 : group * 4 + 4].reshape(512, length)

    jobs = {"down": down, "first": first, "second": second, "out": out, "qkv": qkv}
    spreads = {
        "down": spread_down,
        "first": spread_first,
        "second": spread_second,
        "qkv": spread_qkv,
    }

    ended = []

    def advance(steps):
        for name, step in steps:
            job = jobs[name]
            if step == "pass":
                job.pass_on()
            elif step == "finish":
                job.finish()
                if name in spreads:
                    spreads[name].send()
                    ended.append(name)
            else:
                for distance in range(last * step // 3, last * (step - 1) // 3, -1):
                    job.fold(distance)

    load_turned = load(dy_hbm, turned, 0)
    load_act = load(act_hbm, first_r, 1)
    load_middle = load(middle_hbm, grad_in, 2)
    load_dy = load(dy_own, da_own, 4)
    load_second = load(second_hbm, second_r, 3)
    here.greet(wide=True)
    load_turned.wait()
    load_act.wait()
    down.compute(model_left, first_columns, model_tiles, zones, send=False)
    advance(PLAN[0])
    load_turned = load(n2_hbm, turned, 0)
    load_first = load(first_hbm, first_r, 1)
    load_first.wait()
    load_second.wait()

    own = width // size
    slabs = 256 // own

    def dn2_body(first_w, second_w):
        lane = pl.ds(pl.multiple_of(pl.program_id(0) * 256, 256), 256)
        first_tile = first_w[...].reshape(256, units)
        second_tile = second_w[...].reshape(256, units)

        @pl.loop(0, 4)
        def _(index):
            part = pl.ds(pl.multiple_of(index * rows, rows), rows)
            total = contract_cols(first_r[part, :], first_tile)
            blocks = pl.ds(index * (here.outer // 4), here.outer // 4)
            second_rows = second_r[blocks].reshape(rows, units)
            total = total + contract_cols(second_rows, second_tile)
            lhs[part, lane] = total.astype(BF)

    slab = pl.BlockSpec((slabs, own, units), lambda t: (t, 0, 0))
    pltpu.emit_pipeline(dn2_body, grid=(width // 256,), in_specs=[slab, slab])(
        first_full, second_full
    )
    sum_mlp.send()
    middle_grad[...] = jnp.zeros_like(middle_grad)
    load_turned.wait()
    advance(PLAN[1])
    sum_mlp.pass_on()
    sum_mlp.add_near()
    first.compute(model_left, first_columns, model_tiles, zones)
    load_act = load(act_hbm, first_r, 1)
    advance(PLAN[2])
    sum_mlp.add_far()

    load_middle.wait()
    load_dy.wait()
    gain_rows[0] = jnp.zeros_like(gain_rows[0])
    narrow = 16

    @pl.loop(0, rows // narrow)
    def _(index):
        part = pl.ds(pl.multiple_of(index * narrow, narrow), narrow)
        values = grad_in[part, :]
        scales = lax.rsqrt(jnp.mean(values * values, axis=-1, keepdims=True) + EPSILON)
        normed = values * scales
        update = middle_grad[part, :]
        gain_rows[0, 1:2, :] += jnp.sum(update * normed, axis=0, keepdims=True)
        upper = update * mlp_gain_ref[...]
        inner = jnp.mean(upper * normed, axis=-1, keepdims=True)
        grad = da_own[part, :].astype(F32) + scales * (upper - normed * inner)
        middle_grad[part, :] = grad
        da_own[part, :] = grad.astype(BF)

    da.send()
    advance(PLAN[3])
    second.compute(
        model_left, lambda lane: second_r[:, :, :, lane].reshape(length, -1), model_tiles, zones
    )
    advance(PLAN[4])

    def hidden_body(weight):
        lane = pl.ds(pl.multiple_of(pl.program_id(0) * 256, 256), 256)
        tile = weight[...]

        @pl.loop(0, 4)
        def _(index):
            part = pl.ds(pl.multiple_of(index * rows, rows), rows)
            lhs[part, lane] = dot(first_r[part, :], tile).astype(BF)

    load_act.wait()
    pltpu.emit_pipeline(
        hidden_body,
        grid=(width // 256,),
        in_specs=[pl.BlockSpec((units, 256), lambda t: (0, t))],
    )(down_full)
    da.mate_arrived()
    sum_hidden.send()
    da.forward()
    advance(PLAN[5])
    sum_hidden.pass_on()
    sum_hidden.add_near()
    advance(PLAN[6])
    da.rest_arrived()
    da.finish()
    load_lhs = load(da_hbm, lhs, 0)
    load_own = load(hidden_hbm, da_own, 2)
    load_lhs.wait()

    def dout_body(weight):
        lane = pl.ds(pl.multiple_of(pl.program_id(0) * 256, 256), 256)
        tile = weight[...].reshape(256, width)

        @pl.loop(0, 4)
        def _(index):
            part = pl.ds(pl.multiple_of(index * rows, rows), rows)
            dout_ref[part, lane] = contract_cols(lhs[part, :], tile).astype(BF)

    out_blocks, out_rows = out_full.shape[:2]
    pltpu.emit_pipeline(
        dout_body,
        grid=(out_blocks * out_rows // 256,),
        in_specs=[pl.BlockSpec((256 // out_rows, out_rows, width), lambda t: (t, 0, 0))],
    )(out_full)

    for head in range(heads):
        turned[head] = mixed_ref[:, head * HEAD_DIM : (head + 1) * HEAD_DIM].T
    out.compute(
        lambda group: turned[0:heads].reshape(heads * HEAD_DIM, length),
        lambda lane: lhs[:, lane],
        lambda group: [(zone, 0) for zone in range(heads)],
        1,
        send=False,
    )
    load_turned = load(n1_hbm, turned, 0)
    sum_hidden.add_far()
    for index, peer in enumerate((here.mate, here.far)):
        pl.semaphore_signal(credit.at[index], inc=1, device_id=peer, device_id_type=MESH)

    @pl.loop(0, rows // 32)
    def _(index):
        part = pl.ds(pl.multiple_of(index * 32, 32), 32)
        pair[part, :] = grad_in[part, :].astype(BF)

    store_hidden = load(pair, hidden_out, 1)
    advance(PLAN[7])

    lse_t[...] = lse_ref[...].T[0:8]
    delta[...] = jnp.zeros_like(delta)
    for head in range(heads):
        lane = slice(head * HEAD_DIM, (head + 1) * HEAD_DIM)
        terms = dout_ref[:, lane].astype(F32) * mixed_ref[:, lane].astype(F32)
        delta[:, head : head + 1] = jnp.sum(terms, axis=-1, keepdims=True)
    delta_t[...] = delta[...].T[0:8]
    def through_norm(grad, head, part, gain_ref, gain_row):
        proj = proj_buf[part, :]
        scales = lax.rsqrt(jnp.mean(proj * proj, axis=-1, keepdims=True) + EPSILON)
        normed = proj * scales
        grad = grad.astype(F32)
        upper = grad * cos_ref[part, :] - pltpu.roll(grad, HEAD_DIM // 2, 1) * sin_ref[part, :]
        gain_rows[0, 2:3, gain_row * HEAD_DIM : (gain_row + 1) * HEAD_DIM] += jnp.sum(
            upper * normed, axis=0, keepdims=True
        )
        upper = upper * gain_ref[...]
        inner = jnp.mean(upper * normed, axis=-1, keepdims=True)
        result = (scales * (upper - normed * inner)).astype(BF)
        first_r[part, head * HEAD_DIM : (head + 1) * HEAD_DIM] = result

    for head in range(heads):
        pair_head = head // 2
        load_proj = load(proj_hbm.at[head], proj_buf, 4)
        if head % 2 == 0:
            dk_sum[...] = jnp.zeros_like(dk_sum)
            dv_sum[...] = jnp.zeros_like(dv_sum)
        load_proj.wait()
        for block in range(4):
            end = (block + 1) * rows
            part = pl.ds(block * rows, rows)
            queries = heads_ref[head, part, :]
            keys = heads_ref[heads + pair_head, 0:end, :]
            values = heads_ref[heads + kv_heads + pair_head, 0:end, :]
            out_grad = dout_ref[part, head * HEAD_DIM : (head + 1) * HEAD_DIM]
            scores = contract_cols(keys, queries)
            key_place = lax.broadcasted_iota(jnp.int32, (end, rows), 0)
            query_place = lax.broadcasted_iota(jnp.int32, (end, rows), 1) + block * rows
            allowed = (key_place >= start_ref[:, part]) & (key_place <= query_place)
            weights = jnp.exp(scores * scale - lse_t[head : head + 1, part])
            weights = jnp.where(allowed, weights, 0.0)
            weight_grad = contract_cols(values, out_grad)
            inner = delta_t[head : head + 1, part]
            score_grad = (weights * (weight_grad - inner)).astype(BF)
            dk_sum[0:end, :] += dot(score_grad, queries) * scale
            dv_sum[0:end, :] += dot(weights.astype(BF), out_grad)
            query_grad = (contract_rows(score_grad, keys) * scale).astype(BF)
            through_norm(query_grad, head, part, query_gain_ref, 0)
        if head % 2:
            key = heads + pair_head
            value_at = (heads + kv_heads + pair_head) * HEAD_DIM
            load(proj_hbm.at[key], proj_buf, 4).wait()

            @pl.loop(0, 4)
            def _(index):
                part = pl.ds(pl.multiple_of(index * rows, rows), rows)
                through_norm(dk_sum[part, :].astype(BF), key, part, key_gain_ref, 1)
                first_r[part, value_at : value_at + HEAD_DIM] = dv_sum[part, :].astype(BF)

        advance(PLAN[8 + head])

    load_turned.wait()
    first.sent()
    store_hidden.wait()
    proj_grads = first_r.at[:, 0:qkv_width]
    qkv.compute(model_left, first_columns, model_tiles, zones)
    advance(PLAN[12])

    def dn1_body(weight):
        lane = pl.ds(pl.multiple_of(pl.program_id(0) * 256, 256), 256)
        tile = weight[...].reshape(256, qkv_width)

        @pl.loop(0, 4)
        def _(index):
            part = pl.ds(pl.multiple_of(index * rows, rows), rows)
            lhs[part, lane] = contract_cols(proj_grads[part, :], tile).astype(BF)

    pltpu.emit_pipeline(
        dn1_body,
        grid=(width // 256,),
        in_specs=[pl.BlockSpec((slabs, own, qkv_width), lambda t: (t, 0, 0))],
    )(qkv_full)
    grad_in[...] = jnp.zeros_like(grad_in)
    pl.semaphore_wait(credit.at[0], 1)
    pl.semaphore_wait(credit.at[1], 1)
    sum_attn.send()
    advance(PLAN[13])
    sum_attn.pass_on()
    sum_attn.add_near()
    advance(PLAN[14])
    sum_attn.add_far()
    load_own.wait()

    @pl.loop(0, rows // narrow)
    def _(index):
        part = pl.ds(pl.multiple_of(index * narrow, narrow), narrow)
        values = da_own[part, :].astype(F32)
        scales = lax.rsqrt(jnp.mean(values * values, axis=-1, keepdims=True) + EPSILON)
        normed = values * scales
        update = grad_in[part, :]
        gain_rows[0, 0:1, :] += jnp.sum(update * normed, axis=0, keepdims=True)
        upper = update * attn_gain_ref[...]
        inner = jnp.mean(upper * normed, axis=-1, keepdims=True)
        grad_in[part, :] = middle_grad[part, :] + scales * (upper - normed * inner)

    gain_sum = GainSum(here, gain_rows, gain_got, (gs, gr))
    gain_sum.start()
    advance(PLAN[15])
    hops = list(range(len(gain_sum.peers)))
    slab = wide_rows.shape[0]

    def place_rows(read, target, lane):
        width_here = lane.stop - lane.start

        for index in range(target.shape[0] // slab):
            part = slice(index * slab, (index + 1) * slab)
            wide_rows[:, 0:width_here] = read(part)
            load(wide_rows.at[:, 0:width_here], target.at[part, lane], 3).wait()

    def place_units(read, target, begin, blocks):
        def ordered(part):
            values = [read(seq, part).astype(F32) for seq in range(4)]
            return jnp.concatenate(
                [
                    values[seq][:, block * ff_part : (block + 1) * ff_part]
                    for block in range(blocks)
                    for seq in range(4)
                ],
                axis=1,
            )

        lane = slice(begin * 4 * ff_part, (begin + blocks) * 4 * ff_part)
        place_rows(ordered, target, lane)

    most, tail = chunk - 256, 256

    def place(name):
        spreads[name].arrive()
        if name == "down":
            load(down_rows, stage.at[0], 1).wait()
            place_units(lambda seq, part: stage[0, seq, part, 0:chunk], grad_down, 0, size // 2)
            place_units(
                lambda seq, part: stage[0, seq, part, chunk:units], grad_down, size // 2, size // 2
            )
        elif name == "first":
            load(first_rows, stage.at[0], 1).wait()
            for side, target in enumerate((grad_gate, grad_up)):
                place_units(
                    lambda seq, part: stage[0, seq, part, side * chunk : (side + 1) * chunk],
                    target,
                    0,
                    size // 2,
                )
        elif name == "second":
            load(second_rows, stage.at[0], 1).wait()
            for side, target in enumerate((grad_gate, grad_up)):

                def read(seq, part):
                    at = 2 * most + side * tail
                    return jnp.concatenate(
                        [
                            stage[0, seq, part, side * most : (side + 1) * most],
                            stage[0, seq, part, at : at + tail],
                        ],
                        axis=1,
                    )

                place_units(read, target, size // 2, size // 2)
        else:
            load(qkv_rows, stage.at[0, :, :, thin], 1).wait()
            at = 0
            for target, count in (
                (grad_query, heads * HEAD_DIM),
                (grad_key, kv_heads * HEAD_DIM),
                (grad_value, kv_heads * HEAD_DIM),
            ):

                def side_by_side(part):
                    return jnp.concatenate(
                        [stage[0, seq, part, at : at + count].astype(F32) for seq in range(4)],
                        axis=1,
                    )

                place_rows(side_by_side, target, slice(0, 4 * count))
                at += count

    for index, (name, step) in enumerate(PLAN[16]):
        advance([(name, step)])
        if hops:
            gain_sum.hop(hops.pop(0))
        while ended and ended[0] not in [job for job, _ in PLAN[16][max(0, index - 1) : index + 1]]:
            place(ended.pop(0))
    for index in hops:
        gain_sum.hop(index)
    gains_out[...] = gain_rows[gain_rows.shape[0] - 1]
    for name in ended:
        place(name)
    for job in (down, second, out, qkv):
        job.sent()
    for job in jobs.values():
        job.settle()
    for job in spreads.values():
        job.finish()


def backward(saved, weights, own, gains, tables, starts):
    size = lax.axis_size("shard")
    outer = size // 2
    (n1, dy, n2, act, first, second, proj, heads_all, mixed, lse, middle) = saved
    length, width = heads_all.shape[1], middle.shape[1]
    piece = length // 4
    units = act.shape[1]
    qkv_width = weights[0].shape[2]
    rows = width // (4 * size)
    q_width = mixed.shape[1]

    def shape(*dims, kind=BF):
        return jax.ShapeDtypeStruct(dims, kind)

    results = [
        shape(piece, width, kind=F32),
        shape(8, width, kind=F32),
        shape(1, rows, width, kind=F32),
        shape(rows, 4 * q_width, kind=F32),
        shape(rows, 2 * q_width, kind=F32),
        shape(rows, 2 * q_width, kind=F32),
        shape(piece, width),
        shape(rows, 4 * units, kind=F32),
        shape(rows, 4 * units, kind=F32),
        shape(rows, 4 * units, kind=F32),
        shape(4, rows, units),
        shape(4, rows, units),
        shape(4, rows, units),
        shape(4, rows, qkv_width),
        shape(length, width),
    ]
    results += [shape(3, outer, 4, rows, units)] * 3
    results += [shape(outer, 4, rows, units)] * 2
    results += [shape(outer, 4, rows, qkv_width)] * 3
    results += [shape(outer, 1, rows, width)] * 5
    dma = pltpu.SemaphoreType.DMA
    hops = 3 + outer.bit_length() - 1
    vmem = pltpu.VMEM
    return pl.pallas_call(
        functools.partial(backward_kernel, size),
        out_shape=results,
        in_specs=[ANY] * 7 + [VMEM] * 3 + [ANY] * 8 + [VMEM] * 7,
        out_specs=[VMEM] * 3 + [ANY] * (len(results) - 3),
        scratch_shapes=[
            vmem((length, width), BF),
            vmem((width // 128, 128, length), BF),
            vmem((length, units), BF),
            vmem((outer, 4, rows, units), BF),
            vmem((3, outer, 4, rows, units), BF),
            vmem((3, outer, 4, rows, units), BF),
            vmem((outer, 1, rows, width), BF),
            vmem((outer, 1, rows, width), BF),
            vmem((2, 4, rows, units), BF),
            vmem((2, 1, rows, width), BF),
            vmem((length, q_width), BF),
            vmem((piece, width), BF),
            vmem((2, piece, width), BF),
            vmem((piece, width), BF),
            vmem((piece, width), BF),
            vmem((piece, width), F32),
            vmem((length, HEAD_DIM), F32),
            vmem((8, length), F32),
            vmem((length, 128), F32),
            vmem((8, length), F32),
            vmem((length, HEAD_DIM), F32),
            vmem((length, HEAD_DIM), F32),
            vmem((hops + 1, 8, width), F32),
            vmem((hops, 8, width), F32),
            vmem((16, 2 * units), F32),
            dma((7, outer)),
            dma((7, outer)),
            dma((7, outer)),
            dma((7, outer)),
            dma((7, outer)),
            dma((7, outer)),
            dma((7, 3)),
            dma((4, 3)),
            dma((4, 3)),
            dma((4,)),
            dma((3, 3)),
            dma((3, 3)),
            dma((3,)),
            dma((3,)),
            dma((1,)),
            dma((hops,)),
            dma((hops,)),
            dma((5,)),
            pltpu.SemaphoreType.REGULAR((2,)),
        ],
        compiler_params=pltpu.CompilerParams(
            collective_id=1, has_side_effects=True, vmem_limit_bytes=VMEM_BYTES
        ),
        name="backward_sums",
    )(
        n1,
        dy,
        n2,
        act,
        first,
        second.reshape(outer, 4, rows, units),
        proj,
        heads_all,
        mixed,
        lse,
        middle,
        *own,
        *weights,
        *gains,
        *tables,
        starts.reshape(1, length),
    )


def hand_over_kernel(*refs):
    count = (len(refs) - 1) // 2
    copies = [
        pltpu.make_async_copy(source, target, refs[-1].at[index])
        for index, (source, target) in enumerate(zip(refs[:count], refs[count : 2 * count]))
    ]
    for copy in copies:
        copy.start()
    for copy in copies:
        copy.wait()


def hand_over(*arrays):
    return pl.pallas_call(
        hand_over_kernel,
        out_shape=[jax.ShapeDtypeStruct(array.shape, array.dtype) for array in arrays],
        in_specs=[ANY] * len(arrays),
        out_specs=[ANY] * len(arrays),
        scratch_shapes=[pltpu.SemaphoreType.DMA((len(arrays),))],
        name="hand_over",
    )(*arrays)


def local(
    hidden_in,
    segment_ids,
    norm_attn_gain,
    w_query,
    w_key,
    w_value,
    query_gain,
    key_gain,
    w_out,
    norm_mlp_gain,
    w_gate,
    w_up,
    w_down,
    out_cotangent,
):
    length = hidden_in.shape[1] * 4
    segment = segment_ids[0]
    places = jnp.arange(length, dtype=jnp.int32)
    starts = jnp.sum((segment[None, :] < segment[:, None]).astype(jnp.int32), axis=1)
    cosine, sine = rotary_tables(places - starts)
    signs = jnp.where(jnp.arange(HEAD_DIM) < HEAD_DIM // 2, -1.0, 1.0).astype(F32)
    tables = (cosine, sine * signs)
    gains = (norm_attn_gain[None], norm_mlp_gain[None], query_gain[None], key_gain[None])
    results = forward(
        hidden_in[0],
        out_cotangent[0],
        (w_query, w_key, w_value, w_out, w_gate, w_up, w_down),
        gains,
        tables,
        starts,
    )
    (
        grad_in,
        gain_totals,
        grad_out,
        grad_query,
        grad_key,
        grad_value,
        hidden_out,
        grad_gate,
        grad_up,
        grad_down,
    ) = backward(
        results[8:],
        results[:5],
        (hidden_in[0], out_cotangent[0]),
        gains,
        tables,
        starts,
    )[:10]
    hidden_out, grad_in, grad_query, grad_key, grad_value, grad_out, grad_gate, grad_up = hand_over(
        hidden_out, grad_in, grad_query, grad_key, grad_value, grad_out[0], grad_gate, grad_up
    )
    return (
        hidden_out[None],
        grad_in[None],
        gain_totals[0],
        grad_query,
        grad_key,
        grad_value,
        gain_totals[2, :HEAD_DIM],
        gain_totals[2, HEAD_DIM : 2 * HEAD_DIM],
        grad_out,
        gain_totals[1],
        grad_gate,
        grad_up,
        grad_down.T,
    )


def solution(mesh):
    return jax.shard_map(
        local,
        mesh=mesh,
        in_specs=(
            P("shard", "seq", None),
            P("shard", None),
            P(),
            P("shard", None),
            P("shard", None),
            P("shard", None),
            P(),
            P(),
            P("shard", None),
            P(),
            P("shard", None),
            P("shard", None),
            P("shard", None),
            P("shard", "seq", None),
        ),
        out_specs=(
            P("shard", "seq", None),
            P("shard", "seq", None),
            P(),
            P(("seq", "shard"), None),
            P(("seq", "shard"), None),
            P(("seq", "shard"), None),
            P(),
            P(),
            P(("seq", "shard"), None),
            P(),
            P(("seq", "shard"), None),
            P(("seq", "shard"), None),
            P(None, ("seq", "shard")),
        ),
        check_vma=False,
    )
```

```python
import functools

import jax
import jax.numpy as jnp
from jax import lax
from jax.experimental import pallas as pl
from jax.experimental.pallas import tpu as pltpu
from jax.sharding import PartitionSpec as P

Q_HEADS = 16
KV_HEADS = 8
HEAD_DIM = 128
EPSILON = 1e-06
ROPE_BASE = 1000000.0
NEGATIVE = -1e30
BF = jnp.bfloat16
F32 = jnp.float32
MESH = pl.DeviceIdType.MESH
ANY = pl.BlockSpec(memory_space=pl.ANY)
VMEM = pl.BlockSpec(memory_space=pltpu.VMEM)
VMEM_BYTES = 62 * 1024 * 1024


def rotary_tables(positions):
    inverse = ROPE_BASE ** (-(jnp.arange(HEAD_DIM // 2, dtype=F32) * 2.0) / HEAD_DIM)
    angles = positions.astype(F32)[:, None] * inverse[None, :]
    angles = jnp.concatenate([angles, angles], axis=-1)
    return (jnp.cos(angles), jnp.sin(angles))


def dot(left, right):
    return jnp.dot(left, right, preferred_element_type=F32)


def contract_rows(left, right):
    return lax.dot_general(left, right, (((0,), (0,)), ((), ())), preferred_element_type=F32)


def contract_cols(left, right):
    return lax.dot_general(left, right, (((1,), (1,)), ((), ())), preferred_element_type=F32)


class Place:
    def __init__(self, size):
        self.size = size
        self.outer = size // 2
        self.quarter = size // 4
        self.seq = lax.axis_index("seq")
        self.shard = lax.axis_index("shard")
        self.chip = self.seq // 2
        self.core = lax.rem(self.seq, 2)
        self.place = self.shard // 2
        self.half = lax.rem(self.shard, 2)
        self.far_seq = lax.rem(self.seq + 2, 4)
        self.mate_seq = self.chip * 2 + 1 - self.core
        self.far = {"seq": self.far_seq}
        self.mate = {"seq": self.mate_seq}
        self.twin_shard = self.place * 2 + 1 - self.half
        self.twin = {"shard": self.twin_shard}

    def outer_peer(self, place):
        return {"shard": place * 2 + self.half}

    def line_peers(self):
        peers = []
        step = 1
        while step < self.outer:
            sign = 1 - 2 * lax.rem(self.place // step, 2)
            peers.append(self.outer_peer(self.place + sign * step))
            step *= 2
        return peers

    def greet(self, wide=False):
        barrier = pltpu.get_barrier_semaphore()
        last = self.outer - 1

        def signal(peer):
            pl.semaphore_signal(barrier, inc=1, device_id=peer, device_id_type=MESH)

        peers = [self.far, self.mate, self.twin]
        if wide:
            peers += [{"seq": 3 - self.seq}] + self.line_peers()[1:]
        for peer in peers:
            signal(peer)

        @pl.when(self.place < last)
        def _():
            signal(self.outer_peer(self.place + 1))

        @pl.when(self.place > 0)
        def _():
            signal(self.outer_peer(self.place - 1))

        inner = ((self.place > 0) & (self.place < last)).astype(jnp.int32)
        pl.semaphore_wait(barrier, len(peers) + 1 + inner)


def remote(source, target, send, receive, peer):
    return pltpu.make_async_remote_copy(
        src_ref=source,
        dst_ref=target,
        send_sem=send,
        recv_sem=receive,
        device_id=peer,
        device_id_type=MESH,
    )


class LineGather:
    def __init__(self, here, own, slot, sems):
        self.here, self.own, self.slot = here, own, slot
        self.us, self.ur, self.ds, self.dr = sems
        self.last = here.outer - 1

    def up(self, distance):
        here = self.here
        slot = self.slot(here.place - distance)
        source = slot if distance else self.own
        peer = here.outer_peer(here.place + 1)
        return remote(source, slot, self.us.at[distance], self.ur.at[distance], peer)

    def down(self, distance):
        here = self.here
        slot = self.slot(here.place + distance)
        source = slot if distance else self.own
        peer = here.outer_peer(here.place - 1)
        return remote(source, slot, self.ds.at[distance], self.dr.at[distance], peer)

    def send(self):
        here = self.here

        @pl.when(here.place < self.last)
        def _():
            self.up(0).start()

        @pl.when(here.place > 0)
        def _():
            self.down(0).start()

    def step(self, distance, arrived=lambda place: None):
        here = self.here
        below = here.place - 1 - distance
        above = here.place + 1 + distance

        @pl.when(below >= 0)
        def _():
            slot = self.slot(below)
            remote(slot, slot, self.us.at[0], self.ur.at[distance], here.twin).wait_recv()

            @pl.when(here.place < self.last)
            def _():
                self.up(distance + 1).start()

            arrived(below)

        @pl.when(above <= self.last)
        def _():
            slot = self.slot(above)
            remote(slot, slot, self.ds.at[0], self.dr.at[distance], here.twin).wait_recv()

            @pl.when(here.place > 0)
            def _():
                self.down(distance + 1).start()

            arrived(above)

    def finish(self):
        here = self.here
        for distance in range(self.last):

            @pl.when((here.place - distance >= 0) & (here.place < self.last))
            def _():
                self.up(distance).wait_send()

            @pl.when((here.place + distance <= self.last) & (here.place > 0))
            def _():
                self.down(distance).wait_send()


class RowGather:
    def __init__(self, here, own, whole, sems, spot=lambda shard: shard):
        self.here, self.own, self.whole, self.spot = here, own, whole, spot
        self.ys, self.yr, self.local = sems[4:]
        self.line = LineGather(here, own, self.mine, sems[:4])

    def mine(self, place):
        return self.whole.at[self.spot(place * 2 + self.here.half)]

    def theirs(self, place):
        return self.whole.at[self.spot(place * 2 + 1 - self.here.half)]

    def keep(self):
        return pltpu.make_async_copy(self.own, self.mine(self.here.place), self.local)

    def across(self, place, own=False):
        slot = self.mine(place)
        source = self.own if own else slot
        return remote(source, slot, self.ys.at[place], self.yr.at[place], self.here.twin)

    def arrived(self, place):
        slot = self.theirs(place)
        remote(slot, slot, self.ys.at[place], self.yr.at[place], self.here.twin).wait_recv()

    def send(self):
        self.line.send()
        self.across(self.here.place, own=True).start()
        self.keep().start()

    def step(self, distance):
        self.line.step(distance, lambda place: self.across(place).start())

    def arrive(self):
        self.keep().wait()
        for place in range(self.here.outer):
            self.arrived(place)

    def finish(self):
        self.line.finish()
        for place in range(self.here.outer):
            self.across(place).wait_send()


class TwinFirstGather(RowGather):
    def __init__(self, here, own, whole, sems, twin_sems):
        super().__init__(here, own, whole, sems)
        self.lines = [
            self.line,
            LineGather(here, self.theirs(here.place), self.theirs, twin_sems[:4]),
        ]

    def twin(self):
        self.arrived(self.here.place)
        self.lines[1].send()

    def step(self, distance):
        for line in self.lines:
            line.step(distance)

    def arrive(self):
        self.keep().wait()

    def finish(self):
        for line in self.lines:
            line.finish()
        self.across(self.here.place, own=True).wait_send()


class HeadGather:
    def __init__(self, here, own, whole, sems):
        self.here, self.own, self.whole = here, own, whole
        self.us, self.zr, self.ds, _, self.ys, self.yr, self.local = sems
        self.last = here.outer - 1
        self.count = here.quarter // 2
        self.first = here.seq * self.count
        self.mine = here.place - self.first
        self.inside = (self.mine >= 0) & (self.mine < self.count)

    def slot(self, index):
        return self.whole.at[index * 2 + self.here.half]

    def keep(self):
        return pltpu.make_async_copy(self.own, self.slot(self.mine), self.local)

    def up(self, index, own=False):
        slot = self.slot(index)
        peer = self.here.outer_peer(self.here.place + 1)
        return remote(self.own if own else slot, slot, self.us.at[index], self.zr.at[index], peer)

    def down(self, index, own=False):
        slot = self.slot(index)
        peer = self.here.outer_peer(self.here.place - 1)
        return remote(self.own if own else slot, slot, self.ds.at[index], self.zr.at[index], peer)

    def across(self, index):
        slot = self.slot(index)
        return remote(slot, slot, self.ys.at[index], self.yr.at[index], self.here.twin)

    def send(self):
        @pl.when(self.inside)
        def _():
            self.keep().start()

            @pl.when(self.here.place < self.last)
            def _():
                self.up(self.mine, own=True).start()

            @pl.when(self.here.place > 0)
            def _():
                self.down(self.mine, own=True).start()

    def step(self):
        here = self.here

        @pl.when(self.inside)
        def _():
            self.keep().wait()

        for index in range(self.count):
            slot = self.slot(index)
            arrival = remote(slot, slot, self.us.at[0], self.zr.at[index], here.twin)

            @pl.when(self.mine > index)
            def _():
                arrival.wait_recv()

                @pl.when(here.place < self.last)
                def _():
                    self.up(index).start()

            @pl.when(self.mine < index)
            def _():
                arrival.wait_recv()

                @pl.when(here.place > 0)
                def _():
                    self.down(index).start()

            self.across(index).start()

    def arrive(self):
        for index in range(self.count):
            slot = self.whole.at[index * 2 + 1 - self.here.half]
            remote(
                slot, slot, self.ys.at[index], self.yr.at[index], self.here.twin
            ).wait_recv()

    def finish(self):
        here = self.here
        for index in range(self.count):

            @pl.when((self.mine >= index) & (here.place < self.last))
            def _():
                self.up(index).wait_send()

            @pl.when((self.mine <= index) & (here.place > 0))
            def _():
                self.down(index).wait_send()

            self.across(index).wait_send()


class TokenGather:
    def __init__(self, here, own, whole, sems):
        self.here, self.own, self.whole = here, own, whole
        self.send_sems, self.recv_sems, self.local = sems
        self.rows = whole.shape[0] // 4

    def slot(self, seq):
        return self.whole.at[pl.ds(pl.multiple_of(seq * self.rows, self.rows), self.rows), :]

    def keep(self):
        return pltpu.make_async_copy(self.own, self.slot(self.here.seq), self.local)

    def copy(self, index):
        here = self.here
        slot = self.slot(here.far_seq if index == 2 else here.seq)
        return remote(
            slot if index == 2 else self.own,
            slot,
            self.send_sems.at[index],
            self.recv_sems.at[index],
            here.far if index == 0 else here.mate,
        )

    def send(self):
        self.copy(0).start()
        self.copy(1).start()
        self.keep().start()

    def forward(self):
        self.copy(0).wait_recv()
        self.copy(2).start()

    def mate_arrived(self):
        self.copy(1).wait_recv()

    def rest_arrived(self):
        self.copy(2).wait_recv()
        self.keep().wait()

    def arrive(self):
        self.mate_arrived()
        self.rest_arrived()

    def finish(self):
        for index in range(3):
            self.copy(index).wait_send()


class PieceSum:
    def __init__(self, here, piece, base, give, got, pair, far_got, sems, step):
        self.here, self.piece, self.base, self.step = here, piece, base, step
        self.give, self.got, self.pair, self.far_got = give, got, pair, far_got
        self.send_sems, self.recv_sems = sems

    def to_mate(self, index):
        return remote(
            self.give.at[index],
            self.got.at[index],
            self.send_sems.at[index],
            self.recv_sems.at[index],
            self.here.mate,
        )

    def to_far(self):
        return remote(
            self.pair, self.far_got, self.send_sems.at[2], self.recv_sems.at[2], self.here.far
        )

    def columns(self, body):
        step = self.step

        @pl.loop(0, self.pair.shape[1] // step)
        def _(index):
            body(pl.ds(pl.multiple_of(index * step, step), step))

    def send(self):
        here = self.here
        for index, chip in enumerate((1 - here.chip, here.chip)):
            seq = chip * 2 + 1 - here.core

            def fill(column, index=index, seq=seq):
                self.give[index, :, column] = self.piece(seq, column).astype(BF)

            self.columns(fill)
            self.to_mate(index).start()

    def pass_on(self):
        self.to_mate(0).wait_recv()

        def fill(column):
            term = self.piece(self.here.far_seq, column) + self.got[0, :, column].astype(F32)
            self.pair[:, column] = term.astype(BF)

        self.columns(fill)
        self.to_far().start()

    def add_near(self):
        self.to_mate(1).wait_recv()

        def fill(column):
            term = self.piece(self.here.seq, column) + self.got[1, :, column].astype(F32)
            self.base[:, column] += term

        self.columns(fill)

    def add_far(self):
        self.to_far().wait_recv()

        def fill(column):
            self.base[:, column] += self.far_got[:, column].astype(F32)

        self.columns(fill)
        for copy in (self.to_mate(0), self.to_mate(1), self.to_far()):
            copy.wait_send()


FORWARD_PLAN = (
    (("down", "send"),),
    (),
    (("out", "send"),),
    (("down", 0),),
    (("down", 1), ("down", 2),),
    (("out", 0),),
    (("third", "send"),),
    (),
    (("first", "send"),),
    (),
    (("second", "send"),),
    (),
    (),
    (("first", 0),),
    (),
    (("first", 1), ("first", 2),),
    (("second", "twin"),),
    (("third", 0), ("second", 0), ("third", 1),),
    (("second", 1),),
    (),
    (("third", 2), ("second", 2),),
    (),
)


def forward_kernel(
    size,
    hidden_ref,
    dy_hbm,
    w_query,
    w_key,
    w_value,
    w_out,
    w_gate,
    w_up,
    w_down,
    attn_gain_ref,
    mlp_gain_ref,
    query_gain_ref,
    key_gain_ref,
    cos_ref,
    sin_ref,
    start_ref,
    qkv_full,
    out_full,
    first_full,
    second_full,
    down_full,
    n1_full,
    dy_full,
    n2_full,
    n1_turned,
    dy_turned,
    n2_turned,
    act_out,
    first_pair,
    second_pair,
    proj_ref,
    heads_ref,
    mixed_ref,
    lse_ref,
    middle_ref,
    lhs,
    dy_all,
    turned,
    qkv_w,
    out_w,
    qkv_own,
    out_own,
    down_own,
    dy_own,
    wide_own,
    first_own,
    second_own,
    own_rows,
    give,
    got,
    pair,
    far_got,
    us,
    ur,
    ds,
    dr,
    ys,
    yr,
    row_local,
    ts,
    tr,
    token_local,
    load_sem,
    ss,
    sr,
):
    here = Place(size)
    last = here.outer - 1
    length, width = lhs.shape
    lse_ref[...] = jnp.zeros_like(lse_ref)
    rows = length // 4
    units = act_out.shape[1]
    chunk = units // 2
    tail = 256
    heads = mixed_ref.shape[1] // HEAD_DIM
    kv_heads = heads // 2
    ff_part = units // size

    def sems(index):
        return tuple(kind.at[index] for kind in (us, ur, ds, dr, ys, yr, row_local))

    down_rows = pl.ds(pl.multiple_of(here.seq * ff_part, ff_part), ff_part)
    qkv = RowGather(here, qkv_own, qkv_full, sems(0))
    out = HeadGather(here, out_own, out_full, sems(1))
    down = RowGather(
        here,
        down_own,
        down_full,
        sems(2),
        lambda shard: pl.ds(pl.multiple_of(shard * ff_part, ff_part), ff_part),
    )
    first = RowGather(here, first_own, first_full, sems(3))
    cut = 2 * (chunk - tail)
    second = TwinFirstGather(
        here, second_own.at[:, 0:cut], second_full.at[:, :, 0:cut], sems(4), sems(6)
    )
    third = RowGather(
        here, second_own.at[:, cut : 2 * chunk], second_full.at[:, :, cut : 2 * chunk], sems(5)
    )
    n1 = TokenGather(here, own_rows.at[0], n1_full, (ts.at[0], tr.at[0], token_local.at[0]))
    n2 = TokenGather(here, own_rows.at[1], n2_full, (ts.at[1], tr.at[1], token_local.at[1]))
    dy = TokenGather(here, dy_own, dy_full, (ts.at[2], tr.at[2], token_local.at[2]))

    loads = []
    at = 0
    for index, (weight, count) in enumerate(((w_query, heads), (w_key, kv_heads), (w_value, kv_heads))):
        count = count * HEAD_DIM
        source = weight.at[:, pl.ds(pl.multiple_of(here.seq * count, count), count)]
        loads.append(
            pltpu.make_async_copy(source, qkv_own.at[:, at : at + count], load_sem.at[index])
        )
        at += count
    loads.append(pltpu.make_async_copy(w_down.at[down_rows, :], down_own, load_sem.at[3]))
    loads.append(pltpu.make_async_copy(w_out, out_own, load_sem.at[4]))
    loads.append(pltpu.make_async_copy(dy_hbm, dy_own, load_sem.at[5]))
    loads.append(pltpu.make_async_copy(w_gate, wide_own, load_sem.at[6]))
    for load in loads:
        load.start()
    here.greet()
    for load in loads[:3]:
        load.wait()
    qkv.send()

    def norm_rows(source, gain_ref, target):
        @pl.loop(0, rows // 32)
        def _(index):
            part = pl.ds(pl.multiple_of(index * 32, 32), 32)
            values = source[part, :].astype(F32)
            scales = lax.rsqrt(jnp.mean(values * values, axis=-1, keepdims=True) + EPSILON)
            target[part, :] = (values * scales * gain_ref[...]).astype(BF)

    gathers = {"out": out, "down": down, "first": first, "second": second, "third": third}

    def advance(steps):
        for name, step in steps:
            gather = gathers[name]
            if step == "send":
                gather.send()
            elif step == "twin":
                gather.twin()
            elif name == "out":
                gather.step()
            else:
                for distance in range(last * step // 3, last * (step + 1) // 3):
                    gather.step(distance)

    norm_rows(hidden_ref, attn_gain_ref, own_rows.at[0])
    n1.send()
    for load in loads[3:5]:
        load.wait()
    advance(FORWARD_PLAN[0])
    for load in loads[5:]:
        load.wait()

    most = chunk - tail

    def cut_units(side):
        for seq in range(4):

            @pl.when(here.seq == seq)
            def _():
                @pl.loop(0, wide_own.shape[0] // 16)
                def _(index):
                    part = pl.ds(pl.multiple_of(index * 16, 16), 16)

                    def gathered(begin):
                        pieces = [
                            wide_own[part, (block * 4 + seq) * ff_part : (block * 4 + seq + 1) * ff_part]
                            for block in range(begin, begin + size // 2)
                        ]
                        return jnp.concatenate(pieces, axis=1)

                    first_own[part, side * chunk : (side + 1) * chunk] = gathered(0)
                    rest = gathered(size // 2)
                    second_own[part, side * most : (side + 1) * most] = rest[:, 0:most]
                    at = 2 * most + side * tail
                    second_own[part, at : at + tail] = rest[:, most:]

    cut_units(0)
    load_up = pltpu.make_async_copy(w_up, wide_own, load_sem.at[7])
    load_up.start()
    load_up.wait()
    cut_units(1)
    advance(FORWARD_PLAN[1])
    for third_part in range(3):
        for distance in range(last * third_part // 3, last * (third_part + 1) // 3):
            qkv.step(distance)
        advance(FORWARD_PLAN[2 + third_part])
    n1.forward()
    advance(FORWARD_PLAN[5])
    n1.arrive()
    load_lhs = pltpu.make_async_copy(n1_full, lhs, load_sem.at[0])
    load_lhs.start()
    dy.send()
    advance(FORWARD_PLAN[6])
    qkv.arrive()
    load_qkv = pltpu.make_async_copy(qkv_full, qkv_w, load_sem.at[1])
    load_qkv.start()
    advance(FORWARD_PLAN[7])
    load_lhs.wait()
    load_qkv.wait()

    def project(tile):
        weight = qkv_w[:, :, tile * 256 : tile * 256 + 256].reshape(width, 256)
        gain_ref = query_gain_ref if tile < heads // 2 else key_gain_ref

        @pl.loop(0, 4)
        def _(index):
            part = pl.ds(pl.multiple_of(index * rows, rows), rows)
            both = dot(lhs[part, :], weight)
            for side in range(2):
                head = tile * 2 + side
                proj = both[:, side * HEAD_DIM : (side + 1) * HEAD_DIM]
                if head >= heads + kv_heads:
                    heads_ref[head, part, :] = proj.astype(BF)
                    continue
                proj_ref[head, part, :] = proj
                scales = lax.rsqrt(jnp.mean(proj * proj, axis=-1, keepdims=True) + EPSILON)
                gained = proj * scales * gain_ref[...]
                turned = pltpu.roll(gained, HEAD_DIM // 2, 1)
                heads_ref[head, part, :] = (
                    gained * cos_ref[part, :] + turned * sin_ref[part, :]
                ).astype(BF)

    def attend(head):
        pair_head = head // 2
        for block in range(4):
            end = (block + 1) * rows
            part = pl.ds(block * rows, rows)
            scores = contract_cols(
                heads_ref[head, part, :], heads_ref[heads + pair_head, 0:end, :]
            )
            row_place = lax.broadcasted_iota(jnp.int32, (rows, end), 0) + block * rows
            col_place = lax.broadcasted_iota(jnp.int32, (rows, end), 1)
            allowed = (col_place >= start_ref[part, :]) & (col_place <= row_place)
            raised = jnp.where(allowed, jnp.exp(scores * (HEAD_DIM ** (-0.5))), 0.0)
            sums = jnp.sum(raised, axis=-1, keepdims=True)
            mixed = dot(raised.astype(BF), heads_ref[heads + kv_heads + pair_head, 0:end, :])
            mixed = mixed * (1.0 / sums)
            mixed_ref[part, head * HEAD_DIM : (head + 1) * HEAD_DIM] = mixed.astype(BF)
            lse_ref[part, head : head + 1] = jnp.log(sums)

    tiles = (heads + 2 * kv_heads) // 2
    for tile in range(tiles):
        if tile == tiles // 2:
            advance(FORWARD_PLAN[8])
        project(tile)
    advance(FORWARD_PLAN[9])

    zones = width // 512

    def turn(source, target):
        for seq_group in range(4):
            for zone in range(zones):
                at = (seq_group * zones + zone) * 128
                turned[zone * 4 + seq_group] = source[:, at : at + 128].T
        copy = pltpu.make_async_copy(turned, target, load_sem.at[4])
        copy.start()
        return copy

    for head in range(heads):
        attend(head)
        if head == 1:
            dy.forward()
        advance(FORWARD_PLAN[10 + head])
    dy.arrive()
    load_dy = pltpu.make_async_copy(dy_full, dy_all, load_sem.at[0])
    load_dy.start()

    out.arrive()
    load_out = pltpu.make_async_copy(out_full, out_w, load_sem.at[2])
    load_out.start()
    load_out.wait()

    def out_piece(seq, column):
        part = pl.ds(pl.multiple_of(seq * rows, rows), rows)
        weight = out_w[:, :, column]
        return dot(mixed_ref[part, :], weight.reshape(-1, weight.shape[-1]))

    middle_ref[...] = hidden_ref[...].astype(F32)
    token_sum = PieceSum(
        here, out_piece, middle_ref, give, got, pair, far_got, (ss, sr), 512
    )
    token_sum.send()
    advance(FORWARD_PLAN[14])
    token_sum.pass_on()
    token_sum.add_near()
    store = turn(lhs, n1_turned)
    advance(FORWARD_PLAN[15])
    token_sum.add_far()
    norm_rows(middle_ref, mlp_gain_ref, own_rows.at[1])
    n2.send()
    advance(FORWARD_PLAN[16])
    store.wait()
    load_dy.wait()
    store = turn(dy_all, dy_turned)
    advance(FORWARD_PLAN[17])
    n2.forward()
    advance(FORWARD_PLAN[18])
    n2.arrive()
    load_lhs = pltpu.make_async_copy(n2_full, lhs, load_sem.at[3])
    load_lhs.start()
    down.arrive()
    first.arrive()
    load_lhs.wait()

    def feed(gather, begin, count):
        tiles = count // 256
        spot = begin // 256

        def body(gate_w, up_w, down_w, act_ref, gate_grad, up_grad):
            gate_tile = gate_w[...].reshape(width, 256)
            up_tile = up_w[...].reshape(width, 256)
            down_tile = down_w[...]

            @pl.loop(0, 4)
            def _(index):
                part = pl.ds(pl.multiple_of(index * rows, rows), rows)
                gate = dot(lhs[part, :], gate_tile)
                up = dot(lhs[part, :], up_tile)
                act_grad = contract_cols(dy_all[part, :], down_tile)
                sigmoid = jax.nn.sigmoid(gate)
                silu = gate * sigmoid
                act_ref[part, :] = (silu * up).astype(BF)
                gate_grad[part, :] = (
                    act_grad * up * sigmoid * (1.0 + gate * (1.0 - sigmoid))
                ).astype(BF)
                up_grad[part, :] = (act_grad * silu).astype(BF)

        block = gather.whole.shape[:-1] + (256,)
        grads = first_pair if begin < chunk else second_pair
        first_spot = 0 if begin < chunk + 1 else 2 * (begin - chunk) // 256
        pltpu.emit_pipeline(
            body,
            grid=(tiles,),
            in_specs=[
                pl.BlockSpec(block, lambda t: (0, 0, t)),
                pl.BlockSpec(block, lambda t: (0, 0, t + tiles)),
                pl.BlockSpec((256, width), lambda t: (t + spot, 0)),
            ],
            out_specs=[
                pl.BlockSpec((length, 256), lambda t: (0, t + spot)),
                pl.BlockSpec((length, 256), lambda t: (0, t + first_spot)),
                pl.BlockSpec((length, 256), lambda t: (0, t + first_spot + tiles)),
            ],
        )(gather.whole, gather.whole, down_full, act_out, grads, grads)

    feed(first, 0, chunk)
    advance(FORWARD_PLAN[19])
    store.wait()
    store = turn(lhs, n2_turned)
    advance(FORWARD_PLAN[20])
    second.arrive()
    feed(second, chunk, chunk - tail)
    advance(FORWARD_PLAN[21])
    third.arrive()
    feed(third, 2 * chunk - tail, tail)
    store.wait()
    for gather in (qkv, out, first, second, third, down, n1, n2, dy):
        gather.finish()


def forward(hidden, upstream, weights, gains, tables, starts):
    size = lax.axis_size("shard")
    quarter, outer = size // 4, size // 2
    piece, width = hidden.shape
    length = piece * 4
    heads = Q_HEADS // 4
    kv_heads = KV_HEADS // 4
    w_query, _, _, w_out, w_gate, _, w_down = weights
    own = w_query.shape[0]
    qkv_width = (heads + 2 * kv_heads) * HEAD_DIM
    units = w_down.shape[0] // 4 * size

    def shape(*dims, kind=BF):
        return jax.ShapeDtypeStruct(dims, kind)

    results = [
        shape(size, own, qkv_width),
        shape(quarter, *w_out.shape),
        shape(size, own, units),
        shape(size, own, units),
        shape(units, width),
        shape(length, width),
        shape(length, width),
        shape(length, width),
        shape(width // 128, 128, length),
        shape(width // 128, 128, length),
        shape(width // 128, 128, length),
        shape(length, units),
        shape(length, units),
        shape(length, units),
        shape(heads + kv_heads, length, HEAD_DIM, kind=F32),
        shape(heads + 2 * kv_heads, length, HEAD_DIM),
        shape(length, heads * HEAD_DIM),
        shape(length, 128, kind=F32),
        shape(piece, width, kind=F32),
    ]
    dma = pltpu.SemaphoreType.DMA
    return pl.pallas_call(
        functools.partial(forward_kernel, size),
        out_shape=results,
        in_specs=[VMEM] + [ANY] * 8 + [VMEM] * 7,
        out_specs=[ANY] * 14 + [VMEM] * 5,
        scratch_shapes=[
            pltpu.VMEM((length, width), BF),
            pltpu.VMEM((length, width), BF),
            pltpu.VMEM((width // 128, 128, length), BF),
            pltpu.VMEM((size, own, qkv_width), BF),
            pltpu.VMEM((quarter,) + w_out.shape, BF),
            pltpu.VMEM((own, qkv_width), BF),
            pltpu.VMEM(w_out.shape, BF),
            pltpu.VMEM((w_down.shape[0] // 4, width), BF),
            pltpu.VMEM((piece, width), BF),
            pltpu.VMEM(w_gate.shape, BF),
            pltpu.VMEM((own, units), BF),
            pltpu.VMEM((own, units), BF),
            pltpu.VMEM((2, piece, width), BF),
            pltpu.VMEM((2, piece, width), BF),
            pltpu.VMEM((2, piece, width), BF),
            pltpu.VMEM((piece, width), BF),
            pltpu.VMEM((piece, width), BF),
            dma((7, outer)),
            dma((7, outer)),
            dma((7, outer)),
            dma((7, outer)),
            dma((7, outer)),
            dma((7, outer)),
            dma((7,)),
            dma((3, 3)),
            dma((3, 3)),
            dma((3,)),
            dma((8,)),
            dma((3,)),
            dma((3,)),
        ],
        compiler_params=pltpu.CompilerParams(
            collective_id=0, has_side_effects=True, vmem_limit_bytes=VMEM_BYTES
        ),
        name="forward_gather",
    )(
        hidden,
        upstream,
        *weights,
        *gains,
        *tables,
        starts.reshape(length, 1),
    )


def add_rows(target, sources, step=16):
    groups, rows, _ = target.shape

    @pl.loop(0, groups * (rows // step))
    def _(index):
        group = index // (rows // step)
        part = pl.ds(pl.multiple_of(lax.rem(index, rows // step) * step, step), step)
        total = sources[0][group, part, :].astype(F32)
        for source in sources[1:]:
            total = total + source[group, part, :].astype(F32)
        target[group, part, :] = total.astype(target.dtype)


class RowSum:
    def __init__(self, here, give, keep, near, rising, falling, stage, total, sems):
        self.here, self.give, self.keep = here, give, keep
        self.near, self.rising, self.falling = near, rising, falling
        self.stage, self.total = stage, total
        self.ys, self.yr, self.us, self.ur, self.ds, self.dr, self.load = sems
        self.last = here.outer - 1

    def across(self, place):
        return remote(
            self.give.at[place],
            self.near.at[place],
            self.ys.at[place],
            self.yr.at[place],
            self.here.twin,
        )

    def up(self, place):
        peer = self.here.outer_peer(self.here.place + 1)
        return remote(
            self.keep.at[place], self.rising.at[place], self.us.at[place], self.ur.at[place], peer
        )

    def down(self, place):
        peer = self.here.outer_peer(self.here.place - 1)
        return remote(
            self.keep.at[place], self.falling.at[place], self.ds.at[place], self.dr.at[place], peer
        )

    def arrived(self, slot, send, receive):
        remote(slot, slot, send, receive, self.here.twin).wait_recv()

    def compute(self, left, right, tiles, zones, send=True):
        here = self.here
        own = self.give.shape[2]
        per = 128 // (2 * own)
        width = self.give.shape[3]
        step = 256
        for group in range(zones):
            spots = tiles(group)

            @pl.loop(0, width // step)
            def _(index):
                lane = pl.ds(pl.multiple_of(index * step, step), step)
                terms = dot(left(group), right(lane))
                for spot, (zone, seq_group) in enumerate(spots):
                    for sub in range(per):
                        at = spot * 128 + sub * 2 * own
                        even, odd = terms[at : at + own], terms[at + own : at + 2 * own]
                        place = zone * per + sub
                        mine = jnp.where(here.half == 0, even, odd).astype(BF)
                        theirs = jnp.where(here.half == 0, odd, even).astype(BF)
                        self.keep[place, seq_group, :, lane] = mine
                        self.give[place, seq_group, :, lane] = theirs

            for zone in sorted({zone for zone, _ in spots}) if send else ():
                for sub in range(per):
                    self.across(zone * per + sub).start()

    def fold(self, distance):
        here = self.here
        above = here.place + distance
        below = here.place - distance

        def merge(place, line, receive, first):
            near = pltpu.make_async_copy(self.near.at[place], self.stage.at[0], self.load.at[0])
            self.arrived(self.near.at[place], self.ys.at[place], self.yr.at[place])
            near.start()

            @pl.when(first)
            def _():
                near.wait()
                add_rows(self.keep.at[place], [self.keep.at[place], self.stage.at[0]])

            @pl.when(jnp.logical_not(first))
            def _():
                self.arrived(line.at[place], self.us.at[0], receive.at[place])
                far = pltpu.make_async_copy(line.at[place], self.stage.at[1], self.load.at[1])
                far.start()
                near.wait()
                far.wait()
                add_rows(
                    self.keep.at[place], [self.keep.at[place], self.stage.at[0], self.stage.at[1]]
                )

        @pl.when(above <= self.last)
        def _():
            merge(above, self.rising, self.ur, here.place == 0)
            self.up(above).start()

        @pl.when(below >= 0)
        def _():
            merge(below, self.falling, self.dr, here.place == self.last)
            self.down(below).start()

    def finish(self):
        here = self.here
        place = here.place
        self.arrived(self.near.at[place], self.ys.at[place], self.yr.at[place])
        keep = self.keep.at[place]
        near = pltpu.make_async_copy(self.near.at[place], self.stage.at[0], self.load.at[0])
        low = pltpu.make_async_copy(self.rising.at[place], self.stage.at[1], self.load.at[1])
        high = pltpu.make_async_copy(self.falling.at[place], self.stage.at[1], self.load.at[1])
        near.start()

        @pl.when(place > 0)
        def _():
            self.arrived(self.rising.at[place], self.us.at[0], self.ur.at[place])
            low.start()
            low.wait()

        @pl.when(place == 0)
        def _():
            self.arrived(self.falling.at[place], self.ds.at[0], self.dr.at[place])
            high.start()
            high.wait()

        near.wait()

        @pl.when((place > 0) & (place < self.last))
        def _():
            add_rows(keep, [keep, self.stage.at[0], self.stage.at[1]])
            self.arrived(self.falling.at[place], self.ds.at[0], self.dr.at[place])
            high.start()
            high.wait()
            add_rows(self.total, [keep, self.stage.at[1]])

        @pl.when((place == 0) | (place == self.last))
        def _():
            add_rows(self.total, [keep, self.stage.at[0], self.stage.at[1]])

    def sent(self):
        for place in range(self.here.outer):
            self.across(place).wait_send()

    def settle(self):
        here = self.here
        for place in range(here.outer):

            @pl.when(place > here.place)
            def _():
                self.up(place).wait_send()

            @pl.when(place < here.place)
            def _():
                self.down(place).wait_send()


class LineSum:
    def __init__(self, here, terms, rising, falling, stage, sems):
        self.here, self.terms, self.stage = here, terms, stage
        self.rising, self.falling = rising, falling
        self.us, self.ur, self.ds, self.dr, self.load = sems
        self.last = here.outer - 1

    def up(self, place):
        peer = self.here.outer_peer(self.here.place + 1)
        return remote(
            self.terms.at[place], self.rising.at[place], self.us.at[place], self.ur.at[place], peer
        )

    def down(self, place):
        peer = self.here.outer_peer(self.here.place - 1)
        return remote(
            self.terms.at[place], self.falling.at[place], self.ds.at[place], self.dr.at[place], peer
        )

    def merge(self, place, line, receive):
        slot = line.at[place]
        remote(slot, slot, self.us.at[0], receive.at[place], self.here.twin).wait_recv()
        copy = pltpu.make_async_copy(slot, self.stage.at[0], self.load.at[0])
        copy.start()
        copy.wait()
        add_rows(self.terms.at[place], [self.terms.at[place], self.stage.at[0]])

    def fold(self, distance):
        here = self.here
        above = here.place + distance
        below = here.place - distance

        @pl.when(above <= self.last)
        def _():
            @pl.when(here.place > 0)
            def _():
                self.merge(above, self.rising, self.ur)

            self.up(above).start()

        @pl.when(below >= 0)
        def _():
            @pl.when(here.place < self.last)
            def _():
                self.merge(below, self.falling, self.dr)

            self.down(below).start()

    def gather(self):
        place = self.here.place

        @pl.when(place > 0)
        def _():
            self.merge(place, self.rising, self.ur)

        @pl.when(place < self.last)
        def _():
            self.merge(place, self.falling, self.dr)

    def settle(self):
        here = self.here
        for place in range(here.outer):

            @pl.when(place > here.place)
            def _():
                self.up(place).wait_send()

            @pl.when(place < here.place)
            def _():
                self.down(place).wait_send()


class LineFirstSum(RowSum):
    def __init__(self, here, give, keep, near, lines, stage, total, sems, twin_sems):
        self.here, self.give, self.keep = here, give, keep
        self.near, self.stage, self.total = near, stage, total
        self.ys, self.yr, self.load = sems[0], sems[1], sems[6]
        self.lines = [
            LineSum(here, terms, rising, falling, stage, kinds[2:])
            for terms, (rising, falling), kinds in (
                (give, lines[0], twin_sems),
                (keep, lines[1], sems),
            )
        ]

    def fold(self, distance):
        for line in self.lines:
            line.fold(distance)

    def pass_on(self):
        self.lines[0].gather()
        self.across(self.here.place).start()
        self.lines[1].gather()

    def finish(self):
        place = self.here.place
        self.arrived(self.near.at[place], self.ys.at[place], self.yr.at[place])
        near = pltpu.make_async_copy(self.near.at[place], self.stage.at[0], self.load.at[0])
        near.start()
        near.wait()
        add_rows(self.total, [self.keep.at[place], self.stage.at[0]])

    def sent(self):
        self.across(self.here.place).wait_send()

    def settle(self):
        for line in self.lines:
            line.settle()


class RowSpread:
    def __init__(self, here, rows, whole, sems):
        self.here, self.rows, self.whole = here, rows, whole
        self.send_sems, self.recv_sems, self.local = sems

    def copy(self, amount):
        seq = lax.rem(self.here.seq + amount, 4)
        return remote(
            self.rows.at[seq],
            self.whole.at[self.here.seq],
            self.send_sems.at[amount - 1],
            self.recv_sems.at[amount - 1],
            {"seq": seq},
        )

    def keep(self):
        seq = self.here.seq
        return pltpu.make_async_copy(self.rows.at[seq], self.whole.at[seq], self.local)

    def send(self):
        for amount in (2, 3, 1):
            self.copy(amount).start()
        self.keep().start()

    def arrive(self):
        for amount in (1, 2, 3):
            self.copy(amount).wait_recv()
        self.keep().wait()

    def finish(self):
        for amount in (1, 2, 3):
            self.copy(amount).wait_send()


class TokenSum:
    def __init__(self, here, part, got, pair, far_got, base, sems):
        self.here, self.part, self.got, self.pair = here, part, got, pair
        self.far_got, self.base = far_got, base
        self.send_sems, self.recv_sems = sems
        self.rows = part.shape[0] // 4

    def piece(self, seq):
        return pl.ds(pl.multiple_of(seq * self.rows, self.rows), self.rows)

    def to_mate(self, index):
        here = self.here
        chip = here.chip if index else 1 - here.chip
        seq = chip * 2 + 1 - here.core
        return remote(
            self.part.at[self.piece(seq), :],
            self.got.at[index],
            self.send_sems.at[index],
            self.recv_sems.at[index],
            here.mate,
        )

    def to_far(self):
        return remote(
            self.pair, self.far_got, self.send_sems.at[2], self.recv_sems.at[2], self.here.far
        )

    def send(self):
        self.to_mate(0).start()
        self.to_mate(1).start()

    def loop(self, body):
        @pl.loop(0, self.rows // 32)
        def _(index):
            body(index * 32)

    def pass_on(self):
        self.to_mate(0).wait_recv()
        begin = self.here.far_seq * self.rows

        def body(at):
            part = pl.ds(pl.multiple_of(at, 32), 32)
            source = pl.ds(pl.multiple_of(begin + at, 32), 32)
            total = self.part[source, :].astype(F32) + self.got[0, part, :].astype(F32)
            self.pair[part, :] = total.astype(BF)

        self.loop(body)
        self.to_far().start()

    def add_near(self):
        self.to_mate(1).wait_recv()
        begin = self.here.seq * self.rows

        def body(at):
            part = pl.ds(pl.multiple_of(at, 32), 32)
            source = pl.ds(pl.multiple_of(begin + at, 32), 32)
            self.base[part, :] += self.part[source, :].astype(F32) + self.got[1, part, :].astype(F32)

        self.loop(body)
        self.to_mate(0).wait_send()
        self.to_mate(1).wait_send()

    def add_far(self):
        self.to_far().wait_recv()

        def body(at):
            part = pl.ds(pl.multiple_of(at, 32), 32)
            self.base[part, :] += self.far_got[part, :].astype(F32)

        self.loop(body)
        self.to_far().wait_send()


class GainSum:
    def __init__(self, here, parts, arrived, sems):
        self.here, self.parts, self.arrived = here, parts, arrived
        self.send_sems, self.recv_sems = sems
        self.peers = [here.mate, here.far, here.twin] + here.line_peers()

    def copy(self, index):
        return remote(
            self.parts.at[index],
            self.arrived.at[index],
            self.send_sems.at[index],
            self.recv_sems.at[index],
            self.peers[index],
        )

    def start(self):
        self.copy(0).start()

    def hop(self, index):
        self.copy(index).wait()
        self.parts[index + 1] = self.parts[index] + self.arrived[index]
        if index + 1 < len(self.peers):
            self.copy(index + 1).start()


PLAN = (
    (("down", 3),),
    (("down", 2),),
    (),
    (),
    (("down", 1),),
    (),
    (("first", 3), ("first", 2),),
    (),
    (("first", 1),),
    (),
    (("out", 3), ("out", 2),),
    (),
    (("second", 3), ("second", 2), ("first", "finish"),),
    (("down", "pass"),),
    (("out", 1), ("qkv", 3), ("qkv", 2), ("second", 1),),
    (("out", "pass"), ("qkv", 1),),
    (("second", "finish"), ("out", "finish"), ("down", "finish"), ("qkv", "finish"),),
)


def backward_kernel(
    size,
    n1_hbm,
    dy_hbm,
    n2_hbm,
    act_hbm,
    first_hbm,
    second_hbm,
    proj_hbm,
    heads_ref,
    mixed_ref,
    lse_ref,
    middle_hbm,
    hidden_hbm,
    dy_own,
    qkv_full,
    out_full,
    first_full,
    second_full,
    down_full,
    attn_gain_ref,
    mlp_gain_ref,
    query_gain_ref,
    key_gain_ref,
    cos_ref,
    sin_ref,
    start_ref,
    grad_in,
    gains_out,
    grad_out,
    hidden_out,
    down_rows,
    first_rows,
    second_rows,
    qkv_rows,
    da_hbm,
    near_mlp,
    rising_mlp,
    falling_mlp,
    rising_twin,
    falling_twin,
    near_qkv,
    rising_qkv,
    falling_qkv,
    near_out,
    rising_out,
    falling_out,
    rising_out_twin,
    falling_out_twin,
    lhs,
    turned,
    first_r,
    second_r,
    give,
    keep,
    give_out,
    keep_out,
    stage,
    stage_out,
    dout_ref,
    da_own,
    got,
    far_got,
    pair,
    middle_grad,
    proj_buf,
    lse_t,
    delta,
    delta_t,
    dk_sum,
    dv_sum,
    gain_rows,
    gain_got,
    ys,
    yr,
    us,
    ur,
    ds,
    dr,
    fold_load,
    spread_s,
    spread_r,
    spread_l,
    sum_s,
    sum_r,
    ts,
    tr,
    token_local,
    gs,
    gr,
    load_sem,
    credit,
):
    here = Place(size)
    length, width = lhs.shape
    rows = length // 4
    units = first_r.shape[1]
    chunk = units // 2
    ff_part = units // size
    heads = mixed_ref.shape[1] // HEAD_DIM
    kv_heads = heads // 2
    qkv_width = qkv_full.shape[2]
    last = here.outer - 1
    zones = width // 512
    scale = HEAD_DIM ** (-0.5)

    def load(source, target, index):
        copy = pltpu.make_async_copy(source, target, load_sem.at[index])
        copy.start()
        return copy

    def sems(index):
        return tuple(kind.at[index] for kind in (ys, yr, us, ur, ds, dr, fold_load))

    down = LineFirstSum(
        here,
        give.at[2],
        keep.at[0],
        near_mlp.at[0],
        ((rising_twin, falling_twin), (rising_mlp.at[0], falling_mlp.at[0])),
        stage,
        keep.at[0, here.place],
        sems(0),
        sems(5),
    )
    first, second = [
        RowSum(
            here,
            give.at[2 - index],
            keep.at[index],
            near_mlp.at[index],
            rising_mlp.at[index],
            falling_mlp.at[index],
            stage,
            keep.at[index, here.place],
            sems(index),
        )
        for index in (1, 2)
    ]
    thin = slice(0, qkv_width)
    qkv = RowSum(
        here,
        give.at[1, :, :, :, thin],
        second_r.at[:, :, :, thin],
        near_qkv,
        rising_qkv,
        falling_qkv,
        stage.at[:, :, :, thin],
        second_r.at[here.place, :, :, thin],
        sems(3),
    )
    out = LineFirstSum(
        here,
        give_out,
        keep_out,
        near_out,
        ((rising_out_twin, falling_out_twin), (rising_out, falling_out)),
        stage_out,
        grad_out,
        sems(4),
        sems(6),
    )

    def spread(index, job, whole):
        return RowSpread(
            here, job.total, whole, (spread_s.at[index], spread_r.at[index], spread_l.at[index])
        )

    spread_down = spread(0, down, down_rows)
    spread_first = spread(1, first, first_rows)
    spread_second = spread(2, second, second_rows)
    spread_qkv = spread(3, qkv, qkv_rows)

    def token_sum(index, base):
        return TokenSum(
            here, lhs, got, pair, far_got, base, (sum_s.at[index], sum_r.at[index])
        )

    sum_mlp = token_sum(0, middle_grad)
    sum_hidden = token_sum(1, grad_in)
    sum_attn = token_sum(2, grad_in)
    da = TokenGather(here, da_own, da_hbm, (ts, tr, token_local.at[0]))

    def model_tiles(group):
        return [(group, seq_group) for seq_group in range(4)]

    def first_columns(lane):
        return first_r[:, lane]

    def model_left(group):
        return turned[group * 4 : group * 4 + 4].reshape(512, length)

    jobs = {"down": down, "first": first, "second": second, "out": out, "qkv": qkv}
    spreads = {
        "down": spread_down,
        "first": spread_first,
        "second": spread_second,
        "qkv": spread_qkv,
    }

    def advance(steps):
        for name, step in steps:
            job = jobs[name]
            if step == "pass":
                job.pass_on()
            elif step == "finish":
                job.finish()
                if name in spreads:
                    spreads[name].send()
            else:
                for distance in range(last * step // 3, last * (step - 1) // 3, -1):
                    job.fold(distance)

    load_turned = load(dy_hbm, turned, 0)
    load_act = load(act_hbm, first_r, 1)
    load_middle = load(middle_hbm, grad_in, 2)
    load_dy = load(dy_own, da_own, 4)
    load_second = load(second_hbm, second_r, 3)
    here.greet(wide=True)
    load_turned.wait()
    load_act.wait()
    down.compute(model_left, first_columns, model_tiles, zones, send=False)
    advance(PLAN[0])
    load_turned = load(n2_hbm, turned, 0)
    load_first = load(first_hbm, first_r, 1)
    load_first.wait()
    load_second.wait()

    own = width // size
    slabs = 256 // own

    def dn2_body(first_w, second_w):
        lane = pl.ds(pl.multiple_of(pl.program_id(0) * 256, 256), 256)
        first_tile = first_w[...].reshape(256, units)
        second_tile = second_w[...].reshape(256, units)

        @pl.loop(0, 4)
        def _(index):
            part = pl.ds(pl.multiple_of(index * rows, rows), rows)
            total = contract_cols(first_r[part, :], first_tile)
            blocks = pl.ds(index * (here.outer // 4), here.outer // 4)
            second_rows = second_r[blocks].reshape(rows, units)
            total = total + contract_cols(second_rows, second_tile)
            lhs[part, lane] = total.astype(BF)

    slab = pl.BlockSpec((slabs, own, units), lambda t: (t, 0, 0))
    pltpu.emit_pipeline(dn2_body, grid=(width // 256,), in_specs=[slab, slab])(
        first_full, second_full
    )
    sum_mlp.send()
    middle_grad[...] = jnp.zeros_like(middle_grad)
    load_turned.wait()
    advance(PLAN[1])
    sum_mlp.pass_on()
    sum_mlp.add_near()
    first.compute(model_left, first_columns, model_tiles, zones)
    load_act = load(act_hbm, first_r, 1)
    advance(PLAN[2])
    sum_mlp.add_far()

    load_middle.wait()
    load_dy.wait()
    gain_rows[0] = jnp.zeros_like(gain_rows[0])
    narrow = 16

    @pl.loop(0, rows // narrow)
    def _(index):
        part = pl.ds(pl.multiple_of(index * narrow, narrow), narrow)
        values = grad_in[part, :]
        scales = lax.rsqrt(jnp.mean(values * values, axis=-1, keepdims=True) + EPSILON)
        normed = values * scales
        update = middle_grad[part, :]
        gain_rows[0, 1:2, :] += jnp.sum(update * normed, axis=0, keepdims=True)
        upper = update * mlp_gain_ref[...]
        inner = jnp.mean(upper * normed, axis=-1, keepdims=True)
        grad = da_own[part, :].astype(F32) + scales * (upper - normed * inner)
        middle_grad[part, :] = grad
        da_own[part, :] = grad.astype(BF)

    da.send()
    advance(PLAN[3])
    second.compute(
        model_left, lambda lane: second_r[:, :, :, lane].reshape(length, -1), model_tiles, zones
    )
    advance(PLAN[4])

    def hidden_body(weight):
        lane = pl.ds(pl.multiple_of(pl.program_id(0) * 256, 256), 256)
        tile = weight[...]

        @pl.loop(0, 4)
        def _(index):
            part = pl.ds(pl.multiple_of(index * rows, rows), rows)
            lhs[part, lane] = dot(first_r[part, :], tile).astype(BF)

    load_act.wait()
    pltpu.emit_pipeline(
        hidden_body,
        grid=(width // 256,),
        in_specs=[pl.BlockSpec((units, 256), lambda t: (0, t))],
    )(down_full)
    da.mate_arrived()
    sum_hidden.send()
    da.forward()
    advance(PLAN[5])
    sum_hidden.pass_on()
    sum_hidden.add_near()
    advance(PLAN[6])
    da.rest_arrived()
    da.finish()
    load_lhs = load(da_hbm, lhs, 0)
    load_own = load(hidden_hbm, da_own, 2)
    load_lhs.wait()

    def dout_body(weight):
        lane = pl.ds(pl.multiple_of(pl.program_id(0) * 256, 256), 256)
        tile = weight[...].reshape(256, width)

        @pl.loop(0, 4)
        def _(index):
            part = pl.ds(pl.multiple_of(index * rows, rows), rows)
            dout_ref[part, lane] = contract_cols(lhs[part, :], tile).astype(BF)

    out_blocks, out_rows = out_full.shape[:2]
    pltpu.emit_pipeline(
        dout_body,
        grid=(out_blocks * out_rows // 256,),
        in_specs=[pl.BlockSpec((256 // out_rows, out_rows, width), lambda t: (t, 0, 0))],
    )(out_full)

    for head in range(heads):
        turned[head] = mixed_ref[:, head * HEAD_DIM : (head + 1) * HEAD_DIM].T
    out.compute(
        lambda group: turned[0:heads].reshape(heads * HEAD_DIM, length),
        lambda lane: lhs[:, lane],
        lambda group: [(zone, 0) for zone in range(heads)],
        1,
        send=False,
    )
    load_turned = load(n1_hbm, turned, 0)
    sum_hidden.add_far()
    for index, peer in enumerate((here.mate, here.far)):
        pl.semaphore_signal(credit.at[index], inc=1, device_id=peer, device_id_type=MESH)

    @pl.loop(0, rows // 32)
    def _(index):
        part = pl.ds(pl.multiple_of(index * 32, 32), 32)
        pair[part, :] = grad_in[part, :].astype(BF)

    store_hidden = load(pair, hidden_out, 1)
    advance(PLAN[7])

    lse_t[...] = lse_ref[...].T[0:8]
    delta[...] = jnp.zeros_like(delta)
    for head in range(heads):
        lane = slice(head * HEAD_DIM, (head + 1) * HEAD_DIM)
        terms = dout_ref[:, lane].astype(F32) * mixed_ref[:, lane].astype(F32)
        delta[:, head : head + 1] = jnp.sum(terms, axis=-1, keepdims=True)
    delta_t[...] = delta[...].T[0:8]
    def through_norm(grad, head, part, gain_ref, gain_row):
        proj = proj_buf[part, :]
        scales = lax.rsqrt(jnp.mean(proj * proj, axis=-1, keepdims=True) + EPSILON)
        normed = proj * scales
        grad = grad.astype(F32)
        upper = grad * cos_ref[part, :] - pltpu.roll(grad, HEAD_DIM // 2, 1) * sin_ref[part, :]
        gain_rows[0, 2:3, gain_row * HEAD_DIM : (gain_row + 1) * HEAD_DIM] += jnp.sum(
            upper * normed, axis=0, keepdims=True
        )
        upper = upper * gain_ref[...]
        inner = jnp.mean(upper * normed, axis=-1, keepdims=True)
        result = (scales * (upper - normed * inner)).astype(BF)
        first_r[part, head * HEAD_DIM : (head + 1) * HEAD_DIM] = result

    for head in range(heads):
        pair_head = head // 2
        load_proj = load(proj_hbm.at[head], proj_buf, 4)
        if head % 2 == 0:
            dk_sum[...] = jnp.zeros_like(dk_sum)
            dv_sum[...] = jnp.zeros_like(dv_sum)
        load_proj.wait()
        for block in range(4):
            end = (block + 1) * rows
            part = pl.ds(block * rows, rows)
            queries = heads_ref[head, part, :]
            keys = heads_ref[heads + pair_head, 0:end, :]
            values = heads_ref[heads + kv_heads + pair_head, 0:end, :]
            out_grad = dout_ref[part, head * HEAD_DIM : (head + 1) * HEAD_DIM]
            scores = contract_cols(keys, queries)
            key_place = lax.broadcasted_iota(jnp.int32, (end, rows), 0)
            query_place = lax.broadcasted_iota(jnp.int32, (end, rows), 1) + block * rows
            allowed = (key_place >= start_ref[:, part]) & (key_place <= query_place)
            weights = jnp.exp(scores * scale - lse_t[head : head + 1, part])
            weights = jnp.where(allowed, weights, 0.0)
            weight_grad = contract_cols(values, out_grad)
            inner = delta_t[head : head + 1, part]
            score_grad = (weights * (weight_grad - inner)).astype(BF)
            dk_sum[0:end, :] += dot(score_grad, queries) * scale
            dv_sum[0:end, :] += dot(weights.astype(BF), out_grad)
            query_grad = (contract_rows(score_grad, keys) * scale).astype(BF)
            through_norm(query_grad, head, part, query_gain_ref, 0)
        if head % 2:
            key = heads + pair_head
            value_at = (heads + kv_heads + pair_head) * HEAD_DIM
            load(proj_hbm.at[key], proj_buf, 4).wait()

            @pl.loop(0, 4)
            def _(index):
                part = pl.ds(pl.multiple_of(index * rows, rows), rows)
                through_norm(dk_sum[part, :].astype(BF), key, part, key_gain_ref, 1)
                first_r[part, value_at : value_at + HEAD_DIM] = dv_sum[part, :].astype(BF)

        advance(PLAN[8 + head])

    load_turned.wait()
    first.sent()
    store_hidden.wait()
    proj_grads = first_r.at[:, 0:qkv_width]
    qkv.compute(model_left, first_columns, model_tiles, zones)
    advance(PLAN[12])

    def dn1_body(weight):
        lane = pl.ds(pl.multiple_of(pl.program_id(0) * 256, 256), 256)
        tile = weight[...].reshape(256, qkv_width)

        @pl.loop(0, 4)
        def _(index):
            part = pl.ds(pl.multiple_of(index * rows, rows), rows)
            lhs[part, lane] = contract_cols(proj_grads[part, :], tile).astype(BF)

    pltpu.emit_pipeline(
        dn1_body,
        grid=(width // 256,),
        in_specs=[pl.BlockSpec((slabs, own, qkv_width), lambda t: (t, 0, 0))],
    )(qkv_full)
    grad_in[...] = jnp.zeros_like(grad_in)
    pl.semaphore_wait(credit.at[0], 1)
    pl.semaphore_wait(credit.at[1], 1)
    sum_attn.send()
    advance(PLAN[13])
    sum_attn.pass_on()
    sum_attn.add_near()
    advance(PLAN[14])
    sum_attn.add_far()
    load_own.wait()

    @pl.loop(0, rows // narrow)
    def _(index):
        part = pl.ds(pl.multiple_of(index * narrow, narrow), narrow)
        values = da_own[part, :].astype(F32)
        scales = lax.rsqrt(jnp.mean(values * values, axis=-1, keepdims=True) + EPSILON)
        normed = values * scales
        update = grad_in[part, :]
        gain_rows[0, 0:1, :] += jnp.sum(update * normed, axis=0, keepdims=True)
        upper = update * attn_gain_ref[...]
        inner = jnp.mean(upper * normed, axis=-1, keepdims=True)
        grad_in[part, :] = middle_grad[part, :] + scales * (upper - normed * inner)

    gain_sum = GainSum(here, gain_rows, gain_got, (gs, gr))
    gain_sum.start()
    advance(PLAN[15])
    hops = list(range(len(gain_sum.peers)))
    for name, step in PLAN[16]:
        advance([(name, step)])
        if hops:
            gain_sum.hop(hops.pop(0))
    for index in hops:
        gain_sum.hop(index)
    gains_out[...] = gain_rows[gain_rows.shape[0] - 1]
    for spread_rows in spreads.values():
        spread_rows.arrive()
    for job in (down, second, out, qkv):
        job.sent()
    for job in jobs.values():
        job.settle()
    for job in spreads.values():
        job.finish()


def backward(saved, weights, own, gains, tables, starts):
    size = lax.axis_size("shard")
    outer = size // 2
    (n1, dy, n2, act, first, second, proj, heads_all, mixed, lse, middle) = saved
    length, width = heads_all.shape[1], middle.shape[1]
    piece = length // 4
    units = act.shape[1]
    qkv_width = weights[0].shape[2]
    rows = width // (4 * size)
    q_width = mixed.shape[1]

    def shape(*dims, kind=BF):
        return jax.ShapeDtypeStruct(dims, kind)

    results = [
        shape(piece, width, kind=F32),
        shape(8, width, kind=F32),
        shape(1, rows, width, kind=F32),
        shape(piece, width),
        shape(4, rows, units),
        shape(4, rows, units),
        shape(4, rows, units),
        shape(4, rows, qkv_width),
        shape(length, width),
    ]
    results += [shape(3, outer, 4, rows, units)] * 3
    results += [shape(outer, 4, rows, units)] * 2
    results += [shape(outer, 4, rows, qkv_width)] * 3
    results += [shape(outer, 1, rows, width)] * 5
    dma = pltpu.SemaphoreType.DMA
    hops = 3 + outer.bit_length() - 1
    vmem = pltpu.VMEM
    return pl.pallas_call(
        functools.partial(backward_kernel, size),
        out_shape=results,
        in_specs=[ANY] * 7 + [VMEM] * 3 + [ANY] * 8 + [VMEM] * 7,
        out_specs=[VMEM] * 3 + [ANY] * (len(results) - 3),
        scratch_shapes=[
            vmem((length, width), BF),
            vmem((width // 128, 128, length), BF),
            vmem((length, units), BF),
            vmem((outer, 4, rows, units), BF),
            vmem((3, outer, 4, rows, units), BF),
            vmem((3, outer, 4, rows, units), BF),
            vmem((outer, 1, rows, width), BF),
            vmem((outer, 1, rows, width), BF),
            vmem((2, 4, rows, units), BF),
            vmem((2, 1, rows, width), BF),
            vmem((length, q_width), BF),
            vmem((piece, width), BF),
            vmem((2, piece, width), BF),
            vmem((piece, width), BF),
            vmem((piece, width), BF),
            vmem((piece, width), F32),
            vmem((length, HEAD_DIM), F32),
            vmem((8, length), F32),
            vmem((length, 128), F32),
            vmem((8, length), F32),
            vmem((length, HEAD_DIM), F32),
            vmem((length, HEAD_DIM), F32),
            vmem((hops + 1, 8, width), F32),
            vmem((hops, 8, width), F32),
            dma((7, outer)),
            dma((7, outer)),
            dma((7, outer)),
            dma((7, outer)),
            dma((7, outer)),
            dma((7, outer)),
            dma((7, 3)),
            dma((4, 3)),
            dma((4, 3)),
            dma((4,)),
            dma((3, 3)),
            dma((3, 3)),
            dma((3,)),
            dma((3,)),
            dma((1,)),
            dma((hops,)),
            dma((hops,)),
            dma((5,)),
            pltpu.SemaphoreType.REGULAR((2,)),
        ],
        compiler_params=pltpu.CompilerParams(
            collective_id=1, has_side_effects=True, vmem_limit_bytes=VMEM_BYTES
        ),
        name="backward_sums",
    )(
        n1,
        dy,
        n2,
        act,
        first,
        second.reshape(outer, 4, rows, units),
        proj,
        heads_all,
        mixed,
        lse,
        middle,
        *own,
        *weights,
        *gains,
        *tables,
        starts.reshape(1, length),
    )


def finish_kernel(
    size,
    grad_in,
    gains,
    grad_out,
    hidden_out,
    down_rows,
    first_rows,
    second_rows,
    qkv_rows,
    grad_in_out,
    grad_out_out,
    hidden_out_out,
    grad_query,
    grad_key,
    grad_value,
    grad_gate,
    grad_up,
    grad_down,
    attn_gain,
    mlp_gain,
    head_gains,
    grad_in_buf,
    grad_out_buf,
    hidden_buf,
    down_buf,
    first_buf,
    second_buf,
    qkv_buf,
    query_buf,
    key_buf,
    value_buf,
    gate_buf,
    up_buf,
    wide_buf,
    load_sems,
    store_sems,
):
    units = down_buf.shape[2]
    chunk = units // 2
    ff_part = units // size
    most, tail = chunk - 256, 256
    stores = []

    def load(source, target, index):
        copy = pltpu.make_async_copy(source, target, load_sems.at[index])
        copy.start()
        return copy

    def store(source, target):
        copy = pltpu.make_async_copy(source, target, store_sems.at[len(stores)])
        copy.start()
        stores.append(copy)

    loads = [
        load(source, target, index)
        for index, (source, target) in enumerate(
            (
                (down_rows, down_buf),
                (first_rows, first_buf),
                (second_rows, second_buf),
                (qkv_rows, qkv_buf),
                (grad_in, grad_in_buf),
                (hidden_out, hidden_buf),
                (grad_out, grad_out_buf),
            )
        )
    ]

    def place(read, target):
        @pl.loop(0, target.shape[0] // 16)
        def _(index):
            part = pl.ds(pl.multiple_of(index * 16, 16), 16)
            values = [read(seq, part).astype(F32) for seq in range(4)]
            for begin in range(0, size, size // 8):
                pieces = [
                    values[seq][:, block * ff_part : (block + 1) * ff_part]
                    for block in range(begin, begin + size // 8)
                    for seq in range(4)
                ]
                lane = slice(begin * 4 * ff_part, (begin + size // 8) * 4 * ff_part)
                target[part, lane] = jnp.concatenate(pieces, axis=1)

    def side(index):
        at = 2 * most + index * tail

        def read(seq, part):
            return jnp.concatenate(
                [
                    first_buf[seq, part, index * chunk : (index + 1) * chunk],
                    second_buf[seq, part, index * most : (index + 1) * most],
                    second_buf[seq, part, at : at + tail],
                ],
                axis=1,
            )

        return read

    loads[0].wait()
    place(lambda seq, part: down_buf[seq, part, :], wide_buf)
    store(wide_buf, grad_down)
    loads[1].wait()
    loads[2].wait()
    place(side(0), gate_buf)
    store(gate_buf, grad_gate)
    place(side(1), up_buf)
    store(up_buf, grad_up)
    loads[4].wait()
    store(grad_in_buf, grad_in_out)
    loads[5].wait()
    store(hidden_buf, hidden_out_out)
    loads[6].wait()
    store(grad_out_buf, grad_out_out)
    loads[3].wait()
    at = 0
    for buf, target in ((query_buf, grad_query), (key_buf, grad_key), (value_buf, grad_value)):
        count = buf.shape[1] // 4
        for seq in range(4):
            buf[:, seq * count : (seq + 1) * count] = qkv_buf[seq, :, at : at + count].astype(F32)
        at += count
        store(buf, target)
    attn_gain[...] = gains[0:1, :]
    mlp_gain[...] = gains[1:2, :]
    head_gains[...] = gains[2:3, 0 : 2 * HEAD_DIM]
    for copy in stores:
        copy.wait()


def finish(grad_in, gains, grad_out, hidden_out, down_rows, first_rows, second_rows, qkv_rows):
    size = lax.axis_size("shard")
    piece, width = grad_in.shape
    rows, units = down_rows.shape[1:]
    qkv_width = qkv_rows.shape[2]

    def shape(*dims, kind=F32):
        return jax.ShapeDtypeStruct(dims, kind)

    results = [
        shape(piece, width),
        shape(1, rows, width),
        shape(piece, width, kind=BF),
        shape(rows, 2 * qkv_width),
        shape(rows, qkv_width),
        shape(rows, qkv_width),
        shape(rows, 4 * units),
        shape(rows, 4 * units),
        shape(rows, 4 * units),
        shape(1, width),
        shape(1, width),
        shape(1, 2 * HEAD_DIM),
    ]
    return pl.pallas_call(
        functools.partial(finish_kernel, size),
        out_shape=results,
        in_specs=[ANY, VMEM] + [ANY] * 6,
        out_specs=[ANY] * 9 + [VMEM] * 3,
        scratch_shapes=[
            pltpu.VMEM((piece, width), F32),
            pltpu.VMEM((1, rows, width), F32),
            pltpu.VMEM((piece, width), BF),
            pltpu.VMEM((4, rows, units), BF),
            pltpu.VMEM((4, rows, units), BF),
            pltpu.VMEM((4, rows, units), BF),
            pltpu.VMEM((4, rows, qkv_width), BF),
            pltpu.VMEM((rows, 2 * qkv_width), F32),
            pltpu.VMEM((rows, qkv_width), F32),
            pltpu.VMEM((rows, qkv_width), F32),
            pltpu.VMEM((rows, 4 * units), F32),
            pltpu.VMEM((rows, 4 * units), F32),
            pltpu.VMEM((rows, 4 * units), F32),
            pltpu.SemaphoreType.DMA((7,)),
            pltpu.SemaphoreType.DMA((9,)),
        ],
        compiler_params=pltpu.CompilerParams(vmem_limit_bytes=VMEM_BYTES),
        name="finish",
    )(grad_in, gains, grad_out, hidden_out, down_rows, first_rows, second_rows, qkv_rows)


def local(
    hidden_in,
    segment_ids,
    norm_attn_gain,
    w_query,
    w_key,
    w_value,
    query_gain,
    key_gain,
    w_out,
    norm_mlp_gain,
    w_gate,
    w_up,
    w_down,
    out_cotangent,
):
    length = hidden_in.shape[1] * 4
    segment = segment_ids[0]
    places = jnp.arange(length, dtype=jnp.int32)
    starts = jnp.sum((segment[None, :] < segment[:, None]).astype(jnp.int32), axis=1)
    cosine, sine = rotary_tables(places - starts)
    signs = jnp.where(jnp.arange(HEAD_DIM) < HEAD_DIM // 2, -1.0, 1.0).astype(F32)
    tables = (cosine, sine * signs)
    gains = (norm_attn_gain[None], norm_mlp_gain[None], query_gain[None], key_gain[None])
    results = forward(
        hidden_in[0],
        out_cotangent[0],
        (w_query, w_key, w_value, w_out, w_gate, w_up, w_down),
        gains,
        tables,
        starts,
    )
    (
        grad_in,
        grad_out,
        hidden_out,
        grad_query,
        grad_key,
        grad_value,
        grad_gate,
        grad_up,
        grad_down,
        attn_gain,
        mlp_gain,
        head_gains,
    ) = finish(
        *backward(
            results[8:],
            results[:5],
            (hidden_in[0], out_cotangent[0]),
            gains,
            tables,
            starts,
        )[:8]
    )
    return (
        hidden_out[None],
        grad_in[None],
        attn_gain[0],
        grad_query,
        grad_key,
        grad_value,
        head_gains[0, :HEAD_DIM],
        head_gains[0, HEAD_DIM:],
        grad_out[0],
        mlp_gain[0],
        grad_gate,
        grad_up,
        grad_down.T,
    )


def solution(mesh):
    return jax.shard_map(
        local,
        mesh=mesh,
        in_specs=(
            P("shard", "seq", None),
            P("shard", None),
            P(),
            P("shard", None),
            P("shard", None),
            P("shard", None),
            P(),
            P(),
            P("shard", None),
            P(),
            P("shard", None),
            P("shard", None),
            P("shard", None),
            P("shard", "seq", None),
        ),
        out_specs=(
            P("shard", "seq", None),
            P("shard", "seq", None),
            P(),
            P(("seq", "shard"), None),
            P(("seq", "shard"), None),
            P(("seq", "shard"), None),
            P(),
            P(),
            P(("seq", "shard"), None),
            P(),
            P(("seq", "shard"), None),
            P(("seq", "shard"), None),
            P(None, ("seq", "shard")),
        ),
        check_vma=False,
    )
```

```python
import functools

import jax
import jax.numpy as jnp
import numpy as np
from jax import lax
from jax.experimental import pallas as pl
from jax.experimental.pallas import tpu as pltpu
from jax.sharding import PartitionSpec as P

Q_HEADS = 16
KV_HEADS = 8
HEAD_DIM = 128
EPSILON = 1e-06
ROPE_BASE = 1000000.0
NEGATIVE = -1e30
BF = jnp.bfloat16
F32 = jnp.float32
MESH = pl.DeviceIdType.MESH
ANY = pl.BlockSpec(memory_space=pl.ANY)
VMEM = pl.BlockSpec(memory_space=pltpu.VMEM)
VMEM_BYTES = 62 * 1024 * 1024


def dot(left, right):
    return jnp.dot(left, right, preferred_element_type=F32)


def contract_rows(left, right):
    return lax.dot_general(left, right, (((0,), (0,)), ((), ())), preferred_element_type=F32)


def contract_cols(left, right):
    return lax.dot_general(left, right, (((1,), (1,)), ((), ())), preferred_element_type=F32)


class Place:
    def __init__(self, size):
        self.size = size
        self.outer = size // 2
        self.quarter = size // 4
        self.seq = lax.axis_index("seq")
        self.shard = lax.axis_index("shard")
        self.chip = self.seq // 2
        self.core = lax.rem(self.seq, 2)
        self.place = self.shard // 2
        self.half = lax.rem(self.shard, 2)
        self.far_seq = lax.rem(self.seq + 2, 4)
        self.mate_seq = self.chip * 2 + 1 - self.core
        self.far = {"seq": self.far_seq}
        self.mate = {"seq": self.mate_seq}
        self.twin_shard = self.place * 2 + 1 - self.half
        self.twin = {"shard": self.twin_shard}

    def outer_peer(self, place):
        return {"shard": place * 2 + self.half}

    def line_peers(self):
        peers = []
        step = 1
        while step < self.outer:
            sign = 1 - 2 * lax.rem(self.place // step, 2)
            peers.append(self.outer_peer(self.place + sign * step))
            step *= 2
        return peers

    def greet(self, wide=False):
        barrier = pltpu.get_barrier_semaphore()
        last = self.outer - 1

        def signal(peer):
            pl.semaphore_signal(barrier, inc=1, device_id=peer, device_id_type=MESH)

        peers = [self.far, self.mate, self.twin]
        if wide:
            peers += [{"seq": 3 - self.seq}] + self.line_peers()[1:]
        for peer in peers:
            signal(peer)

        @pl.when(self.place < last)
        def _():
            signal(self.outer_peer(self.place + 1))

        @pl.when(self.place > 0)
        def _():
            signal(self.outer_peer(self.place - 1))

        inner = ((self.place > 0) & (self.place < last)).astype(jnp.int32)
        pl.semaphore_wait(barrier, len(peers) + 1 + inner)


def remote(source, target, send, receive, peer):
    return pltpu.make_async_remote_copy(
        src_ref=source,
        dst_ref=target,
        send_sem=send,
        recv_sem=receive,
        device_id=peer,
        device_id_type=MESH,
    )


class LineGather:
    def __init__(self, here, own, slot, sems):
        self.here, self.own, self.slot = here, own, slot
        self.us, self.ur, self.ds, self.dr = sems
        self.last = here.outer - 1

    def up(self, distance):
        here = self.here
        slot = self.slot(here.place - distance)
        source = slot if distance else self.own
        peer = here.outer_peer(here.place + 1)
        return remote(source, slot, self.us.at[distance], self.ur.at[distance], peer)

    def down(self, distance):
        here = self.here
        slot = self.slot(here.place + distance)
        source = slot if distance else self.own
        peer = here.outer_peer(here.place - 1)
        return remote(source, slot, self.ds.at[distance], self.dr.at[distance], peer)

    def send(self):
        here = self.here

        @pl.when(here.place < self.last)
        def _():
            self.up(0).start()

        @pl.when(here.place > 0)
        def _():
            self.down(0).start()

    def step(self, distance, arrived=lambda place: None):
        here = self.here
        below = here.place - 1 - distance
        above = here.place + 1 + distance

        @pl.when(below >= 0)
        def _():
            slot = self.slot(below)
            remote(slot, slot, self.us.at[0], self.ur.at[distance], here.twin).wait_recv()

            @pl.when(here.place < self.last)
            def _():
                self.up(distance + 1).start()

            arrived(below)

        @pl.when(above <= self.last)
        def _():
            slot = self.slot(above)
            remote(slot, slot, self.ds.at[0], self.dr.at[distance], here.twin).wait_recv()

            @pl.when(here.place > 0)
            def _():
                self.down(distance + 1).start()

            arrived(above)

    def finish(self):
        here = self.here
        for distance in range(self.last):

            @pl.when((here.place - distance >= 0) & (here.place < self.last))
            def _():
                self.up(distance).wait_send()

            @pl.when((here.place + distance <= self.last) & (here.place > 0))
            def _():
                self.down(distance).wait_send()


class RowGather:
    def __init__(self, here, own, whole, sems, spot=lambda shard: shard):
        self.here, self.own, self.whole, self.spot = here, own, whole, spot
        self.ys, self.yr, self.local = sems[4:]
        self.line = LineGather(here, own, self.mine, sems[:4])

    def mine(self, place):
        return self.whole.at[self.spot(place * 2 + self.here.half)]

    def theirs(self, place):
        return self.whole.at[self.spot(place * 2 + 1 - self.here.half)]

    def keep(self):
        return pltpu.make_async_copy(self.own, self.mine(self.here.place), self.local)

    def across(self, place, own=False):
        slot = self.mine(place)
        source = self.own if own else slot
        return remote(source, slot, self.ys.at[place], self.yr.at[place], self.here.twin)

    def arrived(self, place):
        slot = self.theirs(place)
        remote(slot, slot, self.ys.at[place], self.yr.at[place], self.here.twin).wait_recv()

    def send(self):
        self.line.send()
        self.across(self.here.place, own=True).start()
        self.keep().start()

    def step(self, distance):
        self.line.step(distance, lambda place: self.across(place).start())

    def arrive(self):
        self.keep().wait()
        for place in range(self.here.outer):
            self.arrived(place)

    def finish(self):
        self.line.finish()
        for place in range(self.here.outer):
            self.across(place).wait_send()


class TwinFirstGather(RowGather):
    def __init__(self, here, own, whole, sems, twin_sems):
        super().__init__(here, own, whole, sems)
        self.lines = [
            self.line,
            LineGather(here, self.theirs(here.place), self.theirs, twin_sems[:4]),
        ]

    def twin(self):
        self.arrived(self.here.place)
        self.lines[1].send()

    def step(self, distance):
        for line in self.lines:
            line.step(distance)

    def arrive(self):
        self.keep().wait()

    def finish(self):
        for line in self.lines:
            line.finish()
        self.across(self.here.place, own=True).wait_send()


class HeadGather:
    def __init__(self, here, own, whole, sems):
        self.here, self.own, self.whole = here, own, whole
        self.us, self.zr, self.ds, _, self.ys, self.yr, self.local = sems
        self.last = here.outer - 1
        self.count = here.quarter // 2
        self.first = here.seq * self.count
        self.mine = here.place - self.first
        self.inside = (self.mine >= 0) & (self.mine < self.count)

    def slot(self, index):
        return self.whole.at[index * 2 + self.here.half]

    def keep(self):
        return pltpu.make_async_copy(self.own, self.slot(self.mine), self.local)

    def up(self, index, own=False):
        slot = self.slot(index)
        peer = self.here.outer_peer(self.here.place + 1)
        return remote(self.own if own else slot, slot, self.us.at[index], self.zr.at[index], peer)

    def down(self, index, own=False):
        slot = self.slot(index)
        peer = self.here.outer_peer(self.here.place - 1)
        return remote(self.own if own else slot, slot, self.ds.at[index], self.zr.at[index], peer)

    def across(self, index):
        slot = self.slot(index)
        return remote(slot, slot, self.ys.at[index], self.yr.at[index], self.here.twin)

    def send(self):
        @pl.when(self.inside)
        def _():
            self.keep().start()

            @pl.when(self.here.place < self.last)
            def _():
                self.up(self.mine, own=True).start()

            @pl.when(self.here.place > 0)
            def _():
                self.down(self.mine, own=True).start()

    def step(self):
        here = self.here

        @pl.when(self.inside)
        def _():
            self.keep().wait()

        for index in range(self.count):
            slot = self.slot(index)
            arrival = remote(slot, slot, self.us.at[0], self.zr.at[index], here.twin)

            @pl.when(self.mine > index)
            def _():
                arrival.wait_recv()

                @pl.when(here.place < self.last)
                def _():
                    self.up(index).start()

            @pl.when(self.mine < index)
            def _():
                arrival.wait_recv()

                @pl.when(here.place > 0)
                def _():
                    self.down(index).start()

            self.across(index).start()

    def arrive(self):
        for index in range(self.count):
            slot = self.whole.at[index * 2 + 1 - self.here.half]
            remote(
                slot, slot, self.ys.at[index], self.yr.at[index], self.here.twin
            ).wait_recv()

    def finish(self):
        here = self.here
        for index in range(self.count):

            @pl.when((self.mine >= index) & (here.place < self.last))
            def _():
                self.up(index).wait_send()

            @pl.when((self.mine <= index) & (here.place > 0))
            def _():
                self.down(index).wait_send()

            self.across(index).wait_send()


class TokenGather:
    def __init__(self, here, own, whole, sems):
        self.here, self.own, self.whole = here, own, whole
        self.send_sems, self.recv_sems, self.local = sems
        self.rows = whole.shape[0] // 4

    def slot(self, seq):
        return self.whole.at[pl.ds(pl.multiple_of(seq * self.rows, self.rows), self.rows), :]

    def keep(self):
        return pltpu.make_async_copy(self.own, self.slot(self.here.seq), self.local)

    def copy(self, index):
        here = self.here
        slot = self.slot(here.far_seq if index == 2 else here.seq)
        return remote(
            slot if index == 2 else self.own,
            slot,
            self.send_sems.at[index],
            self.recv_sems.at[index],
            here.far if index == 0 else here.mate,
        )

    def send(self):
        self.copy(0).start()
        self.copy(1).start()
        self.keep().start()

    def forward(self):
        self.copy(0).wait_recv()
        self.copy(2).start()

    def mate_arrived(self):
        self.copy(1).wait_recv()

    def rest_arrived(self):
        self.copy(2).wait_recv()
        self.keep().wait()

    def arrive(self):
        self.mate_arrived()
        self.rest_arrived()

    def finish(self):
        for index in range(3):
            self.copy(index).wait_send()


class PieceSum:
    def __init__(self, here, piece, base, give, got, pair, far_got, sems, step):
        self.here, self.piece, self.base, self.step = here, piece, base, step
        self.give, self.got, self.pair, self.far_got = give, got, pair, far_got
        self.send_sems, self.recv_sems = sems

    def to_mate(self, index):
        return remote(
            self.give.at[index],
            self.got.at[index],
            self.send_sems.at[index],
            self.recv_sems.at[index],
            self.here.mate,
        )

    def to_far(self):
        return remote(
            self.pair, self.far_got, self.send_sems.at[2], self.recv_sems.at[2], self.here.far
        )

    def columns(self, body):
        step = self.step

        @pl.loop(0, self.pair.shape[1] // step)
        def _(index):
            body(pl.ds(pl.multiple_of(index * step, step), step))

    def send(self):
        here = self.here
        for index, chip in enumerate((1 - here.chip, here.chip)):
            seq = chip * 2 + 1 - here.core

            def fill(column, index=index, seq=seq):
                self.give[index, :, column] = self.piece(seq, column).astype(BF)

            self.columns(fill)
            self.to_mate(index).start()

    def pass_on(self):
        self.to_mate(0).wait_recv()

        def fill(column):
            term = self.piece(self.here.far_seq, column) + self.got[0, :, column].astype(F32)
            self.pair[:, column] = term.astype(BF)

        self.columns(fill)
        self.to_far().start()

    def add_near(self):
        self.to_mate(1).wait_recv()

        def fill(column):
            term = self.piece(self.here.seq, column) + self.got[1, :, column].astype(F32)
            self.base[:, column] += term

        self.columns(fill)

    def add_far(self):
        self.to_far().wait_recv()

        def fill(column):
            self.base[:, column] += self.far_got[:, column].astype(F32)

        self.columns(fill)
        for copy in (self.to_mate(0), self.to_mate(1), self.to_far()):
            copy.wait_send()


FORWARD_PLAN = (
    (("down", "send"),),
    (),
    (("out", "send"),),
    (("down", 0),),
    (("down", 1), ("down", 2),),
    (("out", 0),),
    (("third", "send"),),
    (),
    (("first", "send"),),
    (),
    (("second", "send"),),
    (),
    (),
    (("first", 0),),
    (),
    (("first", 1), ("first", 2),),
    (("second", "twin"),),
    (("third", 0), ("second", 0), ("third", 1),),
    (("second", 1),),
    (),
    (("third", 2), ("second", 2),),
    (),
)


def forward_kernel(
    size,
    hidden_ref,
    dy_hbm,
    w_query,
    w_key,
    w_value,
    w_out,
    w_gate,
    w_up,
    w_down,
    attn_gain_ref,
    mlp_gain_ref,
    query_gain_ref,
    key_gain_ref,
    inverse_ref,
    segment_ref,
    qkv_full,
    out_full,
    first_full,
    second_full,
    down_full,
    n1_full,
    dy_full,
    n2_full,
    n1_turned,
    dy_turned,
    n2_turned,
    act_out,
    first_pair,
    second_pair,
    proj_ref,
    heads_ref,
    mixed_ref,
    lse_ref,
    middle_ref,
    cos_ref,
    sin_ref,
    start_row,
    lhs,
    dy_all,
    turned,
    qkv_w,
    out_w,
    qkv_own,
    out_own,
    down_own,
    dy_own,
    wide_own,
    first_own,
    second_own,
    own_rows,
    give,
    got,
    pair,
    far_got,
    us,
    ur,
    ds,
    dr,
    ys,
    yr,
    row_local,
    ts,
    tr,
    token_local,
    load_sem,
    ss,
    sr,
    start_ref,
    turned_ids,
):
    here = Place(size)
    last = here.outer - 1
    length, width = lhs.shape
    lse_ref[...] = jnp.zeros_like(lse_ref)
    rows = length // 4
    units = act_out.shape[1]
    chunk = units // 2
    tail = 256
    heads = mixed_ref.shape[1] // HEAD_DIM
    kv_heads = heads // 2
    ff_part = units // size

    def sems(index):
        return tuple(kind.at[index] for kind in (us, ur, ds, dr, ys, yr, row_local))

    down_rows = pl.ds(pl.multiple_of(here.seq * ff_part, ff_part), ff_part)
    qkv = RowGather(here, qkv_own, qkv_full, sems(0))
    out = HeadGather(here, out_own, out_full, sems(1))
    down = RowGather(
        here,
        down_own,
        down_full,
        sems(2),
        lambda shard: pl.ds(pl.multiple_of(shard * ff_part, ff_part), ff_part),
    )
    first = RowGather(here, first_own, first_full, sems(3))
    cut = 2 * (chunk - tail)
    second = TwinFirstGather(
        here, second_own.at[:, 0:cut], second_full.at[:, :, 0:cut], sems(4), sems(6)
    )
    third = RowGather(
        here, second_own.at[:, cut : 2 * chunk], second_full.at[:, :, cut : 2 * chunk], sems(5)
    )
    n1 = TokenGather(here, own_rows.at[0], n1_full, (ts.at[0], tr.at[0], token_local.at[0]))
    n2 = TokenGather(here, own_rows.at[1], n2_full, (ts.at[1], tr.at[1], token_local.at[1]))
    dy = TokenGather(here, dy_own, dy_full, (ts.at[2], tr.at[2], token_local.at[2]))

    loads = []
    at = 0
    for index, (weight, count) in enumerate(((w_query, heads), (w_key, kv_heads), (w_value, kv_heads))):
        count = count * HEAD_DIM
        source = weight.at[:, pl.ds(pl.multiple_of(here.seq * count, count), count)]
        loads.append(
            pltpu.make_async_copy(source, qkv_own.at[:, at : at + count], load_sem.at[index])
        )
        at += count
    loads.append(pltpu.make_async_copy(w_down.at[down_rows, :], down_own, load_sem.at[3]))
    loads.append(pltpu.make_async_copy(w_out, out_own, load_sem.at[4]))
    loads.append(pltpu.make_async_copy(dy_hbm, dy_own, load_sem.at[5]))
    loads.append(pltpu.make_async_copy(w_gate, wide_own, load_sem.at[6]))
    for load in loads:
        load.start()
    here.greet()
    for load in loads[:3]:
        load.wait()
    qkv.send()

    def norm_rows(source, gain_ref, target):
        @pl.loop(0, rows // 32)
        def _(index):
            part = pl.ds(pl.multiple_of(index * 32, 32), 32)
            values = source[part, :].astype(F32)
            scales = lax.rsqrt(jnp.mean(values * values, axis=-1, keepdims=True) + EPSILON)
            target[part, :] = (values * scales * gain_ref[...]).astype(BF)

    gathers = {"out": out, "down": down, "first": first, "second": second, "third": third}

    def advance(steps):
        for name, step in steps:
            gather = gathers[name]
            if step == "send":
                gather.send()
            elif step == "twin":
                gather.twin()
            elif name == "out":
                gather.step()
            else:
                for distance in range(last * step // 3, last * (step + 1) // 3):
                    gather.step(distance)

    norm_rows(hidden_ref, attn_gain_ref, own_rows.at[0])
    n1.send()
    for load in loads[3:5]:
        load.wait()
    advance(FORWARD_PLAN[0])
    for load in loads[5:]:
        load.wait()

    most = chunk - tail

    def cut_units(side):
        for seq in range(4):

            @pl.when(here.seq == seq)
            def _():
                @pl.loop(0, wide_own.shape[0] // 16)
                def _(index):
                    part = pl.ds(pl.multiple_of(index * 16, 16), 16)

                    def gathered(begin):
                        pieces = [
                            wide_own[part, (block * 4 + seq) * ff_part : (block * 4 + seq + 1) * ff_part]
                            for block in range(begin, begin + size // 2)
                        ]
                        return jnp.concatenate(pieces, axis=1)

                    first_own[part, side * chunk : (side + 1) * chunk] = gathered(0)
                    rest = gathered(size // 2)
                    second_own[part, side * most : (side + 1) * most] = rest[:, 0:most]
                    at = 2 * most + side * tail
                    second_own[part, at : at + tail] = rest[:, most:]

    def rotation():
        ids = segment_ref[...].astype(F32)
        turned_ids[...] = jnp.broadcast_to(ids, (128, length)).T
        lane = lax.broadcasted_iota(jnp.int32, (128, 128), 1)

        @pl.loop(0, length // 128)
        def _(index):
            part = pl.ds(pl.multiple_of(index * 128, 128), 128)
            own_ids = turned_ids[part, :]
            count = jnp.zeros((128, 128), F32)
            for at in range(0, length, 128):
                count = count + jnp.where(
                    segment_ref[:, at : at + 128].astype(F32) < own_ids, 1.0, 0.0
                )
            starts = jnp.sum(count, axis=-1, keepdims=True)
            start_ref[part, :] = starts.astype(jnp.int32)
            starts = jnp.broadcast_to(starts, (128, 128))
            turned_ids[part, :] = starts
            places = lax.broadcasted_iota(jnp.int32, (128, 128), 0) + index * 128
            angles = (places.astype(F32) - starts) * inverse_ref[...]
            cos_ref[part, :] = jnp.cos(angles)
            sine = jnp.sin(angles)
            sin_ref[part, :] = jnp.where(lane < HEAD_DIM // 2, -sine, sine)

        start_row[...] = turned_ids[...].T[0:1].astype(jnp.int32)

    cut_units(0)
    load_up = pltpu.make_async_copy(w_up, wide_own, load_sem.at[7])
    load_up.start()
    load_up.wait()
    cut_units(1)
    advance(FORWARD_PLAN[1])
    for third_part in range(3):
        for distance in range(last * third_part // 3, last * (third_part + 1) // 3):
            qkv.step(distance)
        advance(FORWARD_PLAN[2 + third_part])
        if third_part == 0:
            rotation()
    n1.forward()
    advance(FORWARD_PLAN[5])
    n1.arrive()
    load_lhs = pltpu.make_async_copy(n1_full, lhs, load_sem.at[0])
    load_lhs.start()
    dy.send()
    advance(FORWARD_PLAN[6])
    qkv.arrive()
    load_qkv = pltpu.make_async_copy(qkv_full, qkv_w, load_sem.at[1])
    load_qkv.start()
    advance(FORWARD_PLAN[7])
    load_lhs.wait()
    load_qkv.wait()

    def project(tile):
        weight = qkv_w[:, :, tile * 256 : tile * 256 + 256].reshape(width, 256)
        gain_ref = query_gain_ref if tile < heads // 2 else key_gain_ref

        @pl.loop(0, 4)
        def _(index):
            part = pl.ds(pl.multiple_of(index * rows, rows), rows)
            both = dot(lhs[part, :], weight)
            for side in range(2):
                head = tile * 2 + side
                proj = both[:, side * HEAD_DIM : (side + 1) * HEAD_DIM]
                if head >= heads + kv_heads:
                    heads_ref[head, part, :] = proj.astype(BF)
                    continue
                proj_ref[head, part, :] = proj
                scales = lax.rsqrt(jnp.mean(proj * proj, axis=-1, keepdims=True) + EPSILON)
                gained = proj * scales * gain_ref[...]
                turned = pltpu.roll(gained, HEAD_DIM // 2, 1)
                heads_ref[head, part, :] = (
                    gained * cos_ref[part, :] + turned * sin_ref[part, :]
                ).astype(BF)

    def attend(head):
        pair_head = head // 2
        for block in range(4):
            end = (block + 1) * rows
            part = pl.ds(block * rows, rows)
            scores = contract_cols(
                heads_ref[head, part, :], heads_ref[heads + pair_head, 0:end, :]
            )
            row_place = lax.broadcasted_iota(jnp.int32, (rows, end), 0) + block * rows
            col_place = lax.broadcasted_iota(jnp.int32, (rows, end), 1)
            allowed = (col_place >= start_ref[part, :]) & (col_place <= row_place)
            raised = jnp.where(allowed, jnp.exp(scores * (HEAD_DIM ** (-0.5))), 0.0)
            sums = jnp.sum(raised, axis=-1, keepdims=True)
            mixed = dot(raised.astype(BF), heads_ref[heads + kv_heads + pair_head, 0:end, :])
            mixed = mixed * (1.0 / sums)
            mixed_ref[part, head * HEAD_DIM : (head + 1) * HEAD_DIM] = mixed.astype(BF)
            lse_ref[part, head : head + 1] = jnp.log(sums)

    tiles = (heads + 2 * kv_heads) // 2
    for tile in range(tiles):
        if tile == tiles // 2:
            advance(FORWARD_PLAN[8])
        project(tile)
    advance(FORWARD_PLAN[9])

    zones = width // 512

    def turn(source, target):
        for seq_group in range(4):
            for zone in range(zones):
                at = (seq_group * zones + zone) * 128
                turned[zone * 4 + seq_group] = source[:, at : at + 128].T
        copy = pltpu.make_async_copy(turned, target, load_sem.at[4])
        copy.start()
        return copy

    for head in range(heads):
        attend(head)
        if head == 1:
            dy.forward()
        advance(FORWARD_PLAN[10 + head])
    dy.arrive()
    load_dy = pltpu.make_async_copy(dy_full, dy_all, load_sem.at[0])
    load_dy.start()

    out.arrive()
    load_out = pltpu.make_async_copy(out_full, out_w, load_sem.at[2])
    load_out.start()
    load_out.wait()

    def out_piece(seq, column):
        part = pl.ds(pl.multiple_of(seq * rows, rows), rows)
        weight = out_w[:, :, column]
        return dot(mixed_ref[part, :], weight.reshape(-1, weight.shape[-1]))

    middle_ref[...] = hidden_ref[...].astype(F32)
    token_sum = PieceSum(
        here, out_piece, middle_ref, give, got, pair, far_got, (ss, sr), 512
    )
    token_sum.send()
    advance(FORWARD_PLAN[14])
    token_sum.pass_on()
    token_sum.add_near()
    store = turn(lhs, n1_turned)
    advance(FORWARD_PLAN[15])
    token_sum.add_far()
    norm_rows(middle_ref, mlp_gain_ref, own_rows.at[1])
    n2.send()
    advance(FORWARD_PLAN[16])
    store.wait()
    load_dy.wait()
    store = turn(dy_all, dy_turned)
    advance(FORWARD_PLAN[17])
    n2.forward()
    advance(FORWARD_PLAN[18])
    n2.arrive()
    load_lhs = pltpu.make_async_copy(n2_full, lhs, load_sem.at[3])
    load_lhs.start()
    down.arrive()
    first.arrive()
    load_lhs.wait()

    def feed(gather, begin, count):
        tiles = count // 256
        spot = begin // 256

        def body(gate_w, up_w, down_w, act_ref, gate_grad, up_grad):
            gate_tile = gate_w[...].reshape(width, 256)
            up_tile = up_w[...].reshape(width, 256)
            down_tile = down_w[...]

            @pl.loop(0, 4)
            def _(index):
                part = pl.ds(pl.multiple_of(index * rows, rows), rows)
                gate = dot(lhs[part, :], gate_tile)
                up = dot(lhs[part, :], up_tile)
                act_grad = contract_cols(dy_all[part, :], down_tile)
                sigmoid = jax.nn.sigmoid(gate)
                silu = gate * sigmoid
                act_ref[part, :] = (silu * up).astype(BF)
                gate_grad[part, :] = (
                    act_grad * up * sigmoid * (1.0 + gate * (1.0 - sigmoid))
                ).astype(BF)
                up_grad[part, :] = (act_grad * silu).astype(BF)

        block = gather.whole.shape[:-1] + (256,)
        grads = first_pair if begin < chunk else second_pair
        first_spot = 0 if begin < chunk + 1 else 2 * (begin - chunk) // 256
        pltpu.emit_pipeline(
            body,
            grid=(tiles,),
            in_specs=[
                pl.BlockSpec(block, lambda t: (0, 0, t)),
                pl.BlockSpec(block, lambda t: (0, 0, t + tiles)),
                pl.BlockSpec((256, width), lambda t: (t + spot, 0)),
            ],
            out_specs=[
                pl.BlockSpec((length, 256), lambda t: (0, t + spot)),
                pl.BlockSpec((length, 256), lambda t: (0, t + first_spot)),
                pl.BlockSpec((length, 256), lambda t: (0, t + first_spot + tiles)),
            ],
        )(gather.whole, gather.whole, down_full, act_out, grads, grads)

    feed(first, 0, chunk)
    advance(FORWARD_PLAN[19])
    store.wait()
    store = turn(lhs, n2_turned)
    advance(FORWARD_PLAN[20])
    second.arrive()
    feed(second, chunk, chunk - tail)
    advance(FORWARD_PLAN[21])
    third.arrive()
    feed(third, 2 * chunk - tail, tail)
    store.wait()
    for gather in (qkv, out, first, second, third, down, n1, n2, dy):
        gather.finish()


def forward(hidden, upstream, weights, gains, segment):
    size = lax.axis_size("shard")
    quarter, outer = size // 4, size // 2
    piece, width = hidden.shape
    length = piece * 4
    heads = Q_HEADS // 4
    kv_heads = KV_HEADS // 4
    w_query, _, _, w_out, w_gate, _, w_down = weights
    own = w_query.shape[0]
    qkv_width = (heads + 2 * kv_heads) * HEAD_DIM
    units = w_down.shape[0] // 4 * size

    def shape(*dims, kind=BF):
        return jax.ShapeDtypeStruct(dims, kind)

    results = [
        shape(size, own, qkv_width),
        shape(quarter, *w_out.shape),
        shape(size, own, units),
        shape(size, own, units),
        shape(units, width),
        shape(length, width),
        shape(length, width),
        shape(length, width),
        shape(width // 128, 128, length),
        shape(width // 128, 128, length),
        shape(width // 128, 128, length),
        shape(length, units),
        shape(length, units),
        shape(length, units),
        shape(heads + kv_heads, length, HEAD_DIM, kind=F32),
        shape(heads + 2 * kv_heads, length, HEAD_DIM),
        shape(length, heads * HEAD_DIM),
        shape(length, 128, kind=F32),
        shape(piece, width, kind=F32),
        shape(length, HEAD_DIM, kind=F32),
        shape(length, HEAD_DIM, kind=F32),
        shape(1, length, kind=jnp.int32),
    ]
    powers = np.arange(HEAD_DIM // 2, dtype=np.float32) * np.float32(2.0) / np.float32(HEAD_DIM)
    inverse = np.float32(ROPE_BASE) ** -powers
    dma = pltpu.SemaphoreType.DMA
    return pl.pallas_call(
        functools.partial(forward_kernel, size),
        out_shape=results,
        in_specs=[VMEM] + [ANY] * 8 + [VMEM] * 6,
        out_specs=[ANY] * 14 + [VMEM] * 8,
        scratch_shapes=[
            pltpu.VMEM((length, width), BF),
            pltpu.VMEM((length, width), BF),
            pltpu.VMEM((width // 128, 128, length), BF),
            pltpu.VMEM((size, own, qkv_width), BF),
            pltpu.VMEM((quarter,) + w_out.shape, BF),
            pltpu.VMEM((own, qkv_width), BF),
            pltpu.VMEM(w_out.shape, BF),
            pltpu.VMEM((w_down.shape[0] // 4, width), BF),
            pltpu.VMEM((piece, width), BF),
            pltpu.VMEM(w_gate.shape, BF),
            pltpu.VMEM((own, units), BF),
            pltpu.VMEM((own, units), BF),
            pltpu.VMEM((2, piece, width), BF),
            pltpu.VMEM((2, piece, width), BF),
            pltpu.VMEM((2, piece, width), BF),
            pltpu.VMEM((piece, width), BF),
            pltpu.VMEM((piece, width), BF),
            dma((7, outer)),
            dma((7, outer)),
            dma((7, outer)),
            dma((7, outer)),
            dma((7, outer)),
            dma((7, outer)),
            dma((7,)),
            dma((3, 3)),
            dma((3, 3)),
            dma((3,)),
            dma((8,)),
            dma((3,)),
            dma((3,)),
            pltpu.VMEM((length, 1), jnp.int32),
            pltpu.VMEM((length, 128), F32),
        ],
        compiler_params=pltpu.CompilerParams(
            collective_id=0, has_side_effects=True, vmem_limit_bytes=VMEM_BYTES
        ),
        name="forward_gather",
    )(
        hidden,
        upstream,
        *weights,
        *gains,
        jnp.asarray(np.concatenate([inverse, inverse])[None], F32),
        segment[None],
    )


def add_rows(target, sources, step=16):
    groups, rows, _ = target.shape

    @pl.loop(0, groups * (rows // step))
    def _(index):
        group = index // (rows // step)
        part = pl.ds(pl.multiple_of(lax.rem(index, rows // step) * step, step), step)
        total = sources[0][group, part, :].astype(F32)
        for source in sources[1:]:
            total = total + source[group, part, :].astype(F32)
        target[group, part, :] = total.astype(target.dtype)


class RowSum:
    def __init__(self, here, give, keep, near, rising, falling, stage, total, sems):
        self.here, self.give, self.keep = here, give, keep
        self.near, self.rising, self.falling = near, rising, falling
        self.stage, self.total = stage, total
        self.ys, self.yr, self.us, self.ur, self.ds, self.dr, self.load = sems
        self.last = here.outer - 1

    def across(self, place):
        return remote(
            self.give.at[place],
            self.near.at[place],
            self.ys.at[place],
            self.yr.at[place],
            self.here.twin,
        )

    def up(self, place):
        peer = self.here.outer_peer(self.here.place + 1)
        return remote(
            self.keep.at[place], self.rising.at[place], self.us.at[place], self.ur.at[place], peer
        )

    def down(self, place):
        peer = self.here.outer_peer(self.here.place - 1)
        return remote(
            self.keep.at[place], self.falling.at[place], self.ds.at[place], self.dr.at[place], peer
        )

    def arrived(self, slot, send, receive):
        remote(slot, slot, send, receive, self.here.twin).wait_recv()

    def fold(self, distance):
        here = self.here
        above = here.place + distance
        below = here.place - distance

        def merge(place, line, receive, first):
            near = pltpu.make_async_copy(self.near.at[place], self.stage.at[0], self.load.at[0])
            self.arrived(self.near.at[place], self.ys.at[place], self.yr.at[place])
            near.start()

            @pl.when(first)
            def _():
                near.wait()
                add_rows(self.keep.at[place], [self.keep.at[place], self.stage.at[0]])

            @pl.when(jnp.logical_not(first))
            def _():
                self.arrived(line.at[place], self.us.at[0], receive.at[place])
                far = pltpu.make_async_copy(line.at[place], self.stage.at[1], self.load.at[1])
                far.start()
                near.wait()
                far.wait()
                add_rows(
                    self.keep.at[place], [self.keep.at[place], self.stage.at[0], self.stage.at[1]]
                )

        @pl.when(above <= self.last)
        def _():
            merge(above, self.rising, self.ur, here.place == 0)
            self.up(above).start()

        @pl.when(below >= 0)
        def _():
            merge(below, self.falling, self.dr, here.place == self.last)
            self.down(below).start()

    def finish(self):
        here = self.here
        place = here.place
        self.arrived(self.near.at[place], self.ys.at[place], self.yr.at[place])
        keep = self.keep.at[place]
        near = pltpu.make_async_copy(self.near.at[place], self.stage.at[0], self.load.at[0])
        low = pltpu.make_async_copy(self.rising.at[place], self.stage.at[1], self.load.at[1])
        high = pltpu.make_async_copy(self.falling.at[place], self.stage.at[1], self.load.at[1])
        near.start()

        @pl.when(place > 0)
        def _():
            self.arrived(self.rising.at[place], self.us.at[0], self.ur.at[place])
            low.start()
            low.wait()

        @pl.when(place == 0)
        def _():
            self.arrived(self.falling.at[place], self.ds.at[0], self.dr.at[place])
            high.start()
            high.wait()

        near.wait()

        @pl.when((place > 0) & (place < self.last))
        def _():
            add_rows(keep, [keep, self.stage.at[0], self.stage.at[1]])
            self.arrived(self.falling.at[place], self.ds.at[0], self.dr.at[place])
            high.start()
            high.wait()
            add_rows(self.total, [keep, self.stage.at[1]])

        @pl.when((place == 0) | (place == self.last))
        def _():
            add_rows(self.total, [keep, self.stage.at[0], self.stage.at[1]])

    def sent(self):
        for place in range(self.here.outer):
            self.across(place).wait_send()

    def settle(self):
        here = self.here
        for place in range(here.outer):

            @pl.when(place > here.place)
            def _():
                self.up(place).wait_send()

            @pl.when(place < here.place)
            def _():
                self.down(place).wait_send()


def compute_terms(here, give, keep, left, right, tiles, orders, senders):
    own = give.shape[2]
    per = 128 // (2 * own)
    step = 256
    for group, done in orders:
        spots = tiles(group)

        @pl.loop(0, give.shape[3] // step)
        def _(index):
            lane = pl.ds(pl.multiple_of(index * step, step), step)
            terms = dot(left(group), right(lane))
            for spot, (zone, seq_group) in enumerate(spots):
                for sub in range(per):
                    at = spot * 128 + sub * 2 * own
                    even, odd = terms[at : at + own], terms[at + own : at + 2 * own]
                    place = zone * per + sub
                    mine = jnp.where(here.half == 0, even, odd).astype(BF)
                    theirs = jnp.where(here.half == 0, odd, even).astype(BF)
                    keep[place, seq_group, :, lane] = mine
                    give[place, seq_group, :, lane] = theirs

        for zone in done:
            for sub in range(per):
                for sender in senders:
                    sender.across(zone * per + sub).start()


class LineSum:
    def __init__(self, here, terms, rising, falling, stage, sems):
        self.here, self.terms, self.stage = here, terms, stage
        self.rising, self.falling = rising, falling
        self.us, self.ur, self.ds, self.dr, self.load = sems
        self.last = here.outer - 1

    def up(self, place):
        peer = self.here.outer_peer(self.here.place + 1)
        return remote(
            self.terms.at[place], self.rising.at[place], self.us.at[place], self.ur.at[place], peer
        )

    def down(self, place):
        peer = self.here.outer_peer(self.here.place - 1)
        return remote(
            self.terms.at[place], self.falling.at[place], self.ds.at[place], self.dr.at[place], peer
        )

    def merge(self, place, line, receive):
        slot = line.at[place]
        remote(slot, slot, self.us.at[0], receive.at[place], self.here.twin).wait_recv()
        copy = pltpu.make_async_copy(slot, self.stage.at[0], self.load.at[0])
        copy.start()
        copy.wait()
        add_rows(self.terms.at[place], [self.terms.at[place], self.stage.at[0]])

    def fold(self, distance):
        here = self.here
        above = here.place + distance
        below = here.place - distance

        @pl.when(above <= self.last)
        def _():
            @pl.when(here.place > 0)
            def _():
                self.merge(above, self.rising, self.ur)

            self.up(above).start()

        @pl.when(below >= 0)
        def _():
            @pl.when(here.place < self.last)
            def _():
                self.merge(below, self.falling, self.dr)

            self.down(below).start()

    def gather(self):
        place = self.here.place

        @pl.when(place > 0)
        def _():
            self.merge(place, self.rising, self.ur)

        @pl.when(place < self.last)
        def _():
            self.merge(place, self.falling, self.dr)

    def settle(self):
        here = self.here
        for place in range(here.outer):

            @pl.when(place > here.place)
            def _():
                self.up(place).wait_send()

            @pl.when(place < here.place)
            def _():
                self.down(place).wait_send()


class LineFirstSum(RowSum):
    def __init__(self, here, give, keep, near, lines, stage, total, sems, twin_sems):
        self.here, self.give, self.keep = here, give, keep
        self.near, self.stage, self.total = near, stage, total
        self.ys, self.yr, self.load = sems[0], sems[1], sems[6]
        self.lines = [
            LineSum(here, terms, rising, falling, stage, kinds[2:])
            for terms, (rising, falling), kinds in (
                (give, lines[0], twin_sems),
                (keep, lines[1], sems),
            )
        ]

    def fold(self, distance):
        for line in self.lines:
            line.fold(distance)

    def pass_on(self):
        self.lines[0].gather()
        self.across(self.here.place).start()
        self.lines[1].gather()

    def finish(self):
        place = self.here.place
        self.arrived(self.near.at[place], self.ys.at[place], self.yr.at[place])
        near = pltpu.make_async_copy(self.near.at[place], self.stage.at[0], self.load.at[0])
        near.start()
        near.wait()
        add_rows(self.total, [self.keep.at[place], self.stage.at[0]])

    def sent(self):
        self.across(self.here.place).wait_send()

    def settle(self):
        for line in self.lines:
            line.settle()


class RowSpread:
    def __init__(self, here, rows, whole, sems):
        self.here, self.rows, self.whole = here, rows, whole
        self.send_sems, self.recv_sems, self.local = sems

    def copy(self, amount):
        seq = lax.rem(self.here.seq + amount, 4)
        return remote(
            self.rows.at[seq],
            self.whole.at[self.here.seq],
            self.send_sems.at[amount - 1],
            self.recv_sems.at[amount - 1],
            {"seq": seq},
        )

    def keep(self):
        seq = self.here.seq
        return pltpu.make_async_copy(self.rows.at[seq], self.whole.at[seq], self.local)

    def send(self):
        for amount in (2, 3, 1):
            self.copy(amount).start()
        self.keep().start()

    def arrive(self):
        for amount in (1, 2, 3):
            self.copy(amount).wait_recv()
        self.keep().wait()

    def finish(self):
        for amount in (1, 2, 3):
            self.copy(amount).wait_send()


class TokenSum:
    def __init__(self, here, part, got, pair, far_got, base, sems):
        self.here, self.part, self.got, self.pair = here, part, got, pair
        self.far_got, self.base = far_got, base
        self.send_sems, self.recv_sems = sems
        self.rows = part.shape[0] // 4

    def piece(self, seq):
        return pl.ds(pl.multiple_of(seq * self.rows, self.rows), self.rows)

    def to_mate(self, index):
        here = self.here
        chip = here.chip if index else 1 - here.chip
        seq = chip * 2 + 1 - here.core
        return remote(
            self.part.at[self.piece(seq), :],
            self.got.at[index],
            self.send_sems.at[index],
            self.recv_sems.at[index],
            here.mate,
        )

    def to_far(self):
        return remote(
            self.pair, self.far_got, self.send_sems.at[2], self.recv_sems.at[2], self.here.far
        )

    def send(self):
        self.to_mate(0).start()
        self.to_mate(1).start()

    def loop(self, body):
        @pl.loop(0, self.rows // 32)
        def _(index):
            body(index * 32)

    def pass_on(self):
        self.to_mate(0).wait_recv()
        begin = self.here.far_seq * self.rows

        def body(at):
            part = pl.ds(pl.multiple_of(at, 32), 32)
            source = pl.ds(pl.multiple_of(begin + at, 32), 32)
            total = self.part[source, :].astype(F32) + self.got[0, part, :].astype(F32)
            self.pair[part, :] = total.astype(BF)

        self.loop(body)
        self.to_far().start()

    def add_near(self):
        self.to_mate(1).wait_recv()
        begin = self.here.seq * self.rows

        def body(at):
            part = pl.ds(pl.multiple_of(at, 32), 32)
            source = pl.ds(pl.multiple_of(begin + at, 32), 32)
            self.base[part, :] += self.part[source, :].astype(F32) + self.got[1, part, :].astype(F32)

        self.loop(body)
        self.to_mate(0).wait_send()
        self.to_mate(1).wait_send()

    def add_far(self):
        self.to_far().wait_recv()

        def body(at):
            part = pl.ds(pl.multiple_of(at, 32), 32)
            self.base[part, :] += self.far_got[part, :].astype(F32)

        self.loop(body)
        self.to_far().wait_send()


class GainSum:
    def __init__(self, here, parts, arrived, sems):
        self.here, self.parts, self.arrived = here, parts, arrived
        self.send_sems, self.recv_sems = sems
        self.peers = [here.mate, here.far, here.twin] + here.line_peers()

    def copy(self, index):
        return remote(
            self.parts.at[index],
            self.arrived.at[index],
            self.send_sems.at[index],
            self.recv_sems.at[index],
            self.peers[index],
        )

    def start(self):
        self.copy(0).start()

    def hop(self, index):
        self.copy(index).wait()
        self.parts[index + 1] = self.parts[index] + self.arrived[index]
        if index + 1 < len(self.peers):
            self.copy(index + 1).start()


PLAN = (
    (("down_a", 3),),
    (("down_b", 3), ("down_a", 2),),
    (("down_a", 1),),
    (),
    (("first", 3),),
    (("down_b", 2),),
    (("first", 2), ("down_a", "pass"),),
    (),
    (("second", 3), ("first", 1),),
    (),
    (("second", 2),),
    (("first", "finish"),),
    (),
    (("second", 1),),
    (("out", 3), ("query", 3), ("down_b", 1), ("key", 3), ("out", 2), ("down_a", "finish"), ("second", "finish"),),
    (("query", 2), ("key", 2),),
    (("down_b", "finish"), ("query", 1), ("key", 1), ("out", 1), ("query", "finish"), ("key", "finish"), ("out", "finish"),),
)


def backward_kernel(
    size,
    n1_hbm,
    dy_hbm,
    n2_hbm,
    act_hbm,
    first_hbm,
    second_hbm,
    proj_hbm,
    heads_ref,
    mixed_ref,
    lse_ref,
    middle_hbm,
    hidden_hbm,
    dy_own,
    qkv_full,
    out_full,
    first_full,
    second_full,
    down_full,
    attn_gain_ref,
    mlp_gain_ref,
    query_gain_ref,
    key_gain_ref,
    cos_ref,
    sin_ref,
    start_ref,
    grad_in,
    gains_out,
    grad_out,
    hidden_out,
    down_rows,
    first_rows,
    second_rows,
    qkv_rows,
    da_hbm,
    near_mlp,
    rising_mlp,
    falling_mlp,
    rising_twin,
    falling_twin,
    near_qkv,
    rising_qkv,
    falling_qkv,
    near_out,
    rising_out,
    falling_out,
    lhs,
    turned,
    first_r,
    second_r,
    give,
    keep,
    give_out,
    keep_out,
    stage,
    stage_out,
    dout_ref,
    da_own,
    got,
    far_got,
    pair,
    middle_grad,
    proj_buf,
    lse_t,
    delta,
    delta_t,
    dk_sum,
    dv_sum,
    gain_rows,
    gain_got,
    ys,
    yr,
    us,
    ur,
    ds,
    dr,
    fold_load,
    spread_s,
    spread_r,
    spread_l,
    sum_s,
    sum_r,
    ts,
    tr,
    token_local,
    gs,
    gr,
    load_sem,
    credit,
):
    here = Place(size)
    length, width = lhs.shape
    rows = length // 4
    units = first_r.shape[1]
    chunk = units // 2
    ff_part = units // size
    heads = mixed_ref.shape[1] // HEAD_DIM
    kv_heads = heads // 2
    qkv_width = qkv_full.shape[2]
    last = here.outer - 1
    scale = HEAD_DIM ** (-0.5)

    def load(source, target, index):
        copy = pltpu.make_async_copy(source, target, load_sem.at[index])
        copy.start()
        return copy

    def sems(index):
        return tuple(kind.at[index] for kind in (ys, yr, us, ur, ds, dr, fold_load))

    thin = qkv_width // 2
    cut = units * 2 // 3
    lanes = {
        "down_a": slice(0, cut),
        "down_b": slice(cut, units),
        "query": slice(0, thin),
        "key": slice(thin, 2 * thin),
    }

    def part(ref, name):
        return ref.at[:, :, :, lanes[name]]

    def row_sum(index, give_ref, keep_ref, near, rising, falling, stage_ref, total):
        return RowSum(
            here, give_ref, keep_ref, near, rising, falling, stage_ref, total, sems(index)
        )

    jobs = {
        "down_a": LineFirstSum(
            here,
            part(give.at[2], "down_a"),
            part(keep.at[0], "down_a"),
            part(near_mlp.at[0], "down_a"),
            (
                (rising_twin, falling_twin),
                (part(rising_mlp.at[0], "down_a"), part(falling_mlp.at[0], "down_a")),
            ),
            part(stage, "down_a"),
            keep.at[0, here.place, :, :, lanes["down_a"]],
            sems(0),
            sems(5),
        ),
        "down_b": row_sum(
            6,
            part(give.at[2], "down_b"),
            part(keep.at[0], "down_b"),
            part(near_mlp.at[0], "down_b"),
            part(rising_mlp.at[0], "down_b"),
            part(falling_mlp.at[0], "down_b"),
            part(stage, "down_b"),
            keep.at[0, here.place, :, :, lanes["down_b"]],
        ),
        "out": row_sum(
            4, give_out, keep_out, near_out, rising_out, falling_out, stage_out, grad_out
        ),
    }
    for index, name in ((1, "first"), (2, "second")):
        jobs[name] = row_sum(
            index,
            give.at[2 - index],
            keep.at[index],
            near_mlp.at[index],
            rising_mlp.at[index],
            falling_mlp.at[index],
            stage,
            keep.at[index, here.place],
        )
    for index, name in ((3, "query"), (7, "key")):
        jobs[name] = row_sum(
            index,
            part(give.at[1], name),
            part(second_r, name),
            part(near_qkv, name),
            part(rising_qkv, name),
            part(falling_qkv, name),
            part(stage, name),
            second_r.at[here.place, :, :, lanes[name]],
        )
    zones = width // 512

    def zone_at(index):
        zone = here.place // (here.outer // zones)
        return (
            3 * (1 - zone // 2),
            lax.rem(2 + 3 * zone, 5),
            1 + lax.rem(zone, 2),
            zone,
        )[index]

    zone_order = [zone_at(index) for index in range(zones)]
    by_zone = [(zone, (zone,)) for zone in zone_order]

    spreads = {}
    for index, (name, whole) in enumerate(
        (
            ("down_a", down_rows.at[:, :, lanes["down_a"]]),
            ("down_b", down_rows.at[:, :, lanes["down_b"]]),
            ("first", first_rows),
            ("second", second_rows),
            ("query", qkv_rows.at[:, :, lanes["query"]]),
            ("key", qkv_rows.at[:, :, lanes["key"]]),
        )
    ):
        kinds = (spread_s.at[index], spread_r.at[index], spread_l.at[index])
        spreads[name] = RowSpread(here, jobs[name].total, whole, kinds)

    def token_sum(index, base):
        return TokenSum(
            here, lhs, got, pair, far_got, base, (sum_s.at[index], sum_r.at[index])
        )

    sum_mlp = token_sum(0, middle_grad)
    sum_hidden = token_sum(1, grad_in)
    sum_attn = token_sum(2, grad_in)
    da = TokenGather(here, da_own, da_hbm, (ts, tr, token_local.at[0]))

    def model_tiles(group):
        return [(group, seq_group) for seq_group in range(4)]

    def first_columns(lane):
        return first_r[:, lane]

    def model_left(group):
        return turned[pl.ds(group * 4, 4)].reshape(512, length)

    def advance(steps):
        for name, step in steps:
            job = jobs[name]
            if step == "pass":
                job.pass_on()
            elif step == "finish":
                job.finish()
                if name in spreads:
                    spreads[name].send()
            else:
                for distance in range(last * step // 3, last * (step - 1) // 3, -1):
                    job.fold(distance)

    load_turned = load(dy_hbm, turned, 0)
    load_act = load(act_hbm, first_r, 1)
    load_middle = load(middle_hbm, grad_in, 2)
    load_dy = load(dy_own, da_own, 4)
    load_second = load(second_hbm, second_r, 3)
    here.greet(wide=True)
    load_turned.wait()
    load_act.wait()
    def model_terms(give_ref, keep_ref, right, senders):
        compute_terms(
            here, give_ref, keep_ref, model_left, right, model_tiles, by_zone, senders
        )

    model_terms(give.at[2], keep.at[0], first_columns, [jobs["down_b"]])
    advance(PLAN[0])
    load_turned = load(n2_hbm, turned, 0)
    load_first = load(first_hbm, first_r, 1)
    load_first.wait()
    load_second.wait()

    own = width // size
    slabs = 256 // own

    def dn2_body(first_w, second_w):
        lane = pl.ds(pl.multiple_of(pl.program_id(0) * 256, 256), 256)
        first_tile = first_w[...].reshape(256, units)
        second_tile = second_w[...].reshape(256, units)

        @pl.loop(0, 4)
        def _(index):
            part = pl.ds(pl.multiple_of(index * rows, rows), rows)
            total = contract_cols(first_r[part, :], first_tile)
            blocks = pl.ds(index * (here.outer // 4), here.outer // 4)
            second_rows = second_r[blocks].reshape(rows, units)
            total = total + contract_cols(second_rows, second_tile)
            lhs[part, lane] = total.astype(BF)

    slab = pl.BlockSpec((slabs, own, units), lambda t: (t, 0, 0))
    pltpu.emit_pipeline(dn2_body, grid=(width // 256,), in_specs=[slab, slab])(
        first_full, second_full
    )
    sum_mlp.send()
    middle_grad[...] = jnp.zeros_like(middle_grad)
    load_turned.wait()
    advance(PLAN[1])
    sum_mlp.pass_on()
    sum_mlp.add_near()
    model_terms(give.at[1], keep.at[1], first_columns, [jobs["first"]])
    load_act = load(act_hbm, first_r, 1)
    advance(PLAN[2])
    sum_mlp.add_far()

    load_middle.wait()
    load_dy.wait()
    gain_rows[0] = jnp.zeros_like(gain_rows[0])
    narrow = 16

    @pl.loop(0, rows // narrow)
    def _(index):
        part = pl.ds(pl.multiple_of(index * narrow, narrow), narrow)
        values = grad_in[part, :]
        scales = lax.rsqrt(jnp.mean(values * values, axis=-1, keepdims=True) + EPSILON)
        normed = values * scales
        update = middle_grad[part, :]
        gain_rows[0, 1:2, :] += jnp.sum(update * normed, axis=0, keepdims=True)
        upper = update * mlp_gain_ref[...]
        inner = jnp.mean(upper * normed, axis=-1, keepdims=True)
        grad = da_own[part, :].astype(F32) + scales * (upper - normed * inner)
        middle_grad[part, :] = grad
        da_own[part, :] = grad.astype(BF)

    da.send()
    advance(PLAN[3])
    model_terms(
        give.at[0],
        keep.at[2],
        lambda lane: second_r[:, :, :, lane].reshape(length, -1),
        [jobs["second"]],
    )
    advance(PLAN[4])

    def hidden_body(weight):
        lane = pl.ds(pl.multiple_of(pl.program_id(0) * 256, 256), 256)
        tile = weight[...]

        @pl.loop(0, 4)
        def _(index):
            part = pl.ds(pl.multiple_of(index * rows, rows), rows)
            lhs[part, lane] = dot(first_r[part, :], tile).astype(BF)

    load_act.wait()
    pltpu.emit_pipeline(
        hidden_body,
        grid=(width // 256,),
        in_specs=[pl.BlockSpec((units, 256), lambda t: (0, t))],
    )(down_full)
    da.mate_arrived()
    sum_hidden.send()
    da.forward()
    advance(PLAN[5])
    sum_hidden.pass_on()
    sum_hidden.add_near()
    advance(PLAN[6])
    da.rest_arrived()
    da.finish()
    load_lhs = load(da_hbm, lhs, 0)
    load_own = load(hidden_hbm, da_own, 2)
    load_lhs.wait()

    def dout_body(weight):
        lane = pl.ds(pl.multiple_of(pl.program_id(0) * 256, 256), 256)
        tile = weight[...].reshape(256, width)

        @pl.loop(0, 4)
        def _(index):
            part = pl.ds(pl.multiple_of(index * rows, rows), rows)
            dout_ref[part, lane] = contract_cols(lhs[part, :], tile).astype(BF)

    out_blocks, out_rows = out_full.shape[:2]
    pltpu.emit_pipeline(
        dout_body,
        grid=(out_blocks * out_rows // 256,),
        in_specs=[pl.BlockSpec((256 // out_rows, out_rows, width), lambda t: (t, 0, 0))],
    )(out_full)

    for head in range(heads):
        turned[head] = mixed_ref[:, head * HEAD_DIM : (head + 1) * HEAD_DIM].T
    compute_terms(
        here,
        give_out,
        keep_out,
        lambda group: turned[0:heads].reshape(heads * HEAD_DIM, length),
        lambda lane: lhs[:, lane],
        lambda group: [(zone, 0) for zone in range(heads)],
        [(0, zone_order)],
        [jobs["out"]],
    )
    load_turned = load(n1_hbm, turned, 0)
    sum_hidden.add_far()
    for index, peer in enumerate((here.mate, here.far)):
        pl.semaphore_signal(credit.at[index], inc=1, device_id=peer, device_id_type=MESH)

    @pl.loop(0, rows // 32)
    def _(index):
        part = pl.ds(pl.multiple_of(index * 32, 32), 32)
        pair[part, :] = grad_in[part, :].astype(BF)

    store_hidden = load(pair, hidden_out, 1)
    advance(PLAN[7])

    lse_t[...] = lse_ref[...].T[0:8]
    delta[...] = jnp.zeros_like(delta)
    for head in range(heads):
        lane = slice(head * HEAD_DIM, (head + 1) * HEAD_DIM)
        terms = dout_ref[:, lane].astype(F32) * mixed_ref[:, lane].astype(F32)
        delta[:, head : head + 1] = jnp.sum(terms, axis=-1, keepdims=True)
    delta_t[...] = delta[...].T[0:8]
    def through_norm(grad, head, part, gain_ref, gain_row):
        proj = proj_buf[part, :]
        scales = lax.rsqrt(jnp.mean(proj * proj, axis=-1, keepdims=True) + EPSILON)
        normed = proj * scales
        grad = grad.astype(F32)
        upper = grad * cos_ref[part, :] - pltpu.roll(grad, HEAD_DIM // 2, 1) * sin_ref[part, :]
        gain_rows[0, 2:3, gain_row * HEAD_DIM : (gain_row + 1) * HEAD_DIM] += jnp.sum(
            upper * normed, axis=0, keepdims=True
        )
        upper = upper * gain_ref[...]
        inner = jnp.mean(upper * normed, axis=-1, keepdims=True)
        result = (scales * (upper - normed * inner)).astype(BF)
        first_r[part, head * HEAD_DIM : (head + 1) * HEAD_DIM] = result

    for head in range(heads):
        pair_head = head // 2
        load_proj = load(proj_hbm.at[head], proj_buf, 4)
        if head % 2 == 0:
            dk_sum[...] = jnp.zeros_like(dk_sum)
            dv_sum[...] = jnp.zeros_like(dv_sum)
        load_proj.wait()
        for block in range(4):
            end = (block + 1) * rows
            part = pl.ds(block * rows, rows)
            queries = heads_ref[head, part, :]
            keys = heads_ref[heads + pair_head, 0:end, :]
            values = heads_ref[heads + kv_heads + pair_head, 0:end, :]
            out_grad = dout_ref[part, head * HEAD_DIM : (head + 1) * HEAD_DIM]
            scores = contract_cols(keys, queries)
            key_place = lax.broadcasted_iota(jnp.int32, (end, rows), 0)
            query_place = lax.broadcasted_iota(jnp.int32, (end, rows), 1) + block * rows
            allowed = (key_place >= start_ref[:, part]) & (key_place <= query_place)
            weights = jnp.exp(scores * scale - lse_t[head : head + 1, part])
            weights = jnp.where(allowed, weights, 0.0)
            weight_grad = contract_cols(values, out_grad)
            inner = delta_t[head : head + 1, part]
            score_grad = (weights * (weight_grad - inner)).astype(BF)
            dk_sum[0:end, :] += dot(score_grad, queries) * scale
            dv_sum[0:end, :] += dot(weights.astype(BF), out_grad)
            query_grad = (contract_rows(score_grad, keys) * scale).astype(BF)
            through_norm(query_grad, head, part, query_gain_ref, 0)
        if head % 2:
            key = heads + pair_head
            value_at = (heads + kv_heads + pair_head) * HEAD_DIM
            load(proj_hbm.at[key], proj_buf, 4).wait()

            @pl.loop(0, 4)
            def _(index):
                part = pl.ds(pl.multiple_of(index * rows, rows), rows)
                through_norm(dk_sum[part, :].astype(BF), key, part, key_gain_ref, 1)
                first_r[part, value_at : value_at + HEAD_DIM] = dv_sum[part, :].astype(BF)

        advance(PLAN[8 + head])

    load_turned.wait()
    jobs["first"].sent()
    store_hidden.wait()
    proj_grads = first_r.at[:, 0:qkv_width]
    model_terms(
        give.at[1, :, :, :, 0:qkv_width],
        second_r.at[:, :, :, 0:qkv_width],
        first_columns,
        [jobs["query"], jobs["key"]],
    )
    advance(PLAN[12])

    def dn1_body(weight):
        lane = pl.ds(pl.multiple_of(pl.program_id(0) * 256, 256), 256)
        tile = weight[...].reshape(256, qkv_width)

        @pl.loop(0, 4)
        def _(index):
            part = pl.ds(pl.multiple_of(index * rows, rows), rows)
            lhs[part, lane] = contract_cols(proj_grads[part, :], tile).astype(BF)

    pltpu.emit_pipeline(
        dn1_body,
        grid=(width // 256,),
        in_specs=[pl.BlockSpec((slabs, own, qkv_width), lambda t: (t, 0, 0))],
    )(qkv_full)
    grad_in[...] = jnp.zeros_like(grad_in)
    pl.semaphore_wait(credit.at[0], 1)
    pl.semaphore_wait(credit.at[1], 1)
    sum_attn.send()
    advance(PLAN[13])
    sum_attn.pass_on()
    sum_attn.add_near()
    advance(PLAN[14])
    sum_attn.add_far()
    load_own.wait()

    @pl.loop(0, rows // narrow)
    def _(index):
        part = pl.ds(pl.multiple_of(index * narrow, narrow), narrow)
        values = da_own[part, :].astype(F32)
        scales = lax.rsqrt(jnp.mean(values * values, axis=-1, keepdims=True) + EPSILON)
        normed = values * scales
        update = grad_in[part, :]
        gain_rows[0, 0:1, :] += jnp.sum(update * normed, axis=0, keepdims=True)
        upper = update * attn_gain_ref[...]
        inner = jnp.mean(upper * normed, axis=-1, keepdims=True)
        grad_in[part, :] = middle_grad[part, :] + scales * (upper - normed * inner)

    gain_sum = GainSum(here, gain_rows, gain_got, (gs, gr))
    gain_sum.start()
    advance(PLAN[15])
    hops = list(range(len(gain_sum.peers)))
    for name, step in PLAN[16]:
        advance([(name, step)])
        if hops:
            gain_sum.hop(hops.pop(0))
    for index in hops:
        gain_sum.hop(index)
    gains_out[...] = gain_rows[gain_rows.shape[0] - 1]
    for spread_rows in spreads.values():
        spread_rows.arrive()
    for name, job in jobs.items():
        if name != "first":
            job.sent()
    for job in jobs.values():
        job.settle()
    for job in spreads.values():
        job.finish()


def backward(saved, weights, own, gains, tables, starts):
    size = lax.axis_size("shard")
    outer = size // 2
    (n1, dy, n2, act, first, second, proj, heads_all, mixed, lse, middle) = saved
    length, width = heads_all.shape[1], middle.shape[1]
    piece = length // 4
    units = act.shape[1]
    qkv_width = weights[0].shape[2]
    rows = width // (4 * size)
    q_width = mixed.shape[1]

    def shape(*dims, kind=BF):
        return jax.ShapeDtypeStruct(dims, kind)

    results = [
        shape(piece, width, kind=F32),
        shape(8, width, kind=F32),
        shape(1, rows, width, kind=F32),
        shape(piece, width),
        shape(4, rows, units),
        shape(4, rows, units),
        shape(4, rows, units),
        shape(4, rows, qkv_width),
        shape(length, width),
    ]
    results += [shape(3, outer, 4, rows, units)] * 3
    results += [shape(outer, 4, rows, units * 2 // 3)] * 2
    results += [shape(outer, 4, rows, qkv_width)] * 3
    results += [shape(outer, 1, rows, width)] * 3
    dma = pltpu.SemaphoreType.DMA
    hops = 3 + outer.bit_length() - 1
    vmem = pltpu.VMEM
    return pl.pallas_call(
        functools.partial(backward_kernel, size),
        out_shape=results,
        in_specs=[ANY] * 7 + [VMEM] * 3 + [ANY] * 8 + [VMEM] * 7,
        out_specs=[VMEM] * 3 + [ANY] * (len(results) - 3),
        scratch_shapes=[
            vmem((length, width), BF),
            vmem((width // 128, 128, length), BF),
            vmem((length, units), BF),
            vmem((outer, 4, rows, units), BF),
            vmem((3, outer, 4, rows, units), BF),
            vmem((3, outer, 4, rows, units), BF),
            vmem((outer, 1, rows, width), BF),
            vmem((outer, 1, rows, width), BF),
            vmem((2, 4, rows, units), BF),
            vmem((2, 1, rows, width), BF),
            vmem((length, q_width), BF),
            vmem((piece, width), BF),
            vmem((2, piece, width), BF),
            vmem((piece, width), BF),
            vmem((piece, width), BF),
            vmem((piece, width), F32),
            vmem((length, HEAD_DIM), F32),
            vmem((8, length), F32),
            vmem((length, 128), F32),
            vmem((8, length), F32),
            vmem((length, HEAD_DIM), F32),
            vmem((length, HEAD_DIM), F32),
            vmem((hops + 1, 8, width), F32),
            vmem((hops, 8, width), F32),
            dma((8, outer)),
            dma((8, outer)),
            dma((8, outer)),
            dma((8, outer)),
            dma((8, outer)),
            dma((8, outer)),
            dma((8, 3)),
            dma((6, 3)),
            dma((6, 3)),
            dma((6,)),
            dma((3, 3)),
            dma((3, 3)),
            dma((3,)),
            dma((3,)),
            dma((1,)),
            dma((hops,)),
            dma((hops,)),
            dma((5,)),
            pltpu.SemaphoreType.REGULAR((2,)),
        ],
        compiler_params=pltpu.CompilerParams(
            collective_id=1, has_side_effects=True, vmem_limit_bytes=VMEM_BYTES
        ),
        name="backward_sums",
    )(
        n1,
        dy,
        n2,
        act,
        first,
        second.reshape(outer, 4, rows, units),
        proj,
        heads_all,
        mixed,
        lse,
        middle,
        *own,
        *weights,
        *gains,
        *tables,
        starts,
    )


def finish_kernel(
    size,
    grad_in,
    gains,
    grad_out,
    hidden_out,
    down_rows,
    first_rows,
    second_rows,
    qkv_rows,
    grad_in_out,
    grad_out_out,
    hidden_out_out,
    grad_query,
    grad_key,
    grad_value,
    grad_gate,
    grad_up,
    grad_down,
    attn_gain,
    mlp_gain,
    query_gain,
    key_gain,
    grad_in_buf,
    grad_out_buf,
    hidden_buf,
    down_buf,
    first_buf,
    second_buf,
    qkv_buf,
    query_buf,
    key_buf,
    value_buf,
    gate_buf,
    up_buf,
    wide_buf,
    load_sems,
    store_sems,
):
    units = down_buf.shape[2]
    chunk = units // 2
    ff_part = units // size
    most, tail = chunk - 256, 256
    stores = []

    def load(source, target, index):
        copy = pltpu.make_async_copy(source, target, load_sems.at[index])
        copy.start()
        return copy

    def store(source, target):
        copy = pltpu.make_async_copy(source, target, store_sems.at[len(stores)])
        copy.start()
        stores.append(copy)

    loads = [
        load(source, target, index)
        for index, (source, target) in enumerate(
            (
                (down_rows, down_buf),
                (first_rows, first_buf),
                (second_rows, second_buf),
                (qkv_rows, qkv_buf),
                (grad_in, grad_in_buf),
                (hidden_out, hidden_buf),
                (grad_out, grad_out_buf),
            )
        )
    ]

    def place(read, target):
        @pl.loop(0, target.shape[0] // 16)
        def _(index):
            part = pl.ds(pl.multiple_of(index * 16, 16), 16)
            values = [read(seq, part).astype(F32) for seq in range(4)]
            for begin in range(0, size, size // 8):
                pieces = [
                    values[seq][:, block * ff_part : (block + 1) * ff_part]
                    for block in range(begin, begin + size // 8)
                    for seq in range(4)
                ]
                lane = slice(begin * 4 * ff_part, (begin + size // 8) * 4 * ff_part)
                target[part, lane] = jnp.concatenate(pieces, axis=1)

    def side(index):
        at = 2 * most + index * tail

        def read(seq, part):
            return jnp.concatenate(
                [
                    first_buf[seq, part, index * chunk : (index + 1) * chunk],
                    second_buf[seq, part, index * most : (index + 1) * most],
                    second_buf[seq, part, at : at + tail],
                ],
                axis=1,
            )

        return read

    loads[0].wait()
    place(lambda seq, part: down_buf[seq, part, :], wide_buf)
    store(wide_buf, grad_down)
    loads[1].wait()
    loads[2].wait()
    place(side(0), gate_buf)
    store(gate_buf, grad_gate)
    place(side(1), up_buf)
    store(up_buf, grad_up)
    loads[4].wait()
    store(grad_in_buf, grad_in_out)
    loads[5].wait()
    store(hidden_buf, hidden_out_out)
    loads[6].wait()
    store(grad_out_buf, grad_out_out)
    loads[3].wait()
    at = 0
    for buf, target in ((query_buf, grad_query), (key_buf, grad_key), (value_buf, grad_value)):
        count = buf.shape[1] // 4
        for seq in range(4):
            buf[:, seq * count : (seq + 1) * count] = qkv_buf[seq, :, at : at + count].astype(F32)
        at += count
        store(buf, target)
    attn_gain[...] = gains[0:1, :]
    mlp_gain[...] = gains[1:2, :]
    query_gain[...] = gains[2:3, 0:HEAD_DIM]
    key_gain[...] = gains[2:3, HEAD_DIM : 2 * HEAD_DIM]
    for copy in stores:
        copy.wait()


def finish(grad_in, gains, grad_out, hidden_out, down_rows, first_rows, second_rows, qkv_rows):
    size = lax.axis_size("shard")
    piece, width = grad_in.shape
    rows, units = down_rows.shape[1:]
    qkv_width = qkv_rows.shape[2]

    def shape(*dims, kind=F32):
        return jax.ShapeDtypeStruct(dims, kind)

    results = [
        shape(piece, width),
        shape(1, rows, width),
        shape(piece, width, kind=BF),
        shape(rows, 2 * qkv_width),
        shape(rows, qkv_width),
        shape(rows, qkv_width),
        shape(rows, 4 * units),
        shape(rows, 4 * units),
        shape(rows, 4 * units),
        shape(1, width),
        shape(1, width),
        shape(1, HEAD_DIM),
        shape(1, HEAD_DIM),
    ]
    return pl.pallas_call(
        functools.partial(finish_kernel, size),
        out_shape=results,
        in_specs=[ANY, VMEM] + [ANY] * 6,
        out_specs=[ANY] * 9 + [VMEM] * 4,
        scratch_shapes=[
            pltpu.VMEM((piece, width), F32),
            pltpu.VMEM((1, rows, width), F32),
            pltpu.VMEM((piece, width), BF),
            pltpu.VMEM((4, rows, units), BF),
            pltpu.VMEM((4, rows, units), BF),
            pltpu.VMEM((4, rows, units), BF),
            pltpu.VMEM((4, rows, qkv_width), BF),
            pltpu.VMEM((rows, 2 * qkv_width), F32),
            pltpu.VMEM((rows, qkv_width), F32),
            pltpu.VMEM((rows, qkv_width), F32),
            pltpu.VMEM((rows, 4 * units), F32),
            pltpu.VMEM((rows, 4 * units), F32),
            pltpu.VMEM((rows, 4 * units), F32),
            pltpu.SemaphoreType.DMA((7,)),
            pltpu.SemaphoreType.DMA((9,)),
        ],
        compiler_params=pltpu.CompilerParams(vmem_limit_bytes=VMEM_BYTES),
        name="finish",
    )(grad_in, gains, grad_out, hidden_out, down_rows, first_rows, second_rows, qkv_rows)


def local(
    hidden_in,
    segment_ids,
    norm_attn_gain,
    w_query,
    w_key,
    w_value,
    query_gain,
    key_gain,
    w_out,
    norm_mlp_gain,
    w_gate,
    w_up,
    w_down,
    out_cotangent,
):
    segment = segment_ids[0]
    gains = (norm_attn_gain[None], norm_mlp_gain[None], query_gain[None], key_gain[None])
    results = forward(
        hidden_in[0],
        out_cotangent[0],
        (w_query, w_key, w_value, w_out, w_gate, w_up, w_down),
        gains,
        segment,
    )
    (
        grad_in,
        grad_out,
        hidden_out,
        grad_query,
        grad_key,
        grad_value,
        grad_gate,
        grad_up,
        grad_down,
        attn_gain,
        mlp_gain,
        query_grad,
        key_grad,
    ) = finish(
        *backward(
            results[8:19],
            results[:5],
            (hidden_in[0], out_cotangent[0]),
            gains,
            results[19:21],
            results[21],
        )[:8]
    )
    return (
        hidden_out[None],
        grad_in[None],
        attn_gain[0],
        grad_query,
        grad_key,
        grad_value,
        query_grad[0],
        key_grad[0],
        grad_out[0],
        mlp_gain[0],
        grad_gate,
        grad_up,
        grad_down.T,
    )


def solution(mesh):
    return jax.shard_map(
        local,
        mesh=mesh,
        in_specs=(
            P("shard", "seq", None),
            P("shard", None),
            P(),
            P("shard", None),
            P("shard", None),
            P("shard", None),
            P(),
            P(),
            P("shard", None),
            P(),
            P("shard", None),
            P("shard", None),
            P("shard", None),
            P("shard", "seq", None),
        ),
        out_specs=(
            P("shard", "seq", None),
            P("shard", "seq", None),
            P(),
            P(("seq", "shard"), None),
            P(("seq", "shard"), None),
            P(("seq", "shard"), None),
            P(),
            P(),
            P(("seq", "shard"), None),
            P(),
            P(("seq", "shard"), None),
            P(("seq", "shard"), None),
            P(None, ("seq", "shard")),
        ),
        check_vma=False,
    )
```

```python
import functools

import jax
import jax.numpy as jnp
import numpy as np
from jax import lax
from jax.experimental import pallas as pl
from jax.experimental.pallas import tpu as pltpu
from jax.sharding import PartitionSpec as P

Q_HEADS = 16
KV_HEADS = 8
HEAD_DIM = 128
EPSILON = 1e-06
ROPE_BASE = 1000000.0
NEGATIVE = -1e30
BF = jnp.bfloat16
F32 = jnp.float32
MESH = pl.DeviceIdType.MESH
ANY = pl.BlockSpec(memory_space=pl.ANY)
VMEM = pl.BlockSpec(memory_space=pltpu.VMEM)
VMEM_BYTES = 62 * 1024 * 1024


def dot(left, right):
    return jnp.dot(left, right, preferred_element_type=F32)


def contract_rows(left, right):
    return lax.dot_general(left, right, (((0,), (0,)), ((), ())), preferred_element_type=F32)


def contract_cols(left, right):
    return lax.dot_general(left, right, (((1,), (1,)), ((), ())), preferred_element_type=F32)


class Place:
    def __init__(self, size):
        self.size = size
        self.outer = size // 2
        self.quarter = size // 4
        self.seq = lax.axis_index("seq")
        self.shard = lax.axis_index("shard")
        self.chip = self.seq // 2
        self.core = lax.rem(self.seq, 2)
        self.place = self.shard // 2
        self.half = lax.rem(self.shard, 2)
        self.far_seq = lax.rem(self.seq + 2, 4)
        self.mate_seq = self.chip * 2 + 1 - self.core
        self.far = {"seq": self.far_seq}
        self.mate = {"seq": self.mate_seq}
        self.twin_shard = self.place * 2 + 1 - self.half
        self.twin = {"shard": self.twin_shard}

    def outer_peer(self, place):
        return {"shard": place * 2 + self.half}

    def line_peers(self):
        peers = []
        step = 1
        while step < self.outer:
            sign = 1 - 2 * lax.rem(self.place // step, 2)
            peers.append(self.outer_peer(self.place + sign * step))
            step *= 2
        return peers

    def greet(self, wide=False):
        barrier = pltpu.get_barrier_semaphore()
        last = self.outer - 1

        def signal(peer):
            pl.semaphore_signal(barrier, inc=1, device_id=peer, device_id_type=MESH)

        peers = [self.far, self.mate, self.twin]
        if wide:
            peers += [{"seq": 3 - self.seq}] + self.line_peers()[1:]
        for peer in peers:
            signal(peer)

        @pl.when(self.place < last)
        def _():
            signal(self.outer_peer(self.place + 1))

        @pl.when(self.place > 0)
        def _():
            signal(self.outer_peer(self.place - 1))

        inner = ((self.place > 0) & (self.place < last)).astype(jnp.int32)
        pl.semaphore_wait(barrier, len(peers) + 1 + inner)


def remote(source, target, send, receive, peer):
    return pltpu.make_async_remote_copy(
        src_ref=source,
        dst_ref=target,
        send_sem=send,
        recv_sem=receive,
        device_id=peer,
        device_id_type=MESH,
    )


class LineGather:
    def __init__(self, here, own, slot, sems):
        self.here, self.own, self.slot = here, own, slot
        self.us, self.ur, self.ds, self.dr = sems
        self.last = here.outer - 1

    def up(self, distance):
        here = self.here
        slot = self.slot(here.place - distance)
        source = slot if distance else self.own
        peer = here.outer_peer(here.place + 1)
        return remote(source, slot, self.us.at[distance], self.ur.at[distance], peer)

    def down(self, distance):
        here = self.here
        slot = self.slot(here.place + distance)
        source = slot if distance else self.own
        peer = here.outer_peer(here.place - 1)
        return remote(source, slot, self.ds.at[distance], self.dr.at[distance], peer)

    def send(self):
        here = self.here

        @pl.when(here.place < self.last)
        def _():
            self.up(0).start()

        @pl.when(here.place > 0)
        def _():
            self.down(0).start()

    def step(self, distance, arrived=lambda place: None):
        here = self.here
        below = here.place - 1 - distance
        above = here.place + 1 + distance

        @pl.when(below >= 0)
        def _():
            slot = self.slot(below)
            remote(slot, slot, self.us.at[0], self.ur.at[distance], here.twin).wait_recv()

            @pl.when(here.place < self.last)
            def _():
                self.up(distance + 1).start()

            arrived(below)

        @pl.when(above <= self.last)
        def _():
            slot = self.slot(above)
            remote(slot, slot, self.ds.at[0], self.dr.at[distance], here.twin).wait_recv()

            @pl.when(here.place > 0)
            def _():
                self.down(distance + 1).start()

            arrived(above)

    def finish(self):
        here = self.here
        for distance in range(self.last):

            @pl.when((here.place - distance >= 0) & (here.place < self.last))
            def _():
                self.up(distance).wait_send()

            @pl.when((here.place + distance <= self.last) & (here.place > 0))
            def _():
                self.down(distance).wait_send()


class RowGather:
    def __init__(self, here, own, whole, sems, spot=lambda shard: shard):
        self.here, self.own, self.whole, self.spot = here, own, whole, spot
        self.ys, self.yr, self.local = sems[4:]
        self.line = LineGather(here, own, self.mine, sems[:4])

    def mine(self, place):
        return self.whole.at[self.spot(place * 2 + self.here.half)]

    def theirs(self, place):
        return self.whole.at[self.spot(place * 2 + 1 - self.here.half)]

    def keep(self):
        return pltpu.make_async_copy(self.own, self.mine(self.here.place), self.local)

    def across(self, place, own=False):
        slot = self.mine(place)
        source = self.own if own else slot
        return remote(source, slot, self.ys.at[place], self.yr.at[place], self.here.twin)

    def arrived(self, place):
        slot = self.theirs(place)
        remote(slot, slot, self.ys.at[place], self.yr.at[place], self.here.twin).wait_recv()

    def send(self):
        self.line.send()
        self.across(self.here.place, own=True).start()
        self.keep().start()

    def step(self, distance):
        self.line.step(distance, lambda place: self.across(place).start())

    def arrive(self):
        self.keep().wait()
        for place in range(self.here.outer):
            self.arrived(place)

    def finish(self):
        self.line.finish()
        for place in range(self.here.outer):
            self.across(place).wait_send()


class TwinFirstGather(RowGather):
    def __init__(self, here, own, whole, sems, twin_sems):
        super().__init__(here, own, whole, sems)
        self.lines = [
            self.line,
            LineGather(here, self.theirs(here.place), self.theirs, twin_sems[:4]),
        ]

    def twin(self):
        self.arrived(self.here.place)
        self.lines[1].send()

    def step(self, distance):
        for line in self.lines:
            line.step(distance)

    def arrive(self):
        self.keep().wait()

    def finish(self):
        for line in self.lines:
            line.finish()
        self.across(self.here.place, own=True).wait_send()


class HeadGather:
    def __init__(self, here, own, whole, sems):
        self.here, self.own, self.whole = here, own, whole
        self.us, self.zr, self.ds, _, self.ys, self.yr, self.local = sems
        self.last = here.outer - 1
        self.count = here.quarter // 2
        self.first = here.seq * self.count
        self.mine = here.place - self.first
        self.inside = (self.mine >= 0) & (self.mine < self.count)

    def slot(self, index):
        return self.whole.at[index * 2 + self.here.half]

    def keep(self):
        return pltpu.make_async_copy(self.own, self.slot(self.mine), self.local)

    def up(self, index, own=False):
        slot = self.slot(index)
        peer = self.here.outer_peer(self.here.place + 1)
        return remote(self.own if own else slot, slot, self.us.at[index], self.zr.at[index], peer)

    def down(self, index, own=False):
        slot = self.slot(index)
        peer = self.here.outer_peer(self.here.place - 1)
        return remote(self.own if own else slot, slot, self.ds.at[index], self.zr.at[index], peer)

    def across(self, index):
        slot = self.slot(index)
        return remote(slot, slot, self.ys.at[index], self.yr.at[index], self.here.twin)

    def send(self):
        @pl.when(self.inside)
        def _():
            self.keep().start()

            @pl.when(self.here.place < self.last)
            def _():
                self.up(self.mine, own=True).start()

            @pl.when(self.here.place > 0)
            def _():
                self.down(self.mine, own=True).start()

    def step(self):
        here = self.here

        @pl.when(self.inside)
        def _():
            self.keep().wait()

        for index in range(self.count):
            slot = self.slot(index)
            arrival = remote(slot, slot, self.us.at[0], self.zr.at[index], here.twin)

            @pl.when(self.mine > index)
            def _():
                arrival.wait_recv()

                @pl.when(here.place < self.last)
                def _():
                    self.up(index).start()

            @pl.when(self.mine < index)
            def _():
                arrival.wait_recv()

                @pl.when(here.place > 0)
                def _():
                    self.down(index).start()

            self.across(index).start()

    def arrive(self):
        for index in range(self.count):
            slot = self.whole.at[index * 2 + 1 - self.here.half]
            remote(
                slot, slot, self.ys.at[index], self.yr.at[index], self.here.twin
            ).wait_recv()

    def finish(self):
        here = self.here
        for index in range(self.count):

            @pl.when((self.mine >= index) & (here.place < self.last))
            def _():
                self.up(index).wait_send()

            @pl.when((self.mine <= index) & (here.place > 0))
            def _():
                self.down(index).wait_send()

            self.across(index).wait_send()


class TokenGather:
    def __init__(self, here, own, whole, sems):
        self.here, self.own, self.whole = here, own, whole
        self.send_sems, self.recv_sems, self.local = sems
        self.rows = whole.shape[0] // 4

    def slot(self, seq):
        return self.whole.at[pl.ds(pl.multiple_of(seq * self.rows, self.rows), self.rows), :]

    def keep(self):
        return pltpu.make_async_copy(self.own, self.slot(self.here.seq), self.local)

    def copy(self, index):
        here = self.here
        slot = self.slot(here.far_seq if index == 2 else here.seq)
        return remote(
            slot if index == 2 else self.own,
            slot,
            self.send_sems.at[index],
            self.recv_sems.at[index],
            here.far if index == 0 else here.mate,
        )

    def send(self):
        self.copy(0).start()
        self.copy(1).start()
        self.keep().start()

    def forward(self):
        self.copy(0).wait_recv()
        self.copy(2).start()

    def mate_arrived(self):
        self.copy(1).wait_recv()

    def rest_arrived(self):
        self.copy(2).wait_recv()
        self.keep().wait()

    def arrive(self):
        self.mate_arrived()
        self.rest_arrived()

    def finish(self):
        for index in range(3):
            self.copy(index).wait_send()


class PieceSum:
    def __init__(self, here, piece, base, give, got, pair, far_got, sems, step):
        self.here, self.piece, self.base, self.step = here, piece, base, step
        self.give, self.got, self.pair, self.far_got = give, got, pair, far_got
        self.send_sems, self.recv_sems = sems

    def to_mate(self, index):
        return remote(
            self.give.at[index],
            self.got.at[index],
            self.send_sems.at[index],
            self.recv_sems.at[index],
            self.here.mate,
        )

    def to_far(self):
        return remote(
            self.pair, self.far_got, self.send_sems.at[2], self.recv_sems.at[2], self.here.far
        )

    def columns(self, body):
        step = self.step

        @pl.loop(0, self.pair.shape[1] // step)
        def _(index):
            body(pl.ds(pl.multiple_of(index * step, step), step))

    def send(self):
        here = self.here
        for index, chip in enumerate((1 - here.chip, here.chip)):
            seq = chip * 2 + 1 - here.core

            def fill(column, index=index, seq=seq):
                self.give[index, :, column] = self.piece(seq, column).astype(BF)

            self.columns(fill)
            self.to_mate(index).start()

    def pass_on(self):
        self.to_mate(0).wait_recv()

        def fill(column):
            term = self.piece(self.here.far_seq, column) + self.got[0, :, column].astype(F32)
            self.pair[:, column] = term.astype(BF)

        self.columns(fill)
        self.to_far().start()

    def add_near(self):
        self.to_mate(1).wait_recv()

        def fill(column):
            term = self.piece(self.here.seq, column) + self.got[1, :, column].astype(F32)
            self.base[:, column] += term

        self.columns(fill)

    def add_far(self):
        self.to_far().wait_recv()

        def fill(column):
            self.base[:, column] += self.far_got[:, column].astype(F32)

        self.columns(fill)
        for copy in (self.to_mate(0), self.to_mate(1), self.to_far()):
            copy.wait_send()


FORWARD_PLAN = (
    (("down", "send"),),
    (),
    (("out", "send"),),
    (("down", 0),),
    (("down", 1), ("down", 2),),
    (("out", 0),),
    (("third", "send"),),
    (),
    (("first", "send"),),
    (),
    (("second", "send"),),
    (),
    (),
    (("first", 0),),
    (),
    (("first", 1), ("first", 2),),
    (("second", "twin"),),
    (("third", 0), ("second", 0), ("third", 1),),
    (("second", 1),),
    (),
    (("third", 2), ("second", 2),),
    (),
)


def forward_kernel(
    size,
    hidden_ref,
    dy_hbm,
    w_query,
    w_key,
    w_value,
    w_out,
    w_gate,
    w_up,
    w_down,
    attn_gain_ref,
    mlp_gain_ref,
    query_gain_ref,
    key_gain_ref,
    inverse_ref,
    segment_ref,
    qkv_full,
    out_full,
    first_full,
    second_full,
    down_full,
    n1_full,
    dy_full,
    n2_full,
    n1_turned,
    dy_turned,
    n2_turned,
    act_out,
    first_pair,
    second_pair,
    proj_ref,
    heads_ref,
    mixed_ref,
    lse_ref,
    middle_ref,
    cos_ref,
    sin_ref,
    start_row,
    lhs,
    dy_all,
    turned,
    qkv_w,
    out_w,
    qkv_own,
    out_own,
    down_own,
    dy_own,
    wide_own,
    first_own,
    second_own,
    own_rows,
    give,
    got,
    pair,
    far_got,
    us,
    ur,
    ds,
    dr,
    ys,
    yr,
    row_local,
    ts,
    tr,
    token_local,
    load_sem,
    ss,
    sr,
    start_ref,
    turned_ids,
):
    here = Place(size)
    last = here.outer - 1
    length, width = lhs.shape
    lse_ref[...] = jnp.zeros_like(lse_ref)
    rows = length // 4
    units = act_out.shape[1]
    chunk = units // 2
    tail = 256
    heads = mixed_ref.shape[1] // HEAD_DIM
    kv_heads = heads // 2
    ff_part = units // size

    def sems(index):
        return tuple(kind.at[index] for kind in (us, ur, ds, dr, ys, yr, row_local))

    down_rows = pl.ds(pl.multiple_of(here.seq * ff_part, ff_part), ff_part)
    qkv = RowGather(here, qkv_own, qkv_full, sems(0))
    out = HeadGather(here, out_own, out_full, sems(1))
    down = RowGather(
        here,
        down_own,
        down_full,
        sems(2),
        lambda shard: pl.ds(pl.multiple_of(shard * ff_part, ff_part), ff_part),
    )
    first = RowGather(here, first_own, first_full, sems(3))
    cut = 2 * (chunk - tail)
    second = TwinFirstGather(
        here, second_own.at[:, 0:cut], second_full.at[:, :, 0:cut], sems(4), sems(6)
    )
    third = RowGather(
        here, second_own.at[:, cut : 2 * chunk], second_full.at[:, :, cut : 2 * chunk], sems(5)
    )
    n1 = TokenGather(here, own_rows.at[0], n1_full, (ts.at[0], tr.at[0], token_local.at[0]))
    n2 = TokenGather(here, own_rows.at[1], n2_full, (ts.at[1], tr.at[1], token_local.at[1]))
    dy = TokenGather(here, dy_own, dy_full, (ts.at[2], tr.at[2], token_local.at[2]))

    loads = []
    at = 0
    for index, (weight, count) in enumerate(((w_query, heads), (w_key, kv_heads), (w_value, kv_heads))):
        count = count * HEAD_DIM
        source = weight.at[:, pl.ds(pl.multiple_of(here.seq * count, count), count)]
        loads.append(
            pltpu.make_async_copy(source, qkv_own.at[:, at : at + count], load_sem.at[index])
        )
        at += count
    loads.append(pltpu.make_async_copy(w_down.at[down_rows, :], down_own, load_sem.at[3]))
    loads.append(pltpu.make_async_copy(w_out, out_own, load_sem.at[4]))
    loads.append(pltpu.make_async_copy(dy_hbm, dy_own, load_sem.at[5]))
    loads.append(pltpu.make_async_copy(w_gate, wide_own, load_sem.at[6]))
    for load in loads:
        load.start()
    here.greet()
    for load in loads[:3]:
        load.wait()
    qkv.send()

    def norm_rows(source, gain_ref, target):
        @pl.loop(0, rows // 32)
        def _(index):
            part = pl.ds(pl.multiple_of(index * 32, 32), 32)
            values = source[part, :].astype(F32)
            scales = lax.rsqrt(jnp.mean(values * values, axis=-1, keepdims=True) + EPSILON)
            target[part, :] = (values * scales * gain_ref[...]).astype(BF)

    gathers = {"out": out, "down": down, "first": first, "second": second, "third": third}

    def advance(steps):
        for name, step in steps:
            gather = gathers[name]
            if step == "send":
                gather.send()
            elif step == "twin":
                gather.twin()
            elif name == "out":
                gather.step()
            else:
                for distance in range(last * step // 3, last * (step + 1) // 3):
                    gather.step(distance)

    norm_rows(hidden_ref, attn_gain_ref, own_rows.at[0])
    n1.send()
    for load in loads[3:5]:
        load.wait()
    advance(FORWARD_PLAN[0])
    for load in loads[5:]:
        load.wait()

    most = chunk - tail

    def cut_units(side):
        for seq in range(4):

            @pl.when(here.seq == seq)
            def _():
                @pl.loop(0, wide_own.shape[0] // 16)
                def _(index):
                    part = pl.ds(pl.multiple_of(index * 16, 16), 16)

                    def gathered(begin):
                        pieces = [
                            wide_own[part, (block * 4 + seq) * ff_part : (block * 4 + seq + 1) * ff_part]
                            for block in range(begin, begin + size // 2)
                        ]
                        return jnp.concatenate(pieces, axis=1)

                    first_own[part, side * chunk : (side + 1) * chunk] = gathered(0)
                    rest = gathered(size // 2)
                    second_own[part, side * most : (side + 1) * most] = rest[:, 0:most]
                    at = 2 * most + side * tail
                    second_own[part, at : at + tail] = rest[:, most:]

    def rotation():
        ids = segment_ref[...].astype(F32)
        turned_ids[...] = jnp.broadcast_to(ids, (128, length)).T
        lane = lax.broadcasted_iota(jnp.int32, (128, 128), 1)

        @pl.loop(0, length // 128)
        def _(index):
            part = pl.ds(pl.multiple_of(index * 128, 128), 128)
            own_ids = turned_ids[part, :]
            count = jnp.zeros((128, 128), F32)
            for at in range(0, length, 128):
                count = count + jnp.where(
                    segment_ref[:, at : at + 128].astype(F32) < own_ids, 1.0, 0.0
                )
            starts = jnp.sum(count, axis=-1, keepdims=True)
            start_ref[part, :] = starts.astype(jnp.int32)
            starts = jnp.broadcast_to(starts, (128, 128))
            turned_ids[part, :] = starts
            places = lax.broadcasted_iota(jnp.int32, (128, 128), 0) + index * 128
            angles = (places.astype(F32) - starts) * inverse_ref[...]
            cos_ref[part, :] = jnp.cos(angles)
            sine = jnp.sin(angles)
            sin_ref[part, :] = jnp.where(lane < HEAD_DIM // 2, -sine, sine)

        start_row[...] = turned_ids[...].T[0:1].astype(jnp.int32)

    cut_units(0)
    load_up = pltpu.make_async_copy(w_up, wide_own, load_sem.at[7])
    load_up.start()
    load_up.wait()
    cut_units(1)
    advance(FORWARD_PLAN[1])
    for third_part in range(3):
        for distance in range(last * third_part // 3, last * (third_part + 1) // 3):
            qkv.step(distance)
        advance(FORWARD_PLAN[2 + third_part])
        if third_part == 0:
            rotation()
    n1.forward()
    advance(FORWARD_PLAN[5])
    n1.arrive()
    load_lhs = pltpu.make_async_copy(n1_full, lhs, load_sem.at[0])
    load_lhs.start()
    dy.send()
    advance(FORWARD_PLAN[6])
    qkv.arrive()
    load_qkv = pltpu.make_async_copy(qkv_full, qkv_w, load_sem.at[1])
    load_qkv.start()
    advance(FORWARD_PLAN[7])
    load_lhs.wait()
    load_qkv.wait()

    def project(tile):
        weight = qkv_w[:, :, tile * 256 : tile * 256 + 256].reshape(width, 256)
        gain_ref = query_gain_ref if tile < heads // 2 else key_gain_ref

        @pl.loop(0, 4)
        def _(index):
            part = pl.ds(pl.multiple_of(index * rows, rows), rows)
            both = dot(lhs[part, :], weight)
            for side in range(2):
                head = tile * 2 + side
                proj = both[:, side * HEAD_DIM : (side + 1) * HEAD_DIM]
                if head >= heads + kv_heads:
                    heads_ref[head, part, :] = proj.astype(BF)
                    continue
                proj_ref[head, part, :] = proj
                scales = lax.rsqrt(jnp.mean(proj * proj, axis=-1, keepdims=True) + EPSILON)
                gained = proj * scales * gain_ref[...]
                turned = pltpu.roll(gained, HEAD_DIM // 2, 1)
                heads_ref[head, part, :] = (
                    gained * cos_ref[part, :] + turned * sin_ref[part, :]
                ).astype(BF)

    def attend(head):
        pair_head = head // 2
        for block in range(4):
            end = (block + 1) * rows
            part = pl.ds(block * rows, rows)
            scores = contract_cols(
                heads_ref[head, part, :], heads_ref[heads + pair_head, 0:end, :]
            )
            row_place = lax.broadcasted_iota(jnp.int32, (rows, end), 0) + block * rows
            col_place = lax.broadcasted_iota(jnp.int32, (rows, end), 1)
            allowed = (col_place >= start_ref[part, :]) & (col_place <= row_place)
            raised = jnp.where(allowed, jnp.exp(scores * (HEAD_DIM ** (-0.5))), 0.0)
            sums = jnp.sum(raised, axis=-1, keepdims=True)
            mixed = dot(raised.astype(BF), heads_ref[heads + kv_heads + pair_head, 0:end, :])
            mixed = mixed * (1.0 / sums)
            mixed_ref[part, head * HEAD_DIM : (head + 1) * HEAD_DIM] = mixed.astype(BF)
            lse_ref[part, head : head + 1] = jnp.log(sums)

    tiles = (heads + 2 * kv_heads) // 2
    for tile in range(tiles):
        if tile == tiles // 2:
            advance(FORWARD_PLAN[8])
        project(tile)
    advance(FORWARD_PLAN[9])

    zones = width // 512

    def turn(source, target):
        for seq_group in range(4):
            for zone in range(zones):
                at = (seq_group * zones + zone) * 128
                turned[zone * 4 + seq_group] = source[:, at : at + 128].T
        copy = pltpu.make_async_copy(turned, target, load_sem.at[4])
        copy.start()
        return copy

    for head in range(heads):
        attend(head)
        if head == 1:
            dy.forward()
        advance(FORWARD_PLAN[10 + head])
    dy.arrive()
    load_dy = pltpu.make_async_copy(dy_full, dy_all, load_sem.at[0])
    load_dy.start()

    out.arrive()
    load_out = pltpu.make_async_copy(out_full, out_w, load_sem.at[2])
    load_out.start()
    load_out.wait()

    def out_piece(seq, column):
        part = pl.ds(pl.multiple_of(seq * rows, rows), rows)
        weight = out_w[:, :, column]
        return dot(mixed_ref[part, :], weight.reshape(-1, weight.shape[-1]))

    middle_ref[...] = hidden_ref[...].astype(F32)
    token_sum = PieceSum(
        here, out_piece, middle_ref, give, got, pair, far_got, (ss, sr), 512
    )
    token_sum.send()
    advance(FORWARD_PLAN[14])
    token_sum.pass_on()
    token_sum.add_near()
    store = turn(lhs, n1_turned)
    advance(FORWARD_PLAN[15])
    token_sum.add_far()
    norm_rows(middle_ref, mlp_gain_ref, own_rows.at[1])
    n2.send()
    advance(FORWARD_PLAN[16])
    store.wait()
    load_dy.wait()
    store = turn(dy_all, dy_turned)
    advance(FORWARD_PLAN[17])
    n2.forward()
    advance(FORWARD_PLAN[18])
    n2.arrive()
    load_lhs = pltpu.make_async_copy(n2_full, lhs, load_sem.at[3])
    load_lhs.start()
    down.arrive()
    first.arrive()
    load_lhs.wait()

    def feed(gather, begin, count):
        tiles = count // 256
        spot = begin // 256

        def body(gate_w, up_w, down_w, act_ref, gate_grad, up_grad):
            gate_tile = gate_w[...].reshape(width, 256)
            up_tile = up_w[...].reshape(width, 256)
            down_tile = down_w[...]

            @pl.loop(0, 4)
            def _(index):
                part = pl.ds(pl.multiple_of(index * rows, rows), rows)
                gate = dot(lhs[part, :], gate_tile)
                up = dot(lhs[part, :], up_tile)
                act_grad = contract_cols(dy_all[part, :], down_tile)
                sigmoid = jax.nn.sigmoid(gate)
                silu = gate * sigmoid
                act_ref[part, :] = (silu * up).astype(BF)
                gate_grad[part, :] = (
                    act_grad * up * sigmoid * (1.0 + gate * (1.0 - sigmoid))
                ).astype(BF)
                up_grad[part, :] = (act_grad * silu).astype(BF)

        block = gather.whole.shape[:-1] + (256,)
        grads = first_pair if begin < chunk else second_pair
        first_spot = 0 if begin < chunk + 1 else 2 * (begin - chunk) // 256
        pltpu.emit_pipeline(
            body,
            grid=(tiles,),
            in_specs=[
                pl.BlockSpec(block, lambda t: (0, 0, t)),
                pl.BlockSpec(block, lambda t: (0, 0, t + tiles)),
                pl.BlockSpec((256, width), lambda t: (t + spot, 0)),
            ],
            out_specs=[
                pl.BlockSpec((length, 256), lambda t: (0, t + spot)),
                pl.BlockSpec((length, 256), lambda t: (0, t + first_spot)),
                pl.BlockSpec((length, 256), lambda t: (0, t + first_spot + tiles)),
            ],
        )(gather.whole, gather.whole, down_full, act_out, grads, grads)

    feed(first, 0, chunk)
    advance(FORWARD_PLAN[19])
    store.wait()
    store = turn(lhs, n2_turned)
    advance(FORWARD_PLAN[20])
    second.arrive()
    feed(second, chunk, chunk - tail)
    advance(FORWARD_PLAN[21])
    third.arrive()
    feed(third, 2 * chunk - tail, tail)
    store.wait()
    for gather in (qkv, out, first, second, third, down, n1, n2, dy):
        gather.finish()


def forward(hidden, upstream, weights, gains, segment):
    size = lax.axis_size("shard")
    quarter, outer = size // 4, size // 2
    piece, width = hidden.shape
    length = piece * 4
    heads = Q_HEADS // 4
    kv_heads = KV_HEADS // 4
    w_query, _, _, w_out, w_gate, _, w_down = weights
    own = w_query.shape[0]
    qkv_width = (heads + 2 * kv_heads) * HEAD_DIM
    units = w_down.shape[0] // 4 * size

    def shape(*dims, kind=BF):
        return jax.ShapeDtypeStruct(dims, kind)

    results = [
        shape(size, own, qkv_width),
        shape(quarter, *w_out.shape),
        shape(size, own, units),
        shape(size, own, units),
        shape(units, width),
        shape(length, width),
        shape(length, width),
        shape(length, width),
        shape(width // 128, 128, length),
        shape(width // 128, 128, length),
        shape(width // 128, 128, length),
        shape(length, units),
        shape(length, units),
        shape(length, units),
        shape(heads + kv_heads, length, HEAD_DIM, kind=F32),
        shape(heads + 2 * kv_heads, length, HEAD_DIM),
        shape(length, heads * HEAD_DIM),
        shape(length, 128, kind=F32),
        shape(piece, width, kind=F32),
        shape(length, HEAD_DIM, kind=F32),
        shape(length, HEAD_DIM, kind=F32),
        shape(1, length, kind=jnp.int32),
    ]
    powers = np.arange(HEAD_DIM // 2, dtype=np.float32) * np.float32(2.0) / np.float32(HEAD_DIM)
    inverse = np.float32(ROPE_BASE) ** -powers
    dma = pltpu.SemaphoreType.DMA
    return pl.pallas_call(
        functools.partial(forward_kernel, size),
        out_shape=results,
        in_specs=[VMEM] + [ANY] * 8 + [VMEM] * 6,
        out_specs=[ANY] * 14 + [VMEM] * 8,
        scratch_shapes=[
            pltpu.VMEM((length, width), BF),
            pltpu.VMEM((length, width), BF),
            pltpu.VMEM((width // 128, 128, length), BF),
            pltpu.VMEM((size, own, qkv_width), BF),
            pltpu.VMEM((quarter,) + w_out.shape, BF),
            pltpu.VMEM((own, qkv_width), BF),
            pltpu.VMEM(w_out.shape, BF),
            pltpu.VMEM((w_down.shape[0] // 4, width), BF),
            pltpu.VMEM((piece, width), BF),
            pltpu.VMEM(w_gate.shape, BF),
            pltpu.VMEM((own, units), BF),
            pltpu.VMEM((own, units), BF),
            pltpu.VMEM((2, piece, width), BF),
            pltpu.VMEM((2, piece, width), BF),
            pltpu.VMEM((2, piece, width), BF),
            pltpu.VMEM((piece, width), BF),
            pltpu.VMEM((piece, width), BF),
            dma((7, outer)),
            dma((7, outer)),
            dma((7, outer)),
            dma((7, outer)),
            dma((7, outer)),
            dma((7, outer)),
            dma((7,)),
            dma((3, 3)),
            dma((3, 3)),
            dma((3,)),
            dma((8,)),
            dma((3,)),
            dma((3,)),
            pltpu.VMEM((length, 1), jnp.int32),
            pltpu.VMEM((length, 128), F32),
        ],
        compiler_params=pltpu.CompilerParams(
            collective_id=0, has_side_effects=True, vmem_limit_bytes=VMEM_BYTES
        ),
        name="forward_gather",
    )(
        hidden,
        upstream,
        *weights,
        *gains,
        jnp.asarray(np.concatenate([inverse, inverse])[None], F32),
        segment[None],
    )


def add_rows(target, sources, step=16):
    groups, rows, _ = target.shape

    @pl.loop(0, rows // step)
    def _(index):
        part = pl.ds(pl.multiple_of(index * step, step), step)
        for group in range(groups):
            total = sources[0][group, part, :].astype(target.dtype)
            for source in sources[1:]:
                total = total + source[group, part, :].astype(target.dtype)
            target[group, part, :] = total


class RowSum:
    def __init__(self, here, give, keep, near, rising, falling, stage, total, sems):
        self.here, self.give, self.keep = here, give, keep
        self.near, self.rising, self.falling = near, rising, falling
        self.stage, self.total = stage, total
        self.ys, self.yr, self.us, self.ur, self.ds, self.dr, self.load = sems
        self.last = here.outer - 1

    def across(self, place):
        return remote(
            self.give.at[place],
            self.near.at[place],
            self.ys.at[place],
            self.yr.at[place],
            self.here.twin,
        )

    def up(self, place):
        peer = self.here.outer_peer(self.here.place + 1)
        return remote(
            self.keep.at[place], self.rising.at[place], self.us.at[place], self.ur.at[place], peer
        )

    def down(self, place):
        peer = self.here.outer_peer(self.here.place - 1)
        return remote(
            self.keep.at[place], self.falling.at[place], self.ds.at[place], self.dr.at[place], peer
        )

    def arrived(self, slot, send, receive):
        remote(slot, slot, send, receive, self.here.twin).wait_recv()

    def fold(self, distance):
        here = self.here
        above = here.place + distance
        below = here.place - distance

        def merge(place, line, receive, first):
            near = pltpu.make_async_copy(self.near.at[place], self.stage.at[0], self.load.at[0])
            self.arrived(self.near.at[place], self.ys.at[place], self.yr.at[place])
            near.start()

            @pl.when(first)
            def _():
                near.wait()
                add_rows(self.keep.at[place], [self.keep.at[place], self.stage.at[0]])

            @pl.when(jnp.logical_not(first))
            def _():
                self.arrived(line.at[place], self.us.at[0], receive.at[place])
                far = pltpu.make_async_copy(line.at[place], self.stage.at[1], self.load.at[1])
                far.start()
                near.wait()
                far.wait()
                add_rows(
                    self.keep.at[place], [self.keep.at[place], self.stage.at[0], self.stage.at[1]]
                )

        @pl.when(above <= self.last)
        def _():
            merge(above, self.rising, self.ur, here.place == 0)
            self.up(above).start()

        @pl.when(below >= 0)
        def _():
            merge(below, self.falling, self.dr, here.place == self.last)
            self.down(below).start()

    def finish(self):
        here = self.here
        place = here.place
        self.arrived(self.near.at[place], self.ys.at[place], self.yr.at[place])
        keep = self.keep.at[place]
        near = pltpu.make_async_copy(self.near.at[place], self.stage.at[0], self.load.at[0])
        low = pltpu.make_async_copy(self.rising.at[place], self.stage.at[1], self.load.at[1])
        high = pltpu.make_async_copy(self.falling.at[place], self.stage.at[1], self.load.at[1])
        near.start()

        @pl.when(place > 0)
        def _():
            self.arrived(self.rising.at[place], self.us.at[0], self.ur.at[place])
            low.start()
            low.wait()

        @pl.when(place == 0)
        def _():
            self.arrived(self.falling.at[place], self.ds.at[0], self.dr.at[place])
            high.start()
            high.wait()

        near.wait()

        @pl.when((place > 0) & (place < self.last))
        def _():
            add_rows(keep, [keep, self.stage.at[0], self.stage.at[1]])
            self.arrived(self.falling.at[place], self.ds.at[0], self.dr.at[place])
            high.start()
            high.wait()
            add_rows(self.total, [keep, self.stage.at[1]])

        @pl.when((place == 0) | (place == self.last))
        def _():
            add_rows(self.total, [keep, self.stage.at[0], self.stage.at[1]])

    def sent(self):
        for place in range(self.here.outer):
            self.across(place).wait_send()

    def settle(self):
        here = self.here
        for place in range(here.outer):

            @pl.when(place > here.place)
            def _():
                self.up(place).wait_send()

            @pl.when(place < here.place)
            def _():
                self.down(place).wait_send()


def compute_terms(here, give, keep, left, right, tiles, orders, senders):
    own = give.shape[2]
    per = 128 // (2 * own)
    step = 256
    for group, done in orders:
        spots = tiles(group)

        @pl.loop(0, give.shape[3] // step)
        def _(index):
            lane = pl.ds(pl.multiple_of(index * step, step), step)
            terms = dot(left(group), right(lane)).astype(BF)
            for spot, (zone, seq_group) in enumerate(spots):
                for sub in range(per):
                    at = spot * 128 + sub * 2 * own
                    even, odd = terms[at : at + own], terms[at + own : at + 2 * own]
                    place = zone * per + sub
                    keep[place, seq_group, :, lane] = jnp.where(here.half == 0, even, odd)
                    give[place, seq_group, :, lane] = jnp.where(here.half == 0, odd, even)

        for zone in done:
            for sub in range(per):
                for sender in senders:
                    sender.across(zone * per + sub).start()


class LineSum:
    def __init__(self, here, terms, rising, falling, stage, sems):
        self.here, self.terms, self.stage = here, terms, stage
        self.rising, self.falling = rising, falling
        self.us, self.ur, self.ds, self.dr, self.load = sems
        self.last = here.outer - 1

    def up(self, place):
        peer = self.here.outer_peer(self.here.place + 1)
        return remote(
            self.terms.at[place], self.rising.at[place], self.us.at[place], self.ur.at[place], peer
        )

    def down(self, place):
        peer = self.here.outer_peer(self.here.place - 1)
        return remote(
            self.terms.at[place], self.falling.at[place], self.ds.at[place], self.dr.at[place], peer
        )

    def merge(self, place, line, receive):
        slot = line.at[place]
        remote(slot, slot, self.us.at[0], receive.at[place], self.here.twin).wait_recv()
        copy = pltpu.make_async_copy(slot, self.stage.at[0], self.load.at[0])
        copy.start()
        copy.wait()
        add_rows(self.terms.at[place], [self.terms.at[place], self.stage.at[0]])

    def fold(self, distance):
        here = self.here
        above = here.place + distance
        below = here.place - distance

        @pl.when(above <= self.last)
        def _():
            @pl.when(here.place > 0)
            def _():
                self.merge(above, self.rising, self.ur)

            self.up(above).start()

        @pl.when(below >= 0)
        def _():
            @pl.when(here.place < self.last)
            def _():
                self.merge(below, self.falling, self.dr)

            self.down(below).start()

    def gather(self):
        place = self.here.place

        @pl.when(place > 0)
        def _():
            self.merge(place, self.rising, self.ur)

        @pl.when(place < self.last)
        def _():
            self.merge(place, self.falling, self.dr)

    def settle(self):
        here = self.here
        for place in range(here.outer):

            @pl.when(place > here.place)
            def _():
                self.up(place).wait_send()

            @pl.when(place < here.place)
            def _():
                self.down(place).wait_send()


class LineFirstSum(RowSum):
    def __init__(self, here, give, keep, near, lines, stage, total, sems, twin_sems):
        self.here, self.give, self.keep = here, give, keep
        self.near, self.stage, self.total = near, stage, total
        self.ys, self.yr, self.load = sems[0], sems[1], sems[6]
        self.lines = [
            LineSum(here, terms, rising, falling, stage, kinds[2:])
            for terms, (rising, falling), kinds in (
                (give, lines[0], twin_sems),
                (keep, lines[1], sems),
            )
        ]

    def fold(self, distance):
        for line in self.lines:
            line.fold(distance)

    def pass_on(self):
        self.lines[0].gather()
        self.across(self.here.place).start()
        self.lines[1].gather()

    def finish(self):
        place = self.here.place
        self.arrived(self.near.at[place], self.ys.at[place], self.yr.at[place])
        near = pltpu.make_async_copy(self.near.at[place], self.stage.at[0], self.load.at[0])
        near.start()
        near.wait()
        add_rows(self.total, [self.keep.at[place], self.stage.at[0]])

    def sent(self):
        self.across(self.here.place).wait_send()

    def settle(self):
        for line in self.lines:
            line.settle()


class RowSpread:
    def __init__(self, here, rows, whole, sems):
        self.here, self.rows, self.whole = here, rows, whole
        self.send_sems, self.recv_sems, self.local = sems

    def copy(self, amount):
        seq = lax.rem(self.here.seq + amount, 4)
        return remote(
            self.rows.at[seq],
            self.whole.at[self.here.seq],
            self.send_sems.at[amount - 1],
            self.recv_sems.at[amount - 1],
            {"seq": seq},
        )

    def keep(self):
        seq = self.here.seq
        return pltpu.make_async_copy(self.rows.at[seq], self.whole.at[seq], self.local)

    def send(self):
        for amount in (2, 3, 1):
            self.copy(amount).start()
        self.keep().start()

    def arrive(self):
        for amount in (1, 2, 3):
            self.copy(amount).wait_recv()
        self.keep().wait()

    def finish(self):
        for amount in (1, 2, 3):
            self.copy(amount).wait_send()


class TokenSum:
    def __init__(self, here, part, got, pair, far_got, base, sems):
        self.here, self.part, self.got, self.pair = here, part, got, pair
        self.far_got, self.base = far_got, base
        self.send_sems, self.recv_sems = sems
        self.rows = part.shape[0] // 4

    def piece(self, seq):
        return pl.ds(pl.multiple_of(seq * self.rows, self.rows), self.rows)

    def to_mate(self, index):
        here = self.here
        chip = here.chip if index else 1 - here.chip
        seq = chip * 2 + 1 - here.core
        return remote(
            self.part.at[self.piece(seq), :],
            self.got.at[index],
            self.send_sems.at[index],
            self.recv_sems.at[index],
            here.mate,
        )

    def to_far(self):
        return remote(
            self.pair, self.far_got, self.send_sems.at[2], self.recv_sems.at[2], self.here.far
        )

    def send(self):
        self.to_mate(0).start()
        self.to_mate(1).start()

    def loop(self, body):
        @pl.loop(0, self.rows // 32)
        def _(index):
            body(index * 32)

    def pass_on(self):
        self.to_mate(0).wait_recv()
        begin = self.here.far_seq * self.rows

        def body(at):
            part = pl.ds(pl.multiple_of(at, 32), 32)
            source = pl.ds(pl.multiple_of(begin + at, 32), 32)
            total = self.part[source, :].astype(F32) + self.got[0, part, :].astype(F32)
            self.pair[part, :] = total.astype(BF)

        self.loop(body)
        self.to_far().start()

    def add_near(self):
        self.to_mate(1).wait_recv()
        begin = self.here.seq * self.rows

        def body(at):
            part = pl.ds(pl.multiple_of(at, 32), 32)
            source = pl.ds(pl.multiple_of(begin + at, 32), 32)
            self.base[part, :] += self.part[source, :].astype(F32) + self.got[1, part, :].astype(F32)

        self.loop(body)
        self.to_mate(0).wait_send()
        self.to_mate(1).wait_send()

    def add_far(self):
        self.to_far().wait_recv()

        def body(at):
            part = pl.ds(pl.multiple_of(at, 32), 32)
            self.base[part, :] += self.far_got[part, :].astype(F32)

        self.loop(body)
        self.to_far().wait_send()


class GainSum:
    def __init__(self, here, parts, arrived, sems):
        self.here, self.parts, self.arrived = here, parts, arrived
        self.send_sems, self.recv_sems = sems
        self.peers = [here.mate, here.far, here.twin] + here.line_peers()

    def copy(self, index):
        return remote(
            self.parts.at[index],
            self.arrived.at[index],
            self.send_sems.at[index],
            self.recv_sems.at[index],
            self.peers[index],
        )

    def start(self):
        self.copy(0).start()

    def hop(self, index):
        self.copy(index).wait()
        self.parts[index + 1] = self.parts[index] + self.arrived[index]
        if index + 1 < len(self.peers):
            self.copy(index + 1).start()


PLAN = (
    (("down_a", 3),),
    (("down_a", 2), ("down_b", 3),),
    (("down_a", 1), ("down_b", 2),),
    (),
    (),
    (("first", 3), ("down_b", 1),),
    (("first", 2), ("down_b", "finish"),),
    (("second", 3), ("first", 1),),
    (("second", 2),),
    (),
    (("first", "finish"),),
    (("out", 3), ("second", 1),),
    (),
    (("out", 2), ("query", 3), ("down_a", "pass"), ("key", 3), ("out", 1),),
    (("query", 2), ("key", 2), ("second", "finish"), ("out", "finish"), ("query", 1), ("key", 1),),
    (("query", "finish"), ("key", "finish"),),
    (("down_a", "finish"),),
)


def backward_kernel(
    size,
    n1_hbm,
    dy_hbm,
    n2_hbm,
    act_hbm,
    first_hbm,
    second_hbm,
    proj_hbm,
    heads_ref,
    mixed_ref,
    lse_ref,
    middle_hbm,
    hidden_hbm,
    dy_own,
    qkv_full,
    out_full,
    first_full,
    second_full,
    down_full,
    attn_gain_ref,
    mlp_gain_ref,
    query_gain_ref,
    key_gain_ref,
    cos_ref,
    sin_ref,
    start_ref,
    grad_in,
    gains_out,
    grad_out,
    hidden_out,
    down_rows,
    first_rows,
    second_rows,
    qkv_rows,
    da_hbm,
    near_mlp,
    rising_mlp,
    falling_mlp,
    rising_twin,
    falling_twin,
    near_qkv,
    rising_qkv,
    falling_qkv,
    near_out,
    rising_out,
    falling_out,
    lhs,
    turned,
    first_r,
    second_r,
    give,
    keep,
    give_out,
    keep_out,
    stage,
    stage_out,
    dout_ref,
    da_own,
    got,
    far_got,
    pair,
    middle_grad,
    proj_buf,
    lse_t,
    delta,
    delta_t,
    dk_sum,
    dv_sum,
    gain_rows,
    gain_got,
    ys,
    yr,
    us,
    ur,
    ds,
    dr,
    fold_load,
    spread_s,
    spread_r,
    spread_l,
    sum_s,
    sum_r,
    ts,
    tr,
    token_local,
    gs,
    gr,
    load_sem,
    credit,
):
    here = Place(size)
    length, width = lhs.shape
    rows = length // 4
    units = first_r.shape[1]
    chunk = units // 2
    ff_part = units // size
    heads = mixed_ref.shape[1] // HEAD_DIM
    kv_heads = heads // 2
    qkv_width = qkv_full.shape[2]
    last = here.outer - 1
    scale = HEAD_DIM ** (-0.5)

    def load(source, target, index):
        copy = pltpu.make_async_copy(source, target, load_sem.at[index])
        copy.start()
        return copy

    def sems(index):
        return tuple(kind.at[index] for kind in (ys, yr, us, ur, ds, dr, fold_load))

    thin = qkv_width // 2
    cut = units * 2 // 3
    lanes = {
        "down_a": slice(0, cut),
        "down_b": slice(cut, units),
        "query": slice(0, thin),
        "key": slice(thin, 2 * thin),
    }

    def part(ref, name):
        return ref.at[:, :, :, lanes[name]]

    def row_sum(index, give_ref, keep_ref, near, rising, falling, stage_ref, total):
        return RowSum(
            here, give_ref, keep_ref, near, rising, falling, stage_ref, total, sems(index)
        )

    jobs = {
        "down_a": LineFirstSum(
            here,
            part(give.at[2], "down_a"),
            part(keep.at[0], "down_a"),
            part(near_mlp.at[0], "down_a"),
            (
                (rising_twin, falling_twin),
                (part(rising_mlp.at[0], "down_a"), part(falling_mlp.at[0], "down_a")),
            ),
            part(stage, "down_a"),
            keep.at[0, here.place, :, :, lanes["down_a"]],
            sems(0),
            sems(5),
        ),
        "down_b": row_sum(
            6,
            part(give.at[2], "down_b"),
            part(keep.at[0], "down_b"),
            part(near_mlp.at[0], "down_b"),
            part(rising_mlp.at[0], "down_b"),
            part(falling_mlp.at[0], "down_b"),
            part(stage, "down_b"),
            keep.at[0, here.place, :, :, lanes["down_b"]],
        ),
        "out": row_sum(
            4, give_out, keep_out, near_out, rising_out, falling_out, stage_out, grad_out
        ),
    }
    for index, name in ((1, "first"), (2, "second")):
        jobs[name] = row_sum(
            index,
            give.at[2 - index],
            keep.at[index],
            near_mlp.at[index],
            rising_mlp.at[index],
            falling_mlp.at[index],
            stage,
            keep.at[index, here.place],
        )
    for index, name in ((3, "query"), (7, "key")):
        jobs[name] = row_sum(
            index,
            part(give.at[1], name),
            part(second_r, name),
            part(near_qkv, name),
            part(rising_qkv, name),
            part(falling_qkv, name),
            part(stage, name),
            second_r.at[here.place, :, :, lanes[name]],
        )
    zones = width // 512

    def zone_at(index):
        zone = here.place // (here.outer // zones)
        return (
            3 * (1 - zone // 2),
            lax.rem(2 + 3 * zone, 5),
            1 + lax.rem(zone, 2),
            zone,
        )[index]

    zone_order = [zone_at(index) for index in range(zones)]
    by_zone = [(zone, (zone,)) for zone in zone_order]

    spreads = {}
    for index, (name, whole) in enumerate(
        (
            ("down_a", down_rows.at[:, :, lanes["down_a"]]),
            ("down_b", down_rows.at[:, :, lanes["down_b"]]),
            ("first", first_rows),
            ("second", second_rows),
            ("query", qkv_rows.at[:, :, lanes["query"]]),
            ("key", qkv_rows.at[:, :, lanes["key"]]),
        )
    ):
        kinds = (spread_s.at[index], spread_r.at[index], spread_l.at[index])
        spreads[name] = RowSpread(here, jobs[name].total, whole, kinds)

    def token_sum(index, base):
        return TokenSum(
            here, lhs, got, pair, far_got, base, (sum_s.at[index], sum_r.at[index])
        )

    sum_mlp = token_sum(0, middle_grad)
    sum_hidden = token_sum(1, grad_in)
    sum_attn = token_sum(2, grad_in)
    da = TokenGather(here, da_own, da_hbm, (ts, tr, token_local.at[0]))

    def model_tiles(group):
        return [(group, seq_group) for seq_group in range(4)]

    def first_columns(lane):
        return first_r[:, lane]

    def model_left(group):
        return turned[pl.ds(group * 4, 4)].reshape(512, length)

    def advance(steps):
        for name, step in steps:
            job = jobs[name]
            if step == "pass":
                job.pass_on()
            elif step == "finish":
                job.finish()
                if name in spreads:
                    spreads[name].send()
            else:
                for distance in range(last * step // 3, last * (step - 1) // 3, -1):
                    job.fold(distance)

    load_turned = load(dy_hbm, turned, 0)
    load_act = load(act_hbm, first_r, 1)
    load_middle = load(middle_hbm, grad_in, 2)
    load_dy = load(dy_own, da_own, 4)
    load_second = load(second_hbm, second_r, 3)
    here.greet(wide=True)
    load_turned.wait()
    load_act.wait()
    def model_terms(give_ref, keep_ref, right, senders):
        compute_terms(
            here, give_ref, keep_ref, model_left, right, model_tiles, by_zone, senders
        )

    model_terms(give.at[2], keep.at[0], first_columns, [jobs["down_b"]])
    advance(PLAN[0])
    load_turned = load(n2_hbm, turned, 0)
    load_first = load(first_hbm, first_r, 1)
    load_first.wait()
    load_second.wait()

    own = width // size
    slabs = 256 // own

    def dn2_body(first_w, second_w):
        lane = pl.ds(pl.multiple_of(pl.program_id(0) * 256, 256), 256)
        first_tile = first_w[...].reshape(256, units)
        second_tile = second_w[...].reshape(256, units)

        @pl.loop(0, 4)
        def _(index):
            part = pl.ds(pl.multiple_of(index * rows, rows), rows)
            total = contract_cols(first_r[part, :], first_tile)
            blocks = pl.ds(index * (here.outer // 4), here.outer // 4)
            second_rows = second_r[blocks].reshape(rows, units)
            total = total + contract_cols(second_rows, second_tile)
            lhs[part, lane] = total.astype(BF)

    slab = pl.BlockSpec((slabs, own, units), lambda t: (t, 0, 0))
    pltpu.emit_pipeline(dn2_body, grid=(width // 256,), in_specs=[slab, slab])(
        first_full, second_full
    )
    sum_mlp.send()
    middle_grad[...] = jnp.zeros_like(middle_grad)
    load_turned.wait()
    advance(PLAN[1])
    sum_mlp.pass_on()
    sum_mlp.add_near()
    model_terms(give.at[1], keep.at[1], first_columns, [jobs["first"]])
    load_act = load(act_hbm, first_r, 1)
    advance(PLAN[2])
    sum_mlp.add_far()

    load_middle.wait()
    load_dy.wait()
    gain_rows[0] = jnp.zeros_like(gain_rows[0])
    narrow = 16

    @pl.loop(0, rows // narrow)
    def _(index):
        part = pl.ds(pl.multiple_of(index * narrow, narrow), narrow)
        values = grad_in[part, :]
        scales = lax.rsqrt(jnp.mean(values * values, axis=-1, keepdims=True) + EPSILON)
        normed = values * scales
        update = middle_grad[part, :]
        gain_rows[0, 1:2, :] += jnp.sum(update * normed, axis=0, keepdims=True)
        upper = update * mlp_gain_ref[...]
        inner = jnp.mean(upper * normed, axis=-1, keepdims=True)
        grad = da_own[part, :].astype(F32) + scales * (upper - normed * inner)
        middle_grad[part, :] = grad
        da_own[part, :] = grad.astype(BF)

    da.send()
    advance(PLAN[3])
    model_terms(
        give.at[0],
        keep.at[2],
        lambda lane: second_r[:, :, :, lane].reshape(length, -1),
        [jobs["second"]],
    )
    advance(PLAN[4])

    def hidden_body(weight):
        lane = pl.ds(pl.multiple_of(pl.program_id(0) * 256, 256), 256)
        tile = weight[...]

        @pl.loop(0, 4)
        def _(index):
            part = pl.ds(pl.multiple_of(index * rows, rows), rows)
            lhs[part, lane] = dot(first_r[part, :], tile).astype(BF)

    load_act.wait()
    pltpu.emit_pipeline(
        hidden_body,
        grid=(width // 256,),
        in_specs=[pl.BlockSpec((units, 256), lambda t: (0, t))],
    )(down_full)
    da.mate_arrived()
    sum_hidden.send()
    da.forward()
    advance(PLAN[5])
    sum_hidden.pass_on()
    sum_hidden.add_near()
    advance(PLAN[6])
    da.rest_arrived()
    da.finish()
    load_lhs = load(da_hbm, lhs, 0)
    load_own = load(hidden_hbm, da_own, 2)
    load_lhs.wait()

    def dout_body(weight):
        lane = pl.ds(pl.multiple_of(pl.program_id(0) * 256, 256), 256)
        tile = weight[...].reshape(256, width)

        @pl.loop(0, 4)
        def _(index):
            part = pl.ds(pl.multiple_of(index * rows, rows), rows)
            dout_ref[part, lane] = contract_cols(lhs[part, :], tile).astype(BF)

    out_blocks, out_rows = out_full.shape[:2]
    pltpu.emit_pipeline(
        dout_body,
        grid=(out_blocks * out_rows // 256,),
        in_specs=[pl.BlockSpec((256 // out_rows, out_rows, width), lambda t: (t, 0, 0))],
    )(out_full)

    for head in range(heads):
        turned[head] = mixed_ref[:, head * HEAD_DIM : (head + 1) * HEAD_DIM].T
    compute_terms(
        here,
        give_out,
        keep_out,
        lambda group: turned[0:heads].reshape(heads * HEAD_DIM, length),
        lambda lane: lhs[:, lane],
        lambda group: [(zone, 0) for zone in range(heads)],
        [(0, zone_order)],
        [jobs["out"]],
    )
    load_turned = load(n1_hbm, turned, 0)
    sum_hidden.add_far()
    for index, peer in enumerate((here.mate, here.far)):
        pl.semaphore_signal(credit.at[index], inc=1, device_id=peer, device_id_type=MESH)

    @pl.loop(0, rows // 32)
    def _(index):
        part = pl.ds(pl.multiple_of(index * 32, 32), 32)
        pair[part, :] = grad_in[part, :].astype(BF)

    store_hidden = load(pair, hidden_out, 1)
    advance(PLAN[7])

    lse_t[...] = lse_ref[...].T[0:8]
    delta[...] = jnp.zeros_like(delta)
    for head in range(heads):
        lane = slice(head * HEAD_DIM, (head + 1) * HEAD_DIM)
        terms = dout_ref[:, lane].astype(F32) * mixed_ref[:, lane].astype(F32)
        delta[:, head : head + 1] = jnp.sum(terms, axis=-1, keepdims=True)
    delta_t[...] = delta[...].T[0:8]
    def through_norm(grad, head, part, gain_ref, gain_row):
        proj = proj_buf[part, :]
        scales = lax.rsqrt(jnp.mean(proj * proj, axis=-1, keepdims=True) + EPSILON)
        normed = proj * scales
        grad = grad.astype(F32)
        upper = grad * cos_ref[part, :] - pltpu.roll(grad, HEAD_DIM // 2, 1) * sin_ref[part, :]
        gain_rows[0, 2:3, gain_row * HEAD_DIM : (gain_row + 1) * HEAD_DIM] += jnp.sum(
            upper * normed, axis=0, keepdims=True
        )
        upper = upper * gain_ref[...]
        inner = jnp.mean(upper * normed, axis=-1, keepdims=True)
        result = (scales * (upper - normed * inner)).astype(BF)
        first_r[part, head * HEAD_DIM : (head + 1) * HEAD_DIM] = result

    for head in range(heads):
        pair_head = head // 2
        load_proj = load(proj_hbm.at[head], proj_buf, 4)
        if head % 2 == 0:
            dk_sum[...] = jnp.zeros_like(dk_sum)
            dv_sum[...] = jnp.zeros_like(dv_sum)
        for block in range(4):
            end = (block + 1) * rows
            part = pl.ds(block * rows, rows)
            queries = heads_ref[head, part, :]
            keys = heads_ref[heads + pair_head, 0:end, :]
            values = heads_ref[heads + kv_heads + pair_head, 0:end, :]
            out_grad = dout_ref[part, head * HEAD_DIM : (head + 1) * HEAD_DIM]
            scores = contract_cols(keys, queries)
            key_place = lax.broadcasted_iota(jnp.int32, (end, rows), 0)
            query_place = lax.broadcasted_iota(jnp.int32, (end, rows), 1) + block * rows
            allowed = (key_place >= start_ref[:, part]) & (key_place <= query_place)
            weights = jnp.exp(scores * scale - lse_t[head : head + 1, part])
            weights = jnp.where(allowed, weights, 0.0)
            weight_grad = contract_cols(values, out_grad)
            inner = delta_t[head : head + 1, part]
            score_grad = (weights * (weight_grad - inner)).astype(BF)
            dk_sum[0:end, :] += dot(score_grad, queries) * scale
            dv_sum[0:end, :] += dot(weights.astype(BF), out_grad)
            query_grad = (contract_rows(score_grad, keys) * scale).astype(BF)
            if block == 0:
                load_proj.wait()
            through_norm(query_grad, head, part, query_gain_ref, 0)
        if head % 2:
            key = heads + pair_head
            value_at = (heads + kv_heads + pair_head) * HEAD_DIM
            load(proj_hbm.at[key], proj_buf, 4).wait()

            @pl.loop(0, 4)
            def _(index):
                part = pl.ds(pl.multiple_of(index * rows, rows), rows)
                through_norm(dk_sum[part, :].astype(BF), key, part, key_gain_ref, 1)
                first_r[part, value_at : value_at + HEAD_DIM] = dv_sum[part, :].astype(BF)

        advance(PLAN[8 + head])

    load_turned.wait()
    jobs["first"].sent()
    store_hidden.wait()
    proj_grads = first_r.at[:, 0:qkv_width]
    model_terms(
        give.at[1, :, :, :, 0:qkv_width],
        second_r.at[:, :, :, 0:qkv_width],
        first_columns,
        [jobs["query"], jobs["key"]],
    )
    advance(PLAN[12])

    def dn1_body(weight):
        lane = pl.ds(pl.multiple_of(pl.program_id(0) * 256, 256), 256)
        tile = weight[...].reshape(256, qkv_width)

        @pl.loop(0, 4)
        def _(index):
            part = pl.ds(pl.multiple_of(index * rows, rows), rows)
            lhs[part, lane] = contract_cols(proj_grads[part, :], tile).astype(BF)

    pltpu.emit_pipeline(
        dn1_body,
        grid=(width // 256,),
        in_specs=[pl.BlockSpec((slabs, own, qkv_width), lambda t: (t, 0, 0))],
    )(qkv_full)
    grad_in[...] = jnp.zeros_like(grad_in)
    pl.semaphore_wait(credit.at[0], 1)
    pl.semaphore_wait(credit.at[1], 1)
    sum_attn.send()
    advance(PLAN[13])
    sum_attn.pass_on()
    sum_attn.add_near()
    advance(PLAN[14])
    sum_attn.add_far()
    load_own.wait()

    @pl.loop(0, rows // narrow)
    def _(index):
        part = pl.ds(pl.multiple_of(index * narrow, narrow), narrow)
        values = da_own[part, :].astype(F32)
        scales = lax.rsqrt(jnp.mean(values * values, axis=-1, keepdims=True) + EPSILON)
        normed = values * scales
        update = grad_in[part, :]
        gain_rows[0, 0:1, :] += jnp.sum(update * normed, axis=0, keepdims=True)
        upper = update * attn_gain_ref[...]
        inner = jnp.mean(upper * normed, axis=-1, keepdims=True)
        grad_in[part, :] = middle_grad[part, :] + scales * (upper - normed * inner)

    gain_sum = GainSum(here, gain_rows, gain_got, (gs, gr))
    gain_sum.start()
    advance(PLAN[15])
    hops = list(range(len(gain_sum.peers)))
    for name, step in PLAN[16]:
        advance([(name, step)])
        if hops:
            gain_sum.hop(hops.pop(0))
    for index in hops:
        gain_sum.hop(index)
    gains_out[...] = gain_rows[gain_rows.shape[0] - 1]
    for spread_rows in spreads.values():
        spread_rows.arrive()
    for name, job in jobs.items():
        if name != "first":
            job.sent()
    for job in jobs.values():
        job.settle()
    for job in spreads.values():
        job.finish()


def backward(saved, weights, own, gains, tables, starts):
    size = lax.axis_size("shard")
    outer = size // 2
    (n1, dy, n2, act, first, second, proj, heads_all, mixed, lse, middle) = saved
    length, width = heads_all.shape[1], middle.shape[1]
    piece = length // 4
    units = act.shape[1]
    qkv_width = weights[0].shape[2]
    rows = width // (4 * size)
    q_width = mixed.shape[1]

    def shape(*dims, kind=BF):
        return jax.ShapeDtypeStruct(dims, kind)

    results = [
        shape(piece, width, kind=F32),
        shape(8, width, kind=F32),
        shape(1, rows, width, kind=F32),
        shape(piece, width),
        shape(4, rows, units),
        shape(4, rows, units),
        shape(4, rows, units),
        shape(4, rows, qkv_width),
        shape(length, width),
    ]
    results += [shape(3, outer, 4, rows, units)] * 3
    results += [shape(outer, 4, rows, units * 2 // 3)] * 2
    results += [shape(outer, 4, rows, qkv_width)] * 3
    results += [shape(outer, 1, rows, width)] * 3
    dma = pltpu.SemaphoreType.DMA
    hops = 3 + outer.bit_length() - 1
    vmem = pltpu.VMEM
    return pl.pallas_call(
        functools.partial(backward_kernel, size),
        out_shape=results,
        in_specs=[ANY] * 7 + [VMEM] * 3 + [ANY] * 8 + [VMEM] * 7,
        out_specs=[VMEM] * 3 + [ANY] * (len(results) - 3),
        scratch_shapes=[
            vmem((length, width), BF),
            vmem((width // 128, 128, length), BF),
            vmem((length, units), BF),
            vmem((outer, 4, rows, units), BF),
            vmem((3, outer, 4, rows, units), BF),
            vmem((3, outer, 4, rows, units), BF),
            vmem((outer, 1, rows, width), BF),
            vmem((outer, 1, rows, width), BF),
            vmem((2, 4, rows, units), BF),
            vmem((2, 1, rows, width), BF),
            vmem((length, q_width), BF),
            vmem((piece, width), BF),
            vmem((2, piece, width), BF),
            vmem((piece, width), BF),
            vmem((piece, width), BF),
            vmem((piece, width), F32),
            vmem((length, HEAD_DIM), F32),
            vmem((8, length), F32),
            vmem((length, 128), F32),
            vmem((8, length), F32),
            vmem((length, HEAD_DIM), F32),
            vmem((length, HEAD_DIM), F32),
            vmem((hops + 1, 8, width), F32),
            vmem((hops, 8, width), F32),
            dma((8, outer)),
            dma((8, outer)),
            dma((8, outer)),
            dma((8, outer)),
            dma((8, outer)),
            dma((8, outer)),
            dma((8, 3)),
            dma((6, 3)),
            dma((6, 3)),
            dma((6,)),
            dma((3, 3)),
            dma((3, 3)),
            dma((3,)),
            dma((3,)),
            dma((1,)),
            dma((hops,)),
            dma((hops,)),
            dma((5,)),
            pltpu.SemaphoreType.REGULAR((2,)),
        ],
        compiler_params=pltpu.CompilerParams(
            collective_id=1, has_side_effects=True, vmem_limit_bytes=VMEM_BYTES
        ),
        name="backward_sums",
    )(
        n1,
        dy,
        n2,
        act,
        first,
        second.reshape(outer, 4, rows, units),
        proj,
        heads_all,
        mixed,
        lse,
        middle,
        *own,
        *weights,
        *gains,
        *tables,
        starts,
    )


def finish_kernel(
    size,
    grad_in,
    gains,
    grad_out,
    hidden_out,
    down_rows,
    first_rows,
    second_rows,
    qkv_rows,
    grad_in_out,
    grad_out_out,
    hidden_out_out,
    grad_query,
    grad_key,
    grad_value,
    grad_gate,
    grad_up,
    grad_down,
    attn_gain,
    mlp_gain,
    query_gain,
    key_gain,
    grad_in_buf,
    grad_out_buf,
    hidden_buf,
    down_buf,
    first_buf,
    second_buf,
    qkv_buf,
    query_buf,
    key_buf,
    value_buf,
    gate_buf,
    up_buf,
    wide_buf,
    load_sems,
    store_sems,
):
    units = down_buf.shape[2]
    chunk = units // 2
    ff_part = units // size
    most, tail = chunk - 256, 256
    stores = []

    def load(source, target, index):
        copy = pltpu.make_async_copy(source, target, load_sems.at[index])
        copy.start()
        return copy

    def store(source, target):
        copy = pltpu.make_async_copy(source, target, store_sems.at[len(stores)])
        copy.start()
        stores.append(copy)

    loads = [
        load(source, target, index)
        for index, (source, target) in enumerate(
            (
                (down_rows, down_buf),
                (first_rows, first_buf),
                (second_rows, second_buf),
                (qkv_rows, qkv_buf),
                (grad_in, grad_in_buf),
                (hidden_out, hidden_buf),
                (grad_out, grad_out_buf),
            )
        )
    ]

    def place(read, target):
        @pl.loop(0, target.shape[0] // 16)
        def _(index):
            part = pl.ds(pl.multiple_of(index * 16, 16), 16)
            values = [read(seq, part).astype(F32) for seq in range(4)]
            for begin in range(0, size, size // 8):
                pieces = [
                    values[seq][:, block * ff_part : (block + 1) * ff_part]
                    for block in range(begin, begin + size // 8)
                    for seq in range(4)
                ]
                lane = slice(begin * 4 * ff_part, (begin + size // 8) * 4 * ff_part)
                target[part, lane] = jnp.concatenate(pieces, axis=1)

    def side(index):
        at = 2 * most + index * tail

        def read(seq, part):
            return jnp.concatenate(
                [
                    first_buf[seq, part, index * chunk : (index + 1) * chunk],
                    second_buf[seq, part, index * most : (index + 1) * most],
                    second_buf[seq, part, at : at + tail],
                ],
                axis=1,
            )

        return read

    loads[0].wait()
    place(lambda seq, part: down_buf[seq, part, :], wide_buf)
    store(wide_buf, grad_down)
    loads[1].wait()
    loads[2].wait()
    place(side(0), gate_buf)
    store(gate_buf, grad_gate)
    place(side(1), up_buf)
    store(up_buf, grad_up)
    loads[4].wait()
    store(grad_in_buf, grad_in_out)
    loads[5].wait()
    store(hidden_buf, hidden_out_out)
    loads[6].wait()
    store(grad_out_buf, grad_out_out)
    loads[3].wait()
    at = 0
    for buf, target in ((query_buf, grad_query), (key_buf, grad_key), (value_buf, grad_value)):
        count = buf.shape[1] // 4
        for seq in range(4):
            buf[:, seq * count : (seq + 1) * count] = qkv_buf[seq, :, at : at + count].astype(F32)
        at += count
        store(buf, target)
    attn_gain[...] = gains[0:1, :]
    mlp_gain[...] = gains[1:2, :]
    query_gain[...] = gains[2:3, 0:HEAD_DIM]
    key_gain[...] = gains[2:3, HEAD_DIM : 2 * HEAD_DIM]
    for copy in stores:
        copy.wait()


def finish(grad_in, gains, grad_out, hidden_out, down_rows, first_rows, second_rows, qkv_rows):
    size = lax.axis_size("shard")
    piece, width = grad_in.shape
    rows, units = down_rows.shape[1:]
    qkv_width = qkv_rows.shape[2]

    def shape(*dims, kind=F32):
        return jax.ShapeDtypeStruct(dims, kind)

    results = [
        shape(piece, width),
        shape(1, rows, width),
        shape(piece, width, kind=BF),
        shape(rows, 2 * qkv_width),
        shape(rows, qkv_width),
        shape(rows, qkv_width),
        shape(rows, 4 * units),
        shape(rows, 4 * units),
        shape(rows, 4 * units),
        shape(1, width),
        shape(1, width),
        shape(1, HEAD_DIM),
        shape(1, HEAD_DIM),
    ]
    return pl.pallas_call(
        functools.partial(finish_kernel, size),
        out_shape=results,
        in_specs=[ANY, VMEM] + [ANY] * 6,
        out_specs=[ANY] * 9 + [VMEM] * 4,
        scratch_shapes=[
            pltpu.VMEM((piece, width), F32),
            pltpu.VMEM((1, rows, width), F32),
            pltpu.VMEM((piece, width), BF),
            pltpu.VMEM((4, rows, units), BF),
            pltpu.VMEM((4, rows, units), BF),
            pltpu.VMEM((4, rows, units), BF),
            pltpu.VMEM((4, rows, qkv_width), BF),
            pltpu.VMEM((rows, 2 * qkv_width), F32),
            pltpu.VMEM((rows, qkv_width), F32),
            pltpu.VMEM((rows, qkv_width), F32),
            pltpu.VMEM((rows, 4 * units), F32),
            pltpu.VMEM((rows, 4 * units), F32),
            pltpu.VMEM((rows, 4 * units), F32),
            pltpu.SemaphoreType.DMA((7,)),
            pltpu.SemaphoreType.DMA((9,)),
        ],
        compiler_params=pltpu.CompilerParams(vmem_limit_bytes=VMEM_BYTES),
        name="finish",
    )(grad_in, gains, grad_out, hidden_out, down_rows, first_rows, second_rows, qkv_rows)


def local(
    hidden_in,
    segment_ids,
    norm_attn_gain,
    w_query,
    w_key,
    w_value,
    query_gain,
    key_gain,
    w_out,
    norm_mlp_gain,
    w_gate,
    w_up,
    w_down,
    out_cotangent,
):
    segment = segment_ids[0]
    gains = (norm_attn_gain[None], norm_mlp_gain[None], query_gain[None], key_gain[None])
    results = forward(
        hidden_in[0],
        out_cotangent[0],
        (w_query, w_key, w_value, w_out, w_gate, w_up, w_down),
        gains,
        segment,
    )
    (
        grad_in,
        grad_out,
        hidden_out,
        grad_query,
        grad_key,
        grad_value,
        grad_gate,
        grad_up,
        grad_down,
        attn_gain,
        mlp_gain,
        query_grad,
        key_grad,
    ) = finish(
        *backward(
            results[8:19],
            results[:5],
            (hidden_in[0], out_cotangent[0]),
            gains,
            results[19:21],
            results[21],
        )[:8]
    )
    return (
        hidden_out[None],
        grad_in[None],
        attn_gain[0],
        grad_query,
        grad_key,
        grad_value,
        query_grad[0],
        key_grad[0],
        grad_out[0],
        mlp_gain[0],
        grad_gate,
        grad_up,
        grad_down.T,
    )


def solution(mesh):
    return jax.shard_map(
        local,
        mesh=mesh,
        in_specs=(
            P("shard", "seq", None),
            P("shard", None),
            P(),
            P("shard", None),
            P("shard", None),
            P("shard", None),
            P(),
            P(),
            P("shard", None),
            P(),
            P("shard", None),
            P("shard", None),
            P("shard", None),
            P("shard", "seq", None),
        ),
        out_specs=(
            P("shard", "seq", None),
            P("shard", "seq", None),
            P(),
            P(("seq", "shard"), None),
            P(("seq", "shard"), None),
            P(("seq", "shard"), None),
            P(),
            P(),
            P(("seq", "shard"), None),
            P(),
            P(("seq", "shard"), None),
            P(("seq", "shard"), None),
            P(None, ("seq", "shard")),
        ),
        check_vma=False,
    )
```

```python
import functools

import jax
import jax.numpy as jnp
import numpy as np
from jax import lax
from jax.experimental import pallas as pl
from jax.experimental.pallas import tpu as pltpu
from jax.sharding import PartitionSpec as P

Q_HEADS = 16
KV_HEADS = 8
HEAD_DIM = 128
EPSILON = 1e-06
ROPE_BASE = 1000000.0
NEGATIVE = -1e30
BF = jnp.bfloat16
F32 = jnp.float32
MESH = pl.DeviceIdType.MESH
ANY = pl.BlockSpec(memory_space=pl.ANY)
VMEM = pl.BlockSpec(memory_space=pltpu.VMEM)
VMEM_BYTES = 62 * 1024 * 1024


def dot(left, right):
    return jnp.dot(left, right, preferred_element_type=F32)


def contract_rows(left, right):
    return lax.dot_general(left, right, (((0,), (0,)), ((), ())), preferred_element_type=F32)


def contract_cols(left, right):
    return lax.dot_general(left, right, (((1,), (1,)), ((), ())), preferred_element_type=F32)


class Place:
    def __init__(self, size):
        self.size = size
        self.outer = size // 2
        self.quarter = size // 4
        self.seq = lax.axis_index("seq")
        self.shard = lax.axis_index("shard")
        self.chip = self.seq // 2
        self.core = lax.rem(self.seq, 2)
        self.place = self.shard // 2
        self.half = lax.rem(self.shard, 2)
        self.far_seq = lax.rem(self.seq + 2, 4)
        self.mate_seq = self.chip * 2 + 1 - self.core
        self.far = {"seq": self.far_seq}
        self.mate = {"seq": self.mate_seq}
        self.twin_shard = self.place * 2 + 1 - self.half
        self.twin = {"shard": self.twin_shard}

    def outer_peer(self, place):
        return {"shard": place * 2 + self.half}

    def greet(self, wide=False):
        barrier = pltpu.get_barrier_semaphore()
        last = self.outer - 1

        def signal(peer):
            pl.semaphore_signal(barrier, inc=1, device_id=peer, device_id_type=MESH)

        signal(self.far)
        signal(self.mate)
        if wide:
            signal({"seq": 3 - self.seq})
            for amount in range(1, self.size):
                signal({"shard": lax.rem(self.shard + amount, self.size)})
            pl.semaphore_wait(barrier, 2 + self.size)
            return
        signal(self.twin)

        @pl.when(self.place < last)
        def _():
            signal(self.outer_peer(self.place + 1))

        @pl.when(self.place > 0)
        def _():
            signal(self.outer_peer(self.place - 1))

        inner = ((self.place > 0) & (self.place < last)).astype(jnp.int32)
        pl.semaphore_wait(barrier, 4 + inner)


def remote(source, target, send, receive, peer):
    return pltpu.make_async_remote_copy(
        src_ref=source,
        dst_ref=target,
        send_sem=send,
        recv_sem=receive,
        device_id=peer,
        device_id_type=MESH,
    )


class LineGather:
    def __init__(self, here, own, slot, sems):
        self.here, self.own, self.slot = here, own, slot
        self.us, self.ur, self.ds, self.dr = sems
        self.last = here.outer - 1

    def up(self, distance):
        here = self.here
        slot = self.slot(here.place - distance)
        source = slot if distance else self.own
        peer = here.outer_peer(here.place + 1)
        return remote(source, slot, self.us.at[distance], self.ur.at[distance], peer)

    def down(self, distance):
        here = self.here
        slot = self.slot(here.place + distance)
        source = slot if distance else self.own
        peer = here.outer_peer(here.place - 1)
        return remote(source, slot, self.ds.at[distance], self.dr.at[distance], peer)

    def send(self):
        here = self.here

        @pl.when(here.place < self.last)
        def _():
            self.up(0).start()

        @pl.when(here.place > 0)
        def _():
            self.down(0).start()

    def step(self, distance, arrived=lambda place: None):
        here = self.here
        below = here.place - 1 - distance
        above = here.place + 1 + distance

        @pl.when(below >= 0)
        def _():
            slot = self.slot(below)
            remote(slot, slot, self.us.at[0], self.ur.at[distance], here.twin).wait_recv()

            @pl.when(here.place < self.last)
            def _():
                self.up(distance + 1).start()

            arrived(below)

        @pl.when(above <= self.last)
        def _():
            slot = self.slot(above)
            remote(slot, slot, self.ds.at[0], self.dr.at[distance], here.twin).wait_recv()

            @pl.when(here.place > 0)
            def _():
                self.down(distance + 1).start()

            arrived(above)

    def finish(self):
        here = self.here
        for distance in range(self.last):

            @pl.when((here.place - distance >= 0) & (here.place < self.last))
            def _():
                self.up(distance).wait_send()

            @pl.when((here.place + distance <= self.last) & (here.place > 0))
            def _():
                self.down(distance).wait_send()


class RowGather:
    def __init__(self, here, own, whole, sems, spot=lambda shard: shard):
        self.here, self.own, self.whole, self.spot = here, own, whole, spot
        self.ys, self.yr, self.local = sems[4:]
        self.line = LineGather(here, own, self.mine, sems[:4])

    def mine(self, place):
        return self.whole.at[self.spot(place * 2 + self.here.half)]

    def theirs(self, place):
        return self.whole.at[self.spot(place * 2 + 1 - self.here.half)]

    def keep(self):
        return pltpu.make_async_copy(self.own, self.mine(self.here.place), self.local)

    def across(self, place, own=False):
        slot = self.mine(place)
        source = self.own if own else slot
        return remote(source, slot, self.ys.at[place], self.yr.at[place], self.here.twin)

    def arrived(self, place):
        slot = self.theirs(place)
        remote(slot, slot, self.ys.at[place], self.yr.at[place], self.here.twin).wait_recv()

    def send(self):
        self.line.send()
        self.across(self.here.place, own=True).start()
        self.keep().start()

    def step(self, distance):
        self.line.step(distance, lambda place: self.across(place).start())

    def arrive(self):
        self.keep().wait()
        for place in range(self.here.outer):
            self.arrived(place)

    def finish(self):
        self.line.finish()
        for place in range(self.here.outer):
            self.across(place).wait_send()


class TwinFirstGather(RowGather):
    def __init__(self, here, own, whole, sems, twin_sems):
        super().__init__(here, own, whole, sems)
        self.lines = [
            self.line,
            LineGather(here, self.theirs(here.place), self.theirs, twin_sems[:4]),
        ]

    def twin(self):
        self.arrived(self.here.place)
        self.lines[1].send()

    def step(self, distance):
        for line in self.lines:
            line.step(distance)

    def arrive(self):
        self.keep().wait()

    def finish(self):
        for line in self.lines:
            line.finish()
        self.across(self.here.place, own=True).wait_send()


class HeadGather:
    def __init__(self, here, own, whole, sems):
        self.here, self.own, self.whole = here, own, whole
        self.us, self.zr, self.ds, _, self.ys, self.yr, self.local = sems
        self.last = here.outer - 1
        self.count = here.quarter // 2
        self.first = here.seq * self.count
        self.mine = here.place - self.first
        self.inside = (self.mine >= 0) & (self.mine < self.count)

    def slot(self, index):
        return self.whole.at[index * 2 + self.here.half]

    def keep(self):
        return pltpu.make_async_copy(self.own, self.slot(self.mine), self.local)

    def up(self, index, own=False):
        slot = self.slot(index)
        peer = self.here.outer_peer(self.here.place + 1)
        return remote(self.own if own else slot, slot, self.us.at[index], self.zr.at[index], peer)

    def down(self, index, own=False):
        slot = self.slot(index)
        peer = self.here.outer_peer(self.here.place - 1)
        return remote(self.own if own else slot, slot, self.ds.at[index], self.zr.at[index], peer)

    def across(self, index):
        slot = self.slot(index)
        return remote(slot, slot, self.ys.at[index], self.yr.at[index], self.here.twin)

    def send(self):
        @pl.when(self.inside)
        def _():
            self.keep().start()

            @pl.when(self.here.place < self.last)
            def _():
                self.up(self.mine, own=True).start()

            @pl.when(self.here.place > 0)
            def _():
                self.down(self.mine, own=True).start()

    def step(self):
        here = self.here

        @pl.when(self.inside)
        def _():
            self.keep().wait()

        for index in range(self.count):
            slot = self.slot(index)
            arrival = remote(slot, slot, self.us.at[0], self.zr.at[index], here.twin)

            @pl.when(self.mine > index)
            def _():
                arrival.wait_recv()

                @pl.when(here.place < self.last)
                def _():
                    self.up(index).start()

            @pl.when(self.mine < index)
            def _():
                arrival.wait_recv()

                @pl.when(here.place > 0)
                def _():
                    self.down(index).start()

            self.across(index).start()

    def arrive(self):
        for index in range(self.count):
            slot = self.whole.at[index * 2 + 1 - self.here.half]
            remote(
                slot, slot, self.ys.at[index], self.yr.at[index], self.here.twin
            ).wait_recv()

    def finish(self):
        here = self.here
        for index in range(self.count):

            @pl.when((self.mine >= index) & (here.place < self.last))
            def _():
                self.up(index).wait_send()

            @pl.when((self.mine <= index) & (here.place > 0))
            def _():
                self.down(index).wait_send()

            self.across(index).wait_send()


class TokenGather:
    def __init__(self, here, own, whole, sems):
        self.here, self.own, self.whole = here, own, whole
        self.send_sems, self.recv_sems, self.local = sems
        self.rows = whole.shape[0] // 4

    def slot(self, seq):
        return self.whole.at[pl.ds(pl.multiple_of(seq * self.rows, self.rows), self.rows), :]

    def keep(self):
        return pltpu.make_async_copy(self.own, self.slot(self.here.seq), self.local)

    def copy(self, index):
        here = self.here
        slot = self.slot(here.far_seq if index == 2 else here.seq)
        return remote(
            slot if index == 2 else self.own,
            slot,
            self.send_sems.at[index],
            self.recv_sems.at[index],
            here.far if index == 0 else here.mate,
        )

    def send(self):
        self.copy(0).start()
        self.copy(1).start()
        self.keep().start()

    def forward(self):
        self.copy(0).wait_recv()
        self.copy(2).start()

    def mate_arrived(self):
        self.copy(1).wait_recv()

    def rest_arrived(self):
        self.copy(2).wait_recv()
        self.keep().wait()

    def arrive(self):
        self.mate_arrived()
        self.rest_arrived()

    def finish(self):
        for index in range(3):
            self.copy(index).wait_send()


class PieceSum:
    def __init__(self, here, piece, base, give, got, pair, far_got, sems, step):
        self.here, self.piece, self.base, self.step = here, piece, base, step
        self.give, self.got, self.pair, self.far_got = give, got, pair, far_got
        self.send_sems, self.recv_sems = sems

    def to_mate(self, index):
        return remote(
            self.give.at[index],
            self.got.at[index],
            self.send_sems.at[index],
            self.recv_sems.at[index],
            self.here.mate,
        )

    def to_far(self):
        return remote(
            self.pair, self.far_got, self.send_sems.at[2], self.recv_sems.at[2], self.here.far
        )

    def columns(self, body):
        step = self.step

        @pl.loop(0, self.pair.shape[1] // step)
        def _(index):
            body(pl.ds(pl.multiple_of(index * step, step), step))

    def send(self):
        here = self.here
        for index, chip in enumerate((1 - here.chip, here.chip)):
            seq = chip * 2 + 1 - here.core

            def fill(column, index=index, seq=seq):
                self.give[index, :, column] = self.piece(seq, column).astype(BF)

            self.columns(fill)
            self.to_mate(index).start()

    def pass_on(self):
        self.to_mate(0).wait_recv()

        def fill(column):
            term = self.piece(self.here.far_seq, column) + self.got[0, :, column].astype(F32)
            self.pair[:, column] = term.astype(BF)

        self.columns(fill)
        self.to_far().start()

    def add_near(self):
        self.to_mate(1).wait_recv()

        def fill(column):
            term = self.piece(self.here.seq, column) + self.got[1, :, column].astype(F32)
            self.base[:, column] += term

        self.columns(fill)

    def add_far(self):
        self.to_far().wait_recv()

        def fill(column):
            self.base[:, column] += self.far_got[:, column].astype(F32)

        self.columns(fill)
        for copy in (self.to_mate(0), self.to_mate(1), self.to_far()):
            copy.wait_send()


FORWARD_PLAN = (
    (("down", "send"),),
    (),
    (),
    (("down", 0), ("out", "send"),),
    (("second", "send"),),
    (),
    (("down", 1),),
    (("down", 2),),
    (),
    (("out", 0),),
    (("first", "send"),),
    (),
    (),
    (("third", "send"), ("first", 0),),
    (("second", "twin"),),
    (("first", 1), ("second", 0),),
    (("first", 2),),
    (("third", 0),),
    (("second", 1),),
    (("third", 1),),
    (("second", 2), ("third", 2),),
    (),
    (),
)


def forward_kernel(
    size,
    hidden_ref,
    dy_hbm,
    w_query,
    w_key,
    w_value,
    w_out,
    w_gate,
    w_up,
    w_down,
    attn_gain_ref,
    mlp_gain_ref,
    query_gain_ref,
    key_gain_ref,
    inverse_ref,
    segment_ref,
    qkv_full,
    out_full,
    first_full,
    second_full,
    down_full,
    n1_full,
    dy_full,
    n2_full,
    n1_turned,
    dy_turned,
    n2_turned,
    act_out,
    first_pair,
    second_pair,
    proj_ref,
    heads_ref,
    mixed_ref,
    lse_ref,
    middle_ref,
    cos_ref,
    sin_ref,
    start_row,
    lhs,
    dy_all,
    turned,
    qkv_w,
    out_w,
    qkv_own,
    out_own,
    down_own,
    dy_own,
    wide_own,
    first_own,
    second_own,
    own_rows,
    give,
    got,
    pair,
    far_got,
    us,
    ur,
    ds,
    dr,
    ys,
    yr,
    row_local,
    ts,
    tr,
    token_local,
    load_sem,
    ss,
    sr,
    start_ref,
    turned_ids,
):
    here = Place(size)
    last = here.outer - 1
    length, width = lhs.shape
    lse_ref[...] = jnp.zeros_like(lse_ref)
    rows = length // 4
    units = act_out.shape[1]
    chunk = units // 2
    tail = 256
    heads = mixed_ref.shape[1] // HEAD_DIM
    kv_heads = heads // 2
    ff_part = units // size

    def sems(index):
        return tuple(kind.at[index] for kind in (us, ur, ds, dr, ys, yr, row_local))

    down_rows = pl.ds(pl.multiple_of(here.seq * ff_part, ff_part), ff_part)
    qkv = RowGather(here, qkv_own, qkv_full, sems(0))
    out = HeadGather(here, out_own, out_full, sems(1))
    down = RowGather(
        here,
        down_own,
        down_full,
        sems(2),
        lambda shard: pl.ds(pl.multiple_of(shard * ff_part, ff_part), ff_part),
    )
    first = RowGather(here, first_own, first_full, sems(3))
    cut = 2 * (chunk - tail)
    second = TwinFirstGather(
        here, second_own.at[:, 0:cut], second_full.at[:, :, 0:cut], sems(4), sems(6)
    )
    third = RowGather(
        here, second_own.at[:, cut : 2 * chunk], second_full.at[:, :, cut : 2 * chunk], sems(5)
    )
    n1 = TokenGather(here, own_rows.at[0], n1_full, (ts.at[0], tr.at[0], token_local.at[0]))
    n2 = TokenGather(here, own_rows.at[1], n2_full, (ts.at[1], tr.at[1], token_local.at[1]))
    dy = TokenGather(here, dy_own, dy_full, (ts.at[2], tr.at[2], token_local.at[2]))

    loads = []
    at = 0
    for index, (weight, count) in enumerate(((w_query, heads), (w_key, kv_heads), (w_value, kv_heads))):
        count = count * HEAD_DIM
        source = weight.at[:, pl.ds(pl.multiple_of(here.seq * count, count), count)]
        loads.append(
            pltpu.make_async_copy(source, qkv_own.at[:, at : at + count], load_sem.at[index])
        )
        at += count
    loads.append(pltpu.make_async_copy(w_down.at[down_rows, :], down_own, load_sem.at[3]))
    loads.append(pltpu.make_async_copy(w_out, out_own, load_sem.at[4]))
    loads.append(pltpu.make_async_copy(dy_hbm, dy_own, load_sem.at[5]))
    loads.append(pltpu.make_async_copy(w_gate, wide_own, load_sem.at[6]))
    for load in loads:
        load.start()
    here.greet()
    for load in loads[:3]:
        load.wait()
    qkv.send()
    loads[5].wait()
    dy.send()

    def norm_rows(source, gain_ref, target):
        @pl.loop(0, rows // 32)
        def _(index):
            part = pl.ds(pl.multiple_of(index * 32, 32), 32)
            values = source[part, :].astype(F32)
            scales = lax.rsqrt(jnp.mean(values * values, axis=-1, keepdims=True) + EPSILON)
            target[part, :] = (values * scales * gain_ref[...]).astype(BF)

    gathers = {"out": out, "down": down, "first": first, "second": second, "third": third}

    def advance(steps):
        for name, step in steps:
            gather = gathers[name]
            if step == "send":
                gather.send()
            elif step == "twin":
                gather.twin()
            elif name == "out":
                gather.step()
            else:
                for distance in range(last * step // 3, last * (step + 1) // 3):
                    gather.step(distance)

    norm_rows(hidden_ref, attn_gain_ref, own_rows.at[0])
    n1.send()
    for load in loads[3:5]:
        load.wait()
    advance(FORWARD_PLAN[0])
    for load in loads[6:]:
        load.wait()

    most = chunk - tail

    def cut_units(side):
        for seq in range(4):

            @pl.when(here.seq == seq)
            def _():
                @pl.loop(0, wide_own.shape[0] // 16)
                def _(index):
                    part = pl.ds(pl.multiple_of(index * 16, 16), 16)

                    def gathered(begin):
                        pieces = [
                            wide_own[part, (block * 4 + seq) * ff_part : (block * 4 + seq + 1) * ff_part]
                            for block in range(begin, begin + size // 2)
                        ]
                        return jnp.concatenate(pieces, axis=1)

                    first_own[part, side * chunk : (side + 1) * chunk] = gathered(0)
                    rest = gathered(size // 2)
                    second_own[part, side * most : (side + 1) * most] = rest[:, 0:most]
                    at = 2 * most + side * tail
                    second_own[part, at : at + tail] = rest[:, most:]

    def rotation():
        ids = segment_ref[...].astype(F32)
        turned_ids[...] = jnp.broadcast_to(ids, (128, length)).T
        lane = lax.broadcasted_iota(jnp.int32, (128, 128), 1)

        @pl.loop(0, length // 128)
        def _(index):
            part = pl.ds(pl.multiple_of(index * 128, 128), 128)
            own_ids = turned_ids[part, :]
            count = jnp.zeros((128, 128), F32)
            for at in range(0, length, 128):
                count = count + jnp.where(
                    segment_ref[:, at : at + 128].astype(F32) < own_ids, 1.0, 0.0
                )
            starts = jnp.sum(count, axis=-1, keepdims=True)
            start_ref[part, :] = starts.astype(jnp.int32)
            starts = jnp.broadcast_to(starts, (128, 128))
            turned_ids[part, :] = starts
            places = lax.broadcasted_iota(jnp.int32, (128, 128), 0) + index * 128
            angles = (places.astype(F32) - starts) * inverse_ref[...]
            cos_ref[part, :] = jnp.cos(angles)
            sine = jnp.sin(angles)
            sin_ref[part, :] = jnp.where(lane < HEAD_DIM // 2, -sine, sine)

        start_row[...] = turned_ids[...].T[0:1].astype(jnp.int32)

    zones = width // 512

    def turn(source, target):
        for seq_group in range(4):
            for zone in range(zones):
                at = (seq_group * zones + zone) * 128
                turned[zone * 4 + seq_group] = source[:, at : at + 128].T
        copy = pltpu.make_async_copy(turned, target, load_sem.at[4])
        copy.start()
        return copy

    cut_units(0)
    load_up = pltpu.make_async_copy(w_up, wide_own, load_sem.at[7])
    load_up.start()
    load_up.wait()
    cut_units(1)
    advance(FORWARD_PLAN[1])
    for third_part in range(3):
        for distance in range(last * third_part // 3, last * (third_part + 1) // 3):
            qkv.step(distance)
        advance(FORWARD_PLAN[2 + third_part])
        if third_part == 0:
            rotation()
            dy.forward()
    dy.arrive()
    load_dy = pltpu.make_async_copy(dy_full, dy_all, load_sem.at[0])
    load_dy.start()
    load_dy.wait()
    store = turn(dy_all, dy_turned)
    n1.forward()
    advance(FORWARD_PLAN[5])
    n1.arrive()
    load_lhs = pltpu.make_async_copy(n1_full, lhs, load_sem.at[0])
    load_lhs.start()
    advance(FORWARD_PLAN[6])
    qkv.arrive()
    load_qkv = pltpu.make_async_copy(qkv_full, qkv_w, load_sem.at[1])
    load_qkv.start()
    advance(FORWARD_PLAN[7])
    load_lhs.wait()
    load_qkv.wait()

    def project(tile):
        weight = qkv_w[:, :, tile * 256 : tile * 256 + 256].reshape(width, 256)
        gain_ref = query_gain_ref if tile < heads // 2 else key_gain_ref

        @pl.loop(0, 4)
        def _(index):
            part = pl.ds(pl.multiple_of(index * rows, rows), rows)
            both = dot(lhs[part, :], weight)
            for side in range(2):
                head = tile * 2 + side
                proj = both[:, side * HEAD_DIM : (side + 1) * HEAD_DIM]
                if head >= heads + kv_heads:
                    heads_ref[head, part, :] = proj.astype(BF)
                    continue
                proj_ref[head, part, :] = proj
                scales = lax.rsqrt(jnp.mean(proj * proj, axis=-1, keepdims=True) + EPSILON)
                gained = proj * scales * gain_ref[...]
                turned = pltpu.roll(gained, HEAD_DIM // 2, 1)
                heads_ref[head, part, :] = (
                    gained * cos_ref[part, :] + turned * sin_ref[part, :]
                ).astype(BF)

    def attend(head):
        pair_head = head // 2
        for block in range(4):
            end = (block + 1) * rows
            part = pl.ds(block * rows, rows)
            scores = contract_cols(
                heads_ref[head, part, :], heads_ref[heads + pair_head, 0:end, :]
            )
            row_place = lax.broadcasted_iota(jnp.int32, (rows, end), 0) + block * rows
            col_place = lax.broadcasted_iota(jnp.int32, (rows, end), 1)
            allowed = (col_place >= start_ref[part, :]) & (col_place <= row_place)
            raised = jnp.where(allowed, jnp.exp(scores * (HEAD_DIM ** (-0.5))), 0.0)
            sums = jnp.sum(raised, axis=-1, keepdims=True)
            mixed = dot(raised.astype(BF), heads_ref[heads + kv_heads + pair_head, 0:end, :])
            mixed = mixed * (1.0 / sums)
            mixed_ref[part, head * HEAD_DIM : (head + 1) * HEAD_DIM] = mixed.astype(BF)
            lse_ref[part, head : head + 1] = jnp.log(sums)

    tiles = (heads + 2 * kv_heads) // 2
    for tile in range(tiles):
        if tile == tiles // 2:
            advance(FORWARD_PLAN[8])
        project(tile)
    advance(FORWARD_PLAN[9])

    for head in range(heads):
        attend(head)
        advance(FORWARD_PLAN[10 + head])
    out.arrive()
    load_out = pltpu.make_async_copy(out_full, out_w, load_sem.at[2])
    load_out.start()
    load_out.wait()

    def out_piece(seq, column):
        part = pl.ds(pl.multiple_of(seq * rows, rows), rows)
        weight = out_w[:, :, column]
        return dot(mixed_ref[part, :], weight.reshape(-1, weight.shape[-1]))

    middle_ref[...] = hidden_ref[...].astype(F32)
    token_sum = PieceSum(
        here, out_piece, middle_ref, give, got, pair, far_got, (ss, sr), 512
    )
    token_sum.send()
    advance(FORWARD_PLAN[14])
    token_sum.pass_on()
    token_sum.add_near()
    advance(FORWARD_PLAN[15])
    token_sum.add_far()
    norm_rows(middle_ref, mlp_gain_ref, own_rows.at[1])
    n2.send()
    advance(FORWARD_PLAN[16])
    store.wait()
    store = turn(lhs, n1_turned)
    advance(FORWARD_PLAN[17])
    n2.forward()
    advance(FORWARD_PLAN[18])
    n2.arrive()
    load_lhs = pltpu.make_async_copy(n2_full, lhs, load_sem.at[3])
    load_lhs.start()
    down.arrive()
    first.arrive()
    load_lhs.wait()

    def feed(gather, begin, count):
        tiles = count // 256
        spot = begin // 256

        def body(gate_w, up_w, down_w, act_ref, gate_grad, up_grad):
            gate_tile = gate_w[...].reshape(width, 256)
            up_tile = up_w[...].reshape(width, 256)
            down_tile = down_w[...]

            @pl.loop(0, 4)
            def _(index):
                part = pl.ds(pl.multiple_of(index * rows, rows), rows)
                gate = dot(lhs[part, :], gate_tile)
                up = dot(lhs[part, :], up_tile)
                act_grad = contract_cols(dy_all[part, :], down_tile)
                sigmoid = jax.nn.sigmoid(gate)
                silu = gate * sigmoid
                act_ref[part, :] = (silu * up).astype(BF)
                gate_grad[part, :] = (
                    act_grad * up * sigmoid * (1.0 + gate * (1.0 - sigmoid))
                ).astype(BF)
                up_grad[part, :] = (act_grad * silu).astype(BF)

        block = gather.whole.shape[:-1] + (256,)
        grads = first_pair if begin < chunk else second_pair
        first_spot = 0 if begin < chunk + 1 else 2 * (begin - chunk) // 256
        pltpu.emit_pipeline(
            body,
            grid=(tiles,),
            in_specs=[
                pl.BlockSpec(block, lambda t: (0, 0, t)),
                pl.BlockSpec(block, lambda t: (0, 0, t + tiles)),
                pl.BlockSpec((256, width), lambda t: (t + spot, 0)),
            ],
            out_specs=[
                pl.BlockSpec((length, 256), lambda t: (0, t + spot)),
                pl.BlockSpec((length, 256), lambda t: (0, t + first_spot)),
                pl.BlockSpec((length, 256), lambda t: (0, t + first_spot + tiles)),
            ],
        )(gather.whole, gather.whole, down_full, act_out, grads, grads)

    feed(first, 0, chunk)
    advance(FORWARD_PLAN[19])
    store.wait()
    store = turn(lhs, n2_turned)
    advance(FORWARD_PLAN[20])
    second.arrive()
    feed(second, chunk, chunk - tail)
    advance(FORWARD_PLAN[21])
    third.arrive()
    feed(third, 2 * chunk - tail, tail)
    store.wait()
    for gather in (qkv, out, first, second, third, down, n1, n2, dy):
        gather.finish()


def forward(hidden, upstream, weights, gains, segment):
    size = lax.axis_size("shard")
    quarter, outer = size // 4, size // 2
    piece, width = hidden.shape
    length = piece * 4
    heads = Q_HEADS // 4
    kv_heads = KV_HEADS // 4
    w_query, _, _, w_out, w_gate, _, w_down = weights
    own = w_query.shape[0]
    qkv_width = (heads + 2 * kv_heads) * HEAD_DIM
    units = w_down.shape[0] // 4 * size

    def shape(*dims, kind=BF):
        return jax.ShapeDtypeStruct(dims, kind)

    results = [
        shape(size, own, qkv_width),
        shape(quarter, *w_out.shape),
        shape(size, own, units),
        shape(size, own, units),
        shape(units, width),
        shape(length, width),
        shape(length, width),
        shape(length, width),
        shape(width // 128, 128, length),
        shape(width // 128, 128, length),
        shape(width // 128, 128, length),
        shape(length, units),
        shape(length, units),
        shape(length, units),
        shape(heads + kv_heads, length, HEAD_DIM, kind=F32),
        shape(heads + 2 * kv_heads, length, HEAD_DIM),
        shape(length, heads * HEAD_DIM),
        shape(length, 128, kind=F32),
        shape(piece, width, kind=F32),
        shape(length, HEAD_DIM, kind=F32),
        shape(length, HEAD_DIM, kind=F32),
        shape(1, length, kind=jnp.int32),
    ]
    powers = np.arange(HEAD_DIM // 2, dtype=np.float32) * np.float32(2.0) / np.float32(HEAD_DIM)
    inverse = np.float32(ROPE_BASE) ** -powers
    dma = pltpu.SemaphoreType.DMA
    return pl.pallas_call(
        functools.partial(forward_kernel, size),
        out_shape=results,
        in_specs=[VMEM] + [ANY] * 8 + [VMEM] * 6,
        out_specs=[ANY] * 14 + [VMEM] * 8,
        scratch_shapes=[
            pltpu.VMEM((length, width), BF),
            pltpu.VMEM((length, width), BF),
            pltpu.VMEM((width // 128, 128, length), BF),
            pltpu.VMEM((size, own, qkv_width), BF),
            pltpu.VMEM((quarter,) + w_out.shape, BF),
            pltpu.VMEM((own, qkv_width), BF),
            pltpu.VMEM(w_out.shape, BF),
            pltpu.VMEM((w_down.shape[0] // 4, width), BF),
            pltpu.VMEM((piece, width), BF),
            pltpu.VMEM(w_gate.shape, BF),
            pltpu.VMEM((own, units), BF),
            pltpu.VMEM((own, units), BF),
            pltpu.VMEM((2, piece, width), BF),
            pltpu.VMEM((2, piece, width), BF),
            pltpu.VMEM((2, piece, width), BF),
            pltpu.VMEM((piece, width), BF),
            pltpu.VMEM((piece, width), BF),
            dma((7, outer)),
            dma((7, outer)),
            dma((7, outer)),
            dma((7, outer)),
            dma((7, outer)),
            dma((7, outer)),
            dma((7,)),
            dma((3, 3)),
            dma((3, 3)),
            dma((3,)),
            dma((8,)),
            dma((3,)),
            dma((3,)),
            pltpu.VMEM((length, 1), jnp.int32),
            pltpu.VMEM((length, 128), F32),
        ],
        compiler_params=pltpu.CompilerParams(
            collective_id=0, has_side_effects=True, vmem_limit_bytes=VMEM_BYTES
        ),
        name="forward_gather",
    )(
        hidden,
        upstream,
        *weights,
        *gains,
        jnp.asarray(np.concatenate([inverse, inverse])[None], F32),
        segment[None],
    )


def add_rows(target, sources, step=16):
    groups, rows, _ = target.shape

    @pl.loop(0, rows // step)
    def _(index):
        part = pl.ds(pl.multiple_of(index * step, step), step)
        for group in range(groups):
            total = sources[0][group, part, :].astype(target.dtype)
            for source in sources[1:]:
                total = total + source[group, part, :].astype(target.dtype)
            target[group, part, :] = total


class RowSum:
    def __init__(self, here, give, keep, near, rising, falling, stage, total, sems):
        self.here, self.give, self.keep = here, give, keep
        self.near, self.rising, self.falling = near, rising, falling
        self.stage, self.total = stage, total
        self.ys, self.yr, self.us, self.ur, self.ds, self.dr, self.load = sems
        self.last = here.outer - 1

    def across(self, place):
        return remote(
            self.give.at[place],
            self.near.at[place],
            self.ys.at[place],
            self.yr.at[place],
            self.here.twin,
        )

    def up(self, place):
        peer = self.here.outer_peer(self.here.place + 1)
        return remote(
            self.keep.at[place], self.rising.at[place], self.us.at[place], self.ur.at[place], peer
        )

    def down(self, place):
        peer = self.here.outer_peer(self.here.place - 1)
        return remote(
            self.keep.at[place], self.falling.at[place], self.ds.at[place], self.dr.at[place], peer
        )

    def arrived(self, slot, send, receive):
        remote(slot, slot, send, receive, self.here.twin).wait_recv()

    def fold(self, distance):
        here = self.here
        above = here.place + distance
        below = here.place - distance

        def merge(place, line, receive, first):
            near = pltpu.make_async_copy(self.near.at[place], self.stage.at[0], self.load.at[0])
            self.arrived(self.near.at[place], self.ys.at[place], self.yr.at[place])
            near.start()

            @pl.when(first)
            def _():
                near.wait()
                add_rows(self.keep.at[place], [self.keep.at[place], self.stage.at[0]])

            @pl.when(jnp.logical_not(first))
            def _():
                self.arrived(line.at[place], self.us.at[0], receive.at[place])
                far = pltpu.make_async_copy(line.at[place], self.stage.at[1], self.load.at[1])
                far.start()
                near.wait()
                far.wait()
                add_rows(
                    self.keep.at[place], [self.keep.at[place], self.stage.at[0], self.stage.at[1]]
                )

        @pl.when(above <= self.last)
        def _():
            merge(above, self.rising, self.ur, here.place == 0)
            self.up(above).start()

        @pl.when(below >= 0)
        def _():
            merge(below, self.falling, self.dr, here.place == self.last)
            self.down(below).start()

    def finish(self):
        here = self.here
        place = here.place
        self.arrived(self.near.at[place], self.ys.at[place], self.yr.at[place])
        keep = self.keep.at[place]
        near = pltpu.make_async_copy(self.near.at[place], self.stage.at[0], self.load.at[0])
        low = pltpu.make_async_copy(self.rising.at[place], self.stage.at[1], self.load.at[1])
        high = pltpu.make_async_copy(self.falling.at[place], self.stage.at[1], self.load.at[1])
        near.start()

        @pl.when(place > 0)
        def _():
            self.arrived(self.rising.at[place], self.us.at[0], self.ur.at[place])
            low.start()
            low.wait()

        @pl.when(place == 0)
        def _():
            self.arrived(self.falling.at[place], self.ds.at[0], self.dr.at[place])
            high.start()
            high.wait()

        near.wait()

        @pl.when((place > 0) & (place < self.last))
        def _():
            add_rows(keep, [keep, self.stage.at[0], self.stage.at[1]])
            self.arrived(self.falling.at[place], self.ds.at[0], self.dr.at[place])
            high.start()
            high.wait()
            add_rows(self.total, [keep, self.stage.at[1]])

        @pl.when((place == 0) | (place == self.last))
        def _():
            add_rows(self.total, [keep, self.stage.at[0], self.stage.at[1]])

    def sent(self):
        for place in range(self.here.outer):
            self.across(place).wait_send()

    def settle(self):
        here = self.here
        for place in range(here.outer):

            @pl.when(place > here.place)
            def _():
                self.up(place).wait_send()

            @pl.when(place < here.place)
            def _():
                self.down(place).wait_send()


def compute_terms(here, give, keep, left, right, tiles, orders, senders):
    own = give.shape[2]
    per = 128 // (2 * own)
    step = 256
    for group, done in orders:
        spots = tiles(group)

        @pl.loop(0, give.shape[3] // step)
        def _(index):
            lane = pl.ds(pl.multiple_of(index * step, step), step)
            terms = dot(left(group), right(lane)).astype(BF)
            for spot, (zone, seq_group) in enumerate(spots):
                for sub in range(per):
                    at = spot * 128 + sub * 2 * own
                    even, odd = terms[at : at + own], terms[at + own : at + 2 * own]
                    place = zone * per + sub
                    keep[place, seq_group, :, lane] = jnp.where(here.half == 0, even, odd)
                    give[place, seq_group, :, lane] = jnp.where(here.half == 0, odd, even)

        for zone in done:
            for sub in range(per):
                for sender in senders:
                    sender.across(zone * per + sub).start()


class LineSum:
    def __init__(self, here, terms, rising, falling, stage, sems):
        self.here, self.terms, self.stage = here, terms, stage
        self.rising, self.falling = rising, falling
        self.us, self.ur, self.ds, self.dr, self.load = sems
        self.last = here.outer - 1

    def up(self, place):
        peer = self.here.outer_peer(self.here.place + 1)
        return remote(
            self.terms.at[place], self.rising.at[place], self.us.at[place], self.ur.at[place], peer
        )

    def down(self, place):
        peer = self.here.outer_peer(self.here.place - 1)
        return remote(
            self.terms.at[place], self.falling.at[place], self.ds.at[place], self.dr.at[place], peer
        )

    def merge(self, place, line, receive):
        slot = line.at[place]
        remote(slot, slot, self.us.at[0], receive.at[place], self.here.twin).wait_recv()
        copy = pltpu.make_async_copy(slot, self.stage.at[0], self.load.at[0])
        copy.start()
        copy.wait()
        add_rows(self.terms.at[place], [self.terms.at[place], self.stage.at[0]])

    def fold(self, distance):
        here = self.here
        above = here.place + distance
        below = here.place - distance

        @pl.when(above <= self.last)
        def _():
            @pl.when(here.place > 0)
            def _():
                self.merge(above, self.rising, self.ur)

            self.up(above).start()

        @pl.when(below >= 0)
        def _():
            @pl.when(here.place < self.last)
            def _():
                self.merge(below, self.falling, self.dr)

            self.down(below).start()

    def gather(self):
        place = self.here.place

        @pl.when(place > 0)
        def _():
            self.merge(place, self.rising, self.ur)

        @pl.when(place < self.last)
        def _():
            self.merge(place, self.falling, self.dr)

    def settle(self):
        here = self.here
        for place in range(here.outer):

            @pl.when(place > here.place)
            def _():
                self.up(place).wait_send()

            @pl.when(place < here.place)
            def _():
                self.down(place).wait_send()


class LineFirstSum(RowSum):
    def __init__(self, here, give, keep, near, lines, stage, total, sems, twin_sems):
        self.here, self.give, self.keep = here, give, keep
        self.near, self.stage, self.total = near, stage, total
        self.ys, self.yr, self.load = sems[0], sems[1], sems[6]
        self.lines = [
            LineSum(here, terms, rising, falling, stage, kinds[2:])
            for terms, (rising, falling), kinds in (
                (give, lines[0], twin_sems),
                (keep, lines[1], sems),
            )
        ]

    def fold(self, distance):
        for line in self.lines:
            line.fold(distance)

    def pass_on(self):
        self.lines[0].gather()
        self.across(self.here.place).start()
        self.lines[1].gather()

    def finish(self):
        place = self.here.place
        self.arrived(self.near.at[place], self.ys.at[place], self.yr.at[place])
        near = pltpu.make_async_copy(self.near.at[place], self.stage.at[0], self.load.at[0])
        near.start()
        near.wait()
        add_rows(self.total, [self.keep.at[place], self.stage.at[0]])

    def sent(self):
        self.across(self.here.place).wait_send()

    def settle(self):
        for line in self.lines:
            line.settle()


class RowSpread:
    def __init__(self, here, rows, whole, sems):
        self.here, self.rows, self.whole = here, rows, whole
        self.send_sems, self.recv_sems, self.local = sems

    def copy(self, amount):
        seq = lax.rem(self.here.seq + amount, 4)
        return remote(
            self.rows.at[seq],
            self.whole.at[self.here.seq],
            self.send_sems.at[amount - 1],
            self.recv_sems.at[amount - 1],
            {"seq": seq},
        )

    def keep(self):
        seq = self.here.seq
        return pltpu.make_async_copy(self.rows.at[seq], self.whole.at[seq], self.local)

    def send(self):
        for amount in (2, 3, 1):
            self.copy(amount).start()
        self.keep().start()

    def arrive(self):
        for amount in (1, 2, 3):
            self.copy(amount).wait_recv()
        self.keep().wait()

    def finish(self):
        for amount in (1, 2, 3):
            self.copy(amount).wait_send()


class TokenSum:
    def __init__(self, here, part, got, pair, far_got, base, sems):
        self.here, self.part, self.got, self.pair = here, part, got, pair
        self.far_got, self.base = far_got, base
        self.send_sems, self.recv_sems = sems
        self.rows = part.shape[0] // 4

    def piece(self, seq):
        return pl.ds(pl.multiple_of(seq * self.rows, self.rows), self.rows)

    def to_mate(self, index):
        here = self.here
        chip = here.chip if index else 1 - here.chip
        seq = chip * 2 + 1 - here.core
        return remote(
            self.part.at[self.piece(seq), :],
            self.got.at[index],
            self.send_sems.at[index],
            self.recv_sems.at[index],
            here.mate,
        )

    def to_far(self):
        return remote(
            self.pair, self.far_got, self.send_sems.at[2], self.recv_sems.at[2], self.here.far
        )

    def send(self):
        self.to_mate(0).start()
        self.to_mate(1).start()

    def loop(self, body):
        @pl.loop(0, self.rows // 32)
        def _(index):
            body(index * 32)

    def pass_on(self):
        self.to_mate(0).wait_recv()
        begin = self.here.far_seq * self.rows

        def body(at):
            part = pl.ds(pl.multiple_of(at, 32), 32)
            source = pl.ds(pl.multiple_of(begin + at, 32), 32)
            total = self.part[source, :].astype(F32) + self.got[0, part, :].astype(F32)
            self.pair[part, :] = total.astype(BF)

        self.loop(body)
        self.to_far().start()

    def add_near(self):
        self.to_mate(1).wait_recv()
        begin = self.here.seq * self.rows

        def body(at):
            part = pl.ds(pl.multiple_of(at, 32), 32)
            source = pl.ds(pl.multiple_of(begin + at, 32), 32)
            self.base[part, :] += self.part[source, :].astype(F32) + self.got[1, part, :].astype(F32)

        self.loop(body)
        self.to_mate(0).wait_send()
        self.to_mate(1).wait_send()

    def add_far(self):
        self.to_far().wait_recv()

        def body(at):
            part = pl.ds(pl.multiple_of(at, 32), 32)
            self.base[part, :] += self.far_got[part, :].astype(F32)

        self.loop(body)
        self.to_far().wait_send()


class GainSum:
    def __init__(self, here, own, seq_got, middle, shard_got, sems):
        self.here, self.own, self.middle = here, own, middle
        self.seq_got, self.shard_got = seq_got, shard_got
        self.seq_send, self.seq_recv, self.shard_send, self.shard_recv = sems

    def over_seq(self, amount):
        here = self.here
        return remote(
            self.own,
            self.seq_got.at[here.seq],
            self.seq_send.at[amount - 1],
            self.seq_recv.at[amount - 1],
            {"seq": lax.rem(here.seq + amount, 4)},
        )

    def over_shard(self, amount):
        here = self.here
        return remote(
            self.middle,
            self.shard_got.at[here.shard],
            self.shard_send.at[amount - 1],
            self.shard_recv.at[amount - 1],
            {"shard": lax.rem(here.shard + amount, here.size)},
        )

    def start(self):
        for amount in range(1, 4):
            self.over_seq(amount).start()
        self.seq_got[self.here.seq] = self.own[...]

    def turn(self):
        for amount in range(1, 4):
            self.over_seq(amount).wait()
        total = self.seq_got[0]
        for index in range(1, 4):
            total = total + self.seq_got[index]
        self.middle[...] = total
        for amount in range(1, self.here.size):
            self.over_shard(amount).start()
        self.shard_got[self.here.shard] = total

    def finish(self):
        for amount in range(1, self.here.size):
            self.over_shard(amount).wait()
        total = self.shard_got[0]
        for index in range(1, self.here.size):
            total = total + self.shard_got[index]
        return total


PLAN = (
    (("down_a", 3),),
    (("down_a", 2), ("down_b", 3),),
    (("down_a", 1), ("down_b", 2),),
    (),
    (),
    (("first", 3), ("down_b", 1),),
    (("first", 2), ("down_b", "finish"),),
    (("second", 3), ("first", 1),),
    (("second", 2),),
    (),
    (("first", "finish"),),
    (("out", 3), ("second", 1),),
    (),
    (("out", 2), ("query", 3), ("down_a", "pass"), ("key", 3), ("out", 1),),
    (("query", 2), ("key", 2), ("second", "finish"), ("out", "finish"), ("query", 1), ("key", 1),),
    (("query", "finish"), ("key", "finish"),),
    (("down_a", "finish"),),
)


def backward_kernel(
    size,
    n1_hbm,
    dy_hbm,
    n2_hbm,
    act_hbm,
    first_hbm,
    second_hbm,
    proj_hbm,
    heads_ref,
    mixed_ref,
    lse_ref,
    middle_hbm,
    hidden_hbm,
    dy_own,
    qkv_full,
    out_full,
    first_full,
    second_full,
    down_full,
    attn_gain_ref,
    mlp_gain_ref,
    query_gain_ref,
    key_gain_ref,
    cos_ref,
    sin_ref,
    start_ref,
    grad_in,
    gains_out,
    grad_out,
    hidden_out,
    down_rows,
    first_rows,
    second_rows,
    qkv_rows,
    da_hbm,
    near_mlp,
    rising_mlp,
    falling_mlp,
    rising_twin,
    falling_twin,
    near_qkv,
    rising_qkv,
    falling_qkv,
    near_out,
    rising_out,
    falling_out,
    lhs,
    turned,
    first_r,
    second_r,
    give,
    keep,
    give_out,
    keep_out,
    stage,
    stage_out,
    dout_ref,
    da_own,
    got,
    far_got,
    pair,
    middle_grad,
    proj_buf,
    lse_t,
    delta,
    delta_t,
    dk_sum,
    dv_sum,
    gain_row,
    gain_seq,
    gain_middle,
    gain_shard,
    ys,
    yr,
    us,
    ur,
    ds,
    dr,
    fold_load,
    spread_s,
    spread_r,
    spread_l,
    sum_s,
    sum_r,
    ts,
    tr,
    token_local,
    gss,
    gsr,
    gts,
    gtr,
    load_sem,
    credit,
):
    here = Place(size)
    length, width = lhs.shape
    rows = length // 4
    units = first_r.shape[1]
    chunk = units // 2
    ff_part = units // size
    heads = mixed_ref.shape[1] // HEAD_DIM
    kv_heads = heads // 2
    qkv_width = qkv_full.shape[2]
    last = here.outer - 1
    scale = HEAD_DIM ** (-0.5)

    def load(source, target, index):
        copy = pltpu.make_async_copy(source, target, load_sem.at[index])
        copy.start()
        return copy

    def sems(index):
        return tuple(kind.at[index] for kind in (ys, yr, us, ur, ds, dr, fold_load))

    thin = qkv_width // 2
    cut = units * 2 // 3
    lanes = {
        "down_a": slice(0, cut),
        "down_b": slice(cut, units),
        "query": slice(0, thin),
        "key": slice(thin, 2 * thin),
    }

    def part(ref, name):
        return ref.at[:, :, :, lanes[name]]

    def row_sum(index, give_ref, keep_ref, near, rising, falling, stage_ref, total):
        return RowSum(
            here, give_ref, keep_ref, near, rising, falling, stage_ref, total, sems(index)
        )

    jobs = {
        "down_a": LineFirstSum(
            here,
            part(give.at[2], "down_a"),
            part(keep.at[0], "down_a"),
            part(near_mlp.at[0], "down_a"),
            (
                (rising_twin, falling_twin),
                (part(rising_mlp.at[0], "down_a"), part(falling_mlp.at[0], "down_a")),
            ),
            part(stage, "down_a"),
            keep.at[0, here.place, :, :, lanes["down_a"]],
            sems(0),
            sems(5),
        ),
        "down_b": row_sum(
            6,
            part(give.at[2], "down_b"),
            part(keep.at[0], "down_b"),
            part(near_mlp.at[0], "down_b"),
            part(rising_mlp.at[0], "down_b"),
            part(falling_mlp.at[0], "down_b"),
            part(stage, "down_b"),
            keep.at[0, here.place, :, :, lanes["down_b"]],
        ),
        "out": row_sum(
            4, give_out, keep_out, near_out, rising_out, falling_out, stage_out, grad_out
        ),
    }
    for index, name in ((1, "first"), (2, "second")):
        jobs[name] = row_sum(
            index,
            give.at[2 - index],
            keep.at[index],
            near_mlp.at[index],
            rising_mlp.at[index],
            falling_mlp.at[index],
            stage,
            keep.at[index, here.place],
        )
    for index, name in ((3, "query"), (7, "key")):
        jobs[name] = row_sum(
            index,
            part(give.at[1], name),
            part(second_r, name),
            part(near_qkv, name),
            part(rising_qkv, name),
            part(falling_qkv, name),
            part(stage, name),
            second_r.at[here.place, :, :, lanes[name]],
        )
    zones = width // 512

    def zone_at(index):
        zone = here.place // (here.outer // zones)
        return (
            3 * (1 - zone // 2),
            lax.rem(2 + 3 * zone, 5),
            1 + lax.rem(zone, 2),
            zone,
        )[index]

    zone_order = [zone_at(index) for index in range(zones)]
    by_zone = [(zone, (zone,)) for zone in zone_order]

    spreads = {}
    for index, (name, whole) in enumerate(
        (
            ("down_a", down_rows.at[:, :, lanes["down_a"]]),
            ("down_b", down_rows.at[:, :, lanes["down_b"]]),
            ("first", first_rows),
            ("second", second_rows),
            ("query", qkv_rows.at[:, :, lanes["query"]]),
            ("key", qkv_rows.at[:, :, lanes["key"]]),
        )
    ):
        kinds = (spread_s.at[index], spread_r.at[index], spread_l.at[index])
        spreads[name] = RowSpread(here, jobs[name].total, whole, kinds)

    def token_sum(index, base):
        return TokenSum(
            here, lhs, got, pair, far_got, base, (sum_s.at[index], sum_r.at[index])
        )

    sum_mlp = token_sum(0, middle_grad)
    sum_hidden = token_sum(1, grad_in)
    sum_attn = token_sum(2, grad_in)
    da = TokenGather(here, da_own, da_hbm, (ts, tr, token_local.at[0]))

    def model_tiles(group):
        return [(group, seq_group) for seq_group in range(4)]

    def first_columns(lane):
        return first_r[:, lane]

    def model_left(group):
        return turned[pl.ds(group * 4, 4)].reshape(512, length)

    def advance(steps):
        for name, step in steps:
            job = jobs[name]
            if step == "pass":
                job.pass_on()
            elif step == "finish":
                job.finish()
                if name in spreads:
                    spreads[name].send()
            else:
                for distance in range(last * step // 3, last * (step - 1) // 3, -1):
                    job.fold(distance)

    load_turned = load(dy_hbm, turned, 0)
    load_act = load(act_hbm, first_r, 1)
    load_middle = load(middle_hbm, grad_in, 2)
    load_dy = load(dy_own, da_own, 4)
    load_second = load(second_hbm, second_r, 3)
    here.greet(wide=True)
    load_turned.wait()
    load_act.wait()
    def model_terms(give_ref, keep_ref, right, senders):
        compute_terms(
            here, give_ref, keep_ref, model_left, right, model_tiles, by_zone, senders
        )

    model_terms(give.at[2], keep.at[0], first_columns, [jobs["down_b"]])
    advance(PLAN[0])
    load_turned = load(n2_hbm, turned, 0)
    load_first = load(first_hbm, first_r, 1)
    load_first.wait()
    load_second.wait()

    own = width // size
    slabs = 256 // own

    def dn2_body(first_w, second_w):
        lane = pl.ds(pl.multiple_of(pl.program_id(0) * 256, 256), 256)
        first_tile = first_w[...].reshape(256, units)
        second_tile = second_w[...].reshape(256, units)

        @pl.loop(0, 4)
        def _(index):
            part = pl.ds(pl.multiple_of(index * rows, rows), rows)
            total = contract_cols(first_r[part, :], first_tile)
            blocks = pl.ds(index * (here.outer // 4), here.outer // 4)
            second_rows = second_r[blocks].reshape(rows, units)
            total = total + contract_cols(second_rows, second_tile)
            lhs[part, lane] = total.astype(BF)

    slab = pl.BlockSpec((slabs, own, units), lambda t: (t, 0, 0))
    pltpu.emit_pipeline(dn2_body, grid=(width // 256,), in_specs=[slab, slab])(
        first_full, second_full
    )
    sum_mlp.send()
    middle_grad[...] = jnp.zeros_like(middle_grad)
    load_turned.wait()
    advance(PLAN[1])
    sum_mlp.pass_on()
    sum_mlp.add_near()
    model_terms(give.at[1], keep.at[1], first_columns, [jobs["first"]])
    load_act = load(act_hbm, first_r, 1)
    advance(PLAN[2])
    sum_mlp.add_far()

    load_middle.wait()
    load_dy.wait()
    gain_row[...] = jnp.zeros_like(gain_row)
    mlp_lane = slice(2 * HEAD_DIM, 2 * HEAD_DIM + width)
    attn_lane = slice(2 * HEAD_DIM + width, 2 * HEAD_DIM + 2 * width)
    narrow = 16

    @pl.loop(0, rows // narrow)
    def _(index):
        part = pl.ds(pl.multiple_of(index * narrow, narrow), narrow)
        values = grad_in[part, :]
        scales = lax.rsqrt(jnp.mean(values * values, axis=-1, keepdims=True) + EPSILON)
        normed = values * scales
        update = middle_grad[part, :]
        gain_row[:, mlp_lane] += jnp.sum(update * normed, axis=0, keepdims=True)
        upper = update * mlp_gain_ref[...]
        inner = jnp.mean(upper * normed, axis=-1, keepdims=True)
        grad = da_own[part, :].astype(F32) + scales * (upper - normed * inner)
        middle_grad[part, :] = grad
        da_own[part, :] = grad.astype(BF)

    da.send()
    advance(PLAN[3])
    model_terms(
        give.at[0],
        keep.at[2],
        lambda lane: second_r[:, :, :, lane].reshape(length, -1),
        [jobs["second"]],
    )
    advance(PLAN[4])

    def hidden_body(weight):
        lane = pl.ds(pl.multiple_of(pl.program_id(0) * 256, 256), 256)
        tile = weight[...]

        @pl.loop(0, 4)
        def _(index):
            part = pl.ds(pl.multiple_of(index * rows, rows), rows)
            lhs[part, lane] = dot(first_r[part, :], tile).astype(BF)

    load_act.wait()
    pltpu.emit_pipeline(
        hidden_body,
        grid=(width // 256,),
        in_specs=[pl.BlockSpec((units, 256), lambda t: (0, t))],
    )(down_full)
    da.mate_arrived()
    sum_hidden.send()
    da.forward()
    advance(PLAN[5])
    sum_hidden.pass_on()
    sum_hidden.add_near()
    advance(PLAN[6])
    da.rest_arrived()
    da.finish()
    load_lhs = load(da_hbm, lhs, 0)
    load_own = load(hidden_hbm, da_own, 2)
    load_lhs.wait()

    def dout_body(weight):
        lane = pl.ds(pl.multiple_of(pl.program_id(0) * 256, 256), 256)
        tile = weight[...].reshape(256, width)

        @pl.loop(0, 4)
        def _(index):
            part = pl.ds(pl.multiple_of(index * rows, rows), rows)
            dout_ref[part, lane] = contract_cols(lhs[part, :], tile).astype(BF)

    out_blocks, out_rows = out_full.shape[:2]
    pltpu.emit_pipeline(
        dout_body,
        grid=(out_blocks * out_rows // 256,),
        in_specs=[pl.BlockSpec((256 // out_rows, out_rows, width), lambda t: (t, 0, 0))],
    )(out_full)

    for head in range(heads):
        turned[head] = mixed_ref[:, head * HEAD_DIM : (head + 1) * HEAD_DIM].T
    compute_terms(
        here,
        give_out,
        keep_out,
        lambda group: turned[0:heads].reshape(heads * HEAD_DIM, length),
        lambda lane: lhs[:, lane],
        lambda group: [(zone, 0) for zone in range(heads)],
        [(0, zone_order)],
        [jobs["out"]],
    )
    load_turned = load(n1_hbm, turned, 0)
    sum_hidden.add_far()
    for index, peer in enumerate((here.mate, here.far)):
        pl.semaphore_signal(credit.at[index], inc=1, device_id=peer, device_id_type=MESH)

    @pl.loop(0, rows // 32)
    def _(index):
        part = pl.ds(pl.multiple_of(index * 32, 32), 32)
        pair[part, :] = grad_in[part, :].astype(BF)

    store_hidden = load(pair, hidden_out, 1)
    advance(PLAN[7])

    lse_t[...] = lse_ref[...].T[0:8]
    delta[...] = jnp.zeros_like(delta)
    for head in range(heads):
        lane = slice(head * HEAD_DIM, (head + 1) * HEAD_DIM)
        terms = dout_ref[:, lane].astype(F32) * mixed_ref[:, lane].astype(F32)
        delta[:, head : head + 1] = jnp.sum(terms, axis=-1, keepdims=True)
    delta_t[...] = delta[...].T[0:8]
    def through_norm(grad, head, part, gain_ref, which):
        proj = proj_buf[part, :]
        scales = lax.rsqrt(jnp.mean(proj * proj, axis=-1, keepdims=True) + EPSILON)
        normed = proj * scales
        grad = grad.astype(F32)
        upper = grad * cos_ref[part, :] - pltpu.roll(grad, HEAD_DIM // 2, 1) * sin_ref[part, :]
        gain_row[:, which * HEAD_DIM : (which + 1) * HEAD_DIM] += jnp.sum(
            upper * normed, axis=0, keepdims=True
        )
        upper = upper * gain_ref[...]
        inner = jnp.mean(upper * normed, axis=-1, keepdims=True)
        result = (scales * (upper - normed * inner)).astype(BF)
        first_r[part, head * HEAD_DIM : (head + 1) * HEAD_DIM] = result

    for head in range(heads):
        pair_head = head // 2
        load_proj = load(proj_hbm.at[head], proj_buf, 4)
        if head % 2 == 0:
            dk_sum[...] = jnp.zeros_like(dk_sum)
            dv_sum[...] = jnp.zeros_like(dv_sum)
        for block in range(4):
            end = (block + 1) * rows
            part = pl.ds(block * rows, rows)
            queries = heads_ref[head, part, :]
            keys = heads_ref[heads + pair_head, 0:end, :]
            values = heads_ref[heads + kv_heads + pair_head, 0:end, :]
            out_grad = dout_ref[part, head * HEAD_DIM : (head + 1) * HEAD_DIM]
            scores = contract_cols(keys, queries)
            key_place = lax.broadcasted_iota(jnp.int32, (end, rows), 0)
            query_place = lax.broadcasted_iota(jnp.int32, (end, rows), 1) + block * rows
            allowed = (key_place >= start_ref[:, part]) & (key_place <= query_place)
            weights = jnp.exp(scores * scale - lse_t[head : head + 1, part])
            weights = jnp.where(allowed, weights, 0.0)
            weight_grad = contract_cols(values, out_grad)
            inner = delta_t[head : head + 1, part]
            score_grad = (weights * (weight_grad - inner)).astype(BF)
            dk_sum[0:end, :] += dot(score_grad, queries) * scale
            dv_sum[0:end, :] += dot(weights.astype(BF), out_grad)
            query_grad = (contract_rows(score_grad, keys) * scale).astype(BF)
            if block == 0:
                load_proj.wait()
            through_norm(query_grad, head, part, query_gain_ref, 0)
        if head % 2:
            key = heads + pair_head
            value_at = (heads + kv_heads + pair_head) * HEAD_DIM
            load(proj_hbm.at[key], proj_buf, 4).wait()

            @pl.loop(0, 4)
            def _(index):
                part = pl.ds(pl.multiple_of(index * rows, rows), rows)
                through_norm(dk_sum[part, :].astype(BF), key, part, key_gain_ref, 1)
                first_r[part, value_at : value_at + HEAD_DIM] = dv_sum[part, :].astype(BF)

        advance(PLAN[8 + head])

    load_turned.wait()
    jobs["first"].sent()
    store_hidden.wait()
    proj_grads = first_r.at[:, 0:qkv_width]
    model_terms(
        give.at[1, :, :, :, 0:qkv_width],
        second_r.at[:, :, :, 0:qkv_width],
        first_columns,
        [jobs["query"], jobs["key"]],
    )
    advance(PLAN[12])

    def dn1_body(weight):
        lane = pl.ds(pl.multiple_of(pl.program_id(0) * 256, 256), 256)
        tile = weight[...].reshape(256, qkv_width)

        @pl.loop(0, 4)
        def _(index):
            part = pl.ds(pl.multiple_of(index * rows, rows), rows)
            lhs[part, lane] = contract_cols(proj_grads[part, :], tile).astype(BF)

    pltpu.emit_pipeline(
        dn1_body,
        grid=(width // 256,),
        in_specs=[pl.BlockSpec((slabs, own, qkv_width), lambda t: (t, 0, 0))],
    )(qkv_full)
    grad_in[...] = jnp.zeros_like(grad_in)
    pl.semaphore_wait(credit.at[0], 1)
    pl.semaphore_wait(credit.at[1], 1)
    sum_attn.send()
    advance(PLAN[13])
    sum_attn.pass_on()
    sum_attn.add_near()
    advance(PLAN[14])
    sum_attn.add_far()
    load_own.wait()

    @pl.loop(0, rows // narrow)
    def _(index):
        part = pl.ds(pl.multiple_of(index * narrow, narrow), narrow)
        values = da_own[part, :].astype(F32)
        scales = lax.rsqrt(jnp.mean(values * values, axis=-1, keepdims=True) + EPSILON)
        normed = values * scales
        update = grad_in[part, :]
        gain_row[:, attn_lane] += jnp.sum(update * normed, axis=0, keepdims=True)
        upper = update * attn_gain_ref[...]
        inner = jnp.mean(upper * normed, axis=-1, keepdims=True)
        grad_in[part, :] = middle_grad[part, :] + scales * (upper - normed * inner)

    gain_sum = GainSum(here, gain_row, gain_seq, gain_middle, gain_shard, (gss, gsr, gts, gtr))
    gain_sum.start()
    advance(PLAN[15])
    gain_sum.turn()
    advance(PLAN[16])
    gains_out[...] = gain_sum.finish()
    for spread_rows in spreads.values():
        spread_rows.arrive()
    for name, job in jobs.items():
        if name != "first":
            job.sent()
    for job in jobs.values():
        job.settle()
    for job in spreads.values():
        job.finish()


def backward(saved, weights, own, gains, tables, starts):
    size = lax.axis_size("shard")
    outer = size // 2
    (n1, dy, n2, act, first, second, proj, heads_all, mixed, lse, middle) = saved
    length, width = heads_all.shape[1], middle.shape[1]
    piece = length // 4
    units = act.shape[1]
    qkv_width = weights[0].shape[2]
    rows = width // (4 * size)
    q_width = mixed.shape[1]

    def shape(*dims, kind=BF):
        return jax.ShapeDtypeStruct(dims, kind)

    results = [
        shape(piece, width, kind=F32),
        shape(1, 2 * width + 2 * HEAD_DIM, kind=F32),
        shape(1, rows, width, kind=F32),
        shape(piece, width),
        shape(4, rows, units),
        shape(4, rows, units),
        shape(4, rows, units),
        shape(4, rows, qkv_width),
        shape(length, width),
    ]
    results += [shape(3, outer, 4, rows, units)] * 3
    results += [shape(outer, 4, rows, units * 2 // 3)] * 2
    results += [shape(outer, 4, rows, qkv_width)] * 3
    results += [shape(outer, 1, rows, width)] * 3
    dma = pltpu.SemaphoreType.DMA
    vmem = pltpu.VMEM
    return pl.pallas_call(
        functools.partial(backward_kernel, size),
        out_shape=results,
        in_specs=[ANY] * 7 + [VMEM] * 3 + [ANY] * 8 + [VMEM] * 7,
        out_specs=[VMEM] * 3 + [ANY] * (len(results) - 3),
        scratch_shapes=[
            vmem((length, width), BF),
            vmem((width // 128, 128, length), BF),
            vmem((length, units), BF),
            vmem((outer, 4, rows, units), BF),
            vmem((3, outer, 4, rows, units), BF),
            vmem((3, outer, 4, rows, units), BF),
            vmem((outer, 1, rows, width), BF),
            vmem((outer, 1, rows, width), BF),
            vmem((2, 4, rows, units), BF),
            vmem((2, 1, rows, width), BF),
            vmem((length, q_width), BF),
            vmem((piece, width), BF),
            vmem((2, piece, width), BF),
            vmem((piece, width), BF),
            vmem((piece, width), BF),
            vmem((piece, width), F32),
            vmem((length, HEAD_DIM), F32),
            vmem((8, length), F32),
            vmem((length, 128), F32),
            vmem((8, length), F32),
            vmem((length, HEAD_DIM), F32),
            vmem((length, HEAD_DIM), F32),
            vmem((1, 2 * width + 2 * HEAD_DIM), F32),
            vmem((4, 1, 2 * width + 2 * HEAD_DIM), F32),
            vmem((1, 2 * width + 2 * HEAD_DIM), F32),
            vmem((size, 1, 2 * width + 2 * HEAD_DIM), F32),
            dma((8, outer)),
            dma((8, outer)),
            dma((8, outer)),
            dma((8, outer)),
            dma((8, outer)),
            dma((8, outer)),
            dma((8, 3)),
            dma((6, 3)),
            dma((6, 3)),
            dma((6,)),
            dma((3, 3)),
            dma((3, 3)),
            dma((3,)),
            dma((3,)),
            dma((1,)),
            dma((3,)),
            dma((3,)),
            dma((size - 1,)),
            dma((size - 1,)),
            dma((5,)),
            pltpu.SemaphoreType.REGULAR((2,)),
        ],
        compiler_params=pltpu.CompilerParams(
            collective_id=1, has_side_effects=True, vmem_limit_bytes=VMEM_BYTES
        ),
        name="backward_sums",
    )(
        n1,
        dy,
        n2,
        act,
        first,
        second.reshape(outer, 4, rows, units),
        proj,
        heads_all,
        mixed,
        lse,
        middle,
        *own,
        *weights,
        *gains,
        *tables,
        starts,
    )


def finish_kernel(
    size,
    grad_in,
    gains,
    grad_out,
    hidden_out,
    down_rows,
    first_rows,
    second_rows,
    qkv_rows,
    grad_in_out,
    grad_out_out,
    hidden_out_out,
    grad_query,
    grad_key,
    grad_value,
    grad_gate,
    grad_up,
    grad_down,
    attn_gain,
    mlp_gain,
    query_gain,
    key_gain,
    grad_in_buf,
    grad_out_buf,
    hidden_buf,
    down_buf,
    first_buf,
    second_buf,
    qkv_buf,
    query_buf,
    key_buf,
    value_buf,
    gate_buf,
    up_buf,
    wide_buf,
    load_sems,
    store_sems,
):
    units = down_buf.shape[2]
    chunk = units // 2
    ff_part = units // size
    most, tail = chunk - 256, 256
    stores = []

    def load(source, target, index):
        copy = pltpu.make_async_copy(source, target, load_sems.at[index])
        copy.start()
        return copy

    def store(source, target):
        copy = pltpu.make_async_copy(source, target, store_sems.at[len(stores)])
        copy.start()
        stores.append(copy)

    loads = [
        load(source, target, index)
        for index, (source, target) in enumerate(
            (
                (down_rows, down_buf),
                (first_rows, first_buf),
                (second_rows, second_buf),
                (qkv_rows, qkv_buf),
                (grad_in, grad_in_buf),
                (hidden_out, hidden_buf),
                (grad_out, grad_out_buf),
            )
        )
    ]

    def place(read, target):
        @pl.loop(0, target.shape[0] // 16)
        def _(index):
            part = pl.ds(pl.multiple_of(index * 16, 16), 16)
            values = [read(seq, part).astype(F32) for seq in range(4)]
            for begin in range(0, size, size // 8):
                pieces = [
                    values[seq][:, block * ff_part : (block + 1) * ff_part]
                    for block in range(begin, begin + size // 8)
                    for seq in range(4)
                ]
                lane = slice(begin * 4 * ff_part, (begin + size // 8) * 4 * ff_part)
                target[part, lane] = jnp.concatenate(pieces, axis=1)

    def side(index):
        at = 2 * most + index * tail

        def read(seq, part):
            return jnp.concatenate(
                [
                    first_buf[seq, part, index * chunk : (index + 1) * chunk],
                    second_buf[seq, part, index * most : (index + 1) * most],
                    second_buf[seq, part, at : at + tail],
                ],
                axis=1,
            )

        return read

    loads[0].wait()
    place(lambda seq, part: down_buf[seq, part, :], wide_buf)
    store(wide_buf, grad_down)
    loads[1].wait()
    loads[2].wait()
    place(side(0), gate_buf)
    store(gate_buf, grad_gate)
    place(side(1), up_buf)
    store(up_buf, grad_up)
    loads[4].wait()
    store(grad_in_buf, grad_in_out)
    loads[5].wait()
    store(hidden_buf, hidden_out_out)
    loads[6].wait()
    store(grad_out_buf, grad_out_out)
    loads[3].wait()
    at = 0
    for buf, target in ((query_buf, grad_query), (key_buf, grad_key), (value_buf, grad_value)):
        count = buf.shape[1] // 4
        for seq in range(4):
            buf[:, seq * count : (seq + 1) * count] = qkv_buf[seq, :, at : at + count].astype(F32)
        at += count
        store(buf, target)
    at = 0
    for target in (query_gain, key_gain, mlp_gain, attn_gain):
        target[...] = gains[:, at : at + target.shape[1]]
        at += target.shape[1]
    for copy in stores:
        copy.wait()


def finish(grad_in, gains, grad_out, hidden_out, down_rows, first_rows, second_rows, qkv_rows):
    size = lax.axis_size("shard")
    piece, width = grad_in.shape
    rows, units = down_rows.shape[1:]
    qkv_width = qkv_rows.shape[2]

    def shape(*dims, kind=F32):
        return jax.ShapeDtypeStruct(dims, kind)

    results = [
        shape(piece, width),
        shape(1, rows, width),
        shape(piece, width, kind=BF),
        shape(rows, 2 * qkv_width),
        shape(rows, qkv_width),
        shape(rows, qkv_width),
        shape(rows, 4 * units),
        shape(rows, 4 * units),
        shape(rows, 4 * units),
        shape(1, width),
        shape(1, width),
        shape(1, HEAD_DIM),
        shape(1, HEAD_DIM),
    ]
    return pl.pallas_call(
        functools.partial(finish_kernel, size),
        out_shape=results,
        in_specs=[ANY, VMEM] + [ANY] * 6,
        out_specs=[ANY] * 9 + [VMEM] * 4,
        scratch_shapes=[
            pltpu.VMEM((piece, width), F32),
            pltpu.VMEM((1, rows, width), F32),
            pltpu.VMEM((piece, width), BF),
            pltpu.VMEM((4, rows, units), BF),
            pltpu.VMEM((4, rows, units), BF),
            pltpu.VMEM((4, rows, units), BF),
            pltpu.VMEM((4, rows, qkv_width), BF),
            pltpu.VMEM((rows, 2 * qkv_width), F32),
            pltpu.VMEM((rows, qkv_width), F32),
            pltpu.VMEM((rows, qkv_width), F32),
            pltpu.VMEM((rows, 4 * units), F32),
            pltpu.VMEM((rows, 4 * units), F32),
            pltpu.VMEM((rows, 4 * units), F32),
            pltpu.SemaphoreType.DMA((7,)),
            pltpu.SemaphoreType.DMA((9,)),
        ],
        compiler_params=pltpu.CompilerParams(vmem_limit_bytes=VMEM_BYTES),
        name="finish",
    )(grad_in, gains, grad_out, hidden_out, down_rows, first_rows, second_rows, qkv_rows)


def local(
    hidden_in,
    segment_ids,
    norm_attn_gain,
    w_query,
    w_key,
    w_value,
    query_gain,
    key_gain,
    w_out,
    norm_mlp_gain,
    w_gate,
    w_up,
    w_down,
    out_cotangent,
):
    segment = segment_ids[0]
    gains = (norm_attn_gain[None], norm_mlp_gain[None], query_gain[None], key_gain[None])
    results = forward(
        hidden_in[0],
        out_cotangent[0],
        (w_query, w_key, w_value, w_out, w_gate, w_up, w_down),
        gains,
        segment,
    )
    (
        grad_in,
        grad_out,
        hidden_out,
        grad_query,
        grad_key,
        grad_value,
        grad_gate,
        grad_up,
        grad_down,
        attn_gain,
        mlp_gain,
        query_grad,
        key_grad,
    ) = finish(
        *backward(
            results[8:19],
            results[:5],
            (hidden_in[0], out_cotangent[0]),
            gains,
            results[19:21],
            results[21],
        )[:8]
    )
    return (
        hidden_out[None],
        grad_in[None],
        attn_gain[0],
        grad_query,
        grad_key,
        grad_value,
        query_grad[0],
        key_grad[0],
        grad_out[0],
        mlp_gain[0],
        grad_gate,
        grad_up,
        grad_down.T,
    )


def solution(mesh):
    return jax.shard_map(
        local,
        mesh=mesh,
        in_specs=(
            P("shard", "seq", None),
            P("shard", None),
            P(),
            P("shard", None),
            P("shard", None),
            P("shard", None),
            P(),
            P(),
            P("shard", None),
            P(),
            P("shard", None),
            P("shard", None),
            P("shard", None),
            P("shard", "seq", None),
        ),
        out_specs=(
            P("shard", "seq", None),
            P("shard", "seq", None),
            P(),
            P(("seq", "shard"), None),
            P(("seq", "shard"), None),
            P(("seq", "shard"), None),
            P(),
            P(),
            P(("seq", "shard"), None),
            P(),
            P(("seq", "shard"), None),
            P(("seq", "shard"), None),
            P(None, ("seq", "shard")),
        ),
        check_vma=False,
    )
```

```python
import functools

import jax
import jax.numpy as jnp
import numpy as np
from jax import lax
from jax.experimental import pallas as pl
from jax.experimental.pallas import tpu as pltpu
from jax.sharding import PartitionSpec as P

Q_HEADS = 16
KV_HEADS = 8
HEAD_DIM = 128
EPSILON = 1e-06
ROPE_BASE = 1000000.0
NEGATIVE = -1e30
BF = jnp.bfloat16
F32 = jnp.float32
MESH = pl.DeviceIdType.MESH
ANY = pl.BlockSpec(memory_space=pl.ANY)
VMEM = pl.BlockSpec(memory_space=pltpu.VMEM)
VMEM_BYTES = 62 * 1024 * 1024


def dot(left, right):
    return jnp.dot(left, right, preferred_element_type=F32)


def contract_cols(left, right):
    return lax.dot_general(left, right, (((1,), (1,)), ((), ())), preferred_element_type=F32)


class Place:
    def __init__(self, size):
        self.size = size
        self.outer = size // 2
        self.quarter = size // 4
        self.seq = lax.axis_index("seq")
        self.shard = lax.axis_index("shard")
        self.chip = self.seq // 2
        self.core = lax.rem(self.seq, 2)
        self.place = self.shard // 2
        self.half = lax.rem(self.shard, 2)
        self.far_seq = lax.rem(self.seq + 2, 4)
        self.mate_seq = self.chip * 2 + 1 - self.core
        self.far = {"seq": self.far_seq}
        self.mate = {"seq": self.mate_seq}
        self.twin_shard = self.place * 2 + 1 - self.half
        self.twin = {"shard": self.twin_shard}

    def outer_peer(self, place):
        return {"shard": place * 2 + self.half}

    def greet(self, wide=False):
        barrier = pltpu.get_barrier_semaphore()
        last = self.outer - 1

        def signal(peer):
            pl.semaphore_signal(barrier, inc=1, device_id=peer, device_id_type=MESH)

        signal(self.far)
        signal(self.mate)
        if wide:
            signal({"seq": 3 - self.seq})
            for amount in range(1, self.size):
                signal({"shard": lax.rem(self.shard + amount, self.size)})
            pl.semaphore_wait(barrier, 2 + self.size)
            return
        signal(self.twin)

        @pl.when(self.place < last)
        def _():
            signal(self.outer_peer(self.place + 1))

        @pl.when(self.place > 0)
        def _():
            signal(self.outer_peer(self.place - 1))

        inner = ((self.place > 0) & (self.place < last)).astype(jnp.int32)
        pl.semaphore_wait(barrier, 4 + inner)


def remote(source, target, send, receive, peer):
    return pltpu.make_async_remote_copy(
        src_ref=source,
        dst_ref=target,
        send_sem=send,
        recv_sem=receive,
        device_id=peer,
        device_id_type=MESH,
    )


class LineGather:
    def __init__(self, here, own, slot, sems):
        self.here, self.own, self.slot = here, own, slot
        self.us, self.ur, self.ds, self.dr = sems
        self.last = here.outer - 1

    def up(self, distance):
        here = self.here
        slot = self.slot(here.place - distance)
        source = slot if distance else self.own
        peer = here.outer_peer(here.place + 1)
        return remote(source, slot, self.us.at[distance], self.ur.at[distance], peer)

    def down(self, distance):
        here = self.here
        slot = self.slot(here.place + distance)
        source = slot if distance else self.own
        peer = here.outer_peer(here.place - 1)
        return remote(source, slot, self.ds.at[distance], self.dr.at[distance], peer)

    def send(self):
        here = self.here

        @pl.when(here.place < self.last)
        def _():
            self.up(0).start()

        @pl.when(here.place > 0)
        def _():
            self.down(0).start()

    def step(self, distance, arrived=lambda place: None):
        here = self.here
        below = here.place - 1 - distance
        above = here.place + 1 + distance

        @pl.when(below >= 0)
        def _():
            slot = self.slot(below)
            remote(slot, slot, self.us.at[0], self.ur.at[distance], here.twin).wait_recv()

            @pl.when(here.place < self.last)
            def _():
                self.up(distance + 1).start()

            arrived(below)

        @pl.when(above <= self.last)
        def _():
            slot = self.slot(above)
            remote(slot, slot, self.ds.at[0], self.dr.at[distance], here.twin).wait_recv()

            @pl.when(here.place > 0)
            def _():
                self.down(distance + 1).start()

            arrived(above)

    def finish(self):
        here = self.here
        for distance in range(self.last):

            @pl.when((here.place - distance >= 0) & (here.place < self.last))
            def _():
                self.up(distance).wait_send()

            @pl.when((here.place + distance <= self.last) & (here.place > 0))
            def _():
                self.down(distance).wait_send()


class RowGather:
    def __init__(self, here, own, whole, sems, spot=lambda shard: shard):
        self.here, self.own, self.whole, self.spot = here, own, whole, spot
        self.ys, self.yr, self.local = sems[4:]
        self.line = LineGather(here, own, self.mine, sems[:4])

    def mine(self, place):
        return self.whole.at[self.spot(place * 2 + self.here.half)]

    def theirs(self, place):
        return self.whole.at[self.spot(place * 2 + 1 - self.here.half)]

    def keep(self):
        return pltpu.make_async_copy(self.own, self.mine(self.here.place), self.local)

    def across(self, place, own=False):
        slot = self.mine(place)
        source = self.own if own else slot
        return remote(source, slot, self.ys.at[place], self.yr.at[place], self.here.twin)

    def arrived(self, place):
        slot = self.theirs(place)
        remote(slot, slot, self.ys.at[place], self.yr.at[place], self.here.twin).wait_recv()

    def send(self):
        self.line.send()
        self.across(self.here.place, own=True).start()
        self.keep().start()

    def step(self, distance):
        self.line.step(distance, lambda place: self.across(place).start())

    def arrive(self):
        self.keep().wait()
        for place in range(self.here.outer):
            self.arrived(place)

    def finish(self):
        self.line.finish()
        for place in range(self.here.outer):
            self.across(place).wait_send()


class TwinFirstGather(RowGather):
    def __init__(self, here, own, whole, sems, twin_sems):
        super().__init__(here, own, whole, sems)
        self.lines = [
            self.line,
            LineGather(here, self.theirs(here.place), self.theirs, twin_sems[:4]),
        ]

    def twin(self):
        self.arrived(self.here.place)
        self.lines[1].send()

    def step(self, distance):
        for line in self.lines:
            line.step(distance)

    def arrive(self):
        self.keep().wait()

    def finish(self):
        for line in self.lines:
            line.finish()
        self.across(self.here.place, own=True).wait_send()


class HeadGather:
    def __init__(self, here, own, whole, sems):
        self.here, self.own, self.whole = here, own, whole
        self.us, self.zr, self.ds, _, self.ys, self.yr, self.local = sems
        self.last = here.outer - 1
        self.count = here.quarter // 2
        self.first = here.seq * self.count
        self.mine = here.place - self.first
        self.inside = (self.mine >= 0) & (self.mine < self.count)

    def slot(self, index):
        return self.whole.at[index * 2 + self.here.half]

    def keep(self):
        return pltpu.make_async_copy(self.own, self.slot(self.mine), self.local)

    def up(self, index, own=False):
        slot = self.slot(index)
        peer = self.here.outer_peer(self.here.place + 1)
        return remote(self.own if own else slot, slot, self.us.at[index], self.zr.at[index], peer)

    def down(self, index, own=False):
        slot = self.slot(index)
        peer = self.here.outer_peer(self.here.place - 1)
        return remote(self.own if own else slot, slot, self.ds.at[index], self.zr.at[index], peer)

    def across(self, index):
        slot = self.slot(index)
        return remote(slot, slot, self.ys.at[index], self.yr.at[index], self.here.twin)

    def send(self):
        @pl.when(self.inside)
        def _():
            self.keep().start()

            @pl.when(self.here.place < self.last)
            def _():
                self.up(self.mine, own=True).start()

            @pl.when(self.here.place > 0)
            def _():
                self.down(self.mine, own=True).start()

    def step(self):
        here = self.here

        @pl.when(self.inside)
        def _():
            self.keep().wait()

        for index in range(self.count):
            slot = self.slot(index)
            arrival = remote(slot, slot, self.us.at[0], self.zr.at[index], here.twin)

            @pl.when(self.mine > index)
            def _():
                arrival.wait_recv()

                @pl.when(here.place < self.last)
                def _():
                    self.up(index).start()

            @pl.when(self.mine < index)
            def _():
                arrival.wait_recv()

                @pl.when(here.place > 0)
                def _():
                    self.down(index).start()

            self.across(index).start()

    def arrive(self):
        for index in range(self.count):
            slot = self.whole.at[index * 2 + 1 - self.here.half]
            remote(
                slot, slot, self.ys.at[index], self.yr.at[index], self.here.twin
            ).wait_recv()

    def finish(self):
        here = self.here
        for index in range(self.count):

            @pl.when((self.mine >= index) & (here.place < self.last))
            def _():
                self.up(index).wait_send()

            @pl.when((self.mine <= index) & (here.place > 0))
            def _():
                self.down(index).wait_send()

            self.across(index).wait_send()


class TokenGather:
    def __init__(self, here, own, whole, sems):
        self.here, self.own, self.whole = here, own, whole
        self.send_sems, self.recv_sems, self.local = sems
        self.rows = whole.shape[0] // 4

    def slot(self, seq):
        return self.whole.at[pl.ds(pl.multiple_of(seq * self.rows, self.rows), self.rows), :]

    def keep(self):
        return pltpu.make_async_copy(self.own, self.slot(self.here.seq), self.local)

    def copy(self, index):
        here = self.here
        slot = self.slot(here.far_seq if index == 2 else here.seq)
        return remote(
            slot if index == 2 else self.own,
            slot,
            self.send_sems.at[index],
            self.recv_sems.at[index],
            here.far if index == 0 else here.mate,
        )

    def send(self):
        self.copy(0).start()
        self.copy(1).start()
        self.keep().start()

    def forward(self):
        self.copy(0).wait_recv()
        self.copy(2).start()

    def mate_arrived(self):
        self.copy(1).wait_recv()

    def rest_arrived(self):
        self.copy(2).wait_recv()
        self.keep().wait()

    def arrive(self):
        self.mate_arrived()
        self.rest_arrived()

    def finish(self):
        for index in range(3):
            self.copy(index).wait_send()


class PieceSum:
    def __init__(self, here, piece, base, give, got, pair, far_got, sems, step):
        self.here, self.piece, self.base, self.step = here, piece, base, step
        self.give, self.got, self.pair, self.far_got = give, got, pair, far_got
        self.send_sems, self.recv_sems = sems

    def to_mate(self, index):
        return remote(
            self.give.at[index],
            self.got.at[index],
            self.send_sems.at[index],
            self.recv_sems.at[index],
            self.here.mate,
        )

    def to_far(self):
        return remote(
            self.pair, self.far_got, self.send_sems.at[2], self.recv_sems.at[2], self.here.far
        )

    def columns(self, body):
        step = self.step

        @pl.loop(0, self.pair.shape[1] // step)
        def _(index):
            body(pl.ds(pl.multiple_of(index * step, step), step))

    def send(self):
        here = self.here
        for index, chip in enumerate((1 - here.chip, here.chip)):
            seq = chip * 2 + 1 - here.core

            def fill(column, index=index, seq=seq):
                self.give[index, :, column] = self.piece(seq, column).astype(BF)

            self.columns(fill)
            self.to_mate(index).start()

    def pass_on(self):
        self.to_mate(0).wait_recv()

        def fill(column):
            term = self.piece(self.here.far_seq, column) + self.got[0, :, column].astype(F32)
            self.pair[:, column] = term.astype(BF)

        self.columns(fill)
        self.to_far().start()

    def add_near(self):
        self.to_mate(1).wait_recv()

        def fill(column):
            term = self.piece(self.here.seq, column) + self.got[1, :, column].astype(F32)
            self.base[:, column] += term

        self.columns(fill)

    def add_far(self):
        self.to_far().wait_recv()

        def fill(column):
            self.base[:, column] += self.far_got[:, column].astype(F32)

        self.columns(fill)
        for copy in (self.to_mate(0), self.to_mate(1), self.to_far()):
            copy.wait_send()


def identity(size):
    rows = lax.broadcasted_iota(jnp.int32, (size, size), 0)
    columns = lax.broadcasted_iota(jnp.int32, (size, size), 1)
    return jnp.where(rows == columns, 1.0, 0.0).astype(BF)


FORWARD_PLAN = (
    (("down", "send"),),
    (),
    (),
    (("down", 0), ("out", "send"),),
    (("second", "send"),),
    (),
    (("down", 1),),
    (("down", 2),),
    (),
    (("out", 0),),
    (("first", "send"),),
    (),
    (),
    (("third", "send"), ("first", 0),),
    (("second", "twin"),),
    (("first", 1), ("second", 0),),
    (("first", 2),),
    (("third", 0),),
    (("second", 1),),
    (("third", 1),),
    (("second", 2), ("third", 2),),
    (),
    (),
)


def forward_kernel(
    size,
    hidden_ref,
    dy_hbm,
    w_query,
    w_key,
    w_value,
    w_out,
    w_gate,
    w_up,
    w_down,
    attn_gain_ref,
    mlp_gain_ref,
    query_gain_ref,
    key_gain_ref,
    inverse_ref,
    segment_ref,
    qkv_full,
    out_full,
    first_full,
    second_full,
    down_full,
    n1_full,
    dy_full,
    n2_full,
    n1_turned,
    dy_turned,
    n2_turned,
    act_out,
    first_pair,
    second_pair,
    proj_ref,
    heads_ref,
    mixed_ref,
    lse_ref,
    middle_ref,
    cos_ref,
    sin_ref,
    start_row,
    lhs,
    dy_all,
    turned,
    qkv_w,
    out_w,
    qkv_own,
    out_own,
    down_own,
    dy_own,
    wide_own,
    first_own,
    second_own,
    own_rows,
    give,
    got,
    pair,
    far_got,
    us,
    ur,
    ds,
    dr,
    ys,
    yr,
    row_local,
    ts,
    tr,
    token_local,
    load_sem,
    ss,
    sr,
    start_ref,
    turned_ids,
    eye,
):
    here = Place(size)
    last = here.outer - 1
    length, width = lhs.shape
    lse_ref[...] = jnp.zeros_like(lse_ref)
    rows = length // 4
    units = act_out.shape[1]
    chunk = units // 2
    tail = 256
    heads = mixed_ref.shape[1] // HEAD_DIM
    kv_heads = heads // 2
    ff_part = units // size

    def sems(index):
        return tuple(kind.at[index] for kind in (us, ur, ds, dr, ys, yr, row_local))

    down_rows = pl.ds(pl.multiple_of(here.seq * ff_part, ff_part), ff_part)
    qkv = RowGather(here, qkv_own, qkv_full, sems(0))
    out = HeadGather(here, out_own, out_full, sems(1))
    down = RowGather(
        here,
        down_own,
        down_full,
        sems(2),
        lambda shard: pl.ds(pl.multiple_of(shard * ff_part, ff_part), ff_part),
    )
    first = RowGather(here, first_own, first_full, sems(3))
    cut = 2 * (chunk - tail)
    second = TwinFirstGather(
        here, second_own.at[:, 0:cut], second_full.at[:, :, 0:cut], sems(4), sems(6)
    )
    third = RowGather(
        here, second_own.at[:, cut : 2 * chunk], second_full.at[:, :, cut : 2 * chunk], sems(5)
    )
    n1 = TokenGather(here, own_rows.at[0], n1_full, (ts.at[0], tr.at[0], token_local.at[0]))
    n2 = TokenGather(here, own_rows.at[1], n2_full, (ts.at[1], tr.at[1], token_local.at[1]))
    dy = TokenGather(here, dy_own, dy_full, (ts.at[2], tr.at[2], token_local.at[2]))

    loads = []
    at = 0
    for index, (weight, count) in enumerate(((w_query, heads), (w_key, kv_heads), (w_value, kv_heads))):
        count = count * HEAD_DIM
        source = weight.at[:, pl.ds(pl.multiple_of(here.seq * count, count), count)]
        loads.append(
            pltpu.make_async_copy(source, qkv_own.at[:, at : at + count], load_sem.at[index])
        )
        at += count
    loads.append(pltpu.make_async_copy(w_down.at[down_rows, :], down_own, load_sem.at[3]))
    loads.append(pltpu.make_async_copy(w_out, out_own, load_sem.at[4]))
    loads.append(pltpu.make_async_copy(dy_hbm, dy_own, load_sem.at[5]))
    loads.append(pltpu.make_async_copy(w_gate, wide_own, load_sem.at[6]))
    for load in loads:
        load.start()
    here.greet()
    for load in loads[:3]:
        load.wait()
    qkv.send()
    loads[5].wait()
    dy.send()

    def norm_rows(source, gain_ref, target):
        @pl.loop(0, rows // 32)
        def _(index):
            part = pl.ds(pl.multiple_of(index * 32, 32), 32)
            values = source[part, :].astype(F32)
            scales = lax.rsqrt(jnp.mean(values * values, axis=-1, keepdims=True) + EPSILON)
            target[part, :] = (values * scales * gain_ref[...]).astype(BF)

    gathers = {"out": out, "down": down, "first": first, "second": second, "third": third}

    def advance(steps):
        for name, step in steps:
            gather = gathers[name]
            if step == "send":
                gather.send()
            elif step == "twin":
                gather.twin()
            elif name == "out":
                gather.step()
            else:
                for distance in range(last * step // 3, last * (step + 1) // 3):
                    gather.step(distance)

    norm_rows(hidden_ref, attn_gain_ref, own_rows.at[0])
    n1.send()
    for load in loads[3:5]:
        load.wait()
    advance(FORWARD_PLAN[0])
    for load in loads[6:]:
        load.wait()

    most = chunk - tail

    def cut_units(side):
        for seq in range(4):

            @pl.when(here.seq == seq)
            def _():
                @pl.loop(0, wide_own.shape[0] // 16)
                def _(index):
                    part = pl.ds(pl.multiple_of(index * 16, 16), 16)

                    def gathered(begin):
                        pieces = [
                            wide_own[part, (block * 4 + seq) * ff_part : (block * 4 + seq + 1) * ff_part]
                            for block in range(begin, begin + size // 2)
                        ]
                        return jnp.concatenate(pieces, axis=1)

                    first_own[part, side * chunk : (side + 1) * chunk] = gathered(0)
                    rest = gathered(size // 2)
                    second_own[part, side * most : (side + 1) * most] = rest[:, 0:most]
                    at = 2 * most + side * tail
                    second_own[part, at : at + tail] = rest[:, most:]

    eye[...] = identity(256)

    def rotation():
        ids = segment_ref[...].astype(F32)
        turned_ids[...] = jnp.broadcast_to(ids, (128, length)).T
        lane = lax.broadcasted_iota(jnp.int32, (128, 128), 1)

        @pl.loop(0, length // 128)
        def _(index):
            part = pl.ds(pl.multiple_of(index * 128, 128), 128)
            own_ids = turned_ids[part, :]
            count = jnp.zeros((128, 128), F32)
            for at in range(0, length, 128):
                count = count + jnp.where(
                    segment_ref[:, at : at + 128].astype(F32) < own_ids, 1.0, 0.0
                )
            starts = jnp.sum(count, axis=-1, keepdims=True)
            start_ref[part, :] = starts.astype(jnp.int32)
            starts = jnp.broadcast_to(starts, (128, 128))
            turned_ids[part, :] = starts
            places = lax.broadcasted_iota(jnp.int32, (128, 128), 0) + index * 128
            angles = (places.astype(F32) - starts) * inverse_ref[...]
            cos_ref[part, :] = jnp.cos(angles)
            sine = jnp.sin(angles)
            sin_ref[part, :] = jnp.where(lane < HEAD_DIM // 2, -sine, sine)

        start_row[...] = turned_ids[...].T[0:1].astype(jnp.int32)

    zones = width // 512

    def turn(source, target):
        for seq_group in range(4):
            for zone in range(0, zones, 2):
                at = (seq_group * zones + zone) * 128
                both = contract_cols(eye[...], source[:, at : at + 256]).astype(BF)
                turned[zone * 4 + seq_group] = both[0:128]
                turned[zone * 4 + 4 + seq_group] = both[128:256]
        copy = pltpu.make_async_copy(turned, target, load_sem.at[4])
        copy.start()
        return copy

    cut_units(0)
    load_up = pltpu.make_async_copy(w_up, wide_own, load_sem.at[7])
    load_up.start()
    load_up.wait()
    cut_units(1)
    advance(FORWARD_PLAN[1])
    for third_part in range(3):
        for distance in range(last * third_part // 3, last * (third_part + 1) // 3):
            qkv.step(distance)
        advance(FORWARD_PLAN[2 + third_part])
        if third_part == 0:
            rotation()
            dy.forward()
    dy.arrive()
    load_dy = pltpu.make_async_copy(dy_full, dy_all, load_sem.at[0])
    load_dy.start()
    load_dy.wait()
    store = turn(dy_all, dy_turned)
    n1.forward()
    advance(FORWARD_PLAN[5])
    n1.arrive()
    load_lhs = pltpu.make_async_copy(n1_full, lhs, load_sem.at[0])
    load_lhs.start()
    advance(FORWARD_PLAN[6])
    qkv.arrive()
    load_qkv = pltpu.make_async_copy(qkv_full, qkv_w, load_sem.at[1])
    load_qkv.start()
    advance(FORWARD_PLAN[7])
    load_lhs.wait()
    load_qkv.wait()

    def project(tile):
        weight = qkv_w[:, :, tile * 256 : tile * 256 + 256].reshape(width, 256)
        gain_ref = query_gain_ref if tile < heads // 2 else key_gain_ref

        @pl.loop(0, 4)
        def _(index):
            part = pl.ds(pl.multiple_of(index * rows, rows), rows)
            both = dot(lhs[part, :], weight)
            for side in range(2):
                head = tile * 2 + side
                proj = both[:, side * HEAD_DIM : (side + 1) * HEAD_DIM]
                if head >= heads + kv_heads:
                    heads_ref[head, part, :] = proj.astype(BF)
                    continue
                proj_ref[head, part, :] = proj
                scales = lax.rsqrt(jnp.mean(proj * proj, axis=-1, keepdims=True) + EPSILON)
                gained = proj * scales * gain_ref[...]
                turned = pltpu.roll(gained, HEAD_DIM // 2, 1)
                heads_ref[head, part, :] = (
                    gained * cos_ref[part, :] + turned * sin_ref[part, :]
                ).astype(BF)

    def attend(head):
        pair_head = head // 2
        for block in range(4):
            end = (block + 1) * rows
            part = pl.ds(block * rows, rows)
            scores = contract_cols(
                heads_ref[head, part, :], heads_ref[heads + pair_head, 0:end, :]
            )
            row_place = lax.broadcasted_iota(jnp.int32, (rows, end), 0) + block * rows
            col_place = lax.broadcasted_iota(jnp.int32, (rows, end), 1)
            allowed = (col_place >= start_ref[part, :]) & (col_place <= row_place)
            raised = jnp.where(allowed, jnp.exp(scores * (HEAD_DIM ** (-0.5))), 0.0)
            sums = jnp.sum(raised, axis=-1, keepdims=True)
            mixed = dot(raised.astype(BF), heads_ref[heads + kv_heads + pair_head, 0:end, :])
            mixed = mixed * (1.0 / sums)
            mixed_ref[part, head * HEAD_DIM : (head + 1) * HEAD_DIM] = mixed.astype(BF)
            lse_ref[part, head : head + 1] = jnp.log(sums)

    tiles = (heads + 2 * kv_heads) // 2
    for tile in range(tiles):
        if tile == tiles // 2:
            advance(FORWARD_PLAN[8])
        project(tile)
    advance(FORWARD_PLAN[9])

    for head in range(heads):
        attend(head)
        advance(FORWARD_PLAN[10 + head])
    out.arrive()
    load_out = pltpu.make_async_copy(out_full, out_w, load_sem.at[2])
    load_out.start()
    load_out.wait()

    def out_piece(seq, column):
        part = pl.ds(pl.multiple_of(seq * rows, rows), rows)
        weight = out_w[:, :, column]
        return dot(mixed_ref[part, :], weight.reshape(-1, weight.shape[-1]))

    middle_ref[...] = hidden_ref[...].astype(F32)
    token_sum = PieceSum(
        here, out_piece, middle_ref, give, got, pair, far_got, (ss, sr), 512
    )
    token_sum.send()
    advance(FORWARD_PLAN[14])
    token_sum.pass_on()
    token_sum.add_near()
    advance(FORWARD_PLAN[15])
    token_sum.add_far()
    norm_rows(middle_ref, mlp_gain_ref, own_rows.at[1])
    n2.send()
    advance(FORWARD_PLAN[16])
    store.wait()
    store = turn(lhs, n1_turned)
    advance(FORWARD_PLAN[17])
    n2.forward()
    advance(FORWARD_PLAN[18])
    n2.arrive()
    load_lhs = pltpu.make_async_copy(n2_full, lhs, load_sem.at[3])
    load_lhs.start()
    down.arrive()
    first.arrive()
    load_lhs.wait()

    def feed(gather, begin, count):
        tiles = count // 256
        spot = begin // 256

        def body(gate_w, up_w, down_w, act_ref, gate_grad, up_grad):
            gate_tile = gate_w[...].reshape(width, 256)
            up_tile = up_w[...].reshape(width, 256)
            down_tile = down_w[...]

            @pl.loop(0, 4)
            def _(index):
                part = pl.ds(pl.multiple_of(index * rows, rows), rows)
                gate = dot(lhs[part, :], gate_tile)
                up = dot(lhs[part, :], up_tile)
                act_grad = contract_cols(dy_all[part, :], down_tile)
                sigmoid = jax.nn.sigmoid(gate)
                silu = gate * sigmoid
                act_ref[part, :] = (silu * up).astype(BF)
                gate_grad[part, :] = (
                    act_grad * up * sigmoid * (1.0 + gate * (1.0 - sigmoid))
                ).astype(BF)
                up_grad[part, :] = (act_grad * silu).astype(BF)

        block = gather.whole.shape[:-1] + (256,)
        grads = first_pair if begin < chunk else second_pair
        first_spot = 0 if begin < chunk + 1 else 2 * (begin - chunk) // 256
        pltpu.emit_pipeline(
            body,
            grid=(tiles,),
            in_specs=[
                pl.BlockSpec(block, lambda t: (0, 0, t)),
                pl.BlockSpec(block, lambda t: (0, 0, t + tiles)),
                pl.BlockSpec((256, width), lambda t: (t + spot, 0)),
            ],
            out_specs=[
                pl.BlockSpec((length, 256), lambda t: (0, t + spot)),
                pl.BlockSpec((length, 256), lambda t: (0, t + first_spot)),
                pl.BlockSpec((length, 256), lambda t: (0, t + first_spot + tiles)),
            ],
        )(gather.whole, gather.whole, down_full, act_out, grads, grads)

    feed(first, 0, chunk)
    advance(FORWARD_PLAN[19])
    store.wait()
    store = turn(lhs, n2_turned)
    advance(FORWARD_PLAN[20])
    second.arrive()
    feed(second, chunk, chunk - tail)
    advance(FORWARD_PLAN[21])
    third.arrive()
    feed(third, 2 * chunk - tail, tail)
    store.wait()
    for gather in (qkv, out, first, second, third, down, n1, n2, dy):
        gather.finish()


def forward(hidden, upstream, weights, gains, segment):
    size = lax.axis_size("shard")
    quarter, outer = size // 4, size // 2
    piece, width = hidden.shape
    length = piece * 4
    heads = Q_HEADS // 4
    kv_heads = KV_HEADS // 4
    w_query, _, _, w_out, w_gate, _, w_down = weights
    own = w_query.shape[0]
    qkv_width = (heads + 2 * kv_heads) * HEAD_DIM
    units = w_down.shape[0] // 4 * size

    def shape(*dims, kind=BF):
        return jax.ShapeDtypeStruct(dims, kind)

    results = [
        shape(size, own, qkv_width),
        shape(quarter, *w_out.shape),
        shape(size, own, units),
        shape(size, own, units),
        shape(units, width),
        shape(length, width),
        shape(length, width),
        shape(length, width),
        shape(width // 128, 128, length),
        shape(width // 128, 128, length),
        shape(width // 128, 128, length),
        shape(length, units),
        shape(length, units),
        shape(length, units),
        shape(heads + kv_heads, length, HEAD_DIM, kind=F32),
        shape(heads + 2 * kv_heads, length, HEAD_DIM),
        shape(length, heads * HEAD_DIM),
        shape(length, 128, kind=F32),
        shape(piece, width, kind=F32),
        shape(length, HEAD_DIM, kind=F32),
        shape(length, HEAD_DIM, kind=F32),
        shape(1, length, kind=jnp.int32),
    ]
    powers = np.arange(HEAD_DIM // 2, dtype=np.float32) * np.float32(2.0) / np.float32(HEAD_DIM)
    inverse = np.float32(ROPE_BASE) ** -powers
    dma = pltpu.SemaphoreType.DMA
    return pl.pallas_call(
        functools.partial(forward_kernel, size),
        out_shape=results,
        in_specs=[VMEM] + [ANY] * 8 + [VMEM] * 6,
        out_specs=[ANY] * 14 + [VMEM] * 8,
        scratch_shapes=[
            pltpu.VMEM((length, width), BF),
            pltpu.VMEM((length, width), BF),
            pltpu.VMEM((width // 128, 128, length), BF),
            pltpu.VMEM((size, own, qkv_width), BF),
            pltpu.VMEM((quarter,) + w_out.shape, BF),
            pltpu.VMEM((own, qkv_width), BF),
            pltpu.VMEM(w_out.shape, BF),
            pltpu.VMEM((w_down.shape[0] // 4, width), BF),
            pltpu.VMEM((piece, width), BF),
            pltpu.VMEM(w_gate.shape, BF),
            pltpu.VMEM((own, units), BF),
            pltpu.VMEM((own, units), BF),
            pltpu.VMEM((2, piece, width), BF),
            pltpu.VMEM((2, piece, width), BF),
            pltpu.VMEM((2, piece, width), BF),
            pltpu.VMEM((piece, width), BF),
            pltpu.VMEM((piece, width), BF),
            dma((7, outer)),
            dma((7, outer)),
            dma((7, outer)),
            dma((7, outer)),
            dma((7, outer)),
            dma((7, outer)),
            dma((7,)),
            dma((3, 3)),
            dma((3, 3)),
            dma((3,)),
            dma((8,)),
            dma((3,)),
            dma((3,)),
            pltpu.VMEM((length, 1), jnp.int32),
            pltpu.VMEM((length, 128), F32),
            pltpu.VMEM((256, 256), BF),
        ],
        compiler_params=pltpu.CompilerParams(
            collective_id=0, has_side_effects=True, vmem_limit_bytes=VMEM_BYTES
        ),
        name="forward_gather",
    )(
        hidden,
        upstream,
        *weights,
        *gains,
        jnp.asarray(np.concatenate([inverse, inverse])[None], F32),
        segment[None],
    )


def add_rows(target, sources, step=16):
    groups, rows, _ = target.shape

    @pl.loop(0, rows // step)
    def _(index):
        part = pl.ds(pl.multiple_of(index * step, step), step)
        for group in range(groups):
            total = sources[0][group, part, :].astype(target.dtype)
            for source in sources[1:]:
                total = total + source[group, part, :].astype(target.dtype)
            target[group, part, :] = total


class RowSum:
    def __init__(self, here, give, keep, near, rising, falling, stage, total, sems):
        self.here, self.give, self.keep = here, give, keep
        self.near, self.rising, self.falling = near, rising, falling
        self.stage, self.total = stage, total
        self.ys, self.yr, self.us, self.ur, self.ds, self.dr, self.load = sems
        self.last = here.outer - 1

    def across(self, place):
        return remote(
            self.give.at[place],
            self.near.at[place],
            self.ys.at[place],
            self.yr.at[place],
            self.here.twin,
        )

    def up(self, place):
        peer = self.here.outer_peer(self.here.place + 1)
        return remote(
            self.keep.at[place], self.rising.at[place], self.us.at[place], self.ur.at[place], peer
        )

    def down(self, place):
        peer = self.here.outer_peer(self.here.place - 1)
        return remote(
            self.keep.at[place], self.falling.at[place], self.ds.at[place], self.dr.at[place], peer
        )

    def arrived(self, slot, send, receive):
        remote(slot, slot, send, receive, self.here.twin).wait_recv()

    def fold(self, distance):
        here = self.here
        above = here.place + distance
        below = here.place - distance

        def merge(place, line, receive, first):
            near = pltpu.make_async_copy(self.near.at[place], self.stage.at[0], self.load.at[0])
            self.arrived(self.near.at[place], self.ys.at[place], self.yr.at[place])
            near.start()

            @pl.when(first)
            def _():
                near.wait()
                add_rows(self.keep.at[place], [self.keep.at[place], self.stage.at[0]])

            @pl.when(jnp.logical_not(first))
            def _():
                self.arrived(line.at[place], self.us.at[0], receive.at[place])
                far = pltpu.make_async_copy(line.at[place], self.stage.at[1], self.load.at[1])
                far.start()
                near.wait()
                far.wait()
                add_rows(
                    self.keep.at[place], [self.keep.at[place], self.stage.at[0], self.stage.at[1]]
                )

        @pl.when(above <= self.last)
        def _():
            merge(above, self.rising, self.ur, here.place == 0)
            self.up(above).start()

        @pl.when(below >= 0)
        def _():
            merge(below, self.falling, self.dr, here.place == self.last)
            self.down(below).start()

    def finish(self):
        here = self.here
        place = here.place
        self.arrived(self.near.at[place], self.ys.at[place], self.yr.at[place])
        keep = self.keep.at[place]
        near = pltpu.make_async_copy(self.near.at[place], self.stage.at[0], self.load.at[0])
        low = pltpu.make_async_copy(self.rising.at[place], self.stage.at[1], self.load.at[1])
        high = pltpu.make_async_copy(self.falling.at[place], self.stage.at[1], self.load.at[1])
        near.start()

        @pl.when(place > 0)
        def _():
            self.arrived(self.rising.at[place], self.us.at[0], self.ur.at[place])
            low.start()
            low.wait()

        @pl.when(place == 0)
        def _():
            self.arrived(self.falling.at[place], self.ds.at[0], self.dr.at[place])
            high.start()
            high.wait()

        near.wait()

        @pl.when((place > 0) & (place < self.last))
        def _():
            add_rows(keep, [keep, self.stage.at[0], self.stage.at[1]])
            self.arrived(self.falling.at[place], self.ds.at[0], self.dr.at[place])
            high.start()
            high.wait()
            add_rows(self.total, [keep, self.stage.at[1]])

        @pl.when((place == 0) | (place == self.last))
        def _():
            add_rows(self.total, [keep, self.stage.at[0], self.stage.at[1]])

    def sent(self):
        for place in range(self.here.outer):
            self.across(place).wait_send()

    def settle(self):
        here = self.here
        for place in range(here.outer):

            @pl.when(place > here.place)
            def _():
                self.up(place).wait_send()

            @pl.when(place < here.place)
            def _():
                self.down(place).wait_send()


def compute_terms(here, give, keep, left, right, tiles, orders, senders):
    own = give.shape[2]
    per = 128 // (2 * own)
    step = 256
    for group, done in orders:
        spots = tiles(group)

        @pl.loop(0, give.shape[3] // step)
        def _(index):
            lane = pl.ds(pl.multiple_of(index * step, step), step)
            terms = dot(left(group), right(lane)).astype(BF)
            for spot, (zone, seq_group) in enumerate(spots):
                for sub in range(per):
                    at = spot * 128 + sub * 2 * own
                    even, odd = terms[at : at + own], terms[at + own : at + 2 * own]
                    place = zone * per + sub
                    keep[place, seq_group, :, lane] = jnp.where(here.half == 0, even, odd)
                    give[place, seq_group, :, lane] = jnp.where(here.half == 0, odd, even)

        for zone in done:
            for sub in range(per):
                for sender in senders:
                    sender.across(zone * per + sub).start()


class LineSum:
    def __init__(self, here, terms, rising, falling, stage, sems):
        self.here, self.terms, self.stage = here, terms, stage
        self.rising, self.falling = rising, falling
        self.us, self.ur, self.ds, self.dr, self.load = sems
        self.last = here.outer - 1

    def up(self, place):
        peer = self.here.outer_peer(self.here.place + 1)
        return remote(
            self.terms.at[place], self.rising.at[place], self.us.at[place], self.ur.at[place], peer
        )

    def down(self, place):
        peer = self.here.outer_peer(self.here.place - 1)
        return remote(
            self.terms.at[place], self.falling.at[place], self.ds.at[place], self.dr.at[place], peer
        )

    def merge(self, place, line, receive):
        slot = line.at[place]
        remote(slot, slot, self.us.at[0], receive.at[place], self.here.twin).wait_recv()
        copy = pltpu.make_async_copy(slot, self.stage.at[0], self.load.at[0])
        copy.start()
        copy.wait()
        add_rows(self.terms.at[place], [self.terms.at[place], self.stage.at[0]])

    def fold(self, distance):
        here = self.here
        above = here.place + distance
        below = here.place - distance

        @pl.when(above <= self.last)
        def _():
            @pl.when(here.place > 0)
            def _():
                self.merge(above, self.rising, self.ur)

            self.up(above).start()

        @pl.when(below >= 0)
        def _():
            @pl.when(here.place < self.last)
            def _():
                self.merge(below, self.falling, self.dr)

            self.down(below).start()

    def gather(self):
        place = self.here.place

        @pl.when(place > 0)
        def _():
            self.merge(place, self.rising, self.ur)

        @pl.when(place < self.last)
        def _():
            self.merge(place, self.falling, self.dr)

    def settle(self):
        here = self.here
        for place in range(here.outer):

            @pl.when(place > here.place)
            def _():
                self.up(place).wait_send()

            @pl.when(place < here.place)
            def _():
                self.down(place).wait_send()


class LineFirstSum(RowSum):
    def __init__(self, here, give, keep, near, lines, stage, total, sems, twin_sems):
        self.here, self.give, self.keep = here, give, keep
        self.near, self.stage, self.total = near, stage, total
        self.ys, self.yr, self.load = sems[0], sems[1], sems[6]
        self.lines = [
            LineSum(here, terms, rising, falling, stage, kinds[2:])
            for terms, (rising, falling), kinds in (
                (give, lines[0], twin_sems),
                (keep, lines[1], sems),
            )
        ]

    def fold(self, distance):
        for line in self.lines:
            line.fold(distance)

    def pass_on(self):
        self.lines[0].gather()
        self.across(self.here.place).start()
        self.lines[1].gather()

    def finish(self):
        place = self.here.place
        self.arrived(self.near.at[place], self.ys.at[place], self.yr.at[place])
        near = pltpu.make_async_copy(self.near.at[place], self.stage.at[0], self.load.at[0])
        near.start()
        near.wait()
        add_rows(self.total, [self.keep.at[place], self.stage.at[0]])

    def sent(self):
        self.across(self.here.place).wait_send()

    def settle(self):
        for line in self.lines:
            line.settle()


class RowSpread:
    def __init__(self, here, rows, whole, sems):
        self.here, self.rows, self.whole = here, rows, whole
        self.send_sems, self.recv_sems, self.local = sems

    def copy(self, amount):
        seq = lax.rem(self.here.seq + amount, 4)
        return remote(
            self.rows.at[seq],
            self.whole.at[self.here.seq],
            self.send_sems.at[amount - 1],
            self.recv_sems.at[amount - 1],
            {"seq": seq},
        )

    def keep(self):
        seq = self.here.seq
        return pltpu.make_async_copy(self.rows.at[seq], self.whole.at[seq], self.local)

    def send(self):
        for amount in (2, 3, 1):
            self.copy(amount).start()
        self.keep().start()

    def arrive(self):
        for amount in (1, 2, 3):
            self.copy(amount).wait_recv()
        self.keep().wait()

    def finish(self):
        for amount in (1, 2, 3):
            self.copy(amount).wait_send()


class TokenSum:
    def __init__(self, here, part, got, pair, far_got, base, sems):
        self.here, self.part, self.got, self.pair = here, part, got, pair
        self.far_got, self.base = far_got, base
        self.send_sems, self.recv_sems = sems
        self.rows = part.shape[0] // 4

    def piece(self, seq):
        return pl.ds(pl.multiple_of(seq * self.rows, self.rows), self.rows)

    def to_mate(self, index):
        here = self.here
        chip = here.chip if index else 1 - here.chip
        seq = chip * 2 + 1 - here.core
        return remote(
            self.part.at[self.piece(seq), :],
            self.got.at[index],
            self.send_sems.at[index],
            self.recv_sems.at[index],
            here.mate,
        )

    def to_far(self):
        return remote(
            self.pair, self.far_got, self.send_sems.at[2], self.recv_sems.at[2], self.here.far
        )

    def send(self):
        self.to_mate(0).start()
        self.to_mate(1).start()

    def loop(self, body):
        @pl.loop(0, self.rows // 32)
        def _(index):
            body(index * 32)

    def pass_on(self):
        self.to_mate(0).wait_recv()
        begin = self.here.far_seq * self.rows

        def body(at):
            part = pl.ds(pl.multiple_of(at, 32), 32)
            source = pl.ds(pl.multiple_of(begin + at, 32), 32)
            total = self.part[source, :].astype(F32) + self.got[0, part, :].astype(F32)
            self.pair[part, :] = total.astype(BF)

        self.loop(body)
        self.to_far().start()

    def add_near(self):
        self.to_mate(1).wait_recv()
        begin = self.here.seq * self.rows

        def body(at):
            part = pl.ds(pl.multiple_of(at, 32), 32)
            source = pl.ds(pl.multiple_of(begin + at, 32), 32)
            self.base[part, :] += self.part[source, :].astype(F32) + self.got[1, part, :].astype(F32)

        self.loop(body)
        self.to_mate(0).wait_send()
        self.to_mate(1).wait_send()

    def add_far(self):
        self.to_far().wait_recv()

        def body(at):
            part = pl.ds(pl.multiple_of(at, 32), 32)
            self.base[part, :] += self.far_got[part, :].astype(F32)

        self.loop(body)
        self.to_far().wait_send()


class GainSum:
    def __init__(self, here, own, seq_got, middle, shard_got, sems):
        self.here, self.own, self.middle = here, own, middle
        self.seq_got, self.shard_got = seq_got, shard_got
        self.seq_send, self.seq_recv, self.shard_send, self.shard_recv = sems

    def over_seq(self, amount):
        here = self.here
        return remote(
            self.own,
            self.seq_got.at[here.seq],
            self.seq_send.at[amount - 1],
            self.seq_recv.at[amount - 1],
            {"seq": lax.rem(here.seq + amount, 4)},
        )

    def over_shard(self, amount):
        here = self.here
        return remote(
            self.middle,
            self.shard_got.at[here.shard],
            self.shard_send.at[amount - 1],
            self.shard_recv.at[amount - 1],
            {"shard": lax.rem(here.shard + amount, here.size)},
        )

    def start(self):
        for amount in range(1, 4):
            self.over_seq(amount).start()
        self.seq_got[self.here.seq] = self.own[...]

    def turn(self):
        for amount in range(1, 4):
            self.over_seq(amount).wait()
        total = self.seq_got[0]
        for index in range(1, 4):
            total = total + self.seq_got[index]
        self.middle[...] = total
        for amount in range(1, self.here.size):
            self.over_shard(amount).start()
        self.shard_got[self.here.shard] = total

    def finish(self):
        for amount in range(1, self.here.size):
            self.over_shard(amount).wait()
        total = self.shard_got[0]
        for index in range(1, self.here.size):
            total = total + self.shard_got[index]
        return total


PLAN = (
    (("down_a", 3),),
    (("down_a", 2), ("down_b", 3),),
    (("down_a", 1), ("down_b", 2),),
    (),
    (),
    (("first", 3), ("down_b", 1),),
    (("first", 2), ("down_b", "finish"),),
    (("second", 3), ("first", 1),),
    (("second", 2),),
    (),
    (("first", "finish"),),
    (("out", 3), ("second", 1),),
    (),
    (("out", 2), ("query", 3), ("down_a", "pass"), ("key", 3), ("out", 1),),
    (("query", 2), ("key", 2), ("second", "finish"), ("out", "finish"), ("query", 1), ("key", 1),),
    (("query", "finish"), ("key", "finish"),),
    (("down_a", "finish"),),
)


def backward_kernel(
    size,
    n1_hbm,
    dy_hbm,
    n2_hbm,
    act_hbm,
    first_hbm,
    second_hbm,
    proj_hbm,
    heads_ref,
    mixed_ref,
    lse_ref,
    middle_hbm,
    hidden_hbm,
    dy_own,
    qkv_full,
    out_full,
    first_full,
    second_full,
    down_full,
    attn_gain_ref,
    mlp_gain_ref,
    query_gain_ref,
    key_gain_ref,
    cos_ref,
    sin_ref,
    start_ref,
    grad_in,
    gains_out,
    grad_out,
    hidden_out,
    down_rows,
    first_rows,
    second_rows,
    qkv_rows,
    da_hbm,
    near_mlp,
    rising_mlp,
    falling_mlp,
    rising_twin,
    falling_twin,
    near_qkv,
    rising_qkv,
    falling_qkv,
    near_out,
    rising_out,
    falling_out,
    lhs,
    turned,
    first_r,
    second_r,
    give,
    keep,
    give_out,
    keep_out,
    stage,
    stage_out,
    dout_ref,
    da_own,
    got,
    far_got,
    pair,
    middle_grad,
    proj_buf,
    eye,
    keys_turned,
    lse_t,
    delta,
    delta_t,
    dk_sum,
    dv_sum,
    gain_row,
    gain_seq,
    gain_middle,
    gain_shard,
    ys,
    yr,
    us,
    ur,
    ds,
    dr,
    fold_load,
    spread_s,
    spread_r,
    spread_l,
    sum_s,
    sum_r,
    ts,
    tr,
    token_local,
    gss,
    gsr,
    gts,
    gtr,
    load_sem,
    credit,
):
    here = Place(size)
    length, width = lhs.shape
    rows = length // 4
    units = first_r.shape[1]
    chunk = units // 2
    ff_part = units // size
    heads = mixed_ref.shape[1] // HEAD_DIM
    kv_heads = heads // 2
    qkv_width = qkv_full.shape[2]
    last = here.outer - 1
    scale = HEAD_DIM ** (-0.5)

    def load(source, target, index):
        copy = pltpu.make_async_copy(source, target, load_sem.at[index])
        copy.start()
        return copy

    def sems(index):
        return tuple(kind.at[index] for kind in (ys, yr, us, ur, ds, dr, fold_load))

    thin = qkv_width // 2
    cut = units * 2 // 3
    lanes = {
        "down_a": slice(0, cut),
        "down_b": slice(cut, units),
        "query": slice(0, thin),
        "key": slice(thin, 2 * thin),
    }

    def part(ref, name):
        return ref.at[:, :, :, lanes[name]]

    def row_sum(index, give_ref, keep_ref, near, rising, falling, stage_ref, total):
        return RowSum(
            here, give_ref, keep_ref, near, rising, falling, stage_ref, total, sems(index)
        )

    jobs = {
        "down_a": LineFirstSum(
            here,
            part(give.at[2], "down_a"),
            part(keep.at[0], "down_a"),
            part(near_mlp.at[0], "down_a"),
            (
                (rising_twin, falling_twin),
                (part(rising_mlp.at[0], "down_a"), part(falling_mlp.at[0], "down_a")),
            ),
            part(stage, "down_a"),
            keep.at[0, here.place, :, :, lanes["down_a"]],
            sems(0),
            sems(5),
        ),
        "down_b": row_sum(
            6,
            part(give.at[2], "down_b"),
            part(keep.at[0], "down_b"),
            part(near_mlp.at[0], "down_b"),
            part(rising_mlp.at[0], "down_b"),
            part(falling_mlp.at[0], "down_b"),
            part(stage, "down_b"),
            keep.at[0, here.place, :, :, lanes["down_b"]],
        ),
        "out": row_sum(
            4, give_out, keep_out, near_out, rising_out, falling_out, stage_out, grad_out
        ),
    }
    for index, name in ((1, "first"), (2, "second")):
        jobs[name] = row_sum(
            index,
            give.at[2 - index],
            keep.at[index],
            near_mlp.at[index],
            rising_mlp.at[index],
            falling_mlp.at[index],
            stage,
            keep.at[index, here.place],
        )
    for index, name in ((3, "query"), (7, "key")):
        jobs[name] = row_sum(
            index,
            part(give.at[1], name),
            part(second_r, name),
            part(near_qkv, name),
            part(rising_qkv, name),
            part(falling_qkv, name),
            part(stage, name),
            second_r.at[here.place, :, :, lanes[name]],
        )
    zones = width // 512

    def zone_at(index):
        zone = here.place // (here.outer // zones)
        return (
            3 * (1 - zone // 2),
            lax.rem(2 + 3 * zone, 5),
            1 + lax.rem(zone, 2),
            zone,
        )[index]

    zone_order = [zone_at(index) for index in range(zones)]
    by_zone = [(zone, (zone,)) for zone in zone_order]

    spreads = {}
    for index, (name, whole) in enumerate(
        (
            ("down_a", down_rows.at[:, :, lanes["down_a"]]),
            ("down_b", down_rows.at[:, :, lanes["down_b"]]),
            ("first", first_rows),
            ("second", second_rows),
            ("query", qkv_rows.at[:, :, lanes["query"]]),
            ("key", qkv_rows.at[:, :, lanes["key"]]),
        )
    ):
        kinds = (spread_s.at[index], spread_r.at[index], spread_l.at[index])
        spreads[name] = RowSpread(here, jobs[name].total, whole, kinds)

    def token_sum(index, base):
        return TokenSum(
            here, lhs, got, pair, far_got, base, (sum_s.at[index], sum_r.at[index])
        )

    sum_mlp = token_sum(0, middle_grad)
    sum_hidden = token_sum(1, grad_in)
    sum_attn = token_sum(2, grad_in)
    da = TokenGather(here, da_own, da_hbm, (ts, tr, token_local.at[0]))

    def model_tiles(group):
        return [(group, seq_group) for seq_group in range(4)]

    def first_columns(lane):
        return first_r[:, lane]

    def model_left(group):
        return turned[pl.ds(group * 4, 4)].reshape(512, length)

    def advance(steps):
        for name, step in steps:
            job = jobs[name]
            if step == "pass":
                job.pass_on()
            elif step == "finish":
                job.finish()
                if name in spreads:
                    spreads[name].send()
            else:
                for distance in range(last * step // 3, last * (step - 1) // 3, -1):
                    job.fold(distance)

    load_turned = load(dy_hbm, turned, 0)
    load_act = load(act_hbm, first_r, 1)
    load_middle = load(middle_hbm, grad_in, 2)
    load_dy = load(dy_own, da_own, 4)
    load_second = load(second_hbm, second_r, 3)
    eye[...] = identity(HEAD_DIM)
    here.greet(wide=True)
    load_turned.wait()
    load_act.wait()
    def model_terms(give_ref, keep_ref, right, senders):
        compute_terms(
            here, give_ref, keep_ref, model_left, right, model_tiles, by_zone, senders
        )

    model_terms(give.at[2], keep.at[0], first_columns, [jobs["down_b"]])
    advance(PLAN[0])
    load_turned = load(n2_hbm, turned, 0)
    load_first = load(first_hbm, first_r, 1)
    load_first.wait()
    load_second.wait()

    own = width // size
    slabs = 256 // own

    def dn2_body(first_w, second_w):
        lane = pl.ds(pl.multiple_of(pl.program_id(0) * 256, 256), 256)
        first_tile = first_w[...].reshape(256, units)
        second_tile = second_w[...].reshape(256, units)

        @pl.loop(0, 4)
        def _(index):
            part = pl.ds(pl.multiple_of(index * rows, rows), rows)
            total = contract_cols(first_r[part, :], first_tile)
            blocks = pl.ds(index * (here.outer // 4), here.outer // 4)
            second_rows = second_r[blocks].reshape(rows, units)
            total = total + contract_cols(second_rows, second_tile)
            lhs[part, lane] = total.astype(BF)

    slab = pl.BlockSpec((slabs, own, units), lambda t: (t, 0, 0))
    pltpu.emit_pipeline(dn2_body, grid=(width // 256,), in_specs=[slab, slab])(
        first_full, second_full
    )
    sum_mlp.send()
    middle_grad[...] = jnp.zeros_like(middle_grad)
    load_turned.wait()
    advance(PLAN[1])
    sum_mlp.pass_on()
    sum_mlp.add_near()
    model_terms(give.at[1], keep.at[1], first_columns, [jobs["first"]])
    load_act = load(act_hbm, first_r, 1)
    advance(PLAN[2])
    sum_mlp.add_far()

    load_middle.wait()
    load_dy.wait()
    gain_row[...] = jnp.zeros_like(gain_row)
    mlp_lane = slice(2 * HEAD_DIM, 2 * HEAD_DIM + width)
    attn_lane = slice(2 * HEAD_DIM + width, 2 * HEAD_DIM + 2 * width)
    narrow = 16

    @pl.loop(0, rows // narrow)
    def _(index):
        part = pl.ds(pl.multiple_of(index * narrow, narrow), narrow)
        values = grad_in[part, :]
        scales = lax.rsqrt(jnp.mean(values * values, axis=-1, keepdims=True) + EPSILON)
        normed = values * scales
        update = middle_grad[part, :]
        gain_row[:, mlp_lane] += jnp.sum(update * normed, axis=0, keepdims=True)
        upper = update * mlp_gain_ref[...]
        inner = jnp.mean(upper * normed, axis=-1, keepdims=True)
        grad = da_own[part, :].astype(F32) + scales * (upper - normed * inner)
        middle_grad[part, :] = grad
        da_own[part, :] = grad.astype(BF)

    da.send()
    advance(PLAN[3])
    model_terms(
        give.at[0],
        keep.at[2],
        lambda lane: second_r[:, :, :, lane].reshape(length, -1),
        [jobs["second"]],
    )
    advance(PLAN[4])

    def hidden_body(weight):
        lane = pl.ds(pl.multiple_of(pl.program_id(0) * 256, 256), 256)
        tile = weight[...]

        @pl.loop(0, 4)
        def _(index):
            part = pl.ds(pl.multiple_of(index * rows, rows), rows)
            lhs[part, lane] = dot(first_r[part, :], tile).astype(BF)

    load_act.wait()
    pltpu.emit_pipeline(
        hidden_body,
        grid=(width // 256,),
        in_specs=[pl.BlockSpec((units, 256), lambda t: (0, t))],
    )(down_full)
    da.mate_arrived()
    sum_hidden.send()
    da.forward()
    advance(PLAN[5])
    sum_hidden.pass_on()
    sum_hidden.add_near()
    advance(PLAN[6])
    da.rest_arrived()
    da.finish()
    load_lhs = load(da_hbm, lhs, 0)
    load_own = load(hidden_hbm, da_own, 2)
    load_lhs.wait()

    def dout_body(weight):
        lane = pl.ds(pl.multiple_of(pl.program_id(0) * 256, 256), 256)
        tile = weight[...].reshape(256, width)

        @pl.loop(0, 4)
        def _(index):
            part = pl.ds(pl.multiple_of(index * rows, rows), rows)
            dout_ref[part, lane] = contract_cols(lhs[part, :], tile).astype(BF)

    out_blocks, out_rows = out_full.shape[:2]
    pltpu.emit_pipeline(
        dout_body,
        grid=(out_blocks * out_rows // 256,),
        in_specs=[pl.BlockSpec((256 // out_rows, out_rows, width), lambda t: (t, 0, 0))],
    )(out_full)

    for head in range(heads):
        lane = slice(head * HEAD_DIM, (head + 1) * HEAD_DIM)
        turned[head] = contract_cols(eye[...], mixed_ref[:, lane]).astype(BF)
    compute_terms(
        here,
        give_out,
        keep_out,
        lambda group: turned[0:heads].reshape(heads * HEAD_DIM, length),
        lambda lane: lhs[:, lane],
        lambda group: [(zone, 0) for zone in range(heads)],
        [(0, zone_order)],
        [jobs["out"]],
    )
    load_turned = load(n1_hbm, turned, 0)
    sum_hidden.add_far()
    for index, peer in enumerate((here.mate, here.far)):
        pl.semaphore_signal(credit.at[index], inc=1, device_id=peer, device_id_type=MESH)

    @pl.loop(0, rows // 32)
    def _(index):
        part = pl.ds(pl.multiple_of(index * 32, 32), 32)
        pair[part, :] = grad_in[part, :].astype(BF)

    store_hidden = load(pair, hidden_out, 1)
    advance(PLAN[7])

    lse_t[...] = lse_ref[...].T[0:8]
    delta[...] = jnp.zeros_like(delta)
    for head in range(heads):
        lane = slice(head * HEAD_DIM, (head + 1) * HEAD_DIM)
        terms = dout_ref[:, lane].astype(F32) * mixed_ref[:, lane].astype(F32)
        delta[:, head : head + 1] = jnp.sum(terms, axis=-1, keepdims=True)
    delta_t[...] = delta[...].T[0:8]
    def through_norm(grad, head, part, gain_ref, which):
        proj = proj_buf[part, :]
        scales = lax.rsqrt(jnp.mean(proj * proj, axis=-1, keepdims=True) + EPSILON)
        normed = proj * scales
        grad = grad.astype(F32)
        upper = grad * cos_ref[part, :] - pltpu.roll(grad, HEAD_DIM // 2, 1) * sin_ref[part, :]
        gain_row[:, which * HEAD_DIM : (which + 1) * HEAD_DIM] += jnp.sum(
            upper * normed, axis=0, keepdims=True
        )
        upper = upper * gain_ref[...]
        inner = jnp.mean(upper * normed, axis=-1, keepdims=True)
        result = (scales * (upper - normed * inner)).astype(BF)
        first_r[part, head * HEAD_DIM : (head + 1) * HEAD_DIM] = result

    for head in range(heads):
        pair_head = head // 2
        load_proj = load(proj_hbm.at[head], proj_buf, 4)
        if head % 2 == 0:
            dk_sum[...] = jnp.zeros_like(dk_sum)
            dv_sum[...] = jnp.zeros_like(dv_sum)
            keys_turned[...] = contract_cols(eye[...], heads_ref[heads + pair_head]).astype(BF)
        for block in range(4):
            end = (block + 1) * rows
            part = pl.ds(block * rows, rows)
            queries = heads_ref[head, part, :]
            keys = heads_ref[heads + pair_head, 0:end, :]
            values = heads_ref[heads + kv_heads + pair_head, 0:end, :]
            out_grad = dout_ref[part, head * HEAD_DIM : (head + 1) * HEAD_DIM]
            scores = contract_cols(keys, queries)
            key_place = lax.broadcasted_iota(jnp.int32, (end, rows), 0)
            query_place = lax.broadcasted_iota(jnp.int32, (end, rows), 1) + block * rows
            allowed = (key_place >= start_ref[:, part]) & (key_place <= query_place)
            weights = jnp.exp(scores * scale - lse_t[head : head + 1, part])
            weights = jnp.where(allowed, weights, 0.0)
            weight_grad = contract_cols(values, out_grad)
            inner = delta_t[head : head + 1, part]
            score_grad = (weights * (weight_grad - inner)).astype(BF)
            dk_sum[0:end, :] += dot(score_grad, queries) * scale
            dv_sum[0:end, :] += dot(weights.astype(BF), out_grad)
            query_grad = dot(keys_turned[:, 0:end], score_grad).T
            query_grad = (query_grad * scale).astype(BF)
            if block == 0:
                load_proj.wait()
            through_norm(query_grad, head, part, query_gain_ref, 0)
        if head % 2:
            key = heads + pair_head
            value_at = (heads + kv_heads + pair_head) * HEAD_DIM
            load(proj_hbm.at[key], proj_buf, 4).wait()

            @pl.loop(0, 4)
            def _(index):
                part = pl.ds(pl.multiple_of(index * rows, rows), rows)
                through_norm(dk_sum[part, :].astype(BF), key, part, key_gain_ref, 1)
                first_r[part, value_at : value_at + HEAD_DIM] = dv_sum[part, :].astype(BF)

        advance(PLAN[8 + head])

    load_turned.wait()
    jobs["first"].sent()
    store_hidden.wait()
    proj_grads = first_r.at[:, 0:qkv_width]
    model_terms(
        give.at[1, :, :, :, 0:qkv_width],
        second_r.at[:, :, :, 0:qkv_width],
        first_columns,
        [jobs["query"], jobs["key"]],
    )
    advance(PLAN[12])

    def dn1_body(weight):
        lane = pl.ds(pl.multiple_of(pl.program_id(0) * 256, 256), 256)
        tile = weight[...].reshape(256, qkv_width)

        @pl.loop(0, 4)
        def _(index):
            part = pl.ds(pl.multiple_of(index * rows, rows), rows)
            lhs[part, lane] = contract_cols(proj_grads[part, :], tile).astype(BF)

    pltpu.emit_pipeline(
        dn1_body,
        grid=(width // 256,),
        in_specs=[pl.BlockSpec((slabs, own, qkv_width), lambda t: (t, 0, 0))],
    )(qkv_full)
    grad_in[...] = jnp.zeros_like(grad_in)
    pl.semaphore_wait(credit.at[0], 1)
    pl.semaphore_wait(credit.at[1], 1)
    sum_attn.send()
    advance(PLAN[13])
    sum_attn.pass_on()
    sum_attn.add_near()
    advance(PLAN[14])
    sum_attn.add_far()
    load_own.wait()

    @pl.loop(0, rows // narrow)
    def _(index):
        part = pl.ds(pl.multiple_of(index * narrow, narrow), narrow)
        values = da_own[part, :].astype(F32)
        scales = lax.rsqrt(jnp.mean(values * values, axis=-1, keepdims=True) + EPSILON)
        normed = values * scales
        update = grad_in[part, :]
        gain_row[:, attn_lane] += jnp.sum(update * normed, axis=0, keepdims=True)
        upper = update * attn_gain_ref[...]
        inner = jnp.mean(upper * normed, axis=-1, keepdims=True)
        grad_in[part, :] = middle_grad[part, :] + scales * (upper - normed * inner)

    gain_sum = GainSum(here, gain_row, gain_seq, gain_middle, gain_shard, (gss, gsr, gts, gtr))
    gain_sum.start()
    advance(PLAN[15])
    gain_sum.turn()
    advance(PLAN[16])
    gains_out[...] = gain_sum.finish()
    for spread_rows in spreads.values():
        spread_rows.arrive()
    for name, job in jobs.items():
        if name != "first":
            job.sent()
    for job in jobs.values():
        job.settle()
    for job in spreads.values():
        job.finish()


def backward(saved, weights, own, gains, tables, starts):
    size = lax.axis_size("shard")
    outer = size // 2
    (n1, dy, n2, act, first, second, proj, heads_all, mixed, lse, middle) = saved
    length, width = heads_all.shape[1], middle.shape[1]
    piece = length // 4
    units = act.shape[1]
    qkv_width = weights[0].shape[2]
    rows = width // (4 * size)
    q_width = mixed.shape[1]

    def shape(*dims, kind=BF):
        return jax.ShapeDtypeStruct(dims, kind)

    results = [
        shape(piece, width, kind=F32),
        shape(1, 2 * width + 2 * HEAD_DIM, kind=F32),
        shape(1, rows, width, kind=F32),
        shape(piece, width),
        shape(4, rows, units),
        shape(4, rows, units),
        shape(4, rows, units),
        shape(4, rows, qkv_width),
        shape(length, width),
    ]
    results += [shape(3, outer, 4, rows, units)] * 3
    results += [shape(outer, 4, rows, units * 2 // 3)] * 2
    results += [shape(outer, 4, rows, qkv_width)] * 3
    results += [shape(outer, 1, rows, width)] * 3
    dma = pltpu.SemaphoreType.DMA
    vmem = pltpu.VMEM
    return pl.pallas_call(
        functools.partial(backward_kernel, size),
        out_shape=results,
        in_specs=[ANY] * 7 + [VMEM] * 3 + [ANY] * 8 + [VMEM] * 7,
        out_specs=[VMEM] * 3 + [ANY] * (len(results) - 3),
        scratch_shapes=[
            vmem((length, width), BF),
            vmem((width // 128, 128, length), BF),
            vmem((length, units), BF),
            vmem((outer, 4, rows, units), BF),
            vmem((3, outer, 4, rows, units), BF),
            vmem((3, outer, 4, rows, units), BF),
            vmem((outer, 1, rows, width), BF),
            vmem((outer, 1, rows, width), BF),
            vmem((2, 4, rows, units), BF),
            vmem((2, 1, rows, width), BF),
            vmem((length, q_width), BF),
            vmem((piece, width), BF),
            vmem((2, piece, width), BF),
            vmem((piece, width), BF),
            vmem((piece, width), BF),
            vmem((piece, width), F32),
            vmem((length, HEAD_DIM), F32),
            vmem((HEAD_DIM, HEAD_DIM), BF),
            vmem((HEAD_DIM, length), BF),
            vmem((8, length), F32),
            vmem((length, 128), F32),
            vmem((8, length), F32),
            vmem((length, HEAD_DIM), F32),
            vmem((length, HEAD_DIM), F32),
            vmem((1, 2 * width + 2 * HEAD_DIM), F32),
            vmem((4, 1, 2 * width + 2 * HEAD_DIM), F32),
            vmem((1, 2 * width + 2 * HEAD_DIM), F32),
            vmem((size, 1, 2 * width + 2 * HEAD_DIM), F32),
            dma((8, outer)),
            dma((8, outer)),
            dma((8, outer)),
            dma((8, outer)),
            dma((8, outer)),
            dma((8, outer)),
            dma((8, 3)),
            dma((6, 3)),
            dma((6, 3)),
            dma((6,)),
            dma((3, 3)),
            dma((3, 3)),
            dma((3,)),
            dma((3,)),
            dma((1,)),
            dma((3,)),
            dma((3,)),
            dma((size - 1,)),
            dma((size - 1,)),
            dma((5,)),
            pltpu.SemaphoreType.REGULAR((2,)),
        ],
        compiler_params=pltpu.CompilerParams(
            collective_id=1, has_side_effects=True, vmem_limit_bytes=VMEM_BYTES
        ),
        name="backward_sums",
    )(
        n1,
        dy,
        n2,
        act,
        first,
        second.reshape(outer, 4, rows, units),
        proj,
        heads_all,
        mixed,
        lse,
        middle,
        *own,
        *weights,
        *gains,
        *tables,
        starts,
    )


def finish_kernel(
    size,
    grad_in,
    gains,
    grad_out,
    hidden_out,
    down_rows,
    first_rows,
    second_rows,
    qkv_rows,
    grad_in_out,
    grad_out_out,
    hidden_out_out,
    grad_query,
    grad_key,
    grad_value,
    grad_gate,
    grad_up,
    grad_down,
    attn_gain,
    mlp_gain,
    query_gain,
    key_gain,
    grad_in_buf,
    grad_out_buf,
    hidden_buf,
    down_buf,
    first_buf,
    second_buf,
    qkv_buf,
    query_buf,
    key_buf,
    value_buf,
    gate_buf,
    up_buf,
    wide_buf,
    load_sems,
    store_sems,
):
    units = down_buf.shape[2]
    chunk = units // 2
    ff_part = units // size
    most, tail = chunk - 256, 256
    stores = []

    def load(source, target, index):
        copy = pltpu.make_async_copy(source, target, load_sems.at[index])
        copy.start()
        return copy

    def store(source, target):
        copy = pltpu.make_async_copy(source, target, store_sems.at[len(stores)])
        copy.start()
        stores.append(copy)

    loads = [
        load(source, target, index)
        for index, (source, target) in enumerate(
            (
                (down_rows, down_buf),
                (first_rows, first_buf),
                (second_rows, second_buf),
                (qkv_rows, qkv_buf),
                (grad_in, grad_in_buf),
                (hidden_out, hidden_buf),
                (grad_out, grad_out_buf),
            )
        )
    ]

    def place(read, target):
        @pl.loop(0, target.shape[0] // 16)
        def _(index):
            part = pl.ds(pl.multiple_of(index * 16, 16), 16)
            values = [read(seq, part).astype(F32) for seq in range(4)]
            for begin in range(0, size, size // 8):
                pieces = [
                    values[seq][:, block * ff_part : (block + 1) * ff_part]
                    for block in range(begin, begin + size // 8)
                    for seq in range(4)
                ]
                lane = slice(begin * 4 * ff_part, (begin + size // 8) * 4 * ff_part)
                target[part, lane] = jnp.concatenate(pieces, axis=1)

    def side(index):
        at = 2 * most + index * tail

        def read(seq, part):
            return jnp.concatenate(
                [
                    first_buf[seq, part, index * chunk : (index + 1) * chunk],
                    second_buf[seq, part, index * most : (index + 1) * most],
                    second_buf[seq, part, at : at + tail],
                ],
                axis=1,
            )

        return read

    loads[0].wait()
    place(lambda seq, part: down_buf[seq, part, :], wide_buf)
    store(wide_buf, grad_down)
    loads[1].wait()
    loads[2].wait()
    place(side(0), gate_buf)
    store(gate_buf, grad_gate)
    place(side(1), up_buf)
    store(up_buf, grad_up)
    loads[4].wait()
    store(grad_in_buf, grad_in_out)
    loads[5].wait()
    store(hidden_buf, hidden_out_out)
    loads[6].wait()
    store(grad_out_buf, grad_out_out)
    loads[3].wait()
    at = 0
    for buf, target in ((query_buf, grad_query), (key_buf, grad_key), (value_buf, grad_value)):
        count = buf.shape[1] // 4
        for seq in range(4):
            buf[:, seq * count : (seq + 1) * count] = qkv_buf[seq, :, at : at + count].astype(F32)
        at += count
        store(buf, target)
    at = 0
    for target in (query_gain, key_gain, mlp_gain, attn_gain):
        target[...] = gains[:, at : at + target.shape[1]]
        at += target.shape[1]
    for copy in stores:
        copy.wait()


def finish(grad_in, gains, grad_out, hidden_out, down_rows, first_rows, second_rows, qkv_rows):
    size = lax.axis_size("shard")
    piece, width = grad_in.shape
    rows, units = down_rows.shape[1:]
    qkv_width = qkv_rows.shape[2]

    def shape(*dims, kind=F32):
        return jax.ShapeDtypeStruct(dims, kind)

    results = [
        shape(piece, width),
        shape(1, rows, width),
        shape(piece, width, kind=BF),
        shape(rows, 2 * qkv_width),
        shape(rows, qkv_width),
        shape(rows, qkv_width),
        shape(rows, 4 * units),
        shape(rows, 4 * units),
        shape(rows, 4 * units),
        shape(1, width),
        shape(1, width),
        shape(1, HEAD_DIM),
        shape(1, HEAD_DIM),
    ]
    return pl.pallas_call(
        functools.partial(finish_kernel, size),
        out_shape=results,
        in_specs=[ANY, VMEM] + [ANY] * 6,
        out_specs=[ANY] * 9 + [VMEM] * 4,
        scratch_shapes=[
            pltpu.VMEM((piece, width), F32),
            pltpu.VMEM((1, rows, width), F32),
            pltpu.VMEM((piece, width), BF),
            pltpu.VMEM((4, rows, units), BF),
            pltpu.VMEM((4, rows, units), BF),
            pltpu.VMEM((4, rows, units), BF),
            pltpu.VMEM((4, rows, qkv_width), BF),
            pltpu.VMEM((rows, 2 * qkv_width), F32),
            pltpu.VMEM((rows, qkv_width), F32),
            pltpu.VMEM((rows, qkv_width), F32),
            pltpu.VMEM((rows, 4 * units), F32),
            pltpu.VMEM((rows, 4 * units), F32),
            pltpu.VMEM((rows, 4 * units), F32),
            pltpu.SemaphoreType.DMA((7,)),
            pltpu.SemaphoreType.DMA((9,)),
        ],
        compiler_params=pltpu.CompilerParams(vmem_limit_bytes=VMEM_BYTES),
        name="finish",
    )(grad_in, gains, grad_out, hidden_out, down_rows, first_rows, second_rows, qkv_rows)


def local(
    hidden_in,
    segment_ids,
    norm_attn_gain,
    w_query,
    w_key,
    w_value,
    query_gain,
    key_gain,
    w_out,
    norm_mlp_gain,
    w_gate,
    w_up,
    w_down,
    out_cotangent,
):
    segment = segment_ids[0]
    gains = (norm_attn_gain[None], norm_mlp_gain[None], query_gain[None], key_gain[None])
    results = forward(
        hidden_in[0],
        out_cotangent[0],
        (w_query, w_key, w_value, w_out, w_gate, w_up, w_down),
        gains,
        segment,
    )
    (
        grad_in,
        grad_out,
        hidden_out,
        grad_query,
        grad_key,
        grad_value,
        grad_gate,
        grad_up,
        grad_down,
        attn_gain,
        mlp_gain,
        query_grad,
        key_grad,
    ) = finish(
        *backward(
            results[8:19],
            results[:5],
            (hidden_in[0], out_cotangent[0]),
            gains,
            results[19:21],
            results[21],
        )[:8]
    )
    return (
        hidden_out[None],
        grad_in[None],
        attn_gain[0],
        grad_query,
        grad_key,
        grad_value,
        query_grad[0],
        key_grad[0],
        grad_out[0],
        mlp_gain[0],
        grad_gate,
        grad_up,
        grad_down.T,
    )


def solution(mesh):
    return jax.shard_map(
        local,
        mesh=mesh,
        in_specs=(
            P("shard", "seq", None),
            P("shard", None),
            P(),
            P("shard", None),
            P("shard", None),
            P("shard", None),
            P(),
            P(),
            P("shard", None),
            P(),
            P("shard", None),
            P("shard", None),
            P("shard", None),
            P("shard", "seq", None),
        ),
        out_specs=(
            P("shard", "seq", None),
            P("shard", "seq", None),
            P(),
            P(("seq", "shard"), None),
            P(("seq", "shard"), None),
            P(("seq", "shard"), None),
            P(),
            P(),
            P(("seq", "shard"), None),
            P(),
            P(("seq", "shard"), None),
            P(("seq", "shard"), None),
            P(None, ("seq", "shard")),
        ),
        check_vma=False,
    )
```

```python
import functools

import jax
import jax.numpy as jnp
import numpy as np
from jax import lax
from jax.experimental import pallas as pl
from jax.experimental.pallas import tpu as pltpu
from jax.sharding import PartitionSpec as P

Q_HEADS = 16
KV_HEADS = 8
HEAD_DIM = 128
EPSILON = 1e-06
ROPE_BASE = 1000000.0
NEGATIVE = -1e30
BF = jnp.bfloat16
F32 = jnp.float32
MESH = pl.DeviceIdType.MESH
ANY = pl.BlockSpec(memory_space=pl.ANY)
VMEM = pl.BlockSpec(memory_space=pltpu.VMEM)
VMEM_BYTES = 62 * 1024 * 1024


def dot(left, right):
    return jnp.dot(left, right, preferred_element_type=F32)


def contract_cols(left, right):
    return lax.dot_general(left, right, (((1,), (1,)), ((), ())), preferred_element_type=F32)


class Place:
    def __init__(self, size):
        self.size = size
        self.outer = size // 2
        self.quarter = size // 4
        self.seq = lax.axis_index("seq")
        self.shard = lax.axis_index("shard")
        self.chip = self.seq // 2
        self.core = lax.rem(self.seq, 2)
        self.place = self.shard // 2
        self.half = lax.rem(self.shard, 2)
        self.far_seq = lax.rem(self.seq + 2, 4)
        self.mate_seq = self.chip * 2 + 1 - self.core
        self.far = {"seq": self.far_seq}
        self.mate = {"seq": self.mate_seq}
        self.twin_shard = self.place * 2 + 1 - self.half
        self.twin = {"shard": self.twin_shard}

    def outer_peer(self, place):
        return {"shard": place * 2 + self.half}

    def greet(self, wide=False):
        barrier = pltpu.get_barrier_semaphore()
        last = self.outer - 1

        def signal(peer):
            pl.semaphore_signal(barrier, inc=1, device_id=peer, device_id_type=MESH)

        signal(self.far)
        signal(self.mate)
        if wide:
            signal({"seq": 3 - self.seq})
            for amount in range(1, self.size):
                signal({"shard": lax.rem(self.shard + amount, self.size)})
            pl.semaphore_wait(barrier, 2 + self.size)
            return
        signal(self.twin)

        @pl.when(self.place < last)
        def _():
            signal(self.outer_peer(self.place + 1))

        @pl.when(self.place > 0)
        def _():
            signal(self.outer_peer(self.place - 1))

        inner = ((self.place > 0) & (self.place < last)).astype(jnp.int32)
        pl.semaphore_wait(barrier, 4 + inner)


def remote(source, target, send, receive, peer):
    return pltpu.make_async_remote_copy(
        src_ref=source,
        dst_ref=target,
        send_sem=send,
        recv_sem=receive,
        device_id=peer,
        device_id_type=MESH,
    )


class LineGather:
    def __init__(self, here, own, slot, sems):
        self.here, self.own, self.slot = here, own, slot
        self.us, self.ur, self.ds, self.dr = sems
        self.last = here.outer - 1

    def up(self, distance):
        here = self.here
        slot = self.slot(here.place - distance)
        source = slot if distance else self.own
        peer = here.outer_peer(here.place + 1)
        return remote(source, slot, self.us.at[distance], self.ur.at[distance], peer)

    def down(self, distance):
        here = self.here
        slot = self.slot(here.place + distance)
        source = slot if distance else self.own
        peer = here.outer_peer(here.place - 1)
        return remote(source, slot, self.ds.at[distance], self.dr.at[distance], peer)

    def send(self):
        here = self.here

        @pl.when(here.place < self.last)
        def _():
            self.up(0).start()

        @pl.when(here.place > 0)
        def _():
            self.down(0).start()

    def step(self, distance, arrived=lambda place: None):
        here = self.here
        below = here.place - 1 - distance
        above = here.place + 1 + distance

        @pl.when(below >= 0)
        def _():
            slot = self.slot(below)
            remote(slot, slot, self.us.at[0], self.ur.at[distance], here.twin).wait_recv()

            @pl.when(here.place < self.last)
            def _():
                self.up(distance + 1).start()

            arrived(below)

        @pl.when(above <= self.last)
        def _():
            slot = self.slot(above)
            remote(slot, slot, self.ds.at[0], self.dr.at[distance], here.twin).wait_recv()

            @pl.when(here.place > 0)
            def _():
                self.down(distance + 1).start()

            arrived(above)

    def finish(self):
        here = self.here
        for distance in range(self.last):

            @pl.when((here.place - distance >= 0) & (here.place < self.last))
            def _():
                self.up(distance).wait_send()

            @pl.when((here.place + distance <= self.last) & (here.place > 0))
            def _():
                self.down(distance).wait_send()


class RowGather:
    def __init__(self, here, own, whole, sems, spot=lambda shard: shard):
        self.here, self.own, self.whole, self.spot = here, own, whole, spot
        self.ys, self.yr, self.local = sems[4:]
        self.line = LineGather(here, own, self.mine, sems[:4])

    def mine(self, place):
        return self.whole.at[self.spot(place * 2 + self.here.half)]

    def theirs(self, place):
        return self.whole.at[self.spot(place * 2 + 1 - self.here.half)]

    def keep(self):
        return pltpu.make_async_copy(self.own, self.mine(self.here.place), self.local)

    def across(self, place, own=False):
        slot = self.mine(place)
        source = self.own if own else slot
        return remote(source, slot, self.ys.at[place], self.yr.at[place], self.here.twin)

    def arrived(self, place):
        slot = self.theirs(place)
        remote(slot, slot, self.ys.at[place], self.yr.at[place], self.here.twin).wait_recv()

    def send(self):
        self.line.send()
        self.across(self.here.place, own=True).start()
        self.keep().start()

    def step(self, distance):
        self.line.step(distance, lambda place: self.across(place).start())

    def arrive(self):
        self.keep().wait()
        for place in range(self.here.outer):
            self.arrived(place)

    def finish(self):
        self.line.finish()
        for place in range(self.here.outer):
            self.across(place).wait_send()


class TwinFirstGather(RowGather):
    def __init__(self, here, own, whole, sems, twin_sems):
        super().__init__(here, own, whole, sems)
        self.lines = [
            self.line,
            LineGather(here, self.theirs(here.place), self.theirs, twin_sems[:4]),
        ]

    def twin(self):
        self.arrived(self.here.place)
        self.lines[1].send()

    def step(self, distance):
        for line in self.lines:
            line.step(distance)

    def arrive(self):
        self.keep().wait()

    def finish(self):
        for line in self.lines:
            line.finish()
        self.across(self.here.place, own=True).wait_send()


class HeadGather:
    def __init__(self, here, own, whole, sems):
        self.here, self.own, self.whole = here, own, whole
        self.us, self.zr, self.ds, _, self.ys, self.yr, self.local = sems
        self.last = here.outer - 1
        self.count = here.quarter // 2
        self.first = here.seq * self.count
        self.mine = here.place - self.first
        self.inside = (self.mine >= 0) & (self.mine < self.count)

    def slot(self, index):
        return self.whole.at[index * 2 + self.here.half]

    def keep(self):
        return pltpu.make_async_copy(self.own, self.slot(self.mine), self.local)

    def up(self, index, own=False):
        slot = self.slot(index)
        peer = self.here.outer_peer(self.here.place + 1)
        return remote(self.own if own else slot, slot, self.us.at[index], self.zr.at[index], peer)

    def down(self, index, own=False):
        slot = self.slot(index)
        peer = self.here.outer_peer(self.here.place - 1)
        return remote(self.own if own else slot, slot, self.ds.at[index], self.zr.at[index], peer)

    def across(self, index):
        slot = self.slot(index)
        return remote(slot, slot, self.ys.at[index], self.yr.at[index], self.here.twin)

    def send(self):
        @pl.when(self.inside)
        def _():
            self.keep().start()

            @pl.when(self.here.place < self.last)
            def _():
                self.up(self.mine, own=True).start()

            @pl.when(self.here.place > 0)
            def _():
                self.down(self.mine, own=True).start()

    def step(self):
        here = self.here

        @pl.when(self.inside)
        def _():
            self.keep().wait()

        for index in range(self.count):
            slot = self.slot(index)
            arrival = remote(slot, slot, self.us.at[0], self.zr.at[index], here.twin)

            @pl.when(self.mine > index)
            def _():
                arrival.wait_recv()

                @pl.when(here.place < self.last)
                def _():
                    self.up(index).start()

            @pl.when(self.mine < index)
            def _():
                arrival.wait_recv()

                @pl.when(here.place > 0)
                def _():
                    self.down(index).start()

            self.across(index).start()

    def arrive(self):
        for index in range(self.count):
            slot = self.whole.at[index * 2 + 1 - self.here.half]
            remote(
                slot, slot, self.ys.at[index], self.yr.at[index], self.here.twin
            ).wait_recv()

    def finish(self):
        here = self.here
        for index in range(self.count):

            @pl.when((self.mine >= index) & (here.place < self.last))
            def _():
                self.up(index).wait_send()

            @pl.when((self.mine <= index) & (here.place > 0))
            def _():
                self.down(index).wait_send()

            self.across(index).wait_send()


class TokenGather:
    def __init__(self, here, own, whole, sems):
        self.here, self.own, self.whole = here, own, whole
        self.send_sems, self.recv_sems, self.local = sems
        self.rows = whole.shape[0] // 4

    def slot(self, seq):
        return self.whole.at[pl.ds(pl.multiple_of(seq * self.rows, self.rows), self.rows), :]

    def keep(self):
        return pltpu.make_async_copy(self.own, self.slot(self.here.seq), self.local)

    def copy(self, index):
        here = self.here
        slot = self.slot(here.far_seq if index == 2 else here.seq)
        return remote(
            slot if index == 2 else self.own,
            slot,
            self.send_sems.at[index],
            self.recv_sems.at[index],
            here.far if index == 0 else here.mate,
        )

    def send(self):
        self.copy(0).start()
        self.copy(1).start()
        self.keep().start()

    def forward(self):
        self.copy(0).wait_recv()
        self.copy(2).start()

    def mate_arrived(self):
        self.copy(1).wait_recv()

    def rest_arrived(self):
        self.copy(2).wait_recv()
        self.keep().wait()

    def arrive(self):
        self.mate_arrived()
        self.rest_arrived()

    def finish(self):
        for index in range(3):
            self.copy(index).wait_send()


class PieceSum:
    def __init__(self, here, piece, base, give, got, pair, far_got, sems, step):
        self.here, self.piece, self.base, self.step = here, piece, base, step
        self.give, self.got, self.pair, self.far_got = give, got, pair, far_got
        self.send_sems, self.recv_sems = sems

    def to_mate(self, index):
        return remote(
            self.give.at[index],
            self.got.at[index],
            self.send_sems.at[index],
            self.recv_sems.at[index],
            self.here.mate,
        )

    def to_far(self):
        return remote(
            self.pair, self.far_got, self.send_sems.at[2], self.recv_sems.at[2], self.here.far
        )

    def columns(self, body):
        step = self.step

        @pl.loop(0, self.pair.shape[1] // step)
        def _(index):
            body(pl.ds(pl.multiple_of(index * step, step), step))

    def send(self):
        here = self.here
        for index, chip in enumerate((1 - here.chip, here.chip)):
            seq = chip * 2 + 1 - here.core

            def fill(column, index=index, seq=seq):
                self.give[index, :, column] = self.piece(seq, column).astype(BF)

            self.columns(fill)
            self.to_mate(index).start()

    def pass_on(self):
        self.to_mate(0).wait_recv()

        def fill(column):
            term = self.piece(self.here.far_seq, column) + self.got[0, :, column].astype(F32)
            self.pair[:, column] = term.astype(BF)

        self.columns(fill)
        self.to_far().start()

    def add_near(self):
        self.to_mate(1).wait_recv()

        def fill(column):
            term = self.piece(self.here.seq, column) + self.got[1, :, column].astype(F32)
            self.base[:, column] += term

        self.columns(fill)

    def add_far(self):
        self.to_far().wait_recv()

        def fill(column):
            self.base[:, column] += self.far_got[:, column].astype(F32)

        self.columns(fill)
        for copy in (self.to_mate(0), self.to_mate(1), self.to_far()):
            copy.wait_send()


def identity(size):
    rows = lax.broadcasted_iota(jnp.int32, (size, size), 0)
    columns = lax.broadcasted_iota(jnp.int32, (size, size), 1)
    return jnp.where(rows == columns, 1.0, 0.0).astype(BF)


FORWARD_PLAN = (
    (("down", "send"), ("out", "send"),),
    (),
    (("down", 0),),
    (("second", "send"),),
    (),
    (("down", 1), ("down", 2), ("out", 0),),
    (),
    (("first", "send"),),
    (),
    (),
    (),
    (("second", "twin"), ("first", 0),),
    (("third", "send"),),
    (),
    (),
    (("first", 1), ("second", 0),),
    (("first", 2),),
    (("third", 0),),
    (("third", 1), ("second", 1),),
    (),
    (),
    (("third", 2),),
    (),
    (("second", 2),),
    (),
    (),
    (),
)


def forward_kernel(
    size,
    hidden_ref,
    dy_hbm,
    w_query,
    w_key,
    w_value,
    w_out,
    w_gate,
    w_up,
    w_down,
    attn_gain_ref,
    mlp_gain_ref,
    query_gain_ref,
    key_gain_ref,
    inverse_ref,
    segment_ref,
    qkv_full,
    out_full,
    first_full,
    second_full,
    down_full,
    n1_full,
    dy_full,
    n2_full,
    n1_turned,
    dy_turned,
    n2_turned,
    act_out,
    first_pair,
    second_pair,
    down_terms,
    first_terms,
    proj_ref,
    heads_ref,
    mixed_ref,
    lse_ref,
    middle_ref,
    cos_ref,
    sin_ref,
    start_row,
    lhs,
    dy_all,
    turned,
    qkv_w,
    out_w,
    qkv_own,
    out_own,
    down_own,
    dy_own,
    wide_own,
    first_own,
    second_own,
    own_rows,
    give,
    got,
    pair,
    far_got,
    us,
    ur,
    ds,
    dr,
    ys,
    yr,
    row_local,
    ts,
    tr,
    token_local,
    load_sem,
    ss,
    sr,
    start_ref,
    turned_ids,
    eye,
    staging,
    staging_sems,
):
    here = Place(size)
    last = here.outer - 1
    length, width = lhs.shape
    lse_ref[...] = jnp.zeros_like(lse_ref)
    rows = length // 4
    units = act_out.shape[2]
    chunk = units // 2
    tail = 256
    heads = mixed_ref.shape[1] // HEAD_DIM
    kv_heads = heads // 2
    ff_part = units // size
    own = act_out.shape[1]

    def sems(index):
        return tuple(kind.at[index] for kind in (us, ur, ds, dr, ys, yr, row_local))

    down_rows = pl.ds(pl.multiple_of(here.seq * ff_part, ff_part), ff_part)
    qkv = RowGather(here, qkv_own, qkv_full, sems(0))
    out = HeadGather(here, out_own, out_full, sems(1))
    down = RowGather(
        here,
        down_own,
        down_full,
        sems(2),
        lambda shard: pl.ds(pl.multiple_of(shard * ff_part, ff_part), ff_part),
    )
    first = RowGather(here, first_own, first_full, sems(3))
    cut = 2 * (chunk - tail)
    second = TwinFirstGather(
        here, second_own.at[:, 0:cut], second_full.at[:, :, 0:cut], sems(4), sems(6)
    )
    third = RowGather(
        here, second_own.at[:, cut : 2 * chunk], second_full.at[:, :, cut : 2 * chunk], sems(5)
    )
    n1 = TokenGather(here, own_rows.at[0], n1_full, (ts.at[0], tr.at[0], token_local.at[0]))
    n2 = TokenGather(here, own_rows.at[1], n2_full, (ts.at[1], tr.at[1], token_local.at[1]))
    dy = TokenGather(here, dy_own, dy_full, (ts.at[2], tr.at[2], token_local.at[2]))

    loads = []
    at = 0
    for index, (weight, count) in enumerate(((w_query, heads), (w_key, kv_heads), (w_value, kv_heads))):
        count = count * HEAD_DIM
        source = weight.at[:, pl.ds(pl.multiple_of(here.seq * count, count), count)]
        loads.append(
            pltpu.make_async_copy(source, qkv_own.at[:, at : at + count], load_sem.at[index])
        )
        at += count
    loads.append(pltpu.make_async_copy(w_down.at[down_rows, :], down_own, load_sem.at[3]))
    loads.append(pltpu.make_async_copy(w_out, out_own, load_sem.at[4]))
    loads.append(pltpu.make_async_copy(dy_hbm, dy_own, load_sem.at[5]))
    loads.append(pltpu.make_async_copy(w_gate, wide_own, load_sem.at[6]))
    for load in loads:
        load.start()
    here.greet()
    for load in loads[:3]:
        load.wait()
    qkv.send()
    loads[5].wait()
    dy.send()

    def norm_rows(source, gain_ref, target):
        @pl.loop(0, rows // 32)
        def _(index):
            part = pl.ds(pl.multiple_of(index * 32, 32), 32)
            values = source[part, :].astype(F32)
            scales = lax.rsqrt(jnp.mean(values * values, axis=-1, keepdims=True) + EPSILON)
            target[part, :] = (values * scales * gain_ref[...]).astype(BF)

    gathers = {"out": out, "down": down, "first": first, "second": second, "third": third}

    def advance(steps):
        for name, step in steps:
            gather = gathers[name]
            if step == "send":
                gather.send()
            elif step == "twin":
                gather.twin()
            elif name == "out":
                gather.step()
            else:
                for distance in range(last * step // 3, last * (step + 1) // 3):
                    gather.step(distance)

    norm_rows(hidden_ref, attn_gain_ref, own_rows.at[0])
    n1.send()
    for load in loads[3:5]:
        load.wait()
    advance(FORWARD_PLAN[0])
    for load in loads[6:]:
        load.wait()

    most = chunk - tail

    def cut_units(side):
        for seq in range(4):

            @pl.when(here.seq == seq)
            def _():
                @pl.loop(0, wide_own.shape[0] // 16)
                def _(index):
                    part = pl.ds(pl.multiple_of(index * 16, 16), 16)

                    def gathered(begin):
                        pieces = [
                            wide_own[part, (block * 4 + seq) * ff_part : (block * 4 + seq + 1) * ff_part]
                            for block in range(begin, begin + size // 2)
                        ]
                        return jnp.concatenate(pieces, axis=1)

                    first_own[part, side * chunk : (side + 1) * chunk] = gathered(0)
                    rest = gathered(size // 2)
                    second_own[part, side * most : (side + 1) * most] = rest[:, 0:most]
                    at = 2 * most + side * tail
                    second_own[part, at : at + tail] = rest[:, most:]

    eye[...] = identity(256)

    def rotation():
        ids = segment_ref[...].astype(F32)
        turned_ids[...] = jnp.broadcast_to(ids, (128, length)).T
        lane = lax.broadcasted_iota(jnp.int32, (128, 128), 1)

        @pl.loop(0, length // 128)
        def _(index):
            part = pl.ds(pl.multiple_of(index * 128, 128), 128)
            own_ids = turned_ids[part, :]
            count = jnp.zeros((128, 128), F32)
            for at in range(0, length, 128):
                count = count + jnp.where(
                    segment_ref[:, at : at + 128].astype(F32) < own_ids, 1.0, 0.0
                )
            starts = jnp.sum(count, axis=-1, keepdims=True)
            start_ref[part, :] = starts.astype(jnp.int32)
            starts = jnp.broadcast_to(starts, (128, 128))
            turned_ids[part, :] = starts
            places = lax.broadcasted_iota(jnp.int32, (128, 128), 0) + index * 128
            angles = (places.astype(F32) - starts) * inverse_ref[...]
            cos_ref[part, :] = jnp.cos(angles)
            sine = jnp.sin(angles)
            sin_ref[part, :] = jnp.where(lane < HEAD_DIM // 2, -sine, sine)

        start_row[...] = turned_ids[...].T[0:1].astype(jnp.int32)

    zones = width // 512

    def turn(source, target):
        for seq_group in range(4):
            for zone in range(0, zones, 2):
                at = (seq_group * zones + zone) * 128
                both = contract_cols(eye[...], source[:, at : at + 256]).astype(BF)
                turned[zone * 4 + seq_group] = both[0:128]
                turned[zone * 4 + 4 + seq_group] = both[128:256]
        copy = pltpu.make_async_copy(turned, target, load_sem.at[4])
        copy.start()
        return copy

    cut_units(0)
    load_up = pltpu.make_async_copy(w_up, wide_own, load_sem.at[7])
    load_up.start()
    load_up.wait()
    cut_units(1)
    advance(FORWARD_PLAN[1])
    for third_part in range(3):
        for distance in range(last * third_part // 3, last * (third_part + 1) // 3):
            qkv.step(distance)
        advance(FORWARD_PLAN[2 + third_part])
        if third_part == 0:
            rotation()
            dy.forward()
    dy.arrive()
    load_dy = pltpu.make_async_copy(dy_full, dy_all, load_sem.at[0])
    load_dy.start()
    load_dy.wait()
    store = turn(dy_all, dy_turned)
    n1.forward()
    advance(FORWARD_PLAN[5])
    n1.arrive()
    load_lhs = pltpu.make_async_copy(n1_full, lhs, load_sem.at[0])
    load_lhs.start()
    advance(FORWARD_PLAN[6])
    qkv.arrive()
    load_qkv = pltpu.make_async_copy(qkv_full, qkv_w, load_sem.at[1])
    load_qkv.start()
    advance(FORWARD_PLAN[7])
    load_lhs.wait()
    load_qkv.wait()

    def project(tile):
        weight = qkv_w[:, :, tile * 256 : tile * 256 + 256].reshape(width, 256)
        gain_ref = query_gain_ref if tile < heads // 2 else key_gain_ref

        @pl.loop(0, 4)
        def _(index):
            part = pl.ds(pl.multiple_of(index * rows, rows), rows)
            both = dot(lhs[part, :], weight)
            for side in range(2):
                head = tile * 2 + side
                proj = both[:, side * HEAD_DIM : (side + 1) * HEAD_DIM]
                if head >= heads + kv_heads:
                    heads_ref[head, part, :] = proj.astype(BF)
                    continue
                proj_ref[head, part, :] = proj
                scales = lax.rsqrt(jnp.mean(proj * proj, axis=-1, keepdims=True) + EPSILON)
                gained = proj * scales * gain_ref[...]
                turned = pltpu.roll(gained, HEAD_DIM // 2, 1)
                heads_ref[head, part, :] = (
                    gained * cos_ref[part, :] + turned * sin_ref[part, :]
                ).astype(BF)

    def attend(head):
        pair_head = head // 2
        for block in range(4):
            end = (block + 1) * rows
            part = pl.ds(block * rows, rows)
            scores = contract_cols(
                heads_ref[head, part, :], heads_ref[heads + pair_head, 0:end, :]
            )
            row_place = lax.broadcasted_iota(jnp.int32, (rows, end), 0) + block * rows
            col_place = lax.broadcasted_iota(jnp.int32, (rows, end), 1)
            allowed = (col_place >= start_ref[part, :]) & (col_place <= row_place)
            raised = jnp.where(allowed, jnp.exp(scores * (HEAD_DIM ** (-0.5))), 0.0)
            sums = jnp.sum(raised, axis=-1, keepdims=True)
            mixed = dot(raised.astype(BF), heads_ref[heads + kv_heads + pair_head, 0:end, :])
            mixed = mixed * (1.0 / sums)
            mixed_ref[part, head * HEAD_DIM : (head + 1) * HEAD_DIM] = mixed.astype(BF)
            lse_ref[part, head : head + 1] = jnp.log(sums)

    tiles = (heads + 2 * kv_heads) // 2
    for tile in range(tiles):
        if tile == tiles // 2:
            advance(FORWARD_PLAN[8])
        project(tile)
    advance(FORWARD_PLAN[9])

    for head in range(heads):
        attend(head)
        advance(FORWARD_PLAN[10 + head])
    out.arrive()
    load_out = pltpu.make_async_copy(out_full, out_w, load_sem.at[2])
    load_out.start()
    load_out.wait()

    def out_piece(seq, column):
        part = pl.ds(pl.multiple_of(seq * rows, rows), rows)
        weight = out_w[:, :, column]
        return dot(mixed_ref[part, :], weight.reshape(-1, weight.shape[-1]))

    middle_ref[...] = hidden_ref[...].astype(F32)
    token_sum = PieceSum(
        here, out_piece, middle_ref, give, got, pair, far_got, (ss, sr), 512
    )
    token_sum.send()
    advance(FORWARD_PLAN[14])
    token_sum.pass_on()
    token_sum.add_near()
    advance(FORWARD_PLAN[15])
    token_sum.add_far()
    norm_rows(middle_ref, mlp_gain_ref, own_rows.at[1])
    n2.send()
    advance(FORWARD_PLAN[16])
    store.wait()
    store = turn(lhs, n1_turned)
    advance(FORWARD_PLAN[17])
    n2.forward()
    advance(FORWARD_PLAN[18])
    n2.arrive()
    load_lhs = pltpu.make_async_copy(n2_full, lhs, load_sem.at[3])
    load_lhs.start()
    down.arrive()
    first.arrive()
    load_lhs.wait()

    def feed(gather, begin, count):
        tiles = count // 256
        spot = begin // 256

        def body(gate_w, up_w, down_w, act_ref, gate_grad, up_grad):
            gate_tile = gate_w[...].reshape(width, 256)
            up_tile = up_w[...].reshape(width, 256)
            down_tile = down_w[...]

            @pl.loop(0, 4)
            def _(index):
                part = pl.ds(pl.multiple_of(index * rows, rows), rows)
                gate = dot(lhs[part, :], gate_tile)
                up = dot(lhs[part, :], up_tile)
                act_grad = contract_cols(dy_all[part, :], down_tile)
                sigmoid = jax.nn.sigmoid(gate)
                silu = gate * sigmoid
                gate_term = act_grad * up * sigmoid * (1.0 + gate * (1.0 - sigmoid))
                here_blocks = pl.ds(index * (rows // own), rows // own)
                for target, value in (
                    (act_ref, silu * up),
                    (gate_grad, gate_term),
                    (up_grad, act_grad * silu),
                ):
                    target[here_blocks] = value.astype(BF).reshape(rows // own, own, 256)

        block = gather.whole.shape[:-1] + (256,)
        blocked = act_out.shape[:-1] + (256,)
        grads = first_pair if begin < chunk else second_pair
        first_spot = 0 if begin < chunk + 1 else 2 * (begin - chunk) // 256
        pltpu.emit_pipeline(
            body,
            grid=(tiles,),
            in_specs=[
                pl.BlockSpec(block, lambda t: (0, 0, t)),
                pl.BlockSpec(block, lambda t: (0, 0, t + tiles)),
                pl.BlockSpec((256, width), lambda t: (t + spot, 0)),
            ],
            out_specs=[
                pl.BlockSpec(blocked, lambda t: (0, 0, t + spot)),
                pl.BlockSpec(blocked, lambda t: (0, 0, t + first_spot)),
                pl.BlockSpec(blocked, lambda t: (0, 0, t + first_spot + tiles)),
            ],
        )(gather.whole, gather.whole, down_full, act_out, grads, grads)

    def make_terms(rhs, begin, count, target):
        held = qkv_w.at[0 : length // own, :, 0:count]
        copy = pltpu.make_async_copy(rhs.at[:, :, begin : begin + count], held, load_sem.at[0])
        copy.start()
        copy.wait()
        per = staging.shape[2]
        stores = []
        for zone in range(zones):
            buffer = zone % 2
            if zone >= 2:
                stores[zone - 2].wait()

            @pl.loop(0, count // 256)
            def _(index):
                lane = pl.ds(pl.multiple_of(index * 256, 256), 256)
                left = turned[zone * 4 : zone * 4 + 4].reshape(512, length)
                right = qkv_w[0 : length // own, :, lane].reshape(length, 256)
                terms = dot(left, right).astype(BF)
                rows_each = staging.shape[4]
                for group in range(4):
                    for sub in range(per):
                        at = group * 128 + sub * 2 * rows_each
                        even = terms[at : at + rows_each]
                        odd = terms[at + rows_each : at + 2 * rows_each]
                        staging[buffer, 0, sub, group, :, lane] = jnp.where(here.half == 0, even, odd)
                        staging[buffer, 1, sub, group, :, lane] = jnp.where(here.half == 0, odd, even)

            store = pltpu.make_async_copy(
                staging.at[buffer, :, :, :, :, 0:count],
                target.at[:, zone * per : (zone + 1) * per, :, :, begin : begin + count],
                staging_sems.at[buffer],
            )
            store.start()
            stores.append(store)
        for store in stores[-2:]:
            store.wait()

    store.wait()
    load_turned = pltpu.make_async_copy(dy_turned, turned, load_sem.at[3])
    load_turned.start()
    feed(first, 0, chunk)
    advance(FORWARD_PLAN[19])
    load_turned.wait()
    make_terms(act_out, 0, chunk, down_terms)
    advance(FORWARD_PLAN[20])
    store = turn(lhs, n2_turned)
    advance(FORWARD_PLAN[21])
    make_terms(first_pair, 0, chunk, first_terms)
    advance(FORWARD_PLAN[22])
    make_terms(first_pair, chunk, chunk, first_terms)
    advance(FORWARD_PLAN[23])
    store.wait()
    load_turned = pltpu.make_async_copy(dy_turned, turned, load_sem.at[4])
    load_turned.start()
    second.arrive()
    feed(second, chunk, chunk - tail)
    advance(FORWARD_PLAN[24])
    load_turned.wait()
    make_terms(act_out, chunk, chunk - tail, down_terms)
    advance(FORWARD_PLAN[25])
    advance(FORWARD_PLAN[26])
    third.arrive()
    feed(third, 2 * chunk - tail, tail)
    make_terms(act_out, 2 * chunk - tail, tail, down_terms)
    for gather in (qkv, out, first, second, third, down, n1, n2, dy):
        gather.finish()


def forward(hidden, upstream, weights, gains, segment):
    size = lax.axis_size("shard")
    quarter, outer = size // 4, size // 2
    piece, width = hidden.shape
    length = piece * 4
    heads = Q_HEADS // 4
    kv_heads = KV_HEADS // 4
    w_query, _, _, w_out, w_gate, _, w_down = weights
    own = w_query.shape[0]
    qkv_width = (heads + 2 * kv_heads) * HEAD_DIM
    units = w_down.shape[0] // 4 * size

    def shape(*dims, kind=BF):
        return jax.ShapeDtypeStruct(dims, kind)

    results = [
        shape(size, own, qkv_width),
        shape(quarter, *w_out.shape),
        shape(size, own, units),
        shape(size, own, units),
        shape(units, width),
        shape(length, width),
        shape(length, width),
        shape(length, width),
        shape(width // 128, 128, length),
        shape(width // 128, 128, length),
        shape(width // 128, 128, length),
        shape(length // own, own, units),
        shape(length // own, own, units),
        shape(length // own, own, units),
        shape(2, outer, 4, width // (4 * size), units),
        shape(2, outer, 4, width // (4 * size), units),
        shape(heads + kv_heads, length, HEAD_DIM, kind=F32),
        shape(heads + 2 * kv_heads, length, HEAD_DIM),
        shape(length, heads * HEAD_DIM),
        shape(length, 128, kind=F32),
        shape(piece, width, kind=F32),
        shape(length, HEAD_DIM, kind=F32),
        shape(length, HEAD_DIM, kind=F32),
        shape(1, length, kind=jnp.int32),
    ]
    powers = np.arange(HEAD_DIM // 2, dtype=np.float32) * np.float32(2.0) / np.float32(HEAD_DIM)
    inverse = np.float32(ROPE_BASE) ** -powers
    dma = pltpu.SemaphoreType.DMA
    return pl.pallas_call(
        functools.partial(forward_kernel, size),
        out_shape=results,
        in_specs=[VMEM] + [ANY] * 8 + [VMEM] * 6,
        out_specs=[ANY] * 16 + [VMEM] * 8,
        scratch_shapes=[
            pltpu.VMEM((length, width), BF),
            pltpu.VMEM((length, width), BF),
            pltpu.VMEM((width // 128, 128, length), BF),
            pltpu.VMEM((size, own, qkv_width), BF),
            pltpu.VMEM((quarter,) + w_out.shape, BF),
            pltpu.VMEM((own, qkv_width), BF),
            pltpu.VMEM(w_out.shape, BF),
            pltpu.VMEM((w_down.shape[0] // 4, width), BF),
            pltpu.VMEM((piece, width), BF),
            pltpu.VMEM(w_gate.shape, BF),
            pltpu.VMEM((own, units), BF),
            pltpu.VMEM((own, units), BF),
            pltpu.VMEM((2, piece, width), BF),
            pltpu.VMEM((2, piece, width), BF),
            pltpu.VMEM((2, piece, width), BF),
            pltpu.VMEM((piece, width), BF),
            pltpu.VMEM((piece, width), BF),
            dma((7, outer)),
            dma((7, outer)),
            dma((7, outer)),
            dma((7, outer)),
            dma((7, outer)),
            dma((7, outer)),
            dma((7,)),
            dma((3, 3)),
            dma((3, 3)),
            dma((3,)),
            dma((8,)),
            dma((3,)),
            dma((3,)),
            pltpu.VMEM((length, 1), jnp.int32),
            pltpu.VMEM((length, 128), F32),
            pltpu.VMEM((256, 256), BF),
            pltpu.VMEM((2, 2, outer // 4, 4, width // (4 * size), units // 2), BF),
            dma((2,)),
        ],
        compiler_params=pltpu.CompilerParams(
            collective_id=0, has_side_effects=True, vmem_limit_bytes=VMEM_BYTES
        ),
        name="forward_gather",
    )(
        hidden,
        upstream,
        *weights,
        *gains,
        jnp.asarray(np.concatenate([inverse, inverse])[None], F32),
        segment[None],
    )


def add_rows(target, sources, step=16):
    groups, rows, _ = target.shape

    @pl.loop(0, rows // step)
    def _(index):
        part = pl.ds(pl.multiple_of(index * step, step), step)
        for group in range(groups):
            total = sources[0][group, part, :].astype(target.dtype)
            for source in sources[1:]:
                total = total + source[group, part, :].astype(target.dtype)
            target[group, part, :] = total


class RowSum:
    def __init__(self, here, give, keep, near, rising, falling, stage, total, sems):
        self.here, self.give, self.keep = here, give, keep
        self.near, self.rising, self.falling = near, rising, falling
        self.stage, self.total = stage, total
        self.ys, self.yr, self.us, self.ur, self.ds, self.dr, self.load = sems
        self.last = here.outer - 1

    def across(self, place):
        return remote(
            self.give.at[place],
            self.near.at[place],
            self.ys.at[place],
            self.yr.at[place],
            self.here.twin,
        )

    def up(self, place):
        peer = self.here.outer_peer(self.here.place + 1)
        return remote(
            self.keep.at[place], self.rising.at[place], self.us.at[place], self.ur.at[place], peer
        )

    def down(self, place):
        peer = self.here.outer_peer(self.here.place - 1)
        return remote(
            self.keep.at[place], self.falling.at[place], self.ds.at[place], self.dr.at[place], peer
        )

    def arrived(self, slot, send, receive):
        remote(slot, slot, send, receive, self.here.twin).wait_recv()

    def fold(self, distance):
        here = self.here
        above = here.place + distance
        below = here.place - distance

        def merge(place, line, receive, first):
            near = pltpu.make_async_copy(self.near.at[place], self.stage.at[0], self.load.at[0])
            self.arrived(self.near.at[place], self.ys.at[place], self.yr.at[place])
            near.start()

            @pl.when(first)
            def _():
                near.wait()
                add_rows(self.keep.at[place], [self.keep.at[place], self.stage.at[0]])

            @pl.when(jnp.logical_not(first))
            def _():
                self.arrived(line.at[place], self.us.at[0], receive.at[place])
                far = pltpu.make_async_copy(line.at[place], self.stage.at[1], self.load.at[1])
                far.start()
                near.wait()
                far.wait()
                add_rows(
                    self.keep.at[place], [self.keep.at[place], self.stage.at[0], self.stage.at[1]]
                )

        @pl.when(above <= self.last)
        def _():
            merge(above, self.rising, self.ur, here.place == 0)
            self.up(above).start()

        @pl.when(below >= 0)
        def _():
            merge(below, self.falling, self.dr, here.place == self.last)
            self.down(below).start()

    def finish(self):
        here = self.here
        place = here.place
        self.arrived(self.near.at[place], self.ys.at[place], self.yr.at[place])
        keep = self.keep.at[place]
        near = pltpu.make_async_copy(self.near.at[place], self.stage.at[0], self.load.at[0])
        low = pltpu.make_async_copy(self.rising.at[place], self.stage.at[1], self.load.at[1])
        high = pltpu.make_async_copy(self.falling.at[place], self.stage.at[1], self.load.at[1])
        near.start()

        @pl.when(place > 0)
        def _():
            self.arrived(self.rising.at[place], self.us.at[0], self.ur.at[place])
            low.start()
            low.wait()

        @pl.when(place == 0)
        def _():
            self.arrived(self.falling.at[place], self.ds.at[0], self.dr.at[place])
            high.start()
            high.wait()

        near.wait()

        @pl.when((place > 0) & (place < self.last))
        def _():
            add_rows(keep, [keep, self.stage.at[0], self.stage.at[1]])
            self.arrived(self.falling.at[place], self.ds.at[0], self.dr.at[place])
            high.start()
            high.wait()
            add_rows(self.total, [keep, self.stage.at[1]])

        @pl.when((place == 0) | (place == self.last))
        def _():
            add_rows(self.total, [keep, self.stage.at[0], self.stage.at[1]])

    def sent(self):
        for place in range(self.here.outer):
            self.across(place).wait_send()

    def settle(self):
        here = self.here
        for place in range(here.outer):

            @pl.when(place > here.place)
            def _():
                self.up(place).wait_send()

            @pl.when(place < here.place)
            def _():
                self.down(place).wait_send()


def compute_terms(here, give, keep, left, right, tiles, orders, senders):
    own = give.shape[2]
    per = 128 // (2 * own)
    step = 256
    for group, done in orders:
        spots = tiles(group)

        @pl.loop(0, give.shape[3] // step)
        def _(index):
            lane = pl.ds(pl.multiple_of(index * step, step), step)
            terms = dot(left(group), right(lane)).astype(BF)
            for spot, (zone, seq_group) in enumerate(spots):
                for sub in range(per):
                    at = spot * 128 + sub * 2 * own
                    even, odd = terms[at : at + own], terms[at + own : at + 2 * own]
                    place = zone * per + sub
                    keep[place, seq_group, :, lane] = jnp.where(here.half == 0, even, odd)
                    give[place, seq_group, :, lane] = jnp.where(here.half == 0, odd, even)

        for zone in done:
            for sub in range(per):
                for sender in senders:
                    sender.across(zone * per + sub).start()


class LineSum:
    def __init__(self, here, terms, rising, falling, stage, sems):
        self.here, self.terms, self.stage = here, terms, stage
        self.rising, self.falling = rising, falling
        self.us, self.ur, self.ds, self.dr, self.load = sems
        self.last = here.outer - 1

    def up(self, place):
        peer = self.here.outer_peer(self.here.place + 1)
        return remote(
            self.terms.at[place], self.rising.at[place], self.us.at[place], self.ur.at[place], peer
        )

    def down(self, place):
        peer = self.here.outer_peer(self.here.place - 1)
        return remote(
            self.terms.at[place], self.falling.at[place], self.ds.at[place], self.dr.at[place], peer
        )

    def merge(self, place, line, receive):
        slot = line.at[place]
        remote(slot, slot, self.us.at[0], receive.at[place], self.here.twin).wait_recv()
        copy = pltpu.make_async_copy(slot, self.stage.at[0], self.load.at[0])
        copy.start()
        copy.wait()
        add_rows(self.terms.at[place], [self.terms.at[place], self.stage.at[0]])

    def fold(self, distance):
        here = self.here
        above = here.place + distance
        below = here.place - distance

        @pl.when(above <= self.last)
        def _():
            @pl.when(here.place > 0)
            def _():
                self.merge(above, self.rising, self.ur)

            self.up(above).start()

        @pl.when(below >= 0)
        def _():
            @pl.when(here.place < self.last)
            def _():
                self.merge(below, self.falling, self.dr)

            self.down(below).start()

    def gather(self):
        place = self.here.place

        @pl.when(place > 0)
        def _():
            self.merge(place, self.rising, self.ur)

        @pl.when(place < self.last)
        def _():
            self.merge(place, self.falling, self.dr)

    def settle(self):
        here = self.here
        for place in range(here.outer):

            @pl.when(place > here.place)
            def _():
                self.up(place).wait_send()

            @pl.when(place < here.place)
            def _():
                self.down(place).wait_send()


class LineFirstSum(RowSum):
    def __init__(self, here, give, keep, near, lines, stage, total, sems, twin_sems):
        self.here, self.give, self.keep = here, give, keep
        self.near, self.stage, self.total = near, stage, total
        self.ys, self.yr, self.load = sems[0], sems[1], sems[6]
        self.lines = [
            LineSum(here, terms, rising, falling, stage, kinds[2:])
            for terms, (rising, falling), kinds in (
                (give, lines[0], twin_sems),
                (keep, lines[1], sems),
            )
        ]

    def fold(self, distance):
        for line in self.lines:
            line.fold(distance)

    def pass_on(self):
        self.lines[0].gather()
        self.across(self.here.place).start()
        self.lines[1].gather()

    def finish(self):
        place = self.here.place
        self.arrived(self.near.at[place], self.ys.at[place], self.yr.at[place])
        near = pltpu.make_async_copy(self.near.at[place], self.stage.at[0], self.load.at[0])
        near.start()
        near.wait()
        add_rows(self.total, [self.keep.at[place], self.stage.at[0]])

    def sent(self):
        self.across(self.here.place).wait_send()

    def settle(self):
        for line in self.lines:
            line.settle()


class RowSpread:
    def __init__(self, here, rows, whole, sems):
        self.here, self.rows, self.whole = here, rows, whole
        self.send_sems, self.recv_sems, self.local = sems

    def copy(self, amount):
        seq = lax.rem(self.here.seq + amount, 4)
        return remote(
            self.rows.at[seq],
            self.whole.at[self.here.seq],
            self.send_sems.at[amount - 1],
            self.recv_sems.at[amount - 1],
            {"seq": seq},
        )

    def keep(self):
        seq = self.here.seq
        return pltpu.make_async_copy(self.rows.at[seq], self.whole.at[seq], self.local)

    def send(self):
        for amount in (2, 3, 1):
            self.copy(amount).start()
        self.keep().start()

    def arrive(self):
        for amount in (1, 2, 3):
            self.copy(amount).wait_recv()
        self.keep().wait()

    def finish(self):
        for amount in (1, 2, 3):
            self.copy(amount).wait_send()


class TokenSum:
    def __init__(self, here, part, got, pair, far_got, base, sems):
        self.here, self.part, self.got, self.pair = here, part, got, pair
        self.far_got, self.base = far_got, base
        self.send_sems, self.recv_sems = sems
        self.rows = part.shape[0] // 4

    def piece(self, seq):
        return pl.ds(pl.multiple_of(seq * self.rows, self.rows), self.rows)

    def to_mate(self, index):
        here = self.here
        chip = here.chip if index else 1 - here.chip
        seq = chip * 2 + 1 - here.core
        return remote(
            self.part.at[self.piece(seq), :],
            self.got.at[index],
            self.send_sems.at[index],
            self.recv_sems.at[index],
            here.mate,
        )

    def to_far(self):
        return remote(
            self.pair, self.far_got, self.send_sems.at[2], self.recv_sems.at[2], self.here.far
        )

    def send(self):
        self.to_mate(0).start()
        self.to_mate(1).start()

    def loop(self, body):
        @pl.loop(0, self.rows // 32)
        def _(index):
            body(index * 32)

    def pass_on(self):
        self.to_mate(0).wait_recv()
        begin = self.here.far_seq * self.rows

        def body(at):
            part = pl.ds(pl.multiple_of(at, 32), 32)
            source = pl.ds(pl.multiple_of(begin + at, 32), 32)
            total = self.part[source, :].astype(F32) + self.got[0, part, :].astype(F32)
            self.pair[part, :] = total.astype(BF)

        self.loop(body)
        self.to_far().start()

    def add_near(self):
        self.to_mate(1).wait_recv()
        begin = self.here.seq * self.rows

        def body(at):
            part = pl.ds(pl.multiple_of(at, 32), 32)
            source = pl.ds(pl.multiple_of(begin + at, 32), 32)
            self.base[part, :] += self.part[source, :].astype(F32) + self.got[1, part, :].astype(F32)

        self.loop(body)
        self.to_mate(0).wait_send()
        self.to_mate(1).wait_send()

    def add_far(self):
        self.to_far().wait_recv()

        def body(at):
            part = pl.ds(pl.multiple_of(at, 32), 32)
            self.base[part, :] += self.far_got[part, :].astype(F32)

        self.loop(body)
        self.to_far().wait_send()


class GainSum:
    def __init__(self, here, own, seq_got, middle, shard_got, sems):
        self.here, self.own, self.middle = here, own, middle
        self.seq_got, self.shard_got = seq_got, shard_got
        self.seq_send, self.seq_recv, self.shard_send, self.shard_recv = sems

    def over_seq(self, amount):
        here = self.here
        return remote(
            self.own,
            self.seq_got.at[here.seq],
            self.seq_send.at[amount - 1],
            self.seq_recv.at[amount - 1],
            {"seq": lax.rem(here.seq + amount, 4)},
        )

    def over_shard(self, amount):
        here = self.here
        return remote(
            self.middle,
            self.shard_got.at[here.shard],
            self.shard_send.at[amount - 1],
            self.shard_recv.at[amount - 1],
            {"shard": lax.rem(here.shard + amount, here.size)},
        )

    def start(self):
        for amount in range(1, 4):
            self.over_seq(amount).start()
        self.seq_got[self.here.seq] = self.own[...]

    def turn(self):
        for amount in range(1, 4):
            self.over_seq(amount).wait()
        total = self.seq_got[0]
        for index in range(1, 4):
            total = total + self.seq_got[index]
        self.middle[...] = total
        for amount in range(1, self.here.size):
            self.over_shard(amount).start()
        self.shard_got[self.here.shard] = total

    def finish(self):
        for amount in range(1, self.here.size):
            self.over_shard(amount).wait()
        total = self.shard_got[0]
        for index in range(1, self.here.size):
            total = total + self.shard_got[index]
        return total


PLAN = (
    (("down_a", 3),),
    (("down_a", 2),),
    (("down_a", 1),),
    (),
    (("first", 3),),
    (("down_b", 3),),
    (("down_b", 2), ("first", 2),),
    (("second", 3), ("down_b", 1),),
    (),
    (("second", 2), ("first", 1),),
    (),
    (),
    (("second", 1),),
    (("out", 3), ("down_a", "pass"),),
    (("query", 3), ("key", 3), ("down_b", "finish"), ("out", 2), ("query", 2), ("first", "finish"), ("key", 2), ("second", "finish"),),
    (("query", 1), ("key", 1),),
    (("out", 1), ("query", "finish"), ("key", "finish"), ("down_a", "finish"), ("out", "finish"),),
)


def backward_kernel(
    size,
    n1_hbm,
    n2_hbm,
    act_hbm,
    first_hbm,
    second_hbm,
    down_terms,
    first_terms,
    proj_hbm,
    heads_ref,
    mixed_ref,
    lse_ref,
    middle_hbm,
    hidden_hbm,
    dy_own,
    qkv_full,
    out_full,
    first_full,
    second_full,
    down_full,
    attn_gain_ref,
    mlp_gain_ref,
    query_gain_ref,
    key_gain_ref,
    cos_ref,
    sin_ref,
    start_ref,
    grad_in,
    gains_out,
    grad_out,
    hidden_out,
    down_rows,
    first_rows,
    second_rows,
    qkv_rows,
    da_hbm,
    near_mlp,
    rising_mlp,
    falling_mlp,
    rising_twin,
    falling_twin,
    near_qkv,
    rising_qkv,
    falling_qkv,
    near_out,
    rising_out,
    falling_out,
    lhs,
    turned,
    first_r,
    second_r,
    give,
    keep,
    give_out,
    keep_out,
    stage,
    stage_out,
    dout_ref,
    da_own,
    got,
    far_got,
    pair,
    middle_grad,
    proj_buf,
    eye,
    keys_turned,
    lse_t,
    delta,
    delta_t,
    dk_sum,
    dv_sum,
    gain_row,
    gain_seq,
    gain_middle,
    gain_shard,
    ys,
    yr,
    us,
    ur,
    ds,
    dr,
    fold_load,
    spread_s,
    spread_r,
    spread_l,
    sum_s,
    sum_r,
    ts,
    tr,
    token_local,
    gss,
    gsr,
    gts,
    gtr,
    load_sem,
    credit,
):
    here = Place(size)
    length, width = lhs.shape
    rows = length // 4
    units = first_r.shape[1]
    chunk = units // 2
    ff_part = units // size
    heads = mixed_ref.shape[1] // HEAD_DIM
    kv_heads = heads // 2
    qkv_width = qkv_full.shape[2]
    last = here.outer - 1
    scale = HEAD_DIM ** (-0.5)

    def load(source, target, index):
        copy = pltpu.make_async_copy(source, target, load_sem.at[index])
        copy.start()
        return copy

    def sems(index):
        return tuple(kind.at[index] for kind in (ys, yr, us, ur, ds, dr, fold_load))

    thin = qkv_width // 2
    cut = units * 2 // 3
    lanes = {
        "down_a": slice(0, cut),
        "down_b": slice(cut, units),
        "query": slice(0, thin),
        "key": slice(thin, 2 * thin),
    }

    def part(ref, name):
        return ref.at[:, :, :, lanes[name]]

    def row_sum(index, give_ref, keep_ref, near, rising, falling, stage_ref, total):
        return RowSum(
            here, give_ref, keep_ref, near, rising, falling, stage_ref, total, sems(index)
        )

    jobs = {
        "down_a": LineFirstSum(
            here,
            part(give.at[2], "down_a"),
            part(keep.at[0], "down_a"),
            part(near_mlp.at[0], "down_a"),
            (
                (rising_twin, falling_twin),
                (part(rising_mlp.at[0], "down_a"), part(falling_mlp.at[0], "down_a")),
            ),
            part(stage, "down_a"),
            keep.at[0, here.place, :, :, lanes["down_a"]],
            sems(0),
            sems(5),
        ),
        "down_b": row_sum(
            6,
            part(down_terms.at[1], "down_b"),
            part(keep.at[0], "down_b"),
            part(near_mlp.at[0], "down_b"),
            part(rising_mlp.at[0], "down_b"),
            part(falling_mlp.at[0], "down_b"),
            part(stage, "down_b"),
            keep.at[0, here.place, :, :, lanes["down_b"]],
        ),
        "out": row_sum(
            4, give_out, keep_out, near_out, rising_out, falling_out, stage_out, grad_out
        ),
    }
    for index, name in ((1, "first"), (2, "second")):
        jobs[name] = row_sum(
            index,
            first_terms.at[1] if name == "first" else give.at[0],
            keep.at[index],
            near_mlp.at[index],
            rising_mlp.at[index],
            falling_mlp.at[index],
            stage,
            keep.at[index, here.place],
        )
    for index, name in ((3, "query"), (7, "key")):
        jobs[name] = row_sum(
            index,
            part(give.at[1], name),
            part(second_r, name),
            part(near_qkv, name),
            part(rising_qkv, name),
            part(falling_qkv, name),
            part(stage, name),
            second_r.at[here.place, :, :, lanes[name]],
        )
    zones = width // 512

    def zone_at(index):
        zone = here.place // (here.outer // zones)
        return (
            3 * (1 - zone // 2),
            lax.rem(2 + 3 * zone, 5),
            1 + lax.rem(zone, 2),
            zone,
        )[index]

    zone_order = [zone_at(index) for index in range(zones)]
    by_zone = [(zone, (zone,)) for zone in zone_order]

    spreads = {}
    for index, (name, whole) in enumerate(
        (
            ("down_a", down_rows.at[:, :, lanes["down_a"]]),
            ("down_b", down_rows.at[:, :, lanes["down_b"]]),
            ("first", first_rows),
            ("second", second_rows),
            ("query", qkv_rows.at[:, :, lanes["query"]]),
            ("key", qkv_rows.at[:, :, lanes["key"]]),
        )
    ):
        kinds = (spread_s.at[index], spread_r.at[index], spread_l.at[index])
        spreads[name] = RowSpread(here, jobs[name].total, whole, kinds)

    def token_sum(index, base):
        return TokenSum(
            here, lhs, got, pair, far_got, base, (sum_s.at[index], sum_r.at[index])
        )

    sum_mlp = token_sum(0, middle_grad)
    sum_hidden = token_sum(1, grad_in)
    sum_attn = token_sum(2, grad_in)
    da = TokenGather(here, da_own, da_hbm, (ts, tr, token_local.at[0]))

    def model_tiles(group):
        return [(group, seq_group) for seq_group in range(4)]

    def first_columns(lane):
        return first_r[:, lane]

    def model_left(group):
        return turned[pl.ds(group * 4, 4)].reshape(512, length)

    def advance(steps):
        for name, step in steps:
            job = jobs[name]
            if step == "pass":
                job.pass_on()
            elif step == "finish":
                job.finish()
                if name in spreads:
                    spreads[name].send()
            else:
                for distance in range(last * step // 3, last * (step - 1) // 3, -1):
                    job.fold(distance)

    load_first = load(first_hbm, first_r, 1)
    load_keep = load(down_terms.at[0], keep.at[0], 5)
    load_give = load(down_terms.at[1, :, :, :, lanes["down_a"]], part(give.at[2], "down_a"), 6)
    load_first_keep = load(first_terms.at[0], keep.at[1], 7)
    load_turned = load(n2_hbm, turned, 0)
    load_middle = load(middle_hbm, grad_in, 2)
    load_dy = load(dy_own, da_own, 4)
    load_second = load(second_hbm, second_r, 3)
    eye[...] = identity(HEAD_DIM)
    here.greet(wide=True)
    for zone in zone_order:
        for sub in range(here.outer // zones):
            for name in ("first", "down_b"):
                jobs[name].across(zone * (here.outer // zones) + sub).start()

    def model_terms(give_ref, keep_ref, right, senders):
        compute_terms(
            here, give_ref, keep_ref, model_left, right, model_tiles, by_zone, senders
        )

    load_keep.wait()
    load_give.wait()
    advance(PLAN[0])
    load_first.wait()
    load_second.wait()

    own = width // size
    slabs = 256 // own

    def dn2_body(first_w, second_w):
        lane = pl.ds(pl.multiple_of(pl.program_id(0) * 256, 256), 256)
        first_tile = first_w[...].reshape(256, units)
        second_tile = second_w[...].reshape(256, units)

        @pl.loop(0, 4)
        def _(index):
            part = pl.ds(pl.multiple_of(index * rows, rows), rows)
            total = contract_cols(first_r[part, :], first_tile)
            blocks = pl.ds(index * (here.outer // 4), here.outer // 4)
            second_rows = second_r[blocks].reshape(rows, units)
            total = total + contract_cols(second_rows, second_tile)
            lhs[part, lane] = total.astype(BF)

    slab = pl.BlockSpec((slabs, own, units), lambda t: (t, 0, 0))
    pltpu.emit_pipeline(dn2_body, grid=(width // 256,), in_specs=[slab, slab])(
        first_full, second_full
    )
    sum_mlp.send()
    middle_grad[...] = jnp.zeros_like(middle_grad)
    load_turned.wait()
    advance(PLAN[1])
    sum_mlp.pass_on()
    sum_mlp.add_near()
    load_act = load(act_hbm, first_r, 1)
    load_first_keep.wait()
    advance(PLAN[2])
    sum_mlp.add_far()

    load_middle.wait()
    load_dy.wait()
    gain_row[...] = jnp.zeros_like(gain_row)
    mlp_lane = slice(2 * HEAD_DIM, 2 * HEAD_DIM + width)
    attn_lane = slice(2 * HEAD_DIM + width, 2 * HEAD_DIM + 2 * width)
    narrow = 16

    @pl.loop(0, rows // narrow)
    def _(index):
        part = pl.ds(pl.multiple_of(index * narrow, narrow), narrow)
        values = grad_in[part, :]
        scales = lax.rsqrt(jnp.mean(values * values, axis=-1, keepdims=True) + EPSILON)
        normed = values * scales
        update = middle_grad[part, :]
        gain_row[:, mlp_lane] += jnp.sum(update * normed, axis=0, keepdims=True)
        upper = update * mlp_gain_ref[...]
        inner = jnp.mean(upper * normed, axis=-1, keepdims=True)
        grad = da_own[part, :].astype(F32) + scales * (upper - normed * inner)
        middle_grad[part, :] = grad
        da_own[part, :] = grad.astype(BF)

    da.send()
    advance(PLAN[3])
    model_terms(
        give.at[0],
        keep.at[2],
        lambda lane: second_r[:, :, :, lane].reshape(length, -1),
        [jobs["second"]],
    )
    advance(PLAN[4])

    def hidden_body(weight):
        lane = pl.ds(pl.multiple_of(pl.program_id(0) * 256, 256), 256)
        tile = weight[...]

        @pl.loop(0, 4)
        def _(index):
            part = pl.ds(pl.multiple_of(index * rows, rows), rows)
            lhs[part, lane] = dot(first_r[part, :], tile).astype(BF)

    load_act.wait()
    pltpu.emit_pipeline(
        hidden_body,
        grid=(width // 256,),
        in_specs=[pl.BlockSpec((units, 256), lambda t: (0, t))],
    )(down_full)
    da.mate_arrived()
    sum_hidden.send()
    da.forward()
    advance(PLAN[5])
    sum_hidden.pass_on()
    sum_hidden.add_near()
    advance(PLAN[6])
    da.rest_arrived()
    da.finish()
    load_lhs = load(da_hbm, lhs, 0)
    load_own = load(hidden_hbm, da_own, 2)
    load_lhs.wait()

    def dout_body(weight):
        lane = pl.ds(pl.multiple_of(pl.program_id(0) * 256, 256), 256)
        tile = weight[...].reshape(256, width)

        @pl.loop(0, 4)
        def _(index):
            part = pl.ds(pl.multiple_of(index * rows, rows), rows)
            dout_ref[part, lane] = contract_cols(lhs[part, :], tile).astype(BF)

    out_blocks, out_rows = out_full.shape[:2]
    pltpu.emit_pipeline(
        dout_body,
        grid=(out_blocks * out_rows // 256,),
        in_specs=[pl.BlockSpec((256 // out_rows, out_rows, width), lambda t: (t, 0, 0))],
    )(out_full)

    for head in range(heads):
        lane = slice(head * HEAD_DIM, (head + 1) * HEAD_DIM)
        turned[head] = contract_cols(eye[...], mixed_ref[:, lane]).astype(BF)
    compute_terms(
        here,
        give_out,
        keep_out,
        lambda group: turned[0:heads].reshape(heads * HEAD_DIM, length),
        lambda lane: lhs[:, lane],
        lambda group: [(zone, 0) for zone in range(heads)],
        [(0, zone_order)],
        [jobs["out"]],
    )
    load_turned = load(n1_hbm, turned, 0)
    sum_hidden.add_far()
    for index, peer in enumerate((here.mate, here.far)):
        pl.semaphore_signal(credit.at[index], inc=1, device_id=peer, device_id_type=MESH)

    @pl.loop(0, rows // 32)
    def _(index):
        part = pl.ds(pl.multiple_of(index * 32, 32), 32)
        pair[part, :] = grad_in[part, :].astype(BF)

    store_hidden = load(pair, hidden_out, 1)
    advance(PLAN[7])

    lse_t[...] = lse_ref[...].T[0:8]
    delta[...] = jnp.zeros_like(delta)
    for head in range(heads):
        lane = slice(head * HEAD_DIM, (head + 1) * HEAD_DIM)
        terms = dout_ref[:, lane].astype(F32) * mixed_ref[:, lane].astype(F32)
        delta[:, head : head + 1] = jnp.sum(terms, axis=-1, keepdims=True)
    delta_t[...] = delta[...].T[0:8]
    def through_norm(grad, head, part, gain_ref, which):
        proj = proj_buf[part, :]
        scales = lax.rsqrt(jnp.mean(proj * proj, axis=-1, keepdims=True) + EPSILON)
        normed = proj * scales
        grad = grad.astype(F32)
        upper = grad * cos_ref[part, :] - pltpu.roll(grad, HEAD_DIM // 2, 1) * sin_ref[part, :]
        gain_row[:, which * HEAD_DIM : (which + 1) * HEAD_DIM] += jnp.sum(
            upper * normed, axis=0, keepdims=True
        )
        upper = upper * gain_ref[...]
        inner = jnp.mean(upper * normed, axis=-1, keepdims=True)
        result = (scales * (upper - normed * inner)).astype(BF)
        first_r[part, head * HEAD_DIM : (head + 1) * HEAD_DIM] = result

    for head in range(heads):
        pair_head = head // 2
        load_proj = load(proj_hbm.at[head], proj_buf, 4)
        if head % 2 == 0:
            dk_sum[...] = jnp.zeros_like(dk_sum)
            dv_sum[...] = jnp.zeros_like(dv_sum)
            keys_turned[...] = contract_cols(eye[...], heads_ref[heads + pair_head]).astype(BF)
        for block in range(4):
            end = (block + 1) * rows
            part = pl.ds(block * rows, rows)
            queries = heads_ref[head, part, :]
            keys = heads_ref[heads + pair_head, 0:end, :]
            values = heads_ref[heads + kv_heads + pair_head, 0:end, :]
            out_grad = dout_ref[part, head * HEAD_DIM : (head + 1) * HEAD_DIM]
            scores = contract_cols(keys, queries)
            key_place = lax.broadcasted_iota(jnp.int32, (end, rows), 0)
            query_place = lax.broadcasted_iota(jnp.int32, (end, rows), 1) + block * rows
            allowed = (key_place >= start_ref[:, part]) & (key_place <= query_place)
            weights = jnp.exp(scores * scale - lse_t[head : head + 1, part])
            weights = jnp.where(allowed, weights, 0.0)
            weight_grad = contract_cols(values, out_grad)
            inner = delta_t[head : head + 1, part]
            score_grad = (weights * (weight_grad - inner)).astype(BF)
            dk_sum[0:end, :] += dot(score_grad, queries) * scale
            dv_sum[0:end, :] += dot(weights.astype(BF), out_grad)
            query_grad = dot(keys_turned[:, 0:end], score_grad).T
            query_grad = (query_grad * scale).astype(BF)
            if block == 0:
                load_proj.wait()
            through_norm(query_grad, head, part, query_gain_ref, 0)
        if head % 2:
            key = heads + pair_head
            value_at = (heads + kv_heads + pair_head) * HEAD_DIM
            load(proj_hbm.at[key], proj_buf, 4).wait()

            @pl.loop(0, 4)
            def _(index):
                part = pl.ds(pl.multiple_of(index * rows, rows), rows)
                through_norm(dk_sum[part, :].astype(BF), key, part, key_gain_ref, 1)
                first_r[part, value_at : value_at + HEAD_DIM] = dv_sum[part, :].astype(BF)

        advance(PLAN[8 + head])

    load_turned.wait()
    store_hidden.wait()
    proj_grads = first_r.at[:, 0:qkv_width]
    model_terms(
        give.at[1, :, :, :, 0:qkv_width],
        second_r.at[:, :, :, 0:qkv_width],
        first_columns,
        [jobs["query"], jobs["key"]],
    )
    advance(PLAN[12])

    def dn1_body(weight):
        lane = pl.ds(pl.multiple_of(pl.program_id(0) * 256, 256), 256)
        tile = weight[...].reshape(256, qkv_width)

        @pl.loop(0, 4)
        def _(index):
            part = pl.ds(pl.multiple_of(index * rows, rows), rows)
            lhs[part, lane] = contract_cols(proj_grads[part, :], tile).astype(BF)

    pltpu.emit_pipeline(
        dn1_body,
        grid=(width // 256,),
        in_specs=[pl.BlockSpec((slabs, own, qkv_width), lambda t: (t, 0, 0))],
    )(qkv_full)
    grad_in[...] = jnp.zeros_like(grad_in)
    pl.semaphore_wait(credit.at[0], 1)
    pl.semaphore_wait(credit.at[1], 1)
    sum_attn.send()
    advance(PLAN[13])
    sum_attn.pass_on()
    sum_attn.add_near()
    advance(PLAN[14])
    sum_attn.add_far()
    load_own.wait()

    @pl.loop(0, rows // narrow)
    def _(index):
        part = pl.ds(pl.multiple_of(index * narrow, narrow), narrow)
        values = da_own[part, :].astype(F32)
        scales = lax.rsqrt(jnp.mean(values * values, axis=-1, keepdims=True) + EPSILON)
        normed = values * scales
        update = grad_in[part, :]
        gain_row[:, attn_lane] += jnp.sum(update * normed, axis=0, keepdims=True)
        upper = update * attn_gain_ref[...]
        inner = jnp.mean(upper * normed, axis=-1, keepdims=True)
        grad_in[part, :] = middle_grad[part, :] + scales * (upper - normed * inner)

    gain_sum = GainSum(here, gain_row, gain_seq, gain_middle, gain_shard, (gss, gsr, gts, gtr))
    gain_sum.start()
    advance(PLAN[15])
    gain_sum.turn()
    advance(PLAN[16])
    gains_out[...] = gain_sum.finish()
    for spread_rows in spreads.values():
        spread_rows.arrive()
    for job in jobs.values():
        job.sent()
    for job in jobs.values():
        job.settle()
    for job in spreads.values():
        job.finish()


def backward(saved, weights, own, gains, tables, starts):
    size = lax.axis_size("shard")
    outer = size // 2
    (n1, n2, act, first, second, down_terms, first_terms, proj, heads_all, mixed, lse, middle) = saved
    length, width = heads_all.shape[1], middle.shape[1]
    piece = length // 4
    units = act.shape[2]
    qkv_width = weights[0].shape[2]
    rows = width // (4 * size)
    q_width = mixed.shape[1]

    def shape(*dims, kind=BF):
        return jax.ShapeDtypeStruct(dims, kind)

    results = [
        shape(piece, width, kind=F32),
        shape(1, 2 * width + 2 * HEAD_DIM, kind=F32),
        shape(1, rows, width, kind=F32),
        shape(piece, width),
        shape(4, rows, units),
        shape(4, rows, units),
        shape(4, rows, units),
        shape(4, rows, qkv_width),
        shape(length, width),
    ]
    results += [shape(3, outer, 4, rows, units)] * 3
    results += [shape(outer, 4, rows, units * 2 // 3)] * 2
    results += [shape(outer, 4, rows, qkv_width)] * 3
    results += [shape(outer, 1, rows, width)] * 3
    dma = pltpu.SemaphoreType.DMA
    vmem = pltpu.VMEM
    return pl.pallas_call(
        functools.partial(backward_kernel, size),
        out_shape=results,
        in_specs=[ANY] * 8 + [VMEM] * 3 + [ANY] * 8 + [VMEM] * 7,
        out_specs=[VMEM] * 3 + [ANY] * (len(results) - 3),
        scratch_shapes=[
            vmem((length, width), BF),
            vmem((width // 128, 128, length), BF),
            vmem((length, units), BF),
            vmem((outer, 4, rows, units), BF),
            vmem((3, outer, 4, rows, units), BF),
            vmem((3, outer, 4, rows, units), BF),
            vmem((outer, 1, rows, width), BF),
            vmem((outer, 1, rows, width), BF),
            vmem((2, 4, rows, units), BF),
            vmem((2, 1, rows, width), BF),
            vmem((length, q_width), BF),
            vmem((piece, width), BF),
            vmem((2, piece, width), BF),
            vmem((piece, width), BF),
            vmem((piece, width), BF),
            vmem((piece, width), F32),
            vmem((length, HEAD_DIM), F32),
            vmem((HEAD_DIM, HEAD_DIM), BF),
            vmem((HEAD_DIM, length), BF),
            vmem((8, length), F32),
            vmem((length, 128), F32),
            vmem((8, length), F32),
            vmem((length, HEAD_DIM), F32),
            vmem((length, HEAD_DIM), F32),
            vmem((1, 2 * width + 2 * HEAD_DIM), F32),
            vmem((4, 1, 2 * width + 2 * HEAD_DIM), F32),
            vmem((1, 2 * width + 2 * HEAD_DIM), F32),
            vmem((size, 1, 2 * width + 2 * HEAD_DIM), F32),
            dma((8, outer)),
            dma((8, outer)),
            dma((8, outer)),
            dma((8, outer)),
            dma((8, outer)),
            dma((8, outer)),
            dma((8, 3)),
            dma((6, 3)),
            dma((6, 3)),
            dma((6,)),
            dma((3, 3)),
            dma((3, 3)),
            dma((3,)),
            dma((3,)),
            dma((1,)),
            dma((3,)),
            dma((3,)),
            dma((size - 1,)),
            dma((size - 1,)),
            dma((8,)),
            pltpu.SemaphoreType.REGULAR((2,)),
        ],
        compiler_params=pltpu.CompilerParams(
            collective_id=1, has_side_effects=True, vmem_limit_bytes=VMEM_BYTES
        ),
        name="backward_sums",
    )(
        n1,
        n2,
        act.reshape(length, units),
        first.reshape(length, units),
        second.reshape(outer, 4, rows, units),
        down_terms,
        first_terms,
        proj,
        heads_all,
        mixed,
        lse,
        middle,
        *own,
        *weights,
        *gains,
        *tables,
        starts,
    )


def finish_kernel(
    size,
    grad_in,
    gains,
    grad_out,
    hidden_out,
    down_rows,
    first_rows,
    second_rows,
    qkv_rows,
    grad_in_out,
    grad_out_out,
    hidden_out_out,
    grad_query,
    grad_key,
    grad_value,
    grad_gate,
    grad_up,
    grad_down,
    attn_gain,
    mlp_gain,
    query_gain,
    key_gain,
    grad_in_buf,
    grad_out_buf,
    hidden_buf,
    down_buf,
    first_buf,
    second_buf,
    qkv_buf,
    query_buf,
    key_buf,
    value_buf,
    gate_buf,
    up_buf,
    wide_buf,
    load_sems,
    store_sems,
):
    units = down_buf.shape[2]
    chunk = units // 2
    ff_part = units // size
    most, tail = chunk - 256, 256
    stores = []

    def load(source, target, index):
        copy = pltpu.make_async_copy(source, target, load_sems.at[index])
        copy.start()
        return copy

    def store(source, target):
        copy = pltpu.make_async_copy(source, target, store_sems.at[len(stores)])
        copy.start()
        stores.append(copy)

    loads = [
        load(source, target, index)
        for index, (source, target) in enumerate(
            (
                (down_rows, down_buf),
                (first_rows, first_buf),
                (second_rows, second_buf),
                (qkv_rows, qkv_buf),
                (grad_in, grad_in_buf),
                (hidden_out, hidden_buf),
                (grad_out, grad_out_buf),
            )
        )
    ]

    def place(read, target):
        @pl.loop(0, target.shape[0] // 16)
        def _(index):
            part = pl.ds(pl.multiple_of(index * 16, 16), 16)
            values = [read(seq, part).astype(F32) for seq in range(4)]
            for begin in range(0, size, size // 8):
                pieces = [
                    values[seq][:, block * ff_part : (block + 1) * ff_part]
                    for block in range(begin, begin + size // 8)
                    for seq in range(4)
                ]
                lane = slice(begin * 4 * ff_part, (begin + size // 8) * 4 * ff_part)
                target[part, lane] = jnp.concatenate(pieces, axis=1)

    def side(index):
        at = 2 * most + index * tail

        def read(seq, part):
            return jnp.concatenate(
                [
                    first_buf[seq, part, index * chunk : (index + 1) * chunk],
                    second_buf[seq, part, index * most : (index + 1) * most],
                    second_buf[seq, part, at : at + tail],
                ],
                axis=1,
            )

        return read

    loads[0].wait()
    place(lambda seq, part: down_buf[seq, part, :], wide_buf)
    store(wide_buf, grad_down)
    loads[1].wait()
    loads[2].wait()
    place(side(0), gate_buf)
    store(gate_buf, grad_gate)
    place(side(1), up_buf)
    store(up_buf, grad_up)
    loads[4].wait()
    store(grad_in_buf, grad_in_out)
    loads[5].wait()
    store(hidden_buf, hidden_out_out)
    loads[6].wait()
    store(grad_out_buf, grad_out_out)
    loads[3].wait()
    at = 0
    for buf, target in ((query_buf, grad_query), (key_buf, grad_key), (value_buf, grad_value)):
        count = buf.shape[1] // 4
        for seq in range(4):
            buf[:, seq * count : (seq + 1) * count] = qkv_buf[seq, :, at : at + count].astype(F32)
        at += count
        store(buf, target)
    at = 0
    for target in (query_gain, key_gain, mlp_gain, attn_gain):
        target[...] = gains[:, at : at + target.shape[1]]
        at += target.shape[1]
    for copy in stores:
        copy.wait()


def finish(grad_in, gains, grad_out, hidden_out, down_rows, first_rows, second_rows, qkv_rows):
    size = lax.axis_size("shard")
    piece, width = grad_in.shape
    rows, units = down_rows.shape[1:]
    qkv_width = qkv_rows.shape[2]

    def shape(*dims, kind=F32):
        return jax.ShapeDtypeStruct(dims, kind)

    results = [
        shape(piece, width),
        shape(1, rows, width),
        shape(piece, width, kind=BF),
        shape(rows, 2 * qkv_width),
        shape(rows, qkv_width),
        shape(rows, qkv_width),
        shape(rows, 4 * units),
        shape(rows, 4 * units),
        shape(rows, 4 * units),
        shape(1, width),
        shape(1, width),
        shape(1, HEAD_DIM),
        shape(1, HEAD_DIM),
    ]
    return pl.pallas_call(
        functools.partial(finish_kernel, size),
        out_shape=results,
        in_specs=[ANY, VMEM] + [ANY] * 6,
        out_specs=[ANY] * 9 + [VMEM] * 4,
        scratch_shapes=[
            pltpu.VMEM((piece, width), F32),
            pltpu.VMEM((1, rows, width), F32),
            pltpu.VMEM((piece, width), BF),
            pltpu.VMEM((4, rows, units), BF),
            pltpu.VMEM((4, rows, units), BF),
            pltpu.VMEM((4, rows, units), BF),
            pltpu.VMEM((4, rows, qkv_width), BF),
            pltpu.VMEM((rows, 2 * qkv_width), F32),
            pltpu.VMEM((rows, qkv_width), F32),
            pltpu.VMEM((rows, qkv_width), F32),
            pltpu.VMEM((rows, 4 * units), F32),
            pltpu.VMEM((rows, 4 * units), F32),
            pltpu.VMEM((rows, 4 * units), F32),
            pltpu.SemaphoreType.DMA((7,)),
            pltpu.SemaphoreType.DMA((9,)),
        ],
        compiler_params=pltpu.CompilerParams(vmem_limit_bytes=VMEM_BYTES),
        name="finish",
    )(grad_in, gains, grad_out, hidden_out, down_rows, first_rows, second_rows, qkv_rows)


def local(
    hidden_in,
    segment_ids,
    norm_attn_gain,
    w_query,
    w_key,
    w_value,
    query_gain,
    key_gain,
    w_out,
    norm_mlp_gain,
    w_gate,
    w_up,
    w_down,
    out_cotangent,
):
    segment = segment_ids[0]
    gains = (norm_attn_gain[None], norm_mlp_gain[None], query_gain[None], key_gain[None])
    results = forward(
        hidden_in[0],
        out_cotangent[0],
        (w_query, w_key, w_value, w_out, w_gate, w_up, w_down),
        gains,
        segment,
    )
    (
        grad_in,
        grad_out,
        hidden_out,
        grad_query,
        grad_key,
        grad_value,
        grad_gate,
        grad_up,
        grad_down,
        attn_gain,
        mlp_gain,
        query_grad,
        key_grad,
    ) = finish(
        *backward(
            results[8:9] + results[10:21],
            results[:5],
            (hidden_in[0], out_cotangent[0]),
            gains,
            results[21:23],
            results[23],
        )[:8]
    )
    return (
        hidden_out[None],
        grad_in[None],
        attn_gain[0],
        grad_query,
        grad_key,
        grad_value,
        query_grad[0],
        key_grad[0],
        grad_out[0],
        mlp_gain[0],
        grad_gate,
        grad_up,
        grad_down.T,
    )


def solution(mesh):
    return jax.shard_map(
        local,
        mesh=mesh,
        in_specs=(
            P("shard", "seq", None),
            P("shard", None),
            P(),
            P("shard", None),
            P("shard", None),
            P("shard", None),
            P(),
            P(),
            P("shard", None),
            P(),
            P("shard", None),
            P("shard", None),
            P("shard", None),
            P("shard", "seq", None),
        ),
        out_specs=(
            P("shard", "seq", None),
            P("shard", "seq", None),
            P(),
            P(("seq", "shard"), None),
            P(("seq", "shard"), None),
            P(("seq", "shard"), None),
            P(),
            P(),
            P(("seq", "shard"), None),
            P(),
            P(("seq", "shard"), None),
            P(("seq", "shard"), None),
            P(None, ("seq", "shard")),
        ),
        check_vma=False,
    )
```

```python
import functools

import jax
import jax.numpy as jnp
import numpy as np
from jax import lax
from jax.experimental import pallas as pl
from jax.experimental.pallas import tpu as pltpu
from jax.sharding import PartitionSpec as P

Q_HEADS = 16
KV_HEADS = 8
HEAD_DIM = 128
EPSILON = 1e-06
ROPE_BASE = 1000000.0
NEGATIVE = -1e30
BF = jnp.bfloat16
F32 = jnp.float32
MESH = pl.DeviceIdType.MESH
ANY = pl.BlockSpec(memory_space=pl.ANY)
VMEM = pl.BlockSpec(memory_space=pltpu.VMEM)
VMEM_BYTES = 62 * 1024 * 1024


def dot(left, right):
    return jnp.dot(left, right, preferred_element_type=F32)


def contract_cols(left, right):
    return lax.dot_general(left, right, (((1,), (1,)), ((), ())), preferred_element_type=F32)


class Place:
    def __init__(self, size):
        self.size = size
        self.outer = size // 2
        self.quarter = size // 4
        self.seq = lax.axis_index("seq")
        self.shard = lax.axis_index("shard")
        self.chip = self.seq // 2
        self.core = lax.rem(self.seq, 2)
        self.place = self.shard // 2
        self.half = lax.rem(self.shard, 2)
        self.far_seq = lax.rem(self.seq + 2, 4)
        self.mate_seq = self.chip * 2 + 1 - self.core
        self.far = {"seq": self.far_seq}
        self.mate = {"seq": self.mate_seq}
        self.twin_shard = self.place * 2 + 1 - self.half
        self.twin = {"shard": self.twin_shard}

    def outer_peer(self, place):
        return {"shard": place * 2 + self.half}

    def greet(self, wide=False):
        barrier = pltpu.get_barrier_semaphore()
        last = self.outer - 1

        def signal(peer):
            pl.semaphore_signal(barrier, inc=1, device_id=peer, device_id_type=MESH)

        signal(self.far)
        signal(self.mate)
        if wide:
            signal({"seq": 3 - self.seq})
            for amount in range(1, self.size):
                signal({"shard": lax.rem(self.shard + amount, self.size)})
            pl.semaphore_wait(barrier, 2 + self.size)
            return
        signal(self.twin)

        @pl.when(self.place < last)
        def _():
            signal(self.outer_peer(self.place + 1))

        @pl.when(self.place > 0)
        def _():
            signal(self.outer_peer(self.place - 1))

        inner = ((self.place > 0) & (self.place < last)).astype(jnp.int32)
        pl.semaphore_wait(barrier, 4 + inner)


def remote(source, target, send, receive, peer):
    return pltpu.make_async_remote_copy(
        src_ref=source,
        dst_ref=target,
        send_sem=send,
        recv_sem=receive,
        device_id=peer,
        device_id_type=MESH,
    )


class LineGather:
    def __init__(self, here, own, slot, sems):
        self.here, self.own, self.slot = here, own, slot
        self.us, self.ur, self.ds, self.dr = sems
        self.last = here.outer - 1

    def up(self, distance):
        here = self.here
        slot = self.slot(here.place - distance)
        source = slot if distance else self.own
        peer = here.outer_peer(here.place + 1)
        return remote(source, slot, self.us.at[distance], self.ur.at[distance], peer)

    def down(self, distance):
        here = self.here
        slot = self.slot(here.place + distance)
        source = slot if distance else self.own
        peer = here.outer_peer(here.place - 1)
        return remote(source, slot, self.ds.at[distance], self.dr.at[distance], peer)

    def send(self):
        here = self.here

        @pl.when(here.place < self.last)
        def _():
            self.up(0).start()

        @pl.when(here.place > 0)
        def _():
            self.down(0).start()

    def step(self, distance, arrived=lambda place: None):
        here = self.here
        below = here.place - 1 - distance
        above = here.place + 1 + distance

        @pl.when(below >= 0)
        def _():
            slot = self.slot(below)
            remote(slot, slot, self.us.at[0], self.ur.at[distance], here.twin).wait_recv()

            @pl.when(here.place < self.last)
            def _():
                self.up(distance + 1).start()

            arrived(below)

        @pl.when(above <= self.last)
        def _():
            slot = self.slot(above)
            remote(slot, slot, self.ds.at[0], self.dr.at[distance], here.twin).wait_recv()

            @pl.when(here.place > 0)
            def _():
                self.down(distance + 1).start()

            arrived(above)

    def finish(self):
        here = self.here
        for distance in range(self.last):

            @pl.when((here.place - distance >= 0) & (here.place < self.last))
            def _():
                self.up(distance).wait_send()

            @pl.when((here.place + distance <= self.last) & (here.place > 0))
            def _():
                self.down(distance).wait_send()


class RowGather:
    def __init__(self, here, own, whole, sems, spot=lambda shard: shard):
        self.here, self.own, self.whole, self.spot = here, own, whole, spot
        self.ys, self.yr, self.local = sems[4:]
        self.line = LineGather(here, own, self.mine, sems[:4])

    def mine(self, place):
        return self.whole.at[self.spot(place * 2 + self.here.half)]

    def theirs(self, place):
        return self.whole.at[self.spot(place * 2 + 1 - self.here.half)]

    def keep(self):
        return pltpu.make_async_copy(self.own, self.mine(self.here.place), self.local)

    def across(self, place, own=False):
        slot = self.mine(place)
        source = self.own if own else slot
        return remote(source, slot, self.ys.at[place], self.yr.at[place], self.here.twin)

    def arrived(self, place):
        slot = self.theirs(place)
        remote(slot, slot, self.ys.at[place], self.yr.at[place], self.here.twin).wait_recv()

    def send(self):
        self.line.send()
        self.across(self.here.place, own=True).start()
        self.keep().start()

    def step(self, distance):
        self.line.step(distance, lambda place: self.across(place).start())

    def arrive(self):
        self.keep().wait()
        for place in range(self.here.outer):
            self.arrived(place)

    def finish(self):
        self.line.finish()
        for place in range(self.here.outer):
            self.across(place).wait_send()


class TwinFirstGather(RowGather):
    def __init__(self, here, own, whole, sems, twin_sems):
        super().__init__(here, own, whole, sems)
        self.lines = [
            self.line,
            LineGather(here, self.theirs(here.place), self.theirs, twin_sems[:4]),
        ]

    def twin(self):
        self.arrived(self.here.place)
        self.lines[1].send()

    def step(self, distance):
        for line in self.lines:
            line.step(distance)

    def arrive(self):
        self.keep().wait()

    def finish(self):
        for line in self.lines:
            line.finish()
        self.across(self.here.place, own=True).wait_send()


class HeadGather:
    def __init__(self, here, own, whole, sems):
        self.here, self.own, self.whole = here, own, whole
        self.us, self.zr, self.ds, _, self.ys, self.yr, self.local = sems
        self.last = here.outer - 1
        self.count = here.quarter // 2
        self.first = here.seq * self.count
        self.mine = here.place - self.first
        self.inside = (self.mine >= 0) & (self.mine < self.count)

    def slot(self, index):
        return self.whole.at[index * 2 + self.here.half]

    def keep(self):
        return pltpu.make_async_copy(self.own, self.slot(self.mine), self.local)

    def up(self, index, own=False):
        slot = self.slot(index)
        peer = self.here.outer_peer(self.here.place + 1)
        return remote(self.own if own else slot, slot, self.us.at[index], self.zr.at[index], peer)

    def down(self, index, own=False):
        slot = self.slot(index)
        peer = self.here.outer_peer(self.here.place - 1)
        return remote(self.own if own else slot, slot, self.ds.at[index], self.zr.at[index], peer)

    def across(self, index):
        slot = self.slot(index)
        return remote(slot, slot, self.ys.at[index], self.yr.at[index], self.here.twin)

    def send(self):
        @pl.when(self.inside)
        def _():
            self.keep().start()

            @pl.when(self.here.place < self.last)
            def _():
                self.up(self.mine, own=True).start()

            @pl.when(self.here.place > 0)
            def _():
                self.down(self.mine, own=True).start()

    def step(self):
        here = self.here

        @pl.when(self.inside)
        def _():
            self.keep().wait()

        for index in range(self.count):
            slot = self.slot(index)
            arrival = remote(slot, slot, self.us.at[0], self.zr.at[index], here.twin)

            @pl.when(self.mine > index)
            def _():
                arrival.wait_recv()

                @pl.when(here.place < self.last)
                def _():
                    self.up(index).start()

            @pl.when(self.mine < index)
            def _():
                arrival.wait_recv()

                @pl.when(here.place > 0)
                def _():
                    self.down(index).start()

            self.across(index).start()

    def arrive(self):
        for index in range(self.count):
            slot = self.whole.at[index * 2 + 1 - self.here.half]
            remote(
                slot, slot, self.ys.at[index], self.yr.at[index], self.here.twin
            ).wait_recv()

    def finish(self):
        here = self.here
        for index in range(self.count):

            @pl.when((self.mine >= index) & (here.place < self.last))
            def _():
                self.up(index).wait_send()

            @pl.when((self.mine <= index) & (here.place > 0))
            def _():
                self.down(index).wait_send()

            self.across(index).wait_send()


class TokenGather:
    def __init__(self, here, own, whole, sems):
        self.here, self.own, self.whole = here, own, whole
        self.send_sems, self.recv_sems, self.local = sems
        self.rows = whole.shape[0] // 4

    def slot(self, seq):
        return self.whole.at[pl.ds(pl.multiple_of(seq * self.rows, self.rows), self.rows), :]

    def keep(self):
        return pltpu.make_async_copy(self.own, self.slot(self.here.seq), self.local)

    def copy(self, index):
        here = self.here
        slot = self.slot(here.far_seq if index == 2 else here.seq)
        return remote(
            slot if index == 2 else self.own,
            slot,
            self.send_sems.at[index],
            self.recv_sems.at[index],
            here.far if index == 0 else here.mate,
        )

    def send(self):
        self.copy(0).start()
        self.copy(1).start()
        self.keep().start()

    def forward(self):
        self.copy(0).wait_recv()
        self.copy(2).start()

    def mate_arrived(self):
        self.copy(1).wait_recv()

    def rest_arrived(self):
        self.copy(2).wait_recv()
        self.keep().wait()

    def arrive(self):
        self.mate_arrived()
        self.rest_arrived()

    def finish(self):
        for index in range(3):
            self.copy(index).wait_send()


class PieceSum:
    def __init__(self, here, piece, base, give, got, pair, far_got, sems, step):
        self.here, self.piece, self.base, self.step = here, piece, base, step
        self.give, self.got, self.pair, self.far_got = give, got, pair, far_got
        self.send_sems, self.recv_sems = sems

    def to_mate(self, index):
        return remote(
            self.give.at[index],
            self.got.at[index],
            self.send_sems.at[index],
            self.recv_sems.at[index],
            self.here.mate,
        )

    def to_far(self):
        return remote(
            self.pair, self.far_got, self.send_sems.at[2], self.recv_sems.at[2], self.here.far
        )

    def columns(self, body):
        step = self.step

        @pl.loop(0, self.pair.shape[1] // step)
        def _(index):
            body(pl.ds(pl.multiple_of(index * step, step), step))

    def send(self):
        here = self.here
        for index, chip in enumerate((1 - here.chip, here.chip)):
            seq = chip * 2 + 1 - here.core

            def fill(column, index=index, seq=seq):
                self.give[index, :, column] = self.piece(seq, column).astype(BF)

            self.columns(fill)
            self.to_mate(index).start()

    def pass_on(self):
        self.to_mate(0).wait_recv()

        def fill(column):
            term = self.piece(self.here.far_seq, column) + self.got[0, :, column].astype(F32)
            self.pair[:, column] = term.astype(BF)

        self.columns(fill)
        self.to_far().start()

    def add_near(self):
        self.to_mate(1).wait_recv()

        def fill(column):
            term = self.piece(self.here.seq, column) + self.got[1, :, column].astype(F32)
            self.base[:, column] += term

        self.columns(fill)

    def add_far(self):
        self.to_far().wait_recv()

        def fill(column):
            self.base[:, column] += self.far_got[:, column].astype(F32)

        self.columns(fill)
        for copy in (self.to_mate(0), self.to_mate(1), self.to_far()):
            copy.wait_send()


def identity(size):
    rows = lax.broadcasted_iota(jnp.int32, (size, size), 0)
    columns = lax.broadcasted_iota(jnp.int32, (size, size), 1)
    return jnp.where(rows == columns, 1.0, 0.0).astype(BF)


FORWARD_PLAN = (
    (("down", "send"),),
    (),
    (),
    (("down", 0), ("out", "send"),),
    (("second", "send"),),
    (),
    (("down", 1),),
    (("down", 2),),
    (),
    (("out", 0),),
    (("first", "send"),),
    (),
    (),
    (("third", "send"), ("first", 0),),
    (("second", "twin"),),
    (("first", 1), ("second", 0),),
    (("first", 2),),
    (("third", 0),),
    (("second", 1),),
    (("third", 1),),
    (("second", 2), ("third", 2),),
    (),
    (),
)


def forward_kernel(
    size,
    hidden_ref,
    dy_hbm,
    w_query,
    w_key,
    w_value,
    w_out,
    w_gate,
    w_up,
    w_down,
    attn_gain_ref,
    mlp_gain_ref,
    query_gain_ref,
    key_gain_ref,
    inverse_ref,
    segment_ref,
    qkv_full,
    out_full,
    first_full,
    second_full,
    down_full,
    n1_full,
    dy_full,
    n2_full,
    n1_turned,
    dy_turned,
    n2_turned,
    act_out,
    first_pair,
    second_pair,
    proj_ref,
    heads_ref,
    mixed_ref,
    lse_ref,
    middle_ref,
    cos_ref,
    sin_ref,
    start_row,
    lhs,
    dy_all,
    turned,
    qkv_w,
    out_w,
    qkv_own,
    out_own,
    down_own,
    dy_own,
    wide_own,
    first_own,
    second_own,
    own_rows,
    give,
    got,
    pair,
    far_got,
    us,
    ur,
    ds,
    dr,
    ys,
    yr,
    row_local,
    ts,
    tr,
    token_local,
    load_sem,
    ss,
    sr,
    start_ref,
    turned_ids,
    eye,
):
    here = Place(size)
    last = here.outer - 1
    length, width = lhs.shape
    lse_ref[...] = jnp.zeros_like(lse_ref)
    rows = length // 4
    units = act_out.shape[1]
    chunk = units // 2
    tail = 256
    heads = mixed_ref.shape[1] // HEAD_DIM
    kv_heads = heads // 2
    ff_part = units // size

    def sems(index):
        return tuple(kind.at[index] for kind in (us, ur, ds, dr, ys, yr, row_local))

    down_rows = pl.ds(pl.multiple_of(here.seq * ff_part, ff_part), ff_part)
    qkv = RowGather(here, qkv_own, qkv_full, sems(0))
    out = HeadGather(here, out_own, out_full, sems(1))
    down = RowGather(
        here,
        down_own,
        down_full,
        sems(2),
        lambda shard: pl.ds(pl.multiple_of(shard * ff_part, ff_part), ff_part),
    )
    first = RowGather(here, first_own, first_full, sems(3))
    cut = 2 * (chunk - tail)
    second = TwinFirstGather(
        here, second_own.at[:, 0:cut], second_full.at[:, :, 0:cut], sems(4), sems(6)
    )
    third = RowGather(
        here, second_own.at[:, cut : 2 * chunk], second_full.at[:, :, cut : 2 * chunk], sems(5)
    )
    n1 = TokenGather(here, own_rows.at[0], n1_full, (ts.at[0], tr.at[0], token_local.at[0]))
    n2 = TokenGather(here, own_rows.at[1], n2_full, (ts.at[1], tr.at[1], token_local.at[1]))
    dy = TokenGather(here, dy_own, dy_full, (ts.at[2], tr.at[2], token_local.at[2]))

    loads = []
    at = 0
    for index, (weight, count) in enumerate(((w_query, heads), (w_key, kv_heads), (w_value, kv_heads))):
        count = count * HEAD_DIM
        source = weight.at[:, pl.ds(pl.multiple_of(here.seq * count, count), count)]
        loads.append(
            pltpu.make_async_copy(source, qkv_own.at[:, at : at + count], load_sem.at[index])
        )
        at += count
    loads.append(pltpu.make_async_copy(w_down.at[down_rows, :], down_own, load_sem.at[3]))
    loads.append(pltpu.make_async_copy(w_out, out_own, load_sem.at[4]))
    loads.append(pltpu.make_async_copy(dy_hbm, dy_own, load_sem.at[5]))
    loads.append(pltpu.make_async_copy(w_gate, wide_own, load_sem.at[6]))
    for load in loads:
        load.start()
    here.greet()
    for load in loads[:3]:
        load.wait()
    qkv.send()
    loads[5].wait()
    dy.send()

    def norm_rows(source, gain_ref, target):
        @pl.loop(0, rows // 32)
        def _(index):
            part = pl.ds(pl.multiple_of(index * 32, 32), 32)
            values = source[part, :].astype(F32)
            scales = lax.rsqrt(jnp.mean(values * values, axis=-1, keepdims=True) + EPSILON)
            target[part, :] = (values * scales * gain_ref[...]).astype(BF)

    gathers = {"out": out, "down": down, "first": first, "second": second, "third": third}

    def advance(steps):
        for name, step in steps:
            gather = gathers[name]
            if step == "send":
                gather.send()
            elif step == "twin":
                gather.twin()
            elif name == "out":
                gather.step()
            else:
                for distance in range(last * step // 3, last * (step + 1) // 3):
                    gather.step(distance)

    norm_rows(hidden_ref, attn_gain_ref, own_rows.at[0])
    n1.send()
    for load in loads[3:5]:
        load.wait()
    advance(FORWARD_PLAN[0])
    for load in loads[6:]:
        load.wait()

    most = chunk - tail

    def cut_units(side):
        for seq in range(4):

            @pl.when(here.seq == seq)
            def _():
                @pl.loop(0, wide_own.shape[0] // 16)
                def _(index):
                    part = pl.ds(pl.multiple_of(index * 16, 16), 16)

                    def gathered(begin):
                        pieces = [
                            wide_own[part, (block * 4 + seq) * ff_part : (block * 4 + seq + 1) * ff_part]
                            for block in range(begin, begin + size // 2)
                        ]
                        return jnp.concatenate(pieces, axis=1)

                    first_own[part, side * chunk : (side + 1) * chunk] = gathered(0)
                    rest = gathered(size // 2)
                    second_own[part, side * most : (side + 1) * most] = rest[:, 0:most]
                    at = 2 * most + side * tail
                    second_own[part, at : at + tail] = rest[:, most:]

    eye[...] = identity(256)

    def rotation():
        ids = segment_ref[...].astype(F32)
        turned_ids[...] = jnp.broadcast_to(ids, (128, length)).T
        lane = lax.broadcasted_iota(jnp.int32, (128, 128), 1)

        @pl.loop(0, length // 128)
        def _(index):
            part = pl.ds(pl.multiple_of(index * 128, 128), 128)
            own_ids = turned_ids[part, :]
            count = jnp.zeros((128, 128), F32)
            for at in range(0, length, 128):
                count = count + jnp.where(
                    segment_ref[:, at : at + 128].astype(F32) < own_ids, 1.0, 0.0
                )
            starts = jnp.sum(count, axis=-1, keepdims=True)
            start_ref[part, :] = starts.astype(jnp.int32)
            starts = jnp.broadcast_to(starts, (128, 128))
            turned_ids[part, :] = starts
            places = lax.broadcasted_iota(jnp.int32, (128, 128), 0) + index * 128
            angles = (places.astype(F32) - starts) * inverse_ref[...]
            cos_ref[part, :] = jnp.cos(angles)
            sine = jnp.sin(angles)
            sin_ref[part, :] = jnp.where(lane < HEAD_DIM // 2, -sine, sine)

        start_row[...] = turned_ids[...].T[0:1].astype(jnp.int32)

    zones = width // 512

    def turn(source, target):
        for seq_group in range(4):
            for zone in range(0, zones, 2):
                at = (seq_group * zones + zone) * 128
                both = contract_cols(eye[...], source[:, at : at + 256]).astype(BF)
                turned[zone * 4 + seq_group] = both[0:128]
                turned[zone * 4 + 4 + seq_group] = both[128:256]
        copy = pltpu.make_async_copy(turned, target, load_sem.at[4])
        copy.start()
        return copy

    cut_units(0)
    load_up = pltpu.make_async_copy(w_up, wide_own, load_sem.at[7])
    load_up.start()
    load_up.wait()
    cut_units(1)
    advance(FORWARD_PLAN[1])
    for third_part in range(3):
        for distance in range(last * third_part // 3, last * (third_part + 1) // 3):
            qkv.step(distance)
        advance(FORWARD_PLAN[2 + third_part])
        if third_part == 0:
            rotation()
            dy.forward()
    dy.arrive()
    load_dy = pltpu.make_async_copy(dy_full, dy_all, load_sem.at[0])
    load_dy.start()
    load_dy.wait()
    store = turn(dy_all, dy_turned)
    n1.forward()
    advance(FORWARD_PLAN[5])
    n1.arrive()
    load_lhs = pltpu.make_async_copy(n1_full, lhs, load_sem.at[0])
    load_lhs.start()
    advance(FORWARD_PLAN[6])
    qkv.arrive()
    load_qkv = pltpu.make_async_copy(qkv_full, qkv_w, load_sem.at[1])
    load_qkv.start()
    advance(FORWARD_PLAN[7])
    load_lhs.wait()
    load_qkv.wait()

    def project(tile):
        weight = qkv_w[:, :, tile * 256 : tile * 256 + 256].reshape(width, 256)
        gain_ref = query_gain_ref if tile < heads // 2 else key_gain_ref

        @pl.loop(0, 2)
        def _(index):
            part = pl.ds(pl.multiple_of(index * 2 * rows, 2 * rows), 2 * rows)
            both = dot(lhs[part, :], weight)
            for side in range(2):
                head = tile * 2 + side
                proj = both[:, side * HEAD_DIM : (side + 1) * HEAD_DIM]
                if head >= heads + kv_heads:
                    heads_ref[head, part, :] = proj.astype(BF)
                    continue
                proj_ref[head, part, :] = proj
                scales = lax.rsqrt(jnp.mean(proj * proj, axis=-1, keepdims=True) + EPSILON)
                gained = proj * scales * gain_ref[...]
                turned = pltpu.roll(gained, HEAD_DIM // 2, 1)
                heads_ref[head, part, :] = (
                    gained * cos_ref[part, :] + turned * sin_ref[part, :]
                ).astype(BF)

    def attend(head):
        pair_head = head // 2
        for block in range(4):
            end = (block + 1) * rows
            part = pl.ds(block * rows, rows)
            scores = contract_cols(
                heads_ref[head, part, :], heads_ref[heads + pair_head, 0:end, :]
            )
            row_place = lax.broadcasted_iota(jnp.int32, (rows, end), 0) + block * rows
            col_place = lax.broadcasted_iota(jnp.int32, (rows, end), 1)
            allowed = (col_place >= start_ref[part, :]) & (col_place <= row_place)
            raised = jnp.where(allowed, jnp.exp(scores * (HEAD_DIM ** (-0.5))), 0.0)
            sums = jnp.sum(raised, axis=-1, keepdims=True)
            mixed = dot(raised.astype(BF), heads_ref[heads + kv_heads + pair_head, 0:end, :])
            mixed = mixed * (1.0 / sums)
            mixed_ref[part, head * HEAD_DIM : (head + 1) * HEAD_DIM] = mixed.astype(BF)
            lse_ref[part, head : head + 1] = jnp.log(sums)

    tiles = (heads + 2 * kv_heads) // 2
    for tile in range(tiles):
        if tile == tiles // 2:
            advance(FORWARD_PLAN[8])
        project(tile)
    advance(FORWARD_PLAN[9])

    for head in range(heads):
        attend(head)
        advance(FORWARD_PLAN[10 + head])
    out.arrive()
    load_out = pltpu.make_async_copy(out_full, out_w, load_sem.at[2])
    load_out.start()
    load_out.wait()

    def out_piece(seq, column):
        part = pl.ds(pl.multiple_of(seq * rows, rows), rows)
        weight = out_w[:, :, column]
        return dot(mixed_ref[part, :], weight.reshape(-1, weight.shape[-1]))

    middle_ref[...] = hidden_ref[...].astype(F32)
    token_sum = PieceSum(
        here, out_piece, middle_ref, give, got, pair, far_got, (ss, sr), 512
    )
    token_sum.send()
    advance(FORWARD_PLAN[14])
    token_sum.pass_on()
    token_sum.add_near()
    advance(FORWARD_PLAN[15])
    token_sum.add_far()
    norm_rows(middle_ref, mlp_gain_ref, own_rows.at[1])
    n2.send()
    advance(FORWARD_PLAN[16])
    store.wait()
    store = turn(lhs, n1_turned)
    advance(FORWARD_PLAN[17])
    n2.forward()
    advance(FORWARD_PLAN[18])
    n2.arrive()
    load_lhs = pltpu.make_async_copy(n2_full, lhs, load_sem.at[3])
    load_lhs.start()
    down.arrive()
    first.arrive()
    load_lhs.wait()

    def feed(gather, begin, count):
        tiles = count // 256
        spot = begin // 256

        def body(gate_w, up_w, down_w, act_ref, gate_grad, up_grad):
            gate_tile = gate_w[...].reshape(width, 256)
            up_tile = up_w[...].reshape(width, 256)
            down_tile = down_w[...]

            @pl.loop(0, 2)
            def _(index):
                part = pl.ds(pl.multiple_of(index * 2 * rows, 2 * rows), 2 * rows)
                gate = dot(lhs[part, :], gate_tile)
                up = dot(lhs[part, :], up_tile)
                act_grad = contract_cols(dy_all[part, :], down_tile)
                sigmoid = jax.nn.sigmoid(gate)
                silu = gate * sigmoid
                act_ref[part, :] = (silu * up).astype(BF)
                gate_grad[part, :] = (
                    act_grad * up * sigmoid * (1.0 + gate * (1.0 - sigmoid))
                ).astype(BF)
                up_grad[part, :] = (act_grad * silu).astype(BF)

        block = gather.whole.shape[:-1] + (256,)
        grads = first_pair if begin < chunk else second_pair
        first_spot = 0 if begin < chunk + 1 else 2 * (begin - chunk) // 256
        pltpu.emit_pipeline(
            body,
            grid=(tiles,),
            in_specs=[
                pl.BlockSpec(block, lambda t: (0, 0, t)),
                pl.BlockSpec(block, lambda t: (0, 0, t + tiles)),
                pl.BlockSpec((256, width), lambda t: (t + spot, 0)),
            ],
            out_specs=[
                pl.BlockSpec((length, 256), lambda t: (0, t + spot)),
                pl.BlockSpec((length, 256), lambda t: (0, t + first_spot)),
                pl.BlockSpec((length, 256), lambda t: (0, t + first_spot + tiles)),
            ],
        )(gather.whole, gather.whole, down_full, act_out, grads, grads)

    feed(first, 0, chunk)
    advance(FORWARD_PLAN[19])
    store.wait()
    store = turn(lhs, n2_turned)
    advance(FORWARD_PLAN[20])
    second.arrive()
    feed(second, chunk, chunk - tail)
    advance(FORWARD_PLAN[21])
    third.arrive()
    feed(third, 2 * chunk - tail, tail)
    store.wait()
    for gather in (qkv, out, first, second, third, down, n1, n2, dy):
        gather.finish()


def forward(hidden, upstream, weights, gains, segment):
    size = lax.axis_size("shard")
    quarter, outer = size // 4, size // 2
    piece, width = hidden.shape
    length = piece * 4
    heads = Q_HEADS // 4
    kv_heads = KV_HEADS // 4
    w_query, _, _, w_out, w_gate, _, w_down = weights
    own = w_query.shape[0]
    qkv_width = (heads + 2 * kv_heads) * HEAD_DIM
    units = w_down.shape[0] // 4 * size

    def shape(*dims, kind=BF):
        return jax.ShapeDtypeStruct(dims, kind)

    results = [
        shape(size, own, qkv_width),
        shape(quarter, *w_out.shape),
        shape(size, own, units),
        shape(size, own, units),
        shape(units, width),
        shape(length, width),
        shape(length, width),
        shape(length, width),
        shape(width // 128, 128, length),
        shape(width // 128, 128, length),
        shape(width // 128, 128, length),
        shape(length, units),
        shape(length, units),
        shape(length, units),
        shape(heads + kv_heads, length, HEAD_DIM, kind=F32),
        shape(heads + 2 * kv_heads, length, HEAD_DIM),
        shape(length, heads * HEAD_DIM),
        shape(length, 128, kind=F32),
        shape(piece, width, kind=F32),
        shape(length, HEAD_DIM, kind=F32),
        shape(length, HEAD_DIM, kind=F32),
        shape(1, length, kind=jnp.int32),
    ]
    powers = np.arange(HEAD_DIM // 2, dtype=np.float32) * np.float32(2.0) / np.float32(HEAD_DIM)
    inverse = np.float32(ROPE_BASE) ** -powers
    dma = pltpu.SemaphoreType.DMA
    return pl.pallas_call(
        functools.partial(forward_kernel, size),
        out_shape=results,
        in_specs=[VMEM] + [ANY] * 8 + [VMEM] * 6,
        out_specs=[ANY] * 14 + [VMEM] * 8,
        scratch_shapes=[
            pltpu.VMEM((length, width), BF),
            pltpu.VMEM((length, width), BF),
            pltpu.VMEM((width // 128, 128, length), BF),
            pltpu.VMEM((size, own, qkv_width), BF),
            pltpu.VMEM((quarter,) + w_out.shape, BF),
            pltpu.VMEM((own, qkv_width), BF),
            pltpu.VMEM(w_out.shape, BF),
            pltpu.VMEM((w_down.shape[0] // 4, width), BF),
            pltpu.VMEM((piece, width), BF),
            pltpu.VMEM(w_gate.shape, BF),
            pltpu.VMEM((own, units), BF),
            pltpu.VMEM((own, units), BF),
            pltpu.VMEM((2, piece, width), BF),
            pltpu.VMEM((2, piece, width), BF),
            pltpu.VMEM((2, piece, width), BF),
            pltpu.VMEM((piece, width), BF),
            pltpu.VMEM((piece, width), BF),
            dma((7, outer)),
            dma((7, outer)),
            dma((7, outer)),
            dma((7, outer)),
            dma((7, outer)),
            dma((7, outer)),
            dma((7,)),
            dma((3, 3)),
            dma((3, 3)),
            dma((3,)),
            dma((8,)),
            dma((3,)),
            dma((3,)),
            pltpu.VMEM((length, 1), jnp.int32),
            pltpu.VMEM((length, 128), F32),
            pltpu.VMEM((256, 256), BF),
        ],
        compiler_params=pltpu.CompilerParams(
            collective_id=0, has_side_effects=True, vmem_limit_bytes=VMEM_BYTES
        ),
        name="forward_gather",
    )(
        hidden,
        upstream,
        *weights,
        *gains,
        jnp.asarray(np.concatenate([inverse, inverse])[None], F32),
        segment[None],
    )


def add_rows(target, sources, step=16):
    groups, rows, _ = target.shape

    @pl.loop(0, rows // step)
    def _(index):
        part = pl.ds(pl.multiple_of(index * step, step), step)
        for group in range(groups):
            total = sources[0][group, part, :].astype(target.dtype)
            for source in sources[1:]:
                total = total + source[group, part, :].astype(target.dtype)
            target[group, part, :] = total


class RowSum:
    def __init__(self, here, give, keep, near, rising, falling, stage, total, sems):
        self.here, self.give, self.keep = here, give, keep
        self.near, self.rising, self.falling = near, rising, falling
        self.stage, self.total = stage, total
        self.ys, self.yr, self.us, self.ur, self.ds, self.dr, self.load = sems
        self.last = here.outer - 1

    def across(self, place):
        return remote(
            self.give.at[place],
            self.near.at[place],
            self.ys.at[place],
            self.yr.at[place],
            self.here.twin,
        )

    def up(self, place):
        peer = self.here.outer_peer(self.here.place + 1)
        return remote(
            self.keep.at[place], self.rising.at[place], self.us.at[place], self.ur.at[place], peer
        )

    def down(self, place):
        peer = self.here.outer_peer(self.here.place - 1)
        return remote(
            self.keep.at[place], self.falling.at[place], self.ds.at[place], self.dr.at[place], peer
        )

    def arrived(self, slot, send, receive):
        remote(slot, slot, send, receive, self.here.twin).wait_recv()

    def fold(self, distance):
        here = self.here
        above = here.place + distance
        below = here.place - distance

        def merge(place, line, receive, first):
            near = pltpu.make_async_copy(self.near.at[place], self.stage.at[0], self.load.at[0])
            self.arrived(self.near.at[place], self.ys.at[place], self.yr.at[place])
            near.start()

            @pl.when(first)
            def _():
                near.wait()
                add_rows(self.keep.at[place], [self.keep.at[place], self.stage.at[0]])

            @pl.when(jnp.logical_not(first))
            def _():
                self.arrived(line.at[place], self.us.at[0], receive.at[place])
                far = pltpu.make_async_copy(line.at[place], self.stage.at[1], self.load.at[1])
                far.start()
                near.wait()
                far.wait()
                add_rows(
                    self.keep.at[place], [self.keep.at[place], self.stage.at[0], self.stage.at[1]]
                )

        @pl.when(above <= self.last)
        def _():
            merge(above, self.rising, self.ur, here.place == 0)
            self.up(above).start()

        @pl.when(below >= 0)
        def _():
            merge(below, self.falling, self.dr, here.place == self.last)
            self.down(below).start()

    def finish(self):
        here = self.here
        place = here.place
        self.arrived(self.near.at[place], self.ys.at[place], self.yr.at[place])
        keep = self.keep.at[place]
        near = pltpu.make_async_copy(self.near.at[place], self.stage.at[0], self.load.at[0])
        low = pltpu.make_async_copy(self.rising.at[place], self.stage.at[1], self.load.at[1])
        high = pltpu.make_async_copy(self.falling.at[place], self.stage.at[1], self.load.at[1])
        near.start()

        @pl.when(place > 0)
        def _():
            self.arrived(self.rising.at[place], self.us.at[0], self.ur.at[place])
            low.start()
            low.wait()

        @pl.when(place == 0)
        def _():
            self.arrived(self.falling.at[place], self.ds.at[0], self.dr.at[place])
            high.start()
            high.wait()

        near.wait()

        @pl.when((place > 0) & (place < self.last))
        def _():
            add_rows(keep, [keep, self.stage.at[0], self.stage.at[1]])
            self.arrived(self.falling.at[place], self.ds.at[0], self.dr.at[place])
            high.start()
            high.wait()
            add_rows(self.total, [keep, self.stage.at[1]])

        @pl.when((place == 0) | (place == self.last))
        def _():
            add_rows(self.total, [keep, self.stage.at[0], self.stage.at[1]])

    def sent(self):
        for place in range(self.here.outer):
            self.across(place).wait_send()

    def settle(self):
        here = self.here
        for place in range(here.outer):

            @pl.when(place > here.place)
            def _():
                self.up(place).wait_send()

            @pl.when(place < here.place)
            def _():
                self.down(place).wait_send()


def compute_terms(here, give, keep, left, right, tiles, orders, senders):
    own = give.shape[2]
    per = 128 // (2 * own)
    step = 512
    for group, done in orders:
        spots = tiles(group)

        @pl.loop(0, give.shape[3] // step)
        def _(index):
            lane = pl.ds(pl.multiple_of(index * step, step), step)
            terms = dot(left(group), right(lane)).astype(BF)
            for spot, (zone, seq_group) in enumerate(spots):
                for sub in range(per):
                    at = spot * 128 + sub * 2 * own
                    even, odd = terms[at : at + own], terms[at + own : at + 2 * own]
                    place = zone * per + sub
                    keep[place, seq_group, :, lane] = jnp.where(here.half == 0, even, odd)
                    give[place, seq_group, :, lane] = jnp.where(here.half == 0, odd, even)

        for zone in done:
            for sub in range(per):
                for sender in senders:
                    sender.across(zone * per + sub).start()


class LineSum:
    def __init__(self, here, terms, rising, falling, stage, sems):
        self.here, self.terms, self.stage = here, terms, stage
        self.rising, self.falling = rising, falling
        self.us, self.ur, self.ds, self.dr, self.load = sems
        self.last = here.outer - 1

    def up(self, place):
        peer = self.here.outer_peer(self.here.place + 1)
        return remote(
            self.terms.at[place], self.rising.at[place], self.us.at[place], self.ur.at[place], peer
        )

    def down(self, place):
        peer = self.here.outer_peer(self.here.place - 1)
        return remote(
            self.terms.at[place], self.falling.at[place], self.ds.at[place], self.dr.at[place], peer
        )

    def merge(self, place, line, receive):
        slot = line.at[place]
        remote(slot, slot, self.us.at[0], receive.at[place], self.here.twin).wait_recv()
        copy = pltpu.make_async_copy(slot, self.stage.at[0], self.load.at[0])
        copy.start()
        copy.wait()
        add_rows(self.terms.at[place], [self.terms.at[place], self.stage.at[0]])

    def fold(self, distance):
        here = self.here
        above = here.place + distance
        below = here.place - distance

        @pl.when(above <= self.last)
        def _():
            @pl.when(here.place > 0)
            def _():
                self.merge(above, self.rising, self.ur)

            self.up(above).start()

        @pl.when(below >= 0)
        def _():
            @pl.when(here.place < self.last)
            def _():
                self.merge(below, self.falling, self.dr)

            self.down(below).start()

    def gather(self):
        place = self.here.place

        @pl.when(place > 0)
        def _():
            self.merge(place, self.rising, self.ur)

        @pl.when(place < self.last)
        def _():
            self.merge(place, self.falling, self.dr)

    def settle(self):
        here = self.here
        for place in range(here.outer):

            @pl.when(place > here.place)
            def _():
                self.up(place).wait_send()

            @pl.when(place < here.place)
            def _():
                self.down(place).wait_send()


class LineFirstSum(RowSum):
    def __init__(self, here, give, keep, near, lines, stage, total, sems, twin_sems):
        self.here, self.give, self.keep = here, give, keep
        self.near, self.stage, self.total = near, stage, total
        self.ys, self.yr, self.load = sems[0], sems[1], sems[6]
        self.lines = [
            LineSum(here, terms, rising, falling, stage, kinds[2:])
            for terms, (rising, falling), kinds in (
                (give, lines[0], twin_sems),
                (keep, lines[1], sems),
            )
        ]

    def fold(self, distance):
        for line in self.lines:
            line.fold(distance)

    def pass_on(self):
        self.lines[0].gather()
        self.across(self.here.place).start()
        self.lines[1].gather()

    def finish(self):
        place = self.here.place
        self.arrived(self.near.at[place], self.ys.at[place], self.yr.at[place])
        near = pltpu.make_async_copy(self.near.at[place], self.stage.at[0], self.load.at[0])
        near.start()
        near.wait()
        add_rows(self.total, [self.keep.at[place], self.stage.at[0]])

    def sent(self):
        self.across(self.here.place).wait_send()

    def settle(self):
        for line in self.lines:
            line.settle()


class RowSpread:
    def __init__(self, here, rows, whole, sems):
        self.here, self.rows, self.whole = here, rows, whole
        self.send_sems, self.recv_sems, self.local = sems

    def copy(self, amount):
        seq = lax.rem(self.here.seq + amount, 4)
        return remote(
            self.rows.at[seq],
            self.whole.at[self.here.seq],
            self.send_sems.at[amount - 1],
            self.recv_sems.at[amount - 1],
            {"seq": seq},
        )

    def keep(self):
        seq = self.here.seq
        return pltpu.make_async_copy(self.rows.at[seq], self.whole.at[seq], self.local)

    def send(self):
        for amount in (2, 3, 1):
            self.copy(amount).start()
        self.keep().start()

    def arrive(self):
        for amount in (1, 2, 3):
            self.copy(amount).wait_recv()
        self.keep().wait()

    def finish(self):
        for amount in (1, 2, 3):
            self.copy(amount).wait_send()


class TokenSum:
    def __init__(self, here, part, got, pair, far_got, base, sems):
        self.here, self.part, self.got, self.pair = here, part, got, pair
        self.far_got, self.base = far_got, base
        self.send_sems, self.recv_sems = sems
        self.rows = part.shape[0] // 4

    def piece(self, seq):
        return pl.ds(pl.multiple_of(seq * self.rows, self.rows), self.rows)

    def to_mate(self, index):
        here = self.here
        chip = here.chip if index else 1 - here.chip
        seq = chip * 2 + 1 - here.core
        return remote(
            self.part.at[self.piece(seq), :],
            self.got.at[index],
            self.send_sems.at[index],
            self.recv_sems.at[index],
            here.mate,
        )

    def to_far(self):
        return remote(
            self.pair, self.far_got, self.send_sems.at[2], self.recv_sems.at[2], self.here.far
        )

    def send(self):
        self.to_mate(0).start()
        self.to_mate(1).start()

    def loop(self, body):
        @pl.loop(0, self.rows // 32)
        def _(index):
            body(index * 32)

    def pass_on(self):
        self.to_mate(0).wait_recv()
        begin = self.here.far_seq * self.rows

        def body(at):
            part = pl.ds(pl.multiple_of(at, 32), 32)
            source = pl.ds(pl.multiple_of(begin + at, 32), 32)
            total = self.part[source, :].astype(F32) + self.got[0, part, :].astype(F32)
            self.pair[part, :] = total.astype(BF)

        self.loop(body)
        self.to_far().start()

    def add_near(self):
        self.to_mate(1).wait_recv()
        begin = self.here.seq * self.rows

        def body(at):
            part = pl.ds(pl.multiple_of(at, 32), 32)
            source = pl.ds(pl.multiple_of(begin + at, 32), 32)
            self.base[part, :] += self.part[source, :].astype(F32) + self.got[1, part, :].astype(F32)

        self.loop(body)
        self.to_mate(0).wait_send()
        self.to_mate(1).wait_send()

    def add_far(self):
        self.to_far().wait_recv()

        def body(at):
            part = pl.ds(pl.multiple_of(at, 32), 32)
            self.base[part, :] += self.far_got[part, :].astype(F32)

        self.loop(body)
        self.to_far().wait_send()


class GainSum:
    def __init__(self, here, own, seq_got, middle, shard_got, sems):
        self.here, self.own, self.middle = here, own, middle
        self.seq_got, self.shard_got = seq_got, shard_got
        self.seq_send, self.seq_recv, self.shard_send, self.shard_recv = sems

    def over_seq(self, amount):
        here = self.here
        return remote(
            self.own,
            self.seq_got.at[here.seq],
            self.seq_send.at[amount - 1],
            self.seq_recv.at[amount - 1],
            {"seq": lax.rem(here.seq + amount, 4)},
        )

    def over_shard(self, amount):
        here = self.here
        return remote(
            self.middle,
            self.shard_got.at[here.shard],
            self.shard_send.at[amount - 1],
            self.shard_recv.at[amount - 1],
            {"shard": lax.rem(here.shard + amount, here.size)},
        )

    def start(self):
        for amount in range(1, 4):
            self.over_seq(amount).start()
        self.seq_got[self.here.seq] = self.own[...]

    def turn(self):
        for amount in range(1, 4):
            self.over_seq(amount).wait()
        total = self.seq_got[0]
        for index in range(1, 4):
            total = total + self.seq_got[index]
        self.middle[...] = total
        for amount in range(1, self.here.size):
            self.over_shard(amount).start()
        self.shard_got[self.here.shard] = total

    def finish(self):
        for amount in range(1, self.here.size):
            self.over_shard(amount).wait()
        total = self.shard_got[0]
        for index in range(1, self.here.size):
            total = total + self.shard_got[index]
        return total


PLAN = (
    (("down_a", 3),),
    (("down_a", 2), ("down_b", 3),),
    (("down_a", 1), ("down_b", 2),),
    (),
    (),
    (("first", 3), ("down_b", 1),),
    (("first", 2), ("down_b", "finish"),),
    (("second", 3), ("first", 1),),
    (("second", 2),),
    (),
    (("first", "finish"),),
    (("out", 3), ("second", 1),),
    (),
    (("out", 2), ("query", 3), ("down_a", "pass"), ("key", 3), ("out", 1),),
    (("query", 2), ("key", 2), ("second", "finish"), ("out", "finish"), ("query", 1), ("key", 1),),
    (("query", "finish"), ("key", "finish"),),
    (("down_a", "finish"),),
)


def backward_kernel(
    size,
    n1_hbm,
    dy_hbm,
    n2_hbm,
    act_hbm,
    first_hbm,
    second_hbm,
    proj_hbm,
    heads_ref,
    mixed_ref,
    lse_ref,
    middle_hbm,
    hidden_hbm,
    dy_own,
    qkv_full,
    out_full,
    first_full,
    second_full,
    down_full,
    attn_gain_ref,
    mlp_gain_ref,
    query_gain_ref,
    key_gain_ref,
    cos_ref,
    sin_ref,
    start_ref,
    grad_in,
    gains_out,
    grad_out,
    hidden_out,
    down_rows,
    first_rows,
    second_rows,
    qkv_rows,
    da_hbm,
    near_mlp,
    rising_mlp,
    falling_mlp,
    rising_twin,
    falling_twin,
    near_qkv,
    rising_qkv,
    falling_qkv,
    near_out,
    rising_out,
    falling_out,
    lhs,
    turned,
    first_r,
    second_r,
    give,
    keep,
    give_out,
    keep_out,
    stage,
    stage_out,
    dout_ref,
    da_own,
    got,
    far_got,
    pair,
    middle_grad,
    proj_buf,
    eye,
    keys_turned,
    lse_t,
    delta,
    delta_t,
    dk_sum,
    dv_sum,
    gain_row,
    gain_seq,
    gain_middle,
    gain_shard,
    ys,
    yr,
    us,
    ur,
    ds,
    dr,
    fold_load,
    spread_s,
    spread_r,
    spread_l,
    sum_s,
    sum_r,
    ts,
    tr,
    token_local,
    gss,
    gsr,
    gts,
    gtr,
    load_sem,
    credit,
):
    here = Place(size)
    length, width = lhs.shape
    rows = length // 4
    units = first_r.shape[1]
    chunk = units // 2
    ff_part = units // size
    heads = mixed_ref.shape[1] // HEAD_DIM
    kv_heads = heads // 2
    qkv_width = qkv_full.shape[2]
    last = here.outer - 1
    scale = HEAD_DIM ** (-0.5)

    def load(source, target, index):
        copy = pltpu.make_async_copy(source, target, load_sem.at[index])
        copy.start()
        return copy

    def sems(index):
        return tuple(kind.at[index] for kind in (ys, yr, us, ur, ds, dr, fold_load))

    thin = qkv_width // 2
    cut = units * 2 // 3
    lanes = {
        "down_a": slice(0, cut),
        "down_b": slice(cut, units),
        "query": slice(0, thin),
        "key": slice(thin, 2 * thin),
    }

    def part(ref, name):
        return ref.at[:, :, :, lanes[name]]

    def row_sum(index, give_ref, keep_ref, near, rising, falling, stage_ref, total):
        return RowSum(
            here, give_ref, keep_ref, near, rising, falling, stage_ref, total, sems(index)
        )

    jobs = {
        "down_a": LineFirstSum(
            here,
            part(give.at[2], "down_a"),
            part(keep.at[0], "down_a"),
            part(near_mlp.at[0], "down_a"),
            (
                (rising_twin, falling_twin),
                (part(rising_mlp.at[0], "down_a"), part(falling_mlp.at[0], "down_a")),
            ),
            part(stage, "down_a"),
            keep.at[0, here.place, :, :, lanes["down_a"]],
            sems(0),
            sems(5),
        ),
        "down_b": row_sum(
            6,
            part(give.at[2], "down_b"),
            part(keep.at[0], "down_b"),
            part(near_mlp.at[0], "down_b"),
            part(rising_mlp.at[0], "down_b"),
            part(falling_mlp.at[0], "down_b"),
            part(stage, "down_b"),
            keep.at[0, here.place, :, :, lanes["down_b"]],
        ),
        "out": row_sum(
            4, give_out, keep_out, near_out, rising_out, falling_out, stage_out, grad_out
        ),
    }
    for index, name in ((1, "first"), (2, "second")):
        jobs[name] = row_sum(
            index,
            give.at[2 - index],
            keep.at[index],
            near_mlp.at[index],
            rising_mlp.at[index],
            falling_mlp.at[index],
            stage,
            keep.at[index, here.place],
        )
    for index, name in ((3, "query"), (7, "key")):
        jobs[name] = row_sum(
            index,
            part(give.at[1], name),
            part(second_r, name),
            part(near_qkv, name),
            part(rising_qkv, name),
            part(falling_qkv, name),
            part(stage, name),
            second_r.at[here.place, :, :, lanes[name]],
        )
    zones = width // 512

    def zone_at(index):
        zone = here.place // (here.outer // zones)
        return (
            3 * (1 - zone // 2),
            lax.rem(2 + 3 * zone, 5),
            1 + lax.rem(zone, 2),
            zone,
        )[index]

    zone_order = [zone_at(index) for index in range(zones)]
    by_zone = [(zone, (zone,)) for zone in zone_order]

    spreads = {}
    for index, (name, whole) in enumerate(
        (
            ("down_a", down_rows.at[:, :, lanes["down_a"]]),
            ("down_b", down_rows.at[:, :, lanes["down_b"]]),
            ("first", first_rows),
            ("second", second_rows),
            ("query", qkv_rows.at[:, :, lanes["query"]]),
            ("key", qkv_rows.at[:, :, lanes["key"]]),
        )
    ):
        kinds = (spread_s.at[index], spread_r.at[index], spread_l.at[index])
        spreads[name] = RowSpread(here, jobs[name].total, whole, kinds)

    def token_sum(index, base):
        return TokenSum(
            here, lhs, got, pair, far_got, base, (sum_s.at[index], sum_r.at[index])
        )

    sum_mlp = token_sum(0, middle_grad)
    sum_hidden = token_sum(1, grad_in)
    sum_attn = token_sum(2, grad_in)
    da = TokenGather(here, da_own, da_hbm, (ts, tr, token_local.at[0]))

    def model_tiles(group):
        return [(group, seq_group) for seq_group in range(4)]

    def first_columns(lane):
        return first_r[:, lane]

    def model_left(group):
        return turned[pl.ds(group * 4, 4)].reshape(512, length)

    def advance(steps):
        for name, step in steps:
            job = jobs[name]
            if step == "pass":
                job.pass_on()
            elif step == "finish":
                job.finish()
                if name in spreads:
                    spreads[name].send()
            else:
                for distance in range(last * step // 3, last * (step - 1) // 3, -1):
                    job.fold(distance)

    load_turned = load(dy_hbm, turned, 0)
    load_act = load(act_hbm, first_r, 1)
    load_middle = load(middle_hbm, grad_in, 2)
    load_dy = load(dy_own, da_own, 4)
    load_second = load(second_hbm, second_r, 3)
    eye[...] = identity(HEAD_DIM)
    here.greet(wide=True)
    load_turned.wait()
    load_act.wait()
    def model_terms(give_ref, keep_ref, right, senders):
        compute_terms(
            here, give_ref, keep_ref, model_left, right, model_tiles, by_zone, senders
        )

    model_terms(give.at[2], keep.at[0], first_columns, [jobs["down_b"]])
    advance(PLAN[0])
    load_turned = load(n2_hbm, turned, 0)
    load_first = load(first_hbm, first_r, 1)
    load_first.wait()
    load_second.wait()

    own = width // size
    slabs = 256 // own

    def dn2_body(first_w, second_w):
        lane = pl.ds(pl.multiple_of(pl.program_id(0) * 256, 256), 256)
        first_tile = first_w[...].reshape(256, units)
        second_tile = second_w[...].reshape(256, units)

        @pl.loop(0, 2)
        def _(index):
            part = pl.ds(pl.multiple_of(index * 2 * rows, 2 * rows), 2 * rows)
            total = contract_cols(first_r[part, :], first_tile)
            blocks = pl.ds(index * (here.outer // 2), here.outer // 2)
            second_rows = second_r[blocks].reshape(2 * rows, units)
            total = total + contract_cols(second_rows, second_tile)
            lhs[part, lane] = total.astype(BF)

    slab = pl.BlockSpec((slabs, own, units), lambda t: (t, 0, 0))
    pltpu.emit_pipeline(dn2_body, grid=(width // 256,), in_specs=[slab, slab])(
        first_full, second_full
    )
    sum_mlp.send()
    middle_grad[...] = jnp.zeros_like(middle_grad)
    load_turned.wait()
    advance(PLAN[1])
    sum_mlp.pass_on()
    sum_mlp.add_near()
    model_terms(give.at[1], keep.at[1], first_columns, [jobs["first"]])
    load_act = load(act_hbm, first_r, 1)
    advance(PLAN[2])
    sum_mlp.add_far()

    load_middle.wait()
    load_dy.wait()
    gain_row[...] = jnp.zeros_like(gain_row)
    mlp_lane = slice(2 * HEAD_DIM, 2 * HEAD_DIM + width)
    attn_lane = slice(2 * HEAD_DIM + width, 2 * HEAD_DIM + 2 * width)
    narrow = 16

    @pl.loop(0, rows // narrow)
    def _(index):
        part = pl.ds(pl.multiple_of(index * narrow, narrow), narrow)
        values = grad_in[part, :]
        scales = lax.rsqrt(jnp.mean(values * values, axis=-1, keepdims=True) + EPSILON)
        normed = values * scales
        update = middle_grad[part, :]
        gain_row[:, mlp_lane] += jnp.sum(update * normed, axis=0, keepdims=True)
        upper = update * mlp_gain_ref[...]
        inner = jnp.mean(upper * normed, axis=-1, keepdims=True)
        grad = da_own[part, :].astype(F32) + scales * (upper - normed * inner)
        middle_grad[part, :] = grad
        da_own[part, :] = grad.astype(BF)

    da.send()
    advance(PLAN[3])
    model_terms(
        give.at[0],
        keep.at[2],
        lambda lane: second_r[:, :, :, lane].reshape(length, -1),
        [jobs["second"]],
    )
    advance(PLAN[4])

    def hidden_body(weight):
        lane = pl.ds(pl.multiple_of(pl.program_id(0) * 256, 256), 256)
        tile = weight[...]

        @pl.loop(0, 2)
        def _(index):
            part = pl.ds(pl.multiple_of(index * 2 * rows, 2 * rows), 2 * rows)
            lhs[part, lane] = dot(first_r[part, :], tile).astype(BF)

    load_act.wait()
    pltpu.emit_pipeline(
        hidden_body,
        grid=(width // 256,),
        in_specs=[pl.BlockSpec((units, 256), lambda t: (0, t))],
    )(down_full)
    da.mate_arrived()
    sum_hidden.send()
    da.forward()
    advance(PLAN[5])
    sum_hidden.pass_on()
    sum_hidden.add_near()
    advance(PLAN[6])
    da.rest_arrived()
    da.finish()
    load_lhs = load(da_hbm, lhs, 0)
    load_own = load(hidden_hbm, da_own, 2)
    load_lhs.wait()

    def dout_body(weight):
        lane = pl.ds(pl.multiple_of(pl.program_id(0) * 256, 256), 256)
        tile = weight[...].reshape(256, width)

        @pl.loop(0, 2)
        def _(index):
            part = pl.ds(pl.multiple_of(index * 2 * rows, 2 * rows), 2 * rows)
            dout_ref[part, lane] = contract_cols(lhs[part, :], tile).astype(BF)

    out_blocks, out_rows = out_full.shape[:2]
    pltpu.emit_pipeline(
        dout_body,
        grid=(out_blocks * out_rows // 256,),
        in_specs=[pl.BlockSpec((256 // out_rows, out_rows, width), lambda t: (t, 0, 0))],
    )(out_full)

    for head in range(heads):
        lane = slice(head * HEAD_DIM, (head + 1) * HEAD_DIM)
        turned[head] = contract_cols(eye[...], mixed_ref[:, lane]).astype(BF)
    compute_terms(
        here,
        give_out,
        keep_out,
        lambda group: turned[0:heads].reshape(heads * HEAD_DIM, length),
        lambda lane: lhs[:, lane],
        lambda group: [(zone, 0) for zone in range(heads)],
        [(0, zone_order)],
        [jobs["out"]],
    )
    load_turned = load(n1_hbm, turned, 0)
    sum_hidden.add_far()
    for index, peer in enumerate((here.mate, here.far)):
        pl.semaphore_signal(credit.at[index], inc=1, device_id=peer, device_id_type=MESH)

    @pl.loop(0, rows // 32)
    def _(index):
        part = pl.ds(pl.multiple_of(index * 32, 32), 32)
        pair[part, :] = grad_in[part, :].astype(BF)

    store_hidden = load(pair, hidden_out, 1)
    advance(PLAN[7])

    lse_t[...] = lse_ref[...].T[0:8]
    delta[...] = jnp.zeros_like(delta)
    for head in range(heads):
        lane = slice(head * HEAD_DIM, (head + 1) * HEAD_DIM)
        terms = dout_ref[:, lane].astype(F32) * mixed_ref[:, lane].astype(F32)
        delta[:, head : head + 1] = jnp.sum(terms, axis=-1, keepdims=True)
    delta_t[...] = delta[...].T[0:8]
    def through_norm(grad, head, part, gain_ref, which):
        proj = proj_buf[part, :]
        scales = lax.rsqrt(jnp.mean(proj * proj, axis=-1, keepdims=True) + EPSILON)
        normed = proj * scales
        grad = grad.astype(F32)
        upper = grad * cos_ref[part, :] - pltpu.roll(grad, HEAD_DIM // 2, 1) * sin_ref[part, :]
        gain_row[:, which * HEAD_DIM : (which + 1) * HEAD_DIM] += jnp.sum(
            upper * normed, axis=0, keepdims=True
        )
        upper = upper * gain_ref[...]
        inner = jnp.mean(upper * normed, axis=-1, keepdims=True)
        result = (scales * (upper - normed * inner)).astype(BF)
        first_r[part, head * HEAD_DIM : (head + 1) * HEAD_DIM] = result

    for head in range(heads):
        pair_head = head // 2
        load_proj = load(proj_hbm.at[head], proj_buf, 4)
        if head % 2 == 0:
            dk_sum[...] = jnp.zeros_like(dk_sum)
            dv_sum[...] = jnp.zeros_like(dv_sum)
            keys_turned[...] = contract_cols(eye[...], heads_ref[heads + pair_head]).astype(BF)
        for block in range(4):
            end = (block + 1) * rows
            part = pl.ds(block * rows, rows)
            queries = heads_ref[head, part, :]
            keys = heads_ref[heads + pair_head, 0:end, :]
            values = heads_ref[heads + kv_heads + pair_head, 0:end, :]
            out_grad = dout_ref[part, head * HEAD_DIM : (head + 1) * HEAD_DIM]
            scores = contract_cols(keys, queries)
            key_place = lax.broadcasted_iota(jnp.int32, (end, rows), 0)
            query_place = lax.broadcasted_iota(jnp.int32, (end, rows), 1) + block * rows
            allowed = (key_place >= start_ref[:, part]) & (key_place <= query_place)
            weights = jnp.exp(scores * scale - lse_t[head : head + 1, part])
            weights = jnp.where(allowed, weights, 0.0)
            weight_grad = contract_cols(values, out_grad)
            inner = delta_t[head : head + 1, part]
            score_grad = (weights * (weight_grad - inner)).astype(BF)
            dk_sum[0:end, :] += dot(score_grad, queries) * scale
            dv_sum[0:end, :] += dot(weights.astype(BF), out_grad)
            query_grad = dot(keys_turned[:, 0:end], score_grad).T
            query_grad = (query_grad * scale).astype(BF)
            if block == 0:
                load_proj.wait()
            through_norm(query_grad, head, part, query_gain_ref, 0)
        if head % 2:
            key = heads + pair_head
            value_at = (heads + kv_heads + pair_head) * HEAD_DIM
            load(proj_hbm.at[key], proj_buf, 4).wait()

            @pl.loop(0, 4)
            def _(index):
                part = pl.ds(pl.multiple_of(index * rows, rows), rows)
                through_norm(dk_sum[part, :].astype(BF), key, part, key_gain_ref, 1)
                first_r[part, value_at : value_at + HEAD_DIM] = dv_sum[part, :].astype(BF)

        advance(PLAN[8 + head])

    load_turned.wait()
    jobs["first"].sent()
    store_hidden.wait()
    proj_grads = first_r.at[:, 0:qkv_width]
    model_terms(
        give.at[1, :, :, :, 0:qkv_width],
        second_r.at[:, :, :, 0:qkv_width],
        first_columns,
        [jobs["query"], jobs["key"]],
    )
    advance(PLAN[12])

    def dn1_body(weight):
        lane = pl.ds(pl.multiple_of(pl.program_id(0) * 256, 256), 256)
        tile = weight[...].reshape(256, qkv_width)

        @pl.loop(0, 2)
        def _(index):
            part = pl.ds(pl.multiple_of(index * 2 * rows, 2 * rows), 2 * rows)
            lhs[part, lane] = contract_cols(proj_grads[part, :], tile).astype(BF)

    pltpu.emit_pipeline(
        dn1_body,
        grid=(width // 256,),
        in_specs=[pl.BlockSpec((slabs, own, qkv_width), lambda t: (t, 0, 0))],
    )(qkv_full)
    grad_in[...] = jnp.zeros_like(grad_in)
    pl.semaphore_wait(credit.at[0], 1)
    pl.semaphore_wait(credit.at[1], 1)
    sum_attn.send()
    advance(PLAN[13])
    sum_attn.pass_on()
    sum_attn.add_near()
    advance(PLAN[14])
    sum_attn.add_far()
    load_own.wait()

    @pl.loop(0, rows // narrow)
    def _(index):
        part = pl.ds(pl.multiple_of(index * narrow, narrow), narrow)
        values = da_own[part, :].astype(F32)
        scales = lax.rsqrt(jnp.mean(values * values, axis=-1, keepdims=True) + EPSILON)
        normed = values * scales
        update = grad_in[part, :]
        gain_row[:, attn_lane] += jnp.sum(update * normed, axis=0, keepdims=True)
        upper = update * attn_gain_ref[...]
        inner = jnp.mean(upper * normed, axis=-1, keepdims=True)
        grad_in[part, :] = middle_grad[part, :] + scales * (upper - normed * inner)

    gain_sum = GainSum(here, gain_row, gain_seq, gain_middle, gain_shard, (gss, gsr, gts, gtr))
    gain_sum.start()
    advance(PLAN[15])
    gain_sum.turn()
    advance(PLAN[16])
    gains_out[...] = gain_sum.finish()
    for spread_rows in spreads.values():
        spread_rows.arrive()
    for name, job in jobs.items():
        if name != "first":
            job.sent()
    for job in jobs.values():
        job.settle()
    for job in spreads.values():
        job.finish()


def backward(saved, weights, own, gains, tables, starts):
    size = lax.axis_size("shard")
    outer = size // 2
    (n1, dy, n2, act, first, second, proj, heads_all, mixed, lse, middle) = saved
    length, width = heads_all.shape[1], middle.shape[1]
    piece = length // 4
    units = act.shape[1]
    qkv_width = weights[0].shape[2]
    rows = width // (4 * size)
    q_width = mixed.shape[1]

    def shape(*dims, kind=BF):
        return jax.ShapeDtypeStruct(dims, kind)

    results = [
        shape(piece, width, kind=F32),
        shape(1, 2 * width + 2 * HEAD_DIM, kind=F32),
        shape(1, rows, width, kind=F32),
        shape(piece, width),
        shape(4, rows, units),
        shape(4, rows, units),
        shape(4, rows, units),
        shape(4, rows, qkv_width),
        shape(length, width),
    ]
    results += [shape(3, outer, 4, rows, units)] * 3
    results += [shape(outer, 4, rows, units * 2 // 3)] * 2
    results += [shape(outer, 4, rows, qkv_width)] * 3
    results += [shape(outer, 1, rows, width)] * 3
    dma = pltpu.SemaphoreType.DMA
    vmem = pltpu.VMEM
    return pl.pallas_call(
        functools.partial(backward_kernel, size),
        out_shape=results,
        in_specs=[ANY] * 7 + [VMEM] * 3 + [ANY] * 8 + [VMEM] * 7,
        out_specs=[VMEM] * 3 + [ANY] * (len(results) - 3),
        scratch_shapes=[
            vmem((length, width), BF),
            vmem((width // 128, 128, length), BF),
            vmem((length, units), BF),
            vmem((outer, 4, rows, units), BF),
            vmem((3, outer, 4, rows, units), BF),
            vmem((3, outer, 4, rows, units), BF),
            vmem((outer, 1, rows, width), BF),
            vmem((outer, 1, rows, width), BF),
            vmem((2, 4, rows, units), BF),
            vmem((2, 1, rows, width), BF),
            vmem((length, q_width), BF),
            vmem((piece, width), BF),
            vmem((2, piece, width), BF),
            vmem((piece, width), BF),
            vmem((piece, width), BF),
            vmem((piece, width), F32),
            vmem((length, HEAD_DIM), F32),
            vmem((HEAD_DIM, HEAD_DIM), BF),
            vmem((HEAD_DIM, length), BF),
            vmem((8, length), F32),
            vmem((length, 128), F32),
            vmem((8, length), F32),
            vmem((length, HEAD_DIM), F32),
            vmem((length, HEAD_DIM), F32),
            vmem((1, 2 * width + 2 * HEAD_DIM), F32),
            vmem((4, 1, 2 * width + 2 * HEAD_DIM), F32),
            vmem((1, 2 * width + 2 * HEAD_DIM), F32),
            vmem((size, 1, 2 * width + 2 * HEAD_DIM), F32),
            dma((8, outer)),
            dma((8, outer)),
            dma((8, outer)),
            dma((8, outer)),
            dma((8, outer)),
            dma((8, outer)),
            dma((8, 3)),
            dma((6, 3)),
            dma((6, 3)),
            dma((6,)),
            dma((3, 3)),
            dma((3, 3)),
            dma((3,)),
            dma((3,)),
            dma((1,)),
            dma((3,)),
            dma((3,)),
            dma((size - 1,)),
            dma((size - 1,)),
            dma((5,)),
            pltpu.SemaphoreType.REGULAR((2,)),
        ],
        compiler_params=pltpu.CompilerParams(
            collective_id=1, has_side_effects=True, vmem_limit_bytes=VMEM_BYTES
        ),
        name="backward_sums",
    )(
        n1,
        dy,
        n2,
        act,
        first,
        second.reshape(outer, 4, rows, units),
        proj,
        heads_all,
        mixed,
        lse,
        middle,
        *own,
        *weights,
        *gains,
        *tables,
        starts,
    )


def finish_kernel(
    size,
    grad_in,
    gains,
    grad_out,
    hidden_out,
    down_rows,
    first_rows,
    second_rows,
    qkv_rows,
    grad_in_out,
    grad_out_out,
    hidden_out_out,
    grad_query,
    grad_key,
    grad_value,
    grad_gate,
    grad_up,
    grad_down,
    attn_gain,
    mlp_gain,
    query_gain,
    key_gain,
    grad_in_buf,
    grad_out_buf,
    hidden_buf,
    down_buf,
    first_buf,
    second_buf,
    qkv_buf,
    query_buf,
    key_buf,
    value_buf,
    gate_buf,
    up_buf,
    wide_buf,
    load_sems,
    store_sems,
):
    units = down_buf.shape[2]
    chunk = units // 2
    ff_part = units // size
    most, tail = chunk - 256, 256
    stores = []

    def load(source, target, index):
        copy = pltpu.make_async_copy(source, target, load_sems.at[index])
        copy.start()
        return copy

    def store(source, target):
        copy = pltpu.make_async_copy(source, target, store_sems.at[len(stores)])
        copy.start()
        stores.append(copy)

    loads = [
        load(source, target, index)
        for index, (source, target) in enumerate(
            (
                (down_rows, down_buf),
                (first_rows, first_buf),
                (second_rows, second_buf),
                (qkv_rows, qkv_buf),
                (grad_in, grad_in_buf),
                (hidden_out, hidden_buf),
                (grad_out, grad_out_buf),
            )
        )
    ]

    def place(read, target):
        @pl.loop(0, target.shape[0] // 16)
        def _(index):
            part = pl.ds(pl.multiple_of(index * 16, 16), 16)
            values = [read(seq, part).astype(F32) for seq in range(4)]
            for begin in range(0, size, size // 8):
                pieces = [
                    values[seq][:, block * ff_part : (block + 1) * ff_part]
                    for block in range(begin, begin + size // 8)
                    for seq in range(4)
                ]
                lane = slice(begin * 4 * ff_part, (begin + size // 8) * 4 * ff_part)
                target[part, lane] = jnp.concatenate(pieces, axis=1)

    def side(index):
        at = 2 * most + index * tail

        def read(seq, part):
            return jnp.concatenate(
                [
                    first_buf[seq, part, index * chunk : (index + 1) * chunk],
                    second_buf[seq, part, index * most : (index + 1) * most],
                    second_buf[seq, part, at : at + tail],
                ],
                axis=1,
            )

        return read

    loads[0].wait()
    place(lambda seq, part: down_buf[seq, part, :], wide_buf)
    store(wide_buf, grad_down)
    loads[1].wait()
    loads[2].wait()
    place(side(0), gate_buf)
    store(gate_buf, grad_gate)
    place(side(1), up_buf)
    store(up_buf, grad_up)
    loads[4].wait()
    store(grad_in_buf, grad_in_out)
    loads[5].wait()
    store(hidden_buf, hidden_out_out)
    loads[6].wait()
    store(grad_out_buf, grad_out_out)
    loads[3].wait()
    at = 0
    for buf, target in ((query_buf, grad_query), (key_buf, grad_key), (value_buf, grad_value)):
        count = buf.shape[1] // 4
        for seq in range(4):
            buf[:, seq * count : (seq + 1) * count] = qkv_buf[seq, :, at : at + count].astype(F32)
        at += count
        store(buf, target)
    at = 0
    for target in (query_gain, key_gain, mlp_gain, attn_gain):
        target[...] = gains[:, at : at + target.shape[1]]
        at += target.shape[1]
    for copy in stores:
        copy.wait()


def finish(grad_in, gains, grad_out, hidden_out, down_rows, first_rows, second_rows, qkv_rows):
    size = lax.axis_size("shard")
    piece, width = grad_in.shape
    rows, units = down_rows.shape[1:]
    qkv_width = qkv_rows.shape[2]

    def shape(*dims, kind=F32):
        return jax.ShapeDtypeStruct(dims, kind)

    results = [
        shape(piece, width),
        shape(1, rows, width),
        shape(piece, width, kind=BF),
        shape(rows, 2 * qkv_width),
        shape(rows, qkv_width),
        shape(rows, qkv_width),
        shape(rows, 4 * units),
        shape(rows, 4 * units),
        shape(rows, 4 * units),
        shape(1, width),
        shape(1, width),
        shape(1, HEAD_DIM),
        shape(1, HEAD_DIM),
    ]
    return pl.pallas_call(
        functools.partial(finish_kernel, size),
        out_shape=results,
        in_specs=[ANY, VMEM] + [ANY] * 6,
        out_specs=[ANY] * 9 + [VMEM] * 4,
        scratch_shapes=[
            pltpu.VMEM((piece, width), F32),
            pltpu.VMEM((1, rows, width), F32),
            pltpu.VMEM((piece, width), BF),
            pltpu.VMEM((4, rows, units), BF),
            pltpu.VMEM((4, rows, units), BF),
            pltpu.VMEM((4, rows, units), BF),
            pltpu.VMEM((4, rows, qkv_width), BF),
            pltpu.VMEM((rows, 2 * qkv_width), F32),
            pltpu.VMEM((rows, qkv_width), F32),
            pltpu.VMEM((rows, qkv_width), F32),
            pltpu.VMEM((rows, 4 * units), F32),
            pltpu.VMEM((rows, 4 * units), F32),
            pltpu.VMEM((rows, 4 * units), F32),
            pltpu.SemaphoreType.DMA((7,)),
            pltpu.SemaphoreType.DMA((9,)),
        ],
        compiler_params=pltpu.CompilerParams(vmem_limit_bytes=VMEM_BYTES),
        name="finish",
    )(grad_in, gains, grad_out, hidden_out, down_rows, first_rows, second_rows, qkv_rows)


def local(
    hidden_in,
    segment_ids,
    norm_attn_gain,
    w_query,
    w_key,
    w_value,
    query_gain,
    key_gain,
    w_out,
    norm_mlp_gain,
    w_gate,
    w_up,
    w_down,
    out_cotangent,
):
    segment = segment_ids[0]
    gains = (norm_attn_gain[None], norm_mlp_gain[None], query_gain[None], key_gain[None])
    results = forward(
        hidden_in[0],
        out_cotangent[0],
        (w_query, w_key, w_value, w_out, w_gate, w_up, w_down),
        gains,
        segment,
    )
    (
        grad_in,
        grad_out,
        hidden_out,
        grad_query,
        grad_key,
        grad_value,
        grad_gate,
        grad_up,
        grad_down,
        attn_gain,
        mlp_gain,
        query_grad,
        key_grad,
    ) = finish(
        *backward(
            results[8:19],
            results[:5],
            (hidden_in[0], out_cotangent[0]),
            gains,
            results[19:21],
            results[21],
        )[:8]
    )
    return (
        hidden_out[None],
        grad_in[None],
        attn_gain[0],
        grad_query,
        grad_key,
        grad_value,
        query_grad[0],
        key_grad[0],
        grad_out[0],
        mlp_gain[0],
        grad_gate,
        grad_up,
        grad_down.T,
    )


def solution(mesh):
    return jax.shard_map(
        local,
        mesh=mesh,
        in_specs=(
            P("shard", "seq", None),
            P("shard", None),
            P(),
            P("shard", None),
            P("shard", None),
            P("shard", None),
            P(),
            P(),
            P("shard", None),
            P(),
            P("shard", None),
            P("shard", None),
            P("shard", None),
            P("shard", "seq", None),
        ),
        out_specs=(
            P("shard", "seq", None),
            P("shard", "seq", None),
            P(),
            P(("seq", "shard"), None),
            P(("seq", "shard"), None),
            P(("seq", "shard"), None),
            P(),
            P(),
            P(("seq", "shard"), None),
            P(),
            P(("seq", "shard"), None),
            P(("seq", "shard"), None),
            P(None, ("seq", "shard")),
        ),
        check_vma=False,
    )
```

```python
import functools

import jax
import jax.numpy as jnp
import numpy as np
from jax import lax
from jax.experimental import pallas as pl
from jax.experimental.pallas import tpu as pltpu
from jax.sharding import PartitionSpec as P

Q_HEADS = 16
KV_HEADS = 8
HEAD_DIM = 128
EPSILON = 1e-06
ROPE_BASE = 1000000.0
NEGATIVE = -1e30
BF = jnp.bfloat16
F32 = jnp.float32
MESH = pl.DeviceIdType.MESH
ANY = pl.BlockSpec(memory_space=pl.ANY)
VMEM = pl.BlockSpec(memory_space=pltpu.VMEM)
VMEM_BYTES = 62 * 1024 * 1024


def dot(left, right):
    return jnp.dot(left, right, preferred_element_type=F32)


def contract_cols(left, right):
    return lax.dot_general(left, right, (((1,), (1,)), ((), ())), preferred_element_type=F32)


class Place:
    def __init__(self, size):
        self.size = size
        self.outer = size // 2
        self.quarter = size // 4
        self.seq = lax.axis_index("seq")
        self.shard = lax.axis_index("shard")
        self.chip = self.seq // 2
        self.core = lax.rem(self.seq, 2)
        self.place = self.shard // 2
        self.half = lax.rem(self.shard, 2)
        self.far_seq = lax.rem(self.seq + 2, 4)
        self.mate_seq = self.chip * 2 + 1 - self.core
        self.far = {"seq": self.far_seq}
        self.mate = {"seq": self.mate_seq}
        self.twin_shard = self.place * 2 + 1 - self.half
        self.twin = {"shard": self.twin_shard}

    def outer_peer(self, place):
        return {"shard": place * 2 + self.half}

    def greet(self, wide=False):
        barrier = pltpu.get_barrier_semaphore()
        last = self.outer - 1

        def signal(peer):
            pl.semaphore_signal(barrier, inc=1, device_id=peer, device_id_type=MESH)

        signal(self.far)
        signal(self.mate)
        if wide:
            signal({"seq": 3 - self.seq})
            for amount in range(1, self.size):
                signal({"shard": lax.rem(self.shard + amount, self.size)})
            pl.semaphore_wait(barrier, 2 + self.size)
            return
        signal(self.twin)

        @pl.when(self.place < last)
        def _():
            signal(self.outer_peer(self.place + 1))

        @pl.when(self.place > 0)
        def _():
            signal(self.outer_peer(self.place - 1))

        inner = ((self.place > 0) & (self.place < last)).astype(jnp.int32)
        pl.semaphore_wait(barrier, 4 + inner)


def remote(source, target, send, receive, peer):
    return pltpu.make_async_remote_copy(
        src_ref=source,
        dst_ref=target,
        send_sem=send,
        recv_sem=receive,
        device_id=peer,
        device_id_type=MESH,
    )


class LineGather:
    def __init__(self, here, own, slot, sems):
        self.here, self.own, self.slot = here, own, slot
        self.us, self.ur, self.ds, self.dr = sems
        self.last = here.outer - 1

    def up(self, distance):
        here = self.here
        slot = self.slot(here.place - distance)
        source = slot if distance else self.own
        peer = here.outer_peer(here.place + 1)
        return remote(source, slot, self.us.at[distance], self.ur.at[distance], peer)

    def down(self, distance):
        here = self.here
        slot = self.slot(here.place + distance)
        source = slot if distance else self.own
        peer = here.outer_peer(here.place - 1)
        return remote(source, slot, self.ds.at[distance], self.dr.at[distance], peer)

    def send(self):
        here = self.here

        @pl.when(here.place < self.last)
        def _():
            self.up(0).start()

        @pl.when(here.place > 0)
        def _():
            self.down(0).start()

    def step(self, distance, arrived=lambda place: None):
        here = self.here
        below = here.place - 1 - distance
        above = here.place + 1 + distance

        @pl.when(below >= 0)
        def _():
            slot = self.slot(below)
            remote(slot, slot, self.us.at[0], self.ur.at[distance], here.twin).wait_recv()

            @pl.when(here.place < self.last)
            def _():
                self.up(distance + 1).start()

            arrived(below)

        @pl.when(above <= self.last)
        def _():
            slot = self.slot(above)
            remote(slot, slot, self.ds.at[0], self.dr.at[distance], here.twin).wait_recv()

            @pl.when(here.place > 0)
            def _():
                self.down(distance + 1).start()

            arrived(above)

    def finish(self):
        here = self.here
        for distance in range(self.last):

            @pl.when((here.place - distance >= 0) & (here.place < self.last))
            def _():
                self.up(distance).wait_send()

            @pl.when((here.place + distance <= self.last) & (here.place > 0))
            def _():
                self.down(distance).wait_send()


class RowGather:
    def __init__(self, here, own, whole, sems, spot=lambda shard: shard):
        self.here, self.own, self.whole, self.spot = here, own, whole, spot
        self.ys, self.yr, self.local = sems[4:]
        self.line = LineGather(here, own, self.mine, sems[:4])

    def mine(self, place):
        return self.whole.at[self.spot(place * 2 + self.here.half)]

    def theirs(self, place):
        return self.whole.at[self.spot(place * 2 + 1 - self.here.half)]

    def keep(self):
        return pltpu.make_async_copy(self.own, self.mine(self.here.place), self.local)

    def across(self, place, own=False):
        slot = self.mine(place)
        source = self.own if own else slot
        return remote(source, slot, self.ys.at[place], self.yr.at[place], self.here.twin)

    def arrived(self, place):
        slot = self.theirs(place)
        remote(slot, slot, self.ys.at[place], self.yr.at[place], self.here.twin).wait_recv()

    def send(self):
        self.line.send()
        self.across(self.here.place, own=True).start()
        self.keep().start()

    def step(self, distance):
        self.line.step(distance, lambda place: self.across(place).start())

    def arrive(self):
        self.keep().wait()
        for place in range(self.here.outer):
            self.arrived(place)

    def finish(self):
        self.line.finish()
        for place in range(self.here.outer):
            self.across(place).wait_send()


class TwinFirstGather(RowGather):
    def __init__(self, here, own, whole, sems, twin_sems):
        super().__init__(here, own, whole, sems)
        self.lines = [
            self.line,
            LineGather(here, self.theirs(here.place), self.theirs, twin_sems[:4]),
        ]

    def twin(self):
        self.arrived(self.here.place)
        self.lines[1].send()

    def step(self, distance):
        for line in self.lines:
            line.step(distance)

    def arrive(self):
        self.keep().wait()

    def finish(self):
        for line in self.lines:
            line.finish()
        self.across(self.here.place, own=True).wait_send()


class HeadGather:
    def __init__(self, here, own, whole, sems):
        self.here, self.own, self.whole = here, own, whole
        self.us, self.zr, self.ds, _, self.ys, self.yr, self.local = sems
        self.last = here.outer - 1
        self.count = here.quarter // 2
        self.first = here.seq * self.count
        self.mine = here.place - self.first
        self.inside = (self.mine >= 0) & (self.mine < self.count)

    def slot(self, index):
        return self.whole.at[index * 2 + self.here.half]

    def keep(self):
        return pltpu.make_async_copy(self.own, self.slot(self.mine), self.local)

    def up(self, index, own=False):
        slot = self.slot(index)
        peer = self.here.outer_peer(self.here.place + 1)
        return remote(self.own if own else slot, slot, self.us.at[index], self.zr.at[index], peer)

    def down(self, index, own=False):
        slot = self.slot(index)
        peer = self.here.outer_peer(self.here.place - 1)
        return remote(self.own if own else slot, slot, self.ds.at[index], self.zr.at[index], peer)

    def across(self, index):
        slot = self.slot(index)
        return remote(slot, slot, self.ys.at[index], self.yr.at[index], self.here.twin)

    def send(self):
        @pl.when(self.inside)
        def _():
            self.keep().start()

            @pl.when(self.here.place < self.last)
            def _():
                self.up(self.mine, own=True).start()

            @pl.when(self.here.place > 0)
            def _():
                self.down(self.mine, own=True).start()

    def step(self):
        here = self.here

        @pl.when(self.inside)
        def _():
            self.keep().wait()

        for index in range(self.count):
            slot = self.slot(index)
            arrival = remote(slot, slot, self.us.at[0], self.zr.at[index], here.twin)

            @pl.when(self.mine > index)
            def _():
                arrival.wait_recv()

                @pl.when(here.place < self.last)
                def _():
                    self.up(index).start()

            @pl.when(self.mine < index)
            def _():
                arrival.wait_recv()

                @pl.when(here.place > 0)
                def _():
                    self.down(index).start()

            self.across(index).start()

    def arrive(self):
        for index in range(self.count):
            slot = self.whole.at[index * 2 + 1 - self.here.half]
            remote(
                slot, slot, self.ys.at[index], self.yr.at[index], self.here.twin
            ).wait_recv()

    def finish(self):
        here = self.here
        for index in range(self.count):

            @pl.when((self.mine >= index) & (here.place < self.last))
            def _():
                self.up(index).wait_send()

            @pl.when((self.mine <= index) & (here.place > 0))
            def _():
                self.down(index).wait_send()

            self.across(index).wait_send()


class TokenGather:
    def __init__(self, here, own, whole, sems):
        self.here, self.own, self.whole = here, own, whole
        self.send_sems, self.recv_sems, self.local = sems
        self.rows = whole.shape[0] // 4

    def slot(self, seq):
        return self.whole.at[pl.ds(pl.multiple_of(seq * self.rows, self.rows), self.rows), :]

    def keep(self):
        return pltpu.make_async_copy(self.own, self.slot(self.here.seq), self.local)

    def copy(self, index):
        here = self.here
        slot = self.slot(here.far_seq if index == 2 else here.seq)
        return remote(
            slot if index == 2 else self.own,
            slot,
            self.send_sems.at[index],
            self.recv_sems.at[index],
            here.far if index == 0 else here.mate,
        )

    def send(self):
        self.copy(0).start()
        self.copy(1).start()
        self.keep().start()

    def forward(self):
        self.copy(0).wait_recv()
        self.copy(2).start()

    def mate_arrived(self):
        self.copy(1).wait_recv()

    def rest_arrived(self):
        self.copy(2).wait_recv()
        self.keep().wait()

    def arrive(self):
        self.mate_arrived()
        self.rest_arrived()

    def finish(self):
        for index in range(3):
            self.copy(index).wait_send()


class PieceSum:
    def __init__(self, here, piece, base, give, got, pair, far_got, sems, step):
        self.here, self.piece, self.base, self.step = here, piece, base, step
        self.give, self.got, self.pair, self.far_got = give, got, pair, far_got
        self.send_sems, self.recv_sems = sems

    def to_mate(self, index):
        return remote(
            self.give.at[index],
            self.got.at[index],
            self.send_sems.at[index],
            self.recv_sems.at[index],
            self.here.mate,
        )

    def to_far(self):
        return remote(
            self.pair, self.far_got, self.send_sems.at[2], self.recv_sems.at[2], self.here.far
        )

    def columns(self, body):
        step = self.step

        @pl.loop(0, self.pair.shape[1] // step)
        def _(index):
            body(pl.ds(pl.multiple_of(index * step, step), step))

    def send(self):
        here = self.here
        for index, chip in enumerate((1 - here.chip, here.chip)):
            seq = chip * 2 + 1 - here.core

            def fill(column, index=index, seq=seq):
                self.give[index, :, column] = self.piece(seq, column).astype(BF)

            self.columns(fill)
            self.to_mate(index).start()

    def pass_on(self):
        self.to_mate(0).wait_recv()

        def fill(column):
            term = self.piece(self.here.far_seq, column) + self.got[0, :, column].astype(F32)
            self.pair[:, column] = term.astype(BF)

        self.columns(fill)
        self.to_far().start()

    def add_near(self):
        self.to_mate(1).wait_recv()

        def fill(column):
            term = self.piece(self.here.seq, column) + self.got[1, :, column].astype(F32)
            self.base[:, column] += term

        self.columns(fill)

    def add_far(self):
        self.to_far().wait_recv()

        def fill(column):
            self.base[:, column] += self.far_got[:, column].astype(F32)

        self.columns(fill)
        for copy in (self.to_mate(0), self.to_mate(1), self.to_far()):
            copy.wait_send()


def identity(size):
    rows = lax.broadcasted_iota(jnp.int32, (size, size), 0)
    columns = lax.broadcasted_iota(jnp.int32, (size, size), 1)
    return jnp.where(rows == columns, 1.0, 0.0).astype(BF)


FORWARD_PLAN = (
    (("down", "send"),),
    (("out", "send"),),
    (("down", 0),),
    (),
    (),
    (("down", 1), ("down", 2), ("out", 0),),
    (),
    (),
    (("first", "send"),),
    (),
    (("second", "send"),),
    (),
    (),
    (("first", 0),),
    (),
    (),
    (("third", "send"),),
    (("first", 1),),
    (),
    (("second", "twin"), ("second", 0), ("first", 2),),
    (("third", 0),),
    (("second", 1),),
    (),
    (),
    (("third", 1),),
    (),
    (("second", 2), ("third", 2),),
    (),
    (),
)


def forward_kernel(
    size,
    hidden_hbm,
    dy_hbm,
    w_query,
    w_key,
    w_value,
    w_out,
    w_gate,
    w_up,
    w_down,
    attn_gain_ref,
    mlp_gain_ref,
    query_gain_ref,
    key_gain_ref,
    inverse_ref,
    segment_ref,
    qkv_full,
    out_full,
    first_full,
    second_full,
    down_full,
    n1_full,
    dy_full,
    n2_full,
    n1_turned,
    dy_turned,
    n2_turned,
    act_out,
    first_pair,
    second_pair,
    proj_out,
    heads_out,
    mixed_out,
    lse_out,
    middle_out,
    cos_out,
    sin_out,
    start_out,
    lhs,
    dy_all,
    turned,
    qkv_w,
    out_w,
    qkv_own,
    out_own,
    down_own,
    dy_own,
    wide_own,
    first_own,
    second_own,
    own_rows,
    give,
    got,
    pair,
    far_got,
    us,
    ur,
    ds,
    dr,
    ys,
    yr,
    row_local,
    ts,
    tr,
    token_local,
    load_sem,
    ss,
    sr,
    start_ref,
    turned_ids,
    eye,
    hidden_ref,
    proj_ref,
    heads_ref,
    mixed_ref,
    lse_ref,
    middle_ref,
    cos_ref,
    sin_ref,
    start_row,
    store_sems,
):
    here = Place(size)
    last = here.outer - 1
    length, width = lhs.shape
    lse_ref[...] = jnp.zeros_like(lse_ref)
    rows = length // 4
    units = act_out.shape[1]
    chunk = units // 2
    tail = 256
    heads = mixed_ref.shape[1] // HEAD_DIM
    kv_heads = heads // 2
    ff_part = units // size

    def sems(index):
        return tuple(kind.at[index] for kind in (us, ur, ds, dr, ys, yr, row_local))

    down_rows = pl.ds(pl.multiple_of(here.seq * ff_part, ff_part), ff_part)
    qkv = RowGather(here, qkv_own, qkv_full, sems(0))
    out = HeadGather(here, out_own, out_full, sems(1))
    down = RowGather(
        here,
        down_own,
        down_full,
        sems(2),
        lambda shard: pl.ds(pl.multiple_of(shard * ff_part, ff_part), ff_part),
    )
    first = RowGather(here, first_own, first_full, sems(3))
    cut = 2 * (chunk - tail)
    second = TwinFirstGather(
        here, second_own.at[:, 0:cut], second_full.at[:, :, 0:cut], sems(4), sems(6)
    )
    third = RowGather(
        here, second_own.at[:, cut : 2 * chunk], second_full.at[:, :, cut : 2 * chunk], sems(5)
    )
    n1 = TokenGather(here, own_rows.at[0], n1_full, (ts.at[0], tr.at[0], token_local.at[0]))
    n2 = TokenGather(here, own_rows.at[1], n2_full, (ts.at[1], tr.at[1], token_local.at[1]))
    dy = TokenGather(here, dy_own, dy_full, (ts.at[2], tr.at[2], token_local.at[2]))

    loads = []
    stores = []

    def hand_out(*pairs):
        for source, target in pairs:
            copy = pltpu.make_async_copy(source, target, store_sems.at[len(stores)])
            copy.start()
            stores.append(copy)

    load_hidden = pltpu.make_async_copy(hidden_hbm, hidden_ref, load_sem.at[8])
    at = 0
    for index, (weight, count) in enumerate(((w_query, heads), (w_key, kv_heads), (w_value, kv_heads))):
        count = count * HEAD_DIM
        source = weight.at[:, pl.ds(pl.multiple_of(here.seq * count, count), count)]
        loads.append(
            pltpu.make_async_copy(source, qkv_own.at[:, at : at + count], load_sem.at[index])
        )
        at += count
    loads.append(pltpu.make_async_copy(w_down.at[down_rows, :], down_own, load_sem.at[3]))
    loads.append(pltpu.make_async_copy(w_out, out_own, load_sem.at[4]))
    loads.append(pltpu.make_async_copy(dy_hbm, dy_own, load_sem.at[5]))
    loads.append(pltpu.make_async_copy(w_gate, wide_own, load_sem.at[6]))
    for load in loads:
        load.start()
    load_hidden.start()
    here.greet()
    for load in loads[:3]:
        load.wait()
    qkv.send()
    loads[5].wait()
    dy.send()

    def norm_rows(source, gain_ref, target):
        @pl.loop(0, rows // 32)
        def _(index):
            part = pl.ds(pl.multiple_of(index * 32, 32), 32)
            values = source[part, :].astype(F32)
            scales = lax.rsqrt(jnp.mean(values * values, axis=-1, keepdims=True) + EPSILON)
            target[part, :] = (values * scales * gain_ref[...]).astype(BF)

    gathers = {"out": out, "down": down, "first": first, "second": second, "third": third}

    def advance(steps):
        for name, step in steps:
            gather = gathers[name]
            if step == "send":
                gather.send()
            elif step == "twin":
                gather.twin()
            elif name == "out":
                gather.step()
            else:
                for distance in range(last * step // 3, last * (step + 1) // 3):
                    gather.step(distance)

    load_hidden.wait()
    norm_rows(hidden_ref, attn_gain_ref, own_rows.at[0])
    n1.send()
    for load in loads[3:5]:
        load.wait()
    advance(FORWARD_PLAN[0])
    for load in loads[6:]:
        load.wait()

    most = chunk - tail

    def cut_units(side):
        for seq in range(4):

            @pl.when(here.seq == seq)
            def _():
                @pl.loop(0, wide_own.shape[0] // 16)
                def _(index):
                    part = pl.ds(pl.multiple_of(index * 16, 16), 16)

                    def gathered(begin):
                        pieces = [
                            wide_own[part, (block * 4 + seq) * ff_part : (block * 4 + seq + 1) * ff_part]
                            for block in range(begin, begin + size // 2)
                        ]
                        return jnp.concatenate(pieces, axis=1)

                    first_own[part, side * chunk : (side + 1) * chunk] = gathered(0)
                    rest = gathered(size // 2)
                    second_own[part, side * most : (side + 1) * most] = rest[:, 0:most]
                    at = 2 * most + side * tail
                    second_own[part, at : at + tail] = rest[:, most:]

    eye[...] = identity(256)

    def rotation():
        ids = segment_ref[...].astype(F32)
        turned_ids[...] = jnp.broadcast_to(ids, (128, length)).T
        lane = lax.broadcasted_iota(jnp.int32, (128, 128), 1)

        @pl.loop(0, length // 128)
        def _(index):
            part = pl.ds(pl.multiple_of(index * 128, 128), 128)
            own_ids = turned_ids[part, :]
            count = jnp.zeros((128, 128), F32)
            for at in range(0, length, 128):
                count = count + jnp.where(
                    segment_ref[:, at : at + 128].astype(F32) < own_ids, 1.0, 0.0
                )
            starts = jnp.sum(count, axis=-1, keepdims=True)
            start_ref[part, :] = starts.astype(jnp.int32)
            starts = jnp.broadcast_to(starts, (128, 128))
            turned_ids[part, :] = starts
            places = lax.broadcasted_iota(jnp.int32, (128, 128), 0) + index * 128
            angles = (places.astype(F32) - starts) * inverse_ref[...]
            cos_ref[part, :] = jnp.cos(angles)
            sine = jnp.sin(angles)
            sin_ref[part, :] = jnp.where(lane < HEAD_DIM // 2, -sine, sine)

        start_row[...] = turned_ids[...].T[0:1].astype(jnp.int32)

    zones = width // 512

    def turn(source, target):
        for seq_group in range(4):
            for zone in range(0, zones, 2):
                at = (seq_group * zones + zone) * 128
                both = contract_cols(eye[...], source[:, at : at + 256]).astype(BF)
                turned[zone * 4 + seq_group] = both[0:128]
                turned[zone * 4 + 4 + seq_group] = both[128:256]
        copy = pltpu.make_async_copy(turned, target, load_sem.at[4])
        copy.start()
        return copy

    cut_units(0)
    load_up = pltpu.make_async_copy(w_up, wide_own, load_sem.at[7])
    load_up.start()
    load_up.wait()
    cut_units(1)
    advance(FORWARD_PLAN[1])
    for third_part in range(3):
        for distance in range(last * third_part // 3, last * (third_part + 1) // 3):
            qkv.step(distance)
        advance(FORWARD_PLAN[2 + third_part])
        if third_part == 0:
            rotation()
            hand_out((cos_ref, cos_out), (sin_ref, sin_out), (start_row, start_out))
            dy.forward()
    dy.arrive()
    load_dy = pltpu.make_async_copy(dy_full, dy_all, load_sem.at[0])
    load_dy.start()
    load_dy.wait()
    store = turn(dy_all, dy_turned)
    n1.forward()
    advance(FORWARD_PLAN[5])
    n1.arrive()
    load_lhs = pltpu.make_async_copy(n1_full, lhs, load_sem.at[0])
    load_lhs.start()
    advance(FORWARD_PLAN[6])
    qkv.arrive()
    load_qkv = pltpu.make_async_copy(qkv_full, qkv_w, load_sem.at[1])
    load_qkv.start()
    advance(FORWARD_PLAN[7])
    load_lhs.wait()
    load_qkv.wait()

    def project(tile):
        weight = qkv_w[:, :, tile * 256 : tile * 256 + 256].reshape(width, 256)
        gain_ref = query_gain_ref if tile < heads // 2 else key_gain_ref

        @pl.loop(0, 2)
        def _(index):
            part = pl.ds(pl.multiple_of(index * 2 * rows, 2 * rows), 2 * rows)
            both = dot(lhs[part, :], weight)
            for side in range(2):
                head = tile * 2 + side
                proj = both[:, side * HEAD_DIM : (side + 1) * HEAD_DIM]
                if head >= heads + kv_heads:
                    heads_ref[head, part, :] = proj.astype(BF)
                    continue
                proj_ref[head, part, :] = proj
                scales = lax.rsqrt(jnp.mean(proj * proj, axis=-1, keepdims=True) + EPSILON)
                gained = proj * scales * gain_ref[...]
                turned = pltpu.roll(gained, HEAD_DIM // 2, 1)
                heads_ref[head, part, :] = (
                    gained * cos_ref[part, :] + turned * sin_ref[part, :]
                ).astype(BF)

    def attend(head, blocks):
        pair_head = head // 2
        for block in blocks:
            end = (block + 1) * rows
            part = pl.ds(block * rows, rows)
            scores = contract_cols(
                heads_ref[head, part, :], heads_ref[heads + pair_head, 0:end, :]
            )
            row_place = lax.broadcasted_iota(jnp.int32, (rows, end), 0) + block * rows
            col_place = lax.broadcasted_iota(jnp.int32, (rows, end), 1)
            allowed = (col_place >= start_ref[part, :]) & (col_place <= row_place)
            raised = jnp.where(allowed, jnp.exp(scores * (HEAD_DIM ** (-0.5))), 0.0)
            sums = jnp.sum(raised, axis=-1, keepdims=True)
            mixed = dot(raised.astype(BF), heads_ref[heads + kv_heads + pair_head, 0:end, :])
            mixed = mixed * (1.0 / sums)
            mixed_ref[part, head * HEAD_DIM : (head + 1) * HEAD_DIM] = mixed.astype(BF)
            lse_ref[part, head : head + 1] = jnp.log(sums)

    tiles = (heads + 2 * kv_heads) // 2
    for tile in range(tiles):
        if tile == tiles // 2:
            advance(FORWARD_PLAN[8])
        project(tile)
    hand_out((proj_ref, proj_out), (heads_ref, heads_out))
    advance(FORWARD_PLAN[9])

    for head in range(heads):
        attend(head, (0, 1, 2))
        advance(FORWARD_PLAN[10 + 2 * head])
        attend(head, (3,))
        advance(FORWARD_PLAN[11 + 2 * head])
    hand_out((mixed_ref, mixed_out), (lse_ref, lse_out))

    out.arrive()
    load_out = pltpu.make_async_copy(out_full, out_w, load_sem.at[2])
    load_out.start()
    load_out.wait()

    def out_piece(seq, column):
        part = pl.ds(pl.multiple_of(seq * rows, rows), rows)
        weight = out_w[:, :, column]
        return dot(mixed_ref[part, :], weight.reshape(-1, weight.shape[-1]))

    middle_ref[...] = hidden_ref[...].astype(F32)
    token_sum = PieceSum(
        here, out_piece, middle_ref, give, got, pair, far_got, (ss, sr), 512
    )
    token_sum.send()
    advance(FORWARD_PLAN[18])
    token_sum.pass_on()
    token_sum.add_near()
    advance(FORWARD_PLAN[19])
    token_sum.add_far()
    hand_out((middle_ref, middle_out))
    norm_rows(middle_ref, mlp_gain_ref, own_rows.at[1])
    n2.send()
    advance(FORWARD_PLAN[20])
    store.wait()
    store = turn(lhs, n1_turned)
    advance(FORWARD_PLAN[21])
    n2.forward()
    advance(FORWARD_PLAN[22])
    n2.arrive()
    load_lhs = pltpu.make_async_copy(n2_full, lhs, load_sem.at[3])
    load_lhs.start()
    down.arrive()
    first.arrive()
    load_lhs.wait()

    def feed(gather, begin, count, between=()):
        tiles = count // 256
        spot = begin // 256

        def body(gate_w, up_w, down_w, act_ref, gate_grad, up_grad):
            gate_tile = gate_w[...].reshape(width, 256)
            up_tile = up_w[...].reshape(width, 256)
            down_tile = down_w[...]
            for index, steps in enumerate(between):
                if steps:
                    pl.when(pl.program_id(0) == index + 1)(lambda steps=steps: advance(steps))

            @pl.loop(0, 2)
            def _(index):
                part = pl.ds(pl.multiple_of(index * 2 * rows, 2 * rows), 2 * rows)
                gate = dot(lhs[part, :], gate_tile)
                up = dot(lhs[part, :], up_tile)
                act_grad = contract_cols(dy_all[part, :], down_tile)
                sigmoid = jax.nn.sigmoid(gate)
                silu = gate * sigmoid
                act_ref[part, :] = (silu * up).astype(BF)
                gate_grad[part, :] = (
                    act_grad * up * sigmoid * (1.0 + gate * (1.0 - sigmoid))
                ).astype(BF)
                up_grad[part, :] = (act_grad * silu).astype(BF)

        block = gather.whole.shape[:-1] + (256,)
        grads = first_pair if begin < chunk else second_pair
        first_spot = 0 if begin < chunk + 1 else 2 * (begin - chunk) // 256
        pltpu.emit_pipeline(
            body,
            grid=(tiles,),
            in_specs=[
                pl.BlockSpec(block, lambda t: (0, 0, t)),
                pl.BlockSpec(block, lambda t: (0, 0, t + tiles)),
                pl.BlockSpec((256, width), lambda t: (t + spot, 0)),
            ],
            out_specs=[
                pl.BlockSpec((length, 256), lambda t: (0, t + spot)),
                pl.BlockSpec((length, 256), lambda t: (0, t + first_spot)),
                pl.BlockSpec((length, 256), lambda t: (0, t + first_spot + tiles)),
            ],
        )(gather.whole, gather.whole, down_full, act_out, grads, grads)

    feed(first, 0, chunk, (FORWARD_PLAN[23], FORWARD_PLAN[24]))
    advance(FORWARD_PLAN[25])
    store.wait()
    store = turn(lhs, n2_turned)
    advance(FORWARD_PLAN[26])
    second.arrive()
    feed(second, chunk, chunk - tail, (FORWARD_PLAN[27],))
    advance(FORWARD_PLAN[28])
    third.arrive()
    feed(third, 2 * chunk - tail, tail)
    store.wait()
    for copy in stores:
        copy.wait()
    for gather in (qkv, out, first, second, third, down, n1, n2, dy):
        gather.finish()


def forward(hidden, upstream, weights, gains, segment):
    size = lax.axis_size("shard")
    quarter, outer = size // 4, size // 2
    piece, width = hidden.shape
    length = piece * 4
    heads = Q_HEADS // 4
    kv_heads = KV_HEADS // 4
    w_query, _, _, w_out, w_gate, _, w_down = weights
    own = w_query.shape[0]
    qkv_width = (heads + 2 * kv_heads) * HEAD_DIM
    units = w_down.shape[0] // 4 * size

    def shape(*dims, kind=BF):
        return jax.ShapeDtypeStruct(dims, kind)

    results = [
        shape(size, own, qkv_width),
        shape(quarter, *w_out.shape),
        shape(size, own, units),
        shape(size, own, units),
        shape(units, width),
        shape(length, width),
        shape(length, width),
        shape(length, width),
        shape(width // 128, 128, length),
        shape(width // 128, 128, length),
        shape(width // 128, 128, length),
        shape(length, units),
        shape(length, units),
        shape(length, units),
        shape(heads + kv_heads, length, HEAD_DIM, kind=F32),
        shape(heads + 2 * kv_heads, length, HEAD_DIM),
        shape(length, heads * HEAD_DIM),
        shape(length, 128, kind=F32),
        shape(piece, width, kind=F32),
        shape(length, HEAD_DIM, kind=F32),
        shape(length, HEAD_DIM, kind=F32),
        shape(1, length, kind=jnp.int32),
    ]
    powers = np.arange(HEAD_DIM // 2, dtype=np.float32) * np.float32(2.0) / np.float32(HEAD_DIM)
    inverse = np.float32(ROPE_BASE) ** -powers
    dma = pltpu.SemaphoreType.DMA
    return pl.pallas_call(
        functools.partial(forward_kernel, size),
        out_shape=results,
        in_specs=[ANY] * 9 + [VMEM] * 6,
        out_specs=[ANY] * 22,
        scratch_shapes=[
            pltpu.VMEM((length, width), BF),
            pltpu.VMEM((length, width), BF),
            pltpu.VMEM((width // 128, 128, length), BF),
            pltpu.VMEM((size, own, qkv_width), BF),
            pltpu.VMEM((quarter,) + w_out.shape, BF),
            pltpu.VMEM((own, qkv_width), BF),
            pltpu.VMEM(w_out.shape, BF),
            pltpu.VMEM((w_down.shape[0] // 4, width), BF),
            pltpu.VMEM((piece, width), BF),
            pltpu.VMEM(w_gate.shape, BF),
            pltpu.VMEM((own, units), BF),
            pltpu.VMEM((own, units), BF),
            pltpu.VMEM((2, piece, width), BF),
            pltpu.VMEM((2, piece, width), BF),
            pltpu.VMEM((2, piece, width), BF),
            pltpu.VMEM((piece, width), BF),
            pltpu.VMEM((piece, width), BF),
            dma((7, outer)),
            dma((7, outer)),
            dma((7, outer)),
            dma((7, outer)),
            dma((7, outer)),
            dma((7, outer)),
            dma((7,)),
            dma((3, 3)),
            dma((3, 3)),
            dma((3,)),
            dma((9,)),
            dma((3,)),
            dma((3,)),
            pltpu.VMEM((length, 1), jnp.int32),
            pltpu.VMEM((length, 128), F32),
            pltpu.VMEM((256, 256), BF),
            pltpu.VMEM((piece, width), BF),
            pltpu.VMEM((heads + kv_heads, length, HEAD_DIM), F32),
            pltpu.VMEM((heads + 2 * kv_heads, length, HEAD_DIM), BF),
            pltpu.VMEM((length, heads * HEAD_DIM), BF),
            pltpu.VMEM((length, 128), F32),
            pltpu.VMEM((piece, width), F32),
            pltpu.VMEM((length, HEAD_DIM), F32),
            pltpu.VMEM((length, HEAD_DIM), F32),
            pltpu.VMEM((1, length), jnp.int32),
            dma((8,)),
        ],
        compiler_params=pltpu.CompilerParams(
            collective_id=0, has_side_effects=True, vmem_limit_bytes=VMEM_BYTES
        ),
        name="forward_gather",
    )(
        hidden,
        upstream,
        *weights,
        *gains,
        jnp.asarray(np.concatenate([inverse, inverse])[None], F32),
        segment[None],
    )


def add_rows(target, sources, step=16):
    groups, rows, _ = target.shape

    @pl.loop(0, rows // step)
    def _(index):
        part = pl.ds(pl.multiple_of(index * step, step), step)
        for group in range(groups):
            total = sources[0][group, part, :].astype(target.dtype)
            for source in sources[1:]:
                total = total + source[group, part, :].astype(target.dtype)
            target[group, part, :] = total


class RowSum:
    def __init__(self, here, give, keep, near, rising, falling, stage, total, sems):
        self.here, self.give, self.keep = here, give, keep
        self.near, self.rising, self.falling = near, rising, falling
        self.stage, self.total = stage, total
        self.ys, self.yr, self.us, self.ur, self.ds, self.dr, self.load = sems
        self.last = here.outer - 1

    def across(self, place):
        return remote(
            self.give.at[place],
            self.near.at[place],
            self.ys.at[place],
            self.yr.at[place],
            self.here.twin,
        )

    def up(self, place):
        peer = self.here.outer_peer(self.here.place + 1)
        return remote(
            self.keep.at[place], self.rising.at[place], self.us.at[place], self.ur.at[place], peer
        )

    def down(self, place):
        peer = self.here.outer_peer(self.here.place - 1)
        return remote(
            self.keep.at[place], self.falling.at[place], self.ds.at[place], self.dr.at[place], peer
        )

    def arrived(self, slot, send, receive):
        remote(slot, slot, send, receive, self.here.twin).wait_recv()

    def fold(self, distance):
        here = self.here
        above = here.place + distance
        below = here.place - distance

        def merge(place, line, receive, first):
            near = pltpu.make_async_copy(self.near.at[place], self.stage.at[0], self.load.at[0])
            self.arrived(self.near.at[place], self.ys.at[place], self.yr.at[place])
            near.start()

            @pl.when(first)
            def _():
                near.wait()
                add_rows(self.keep.at[place], [self.keep.at[place], self.stage.at[0]])

            @pl.when(jnp.logical_not(first))
            def _():
                self.arrived(line.at[place], self.us.at[0], receive.at[place])
                far = pltpu.make_async_copy(line.at[place], self.stage.at[1], self.load.at[1])
                far.start()
                near.wait()
                far.wait()
                add_rows(
                    self.keep.at[place], [self.keep.at[place], self.stage.at[0], self.stage.at[1]]
                )

        @pl.when(above <= self.last)
        def _():
            merge(above, self.rising, self.ur, here.place == 0)
            self.up(above).start()

        @pl.when(below >= 0)
        def _():
            merge(below, self.falling, self.dr, here.place == self.last)
            self.down(below).start()

    def finish(self):
        here = self.here
        place = here.place
        self.arrived(self.near.at[place], self.ys.at[place], self.yr.at[place])
        keep = self.keep.at[place]
        near = pltpu.make_async_copy(self.near.at[place], self.stage.at[0], self.load.at[0])
        low = pltpu.make_async_copy(self.rising.at[place], self.stage.at[1], self.load.at[1])
        high = pltpu.make_async_copy(self.falling.at[place], self.stage.at[1], self.load.at[1])
        near.start()

        @pl.when(place > 0)
        def _():
            self.arrived(self.rising.at[place], self.us.at[0], self.ur.at[place])
            low.start()
            low.wait()

        @pl.when(place == 0)
        def _():
            self.arrived(self.falling.at[place], self.ds.at[0], self.dr.at[place])
            high.start()
            high.wait()

        near.wait()

        @pl.when((place > 0) & (place < self.last))
        def _():
            add_rows(keep, [keep, self.stage.at[0], self.stage.at[1]])
            self.arrived(self.falling.at[place], self.ds.at[0], self.dr.at[place])
            high.start()
            high.wait()
            add_rows(self.total, [keep, self.stage.at[1]])

        @pl.when((place == 0) | (place == self.last))
        def _():
            add_rows(self.total, [keep, self.stage.at[0], self.stage.at[1]])

    def sent(self):
        for place in range(self.here.outer):
            self.across(place).wait_send()

    def settle(self):
        here = self.here
        for place in range(here.outer):

            @pl.when(place > here.place)
            def _():
                self.up(place).wait_send()

            @pl.when(place < here.place)
            def _():
                self.down(place).wait_send()


def compute_terms(here, give, keep, left, right, tiles, orders, senders):
    own = give.shape[2]
    per = 128 // (2 * own)
    step = 512
    for group, done in orders:
        spots = tiles(group)

        @pl.loop(0, give.shape[3] // step)
        def _(index):
            lane = pl.ds(pl.multiple_of(index * step, step), step)
            terms = dot(left(group), right(lane)).astype(BF)
            for spot, (zone, seq_group) in enumerate(spots):
                for sub in range(per):
                    at = spot * 128 + sub * 2 * own
                    even, odd = terms[at : at + own], terms[at + own : at + 2 * own]
                    place = zone * per + sub
                    keep[place, seq_group, :, lane] = jnp.where(here.half == 0, even, odd)
                    give[place, seq_group, :, lane] = jnp.where(here.half == 0, odd, even)

        for zone in done:
            for sub in range(per):
                for sender in senders:
                    sender.across(zone * per + sub).start()


class LineSum:
    def __init__(self, here, terms, rising, falling, stage, sems):
        self.here, self.terms, self.stage = here, terms, stage
        self.rising, self.falling = rising, falling
        self.us, self.ur, self.ds, self.dr, self.load = sems
        self.last = here.outer - 1

    def up(self, place):
        peer = self.here.outer_peer(self.here.place + 1)
        return remote(
            self.terms.at[place], self.rising.at[place], self.us.at[place], self.ur.at[place], peer
        )

    def down(self, place):
        peer = self.here.outer_peer(self.here.place - 1)
        return remote(
            self.terms.at[place], self.falling.at[place], self.ds.at[place], self.dr.at[place], peer
        )

    def merge(self, place, line, receive):
        slot = line.at[place]
        remote(slot, slot, self.us.at[0], receive.at[place], self.here.twin).wait_recv()
        copy = pltpu.make_async_copy(slot, self.stage.at[0], self.load.at[0])
        copy.start()
        copy.wait()
        add_rows(self.terms.at[place], [self.terms.at[place], self.stage.at[0]])

    def fold(self, distance):
        here = self.here
        above = here.place + distance
        below = here.place - distance

        @pl.when(above <= self.last)
        def _():
            @pl.when(here.place > 0)
            def _():
                self.merge(above, self.rising, self.ur)

            self.up(above).start()

        @pl.when(below >= 0)
        def _():
            @pl.when(here.place < self.last)
            def _():
                self.merge(below, self.falling, self.dr)

            self.down(below).start()

    def gather(self):
        place = self.here.place

        @pl.when(place > 0)
        def _():
            self.merge(place, self.rising, self.ur)

        @pl.when(place < self.last)
        def _():
            self.merge(place, self.falling, self.dr)

    def settle(self):
        here = self.here
        for place in range(here.outer):

            @pl.when(place > here.place)
            def _():
                self.up(place).wait_send()

            @pl.when(place < here.place)
            def _():
                self.down(place).wait_send()


class LineFirstSum(RowSum):
    def __init__(self, here, give, keep, near, lines, stage, total, sems, twin_sems):
        self.here, self.give, self.keep = here, give, keep
        self.near, self.stage, self.total = near, stage, total
        self.ys, self.yr, self.load = sems[0], sems[1], sems[6]
        self.lines = [
            LineSum(here, terms, rising, falling, stage, kinds[2:])
            for terms, (rising, falling), kinds in (
                (give, lines[0], twin_sems),
                (keep, lines[1], sems),
            )
        ]

    def fold(self, distance):
        for line in self.lines:
            line.fold(distance)

    def pass_on(self):
        self.lines[0].gather()
        self.across(self.here.place).start()
        self.lines[1].gather()

    def finish(self):
        place = self.here.place
        self.arrived(self.near.at[place], self.ys.at[place], self.yr.at[place])
        near = pltpu.make_async_copy(self.near.at[place], self.stage.at[0], self.load.at[0])
        near.start()
        near.wait()
        add_rows(self.total, [self.keep.at[place], self.stage.at[0]])

    def sent(self):
        self.across(self.here.place).wait_send()

    def settle(self):
        for line in self.lines:
            line.settle()


class RowSpread:
    def __init__(self, here, rows, whole, sems):
        self.here, self.rows, self.whole = here, rows, whole
        self.send_sems, self.recv_sems, self.local = sems

    def copy(self, amount):
        seq = lax.rem(self.here.seq + amount, 4)
        return remote(
            self.rows.at[seq],
            self.whole.at[self.here.seq],
            self.send_sems.at[amount - 1],
            self.recv_sems.at[amount - 1],
            {"seq": seq},
        )

    def keep(self):
        seq = self.here.seq
        return pltpu.make_async_copy(self.rows.at[seq], self.whole.at[seq], self.local)

    def send(self):
        for amount in (2, 3, 1):
            self.copy(amount).start()
        self.keep().start()

    def arrive(self):
        for amount in (1, 2, 3):
            self.copy(amount).wait_recv()
        self.keep().wait()

    def finish(self):
        for amount in (1, 2, 3):
            self.copy(amount).wait_send()


class TokenSum:
    def __init__(self, here, part, got, pair, far_got, base, sems):
        self.here, self.part, self.got, self.pair = here, part, got, pair
        self.far_got, self.base = far_got, base
        self.send_sems, self.recv_sems = sems
        self.rows = part.shape[0] // 4

    def piece(self, seq):
        return pl.ds(pl.multiple_of(seq * self.rows, self.rows), self.rows)

    def to_mate(self, index):
        here = self.here
        chip = here.chip if index else 1 - here.chip
        seq = chip * 2 + 1 - here.core
        return remote(
            self.part.at[self.piece(seq), :],
            self.got.at[index],
            self.send_sems.at[index],
            self.recv_sems.at[index],
            here.mate,
        )

    def to_far(self):
        return remote(
            self.pair, self.far_got, self.send_sems.at[2], self.recv_sems.at[2], self.here.far
        )

    def send(self):
        self.to_mate(0).start()
        self.to_mate(1).start()

    def loop(self, body):
        @pl.loop(0, self.rows // 32)
        def _(index):
            body(index * 32)

    def pass_on(self):
        self.to_mate(0).wait_recv()
        begin = self.here.far_seq * self.rows

        def body(at):
            part = pl.ds(pl.multiple_of(at, 32), 32)
            source = pl.ds(pl.multiple_of(begin + at, 32), 32)
            total = self.part[source, :].astype(F32) + self.got[0, part, :].astype(F32)
            self.pair[part, :] = total.astype(BF)

        self.loop(body)
        self.to_far().start()

    def add_near(self):
        self.to_mate(1).wait_recv()
        begin = self.here.seq * self.rows

        def body(at):
            part = pl.ds(pl.multiple_of(at, 32), 32)
            source = pl.ds(pl.multiple_of(begin + at, 32), 32)
            self.base[part, :] += self.part[source, :].astype(F32) + self.got[1, part, :].astype(F32)

        self.loop(body)
        self.to_mate(0).wait_send()
        self.to_mate(1).wait_send()

    def add_far(self):
        self.to_far().wait_recv()

        def body(at):
            part = pl.ds(pl.multiple_of(at, 32), 32)
            self.base[part, :] += self.far_got[part, :].astype(F32)

        self.loop(body)
        self.to_far().wait_send()


class GainSum:
    def __init__(self, here, own, seq_got, middle, shard_got, sems):
        self.here, self.own, self.middle = here, own, middle
        self.seq_got, self.shard_got = seq_got, shard_got
        self.seq_send, self.seq_recv, self.shard_send, self.shard_recv = sems

    def over_seq(self, amount):
        here = self.here
        return remote(
            self.own,
            self.seq_got.at[here.seq],
            self.seq_send.at[amount - 1],
            self.seq_recv.at[amount - 1],
            {"seq": lax.rem(here.seq + amount, 4)},
        )

    def over_shard(self, amount):
        here = self.here
        return remote(
            self.middle,
            self.shard_got.at[here.shard],
            self.shard_send.at[amount - 1],
            self.shard_recv.at[amount - 1],
            {"shard": lax.rem(here.shard + amount, here.size)},
        )

    def start(self):
        for amount in range(1, 4):
            self.over_seq(amount).start()
        self.seq_got[self.here.seq] = self.own[...]

    def turn(self):
        for amount in range(1, 4):
            self.over_seq(amount).wait()
        total = self.seq_got[0]
        for index in range(1, 4):
            total = total + self.seq_got[index]
        self.middle[...] = total
        for amount in range(1, self.here.size):
            self.over_shard(amount).start()
        self.shard_got[self.here.shard] = total

    def finish(self):
        for amount in range(1, self.here.size):
            self.over_shard(amount).wait()
        total = self.shard_got[0]
        for index in range(1, self.here.size):
            total = total + self.shard_got[index]
        return total


PLAN = (
    (("down_a", 3),),
    (("down_a", 2), ("down_b", 3),),
    (("down_a", 1), ("down_b", 2),),
    (),
    (),
    (("first", 3), ("down_b", 1),),
    (("first", 2), ("down_b", "finish"),),
    (("second", 3), ("first", 1),),
    (("second", 2),),
    (),
    (("first", "finish"),),
    (("out", 3), ("second", 1),),
    (),
    (("out", 2), ("query", 3), ("down_a", "pass"), ("key", 3), ("out", 1),),
    (("query", 2), ("key", 2), ("second", "finish"), ("out", "finish"), ("query", 1), ("key", 1),),
    (("query", "finish"), ("key", "finish"),),
    (("down_a", "finish"),),
)


def backward_kernel(
    size,
    n1_hbm,
    dy_hbm,
    n2_hbm,
    act_hbm,
    first_hbm,
    second_hbm,
    proj_hbm,
    heads_hbm,
    mixed_hbm,
    lse_hbm,
    middle_hbm,
    hidden_hbm,
    dy_own,
    qkv_full,
    out_full,
    first_full,
    second_full,
    down_full,
    attn_gain_ref,
    mlp_gain_ref,
    query_gain_ref,
    key_gain_ref,
    cos_hbm,
    sin_hbm,
    start_hbm,
    grad_in_out,
    gains_out,
    grad_out_out,
    hidden_out,
    down_rows,
    first_rows,
    second_rows,
    qkv_rows,
    da_hbm,
    near_mlp,
    rising_mlp,
    falling_mlp,
    rising_twin,
    falling_twin,
    near_qkv,
    rising_qkv,
    falling_qkv,
    near_out,
    rising_out,
    falling_out,
    lhs,
    turned,
    first_r,
    second_r,
    give,
    keep,
    give_out,
    keep_out,
    stage,
    stage_out,
    dout_ref,
    da_own,
    got,
    far_got,
    pair,
    middle_grad,
    proj_buf,
    eye,
    keys_turned,
    lse_t,
    delta,
    delta_t,
    dk_sum,
    dv_sum,
    gain_row,
    gain_seq,
    gain_middle,
    gain_shard,
    ys,
    yr,
    us,
    ur,
    ds,
    dr,
    fold_load,
    spread_s,
    spread_r,
    spread_l,
    sum_s,
    sum_r,
    ts,
    tr,
    token_local,
    gss,
    gsr,
    gts,
    gtr,
    load_sem,
    credit,
    grad_in,
    grad_out,
    heads_ref,
    mixed_ref,
    lse_ref,
    cos_ref,
    sin_ref,
    start_ref,
    store_sems,
):
    here = Place(size)
    length, width = lhs.shape
    rows = length // 4
    units = first_r.shape[1]
    chunk = units // 2
    ff_part = units // size
    heads = mixed_ref.shape[1] // HEAD_DIM
    kv_heads = heads // 2
    qkv_width = qkv_full.shape[2]
    last = here.outer - 1
    scale = HEAD_DIM ** (-0.5)

    def load(source, target, index):
        copy = pltpu.make_async_copy(source, target, load_sem.at[index])
        copy.start()
        return copy

    def sems(index):
        return tuple(kind.at[index] for kind in (ys, yr, us, ur, ds, dr, fold_load))

    thin = qkv_width // 2
    cut = units * 2 // 3
    lanes = {
        "down_a": slice(0, cut),
        "down_b": slice(cut, units),
        "query": slice(0, thin),
        "key": slice(thin, 2 * thin),
    }

    def part(ref, name):
        return ref.at[:, :, :, lanes[name]]

    def row_sum(index, give_ref, keep_ref, near, rising, falling, stage_ref, total):
        return RowSum(
            here, give_ref, keep_ref, near, rising, falling, stage_ref, total, sems(index)
        )

    jobs = {
        "down_a": LineFirstSum(
            here,
            part(give.at[2], "down_a"),
            part(keep.at[0], "down_a"),
            part(near_mlp.at[0], "down_a"),
            (
                (rising_twin, falling_twin),
                (part(rising_mlp.at[0], "down_a"), part(falling_mlp.at[0], "down_a")),
            ),
            part(stage, "down_a"),
            keep.at[0, here.place, :, :, lanes["down_a"]],
            sems(0),
            sems(5),
        ),
        "down_b": row_sum(
            6,
            part(give.at[2], "down_b"),
            part(keep.at[0], "down_b"),
            part(near_mlp.at[0], "down_b"),
            part(rising_mlp.at[0], "down_b"),
            part(falling_mlp.at[0], "down_b"),
            part(stage, "down_b"),
            keep.at[0, here.place, :, :, lanes["down_b"]],
        ),
        "out": row_sum(
            4, give_out, keep_out, near_out, rising_out, falling_out, stage_out, grad_out
        ),
    }
    for index, name in ((1, "first"), (2, "second")):
        jobs[name] = row_sum(
            index,
            give.at[2 - index],
            keep.at[index],
            near_mlp.at[index],
            rising_mlp.at[index],
            falling_mlp.at[index],
            stage,
            keep.at[index, here.place],
        )
    for index, name in ((3, "query"), (7, "key")):
        jobs[name] = row_sum(
            index,
            part(give.at[1], name),
            part(second_r, name),
            part(near_qkv, name),
            part(rising_qkv, name),
            part(falling_qkv, name),
            part(stage, name),
            second_r.at[here.place, :, :, lanes[name]],
        )
    zones = width // 512

    def zone_at(index):
        zone = here.place // (here.outer // zones)
        return (
            3 * (1 - zone // 2),
            lax.rem(2 + 3 * zone, 5),
            1 + lax.rem(zone, 2),
            zone,
        )[index]

    zone_order = [zone_at(index) for index in range(zones)]
    by_zone = [(zone, (zone,)) for zone in zone_order]

    spreads = {}
    for index, (name, whole) in enumerate(
        (
            ("down_a", down_rows.at[:, :, lanes["down_a"]]),
            ("down_b", down_rows.at[:, :, lanes["down_b"]]),
            ("first", first_rows),
            ("second", second_rows),
            ("query", qkv_rows.at[:, :, lanes["query"]]),
            ("key", qkv_rows.at[:, :, lanes["key"]]),
        )
    ):
        kinds = (spread_s.at[index], spread_r.at[index], spread_l.at[index])
        spreads[name] = RowSpread(here, jobs[name].total, whole, kinds)

    def token_sum(index, base):
        return TokenSum(
            here, lhs, got, pair, far_got, base, (sum_s.at[index], sum_r.at[index])
        )

    sum_mlp = token_sum(0, middle_grad)
    sum_hidden = token_sum(1, grad_in)
    sum_attn = token_sum(2, grad_in)
    da = TokenGather(here, da_own, da_hbm, (ts, tr, token_local.at[0]))

    def model_tiles(group):
        return [(group, seq_group) for seq_group in range(4)]

    def first_columns(lane):
        return first_r[:, lane]

    def model_left(group):
        return turned[pl.ds(group * 4, 4)].reshape(512, length)

    def advance(steps):
        for name, step in steps:
            job = jobs[name]
            if step == "pass":
                job.pass_on()
            elif step == "finish":
                job.finish()
                if name in spreads:
                    spreads[name].send()
            else:
                for distance in range(last * step // 3, last * (step - 1) // 3, -1):
                    job.fold(distance)

    load_turned = load(dy_hbm, turned, 0)
    load_act = load(act_hbm, first_r, 1)
    load_middle = load(middle_hbm, grad_in, 2)
    load_dy = load(dy_own, da_own, 4)
    load_second = load(second_hbm, second_r, 3)
    eye[...] = identity(HEAD_DIM)
    late_loads = [
        load(source, target, 5 + index)
        for index, (source, target) in enumerate(
            (
                (mixed_hbm, mixed_ref),
                (lse_hbm, lse_ref),
                (heads_hbm, heads_ref),
                (cos_hbm, cos_ref),
                (sin_hbm, sin_ref),
                (start_hbm, start_ref),
            )
        )
    ]
    here.greet(wide=True)
    load_turned.wait()
    load_act.wait()
    def model_terms(give_ref, keep_ref, right, senders):
        compute_terms(
            here, give_ref, keep_ref, model_left, right, model_tiles, by_zone, senders
        )

    model_terms(give.at[2], keep.at[0], first_columns, [jobs["down_b"]])
    advance(PLAN[0])
    load_turned = load(n2_hbm, turned, 0)
    load_first = load(first_hbm, first_r, 1)
    load_first.wait()
    load_second.wait()

    own = width // size
    slabs = 256 // own

    def dn2_body(first_w, second_w):
        lane = pl.ds(pl.multiple_of(pl.program_id(0) * 256, 256), 256)
        first_tile = first_w[...].reshape(256, units)
        second_tile = second_w[...].reshape(256, units)

        @pl.loop(0, 2)
        def _(index):
            part = pl.ds(pl.multiple_of(index * 2 * rows, 2 * rows), 2 * rows)
            total = contract_cols(first_r[part, :], first_tile)
            blocks = pl.ds(index * (here.outer // 2), here.outer // 2)
            second_rows = second_r[blocks].reshape(2 * rows, units)
            total = total + contract_cols(second_rows, second_tile)
            lhs[part, lane] = total.astype(BF)

    slab = pl.BlockSpec((slabs, own, units), lambda t: (t, 0, 0))
    pltpu.emit_pipeline(dn2_body, grid=(width // 256,), in_specs=[slab, slab])(
        first_full, second_full
    )
    sum_mlp.send()
    middle_grad[...] = jnp.zeros_like(middle_grad)
    load_turned.wait()
    advance(PLAN[1])
    sum_mlp.pass_on()
    sum_mlp.add_near()
    model_terms(give.at[1], keep.at[1], first_columns, [jobs["first"]])
    load_act = load(act_hbm, first_r, 1)
    advance(PLAN[2])
    sum_mlp.add_far()

    load_middle.wait()
    load_dy.wait()
    gain_row[...] = jnp.zeros_like(gain_row)
    mlp_lane = slice(2 * HEAD_DIM, 2 * HEAD_DIM + width)
    attn_lane = slice(2 * HEAD_DIM + width, 2 * HEAD_DIM + 2 * width)
    narrow = 16

    @pl.loop(0, rows // narrow)
    def _(index):
        part = pl.ds(pl.multiple_of(index * narrow, narrow), narrow)
        values = grad_in[part, :]
        scales = lax.rsqrt(jnp.mean(values * values, axis=-1, keepdims=True) + EPSILON)
        normed = values * scales
        update = middle_grad[part, :]
        gain_row[:, mlp_lane] += jnp.sum(update * normed, axis=0, keepdims=True)
        upper = update * mlp_gain_ref[...]
        inner = jnp.mean(upper * normed, axis=-1, keepdims=True)
        grad = da_own[part, :].astype(F32) + scales * (upper - normed * inner)
        middle_grad[part, :] = grad
        da_own[part, :] = grad.astype(BF)

    da.send()
    advance(PLAN[3])
    model_terms(
        give.at[0],
        keep.at[2],
        lambda lane: second_r[:, :, :, lane].reshape(length, -1),
        [jobs["second"]],
    )
    advance(PLAN[4])

    def hidden_body(weight):
        lane = pl.ds(pl.multiple_of(pl.program_id(0) * 256, 256), 256)
        tile = weight[...]

        @pl.loop(0, 2)
        def _(index):
            part = pl.ds(pl.multiple_of(index * 2 * rows, 2 * rows), 2 * rows)
            lhs[part, lane] = dot(first_r[part, :], tile).astype(BF)

    load_act.wait()
    pltpu.emit_pipeline(
        hidden_body,
        grid=(width // 256,),
        in_specs=[pl.BlockSpec((units, 256), lambda t: (0, t))],
    )(down_full)
    da.mate_arrived()
    sum_hidden.send()
    da.forward()
    advance(PLAN[5])
    sum_hidden.pass_on()
    sum_hidden.add_near()
    advance(PLAN[6])
    da.rest_arrived()
    da.finish()
    load_lhs = load(da_hbm, lhs, 0)
    load_own = load(hidden_hbm, da_own, 2)
    load_lhs.wait()

    def dout_body(weight):
        lane = pl.ds(pl.multiple_of(pl.program_id(0) * 256, 256), 256)
        tile = weight[...].reshape(256, width)

        @pl.loop(0, 2)
        def _(index):
            part = pl.ds(pl.multiple_of(index * 2 * rows, 2 * rows), 2 * rows)
            dout_ref[part, lane] = contract_cols(lhs[part, :], tile).astype(BF)

    out_blocks, out_rows = out_full.shape[:2]
    pltpu.emit_pipeline(
        dout_body,
        grid=(out_blocks * out_rows // 256,),
        in_specs=[pl.BlockSpec((256 // out_rows, out_rows, width), lambda t: (t, 0, 0))],
    )(out_full)

    for late in late_loads:
        late.wait()
    for head in range(heads):
        lane = slice(head * HEAD_DIM, (head + 1) * HEAD_DIM)
        turned[head] = contract_cols(eye[...], mixed_ref[:, lane]).astype(BF)
    compute_terms(
        here,
        give_out,
        keep_out,
        lambda group: turned[0:heads].reshape(heads * HEAD_DIM, length),
        lambda lane: lhs[:, lane],
        lambda group: [(zone, 0) for zone in range(heads)],
        [(0, zone_order)],
        [jobs["out"]],
    )
    load_turned = load(n1_hbm, turned, 0)
    sum_hidden.add_far()
    for index, peer in enumerate((here.mate, here.far)):
        pl.semaphore_signal(credit.at[index], inc=1, device_id=peer, device_id_type=MESH)

    @pl.loop(0, rows // 32)
    def _(index):
        part = pl.ds(pl.multiple_of(index * 32, 32), 32)
        pair[part, :] = grad_in[part, :].astype(BF)

    store_hidden = load(pair, hidden_out, 1)
    advance(PLAN[7])

    lse_t[...] = lse_ref[...].T[0:8]
    delta[...] = jnp.zeros_like(delta)
    for head in range(heads):
        lane = slice(head * HEAD_DIM, (head + 1) * HEAD_DIM)
        terms = dout_ref[:, lane].astype(F32) * mixed_ref[:, lane].astype(F32)
        delta[:, head : head + 1] = jnp.sum(terms, axis=-1, keepdims=True)
    delta_t[...] = delta[...].T[0:8]
    def through_norm(grad, head, part, gain_ref, which):
        proj = proj_buf[part, :]
        scales = lax.rsqrt(jnp.mean(proj * proj, axis=-1, keepdims=True) + EPSILON)
        normed = proj * scales
        grad = grad.astype(F32)
        upper = grad * cos_ref[part, :] - pltpu.roll(grad, HEAD_DIM // 2, 1) * sin_ref[part, :]
        gain_row[:, which * HEAD_DIM : (which + 1) * HEAD_DIM] += jnp.sum(
            upper * normed, axis=0, keepdims=True
        )
        upper = upper * gain_ref[...]
        inner = jnp.mean(upper * normed, axis=-1, keepdims=True)
        result = (scales * (upper - normed * inner)).astype(BF)
        first_r[part, head * HEAD_DIM : (head + 1) * HEAD_DIM] = result

    for head in range(heads):
        pair_head = head // 2
        load_proj = load(proj_hbm.at[head], proj_buf, 4)
        if head % 2 == 0:
            dk_sum[...] = jnp.zeros_like(dk_sum)
            dv_sum[...] = jnp.zeros_like(dv_sum)
            keys_turned[...] = contract_cols(eye[...], heads_ref[heads + pair_head]).astype(BF)
        for block in range(4):
            end = (block + 1) * rows
            part = pl.ds(block * rows, rows)
            queries = heads_ref[head, part, :]
            keys = heads_ref[heads + pair_head, 0:end, :]
            values = heads_ref[heads + kv_heads + pair_head, 0:end, :]
            out_grad = dout_ref[part, head * HEAD_DIM : (head + 1) * HEAD_DIM]
            scores = contract_cols(keys, queries)
            key_place = lax.broadcasted_iota(jnp.int32, (end, rows), 0)
            query_place = lax.broadcasted_iota(jnp.int32, (end, rows), 1) + block * rows
            allowed = (key_place >= start_ref[:, part]) & (key_place <= query_place)
            weights = jnp.exp(scores * scale - lse_t[head : head + 1, part])
            weights = jnp.where(allowed, weights, 0.0)
            weight_grad = contract_cols(values, out_grad)
            inner = delta_t[head : head + 1, part]
            score_grad = (weights * (weight_grad - inner)).astype(BF)
            dk_sum[0:end, :] += dot(score_grad, queries) * scale
            dv_sum[0:end, :] += dot(weights.astype(BF), out_grad)
            query_grad = dot(keys_turned[:, 0:end], score_grad).T
            query_grad = (query_grad * scale).astype(BF)
            if block == 0:
                load_proj.wait()
            through_norm(query_grad, head, part, query_gain_ref, 0)
        if head % 2:
            key = heads + pair_head
            value_at = (heads + kv_heads + pair_head) * HEAD_DIM
            load(proj_hbm.at[key], proj_buf, 4).wait()

            @pl.loop(0, 4)
            def _(index):
                part = pl.ds(pl.multiple_of(index * rows, rows), rows)
                through_norm(dk_sum[part, :].astype(BF), key, part, key_gain_ref, 1)
                first_r[part, value_at : value_at + HEAD_DIM] = dv_sum[part, :].astype(BF)

        advance(PLAN[8 + head])

    load_turned.wait()
    jobs["first"].sent()
    store_hidden.wait()
    proj_grads = first_r.at[:, 0:qkv_width]
    model_terms(
        give.at[1, :, :, :, 0:qkv_width],
        second_r.at[:, :, :, 0:qkv_width],
        first_columns,
        [jobs["query"], jobs["key"]],
    )
    advance(PLAN[12])

    def dn1_body(weight):
        lane = pl.ds(pl.multiple_of(pl.program_id(0) * 256, 256), 256)
        tile = weight[...].reshape(256, qkv_width)

        @pl.loop(0, 2)
        def _(index):
            part = pl.ds(pl.multiple_of(index * 2 * rows, 2 * rows), 2 * rows)
            lhs[part, lane] = contract_cols(proj_grads[part, :], tile).astype(BF)

    pltpu.emit_pipeline(
        dn1_body,
        grid=(width // 256,),
        in_specs=[pl.BlockSpec((slabs, own, qkv_width), lambda t: (t, 0, 0))],
    )(qkv_full)
    grad_in[...] = jnp.zeros_like(grad_in)
    pl.semaphore_wait(credit.at[0], 1)
    pl.semaphore_wait(credit.at[1], 1)
    sum_attn.send()
    advance(PLAN[13])
    sum_attn.pass_on()
    sum_attn.add_near()
    advance(PLAN[14])
    sum_attn.add_far()
    load_own.wait()

    @pl.loop(0, rows // narrow)
    def _(index):
        part = pl.ds(pl.multiple_of(index * narrow, narrow), narrow)
        values = da_own[part, :].astype(F32)
        scales = lax.rsqrt(jnp.mean(values * values, axis=-1, keepdims=True) + EPSILON)
        normed = values * scales
        update = grad_in[part, :]
        gain_row[:, attn_lane] += jnp.sum(update * normed, axis=0, keepdims=True)
        upper = update * attn_gain_ref[...]
        inner = jnp.mean(upper * normed, axis=-1, keepdims=True)
        grad_in[part, :] = middle_grad[part, :] + scales * (upper - normed * inner)

    store_in = pltpu.make_async_copy(grad_in, grad_in_out, store_sems.at[0])
    store_in.start()
    gain_sum = GainSum(here, gain_row, gain_seq, gain_middle, gain_shard, (gss, gsr, gts, gtr))
    gain_sum.start()
    advance(PLAN[15])
    gain_sum.turn()
    advance(PLAN[16])
    gains_out[...] = gain_sum.finish()
    store_out = pltpu.make_async_copy(grad_out, grad_out_out, store_sems.at[1])
    store_out.start()
    for spread_rows in spreads.values():
        spread_rows.arrive()
    store_in.wait()
    store_out.wait()
    for name, job in jobs.items():
        if name != "first":
            job.sent()
    for job in jobs.values():
        job.settle()
    for job in spreads.values():
        job.finish()


def backward(saved, weights, own, gains, tables, starts):
    size = lax.axis_size("shard")
    outer = size // 2
    (n1, dy, n2, act, first, second, proj, heads_all, mixed, lse, middle) = saved
    length, width = heads_all.shape[1], middle.shape[1]
    piece = length // 4
    units = act.shape[1]
    qkv_width = weights[0].shape[2]
    rows = width // (4 * size)
    q_width = mixed.shape[1]

    def shape(*dims, kind=BF):
        return jax.ShapeDtypeStruct(dims, kind)

    results = [
        shape(piece, width, kind=F32),
        shape(1, 2 * width + 2 * HEAD_DIM, kind=F32),
        shape(1, rows, width, kind=F32),
        shape(piece, width),
        shape(4, rows, units),
        shape(4, rows, units),
        shape(4, rows, units),
        shape(4, rows, qkv_width),
        shape(length, width),
    ]
    results += [shape(3, outer, 4, rows, units)] * 3
    results += [shape(outer, 4, rows, units * 2 // 3)] * 2
    results += [shape(outer, 4, rows, qkv_width)] * 3
    results += [shape(outer, 1, rows, width)] * 3
    dma = pltpu.SemaphoreType.DMA
    vmem = pltpu.VMEM
    return pl.pallas_call(
        functools.partial(backward_kernel, size),
        out_shape=results,
        in_specs=[ANY] * 18 + [VMEM] * 4 + [ANY] * 3,
        out_specs=[ANY, VMEM] + [ANY] * (len(results) - 2),
        scratch_shapes=[
            vmem((length, width), BF),
            vmem((width // 128, 128, length), BF),
            vmem((length, units), BF),
            vmem((outer, 4, rows, units), BF),
            vmem((3, outer, 4, rows, units), BF),
            vmem((3, outer, 4, rows, units), BF),
            vmem((outer, 1, rows, width), BF),
            vmem((outer, 1, rows, width), BF),
            vmem((2, 4, rows, units), BF),
            vmem((2, 1, rows, width), BF),
            vmem((length, q_width), BF),
            vmem((piece, width), BF),
            vmem((2, piece, width), BF),
            vmem((piece, width), BF),
            vmem((piece, width), BF),
            vmem((piece, width), F32),
            vmem((length, HEAD_DIM), F32),
            vmem((HEAD_DIM, HEAD_DIM), BF),
            vmem((HEAD_DIM, length), BF),
            vmem((8, length), F32),
            vmem((length, 128), F32),
            vmem((8, length), F32),
            vmem((length, HEAD_DIM), F32),
            vmem((length, HEAD_DIM), F32),
            vmem((1, 2 * width + 2 * HEAD_DIM), F32),
            vmem((4, 1, 2 * width + 2 * HEAD_DIM), F32),
            vmem((1, 2 * width + 2 * HEAD_DIM), F32),
            vmem((size, 1, 2 * width + 2 * HEAD_DIM), F32),
            dma((8, outer)),
            dma((8, outer)),
            dma((8, outer)),
            dma((8, outer)),
            dma((8, outer)),
            dma((8, outer)),
            dma((8, 3)),
            dma((6, 3)),
            dma((6, 3)),
            dma((6,)),
            dma((3, 3)),
            dma((3, 3)),
            dma((3,)),
            dma((3,)),
            dma((1,)),
            dma((3,)),
            dma((3,)),
            dma((size - 1,)),
            dma((size - 1,)),
            dma((11,)),
            pltpu.SemaphoreType.REGULAR((2,)),
            vmem((piece, width), F32),
            vmem((1, rows, width), F32),
            vmem(heads_all.shape, BF),
            vmem(mixed.shape, BF),
            vmem(lse.shape, F32),
            vmem((length, HEAD_DIM), F32),
            vmem((length, HEAD_DIM), F32),
            vmem((1, length), jnp.int32),
            dma((2,)),
        ],
        compiler_params=pltpu.CompilerParams(
            collective_id=1, has_side_effects=True, vmem_limit_bytes=VMEM_BYTES
        ),
        name="backward_sums",
    )(
        n1,
        dy,
        n2,
        act,
        first,
        second.reshape(outer, 4, rows, units),
        proj,
        heads_all,
        mixed,
        lse,
        middle,
        *own,
        *weights,
        *gains,
        *tables,
        starts,
    )


def finish_kernel(
    size,
    grad_in,
    gains,
    grad_out,
    hidden_out,
    down_rows,
    first_rows,
    second_rows,
    qkv_rows,
    grad_in_out,
    grad_out_out,
    hidden_out_out,
    grad_query,
    grad_key,
    grad_value,
    grad_gate,
    grad_up,
    grad_down,
    attn_gain,
    mlp_gain,
    query_gain,
    key_gain,
    grad_in_buf,
    grad_out_buf,
    hidden_buf,
    down_buf,
    first_buf,
    second_buf,
    qkv_buf,
    query_buf,
    key_buf,
    value_buf,
    gate_buf,
    up_buf,
    wide_buf,
    load_sems,
    store_sems,
):
    units = down_buf.shape[2]
    chunk = units // 2
    ff_part = units // size
    most, tail = chunk - 256, 256
    stores = []

    def load(source, target, index):
        copy = pltpu.make_async_copy(source, target, load_sems.at[index])
        copy.start()
        return copy

    def store(source, target):
        copy = pltpu.make_async_copy(source, target, store_sems.at[len(stores)])
        copy.start()
        stores.append(copy)

    loads = [
        load(source, target, index)
        for index, (source, target) in enumerate(
            (
                (down_rows, down_buf),
                (first_rows, first_buf),
                (second_rows, second_buf),
                (qkv_rows, qkv_buf),
                (grad_in, grad_in_buf),
                (hidden_out, hidden_buf),
                (grad_out, grad_out_buf),
            )
        )
    ]

    def place(read, target):
        @pl.loop(0, target.shape[0] // 16)
        def _(index):
            part = pl.ds(pl.multiple_of(index * 16, 16), 16)
            values = [read(seq, part).astype(F32) for seq in range(4)]
            for begin in range(0, size, size // 8):
                pieces = [
                    values[seq][:, block * ff_part : (block + 1) * ff_part]
                    for block in range(begin, begin + size // 8)
                    for seq in range(4)
                ]
                lane = slice(begin * 4 * ff_part, (begin + size // 8) * 4 * ff_part)
                target[part, lane] = jnp.concatenate(pieces, axis=1)

    def side(index):
        at = 2 * most + index * tail

        def read(seq, part):
            return jnp.concatenate(
                [
                    first_buf[seq, part, index * chunk : (index + 1) * chunk],
                    second_buf[seq, part, index * most : (index + 1) * most],
                    second_buf[seq, part, at : at + tail],
                ],
                axis=1,
            )

        return read

    loads[0].wait()
    place(lambda seq, part: down_buf[seq, part, :], wide_buf)
    store(wide_buf, grad_down)
    loads[1].wait()
    loads[2].wait()
    place(side(0), gate_buf)
    store(gate_buf, grad_gate)
    place(side(1), up_buf)
    store(up_buf, grad_up)
    loads[4].wait()
    store(grad_in_buf, grad_in_out)
    loads[5].wait()
    store(hidden_buf, hidden_out_out)
    loads[6].wait()
    store(grad_out_buf, grad_out_out)
    loads[3].wait()
    at = 0
    for buf, target in ((query_buf, grad_query), (key_buf, grad_key), (value_buf, grad_value)):
        count = buf.shape[1] // 4
        for seq in range(4):
            buf[:, seq * count : (seq + 1) * count] = qkv_buf[seq, :, at : at + count].astype(F32)
        at += count
        store(buf, target)
    at = 0
    for target in (query_gain, key_gain, mlp_gain, attn_gain):
        target[...] = gains[:, at : at + target.shape[1]]
        at += target.shape[1]
    for copy in stores:
        copy.wait()


def finish(grad_in, gains, grad_out, hidden_out, down_rows, first_rows, second_rows, qkv_rows):
    size = lax.axis_size("shard")
    piece, width = grad_in.shape
    rows, units = down_rows.shape[1:]
    qkv_width = qkv_rows.shape[2]

    def shape(*dims, kind=F32):
        return jax.ShapeDtypeStruct(dims, kind)

    results = [
        shape(piece, width),
        shape(1, rows, width),
        shape(piece, width, kind=BF),
        shape(rows, 2 * qkv_width),
        shape(rows, qkv_width),
        shape(rows, qkv_width),
        shape(rows, 4 * units),
        shape(rows, 4 * units),
        shape(rows, 4 * units),
        shape(1, width),
        shape(1, width),
        shape(1, HEAD_DIM),
        shape(1, HEAD_DIM),
    ]
    return pl.pallas_call(
        functools.partial(finish_kernel, size),
        out_shape=results,
        in_specs=[ANY, VMEM] + [ANY] * 6,
        out_specs=[ANY] * 9 + [VMEM] * 4,
        scratch_shapes=[
            pltpu.VMEM((piece, width), F32),
            pltpu.VMEM((1, rows, width), F32),
            pltpu.VMEM((piece, width), BF),
            pltpu.VMEM((4, rows, units), BF),
            pltpu.VMEM((4, rows, units), BF),
            pltpu.VMEM((4, rows, units), BF),
            pltpu.VMEM((4, rows, qkv_width), BF),
            pltpu.VMEM((rows, 2 * qkv_width), F32),
            pltpu.VMEM((rows, qkv_width), F32),
            pltpu.VMEM((rows, qkv_width), F32),
            pltpu.VMEM((rows, 4 * units), F32),
            pltpu.VMEM((rows, 4 * units), F32),
            pltpu.VMEM((rows, 4 * units), F32),
            pltpu.SemaphoreType.DMA((7,)),
            pltpu.SemaphoreType.DMA((9,)),
        ],
        compiler_params=pltpu.CompilerParams(vmem_limit_bytes=VMEM_BYTES),
        name="finish",
    )(grad_in, gains, grad_out, hidden_out, down_rows, first_rows, second_rows, qkv_rows)


def local(
    hidden_in,
    segment_ids,
    norm_attn_gain,
    w_query,
    w_key,
    w_value,
    query_gain,
    key_gain,
    w_out,
    norm_mlp_gain,
    w_gate,
    w_up,
    w_down,
    out_cotangent,
):
    segment = segment_ids[0]
    gains = (norm_attn_gain[None], norm_mlp_gain[None], query_gain[None], key_gain[None])
    results = forward(
        hidden_in[0],
        out_cotangent[0],
        (w_query, w_key, w_value, w_out, w_gate, w_up, w_down),
        gains,
        segment,
    )
    (
        grad_in,
        grad_out,
        hidden_out,
        grad_query,
        grad_key,
        grad_value,
        grad_gate,
        grad_up,
        grad_down,
        attn_gain,
        mlp_gain,
        query_grad,
        key_grad,
    ) = finish(
        *backward(
            results[8:19],
            results[:5],
            (hidden_in[0], out_cotangent[0]),
            gains,
            results[19:21],
            results[21],
        )[:8]
    )
    return (
        hidden_out[None],
        grad_in[None],
        attn_gain[0],
        grad_query,
        grad_key,
        grad_value,
        query_grad[0],
        key_grad[0],
        grad_out[0],
        mlp_gain[0],
        grad_gate,
        grad_up,
        grad_down.T,
    )


def solution(mesh):
    return jax.shard_map(
        local,
        mesh=mesh,
        in_specs=(
            P("shard", "seq", None),
            P("shard", None),
            P(),
            P("shard", None),
            P("shard", None),
            P("shard", None),
            P(),
            P(),
            P("shard", None),
            P(),
            P("shard", None),
            P("shard", None),
            P("shard", None),
            P("shard", "seq", None),
        ),
        out_specs=(
            P("shard", "seq", None),
            P("shard", "seq", None),
            P(),
            P(("seq", "shard"), None),
            P(("seq", "shard"), None),
            P(("seq", "shard"), None),
            P(),
            P(),
            P(("seq", "shard"), None),
            P(),
            P(("seq", "shard"), None),
            P(("seq", "shard"), None),
            P(None, ("seq", "shard")),
        ),
        check_vma=False,
    )
```

```python
import functools

import jax
import jax.numpy as jnp
import numpy as np
from jax import lax
from jax.experimental import pallas as pl
from jax.experimental.pallas import tpu as pltpu
from jax.sharding import PartitionSpec as P

Q_HEADS = 16
KV_HEADS = 8
HEAD_DIM = 128
EPSILON = 1e-06
ROPE_BASE = 1000000.0
NEGATIVE = -1e30
BF = jnp.bfloat16
F32 = jnp.float32
MESH = pl.DeviceIdType.MESH
ANY = pl.BlockSpec(memory_space=pl.ANY)
VMEM = pl.BlockSpec(memory_space=pltpu.VMEM)
VMEM_BYTES = 62 * 1024 * 1024


def dot(left, right):
    return jnp.dot(left, right, preferred_element_type=F32)


def contract_cols(left, right):
    return lax.dot_general(left, right, (((1,), (1,)), ((), ())), preferred_element_type=F32)


class Place:
    def __init__(self, size):
        self.size = size
        self.outer = size // 2
        self.quarter = size // 4
        self.seq = lax.axis_index("seq")
        self.shard = lax.axis_index("shard")
        self.chip = self.seq // 2
        self.core = lax.rem(self.seq, 2)
        self.place = self.shard // 2
        self.half = lax.rem(self.shard, 2)
        self.far_seq = lax.rem(self.seq + 2, 4)
        self.mate_seq = self.chip * 2 + 1 - self.core
        self.far = {"seq": self.far_seq}
        self.mate = {"seq": self.mate_seq}
        self.twin_shard = self.place * 2 + 1 - self.half
        self.twin = {"shard": self.twin_shard}

    def outer_peer(self, place):
        return {"shard": place * 2 + self.half}

    def greet(self, wide=False):
        barrier = pltpu.get_barrier_semaphore()
        last = self.outer - 1

        def signal(peer):
            pl.semaphore_signal(barrier, inc=1, device_id=peer, device_id_type=MESH)

        signal(self.far)
        signal(self.mate)
        if wide:
            signal({"seq": 3 - self.seq})
            for amount in range(1, self.size):
                signal({"shard": lax.rem(self.shard + amount, self.size)})
            pl.semaphore_wait(barrier, 2 + self.size)
            return
        signal(self.twin)

        @pl.when(self.place < last)
        def _():
            signal(self.outer_peer(self.place + 1))

        @pl.when(self.place > 0)
        def _():
            signal(self.outer_peer(self.place - 1))

        inner = ((self.place > 0) & (self.place < last)).astype(jnp.int32)
        pl.semaphore_wait(barrier, 4 + inner)


def remote(source, target, send, receive, peer):
    return pltpu.make_async_remote_copy(
        src_ref=source,
        dst_ref=target,
        send_sem=send,
        recv_sem=receive,
        device_id=peer,
        device_id_type=MESH,
    )


class LineGather:
    def __init__(self, here, own, slot, sems):
        self.here, self.own, self.slot = here, own, slot
        self.us, self.ur, self.ds, self.dr = sems
        self.last = here.outer - 1

    def up(self, distance):
        here = self.here
        slot = self.slot(here.place - distance)
        source = slot if distance else self.own
        peer = here.outer_peer(here.place + 1)
        return remote(source, slot, self.us.at[distance], self.ur.at[distance], peer)

    def down(self, distance):
        here = self.here
        slot = self.slot(here.place + distance)
        source = slot if distance else self.own
        peer = here.outer_peer(here.place - 1)
        return remote(source, slot, self.ds.at[distance], self.dr.at[distance], peer)

    def send(self):
        here = self.here

        @pl.when(here.place < self.last)
        def _():
            self.up(0).start()

        @pl.when(here.place > 0)
        def _():
            self.down(0).start()

    def step(self, distance, arrived=lambda place: None):
        here = self.here
        below = here.place - 1 - distance
        above = here.place + 1 + distance

        @pl.when(below >= 0)
        def _():
            slot = self.slot(below)
            remote(slot, slot, self.us.at[0], self.ur.at[distance], here.twin).wait_recv()

            @pl.when(here.place < self.last)
            def _():
                self.up(distance + 1).start()

            arrived(below)

        @pl.when(above <= self.last)
        def _():
            slot = self.slot(above)
            remote(slot, slot, self.ds.at[0], self.dr.at[distance], here.twin).wait_recv()

            @pl.when(here.place > 0)
            def _():
                self.down(distance + 1).start()

            arrived(above)

    def finish(self):
        here = self.here
        for distance in range(self.last):

            @pl.when((here.place - distance >= 0) & (here.place < self.last))
            def _():
                self.up(distance).wait_send()

            @pl.when((here.place + distance <= self.last) & (here.place > 0))
            def _():
                self.down(distance).wait_send()


class RowGather:
    def __init__(self, here, own, whole, sems, spot=lambda shard: shard):
        self.here, self.own, self.whole, self.spot = here, own, whole, spot
        self.ys, self.yr, self.local = sems[4:]
        self.line = LineGather(here, own, self.mine, sems[:4])

    def mine(self, place):
        return self.whole.at[self.spot(place * 2 + self.here.half)]

    def theirs(self, place):
        return self.whole.at[self.spot(place * 2 + 1 - self.here.half)]

    def keep(self):
        return pltpu.make_async_copy(self.own, self.mine(self.here.place), self.local)

    def across(self, place, own=False):
        slot = self.mine(place)
        source = self.own if own else slot
        return remote(source, slot, self.ys.at[place], self.yr.at[place], self.here.twin)

    def arrived(self, place):
        slot = self.theirs(place)
        remote(slot, slot, self.ys.at[place], self.yr.at[place], self.here.twin).wait_recv()

    def send(self):
        self.line.send()
        self.across(self.here.place, own=True).start()
        self.keep().start()

    def step(self, distance):
        self.line.step(distance, lambda place: self.across(place).start())

    def arrive(self):
        self.keep().wait()
        for place in range(self.here.outer):
            self.arrived(place)

    def finish(self):
        self.line.finish()
        for place in range(self.here.outer):
            self.across(place).wait_send()


class TwinFirstGather(RowGather):
    def __init__(self, here, own, whole, sems, twin_sems):
        super().__init__(here, own, whole, sems)
        self.lines = [
            self.line,
            LineGather(here, self.theirs(here.place), self.theirs, twin_sems[:4]),
        ]

    def twin(self):
        self.arrived(self.here.place)
        self.lines[1].send()

    def step(self, distance):
        for line in self.lines:
            line.step(distance)

    def arrive(self):
        self.keep().wait()

    def finish(self):
        for line in self.lines:
            line.finish()
        self.across(self.here.place, own=True).wait_send()


class HeadGather:
    def __init__(self, here, own, whole, sems):
        self.here, self.own, self.whole = here, own, whole
        self.us, self.zr, self.ds, _, self.ys, self.yr, self.local = sems
        self.last = here.outer - 1
        self.count = here.quarter // 2
        self.first = here.seq * self.count
        self.mine = here.place - self.first
        self.inside = (self.mine >= 0) & (self.mine < self.count)

    def slot(self, index):
        return self.whole.at[index * 2 + self.here.half]

    def keep(self):
        return pltpu.make_async_copy(self.own, self.slot(self.mine), self.local)

    def up(self, index, own=False):
        slot = self.slot(index)
        peer = self.here.outer_peer(self.here.place + 1)
        return remote(self.own if own else slot, slot, self.us.at[index], self.zr.at[index], peer)

    def down(self, index, own=False):
        slot = self.slot(index)
        peer = self.here.outer_peer(self.here.place - 1)
        return remote(self.own if own else slot, slot, self.ds.at[index], self.zr.at[index], peer)

    def across(self, index):
        slot = self.slot(index)
        return remote(slot, slot, self.ys.at[index], self.yr.at[index], self.here.twin)

    def send(self):
        @pl.when(self.inside)
        def _():
            self.keep().start()

            @pl.when(self.here.place < self.last)
            def _():
                self.up(self.mine, own=True).start()

            @pl.when(self.here.place > 0)
            def _():
                self.down(self.mine, own=True).start()

    def step(self):
        here = self.here

        @pl.when(self.inside)
        def _():
            self.keep().wait()

        for index in range(self.count):
            slot = self.slot(index)
            arrival = remote(slot, slot, self.us.at[0], self.zr.at[index], here.twin)

            @pl.when(self.mine > index)
            def _():
                arrival.wait_recv()

                @pl.when(here.place < self.last)
                def _():
                    self.up(index).start()

            @pl.when(self.mine < index)
            def _():
                arrival.wait_recv()

                @pl.when(here.place > 0)
                def _():
                    self.down(index).start()

            self.across(index).start()

    def arrive(self):
        for index in range(self.count):
            slot = self.whole.at[index * 2 + 1 - self.here.half]
            remote(
                slot, slot, self.ys.at[index], self.yr.at[index], self.here.twin
            ).wait_recv()

    def finish(self):
        here = self.here
        for index in range(self.count):

            @pl.when((self.mine >= index) & (here.place < self.last))
            def _():
                self.up(index).wait_send()

            @pl.when((self.mine <= index) & (here.place > 0))
            def _():
                self.down(index).wait_send()

            self.across(index).wait_send()


class TokenGather:
    def __init__(self, here, own, whole, sems):
        self.here, self.own, self.whole = here, own, whole
        self.send_sems, self.recv_sems, self.local = sems
        self.rows = whole.shape[0] // 4

    def slot(self, seq):
        return self.whole.at[pl.ds(pl.multiple_of(seq * self.rows, self.rows), self.rows), :]

    def keep(self):
        return pltpu.make_async_copy(self.own, self.slot(self.here.seq), self.local)

    def copy(self, index):
        here = self.here
        slot = self.slot(here.far_seq if index == 2 else here.seq)
        return remote(
            slot if index == 2 else self.own,
            slot,
            self.send_sems.at[index],
            self.recv_sems.at[index],
            here.far if index == 0 else here.mate,
        )

    def send(self):
        self.copy(0).start()
        self.copy(1).start()
        self.keep().start()

    def forward(self):
        self.copy(0).wait_recv()
        self.copy(2).start()

    def mate_arrived(self):
        self.copy(1).wait_recv()

    def rest_arrived(self):
        self.copy(2).wait_recv()
        self.keep().wait()

    def arrive(self):
        self.mate_arrived()
        self.rest_arrived()

    def finish(self):
        for index in range(3):
            self.copy(index).wait_send()


class PieceSum:
    def __init__(self, here, piece, base, give, got, pair, far_got, sems, step):
        self.here, self.piece, self.base, self.step = here, piece, base, step
        self.give, self.got, self.pair, self.far_got = give, got, pair, far_got
        self.send_sems, self.recv_sems = sems

    def to_mate(self, index):
        return remote(
            self.give.at[index],
            self.got.at[index],
            self.send_sems.at[index],
            self.recv_sems.at[index],
            self.here.mate,
        )

    def to_far(self):
        return remote(
            self.pair, self.far_got, self.send_sems.at[2], self.recv_sems.at[2], self.here.far
        )

    def columns(self, body):
        step = self.step

        @pl.loop(0, self.pair.shape[1] // step)
        def _(index):
            body(pl.ds(pl.multiple_of(index * step, step), step))

    def send(self):
        here = self.here
        for index, chip in enumerate((1 - here.chip, here.chip)):
            seq = chip * 2 + 1 - here.core

            def fill(column, index=index, seq=seq):
                self.give[index, :, column] = self.piece(seq, column).astype(BF)

            self.columns(fill)
            self.to_mate(index).start()

    def pass_on(self):
        self.to_mate(0).wait_recv()

        def fill(column):
            term = self.piece(self.here.far_seq, column) + self.got[0, :, column].astype(F32)
            self.pair[:, column] = term.astype(BF)

        self.columns(fill)
        self.to_far().start()

    def add_near(self):
        self.to_mate(1).wait_recv()

        def fill(column):
            term = self.piece(self.here.seq, column) + self.got[1, :, column].astype(F32)
            self.base[:, column] += term

        self.columns(fill)

    def add_far(self):
        self.to_far().wait_recv()

        def fill(column):
            self.base[:, column] += self.far_got[:, column].astype(F32)

        self.columns(fill)
        for copy in (self.to_mate(0), self.to_mate(1), self.to_far()):
            copy.wait_send()


def identity(size):
    rows = lax.broadcasted_iota(jnp.int32, (size, size), 0)
    columns = lax.broadcasted_iota(jnp.int32, (size, size), 1)
    return jnp.where(rows == columns, 1.0, 0.0).astype(BF)


FORWARD_PLAN = (
    (("down", "send"),),
    (("out", "send"),),
    (("down", 0),),
    (),
    (),
    (("down", 1), ("down", 2), ("out", 0),),
    (),
    (),
    (("first", "send"),),
    (),
    (("second", "send"),),
    (),
    (),
    (("first", 0),),
    (),
    (),
    (("third", "send"),),
    (("first", 1),),
    (),
    (("second", "twin"), ("second", 0), ("first", 2),),
    (("third", 0),),
    (("second", 1),),
    (),
    (),
    (("third", 1),),
    (),
    (("second", 2), ("third", 2),),
    (),
    (),
)


def forward_kernel(
    size,
    hidden_hbm,
    dy_hbm,
    w_query,
    w_key,
    w_value,
    w_out,
    w_gate,
    w_up,
    w_down,
    attn_gain_ref,
    mlp_gain_ref,
    query_gain_ref,
    key_gain_ref,
    inverse_ref,
    segment_ref,
    qkv_full,
    out_full,
    first_full,
    second_full,
    down_full,
    n1_full,
    dy_full,
    n2_full,
    n1_turned,
    dy_turned,
    n2_turned,
    act_out,
    first_pair,
    second_pair,
    proj_out,
    heads_out,
    mixed_out,
    lse_out,
    middle_out,
    cos_out,
    sin_out,
    start_out,
    lhs,
    dy_all,
    turned,
    qkv_w,
    out_w,
    qkv_own,
    out_own,
    down_own,
    dy_own,
    wide_own,
    first_own,
    second_own,
    own_rows,
    give,
    got,
    pair,
    far_got,
    us,
    ur,
    ds,
    dr,
    ys,
    yr,
    row_local,
    ts,
    tr,
    token_local,
    load_sem,
    ss,
    sr,
    start_ref,
    turned_ids,
    eye,
    hidden_ref,
    proj_ref,
    heads_ref,
    mixed_ref,
    lse_ref,
    middle_ref,
    cos_ref,
    sin_ref,
    start_row,
    store_sems,
):
    here = Place(size)
    last = here.outer - 1
    length, width = lhs.shape
    lse_ref[...] = jnp.zeros_like(lse_ref)
    rows = length // 4
    units = act_out.shape[1]
    chunk = units // 2
    tail = 256
    heads = mixed_ref.shape[1] // HEAD_DIM
    kv_heads = heads // 2
    ff_part = units // size

    def sems(index):
        return tuple(kind.at[index] for kind in (us, ur, ds, dr, ys, yr, row_local))

    down_rows = pl.ds(pl.multiple_of(here.seq * ff_part, ff_part), ff_part)
    qkv = RowGather(here, qkv_own, qkv_full, sems(0))
    out = HeadGather(here, out_own, out_full, sems(1))
    down = RowGather(
        here,
        down_own,
        down_full,
        sems(2),
        lambda shard: pl.ds(pl.multiple_of(shard * ff_part, ff_part), ff_part),
    )
    first = RowGather(here, first_own, first_full, sems(3))
    cut = 2 * (chunk - tail)
    second = TwinFirstGather(
        here, second_own.at[:, 0:cut], second_full.at[:, :, 0:cut], sems(4), sems(6)
    )
    third = RowGather(
        here, second_own.at[:, cut : 2 * chunk], second_full.at[:, :, cut : 2 * chunk], sems(5)
    )
    n1 = TokenGather(here, own_rows.at[0], n1_full, (ts.at[0], tr.at[0], token_local.at[0]))
    n2 = TokenGather(here, own_rows.at[1], n2_full, (ts.at[1], tr.at[1], token_local.at[1]))
    dy = TokenGather(here, dy_own, dy_full, (ts.at[2], tr.at[2], token_local.at[2]))

    loads = []
    stores = []

    def hand_out(*pairs):
        for source, target in pairs:
            copy = pltpu.make_async_copy(source, target, store_sems.at[len(stores)])
            copy.start()
            stores.append(copy)

    load_hidden = pltpu.make_async_copy(hidden_hbm, hidden_ref, load_sem.at[8])
    at = 0
    for index, (weight, count) in enumerate(((w_query, heads), (w_key, kv_heads), (w_value, kv_heads))):
        count = count * HEAD_DIM
        source = weight.at[:, pl.ds(pl.multiple_of(here.seq * count, count), count)]
        loads.append(
            pltpu.make_async_copy(source, qkv_own.at[:, at : at + count], load_sem.at[index])
        )
        at += count
    loads.append(pltpu.make_async_copy(w_down.at[down_rows, :], down_own, load_sem.at[3]))
    loads.append(pltpu.make_async_copy(w_out, out_own, load_sem.at[4]))
    loads.append(pltpu.make_async_copy(dy_hbm, dy_own, load_sem.at[5]))
    loads.append(pltpu.make_async_copy(w_gate, wide_own, load_sem.at[6]))
    for load in loads:
        load.start()
    load_hidden.start()
    here.greet()
    for load in loads[:3]:
        load.wait()
    qkv.send()
    loads[5].wait()
    dy.send()

    def norm_rows(source, gain_ref, target):
        @pl.loop(0, rows // 32)
        def _(index):
            part = pl.ds(pl.multiple_of(index * 32, 32), 32)
            values = source[part, :].astype(F32)
            scales = lax.rsqrt(jnp.mean(values * values, axis=-1, keepdims=True) + EPSILON)
            target[part, :] = (values * scales * gain_ref[...]).astype(BF)

    gathers = {"out": out, "down": down, "first": first, "second": second, "third": third}

    def advance(steps):
        for name, step in steps:
            gather = gathers[name]
            if step == "send":
                gather.send()
            elif step == "twin":
                gather.twin()
            elif name == "out":
                gather.step()
            else:
                for distance in range(last * step // 3, last * (step + 1) // 3):
                    gather.step(distance)

    load_hidden.wait()
    norm_rows(hidden_ref, attn_gain_ref, own_rows.at[0])
    n1.send()
    for load in loads[3:5]:
        load.wait()
    advance(FORWARD_PLAN[0])
    for load in loads[6:]:
        load.wait()

    most = chunk - tail

    def cut_units(side):
        for seq in range(4):

            @pl.when(here.seq == seq)
            def _():
                @pl.loop(0, wide_own.shape[0] // 16)
                def _(index):
                    part = pl.ds(pl.multiple_of(index * 16, 16), 16)

                    def gathered(begin):
                        pieces = [
                            wide_own[part, (block * 4 + seq) * ff_part : (block * 4 + seq + 1) * ff_part]
                            for block in range(begin, begin + size // 2)
                        ]
                        return jnp.concatenate(pieces, axis=1)

                    first_own[part, side * chunk : (side + 1) * chunk] = gathered(0)
                    rest = gathered(size // 2)
                    second_own[part, side * most : (side + 1) * most] = rest[:, 0:most]
                    at = 2 * most + side * tail
                    second_own[part, at : at + tail] = rest[:, most:]

    eye[...] = identity(256)

    def rotation():
        ids = segment_ref[...].astype(F32)
        turned_ids[...] = jnp.broadcast_to(ids, (128, length)).T
        lane = lax.broadcasted_iota(jnp.int32, (128, 128), 1)

        @pl.loop(0, length // 128)
        def _(index):
            part = pl.ds(pl.multiple_of(index * 128, 128), 128)
            own_ids = turned_ids[part, :]
            count = jnp.zeros((128, 128), F32)
            for at in range(0, length, 128):
                count = count + jnp.where(
                    segment_ref[:, at : at + 128].astype(F32) < own_ids, 1.0, 0.0
                )
            starts = jnp.sum(count, axis=-1, keepdims=True)
            start_ref[part, :] = starts.astype(jnp.int32)
            starts = jnp.broadcast_to(starts, (128, 128))
            turned_ids[part, :] = starts
            places = lax.broadcasted_iota(jnp.int32, (128, 128), 0) + index * 128
            angles = (places.astype(F32) - starts) * inverse_ref[...]
            cos_ref[part, :] = jnp.cos(angles)
            sine = jnp.sin(angles)
            sin_ref[part, :] = jnp.where(lane < HEAD_DIM // 2, -sine, sine)

        start_row[...] = turned_ids[...].T[0:1].astype(jnp.int32)

    zones = width // 512

    def turn(source, target):
        for seq_group in range(4):
            for zone in range(0, zones, 2):
                at = (seq_group * zones + zone) * 128
                both = contract_cols(eye[...], source[:, at : at + 256]).astype(BF)
                turned[zone * 4 + seq_group] = both[0:128]
                turned[zone * 4 + 4 + seq_group] = both[128:256]
        copy = pltpu.make_async_copy(turned, target, load_sem.at[4])
        copy.start()
        return copy

    cut_units(0)
    load_up = pltpu.make_async_copy(w_up, wide_own, load_sem.at[7])
    load_up.start()
    load_up.wait()
    cut_units(1)
    advance(FORWARD_PLAN[1])
    for third_part in range(3):
        for distance in range(last * third_part // 3, last * (third_part + 1) // 3):
            qkv.step(distance)
        advance(FORWARD_PLAN[2 + third_part])
        if third_part == 0:
            rotation()
            hand_out((cos_ref, cos_out), (sin_ref, sin_out), (start_row, start_out))
            dy.forward()
    dy.arrive()
    load_dy = pltpu.make_async_copy(dy_full, dy_all, load_sem.at[0])
    load_dy.start()
    load_dy.wait()
    store = turn(dy_all, dy_turned)
    n1.forward()
    advance(FORWARD_PLAN[5])
    n1.arrive()
    load_lhs = pltpu.make_async_copy(n1_full, lhs, load_sem.at[0])
    load_lhs.start()
    advance(FORWARD_PLAN[6])
    qkv.arrive()
    load_qkv = pltpu.make_async_copy(qkv_full, qkv_w, load_sem.at[1])
    load_qkv.start()
    advance(FORWARD_PLAN[7])
    load_lhs.wait()
    load_qkv.wait()

    def project(tile):
        weight = qkv_w[:, :, tile * 256 : tile * 256 + 256].reshape(width, 256)
        gain_ref = query_gain_ref if tile < heads // 2 else key_gain_ref

        @pl.loop(0, 2)
        def _(index):
            part = pl.ds(pl.multiple_of(index * 2 * rows, 2 * rows), 2 * rows)
            both = dot(lhs[part, :], weight)
            for side in range(2):
                head = tile * 2 + side
                proj = both[:, side * HEAD_DIM : (side + 1) * HEAD_DIM]
                if head >= heads + kv_heads:
                    heads_ref[head, part, :] = proj.astype(BF)
                    continue
                proj_ref[head, part, :] = proj
                scales = lax.rsqrt(jnp.mean(proj * proj, axis=-1, keepdims=True) + EPSILON)
                gained = proj * scales * gain_ref[...]
                turned = pltpu.roll(gained, HEAD_DIM // 2, 1)
                heads_ref[head, part, :] = (
                    gained * cos_ref[part, :] + turned * sin_ref[part, :]
                ).astype(BF)

    def attend(head, blocks):
        pair_head = head // 2
        for block in blocks:
            end = (block + 1) * rows
            part = pl.ds(block * rows, rows)
            scores = contract_cols(
                heads_ref[head, part, :], heads_ref[heads + pair_head, 0:end, :]
            )
            row_place = lax.broadcasted_iota(jnp.int32, (rows, end), 0) + block * rows
            col_place = lax.broadcasted_iota(jnp.int32, (rows, end), 1)
            allowed = (col_place >= start_ref[part, :]) & (col_place <= row_place)
            raised = jnp.where(allowed, jnp.exp(scores * (HEAD_DIM ** (-0.5))), 0.0)
            sums = jnp.sum(raised, axis=-1, keepdims=True)
            mixed = dot(raised.astype(BF), heads_ref[heads + kv_heads + pair_head, 0:end, :])
            mixed = mixed * (1.0 / sums)
            mixed_ref[part, head * HEAD_DIM : (head + 1) * HEAD_DIM] = mixed.astype(BF)
            lse_ref[part, head : head + 1] = jnp.log(sums)

    tiles = (heads + 2 * kv_heads) // 2
    for tile in range(tiles):
        if tile == tiles // 2:
            advance(FORWARD_PLAN[8])
        project(tile)
    hand_out((proj_ref, proj_out), (heads_ref, heads_out))
    advance(FORWARD_PLAN[9])

    for head in range(heads):
        attend(head, (0, 1, 2))
        advance(FORWARD_PLAN[10 + 2 * head])
        attend(head, (3,))
        advance(FORWARD_PLAN[11 + 2 * head])
    hand_out((mixed_ref, mixed_out), (lse_ref, lse_out))

    out.arrive()
    load_out = pltpu.make_async_copy(out_full, out_w, load_sem.at[2])
    load_out.start()
    load_out.wait()

    def out_piece(seq, column):
        part = pl.ds(pl.multiple_of(seq * rows, rows), rows)
        weight = out_w[:, :, column]
        return dot(mixed_ref[part, :], weight.reshape(-1, weight.shape[-1]))

    middle_ref[...] = hidden_ref[...].astype(F32)
    token_sum = PieceSum(
        here, out_piece, middle_ref, give, got, pair, far_got, (ss, sr), 512
    )
    token_sum.send()
    advance(FORWARD_PLAN[18])
    token_sum.pass_on()
    token_sum.add_near()
    advance(FORWARD_PLAN[19])
    token_sum.add_far()
    hand_out((middle_ref, middle_out))
    norm_rows(middle_ref, mlp_gain_ref, own_rows.at[1])
    n2.send()
    advance(FORWARD_PLAN[20])
    store.wait()
    store = turn(lhs, n1_turned)
    advance(FORWARD_PLAN[21])
    n2.forward()
    advance(FORWARD_PLAN[22])
    n2.arrive()
    load_lhs = pltpu.make_async_copy(n2_full, lhs, load_sem.at[3])
    load_lhs.start()
    down.arrive()
    first.arrive()
    load_lhs.wait()

    def feed(gather, begin, count, between=()):
        tiles = count // 256
        spot = begin // 256

        def body(gate_w, up_w, down_w, act_ref, gate_grad, up_grad):
            gate_tile = gate_w[...].reshape(width, 256)
            up_tile = up_w[...].reshape(width, 256)
            down_tile = down_w[...]
            for index, steps in enumerate(between):
                if steps:
                    pl.when(pl.program_id(0) == index + 1)(lambda steps=steps: advance(steps))

            @pl.loop(0, 2)
            def _(index):
                part = pl.ds(pl.multiple_of(index * 2 * rows, 2 * rows), 2 * rows)
                gate = dot(lhs[part, :], gate_tile)
                up = dot(lhs[part, :], up_tile)
                act_grad = contract_cols(dy_all[part, :], down_tile)
                sigmoid = jax.nn.sigmoid(gate)
                silu = gate * sigmoid
                act_ref[part, :] = (silu * up).astype(BF)
                gate_grad[part, :] = (
                    act_grad * up * sigmoid * (1.0 + gate * (1.0 - sigmoid))
                ).astype(BF)
                up_grad[part, :] = (act_grad * silu).astype(BF)

        block = gather.whole.shape[:-1] + (256,)
        grads = first_pair if begin < chunk else second_pair
        first_spot = 0 if begin < chunk + 1 else 2 * (begin - chunk) // 256
        pltpu.emit_pipeline(
            body,
            grid=(tiles,),
            in_specs=[
                pl.BlockSpec(block, lambda t: (0, 0, t)),
                pl.BlockSpec(block, lambda t: (0, 0, t + tiles)),
                pl.BlockSpec((256, width), lambda t: (t + spot, 0)),
            ],
            out_specs=[
                pl.BlockSpec((length, 256), lambda t: (0, t + spot)),
                pl.BlockSpec((length, 256), lambda t: (0, t + first_spot)),
                pl.BlockSpec((length, 256), lambda t: (0, t + first_spot + tiles)),
            ],
        )(gather.whole, gather.whole, down_full, act_out, grads, grads)

    feed(first, 0, chunk, (FORWARD_PLAN[23], FORWARD_PLAN[24]))
    advance(FORWARD_PLAN[25])
    store.wait()
    store = turn(lhs, n2_turned)
    advance(FORWARD_PLAN[26])
    second.arrive()
    feed(second, chunk, chunk - tail, (FORWARD_PLAN[27],))
    advance(FORWARD_PLAN[28])
    third.arrive()
    feed(third, 2 * chunk - tail, tail)
    store.wait()
    for copy in stores:
        copy.wait()
    for gather in (qkv, out, first, second, third, down, n1, n2, dy):
        gather.finish()


def forward(hidden, upstream, weights, gains, segment):
    size = lax.axis_size("shard")
    quarter, outer = size // 4, size // 2
    piece, width = hidden.shape
    length = piece * 4
    heads = Q_HEADS // 4
    kv_heads = KV_HEADS // 4
    w_query, _, _, w_out, w_gate, _, w_down = weights
    own = w_query.shape[0]
    qkv_width = (heads + 2 * kv_heads) * HEAD_DIM
    units = w_down.shape[0] // 4 * size

    def shape(*dims, kind=BF):
        return jax.ShapeDtypeStruct(dims, kind)

    results = [
        shape(size, own, qkv_width),
        shape(quarter, *w_out.shape),
        shape(size, own, units),
        shape(size, own, units),
        shape(units, width),
        shape(length, width),
        shape(length, width),
        shape(length, width),
        shape(width // 128, 128, length),
        shape(width // 128, 128, length),
        shape(width // 128, 128, length),
        shape(length, units),
        shape(length, units),
        shape(length, units),
        shape(heads + kv_heads, length, HEAD_DIM, kind=F32),
        shape(heads + 2 * kv_heads, length, HEAD_DIM),
        shape(length, heads * HEAD_DIM),
        shape(length, 128, kind=F32),
        shape(piece, width, kind=F32),
        shape(length, HEAD_DIM, kind=F32),
        shape(length, HEAD_DIM, kind=F32),
        shape(1, length, kind=jnp.int32),
    ]
    powers = np.arange(HEAD_DIM // 2, dtype=np.float32) * np.float32(2.0) / np.float32(HEAD_DIM)
    inverse = np.float32(ROPE_BASE) ** -powers
    dma = pltpu.SemaphoreType.DMA
    return pl.pallas_call(
        functools.partial(forward_kernel, size),
        out_shape=results,
        in_specs=[ANY] * 9 + [VMEM] * 6,
        out_specs=[ANY] * 22,
        scratch_shapes=[
            pltpu.VMEM((length, width), BF),
            pltpu.VMEM((length, width), BF),
            pltpu.VMEM((width // 128, 128, length), BF),
            pltpu.VMEM((size, own, qkv_width), BF),
            pltpu.VMEM((quarter,) + w_out.shape, BF),
            pltpu.VMEM((own, qkv_width), BF),
            pltpu.VMEM(w_out.shape, BF),
            pltpu.VMEM((w_down.shape[0] // 4, width), BF),
            pltpu.VMEM((piece, width), BF),
            pltpu.VMEM(w_gate.shape, BF),
            pltpu.VMEM((own, units), BF),
            pltpu.VMEM((own, units), BF),
            pltpu.VMEM((2, piece, width), BF),
            pltpu.VMEM((2, piece, width), BF),
            pltpu.VMEM((2, piece, width), BF),
            pltpu.VMEM((piece, width), BF),
            pltpu.VMEM((piece, width), BF),
            dma((7, outer)),
            dma((7, outer)),
            dma((7, outer)),
            dma((7, outer)),
            dma((7, outer)),
            dma((7, outer)),
            dma((7,)),
            dma((3, 3)),
            dma((3, 3)),
            dma((3,)),
            dma((9,)),
            dma((3,)),
            dma((3,)),
            pltpu.VMEM((length, 1), jnp.int32),
            pltpu.VMEM((length, 128), F32),
            pltpu.VMEM((256, 256), BF),
            pltpu.VMEM((piece, width), BF),
            pltpu.VMEM((heads + kv_heads, length, HEAD_DIM), F32),
            pltpu.VMEM((heads + 2 * kv_heads, length, HEAD_DIM), BF),
            pltpu.VMEM((length, heads * HEAD_DIM), BF),
            pltpu.VMEM((length, 128), F32),
            pltpu.VMEM((piece, width), F32),
            pltpu.VMEM((length, HEAD_DIM), F32),
            pltpu.VMEM((length, HEAD_DIM), F32),
            pltpu.VMEM((1, length), jnp.int32),
            dma((8,)),
        ],
        compiler_params=pltpu.CompilerParams(
            collective_id=0, has_side_effects=True, vmem_limit_bytes=VMEM_BYTES
        ),
        name="forward_gather",
    )(
        hidden,
        upstream,
        *weights,
        *gains,
        jnp.asarray(np.concatenate([inverse, inverse])[None], F32),
        segment[None],
    )


def add_rows(target, sources, step=16):
    groups, rows, _ = target.shape

    @pl.loop(0, rows // step)
    def _(index):
        part = pl.ds(pl.multiple_of(index * step, step), step)
        for group in range(groups):
            total = sources[0][group, part, :].astype(target.dtype)
            for source in sources[1:]:
                total = total + source[group, part, :].astype(target.dtype)
            target[group, part, :] = total


class RowSum:
    def __init__(self, here, give, keep, near, rising, falling, stage, total, sems):
        self.here, self.give, self.keep = here, give, keep
        self.near, self.rising, self.falling = near, rising, falling
        self.stage, self.total = stage, total
        self.ys, self.yr, self.us, self.ur, self.ds, self.dr, self.load = sems
        self.last = here.outer - 1

    def across(self, place):
        return remote(
            self.give.at[place],
            self.near.at[place],
            self.ys.at[place],
            self.yr.at[place],
            self.here.twin,
        )

    def up(self, place):
        peer = self.here.outer_peer(self.here.place + 1)
        return remote(
            self.keep.at[place], self.rising.at[place], self.us.at[place], self.ur.at[place], peer
        )

    def down(self, place):
        peer = self.here.outer_peer(self.here.place - 1)
        return remote(
            self.keep.at[place], self.falling.at[place], self.ds.at[place], self.dr.at[place], peer
        )

    def arrived(self, slot, send, receive):
        remote(slot, slot, send, receive, self.here.twin).wait_recv()

    def fold(self, distance):
        here = self.here
        above = here.place + distance
        below = here.place - distance

        def merge(place, line, receive, first):
            near = pltpu.make_async_copy(self.near.at[place], self.stage.at[0], self.load.at[0])
            self.arrived(self.near.at[place], self.ys.at[place], self.yr.at[place])
            near.start()

            @pl.when(first)
            def _():
                near.wait()
                add_rows(self.keep.at[place], [self.keep.at[place], self.stage.at[0]])

            @pl.when(jnp.logical_not(first))
            def _():
                self.arrived(line.at[place], self.us.at[0], receive.at[place])
                far = pltpu.make_async_copy(line.at[place], self.stage.at[1], self.load.at[1])
                far.start()
                near.wait()
                far.wait()
                add_rows(
                    self.keep.at[place], [self.keep.at[place], self.stage.at[0], self.stage.at[1]]
                )

        @pl.when(above <= self.last)
        def _():
            merge(above, self.rising, self.ur, here.place == 0)
            self.up(above).start()

        @pl.when(below >= 0)
        def _():
            merge(below, self.falling, self.dr, here.place == self.last)
            self.down(below).start()

    def finish(self):
        here = self.here
        place = here.place
        self.arrived(self.near.at[place], self.ys.at[place], self.yr.at[place])
        keep = self.keep.at[place]
        near = pltpu.make_async_copy(self.near.at[place], self.stage.at[0], self.load.at[0])
        low = pltpu.make_async_copy(self.rising.at[place], self.stage.at[1], self.load.at[1])
        high = pltpu.make_async_copy(self.falling.at[place], self.stage.at[1], self.load.at[1])
        near.start()

        @pl.when(place > 0)
        def _():
            self.arrived(self.rising.at[place], self.us.at[0], self.ur.at[place])
            low.start()
            low.wait()

        @pl.when(place == 0)
        def _():
            self.arrived(self.falling.at[place], self.ds.at[0], self.dr.at[place])
            high.start()
            high.wait()

        near.wait()

        @pl.when((place > 0) & (place < self.last))
        def _():
            add_rows(keep, [keep, self.stage.at[0], self.stage.at[1]])
            self.arrived(self.falling.at[place], self.ds.at[0], self.dr.at[place])
            high.start()
            high.wait()
            add_rows(self.total, [keep, self.stage.at[1]])

        @pl.when((place == 0) | (place == self.last))
        def _():
            add_rows(self.total, [keep, self.stage.at[0], self.stage.at[1]])

    def sent(self):
        for place in range(self.here.outer):
            self.across(place).wait_send()

    def settle(self):
        here = self.here
        for place in range(here.outer):

            @pl.when(place > here.place)
            def _():
                self.up(place).wait_send()

            @pl.when(place < here.place)
            def _():
                self.down(place).wait_send()


def compute_terms(here, give, keep, left, right, tiles, orders, senders):
    own = give.shape[2]
    per = 128 // (2 * own)
    step = 768 if give.shape[3] % 768 == 0 else 512
    for group, done in orders:
        spots = tiles(group)

        @pl.loop(0, give.shape[3] // step)
        def _(index):
            lane = pl.ds(pl.multiple_of(index * step, step), step)
            terms = dot(left(group), right(lane)).astype(BF)
            for spot, (zone, seq_group) in enumerate(spots):
                for sub in range(per):
                    at = spot * 128 + sub * 2 * own
                    even, odd = terms[at : at + own], terms[at + own : at + 2 * own]
                    place = zone * per + sub
                    keep[place, seq_group, :, lane] = jnp.where(here.half == 0, even, odd)
                    give[place, seq_group, :, lane] = jnp.where(here.half == 0, odd, even)

        for zone in done:
            for sub in range(per):
                for sender in senders:
                    sender.across(zone * per + sub).start()


class LineSum:
    def __init__(self, here, terms, rising, falling, stage, sems):
        self.here, self.terms, self.stage = here, terms, stage
        self.rising, self.falling = rising, falling
        self.us, self.ur, self.ds, self.dr, self.load = sems
        self.last = here.outer - 1

    def up(self, place):
        peer = self.here.outer_peer(self.here.place + 1)
        return remote(
            self.terms.at[place], self.rising.at[place], self.us.at[place], self.ur.at[place], peer
        )

    def down(self, place):
        peer = self.here.outer_peer(self.here.place - 1)
        return remote(
            self.terms.at[place], self.falling.at[place], self.ds.at[place], self.dr.at[place], peer
        )

    def merge(self, place, line, receive):
        slot = line.at[place]
        remote(slot, slot, self.us.at[0], receive.at[place], self.here.twin).wait_recv()
        copy = pltpu.make_async_copy(slot, self.stage.at[0], self.load.at[0])
        copy.start()
        copy.wait()
        add_rows(self.terms.at[place], [self.terms.at[place], self.stage.at[0]])

    def fold(self, distance):
        here = self.here
        above = here.place + distance
        below = here.place - distance

        @pl.when(above <= self.last)
        def _():
            @pl.when(here.place > 0)
            def _():
                self.merge(above, self.rising, self.ur)

            self.up(above).start()

        @pl.when(below >= 0)
        def _():
            @pl.when(here.place < self.last)
            def _():
                self.merge(below, self.falling, self.dr)

            self.down(below).start()

    def gather(self):
        place = self.here.place

        @pl.when(place > 0)
        def _():
            self.merge(place, self.rising, self.ur)

        @pl.when(place < self.last)
        def _():
            self.merge(place, self.falling, self.dr)

    def settle(self):
        here = self.here
        for place in range(here.outer):

            @pl.when(place > here.place)
            def _():
                self.up(place).wait_send()

            @pl.when(place < here.place)
            def _():
                self.down(place).wait_send()


class LineFirstSum(RowSum):
    def __init__(self, here, give, keep, near, lines, stage, total, sems, twin_sems):
        self.here, self.give, self.keep = here, give, keep
        self.near, self.stage, self.total = near, stage, total
        self.ys, self.yr, self.load = sems[0], sems[1], sems[6]
        self.lines = [
            LineSum(here, terms, rising, falling, stage, kinds[2:])
            for terms, (rising, falling), kinds in (
                (give, lines[0], twin_sems),
                (keep, lines[1], sems),
            )
        ]

    def fold(self, distance):
        for line in self.lines:
            line.fold(distance)

    def pass_on(self):
        self.lines[0].gather()
        self.across(self.here.place).start()
        self.lines[1].gather()

    def finish(self):
        place = self.here.place
        self.arrived(self.near.at[place], self.ys.at[place], self.yr.at[place])
        near = pltpu.make_async_copy(self.near.at[place], self.stage.at[0], self.load.at[0])
        near.start()
        near.wait()
        add_rows(self.total, [self.keep.at[place], self.stage.at[0]])

    def sent(self):
        self.across(self.here.place).wait_send()

    def settle(self):
        for line in self.lines:
            line.settle()


class RowSpread:
    def __init__(self, here, rows, whole, sems):
        self.here, self.rows, self.whole = here, rows, whole
        self.send_sems, self.recv_sems, self.local = sems

    def copy(self, amount):
        seq = lax.rem(self.here.seq + amount, 4)
        return remote(
            self.rows.at[seq],
            self.whole.at[self.here.seq],
            self.send_sems.at[amount - 1],
            self.recv_sems.at[amount - 1],
            {"seq": seq},
        )

    def keep(self):
        seq = self.here.seq
        return pltpu.make_async_copy(self.rows.at[seq], self.whole.at[seq], self.local)

    def send(self):
        for amount in (2, 3, 1):
            self.copy(amount).start()
        self.keep().start()

    def arrive(self):
        for amount in (1, 2, 3):
            self.copy(amount).wait_recv()
        self.keep().wait()

    def finish(self):
        for amount in (1, 2, 3):
            self.copy(amount).wait_send()


class TokenSum:
    def __init__(self, here, part, got, pair, far_got, base, sems):
        self.here, self.part, self.got, self.pair = here, part, got, pair
        self.far_got, self.base = far_got, base
        self.send_sems, self.recv_sems = sems
        self.rows = part.shape[0] // 4

    def piece(self, seq):
        return pl.ds(pl.multiple_of(seq * self.rows, self.rows), self.rows)

    def to_mate(self, index):
        here = self.here
        chip = here.chip if index else 1 - here.chip
        seq = chip * 2 + 1 - here.core
        return remote(
            self.part.at[self.piece(seq), :],
            self.got.at[index],
            self.send_sems.at[index],
            self.recv_sems.at[index],
            here.mate,
        )

    def to_far(self):
        return remote(
            self.pair, self.far_got, self.send_sems.at[2], self.recv_sems.at[2], self.here.far
        )

    def send(self):
        self.to_mate(0).start()
        self.to_mate(1).start()

    def loop(self, body):
        @pl.loop(0, self.rows // 32)
        def _(index):
            body(index * 32)

    def pass_on(self):
        self.to_mate(0).wait_recv()
        begin = self.here.far_seq * self.rows

        def body(at):
            part = pl.ds(pl.multiple_of(at, 32), 32)
            source = pl.ds(pl.multiple_of(begin + at, 32), 32)
            total = self.part[source, :].astype(F32) + self.got[0, part, :].astype(F32)
            self.pair[part, :] = total.astype(BF)

        self.loop(body)
        self.to_far().start()

    def add_near(self):
        self.to_mate(1).wait_recv()
        begin = self.here.seq * self.rows

        def body(at):
            part = pl.ds(pl.multiple_of(at, 32), 32)
            source = pl.ds(pl.multiple_of(begin + at, 32), 32)
            self.base[part, :] += self.part[source, :].astype(F32) + self.got[1, part, :].astype(F32)

        self.loop(body)
        self.to_mate(0).wait_send()
        self.to_mate(1).wait_send()

    def add_far(self):
        self.to_far().wait_recv()

        def body(at):
            part = pl.ds(pl.multiple_of(at, 32), 32)
            self.base[part, :] += self.far_got[part, :].astype(F32)

        self.loop(body)
        self.to_far().wait_send()


class GainSum:
    def __init__(self, here, own, seq_got, middle, shard_got, sems):
        self.here, self.own, self.middle = here, own, middle
        self.seq_got, self.shard_got = seq_got, shard_got
        self.seq_send, self.seq_recv, self.shard_send, self.shard_recv = sems

    def over_seq(self, amount):
        here = self.here
        return remote(
            self.own,
            self.seq_got.at[here.seq],
            self.seq_send.at[amount - 1],
            self.seq_recv.at[amount - 1],
            {"seq": lax.rem(here.seq + amount, 4)},
        )

    def over_shard(self, amount):
        here = self.here
        return remote(
            self.middle,
            self.shard_got.at[here.shard],
            self.shard_send.at[amount - 1],
            self.shard_recv.at[amount - 1],
            {"shard": lax.rem(here.shard + amount, here.size)},
        )

    def start(self):
        for amount in range(1, 4):
            self.over_seq(amount).start()
        self.seq_got[self.here.seq] = self.own[...]

    def turn(self):
        for amount in range(1, 4):
            self.over_seq(amount).wait()
        total = self.seq_got[0]
        for index in range(1, 4):
            total = total + self.seq_got[index]
        self.middle[...] = total
        for amount in range(1, self.here.size):
            self.over_shard(amount).start()
        self.shard_got[self.here.shard] = total

    def finish(self):
        for amount in range(1, self.here.size):
            self.over_shard(amount).wait()
        total = self.shard_got[0]
        for index in range(1, self.here.size):
            total = total + self.shard_got[index]
        return total


PLAN = (
    (("down_a", 3),),
    (("down_a", 2), ("down_b", 3),),
    (("down_a", 1), ("down_b", 2),),
    (),
    (),
    (("first", 3), ("down_b", 1),),
    (("first", 2), ("down_b", "finish"),),
    (("second", 3), ("first", 1),),
    (("second", 2),),
    (),
    (("first", "finish"),),
    (("out", 3), ("second", 1),),
    (),
    (("out", 2), ("query", 3), ("down_a", "pass"), ("key", 3), ("out", 1),),
    (("query", 2), ("key", 2), ("second", "finish"), ("out", "finish"), ("query", 1), ("key", 1),),
    (("query", "finish"), ("key", "finish"),),
    (("down_a", "finish"),),
)


def backward_kernel(
    size,
    n1_hbm,
    dy_hbm,
    n2_hbm,
    act_hbm,
    first_hbm,
    second_hbm,
    proj_hbm,
    heads_hbm,
    mixed_hbm,
    lse_hbm,
    middle_hbm,
    hidden_hbm,
    dy_own,
    qkv_full,
    out_full,
    first_full,
    second_full,
    down_full,
    attn_gain_ref,
    mlp_gain_ref,
    query_gain_ref,
    key_gain_ref,
    cos_hbm,
    sin_hbm,
    start_hbm,
    grad_in_out,
    gains_out,
    grad_out_out,
    hidden_out,
    down_rows,
    first_rows,
    second_rows,
    qkv_rows,
    da_hbm,
    near_mlp,
    rising_mlp,
    falling_mlp,
    rising_twin,
    falling_twin,
    near_qkv,
    rising_qkv,
    falling_qkv,
    near_out,
    rising_out,
    falling_out,
    lhs,
    turned,
    first_r,
    second_r,
    give,
    keep,
    give_out,
    keep_out,
    stage,
    stage_out,
    dout_ref,
    da_own,
    got,
    far_got,
    pair,
    middle_grad,
    proj_buf,
    eye,
    keys_turned,
    lse_t,
    delta,
    delta_t,
    dk_sum,
    dv_sum,
    gain_row,
    gain_seq,
    gain_middle,
    gain_shard,
    ys,
    yr,
    us,
    ur,
    ds,
    dr,
    fold_load,
    spread_s,
    spread_r,
    spread_l,
    sum_s,
    sum_r,
    ts,
    tr,
    token_local,
    gss,
    gsr,
    gts,
    gtr,
    load_sem,
    credit,
    grad_in,
    grad_out,
    heads_ref,
    mixed_ref,
    lse_ref,
    cos_ref,
    sin_ref,
    start_ref,
    store_sems,
):
    here = Place(size)
    length, width = lhs.shape
    rows = length // 4
    units = first_r.shape[1]
    chunk = units // 2
    ff_part = units // size
    heads = mixed_ref.shape[1] // HEAD_DIM
    kv_heads = heads // 2
    qkv_width = qkv_full.shape[2]
    last = here.outer - 1
    scale = HEAD_DIM ** (-0.5)

    def load(source, target, index):
        copy = pltpu.make_async_copy(source, target, load_sem.at[index])
        copy.start()
        return copy

    def sems(index):
        return tuple(kind.at[index] for kind in (ys, yr, us, ur, ds, dr, fold_load))

    thin = qkv_width // 2
    cut = units * 2 // 3
    lanes = {
        "down_a": slice(0, cut),
        "down_b": slice(cut, units),
        "query": slice(0, thin),
        "key": slice(thin, 2 * thin),
    }

    def part(ref, name):
        return ref.at[:, :, :, lanes[name]]

    def row_sum(index, give_ref, keep_ref, near, rising, falling, stage_ref, total):
        return RowSum(
            here, give_ref, keep_ref, near, rising, falling, stage_ref, total, sems(index)
        )

    jobs = {
        "down_a": LineFirstSum(
            here,
            part(give.at[2], "down_a"),
            part(keep.at[0], "down_a"),
            part(near_mlp.at[0], "down_a"),
            (
                (rising_twin, falling_twin),
                (part(rising_mlp.at[0], "down_a"), part(falling_mlp.at[0], "down_a")),
            ),
            part(stage, "down_a"),
            keep.at[0, here.place, :, :, lanes["down_a"]],
            sems(0),
            sems(5),
        ),
        "down_b": row_sum(
            6,
            part(give.at[2], "down_b"),
            part(keep.at[0], "down_b"),
            part(near_mlp.at[0], "down_b"),
            part(rising_mlp.at[0], "down_b"),
            part(falling_mlp.at[0], "down_b"),
            part(stage, "down_b"),
            keep.at[0, here.place, :, :, lanes["down_b"]],
        ),
        "out": row_sum(
            4, give_out, keep_out, near_out, rising_out, falling_out, stage_out, grad_out
        ),
    }
    for index, name in ((1, "first"), (2, "second")):
        jobs[name] = row_sum(
            index,
            give.at[2 - index],
            keep.at[index],
            near_mlp.at[index],
            rising_mlp.at[index],
            falling_mlp.at[index],
            stage,
            keep.at[index, here.place],
        )
    for index, name in ((3, "query"), (7, "key")):
        jobs[name] = row_sum(
            index,
            part(give.at[1], name),
            part(second_r, name),
            part(near_qkv, name),
            part(rising_qkv, name),
            part(falling_qkv, name),
            part(stage, name),
            second_r.at[here.place, :, :, lanes[name]],
        )
    zones = width // 512

    def zone_at(index):
        zone = here.place // (here.outer // zones)
        return (
            3 * (1 - zone // 2),
            lax.rem(2 + 3 * zone, 5),
            1 + lax.rem(zone, 2),
            zone,
        )[index]

    zone_order = [zone_at(index) for index in range(zones)]
    by_zone = [(zone, (zone,)) for zone in zone_order]

    spreads = {}
    for index, (name, whole) in enumerate(
        (
            ("down_a", down_rows.at[:, :, lanes["down_a"]]),
            ("down_b", down_rows.at[:, :, lanes["down_b"]]),
            ("first", first_rows),
            ("second", second_rows),
            ("query", qkv_rows.at[:, :, lanes["query"]]),
            ("key", qkv_rows.at[:, :, lanes["key"]]),
        )
    ):
        kinds = (spread_s.at[index], spread_r.at[index], spread_l.at[index])
        spreads[name] = RowSpread(here, jobs[name].total, whole, kinds)

    def token_sum(index, base):
        return TokenSum(
            here, lhs, got, pair, far_got, base, (sum_s.at[index], sum_r.at[index])
        )

    sum_mlp = token_sum(0, middle_grad)
    sum_hidden = token_sum(1, grad_in)
    sum_attn = token_sum(2, grad_in)
    da = TokenGather(here, da_own, da_hbm, (ts, tr, token_local.at[0]))

    def model_tiles(group):
        return [(group, seq_group) for seq_group in range(4)]

    def first_columns(lane):
        return first_r[:, lane]

    def model_left(group):
        return turned[pl.ds(group * 4, 4)].reshape(512, length)

    def advance(steps):
        for name, step in steps:
            job = jobs[name]
            if step == "pass":
                job.pass_on()
            elif step == "finish":
                job.finish()
                if name in spreads:
                    spreads[name].send()
            else:
                for distance in range(last * step // 3, last * (step - 1) // 3, -1):
                    job.fold(distance)

    load_turned = load(dy_hbm, turned, 0)
    load_act = load(act_hbm, lhs.at[:, 0:units], 1)
    eye[...] = identity(HEAD_DIM)
    here.greet(wide=True)
    load_turned.wait()
    load_act.wait()
    load_first = load(first_hbm, first_r, 1)
    load_second = load(second_hbm, second_r, 3)
    load_middle = load(middle_hbm, grad_in, 2)
    load_dy = load(dy_own, da_own, 4)
    late_loads = [
        load(source, target, 5 + index)
        for index, (source, target) in enumerate(
            (
                (mixed_hbm, mixed_ref),
                (lse_hbm, lse_ref),
                (heads_hbm, heads_ref),
                (cos_hbm, cos_ref),
                (sin_hbm, sin_ref),
                (start_hbm, start_ref),
            )
        )
    ]
    def model_terms(give_ref, keep_ref, right, senders):
        compute_terms(
            here, give_ref, keep_ref, model_left, right, model_tiles, by_zone, senders
        )

    model_terms(give.at[2], keep.at[0], lambda lane: lhs[:, lane], [jobs["down_b"]])
    advance(PLAN[0])
    load_turned = load(n2_hbm, turned, 0)
    load_first.wait()
    load_second.wait()

    own = width // size
    slabs = 256 // own

    def dn2_body(first_w, second_w):
        lane = pl.ds(pl.multiple_of(pl.program_id(0) * 256, 256), 256)
        first_tile = first_w[...].reshape(256, units)
        second_tile = second_w[...].reshape(256, units)

        @pl.loop(0, 2)
        def _(index):
            part = pl.ds(pl.multiple_of(index * 2 * rows, 2 * rows), 2 * rows)
            total = contract_cols(first_r[part, :], first_tile)
            blocks = pl.ds(index * (here.outer // 2), here.outer // 2)
            second_rows = second_r[blocks].reshape(2 * rows, units)
            total = total + contract_cols(second_rows, second_tile)
            lhs[part, lane] = total.astype(BF)

    slab = pl.BlockSpec((slabs, own, units), lambda t: (t, 0, 0))
    pltpu.emit_pipeline(dn2_body, grid=(width // 256,), in_specs=[slab, slab])(
        first_full, second_full
    )
    sum_mlp.send()
    middle_grad[...] = jnp.zeros_like(middle_grad)
    load_turned.wait()
    advance(PLAN[1])
    sum_mlp.pass_on()
    sum_mlp.add_near()
    model_terms(give.at[1], keep.at[1], first_columns, [jobs["first"]])
    load_act = load(act_hbm, first_r, 1)
    advance(PLAN[2])
    sum_mlp.add_far()

    load_middle.wait()
    load_dy.wait()
    gain_row[...] = jnp.zeros_like(gain_row)
    mlp_lane = slice(2 * HEAD_DIM, 2 * HEAD_DIM + width)
    attn_lane = slice(2 * HEAD_DIM + width, 2 * HEAD_DIM + 2 * width)
    narrow = 16

    @pl.loop(0, rows // narrow)
    def _(index):
        part = pl.ds(pl.multiple_of(index * narrow, narrow), narrow)
        values = grad_in[part, :]
        scales = lax.rsqrt(jnp.mean(values * values, axis=-1, keepdims=True) + EPSILON)
        normed = values * scales
        update = middle_grad[part, :]
        gain_row[:, mlp_lane] += jnp.sum(update * normed, axis=0, keepdims=True)
        upper = update * mlp_gain_ref[...]
        inner = jnp.mean(upper * normed, axis=-1, keepdims=True)
        grad = da_own[part, :].astype(F32) + scales * (upper - normed * inner)
        middle_grad[part, :] = grad
        da_own[part, :] = grad.astype(BF)

    da.send()
    advance(PLAN[3])
    model_terms(
        give.at[0],
        keep.at[2],
        lambda lane: second_r[:, :, :, lane].reshape(length, -1),
        [jobs["second"]],
    )
    advance(PLAN[4])

    def hidden_body(weight):
        lane = pl.ds(pl.multiple_of(pl.program_id(0) * 256, 256), 256)
        tile = weight[...]

        @pl.loop(0, 2)
        def _(index):
            part = pl.ds(pl.multiple_of(index * 2 * rows, 2 * rows), 2 * rows)
            lhs[part, lane] = dot(first_r[part, :], tile).astype(BF)

    load_act.wait()
    pltpu.emit_pipeline(
        hidden_body,
        grid=(width // 256,),
        in_specs=[pl.BlockSpec((units, 256), lambda t: (0, t))],
    )(down_full)
    da.mate_arrived()
    sum_hidden.send()
    da.forward()
    advance(PLAN[5])
    sum_hidden.pass_on()
    sum_hidden.add_near()
    advance(PLAN[6])
    da.rest_arrived()
    da.finish()
    load_lhs = load(da_hbm, lhs, 0)
    load_own = load(hidden_hbm, da_own, 2)
    load_lhs.wait()

    def dout_body(weight):
        lane = pl.ds(pl.multiple_of(pl.program_id(0) * 256, 256), 256)
        tile = weight[...].reshape(256, width)

        @pl.loop(0, 2)
        def _(index):
            part = pl.ds(pl.multiple_of(index * 2 * rows, 2 * rows), 2 * rows)
            dout_ref[part, lane] = contract_cols(lhs[part, :], tile).astype(BF)

    out_blocks, out_rows = out_full.shape[:2]
    pltpu.emit_pipeline(
        dout_body,
        grid=(out_blocks * out_rows // 256,),
        in_specs=[pl.BlockSpec((256 // out_rows, out_rows, width), lambda t: (t, 0, 0))],
    )(out_full)

    for late in late_loads:
        late.wait()
    for head in range(heads):
        lane = slice(head * HEAD_DIM, (head + 1) * HEAD_DIM)
        turned[head] = contract_cols(eye[...], mixed_ref[:, lane]).astype(BF)
    compute_terms(
        here,
        give_out,
        keep_out,
        lambda group: turned[0:heads].reshape(heads * HEAD_DIM, length),
        lambda lane: lhs[:, lane],
        lambda group: [(zone, 0) for zone in range(heads)],
        [(0, zone_order)],
        [jobs["out"]],
    )
    load_turned = load(n1_hbm, turned, 0)
    sum_hidden.add_far()
    for index, peer in enumerate((here.mate, here.far)):
        pl.semaphore_signal(credit.at[index], inc=1, device_id=peer, device_id_type=MESH)

    @pl.loop(0, rows // 32)
    def _(index):
        part = pl.ds(pl.multiple_of(index * 32, 32), 32)
        pair[part, :] = grad_in[part, :].astype(BF)

    store_hidden = load(pair, hidden_out, 1)
    advance(PLAN[7])

    lse_t[...] = lse_ref[...].T[0:8]
    delta[...] = jnp.zeros_like(delta)
    for head in range(heads):
        lane = slice(head * HEAD_DIM, (head + 1) * HEAD_DIM)
        terms = dout_ref[:, lane].astype(F32) * mixed_ref[:, lane].astype(F32)
        delta[:, head : head + 1] = jnp.sum(terms, axis=-1, keepdims=True)
    delta_t[...] = delta[...].T[0:8]
    def through_norm(grad, head, part, gain_ref, which):
        proj = proj_buf[part, :]
        scales = lax.rsqrt(jnp.mean(proj * proj, axis=-1, keepdims=True) + EPSILON)
        normed = proj * scales
        grad = grad.astype(F32)
        upper = grad * cos_ref[part, :] - pltpu.roll(grad, HEAD_DIM // 2, 1) * sin_ref[part, :]
        gain_row[:, which * HEAD_DIM : (which + 1) * HEAD_DIM] += jnp.sum(
            upper * normed, axis=0, keepdims=True
        )
        upper = upper * gain_ref[...]
        inner = jnp.mean(upper * normed, axis=-1, keepdims=True)
        result = (scales * (upper - normed * inner)).astype(BF)
        first_r[part, head * HEAD_DIM : (head + 1) * HEAD_DIM] = result

    for head in range(heads):
        pair_head = head // 2
        load_proj = load(proj_hbm.at[head], proj_buf, 4)
        if head % 2 == 0:
            dk_sum[...] = jnp.zeros_like(dk_sum)
            dv_sum[...] = jnp.zeros_like(dv_sum)
            keys_turned[...] = contract_cols(eye[...], heads_ref[heads + pair_head]).astype(BF)
        for block in range(4):
            end = (block + 1) * rows
            part = pl.ds(block * rows, rows)
            queries = heads_ref[head, part, :]
            keys = heads_ref[heads + pair_head, 0:end, :]
            values = heads_ref[heads + kv_heads + pair_head, 0:end, :]
            out_grad = dout_ref[part, head * HEAD_DIM : (head + 1) * HEAD_DIM]
            scores = contract_cols(keys, queries)
            key_place = lax.broadcasted_iota(jnp.int32, (end, rows), 0)
            query_place = lax.broadcasted_iota(jnp.int32, (end, rows), 1) + block * rows
            allowed = (key_place >= start_ref[:, part]) & (key_place <= query_place)
            weights = jnp.exp(scores * scale - lse_t[head : head + 1, part])
            weights = jnp.where(allowed, weights, 0.0)
            weight_grad = contract_cols(values, out_grad)
            inner = delta_t[head : head + 1, part]
            score_grad = (weights * (weight_grad - inner)).astype(BF)
            dk_sum[0:end, :] += dot(score_grad, queries) * scale
            dv_sum[0:end, :] += dot(weights.astype(BF), out_grad)
            query_grad = dot(keys_turned[:, 0:end], score_grad).T
            query_grad = (query_grad * scale).astype(BF)
            if block == 0:
                load_proj.wait()
            through_norm(query_grad, head, part, query_gain_ref, 0)
        if head % 2:
            key = heads + pair_head
            value_at = (heads + kv_heads + pair_head) * HEAD_DIM
            load(proj_hbm.at[key], proj_buf, 4).wait()

            @pl.loop(0, 4)
            def _(index):
                part = pl.ds(pl.multiple_of(index * rows, rows), rows)
                through_norm(dk_sum[part, :].astype(BF), key, part, key_gain_ref, 1)
                first_r[part, value_at : value_at + HEAD_DIM] = dv_sum[part, :].astype(BF)

        advance(PLAN[8 + head])

    load_turned.wait()
    jobs["first"].sent()
    store_hidden.wait()
    proj_grads = first_r.at[:, 0:qkv_width]
    model_terms(
        give.at[1, :, :, :, 0:qkv_width],
        second_r.at[:, :, :, 0:qkv_width],
        first_columns,
        [jobs["query"], jobs["key"]],
    )
    advance(PLAN[12])

    def dn1_body(weight):
        lane = pl.ds(pl.multiple_of(pl.program_id(0) * 256, 256), 256)
        tile = weight[...].reshape(256, qkv_width)

        @pl.loop(0, 2)
        def _(index):
            part = pl.ds(pl.multiple_of(index * 2 * rows, 2 * rows), 2 * rows)
            lhs[part, lane] = contract_cols(proj_grads[part, :], tile).astype(BF)

    pltpu.emit_pipeline(
        dn1_body,
        grid=(width // 256,),
        in_specs=[pl.BlockSpec((slabs, own, qkv_width), lambda t: (t, 0, 0))],
    )(qkv_full)
    grad_in[...] = jnp.zeros_like(grad_in)
    pl.semaphore_wait(credit.at[0], 1)
    pl.semaphore_wait(credit.at[1], 1)
    sum_attn.send()
    advance(PLAN[13])
    sum_attn.pass_on()
    sum_attn.add_near()
    advance(PLAN[14])
    sum_attn.add_far()
    load_own.wait()

    @pl.loop(0, rows // narrow)
    def _(index):
        part = pl.ds(pl.multiple_of(index * narrow, narrow), narrow)
        values = da_own[part, :].astype(F32)
        scales = lax.rsqrt(jnp.mean(values * values, axis=-1, keepdims=True) + EPSILON)
        normed = values * scales
        update = grad_in[part, :]
        gain_row[:, attn_lane] += jnp.sum(update * normed, axis=0, keepdims=True)
        upper = update * attn_gain_ref[...]
        inner = jnp.mean(upper * normed, axis=-1, keepdims=True)
        grad_in[part, :] = middle_grad[part, :] + scales * (upper - normed * inner)

    store_in = pltpu.make_async_copy(grad_in, grad_in_out, store_sems.at[0])
    store_in.start()
    gain_sum = GainSum(here, gain_row, gain_seq, gain_middle, gain_shard, (gss, gsr, gts, gtr))
    gain_sum.start()
    advance(PLAN[15])
    gain_sum.turn()
    advance(PLAN[16])
    gains_out[...] = gain_sum.finish()
    store_out = pltpu.make_async_copy(grad_out, grad_out_out, store_sems.at[1])
    store_out.start()
    for spread_rows in spreads.values():
        spread_rows.arrive()
    store_in.wait()
    store_out.wait()
    for name, job in jobs.items():
        if name != "first":
            job.sent()
    for job in jobs.values():
        job.settle()
    for job in spreads.values():
        job.finish()


def backward(saved, weights, own, gains, tables, starts):
    size = lax.axis_size("shard")
    outer = size // 2
    (n1, dy, n2, act, first, second, proj, heads_all, mixed, lse, middle) = saved
    length, width = heads_all.shape[1], middle.shape[1]
    piece = length // 4
    units = act.shape[1]
    qkv_width = weights[0].shape[2]
    rows = width // (4 * size)
    q_width = mixed.shape[1]

    def shape(*dims, kind=BF):
        return jax.ShapeDtypeStruct(dims, kind)

    results = [
        shape(piece, width, kind=F32),
        shape(1, 2 * width + 2 * HEAD_DIM, kind=F32),
        shape(1, rows, width, kind=F32),
        shape(piece, width),
        shape(4, rows, units),
        shape(4, rows, units),
        shape(4, rows, units),
        shape(4, rows, qkv_width),
        shape(length, width),
    ]
    results += [shape(3, outer, 4, rows, units)] * 3
    results += [shape(outer, 4, rows, units * 2 // 3)] * 2
    results += [shape(outer, 4, rows, qkv_width)] * 3
    results += [shape(outer, 1, rows, width)] * 3
    dma = pltpu.SemaphoreType.DMA
    vmem = pltpu.VMEM
    return pl.pallas_call(
        functools.partial(backward_kernel, size),
        out_shape=results,
        in_specs=[ANY] * 18 + [VMEM] * 4 + [ANY] * 3,
        out_specs=[ANY, VMEM] + [ANY] * (len(results) - 2),
        scratch_shapes=[
            vmem((length, width), BF),
            vmem((width // 128, 128, length), BF),
            vmem((length, units), BF),
            vmem((outer, 4, rows, units), BF),
            vmem((3, outer, 4, rows, units), BF),
            vmem((3, outer, 4, rows, units), BF),
            vmem((outer, 1, rows, width), BF),
            vmem((outer, 1, rows, width), BF),
            vmem((2, 4, rows, units), BF),
            vmem((2, 1, rows, width), BF),
            vmem((length, q_width), BF),
            vmem((piece, width), BF),
            vmem((2, piece, width), BF),
            vmem((piece, width), BF),
            vmem((piece, width), BF),
            vmem((piece, width), F32),
            vmem((length, HEAD_DIM), F32),
            vmem((HEAD_DIM, HEAD_DIM), BF),
            vmem((HEAD_DIM, length), BF),
            vmem((8, length), F32),
            vmem((length, 128), F32),
            vmem((8, length), F32),
            vmem((length, HEAD_DIM), F32),
            vmem((length, HEAD_DIM), F32),
            vmem((1, 2 * width + 2 * HEAD_DIM), F32),
            vmem((4, 1, 2 * width + 2 * HEAD_DIM), F32),
            vmem((1, 2 * width + 2 * HEAD_DIM), F32),
            vmem((size, 1, 2 * width + 2 * HEAD_DIM), F32),
            dma((8, outer)),
            dma((8, outer)),
            dma((8, outer)),
            dma((8, outer)),
            dma((8, outer)),
            dma((8, outer)),
            dma((8, 3)),
            dma((6, 3)),
            dma((6, 3)),
            dma((6,)),
            dma((3, 3)),
            dma((3, 3)),
            dma((3,)),
            dma((3,)),
            dma((1,)),
            dma((3,)),
            dma((3,)),
            dma((size - 1,)),
            dma((size - 1,)),
            dma((11,)),
            pltpu.SemaphoreType.REGULAR((2,)),
            vmem((piece, width), F32),
            vmem((1, rows, width), F32),
            vmem(heads_all.shape, BF),
            vmem(mixed.shape, BF),
            vmem(lse.shape, F32),
            vmem((length, HEAD_DIM), F32),
            vmem((length, HEAD_DIM), F32),
            vmem((1, length), jnp.int32),
            dma((2,)),
        ],
        compiler_params=pltpu.CompilerParams(
            collective_id=1, has_side_effects=True, vmem_limit_bytes=VMEM_BYTES
        ),
        name="backward_sums",
    )(
        n1,
        dy,
        n2,
        act,
        first,
        second.reshape(outer, 4, rows, units),
        proj,
        heads_all,
        mixed,
        lse,
        middle,
        *own,
        *weights,
        *gains,
        *tables,
        starts,
    )


def finish_kernel(
    size,
    grad_in,
    gains,
    grad_out,
    hidden_out,
    down_rows,
    first_rows,
    second_rows,
    qkv_rows,
    grad_in_out,
    grad_out_out,
    hidden_out_out,
    grad_query,
    grad_key,
    grad_value,
    grad_gate,
    grad_up,
    grad_down,
    attn_gain,
    mlp_gain,
    query_gain,
    key_gain,
    grad_in_buf,
    grad_out_buf,
    hidden_buf,
    down_buf,
    first_buf,
    second_buf,
    qkv_buf,
    query_buf,
    key_buf,
    value_buf,
    gate_buf,
    up_buf,
    wide_buf,
    load_sems,
    store_sems,
):
    units = down_buf.shape[2]
    chunk = units // 2
    ff_part = units // size
    most, tail = chunk - 256, 256
    stores = []

    def load(source, target, index):
        copy = pltpu.make_async_copy(source, target, load_sems.at[index])
        copy.start()
        return copy

    def store(source, target):
        copy = pltpu.make_async_copy(source, target, store_sems.at[len(stores)])
        copy.start()
        stores.append(copy)

    loads = [
        load(source, target, index)
        for index, (source, target) in enumerate(
            (
                (down_rows, down_buf),
                (first_rows, first_buf),
                (second_rows, second_buf),
                (qkv_rows, qkv_buf),
                (grad_in, grad_in_buf),
                (hidden_out, hidden_buf),
                (grad_out, grad_out_buf),
            )
        )
    ]

    def place(read, target):
        @pl.loop(0, target.shape[0] // 16)
        def _(index):
            part = pl.ds(pl.multiple_of(index * 16, 16), 16)
            values = [read(seq, part).astype(F32) for seq in range(4)]
            for begin in range(0, size, size // 8):
                pieces = [
                    values[seq][:, block * ff_part : (block + 1) * ff_part]
                    for block in range(begin, begin + size // 8)
                    for seq in range(4)
                ]
                lane = slice(begin * 4 * ff_part, (begin + size // 8) * 4 * ff_part)
                target[part, lane] = jnp.concatenate(pieces, axis=1)

    def side(index):
        at = 2 * most + index * tail

        def read(seq, part):
            return jnp.concatenate(
                [
                    first_buf[seq, part, index * chunk : (index + 1) * chunk],
                    second_buf[seq, part, index * most : (index + 1) * most],
                    second_buf[seq, part, at : at + tail],
                ],
                axis=1,
            )

        return read

    loads[4].wait()
    store(grad_in_buf, grad_in_out)
    loads[5].wait()
    store(hidden_buf, hidden_out_out)
    loads[6].wait()
    store(grad_out_buf, grad_out_out)
    loads[0].wait()
    place(lambda seq, part: down_buf[seq, part, :], wide_buf)
    store(wide_buf, grad_down)
    loads[1].wait()
    loads[2].wait()
    place(side(0), gate_buf)
    store(gate_buf, grad_gate)
    place(side(1), up_buf)
    store(up_buf, grad_up)
    loads[3].wait()
    at = 0
    for buf, target in ((query_buf, grad_query), (key_buf, grad_key), (value_buf, grad_value)):
        count = buf.shape[1] // 4
        for seq in range(4):
            buf[:, seq * count : (seq + 1) * count] = qkv_buf[seq, :, at : at + count].astype(F32)
        at += count
        store(buf, target)
    at = 0
    for target in (query_gain, key_gain, mlp_gain, attn_gain):
        target[...] = gains[:, at : at + target.shape[1]]
        at += target.shape[1]
    for copy in stores:
        copy.wait()


def finish(grad_in, gains, grad_out, hidden_out, down_rows, first_rows, second_rows, qkv_rows):
    size = lax.axis_size("shard")
    piece, width = grad_in.shape
    rows, units = down_rows.shape[1:]
    qkv_width = qkv_rows.shape[2]

    def shape(*dims, kind=F32):
        return jax.ShapeDtypeStruct(dims, kind)

    results = [
        shape(piece, width),
        shape(1, rows, width),
        shape(piece, width, kind=BF),
        shape(rows, 2 * qkv_width),
        shape(rows, qkv_width),
        shape(rows, qkv_width),
        shape(rows, 4 * units),
        shape(rows, 4 * units),
        shape(rows, 4 * units),
        shape(1, width),
        shape(1, width),
        shape(1, HEAD_DIM),
        shape(1, HEAD_DIM),
    ]
    return pl.pallas_call(
        functools.partial(finish_kernel, size),
        out_shape=results,
        in_specs=[ANY, VMEM] + [ANY] * 6,
        out_specs=[ANY] * 9 + [VMEM] * 4,
        scratch_shapes=[
            pltpu.VMEM((piece, width), F32),
            pltpu.VMEM((1, rows, width), F32),
            pltpu.VMEM((piece, width), BF),
            pltpu.VMEM((4, rows, units), BF),
            pltpu.VMEM((4, rows, units), BF),
            pltpu.VMEM((4, rows, units), BF),
            pltpu.VMEM((4, rows, qkv_width), BF),
            pltpu.VMEM((rows, 2 * qkv_width), F32),
            pltpu.VMEM((rows, qkv_width), F32),
            pltpu.VMEM((rows, qkv_width), F32),
            pltpu.VMEM((rows, 4 * units), F32),
            pltpu.VMEM((rows, 4 * units), F32),
            pltpu.VMEM((rows, 4 * units), F32),
            pltpu.SemaphoreType.DMA((7,)),
            pltpu.SemaphoreType.DMA((9,)),
        ],
        compiler_params=pltpu.CompilerParams(vmem_limit_bytes=VMEM_BYTES),
        name="finish",
    )(grad_in, gains, grad_out, hidden_out, down_rows, first_rows, second_rows, qkv_rows)


def local(
    hidden_in,
    segment_ids,
    norm_attn_gain,
    w_query,
    w_key,
    w_value,
    query_gain,
    key_gain,
    w_out,
    norm_mlp_gain,
    w_gate,
    w_up,
    w_down,
    out_cotangent,
):
    segment = segment_ids[0]
    gains = (norm_attn_gain[None], norm_mlp_gain[None], query_gain[None], key_gain[None])
    results = forward(
        hidden_in[0],
        out_cotangent[0],
        (w_query, w_key, w_value, w_out, w_gate, w_up, w_down),
        gains,
        segment,
    )
    (
        grad_in,
        grad_out,
        hidden_out,
        grad_query,
        grad_key,
        grad_value,
        grad_gate,
        grad_up,
        grad_down,
        attn_gain,
        mlp_gain,
        query_grad,
        key_grad,
    ) = finish(
        *backward(
            results[8:19],
            results[:5],
            (hidden_in[0], out_cotangent[0]),
            gains,
            results[19:21],
            results[21],
        )[:8]
    )
    return (
        hidden_out[None],
        grad_in[None],
        attn_gain[0],
        grad_query,
        grad_key,
        grad_value,
        query_grad[0],
        key_grad[0],
        grad_out[0],
        mlp_gain[0],
        grad_gate,
        grad_up,
        grad_down.T,
    )


def solution(mesh):
    return jax.shard_map(
        local,
        mesh=mesh,
        in_specs=(
            P("shard", "seq", None),
            P("shard", None),
            P(),
            P("shard", None),
            P("shard", None),
            P("shard", None),
            P(),
            P(),
            P("shard", None),
            P(),
            P("shard", None),
            P("shard", None),
            P("shard", None),
            P("shard", "seq", None),
        ),
        out_specs=(
            P("shard", "seq", None),
            P("shard", "seq", None),
            P(),
            P(("seq", "shard"), None),
            P(("seq", "shard"), None),
            P(("seq", "shard"), None),
            P(),
            P(),
            P(("seq", "shard"), None),
            P(),
            P(("seq", "shard"), None),
            P(("seq", "shard"), None),
            P(None, ("seq", "shard")),
        ),
        check_vma=False,
    )
```

```python
import functools

import jax
import jax.numpy as jnp
import numpy as np
from jax import lax
from jax.experimental import pallas as pl
from jax.experimental.pallas import tpu as pltpu
from jax.sharding import PartitionSpec as P

Q_HEADS = 16
KV_HEADS = 8
HEAD_DIM = 128
EPSILON = 1e-06
ROPE_BASE = 1000000.0
NEGATIVE = -1e30
BF = jnp.bfloat16
F32 = jnp.float32
MESH = pl.DeviceIdType.MESH
ANY = pl.BlockSpec(memory_space=pl.ANY)
VMEM = pl.BlockSpec(memory_space=pltpu.VMEM)
VMEM_BYTES = 62 * 1024 * 1024


def dot(left, right):
    return jnp.dot(left, right, preferred_element_type=F32)


def contract_cols(left, right):
    return lax.dot_general(left, right, (((1,), (1,)), ((), ())), preferred_element_type=F32)


class Place:
    def __init__(self, size):
        self.size = size
        self.outer = size // 2
        self.quarter = size // 4
        self.seq = lax.axis_index("seq")
        self.shard = lax.axis_index("shard")
        self.chip = self.seq // 2
        self.core = lax.rem(self.seq, 2)
        self.place = self.shard // 2
        self.half = lax.rem(self.shard, 2)
        self.far_seq = lax.rem(self.seq + 2, 4)
        self.mate_seq = self.chip * 2 + 1 - self.core
        self.far = {"seq": self.far_seq}
        self.mate = {"seq": self.mate_seq}
        self.twin_shard = self.place * 2 + 1 - self.half
        self.twin = {"shard": self.twin_shard}

    def outer_peer(self, place):
        return {"shard": place * 2 + self.half}

    def greet(self, wide=False):
        barrier = pltpu.get_barrier_semaphore()
        last = self.outer - 1

        def signal(peer):
            pl.semaphore_signal(barrier, inc=1, device_id=peer, device_id_type=MESH)

        signal(self.far)
        signal(self.mate)
        if wide:
            signal({"seq": 3 - self.seq})
            for amount in range(1, self.size):
                signal({"shard": lax.rem(self.shard + amount, self.size)})
            pl.semaphore_wait(barrier, 2 + self.size)
            return
        signal(self.twin)

        @pl.when(self.place < last)
        def _():
            signal(self.outer_peer(self.place + 1))

        @pl.when(self.place > 0)
        def _():
            signal(self.outer_peer(self.place - 1))

        inner = ((self.place > 0) & (self.place < last)).astype(jnp.int32)
        pl.semaphore_wait(barrier, 4 + inner)


def remote(source, target, send, receive, peer):
    return pltpu.make_async_remote_copy(
        src_ref=source,
        dst_ref=target,
        send_sem=send,
        recv_sem=receive,
        device_id=peer,
        device_id_type=MESH,
    )


class LineGather:
    def __init__(self, here, own, slot, sems):
        self.here, self.own, self.slot = here, own, slot
        self.us, self.ur, self.ds, self.dr = sems
        self.last = here.outer - 1

    def up(self, distance):
        here = self.here
        slot = self.slot(here.place - distance)
        source = slot if distance else self.own
        peer = here.outer_peer(here.place + 1)
        return remote(source, slot, self.us.at[distance], self.ur.at[distance], peer)

    def down(self, distance):
        here = self.here
        slot = self.slot(here.place + distance)
        source = slot if distance else self.own
        peer = here.outer_peer(here.place - 1)
        return remote(source, slot, self.ds.at[distance], self.dr.at[distance], peer)

    def send(self):
        here = self.here

        @pl.when(here.place < self.last)
        def _():
            self.up(0).start()

        @pl.when(here.place > 0)
        def _():
            self.down(0).start()

    def step(self, distance, arrived=lambda place: None):
        here = self.here
        below = here.place - 1 - distance
        above = here.place + 1 + distance

        @pl.when(below >= 0)
        def _():
            slot = self.slot(below)
            remote(slot, slot, self.us.at[0], self.ur.at[distance], here.twin).wait_recv()

            @pl.when(here.place < self.last)
            def _():
                self.up(distance + 1).start()

            arrived(below)

        @pl.when(above <= self.last)
        def _():
            slot = self.slot(above)
            remote(slot, slot, self.ds.at[0], self.dr.at[distance], here.twin).wait_recv()

            @pl.when(here.place > 0)
            def _():
                self.down(distance + 1).start()

            arrived(above)

    def finish(self):
        here = self.here
        for distance in range(self.last):

            @pl.when((here.place - distance >= 0) & (here.place < self.last))
            def _():
                self.up(distance).wait_send()

            @pl.when((here.place + distance <= self.last) & (here.place > 0))
            def _():
                self.down(distance).wait_send()


class RowGather:
    def __init__(self, here, own, whole, sems, spot=lambda shard: shard):
        self.here, self.own, self.whole, self.spot = here, own, whole, spot
        self.ys, self.yr, self.local = sems[4:]
        self.line = LineGather(here, own, self.mine, sems[:4])

    def mine(self, place):
        return self.whole.at[self.spot(place * 2 + self.here.half)]

    def theirs(self, place):
        return self.whole.at[self.spot(place * 2 + 1 - self.here.half)]

    def keep(self):
        return pltpu.make_async_copy(self.own, self.mine(self.here.place), self.local)

    def across(self, place, own=False):
        slot = self.mine(place)
        source = self.own if own else slot
        return remote(source, slot, self.ys.at[place], self.yr.at[place], self.here.twin)

    def arrived(self, place):
        slot = self.theirs(place)
        remote(slot, slot, self.ys.at[place], self.yr.at[place], self.here.twin).wait_recv()

    def send(self):
        self.line.send()
        self.across(self.here.place, own=True).start()
        self.keep().start()

    def step(self, distance):
        self.line.step(distance, lambda place: self.across(place).start())

    def arrive(self):
        self.keep().wait()
        for place in range(self.here.outer):
            self.arrived(place)

    def finish(self):
        self.line.finish()
        for place in range(self.here.outer):
            self.across(place).wait_send()


class TwinFirstGather(RowGather):
    def __init__(self, here, own, whole, sems, twin_sems):
        super().__init__(here, own, whole, sems)
        self.lines = [
            self.line,
            LineGather(here, self.theirs(here.place), self.theirs, twin_sems[:4]),
        ]

    def twin(self):
        self.arrived(self.here.place)
        self.lines[1].send()

    def step(self, distance):
        for line in self.lines:
            line.step(distance)

    def arrive(self):
        self.keep().wait()

    def finish(self):
        for line in self.lines:
            line.finish()
        self.across(self.here.place, own=True).wait_send()


class HeadGather:
    def __init__(self, here, own, whole, sems):
        self.here, self.own, self.whole = here, own, whole
        self.us, self.zr, self.ds, _, self.ys, self.yr, self.local = sems
        self.last = here.outer - 1
        self.count = here.quarter // 2
        self.first = here.seq * self.count
        self.mine = here.place - self.first
        self.inside = (self.mine >= 0) & (self.mine < self.count)

    def slot(self, index):
        return self.whole.at[index * 2 + self.here.half]

    def keep(self):
        return pltpu.make_async_copy(self.own, self.slot(self.mine), self.local)

    def up(self, index, own=False):
        slot = self.slot(index)
        peer = self.here.outer_peer(self.here.place + 1)
        return remote(self.own if own else slot, slot, self.us.at[index], self.zr.at[index], peer)

    def down(self, index, own=False):
        slot = self.slot(index)
        peer = self.here.outer_peer(self.here.place - 1)
        return remote(self.own if own else slot, slot, self.ds.at[index], self.zr.at[index], peer)

    def across(self, index):
        slot = self.slot(index)
        return remote(slot, slot, self.ys.at[index], self.yr.at[index], self.here.twin)

    def send(self):
        @pl.when(self.inside)
        def _():
            self.keep().start()

            @pl.when(self.here.place < self.last)
            def _():
                self.up(self.mine, own=True).start()

            @pl.when(self.here.place > 0)
            def _():
                self.down(self.mine, own=True).start()

    def step(self):
        here = self.here

        @pl.when(self.inside)
        def _():
            self.keep().wait()

        for index in range(self.count):
            slot = self.slot(index)
            arrival = remote(slot, slot, self.us.at[0], self.zr.at[index], here.twin)

            @pl.when(self.mine > index)
            def _():
                arrival.wait_recv()

                @pl.when(here.place < self.last)
                def _():
                    self.up(index).start()

            @pl.when(self.mine < index)
            def _():
                arrival.wait_recv()

                @pl.when(here.place > 0)
                def _():
                    self.down(index).start()

            self.across(index).start()

    def arrive(self):
        for index in range(self.count):
            slot = self.whole.at[index * 2 + 1 - self.here.half]
            remote(
                slot, slot, self.ys.at[index], self.yr.at[index], self.here.twin
            ).wait_recv()

    def finish(self):
        here = self.here
        for index in range(self.count):

            @pl.when((self.mine >= index) & (here.place < self.last))
            def _():
                self.up(index).wait_send()

            @pl.when((self.mine <= index) & (here.place > 0))
            def _():
                self.down(index).wait_send()

            self.across(index).wait_send()


class TokenGather:
    def __init__(self, here, own, whole, sems, parts=1):
        self.here, self.own, self.whole, self.parts = here, own, whole, parts
        self.send_sems, self.recv_sems, self.local = sems
        self.rows = whole.shape[0] // 4

    def slot(self, seq):
        return self.whole.at[pl.ds(pl.multiple_of(seq * self.rows, self.rows), self.rows), :]

    def keep(self):
        return pltpu.make_async_copy(self.own, self.slot(self.here.seq), self.local)

    def copy(self, kind, part=0):
        here = self.here
        count = self.rows // self.parts
        seq = here.far_seq if kind == 2 else here.seq
        slot = self.whole.at[
            pl.ds(pl.multiple_of(seq * self.rows + part * count, count), count), :
        ]
        own = self.own.at[part * count : (part + 1) * count, :]
        index = kind * self.parts + part
        return remote(
            slot if kind == 2 else own,
            slot,
            self.send_sems.at[index],
            self.recv_sems.at[index],
            here.far if kind == 0 else here.mate,
        )

    def send(self, part=0):
        self.copy(0, part).start()
        self.copy(1, part).start()
        if part == self.parts - 1:
            self.keep().start()

    def forward(self):
        for part in range(self.parts):
            self.copy(0, part).wait_recv()
            self.copy(2, part).start()

    def mate_arrived(self):
        for part in range(self.parts):
            self.copy(1, part).wait_recv()

    def rest_arrived(self):
        for part in range(self.parts):
            self.copy(2, part).wait_recv()
        self.keep().wait()

    def arrive(self):
        self.mate_arrived()
        self.rest_arrived()

    def finish(self):
        for kind in range(3):
            for part in range(self.parts):
                self.copy(kind, part).wait_send()


class PieceSum:
    def __init__(self, here, piece, base, give, got, pair, far_got, sems, step):
        self.here, self.piece, self.base, self.step = here, piece, base, step
        self.give, self.got, self.pair, self.far_got = give, got, pair, far_got
        self.send_sems, self.recv_sems = sems

    def to_mate(self, index):
        return remote(
            self.give.at[index],
            self.got.at[index],
            self.send_sems.at[index],
            self.recv_sems.at[index],
            self.here.mate,
        )

    def to_far(self):
        return remote(
            self.pair, self.far_got, self.send_sems.at[2], self.recv_sems.at[2], self.here.far
        )

    def columns(self, body):
        step = self.step

        @pl.loop(0, self.pair.shape[1] // step)
        def _(index):
            body(pl.ds(pl.multiple_of(index * step, step), step))

    def send(self):
        here = self.here
        for index, chip in enumerate((1 - here.chip, here.chip)):
            seq = chip * 2 + 1 - here.core

            def fill(column, index=index, seq=seq):
                self.give[index, :, column] = self.piece(seq, column).astype(BF)

            self.columns(fill)
            self.to_mate(index).start()

    def pass_on(self):
        self.to_mate(0).wait_recv()

        def fill(column):
            term = self.piece(self.here.far_seq, column) + self.got[0, :, column].astype(F32)
            self.pair[:, column] = term.astype(BF)

        self.columns(fill)
        self.to_far().start()

    def add_near(self):
        self.to_mate(1).wait_recv()

        def fill(column):
            term = self.piece(self.here.seq, column) + self.got[1, :, column].astype(F32)
            self.base[:, column] += term

        self.columns(fill)

    def add_far(self):
        self.to_far().wait_recv()

        def fill(column):
            self.base[:, column] += self.far_got[:, column].astype(F32)

        self.columns(fill)
        for copy in (self.to_mate(0), self.to_mate(1), self.to_far()):
            copy.wait_send()


def identity(size):
    rows = lax.broadcasted_iota(jnp.int32, (size, size), 0)
    columns = lax.broadcasted_iota(jnp.int32, (size, size), 1)
    return jnp.where(rows == columns, 1.0, 0.0).astype(BF)


FORWARD_PLAN = (
    (("down", "send"),),
    (("out", "send"),),
    (("down", 0),),
    (),
    (),
    (("down", 1), ("down", 2), ("out", 0),),
    (),
    (),
    (("first", "send"),),
    (),
    (("second", "send"),),
    (),
    (),
    (("first", 0),),
    (),
    (),
    (("third", "send"),),
    (("first", 1),),
    (),
    (("second", "twin"), ("second", 0), ("first", 2),),
    (("third", 0),),
    (("second", 1),),
    (),
    (),
    (("third", 1),),
    (),
    (("second", 2), ("third", 2),),
    (),
    (),
)


def forward_kernel(
    size,
    hidden_hbm,
    dy_hbm,
    w_query,
    w_key,
    w_value,
    w_out,
    w_gate,
    w_up,
    w_down,
    attn_gain_ref,
    mlp_gain_ref,
    query_gain_ref,
    key_gain_ref,
    inverse_ref,
    segment_ref,
    qkv_full,
    out_full,
    first_full,
    second_full,
    down_full,
    n1_full,
    dy_full,
    n2_full,
    n1_turned,
    dy_turned,
    n2_turned,
    act_out,
    first_pair,
    second_pair,
    proj_out,
    heads_out,
    mixed_out,
    lse_out,
    middle_out,
    cos_out,
    sin_out,
    start_out,
    lhs,
    dy_all,
    turned,
    qkv_w,
    out_w,
    qkv_own,
    out_own,
    down_own,
    dy_own,
    wide_own,
    first_own,
    second_own,
    own_rows,
    give,
    got,
    pair,
    far_got,
    us,
    ur,
    ds,
    dr,
    ys,
    yr,
    row_local,
    ts,
    tr,
    token_local,
    load_sem,
    ss,
    sr,
    start_ref,
    turned_ids,
    eye,
    hidden_ref,
    proj_ref,
    heads_ref,
    mixed_ref,
    lse_ref,
    middle_ref,
    cos_ref,
    sin_ref,
    start_row,
    store_sems,
):
    here = Place(size)
    last = here.outer - 1
    length, width = lhs.shape
    lse_ref[...] = jnp.zeros_like(lse_ref)
    rows = length // 4
    units = act_out.shape[1]
    chunk = units // 2
    tail = 256
    heads = mixed_ref.shape[1] // HEAD_DIM
    kv_heads = heads // 2
    ff_part = units // size

    def sems(index):
        return tuple(kind.at[index] for kind in (us, ur, ds, dr, ys, yr, row_local))

    down_rows = pl.ds(pl.multiple_of(here.seq * ff_part, ff_part), ff_part)
    qkv = RowGather(here, qkv_own, qkv_full, sems(0))
    out = HeadGather(here, out_own, out_full, sems(1))
    down = RowGather(
        here,
        down_own,
        down_full,
        sems(2),
        lambda shard: pl.ds(pl.multiple_of(shard * ff_part, ff_part), ff_part),
    )
    first = RowGather(here, first_own, first_full, sems(3))
    cut = 2 * (chunk - tail)
    second = TwinFirstGather(
        here, second_own.at[:, 0:cut], second_full.at[:, :, 0:cut], sems(4), sems(6)
    )
    third = RowGather(
        here, second_own.at[:, cut : 2 * chunk], second_full.at[:, :, cut : 2 * chunk], sems(5)
    )
    n1 = TokenGather(here, own_rows.at[0], n1_full, (ts.at[0], tr.at[0], token_local.at[0]))
    n2 = TokenGather(here, own_rows.at[1], n2_full, (ts.at[1], tr.at[1], token_local.at[1]))
    dy = TokenGather(here, dy_own, dy_full, (ts.at[2], tr.at[2], token_local.at[2]))

    loads = []
    stores = []

    def hand_out(*pairs):
        for source, target in pairs:
            copy = pltpu.make_async_copy(source, target, store_sems.at[len(stores)])
            copy.start()
            stores.append(copy)

    load_hidden = pltpu.make_async_copy(hidden_hbm, hidden_ref, load_sem.at[8])
    at = 0
    for index, (weight, count) in enumerate(((w_query, heads), (w_key, kv_heads), (w_value, kv_heads))):
        count = count * HEAD_DIM
        source = weight.at[:, pl.ds(pl.multiple_of(here.seq * count, count), count)]
        loads.append(
            pltpu.make_async_copy(source, qkv_own.at[:, at : at + count], load_sem.at[index])
        )
        at += count
    loads.append(pltpu.make_async_copy(w_down.at[down_rows, :], down_own, load_sem.at[3]))
    loads.append(pltpu.make_async_copy(w_out, out_own, load_sem.at[4]))
    loads.append(pltpu.make_async_copy(dy_hbm, dy_own, load_sem.at[5]))
    loads.append(pltpu.make_async_copy(w_gate, wide_own, load_sem.at[6]))
    for load in loads:
        load.start()
    load_hidden.start()
    here.greet()
    for load in loads[:3]:
        load.wait()
    qkv.send()
    loads[5].wait()
    dy.send()

    def norm_rows(source, gain_ref, target):
        @pl.loop(0, rows // 32)
        def _(index):
            part = pl.ds(pl.multiple_of(index * 32, 32), 32)
            values = source[part, :].astype(F32)
            scales = lax.rsqrt(jnp.mean(values * values, axis=-1, keepdims=True) + EPSILON)
            target[part, :] = (values * scales * gain_ref[...]).astype(BF)

    gathers = {"out": out, "down": down, "first": first, "second": second, "third": third}

    def advance(steps):
        for name, step in steps:
            gather = gathers[name]
            if step == "send":
                gather.send()
            elif step == "twin":
                gather.twin()
            elif name == "out":
                gather.step()
            else:
                for distance in range(last * step // 3, last * (step + 1) // 3):
                    gather.step(distance)

    load_hidden.wait()
    norm_rows(hidden_ref, attn_gain_ref, own_rows.at[0])
    n1.send()
    for load in loads[3:5]:
        load.wait()
    advance(FORWARD_PLAN[0])
    for load in loads[6:]:
        load.wait()

    most = chunk - tail

    def cut_units(side):
        for seq in range(4):

            @pl.when(here.seq == seq)
            def _():
                @pl.loop(0, wide_own.shape[0] // 16)
                def _(index):
                    part = pl.ds(pl.multiple_of(index * 16, 16), 16)

                    def gathered(begin):
                        pieces = [
                            wide_own[part, (block * 4 + seq) * ff_part : (block * 4 + seq + 1) * ff_part]
                            for block in range(begin, begin + size // 2)
                        ]
                        return jnp.concatenate(pieces, axis=1)

                    first_own[part, side * chunk : (side + 1) * chunk] = gathered(0)
                    rest = gathered(size // 2)
                    second_own[part, side * most : (side + 1) * most] = rest[:, 0:most]
                    at = 2 * most + side * tail
                    second_own[part, at : at + tail] = rest[:, most:]

    eye[...] = identity(256)

    def rotation():
        ids = segment_ref[...].astype(F32)
        turned_ids[...] = jnp.broadcast_to(ids, (128, length)).T
        lane = lax.broadcasted_iota(jnp.int32, (128, 128), 1)

        @pl.loop(0, length // 128)
        def _(index):
            part = pl.ds(pl.multiple_of(index * 128, 128), 128)
            own_ids = turned_ids[part, :]
            count = jnp.zeros((128, 128), F32)
            for at in range(0, length, 128):
                count = count + jnp.where(
                    segment_ref[:, at : at + 128].astype(F32) < own_ids, 1.0, 0.0
                )
            starts = jnp.sum(count, axis=-1, keepdims=True)
            start_ref[part, :] = starts.astype(jnp.int32)
            starts = jnp.broadcast_to(starts, (128, 128))
            turned_ids[part, :] = starts
            places = lax.broadcasted_iota(jnp.int32, (128, 128), 0) + index * 128
            angles = (places.astype(F32) - starts) * inverse_ref[...]
            cos_ref[part, :] = jnp.cos(angles)
            sine = jnp.sin(angles)
            sin_ref[part, :] = jnp.where(lane < HEAD_DIM // 2, -sine, sine)

        start_row[...] = turned_ids[...].T[0:1].astype(jnp.int32)

    zones = width // 512

    def turn(source, target):
        for seq_group in range(4):
            for zone in range(0, zones, 2):
                at = (seq_group * zones + zone) * 128
                both = contract_cols(eye[...], source[:, at : at + 256]).astype(BF)
                turned[zone * 4 + seq_group] = both[0:128]
                turned[zone * 4 + 4 + seq_group] = both[128:256]
        copy = pltpu.make_async_copy(turned, target, load_sem.at[4])
        copy.start()
        return copy

    cut_units(0)
    load_up = pltpu.make_async_copy(w_up, wide_own, load_sem.at[7])
    load_up.start()
    load_up.wait()
    cut_units(1)
    advance(FORWARD_PLAN[1])
    for third_part in range(3):
        for distance in range(last * third_part // 3, last * (third_part + 1) // 3):
            qkv.step(distance)
        advance(FORWARD_PLAN[2 + third_part])
        if third_part == 0:
            rotation()
            hand_out((cos_ref, cos_out), (sin_ref, sin_out), (start_row, start_out))
            dy.forward()
    dy.arrive()
    load_dy = pltpu.make_async_copy(dy_full, dy_all, load_sem.at[0])
    load_dy.start()
    load_dy.wait()
    store = turn(dy_all, dy_turned)
    n1.forward()
    advance(FORWARD_PLAN[5])
    n1.arrive()
    load_lhs = pltpu.make_async_copy(n1_full, lhs, load_sem.at[0])
    load_lhs.start()
    advance(FORWARD_PLAN[6])
    qkv.arrive()
    load_qkv = pltpu.make_async_copy(qkv_full, qkv_w, load_sem.at[1])
    load_qkv.start()
    advance(FORWARD_PLAN[7])
    load_lhs.wait()
    load_qkv.wait()

    def project(tile):
        weight = qkv_w[:, :, tile * 256 : tile * 256 + 256].reshape(width, 256)
        gain_ref = query_gain_ref if tile < heads // 2 else key_gain_ref

        @pl.loop(0, 2)
        def _(index):
            part = pl.ds(pl.multiple_of(index * 2 * rows, 2 * rows), 2 * rows)
            both = dot(lhs[part, :], weight)
            for side in range(2):
                head = tile * 2 + side
                proj = both[:, side * HEAD_DIM : (side + 1) * HEAD_DIM]
                if head >= heads + kv_heads:
                    heads_ref[head, part, :] = proj.astype(BF)
                    continue
                proj_ref[head, part, :] = proj
                scales = lax.rsqrt(jnp.mean(proj * proj, axis=-1, keepdims=True) + EPSILON)
                gained = proj * scales * gain_ref[...]
                turned = pltpu.roll(gained, HEAD_DIM // 2, 1)
                heads_ref[head, part, :] = (
                    gained * cos_ref[part, :] + turned * sin_ref[part, :]
                ).astype(BF)

    def attend(head, blocks):
        pair_head = head // 2
        for block in blocks:
            end = (block + 1) * rows
            part = pl.ds(block * rows, rows)
            scores = contract_cols(
                heads_ref[head, part, :], heads_ref[heads + pair_head, 0:end, :]
            )
            row_place = lax.broadcasted_iota(jnp.int32, (rows, end), 0) + block * rows
            col_place = lax.broadcasted_iota(jnp.int32, (rows, end), 1)
            allowed = (col_place >= start_ref[part, :]) & (col_place <= row_place)
            raised = jnp.where(allowed, jnp.exp(scores * (HEAD_DIM ** (-0.5))), 0.0)
            sums = jnp.sum(raised, axis=-1, keepdims=True)
            mixed = dot(raised.astype(BF), heads_ref[heads + kv_heads + pair_head, 0:end, :])
            mixed = mixed * (1.0 / sums)
            mixed_ref[part, head * HEAD_DIM : (head + 1) * HEAD_DIM] = mixed.astype(BF)
            lse_ref[part, head : head + 1] = jnp.log(sums)

    tiles = (heads + 2 * kv_heads) // 2
    for tile in range(tiles):
        if tile == tiles // 2:
            advance(FORWARD_PLAN[8])
        project(tile)
    hand_out((proj_ref, proj_out), (heads_ref, heads_out))
    advance(FORWARD_PLAN[9])

    for head in range(heads):
        attend(head, (0, 1, 2))
        advance(FORWARD_PLAN[10 + 2 * head])
        attend(head, (3,))
        advance(FORWARD_PLAN[11 + 2 * head])
    hand_out((mixed_ref, mixed_out), (lse_ref, lse_out))

    out.arrive()
    load_out = pltpu.make_async_copy(out_full, out_w, load_sem.at[2])
    load_out.start()
    load_out.wait()

    def out_piece(seq, column):
        part = pl.ds(pl.multiple_of(seq * rows, rows), rows)
        weight = out_w[:, :, column]
        return dot(mixed_ref[part, :], weight.reshape(-1, weight.shape[-1]))

    middle_ref[...] = hidden_ref[...].astype(F32)
    token_sum = PieceSum(
        here, out_piece, middle_ref, give, got, pair, far_got, (ss, sr), 512
    )
    token_sum.send()
    advance(FORWARD_PLAN[18])
    token_sum.pass_on()
    token_sum.add_near()
    advance(FORWARD_PLAN[19])
    token_sum.add_far()
    hand_out((middle_ref, middle_out))
    norm_rows(middle_ref, mlp_gain_ref, own_rows.at[1])
    n2.send()
    advance(FORWARD_PLAN[20])
    store.wait()
    store = turn(lhs, n1_turned)
    advance(FORWARD_PLAN[21])
    n2.forward()
    advance(FORWARD_PLAN[22])
    n2.arrive()
    load_lhs = pltpu.make_async_copy(n2_full, lhs, load_sem.at[3])
    load_lhs.start()
    down.arrive()
    first.arrive()
    load_lhs.wait()

    def feed(gather, begin, count, between=()):
        tiles = count // 256
        spot = begin // 256

        def body(gate_w, up_w, down_w, act_ref, gate_grad, up_grad):
            gate_tile = gate_w[...].reshape(width, 256)
            up_tile = up_w[...].reshape(width, 256)
            down_tile = down_w[...]
            for index, steps in enumerate(between):
                if steps:
                    pl.when(pl.program_id(0) == index + 1)(lambda steps=steps: advance(steps))

            @pl.loop(0, 2)
            def _(index):
                part = pl.ds(pl.multiple_of(index * 2 * rows, 2 * rows), 2 * rows)
                gate = dot(lhs[part, :], gate_tile)
                up = dot(lhs[part, :], up_tile)
                act_grad = contract_cols(dy_all[part, :], down_tile)
                sigmoid = jax.nn.sigmoid(gate)
                silu = gate * sigmoid
                act_ref[part, :] = (silu * up).astype(BF)
                gate_grad[part, :] = (
                    act_grad * up * sigmoid * (1.0 + gate * (1.0 - sigmoid))
                ).astype(BF)
                up_grad[part, :] = (act_grad * silu).astype(BF)

        block = gather.whole.shape[:-1] + (256,)
        grads = first_pair if begin < chunk else second_pair
        first_spot = 0 if begin < chunk + 1 else 2 * (begin - chunk) // 256
        pltpu.emit_pipeline(
            body,
            grid=(tiles,),
            in_specs=[
                pl.BlockSpec(block, lambda t: (0, 0, t)),
                pl.BlockSpec(block, lambda t: (0, 0, t + tiles)),
                pl.BlockSpec((256, width), lambda t: (t + spot, 0)),
            ],
            out_specs=[
                pl.BlockSpec((length, 256), lambda t: (0, t + spot)),
                pl.BlockSpec((length, 256), lambda t: (0, t + first_spot)),
                pl.BlockSpec((length, 256), lambda t: (0, t + first_spot + tiles)),
            ],
        )(gather.whole, gather.whole, down_full, act_out, grads, grads)

    feed(first, 0, chunk, (FORWARD_PLAN[23], FORWARD_PLAN[24]))
    advance(FORWARD_PLAN[25])
    store.wait()
    store = turn(lhs, n2_turned)
    advance(FORWARD_PLAN[26])
    second.arrive()
    feed(second, chunk, chunk - tail, (FORWARD_PLAN[27],))
    advance(FORWARD_PLAN[28])
    third.arrive()
    feed(third, 2 * chunk - tail, tail)
    store.wait()
    for copy in stores:
        copy.wait()
    for gather in (qkv, out, first, second, third, down, n1, n2, dy):
        gather.finish()


def forward(hidden, upstream, weights, gains, segment):
    size = lax.axis_size("shard")
    quarter, outer = size // 4, size // 2
    piece, width = hidden.shape
    length = piece * 4
    heads = Q_HEADS // 4
    kv_heads = KV_HEADS // 4
    w_query, _, _, w_out, w_gate, _, w_down = weights
    own = w_query.shape[0]
    qkv_width = (heads + 2 * kv_heads) * HEAD_DIM
    units = w_down.shape[0] // 4 * size

    def shape(*dims, kind=BF):
        return jax.ShapeDtypeStruct(dims, kind)

    results = [
        shape(size, own, qkv_width),
        shape(quarter, *w_out.shape),
        shape(size, own, units),
        shape(size, own, units),
        shape(units, width),
        shape(length, width),
        shape(length, width),
        shape(length, width),
        shape(width // 128, 128, length),
        shape(width // 128, 128, length),
        shape(width // 128, 128, length),
        shape(length, units),
        shape(length, units),
        shape(length, units),
        shape(heads + kv_heads, length, HEAD_DIM, kind=F32),
        shape(heads + 2 * kv_heads, length, HEAD_DIM),
        shape(length, heads * HEAD_DIM),
        shape(length, 128, kind=F32),
        shape(piece, width, kind=F32),
        shape(length, HEAD_DIM, kind=F32),
        shape(length, HEAD_DIM, kind=F32),
        shape(1, length, kind=jnp.int32),
    ]
    powers = np.arange(HEAD_DIM // 2, dtype=np.float32) * np.float32(2.0) / np.float32(HEAD_DIM)
    inverse = np.float32(ROPE_BASE) ** -powers
    dma = pltpu.SemaphoreType.DMA
    return pl.pallas_call(
        functools.partial(forward_kernel, size),
        out_shape=results,
        in_specs=[ANY] * 9 + [VMEM] * 6,
        out_specs=[ANY] * 22,
        scratch_shapes=[
            pltpu.VMEM((length, width), BF),
            pltpu.VMEM((length, width), BF),
            pltpu.VMEM((width // 128, 128, length), BF),
            pltpu.VMEM((size, own, qkv_width), BF),
            pltpu.VMEM((quarter,) + w_out.shape, BF),
            pltpu.VMEM((own, qkv_width), BF),
            pltpu.VMEM(w_out.shape, BF),
            pltpu.VMEM((w_down.shape[0] // 4, width), BF),
            pltpu.VMEM((piece, width), BF),
            pltpu.VMEM(w_gate.shape, BF),
            pltpu.VMEM((own, units), BF),
            pltpu.VMEM((own, units), BF),
            pltpu.VMEM((2, piece, width), BF),
            pltpu.VMEM((2, piece, width), BF),
            pltpu.VMEM((2, piece, width), BF),
            pltpu.VMEM((piece, width), BF),
            pltpu.VMEM((piece, width), BF),
            dma((7, outer)),
            dma((7, outer)),
            dma((7, outer)),
            dma((7, outer)),
            dma((7, outer)),
            dma((7, outer)),
            dma((7,)),
            dma((3, 3)),
            dma((3, 3)),
            dma((3,)),
            dma((9,)),
            dma((3,)),
            dma((3,)),
            pltpu.VMEM((length, 1), jnp.int32),
            pltpu.VMEM((length, 128), F32),
            pltpu.VMEM((256, 256), BF),
            pltpu.VMEM((piece, width), BF),
            pltpu.VMEM((heads + kv_heads, length, HEAD_DIM), F32),
            pltpu.VMEM((heads + 2 * kv_heads, length, HEAD_DIM), BF),
            pltpu.VMEM((length, heads * HEAD_DIM), BF),
            pltpu.VMEM((length, 128), F32),
            pltpu.VMEM((piece, width), F32),
            pltpu.VMEM((length, HEAD_DIM), F32),
            pltpu.VMEM((length, HEAD_DIM), F32),
            pltpu.VMEM((1, length), jnp.int32),
            dma((8,)),
        ],
        compiler_params=pltpu.CompilerParams(
            collective_id=0, has_side_effects=True, vmem_limit_bytes=VMEM_BYTES
        ),
        name="forward_gather",
    )(
        hidden,
        upstream,
        *weights,
        *gains,
        jnp.asarray(np.concatenate([inverse, inverse])[None], F32),
        segment[None],
    )


def add_rows(target, sources, step=16):
    groups, rows, _ = target.shape

    @pl.loop(0, rows // step)
    def _(index):
        part = pl.ds(pl.multiple_of(index * step, step), step)
        for group in range(groups):
            total = sources[0][group, part, :].astype(target.dtype)
            for source in sources[1:]:
                total = total + source[group, part, :].astype(target.dtype)
            target[group, part, :] = total


class RowSum:
    def __init__(self, here, give, keep, near, rising, falling, stage, total, sems):
        self.here, self.give, self.keep = here, give, keep
        self.near, self.rising, self.falling = near, rising, falling
        self.stage, self.total = stage, total
        self.ys, self.yr, self.us, self.ur, self.ds, self.dr, self.load = sems
        self.last = here.outer - 1

    def across(self, place):
        return remote(
            self.give.at[place],
            self.near.at[place],
            self.ys.at[place],
            self.yr.at[place],
            self.here.twin,
        )

    def up(self, place):
        peer = self.here.outer_peer(self.here.place + 1)
        return remote(
            self.keep.at[place], self.rising.at[place], self.us.at[place], self.ur.at[place], peer
        )

    def down(self, place):
        peer = self.here.outer_peer(self.here.place - 1)
        return remote(
            self.keep.at[place], self.falling.at[place], self.ds.at[place], self.dr.at[place], peer
        )

    def arrived(self, slot, send, receive):
        remote(slot, slot, send, receive, self.here.twin).wait_recv()

    def fold(self, distance):
        here = self.here
        above = here.place + distance
        below = here.place - distance

        def merge(place, line, receive, first):
            near = pltpu.make_async_copy(self.near.at[place], self.stage.at[0], self.load.at[0])
            self.arrived(self.near.at[place], self.ys.at[place], self.yr.at[place])
            near.start()

            @pl.when(first)
            def _():
                near.wait()
                add_rows(self.keep.at[place], [self.keep.at[place], self.stage.at[0]])

            @pl.when(jnp.logical_not(first))
            def _():
                self.arrived(line.at[place], self.us.at[0], receive.at[place])
                far = pltpu.make_async_copy(line.at[place], self.stage.at[1], self.load.at[1])
                far.start()
                near.wait()
                far.wait()
                add_rows(
                    self.keep.at[place], [self.keep.at[place], self.stage.at[0], self.stage.at[1]]
                )

        @pl.when(above <= self.last)
        def _():
            merge(above, self.rising, self.ur, here.place == 0)
            self.up(above).start()

        @pl.when(below >= 0)
        def _():
            merge(below, self.falling, self.dr, here.place == self.last)
            self.down(below).start()

    def finish(self):
        here = self.here
        place = here.place
        self.arrived(self.near.at[place], self.ys.at[place], self.yr.at[place])
        keep = self.keep.at[place]
        near = pltpu.make_async_copy(self.near.at[place], self.stage.at[0], self.load.at[0])
        low = pltpu.make_async_copy(self.rising.at[place], self.stage.at[1], self.load.at[1])
        high = pltpu.make_async_copy(self.falling.at[place], self.stage.at[1], self.load.at[1])
        near.start()

        @pl.when(place > 0)
        def _():
            self.arrived(self.rising.at[place], self.us.at[0], self.ur.at[place])
            low.start()
            low.wait()

        @pl.when(place == 0)
        def _():
            self.arrived(self.falling.at[place], self.ds.at[0], self.dr.at[place])
            high.start()
            high.wait()

        near.wait()

        @pl.when((place > 0) & (place < self.last))
        def _():
            add_rows(keep, [keep, self.stage.at[0], self.stage.at[1]])
            self.arrived(self.falling.at[place], self.ds.at[0], self.dr.at[place])
            high.start()
            high.wait()
            add_rows(self.total, [keep, self.stage.at[1]])

        @pl.when((place == 0) | (place == self.last))
        def _():
            add_rows(self.total, [keep, self.stage.at[0], self.stage.at[1]])

    def sent(self):
        for place in range(self.here.outer):
            self.across(place).wait_send()

    def settle(self):
        here = self.here
        for place in range(here.outer):

            @pl.when(place > here.place)
            def _():
                self.up(place).wait_send()

            @pl.when(place < here.place)
            def _():
                self.down(place).wait_send()


def compute_terms(here, give, keep, left, right, tiles, orders, senders):
    own = give.shape[2]
    per = 128 // (2 * own)
    step = 768 if give.shape[3] % 768 == 0 else 512
    for group, done in orders:
        spots = tiles(group)

        @pl.loop(0, give.shape[3] // step)
        def _(index):
            lane = pl.ds(pl.multiple_of(index * step, step), step)
            terms = dot(left(group), right(lane)).astype(BF)
            for spot, (zone, seq_group) in enumerate(spots):
                for sub in range(per):
                    at = spot * 128 + sub * 2 * own
                    even, odd = terms[at : at + own], terms[at + own : at + 2 * own]
                    place = zone * per + sub
                    keep[place, seq_group, :, lane] = jnp.where(here.half == 0, even, odd)
                    give[place, seq_group, :, lane] = jnp.where(here.half == 0, odd, even)

        for zone in done:
            for sub in range(per):
                for sender in senders:
                    sender.across(zone * per + sub).start()


class LineSum:
    def __init__(self, here, terms, rising, falling, stage, sems):
        self.here, self.terms, self.stage = here, terms, stage
        self.rising, self.falling = rising, falling
        self.us, self.ur, self.ds, self.dr, self.load = sems
        self.last = here.outer - 1

    def up(self, place):
        peer = self.here.outer_peer(self.here.place + 1)
        return remote(
            self.terms.at[place], self.rising.at[place], self.us.at[place], self.ur.at[place], peer
        )

    def down(self, place):
        peer = self.here.outer_peer(self.here.place - 1)
        return remote(
            self.terms.at[place], self.falling.at[place], self.ds.at[place], self.dr.at[place], peer
        )

    def merge(self, place, line, receive):
        slot = line.at[place]
        remote(slot, slot, self.us.at[0], receive.at[place], self.here.twin).wait_recv()
        copy = pltpu.make_async_copy(slot, self.stage.at[0], self.load.at[0])
        copy.start()
        copy.wait()
        add_rows(self.terms.at[place], [self.terms.at[place], self.stage.at[0]])

    def fold(self, distance):
        here = self.here
        above = here.place + distance
        below = here.place - distance

        @pl.when(above <= self.last)
        def _():
            @pl.when(here.place > 0)
            def _():
                self.merge(above, self.rising, self.ur)

            self.up(above).start()

        @pl.when(below >= 0)
        def _():
            @pl.when(here.place < self.last)
            def _():
                self.merge(below, self.falling, self.dr)

            self.down(below).start()

    def gather(self):
        place = self.here.place

        @pl.when(place > 0)
        def _():
            self.merge(place, self.rising, self.ur)

        @pl.when(place < self.last)
        def _():
            self.merge(place, self.falling, self.dr)

    def settle(self):
        here = self.here
        for place in range(here.outer):

            @pl.when(place > here.place)
            def _():
                self.up(place).wait_send()

            @pl.when(place < here.place)
            def _():
                self.down(place).wait_send()


class LineFirstSum(RowSum):
    def __init__(self, here, give, keep, near, lines, stage, total, sems, twin_sems):
        self.here, self.give, self.keep = here, give, keep
        self.near, self.stage, self.total = near, stage, total
        self.ys, self.yr, self.load = sems[0], sems[1], sems[6]
        self.lines = [
            LineSum(here, terms, rising, falling, stage, kinds[2:])
            for terms, (rising, falling), kinds in (
                (give, lines[0], twin_sems),
                (keep, lines[1], sems),
            )
        ]

    def fold(self, distance):
        for line in self.lines:
            line.fold(distance)

    def pass_on(self):
        self.lines[0].gather()
        self.across(self.here.place).start()
        self.lines[1].gather()

    def finish(self):
        place = self.here.place
        self.arrived(self.near.at[place], self.ys.at[place], self.yr.at[place])
        near = pltpu.make_async_copy(self.near.at[place], self.stage.at[0], self.load.at[0])
        near.start()
        near.wait()
        add_rows(self.total, [self.keep.at[place], self.stage.at[0]])

    def sent(self):
        self.across(self.here.place).wait_send()

    def settle(self):
        for line in self.lines:
            line.settle()


class RowSpread:
    def __init__(self, here, rows, whole, sems):
        self.here, self.rows, self.whole = here, rows, whole
        self.send_sems, self.recv_sems, self.local = sems

    def copy(self, amount):
        seq = lax.rem(self.here.seq + amount, 4)
        return remote(
            self.rows.at[seq],
            self.whole.at[self.here.seq],
            self.send_sems.at[amount - 1],
            self.recv_sems.at[amount - 1],
            {"seq": seq},
        )

    def keep(self):
        seq = self.here.seq
        return pltpu.make_async_copy(self.rows.at[seq], self.whole.at[seq], self.local)

    def send(self):
        for amount in (2, 3, 1):
            self.copy(amount).start()
        self.keep().start()

    def arrive(self):
        for amount in (1, 2, 3):
            self.copy(amount).wait_recv()
        self.keep().wait()

    def finish(self):
        for amount in (1, 2, 3):
            self.copy(amount).wait_send()


class TokenSum:
    def __init__(self, here, part, got, pair, far_got, base, sems):
        self.here, self.part, self.got, self.pair = here, part, got, pair
        self.far_got, self.base = far_got, base
        self.send_sems, self.recv_sems = sems
        self.rows = part.shape[0] // 4

    def piece(self, seq):
        return pl.ds(pl.multiple_of(seq * self.rows, self.rows), self.rows)

    def to_mate(self, index):
        here = self.here
        chip = here.chip if index else 1 - here.chip
        seq = chip * 2 + 1 - here.core
        return remote(
            self.part.at[self.piece(seq), :],
            self.got.at[index],
            self.send_sems.at[index],
            self.recv_sems.at[index],
            here.mate,
        )

    def to_far(self, half):
        count = self.rows // 2
        part = slice(half * count, (half + 1) * count)
        return remote(
            self.pair.at[part, :],
            self.far_got.at[part, :],
            self.send_sems.at[2 + half],
            self.recv_sems.at[2 + half],
            self.here.far,
        )

    def send(self):
        self.to_mate(0).start()
        self.to_mate(1).start()

    def loop(self, body, begin=0, count=None):
        @pl.loop(0, (count or self.rows) // 32)
        def _(index):
            body(begin + index * 32)

    def pass_on(self):
        self.to_mate(0).wait_recv()
        first = self.here.far_seq * self.rows

        def body(at):
            part = pl.ds(pl.multiple_of(at, 32), 32)
            source = pl.ds(pl.multiple_of(first + at, 32), 32)
            total = self.part[source, :].astype(F32) + self.got[0, part, :].astype(F32)
            self.pair[part, :] = total.astype(BF)

        for half in range(2):
            self.loop(body, half * (self.rows // 2), self.rows // 2)
            self.to_far(half).start()

    def add_near(self):
        self.to_mate(1).wait_recv()
        first = self.here.seq * self.rows

        def body(at):
            part = pl.ds(pl.multiple_of(at, 32), 32)
            source = pl.ds(pl.multiple_of(first + at, 32), 32)
            self.base[part, :] += self.part[source, :].astype(F32) + self.got[1, part, :].astype(F32)

        self.loop(body)
        self.to_mate(0).wait_send()
        self.to_mate(1).wait_send()

    def add_far(self, half):
        self.to_far(half).wait_recv()

        def body(at):
            part = pl.ds(pl.multiple_of(at, 32), 32)
            self.base[part, :] += self.far_got[part, :].astype(F32)

        self.loop(body, half * (self.rows // 2), self.rows // 2)
        self.to_far(half).wait_send()


class GainSum:
    def __init__(self, here, own, seq_got, middle, shard_got, sems):
        self.here, self.own, self.middle = here, own, middle
        self.seq_got, self.shard_got = seq_got, shard_got
        self.seq_send, self.seq_recv, self.shard_send, self.shard_recv = sems

    def over_seq(self, amount):
        here = self.here
        return remote(
            self.own,
            self.seq_got.at[here.seq],
            self.seq_send.at[amount - 1],
            self.seq_recv.at[amount - 1],
            {"seq": lax.rem(here.seq + amount, 4)},
        )

    def over_shard(self, amount):
        here = self.here
        return remote(
            self.middle,
            self.shard_got.at[here.shard],
            self.shard_send.at[amount - 1],
            self.shard_recv.at[amount - 1],
            {"shard": lax.rem(here.shard + amount, here.size)},
        )

    def start(self):
        for amount in range(1, 4):
            self.over_seq(amount).start()
        self.seq_got[self.here.seq] = self.own[...]

    def turn(self):
        for amount in range(1, 4):
            self.over_seq(amount).wait()
        total = self.seq_got[0]
        for index in range(1, 4):
            total = total + self.seq_got[index]
        self.middle[...] = total
        for amount in range(1, self.here.size):
            self.over_shard(amount).start()
        self.shard_got[self.here.shard] = total

    def finish(self):
        for amount in range(1, self.here.size):
            self.over_shard(amount).wait()
        total = self.shard_got[0]
        for index in range(1, self.here.size):
            total = total + self.shard_got[index]
        return total


PLAN = (
    (("down_a", 3),),
    (("down_a", 2), ("down_b", 3),),
    (("down_a", 1), ("down_b", 2),),
    (),
    (),
    (("first", 3), ("down_b", 1),),
    (("first", 2), ("down_b", "finish"),),
    (("second", 3), ("first", 1),),
    (("second", 2),),
    (),
    (("first", "finish"),),
    (("out", 3), ("second", 1),),
    (),
    (("out", 2), ("query", 3), ("down_a", "pass"), ("key", 3), ("out", 1),),
    (("query", 2), ("key", 2), ("second", "finish"), ("out", "finish"), ("query", 1), ("key", 1),),
    (("query", "finish"), ("key", "finish"),),
    (("down_a", "finish"),),
)


def backward_kernel(
    size,
    n1_hbm,
    dy_hbm,
    n2_hbm,
    act_hbm,
    first_hbm,
    second_hbm,
    proj_hbm,
    heads_hbm,
    mixed_hbm,
    lse_hbm,
    middle_hbm,
    hidden_hbm,
    dy_own,
    qkv_full,
    out_full,
    first_full,
    second_full,
    down_full,
    attn_gain_ref,
    mlp_gain_ref,
    query_gain_ref,
    key_gain_ref,
    cos_hbm,
    sin_hbm,
    start_hbm,
    grad_in_out,
    gains_out,
    grad_out_out,
    hidden_out,
    down_rows,
    first_rows,
    second_rows,
    qkv_rows,
    da_hbm,
    near_mlp,
    rising_mlp,
    falling_mlp,
    rising_twin,
    falling_twin,
    near_qkv,
    rising_qkv,
    falling_qkv,
    near_out,
    rising_out,
    falling_out,
    lhs,
    turned,
    first_r,
    second_r,
    give,
    keep,
    give_out,
    keep_out,
    stage,
    stage_out,
    dout_ref,
    da_own,
    got,
    far_got,
    pair,
    middle_grad,
    proj_buf,
    eye,
    keys_turned,
    lse_t,
    delta,
    delta_t,
    dk_sum,
    dv_sum,
    gain_row,
    gain_seq,
    gain_middle,
    gain_shard,
    ys,
    yr,
    us,
    ur,
    ds,
    dr,
    fold_load,
    spread_s,
    spread_r,
    spread_l,
    sum_s,
    sum_r,
    ts,
    tr,
    token_local,
    gss,
    gsr,
    gts,
    gtr,
    load_sem,
    credit,
    grad_in,
    grad_out,
    heads_ref,
    mixed_ref,
    lse_ref,
    cos_ref,
    sin_ref,
    start_ref,
    store_sems,
):
    here = Place(size)
    length, width = lhs.shape
    rows = length // 4
    units = first_r.shape[1]
    chunk = units // 2
    ff_part = units // size
    heads = mixed_ref.shape[1] // HEAD_DIM
    kv_heads = heads // 2
    qkv_width = qkv_full.shape[2]
    last = here.outer - 1
    scale = HEAD_DIM ** (-0.5)

    def load(source, target, index):
        copy = pltpu.make_async_copy(source, target, load_sem.at[index])
        copy.start()
        return copy

    def sems(index):
        return tuple(kind.at[index] for kind in (ys, yr, us, ur, ds, dr, fold_load))

    thin = qkv_width // 2
    cut = units * 2 // 3
    lanes = {
        "down_a": slice(0, cut),
        "down_b": slice(cut, units),
        "query": slice(0, thin),
        "key": slice(thin, 2 * thin),
    }

    def part(ref, name):
        return ref.at[:, :, :, lanes[name]]

    def row_sum(index, give_ref, keep_ref, near, rising, falling, stage_ref, total):
        return RowSum(
            here, give_ref, keep_ref, near, rising, falling, stage_ref, total, sems(index)
        )

    jobs = {
        "down_a": LineFirstSum(
            here,
            part(give.at[2], "down_a"),
            part(keep.at[0], "down_a"),
            part(near_mlp.at[0], "down_a"),
            (
                (rising_twin, falling_twin),
                (part(rising_mlp.at[0], "down_a"), part(falling_mlp.at[0], "down_a")),
            ),
            part(stage, "down_a"),
            keep.at[0, here.place, :, :, lanes["down_a"]],
            sems(0),
            sems(5),
        ),
        "down_b": row_sum(
            6,
            part(give.at[2], "down_b"),
            part(keep.at[0], "down_b"),
            part(near_mlp.at[0], "down_b"),
            part(rising_mlp.at[0], "down_b"),
            part(falling_mlp.at[0], "down_b"),
            part(stage, "down_b"),
            keep.at[0, here.place, :, :, lanes["down_b"]],
        ),
        "out": row_sum(
            4, give_out, keep_out, near_out, rising_out, falling_out, stage_out, grad_out
        ),
    }
    for index, name in ((1, "first"), (2, "second")):
        jobs[name] = row_sum(
            index,
            give.at[2 - index],
            keep.at[index],
            near_mlp.at[index],
            rising_mlp.at[index],
            falling_mlp.at[index],
            stage,
            keep.at[index, here.place],
        )
    for index, name in ((3, "query"), (7, "key")):
        jobs[name] = row_sum(
            index,
            part(give.at[1], name),
            part(second_r, name),
            part(near_qkv, name),
            part(rising_qkv, name),
            part(falling_qkv, name),
            part(stage, name),
            second_r.at[here.place, :, :, lanes[name]],
        )
    zones = width // 512

    def zone_at(index):
        zone = here.place // (here.outer // zones)
        return (
            3 * (1 - zone // 2),
            lax.rem(2 + 3 * zone, 5),
            1 + lax.rem(zone, 2),
            zone,
        )[index]

    zone_order = [zone_at(index) for index in range(zones)]
    by_zone = [(zone, (zone,)) for zone in zone_order]

    spreads = {}
    for index, (name, whole) in enumerate(
        (
            ("down_a", down_rows.at[:, :, lanes["down_a"]]),
            ("down_b", down_rows.at[:, :, lanes["down_b"]]),
            ("first", first_rows),
            ("second", second_rows),
            ("query", qkv_rows.at[:, :, lanes["query"]]),
            ("key", qkv_rows.at[:, :, lanes["key"]]),
        )
    ):
        kinds = (spread_s.at[index], spread_r.at[index], spread_l.at[index])
        spreads[name] = RowSpread(here, jobs[name].total, whole, kinds)

    def token_sum(index, base):
        return TokenSum(
            here, lhs, got, pair, far_got, base, (sum_s.at[index], sum_r.at[index])
        )

    sum_mlp = token_sum(0, middle_grad)
    sum_hidden = token_sum(1, grad_in)
    sum_attn = token_sum(2, grad_in)
    da = TokenGather(here, da_own, da_hbm, (ts, tr, token_local.at[0]), parts=2)

    def model_tiles(group):
        return [(group, seq_group) for seq_group in range(4)]

    def first_columns(lane):
        return first_r[:, lane]

    def model_left(group):
        return turned[pl.ds(group * 4, 4)].reshape(512, length)

    def advance(steps):
        for name, step in steps:
            job = jobs[name]
            if step == "pass":
                job.pass_on()
            elif step == "finish":
                job.finish()
                if name in spreads:
                    spreads[name].send()
            else:
                for distance in range(last * step // 3, last * (step - 1) // 3, -1):
                    job.fold(distance)

    load_turned = load(dy_hbm, turned, 0)
    load_act = load(act_hbm, lhs.at[:, 0:units], 1)
    eye[...] = identity(HEAD_DIM)
    here.greet(wide=True)
    load_turned.wait()
    load_act.wait()
    load_first = load(first_hbm, first_r, 1)
    load_second = load(second_hbm, second_r, 3)
    load_middle = load(middle_hbm, grad_in, 2)
    load_dy = load(dy_own, da_own, 4)
    late_loads = [
        load(source, target, 5 + index)
        for index, (source, target) in enumerate(
            (
                (mixed_hbm, mixed_ref),
                (lse_hbm, lse_ref),
                (heads_hbm, heads_ref),
                (cos_hbm, cos_ref),
                (sin_hbm, sin_ref),
                (start_hbm, start_ref),
            )
        )
    ]
    def model_terms(give_ref, keep_ref, right, senders):
        compute_terms(
            here, give_ref, keep_ref, model_left, right, model_tiles, by_zone, senders
        )

    model_terms(give.at[2], keep.at[0], lambda lane: lhs[:, lane], [jobs["down_b"]])
    advance(PLAN[0])
    load_turned = load(n2_hbm, turned, 0)
    load_first.wait()
    load_second.wait()

    own = width // size
    slabs = 256 // own

    def dn2_body(first_w, second_w):
        lane = pl.ds(pl.multiple_of(pl.program_id(0) * 256, 256), 256)
        first_tile = first_w[...].reshape(256, units)
        second_tile = second_w[...].reshape(256, units)

        @pl.loop(0, 2)
        def _(index):
            part = pl.ds(pl.multiple_of(index * 2 * rows, 2 * rows), 2 * rows)
            total = contract_cols(first_r[part, :], first_tile)
            blocks = pl.ds(index * (here.outer // 2), here.outer // 2)
            second_rows = second_r[blocks].reshape(2 * rows, units)
            total = total + contract_cols(second_rows, second_tile)
            lhs[part, lane] = total.astype(BF)

    slab = pl.BlockSpec((slabs, own, units), lambda t: (t, 0, 0))
    pltpu.emit_pipeline(dn2_body, grid=(width // 256,), in_specs=[slab, slab])(
        first_full, second_full
    )
    sum_mlp.send()
    middle_grad[...] = jnp.zeros_like(middle_grad)
    load_turned.wait()
    advance(PLAN[1])
    sum_mlp.pass_on()
    sum_mlp.add_near()
    model_terms(give.at[1], keep.at[1], first_columns, [jobs["first"]])
    load_act = load(act_hbm, first_r, 1)
    advance(PLAN[2])

    load_middle.wait()
    load_dy.wait()
    gain_row[...] = jnp.zeros_like(gain_row)
    mlp_lane = slice(2 * HEAD_DIM, 2 * HEAD_DIM + width)
    attn_lane = slice(2 * HEAD_DIM + width, 2 * HEAD_DIM + 2 * width)
    narrow = 16

    for half in range(2):
        sum_mlp.add_far(half)

        @pl.loop(0, rows // 2 // narrow)
        def _(index):
            at = half * (rows // 2) + index * narrow
            part = pl.ds(pl.multiple_of(at, narrow), narrow)
            values = grad_in[part, :]
            scales = lax.rsqrt(jnp.mean(values * values, axis=-1, keepdims=True) + EPSILON)
            normed = values * scales
            update = middle_grad[part, :]
            gain_row[:, mlp_lane] += jnp.sum(update * normed, axis=0, keepdims=True)
            upper = update * mlp_gain_ref[...]
            inner = jnp.mean(upper * normed, axis=-1, keepdims=True)
            grad = da_own[part, :].astype(F32) + scales * (upper - normed * inner)
            middle_grad[part, :] = grad
            da_own[part, :] = grad.astype(BF)

        da.send(half)

    advance(PLAN[3])
    model_terms(
        give.at[0],
        keep.at[2],
        lambda lane: second_r[:, :, :, lane].reshape(length, -1),
        [jobs["second"]],
    )
    advance(PLAN[4])

    def hidden_body(weight):
        lane = pl.ds(pl.multiple_of(pl.program_id(0) * 256, 256), 256)
        tile = weight[...]

        @pl.loop(0, 2)
        def _(index):
            part = pl.ds(pl.multiple_of(index * 2 * rows, 2 * rows), 2 * rows)
            lhs[part, lane] = dot(first_r[part, :], tile).astype(BF)

    load_act.wait()
    pltpu.emit_pipeline(
        hidden_body,
        grid=(width // 256,),
        in_specs=[pl.BlockSpec((units, 256), lambda t: (0, t))],
    )(down_full)
    da.mate_arrived()
    sum_hidden.send()
    da.forward()
    advance(PLAN[5])
    sum_hidden.pass_on()
    sum_hidden.add_near()
    advance(PLAN[6])
    da.rest_arrived()
    da.finish()
    load_lhs = load(da_hbm, lhs, 0)
    load_own = load(hidden_hbm, da_own, 2)
    load_lhs.wait()

    def dout_body(weight):
        lane = pl.ds(pl.multiple_of(pl.program_id(0) * 256, 256), 256)
        tile = weight[...].reshape(256, width)

        @pl.loop(0, 2)
        def _(index):
            part = pl.ds(pl.multiple_of(index * 2 * rows, 2 * rows), 2 * rows)
            dout_ref[part, lane] = contract_cols(lhs[part, :], tile).astype(BF)

    out_blocks, out_rows = out_full.shape[:2]
    pltpu.emit_pipeline(
        dout_body,
        grid=(out_blocks * out_rows // 256,),
        in_specs=[pl.BlockSpec((256 // out_rows, out_rows, width), lambda t: (t, 0, 0))],
    )(out_full)

    for late in late_loads:
        late.wait()
    for head in range(heads):
        lane = slice(head * HEAD_DIM, (head + 1) * HEAD_DIM)
        turned[head] = contract_cols(eye[...], mixed_ref[:, lane]).astype(BF)
    compute_terms(
        here,
        give_out,
        keep_out,
        lambda group: turned[0:heads].reshape(heads * HEAD_DIM, length),
        lambda lane: lhs[:, lane],
        lambda group: [(zone, 0) for zone in range(heads)],
        [(0, zone_order)],
        [jobs["out"]],
    )
    load_turned = load(n1_hbm, turned, 0)
    sum_hidden.add_far(0)
    sum_hidden.add_far(1)
    for index, peer in enumerate((here.mate, here.far)):
        pl.semaphore_signal(credit.at[index], inc=1, device_id=peer, device_id_type=MESH)

    @pl.loop(0, rows // 32)
    def _(index):
        part = pl.ds(pl.multiple_of(index * 32, 32), 32)
        pair[part, :] = grad_in[part, :].astype(BF)

    store_hidden = load(pair, hidden_out, 1)
    advance(PLAN[7])

    lse_t[...] = lse_ref[...].T[0:8]
    delta[...] = jnp.zeros_like(delta)
    for head in range(heads):
        lane = slice(head * HEAD_DIM, (head + 1) * HEAD_DIM)
        terms = dout_ref[:, lane].astype(F32) * mixed_ref[:, lane].astype(F32)
        delta[:, head : head + 1] = jnp.sum(terms, axis=-1, keepdims=True)
    delta_t[...] = delta[...].T[0:8]
    def through_norm(grad, head, part, gain_ref, which):
        proj = proj_buf[part, :]
        scales = lax.rsqrt(jnp.mean(proj * proj, axis=-1, keepdims=True) + EPSILON)
        normed = proj * scales
        grad = grad.astype(F32)
        upper = grad * cos_ref[part, :] - pltpu.roll(grad, HEAD_DIM // 2, 1) * sin_ref[part, :]
        gain_row[:, which * HEAD_DIM : (which + 1) * HEAD_DIM] += jnp.sum(
            upper * normed, axis=0, keepdims=True
        )
        upper = upper * gain_ref[...]
        inner = jnp.mean(upper * normed, axis=-1, keepdims=True)
        result = (scales * (upper - normed * inner)).astype(BF)
        first_r[part, head * HEAD_DIM : (head + 1) * HEAD_DIM] = result

    for head in range(heads):
        pair_head = head // 2
        load_proj = load(proj_hbm.at[head], proj_buf, 4)
        if head % 2 == 0:
            dk_sum[...] = jnp.zeros_like(dk_sum)
            dv_sum[...] = jnp.zeros_like(dv_sum)
            keys_turned[...] = contract_cols(eye[...], heads_ref[heads + pair_head]).astype(BF)
        for block in range(4):
            end = (block + 1) * rows
            part = pl.ds(block * rows, rows)
            queries = heads_ref[head, part, :]
            keys = heads_ref[heads + pair_head, 0:end, :]
            values = heads_ref[heads + kv_heads + pair_head, 0:end, :]
            out_grad = dout_ref[part, head * HEAD_DIM : (head + 1) * HEAD_DIM]
            scores = contract_cols(keys, queries)
            key_place = lax.broadcasted_iota(jnp.int32, (end, rows), 0)
            query_place = lax.broadcasted_iota(jnp.int32, (end, rows), 1) + block * rows
            allowed = (key_place >= start_ref[:, part]) & (key_place <= query_place)
            weights = jnp.exp(scores * scale - lse_t[head : head + 1, part])
            weights = jnp.where(allowed, weights, 0.0)
            weight_grad = contract_cols(values, out_grad)
            inner = delta_t[head : head + 1, part]
            score_grad = (weights * (weight_grad - inner)).astype(BF)
            dk_sum[0:end, :] += dot(score_grad, queries) * scale
            dv_sum[0:end, :] += dot(weights.astype(BF), out_grad)
            query_grad = dot(keys_turned[:, 0:end], score_grad).T
            query_grad = (query_grad * scale).astype(BF)
            if block == 0:
                load_proj.wait()
            through_norm(query_grad, head, part, query_gain_ref, 0)
        if head % 2:
            key = heads + pair_head
            value_at = (heads + kv_heads + pair_head) * HEAD_DIM
            load(proj_hbm.at[key], proj_buf, 4).wait()

            @pl.loop(0, 4)
            def _(index):
                part = pl.ds(pl.multiple_of(index * rows, rows), rows)
                through_norm(dk_sum[part, :].astype(BF), key, part, key_gain_ref, 1)
                first_r[part, value_at : value_at + HEAD_DIM] = dv_sum[part, :].astype(BF)

        advance(PLAN[8 + head])

    load_turned.wait()
    jobs["first"].sent()
    store_hidden.wait()
    proj_grads = first_r.at[:, 0:qkv_width]
    model_terms(
        give.at[1, :, :, :, 0:qkv_width],
        second_r.at[:, :, :, 0:qkv_width],
        first_columns,
        [jobs["query"], jobs["key"]],
    )
    advance(PLAN[12])

    def dn1_body(weight):
        lane = pl.ds(pl.multiple_of(pl.program_id(0) * 256, 256), 256)
        tile = weight[...].reshape(256, qkv_width)

        @pl.loop(0, 2)
        def _(index):
            part = pl.ds(pl.multiple_of(index * 2 * rows, 2 * rows), 2 * rows)
            lhs[part, lane] = contract_cols(proj_grads[part, :], tile).astype(BF)

    pltpu.emit_pipeline(
        dn1_body,
        grid=(width // 256,),
        in_specs=[pl.BlockSpec((slabs, own, qkv_width), lambda t: (t, 0, 0))],
    )(qkv_full)
    grad_in[...] = jnp.zeros_like(grad_in)
    pl.semaphore_wait(credit.at[0], 1)
    pl.semaphore_wait(credit.at[1], 1)
    sum_attn.send()
    advance(PLAN[13])
    sum_attn.pass_on()
    sum_attn.add_near()
    advance(PLAN[14])
    sum_attn.add_far(0)
    sum_attn.add_far(1)
    load_own.wait()

    @pl.loop(0, rows // narrow)
    def _(index):
        part = pl.ds(pl.multiple_of(index * narrow, narrow), narrow)
        values = da_own[part, :].astype(F32)
        scales = lax.rsqrt(jnp.mean(values * values, axis=-1, keepdims=True) + EPSILON)
        normed = values * scales
        update = grad_in[part, :]
        gain_row[:, attn_lane] += jnp.sum(update * normed, axis=0, keepdims=True)
        upper = update * attn_gain_ref[...]
        inner = jnp.mean(upper * normed, axis=-1, keepdims=True)
        grad_in[part, :] = middle_grad[part, :] + scales * (upper - normed * inner)

    store_in = pltpu.make_async_copy(grad_in, grad_in_out, store_sems.at[0])
    store_in.start()
    gain_sum = GainSum(here, gain_row, gain_seq, gain_middle, gain_shard, (gss, gsr, gts, gtr))
    gain_sum.start()
    advance(PLAN[15])
    gain_sum.turn()
    advance(PLAN[16])
    gains_out[...] = gain_sum.finish()
    store_out = pltpu.make_async_copy(grad_out, grad_out_out, store_sems.at[1])
    store_out.start()
    for spread_rows in spreads.values():
        spread_rows.arrive()
    store_in.wait()
    store_out.wait()
    for name, job in jobs.items():
        if name != "first":
            job.sent()
    for job in jobs.values():
        job.settle()
    for job in spreads.values():
        job.finish()


def backward(saved, weights, own, gains, tables, starts):
    size = lax.axis_size("shard")
    outer = size // 2
    (n1, dy, n2, act, first, second, proj, heads_all, mixed, lse, middle) = saved
    length, width = heads_all.shape[1], middle.shape[1]
    piece = length // 4
    units = act.shape[1]
    qkv_width = weights[0].shape[2]
    rows = width // (4 * size)
    q_width = mixed.shape[1]

    def shape(*dims, kind=BF):
        return jax.ShapeDtypeStruct(dims, kind)

    results = [
        shape(piece, width, kind=F32),
        shape(1, 2 * width + 2 * HEAD_DIM, kind=F32),
        shape(1, rows, width, kind=F32),
        shape(piece, width),
        shape(4, rows, units),
        shape(4, rows, units),
        shape(4, rows, units),
        shape(4, rows, qkv_width),
        shape(length, width),
    ]
    results += [shape(3, outer, 4, rows, units)] * 3
    results += [shape(outer, 4, rows, units * 2 // 3)] * 2
    results += [shape(outer, 4, rows, qkv_width)] * 3
    results += [shape(outer, 1, rows, width)] * 3
    dma = pltpu.SemaphoreType.DMA
    vmem = pltpu.VMEM
    return pl.pallas_call(
        functools.partial(backward_kernel, size),
        out_shape=results,
        in_specs=[ANY] * 18 + [VMEM] * 4 + [ANY] * 3,
        out_specs=[ANY, VMEM] + [ANY] * (len(results) - 2),
        scratch_shapes=[
            vmem((length, width), BF),
            vmem((width // 128, 128, length), BF),
            vmem((length, units), BF),
            vmem((outer, 4, rows, units), BF),
            vmem((3, outer, 4, rows, units), BF),
            vmem((3, outer, 4, rows, units), BF),
            vmem((outer, 1, rows, width), BF),
            vmem((outer, 1, rows, width), BF),
            vmem((2, 4, rows, units), BF),
            vmem((2, 1, rows, width), BF),
            vmem((length, q_width), BF),
            vmem((piece, width), BF),
            vmem((2, piece, width), BF),
            vmem((piece, width), BF),
            vmem((piece, width), BF),
            vmem((piece, width), F32),
            vmem((length, HEAD_DIM), F32),
            vmem((HEAD_DIM, HEAD_DIM), BF),
            vmem((HEAD_DIM, length), BF),
            vmem((8, length), F32),
            vmem((length, 128), F32),
            vmem((8, length), F32),
            vmem((length, HEAD_DIM), F32),
            vmem((length, HEAD_DIM), F32),
            vmem((1, 2 * width + 2 * HEAD_DIM), F32),
            vmem((4, 1, 2 * width + 2 * HEAD_DIM), F32),
            vmem((1, 2 * width + 2 * HEAD_DIM), F32),
            vmem((size, 1, 2 * width + 2 * HEAD_DIM), F32),
            dma((8, outer)),
            dma((8, outer)),
            dma((8, outer)),
            dma((8, outer)),
            dma((8, outer)),
            dma((8, outer)),
            dma((8, 3)),
            dma((6, 3)),
            dma((6, 3)),
            dma((6,)),
            dma((3, 4)),
            dma((3, 4)),
            dma((6,)),
            dma((6,)),
            dma((1,)),
            dma((3,)),
            dma((3,)),
            dma((size - 1,)),
            dma((size - 1,)),
            dma((11,)),
            pltpu.SemaphoreType.REGULAR((2,)),
            vmem((piece, width), F32),
            vmem((1, rows, width), F32),
            vmem(heads_all.shape, BF),
            vmem(mixed.shape, BF),
            vmem(lse.shape, F32),
            vmem((length, HEAD_DIM), F32),
            vmem((length, HEAD_DIM), F32),
            vmem((1, length), jnp.int32),
            dma((2,)),
        ],
        compiler_params=pltpu.CompilerParams(
            collective_id=1, has_side_effects=True, vmem_limit_bytes=VMEM_BYTES
        ),
        name="backward_sums",
    )(
        n1,
        dy,
        n2,
        act,
        first,
        second.reshape(outer, 4, rows, units),
        proj,
        heads_all,
        mixed,
        lse,
        middle,
        *own,
        *weights,
        *gains,
        *tables,
        starts,
    )


def finish_kernel(
    size,
    grad_in,
    gains,
    grad_out,
    hidden_out,
    down_rows,
    first_rows,
    second_rows,
    qkv_rows,
    grad_in_out,
    grad_out_out,
    hidden_out_out,
    grad_query,
    grad_key,
    grad_value,
    grad_gate,
    grad_up,
    grad_down,
    attn_gain,
    mlp_gain,
    query_gain,
    key_gain,
    grad_in_buf,
    grad_out_buf,
    hidden_buf,
    down_buf,
    first_buf,
    second_buf,
    qkv_buf,
    query_buf,
    key_buf,
    value_buf,
    gate_buf,
    up_buf,
    wide_buf,
    load_sems,
    store_sems,
):
    units = down_buf.shape[2]
    chunk = units // 2
    ff_part = units // size
    most, tail = chunk - 256, 256
    stores = []

    def load(source, target, index):
        copy = pltpu.make_async_copy(source, target, load_sems.at[index])
        copy.start()
        return copy

    def store(source, target):
        copy = pltpu.make_async_copy(source, target, store_sems.at[len(stores)])
        copy.start()
        stores.append(copy)

    loads = [
        load(source, target, index)
        for index, (source, target) in enumerate(
            (
                (down_rows, down_buf),
                (first_rows, first_buf),
                (second_rows, second_buf),
                (qkv_rows, qkv_buf),
                (grad_in, grad_in_buf),
                (hidden_out, hidden_buf),
                (grad_out, grad_out_buf),
            )
        )
    ]

    def place(read, target):
        @pl.loop(0, target.shape[0] // 16)
        def _(index):
            part = pl.ds(pl.multiple_of(index * 16, 16), 16)
            values = [read(seq, part).astype(F32) for seq in range(4)]
            for begin in range(0, size, size // 8):
                pieces = [
                    values[seq][:, block * ff_part : (block + 1) * ff_part]
                    for block in range(begin, begin + size // 8)
                    for seq in range(4)
                ]
                lane = slice(begin * 4 * ff_part, (begin + size // 8) * 4 * ff_part)
                target[part, lane] = jnp.concatenate(pieces, axis=1)

    def side(index):
        at = 2 * most + index * tail

        def read(seq, part):
            return jnp.concatenate(
                [
                    first_buf[seq, part, index * chunk : (index + 1) * chunk],
                    second_buf[seq, part, index * most : (index + 1) * most],
                    second_buf[seq, part, at : at + tail],
                ],
                axis=1,
            )

        return read

    loads[0].wait()
    place(lambda seq, part: down_buf[seq, part, :], wide_buf)
    store(wide_buf, grad_down)
    loads[1].wait()
    loads[2].wait()
    place(side(0), gate_buf)
    store(gate_buf, grad_gate)
    place(side(1), up_buf)
    store(up_buf, grad_up)
    loads[4].wait()
    store(grad_in_buf, grad_in_out)
    loads[5].wait()
    store(hidden_buf, hidden_out_out)
    loads[6].wait()
    store(grad_out_buf, grad_out_out)
    loads[3].wait()
    at = 0
    for buf, target in ((query_buf, grad_query), (key_buf, grad_key), (value_buf, grad_value)):
        count = buf.shape[1] // 4
        for seq in range(4):
            buf[:, seq * count : (seq + 1) * count] = qkv_buf[seq, :, at : at + count].astype(F32)
        at += count
        store(buf, target)
    at = 0
    for target in (query_gain, key_gain, mlp_gain, attn_gain):
        target[...] = gains[:, at : at + target.shape[1]]
        at += target.shape[1]
    for copy in stores:
        copy.wait()


def finish(grad_in, gains, grad_out, hidden_out, down_rows, first_rows, second_rows, qkv_rows):
    size = lax.axis_size("shard")
    piece, width = grad_in.shape
    rows, units = down_rows.shape[1:]
    qkv_width = qkv_rows.shape[2]

    def shape(*dims, kind=F32):
        return jax.ShapeDtypeStruct(dims, kind)

    results = [
        shape(piece, width),
        shape(1, rows, width),
        shape(piece, width, kind=BF),
        shape(rows, 2 * qkv_width),
        shape(rows, qkv_width),
        shape(rows, qkv_width),
        shape(rows, 4 * units),
        shape(rows, 4 * units),
        shape(rows, 4 * units),
        shape(1, width),
        shape(1, width),
        shape(1, HEAD_DIM),
        shape(1, HEAD_DIM),
    ]
    return pl.pallas_call(
        functools.partial(finish_kernel, size),
        out_shape=results,
        in_specs=[ANY, VMEM] + [ANY] * 6,
        out_specs=[ANY] * 9 + [VMEM] * 4,
        scratch_shapes=[
            pltpu.VMEM((piece, width), F32),
            pltpu.VMEM((1, rows, width), F32),
            pltpu.VMEM((piece, width), BF),
            pltpu.VMEM((4, rows, units), BF),
            pltpu.VMEM((4, rows, units), BF),
            pltpu.VMEM((4, rows, units), BF),
            pltpu.VMEM((4, rows, qkv_width), BF),
            pltpu.VMEM((rows, 2 * qkv_width), F32),
            pltpu.VMEM((rows, qkv_width), F32),
            pltpu.VMEM((rows, qkv_width), F32),
            pltpu.VMEM((rows, 4 * units), F32),
            pltpu.VMEM((rows, 4 * units), F32),
            pltpu.VMEM((rows, 4 * units), F32),
            pltpu.SemaphoreType.DMA((7,)),
            pltpu.SemaphoreType.DMA((9,)),
        ],
        compiler_params=pltpu.CompilerParams(vmem_limit_bytes=VMEM_BYTES),
        name="finish",
    )(grad_in, gains, grad_out, hidden_out, down_rows, first_rows, second_rows, qkv_rows)


def local(
    hidden_in,
    segment_ids,
    norm_attn_gain,
    w_query,
    w_key,
    w_value,
    query_gain,
    key_gain,
    w_out,
    norm_mlp_gain,
    w_gate,
    w_up,
    w_down,
    out_cotangent,
):
    segment = segment_ids[0]
    gains = (norm_attn_gain[None], norm_mlp_gain[None], query_gain[None], key_gain[None])
    results = forward(
        hidden_in[0],
        out_cotangent[0],
        (w_query, w_key, w_value, w_out, w_gate, w_up, w_down),
        gains,
        segment,
    )
    (
        grad_in,
        grad_out,
        hidden_out,
        grad_query,
        grad_key,
        grad_value,
        grad_gate,
        grad_up,
        grad_down,
        attn_gain,
        mlp_gain,
        query_grad,
        key_grad,
    ) = finish(
        *backward(
            results[8:19],
            results[:5],
            (hidden_in[0], out_cotangent[0]),
            gains,
            results[19:21],
            results[21],
        )[:8]
    )
    return (
        hidden_out[None],
        grad_in[None],
        attn_gain[0],
        grad_query,
        grad_key,
        grad_value,
        query_grad[0],
        key_grad[0],
        grad_out[0],
        mlp_gain[0],
        grad_gate,
        grad_up,
        grad_down.T,
    )


def solution(mesh):
    return jax.shard_map(
        local,
        mesh=mesh,
        in_specs=(
            P("shard", "seq", None),
            P("shard", None),
            P(),
            P("shard", None),
            P("shard", None),
            P("shard", None),
            P(),
            P(),
            P("shard", None),
            P(),
            P("shard", None),
            P("shard", None),
            P("shard", None),
            P("shard", "seq", None),
        ),
        out_specs=(
            P("shard", "seq", None),
            P("shard", "seq", None),
            P(),
            P(("seq", "shard"), None),
            P(("seq", "shard"), None),
            P(("seq", "shard"), None),
            P(),
            P(),
            P(("seq", "shard"), None),
            P(),
            P(("seq", "shard"), None),
            P(("seq", "shard"), None),
            P(None, ("seq", "shard")),
        ),
        check_vma=False,
    )
```

```python
import functools

import jax
import jax.numpy as jnp
import numpy as np
from jax import lax
from jax.experimental import pallas as pl
from jax.experimental.pallas import tpu as pltpu
from jax.sharding import PartitionSpec as P

Q_HEADS = 16
KV_HEADS = 8
HEAD_DIM = 128
EPSILON = 1e-06
ROPE_BASE = 1000000.0
NEGATIVE = -1e30
BF = jnp.bfloat16
F32 = jnp.float32
MESH = pl.DeviceIdType.MESH
ANY = pl.BlockSpec(memory_space=pl.ANY)
VMEM = pl.BlockSpec(memory_space=pltpu.VMEM)
VMEM_BYTES = 62 * 1024 * 1024


def dot(left, right):
    return jnp.dot(left, right, preferred_element_type=F32)


def contract_cols(left, right):
    return lax.dot_general(left, right, (((1,), (1,)), ((), ())), preferred_element_type=F32)


class Place:
    def __init__(self, size):
        self.size = size
        self.outer = size // 2
        self.quarter = size // 4
        self.seq = lax.axis_index("seq")
        self.shard = lax.axis_index("shard")
        self.chip = self.seq // 2
        self.core = lax.rem(self.seq, 2)
        self.place = self.shard // 2
        self.half = lax.rem(self.shard, 2)
        self.far_seq = lax.rem(self.seq + 2, 4)
        self.mate_seq = self.chip * 2 + 1 - self.core
        self.far = {"seq": self.far_seq}
        self.mate = {"seq": self.mate_seq}
        self.twin_shard = self.place * 2 + 1 - self.half
        self.twin = {"shard": self.twin_shard}

    def outer_peer(self, place):
        return {"shard": place * 2 + self.half}

    def greet(self, wide=False):
        barrier = pltpu.get_barrier_semaphore()
        last = self.outer - 1

        def signal(peer):
            pl.semaphore_signal(barrier, inc=1, device_id=peer, device_id_type=MESH)

        signal(self.far)
        signal(self.mate)
        if wide:
            signal({"seq": 3 - self.seq})
            for amount in range(1, self.size):
                signal({"shard": lax.rem(self.shard + amount, self.size)})
            pl.semaphore_wait(barrier, 2 + self.size)
            return
        signal(self.twin)

        @pl.when(self.place < last)
        def _():
            signal(self.outer_peer(self.place + 1))

        @pl.when(self.place > 0)
        def _():
            signal(self.outer_peer(self.place - 1))

        inner = ((self.place > 0) & (self.place < last)).astype(jnp.int32)
        pl.semaphore_wait(barrier, 4 + inner)


def remote(source, target, send, receive, peer):
    return pltpu.make_async_remote_copy(
        src_ref=source,
        dst_ref=target,
        send_sem=send,
        recv_sem=receive,
        device_id=peer,
        device_id_type=MESH,
    )


class LineGather:
    def __init__(self, here, own, slot, sems):
        self.here, self.own, self.slot = here, own, slot
        self.us, self.ur, self.ds, self.dr = sems
        self.last = here.outer - 1

    def up(self, distance):
        here = self.here
        slot = self.slot(here.place - distance)
        source = slot if distance else self.own
        peer = here.outer_peer(here.place + 1)
        return remote(source, slot, self.us.at[distance], self.ur.at[distance], peer)

    def down(self, distance):
        here = self.here
        slot = self.slot(here.place + distance)
        source = slot if distance else self.own
        peer = here.outer_peer(here.place - 1)
        return remote(source, slot, self.ds.at[distance], self.dr.at[distance], peer)

    def send(self):
        here = self.here

        @pl.when(here.place < self.last)
        def _():
            self.up(0).start()

        @pl.when(here.place > 0)
        def _():
            self.down(0).start()

    def step(self, distance, arrived=lambda place: None):
        here = self.here
        below = here.place - 1 - distance
        above = here.place + 1 + distance

        @pl.when(below >= 0)
        def _():
            slot = self.slot(below)
            remote(slot, slot, self.us.at[0], self.ur.at[distance], here.twin).wait_recv()

            @pl.when(here.place < self.last)
            def _():
                self.up(distance + 1).start()

            arrived(below)

        @pl.when(above <= self.last)
        def _():
            slot = self.slot(above)
            remote(slot, slot, self.ds.at[0], self.dr.at[distance], here.twin).wait_recv()

            @pl.when(here.place > 0)
            def _():
                self.down(distance + 1).start()

            arrived(above)

    def finish(self):
        here = self.here
        for distance in range(self.last):

            @pl.when((here.place - distance >= 0) & (here.place < self.last))
            def _():
                self.up(distance).wait_send()

            @pl.when((here.place + distance <= self.last) & (here.place > 0))
            def _():
                self.down(distance).wait_send()


class RowGather:
    def __init__(self, here, own, whole, sems, spot=lambda shard: shard):
        self.here, self.own, self.whole, self.spot = here, own, whole, spot
        self.ys, self.yr, self.local = sems[4:]
        self.line = LineGather(here, own, self.mine, sems[:4])

    def mine(self, place):
        return self.whole.at[self.spot(place * 2 + self.here.half)]

    def theirs(self, place):
        return self.whole.at[self.spot(place * 2 + 1 - self.here.half)]

    def keep(self):
        return pltpu.make_async_copy(self.own, self.mine(self.here.place), self.local)

    def across(self, place, own=False):
        slot = self.mine(place)
        source = self.own if own else slot
        return remote(source, slot, self.ys.at[place], self.yr.at[place], self.here.twin)

    def arrived(self, place):
        slot = self.theirs(place)
        remote(slot, slot, self.ys.at[place], self.yr.at[place], self.here.twin).wait_recv()

    def send(self):
        self.line.send()
        self.across(self.here.place, own=True).start()
        self.keep().start()

    def step(self, distance):
        self.line.step(distance, lambda place: self.across(place).start())

    def arrive(self):
        self.keep().wait()
        for place in range(self.here.outer):
            self.arrived(place)

    def finish(self):
        self.line.finish()
        for place in range(self.here.outer):
            self.across(place).wait_send()


class TwinFirstGather(RowGather):
    def __init__(self, here, own, whole, sems, twin_sems):
        super().__init__(here, own, whole, sems)
        self.lines = [
            self.line,
            LineGather(here, self.theirs(here.place), self.theirs, twin_sems[:4]),
        ]

    def twin(self):
        self.arrived(self.here.place)
        self.lines[1].send()

    def step(self, distance):
        for line in self.lines:
            line.step(distance)

    def arrive(self):
        self.keep().wait()

    def finish(self):
        for line in self.lines:
            line.finish()
        self.across(self.here.place, own=True).wait_send()


class HeadGather:
    def __init__(self, here, own, whole, sems):
        self.here, self.own, self.whole = here, own, whole
        self.us, self.zr, self.ds, _, self.ys, self.yr, self.local = sems
        self.last = here.outer - 1
        self.count = here.quarter // 2
        self.first = here.seq * self.count
        self.mine = here.place - self.first
        self.inside = (self.mine >= 0) & (self.mine < self.count)

    def slot(self, index):
        return self.whole.at[index * 2 + self.here.half]

    def keep(self):
        return pltpu.make_async_copy(self.own, self.slot(self.mine), self.local)

    def up(self, index, own=False):
        slot = self.slot(index)
        peer = self.here.outer_peer(self.here.place + 1)
        return remote(self.own if own else slot, slot, self.us.at[index], self.zr.at[index], peer)

    def down(self, index, own=False):
        slot = self.slot(index)
        peer = self.here.outer_peer(self.here.place - 1)
        return remote(self.own if own else slot, slot, self.ds.at[index], self.zr.at[index], peer)

    def across(self, index):
        slot = self.slot(index)
        return remote(slot, slot, self.ys.at[index], self.yr.at[index], self.here.twin)

    def send(self):
        @pl.when(self.inside)
        def _():
            self.keep().start()

            @pl.when(self.here.place < self.last)
            def _():
                self.up(self.mine, own=True).start()

            @pl.when(self.here.place > 0)
            def _():
                self.down(self.mine, own=True).start()

    def step(self):
        here = self.here

        @pl.when(self.inside)
        def _():
            self.keep().wait()

        for index in range(self.count):
            slot = self.slot(index)
            arrival = remote(slot, slot, self.us.at[0], self.zr.at[index], here.twin)

            @pl.when(self.mine > index)
            def _():
                arrival.wait_recv()

                @pl.when(here.place < self.last)
                def _():
                    self.up(index).start()

            @pl.when(self.mine < index)
            def _():
                arrival.wait_recv()

                @pl.when(here.place > 0)
                def _():
                    self.down(index).start()

            self.across(index).start()

    def arrive(self):
        for index in range(self.count):
            slot = self.whole.at[index * 2 + 1 - self.here.half]
            remote(
                slot, slot, self.ys.at[index], self.yr.at[index], self.here.twin
            ).wait_recv()

    def finish(self):
        here = self.here
        for index in range(self.count):

            @pl.when((self.mine >= index) & (here.place < self.last))
            def _():
                self.up(index).wait_send()

            @pl.when((self.mine <= index) & (here.place > 0))
            def _():
                self.down(index).wait_send()

            self.across(index).wait_send()


class TokenGather:
    def __init__(self, here, own, whole, sems, parts=1):
        self.here, self.own, self.whole, self.parts = here, own, whole, parts
        self.send_sems, self.recv_sems, self.local = sems
        self.rows = whole.shape[0] // 4

    def slot(self, seq):
        return self.whole.at[pl.ds(pl.multiple_of(seq * self.rows, self.rows), self.rows), :]

    def keep(self):
        return pltpu.make_async_copy(self.own, self.slot(self.here.seq), self.local)

    def copy(self, kind, part=0):
        here = self.here
        count = self.rows // self.parts
        seq = here.far_seq if kind == 2 else here.seq
        slot = self.whole.at[
            pl.ds(pl.multiple_of(seq * self.rows + part * count, count), count), :
        ]
        own = self.own.at[part * count : (part + 1) * count, :]
        index = kind * self.parts + part
        return remote(
            slot if kind == 2 else own,
            slot,
            self.send_sems.at[index],
            self.recv_sems.at[index],
            here.far if kind == 0 else here.mate,
        )

    def send(self, part=0):
        self.copy(0, part).start()
        self.copy(1, part).start()
        if part == self.parts - 1:
            self.keep().start()

    def forward(self):
        for part in range(self.parts):
            self.copy(0, part).wait_recv()
            self.copy(2, part).start()

    def mate_arrived(self):
        for part in range(self.parts):
            self.copy(1, part).wait_recv()

    def rest_arrived(self):
        for part in range(self.parts):
            self.copy(2, part).wait_recv()
        self.keep().wait()

    def arrive(self):
        self.mate_arrived()
        self.rest_arrived()

    def finish(self):
        for kind in range(3):
            for part in range(self.parts):
                self.copy(kind, part).wait_send()


class PieceSum:
    def __init__(self, here, piece, base, give, got, pair, far_got, sems, step):
        self.here, self.piece, self.base, self.step = here, piece, base, step
        self.give, self.got, self.pair, self.far_got = give, got, pair, far_got
        self.send_sems, self.recv_sems = sems

    def to_mate(self, index):
        return remote(
            self.give.at[index],
            self.got.at[index],
            self.send_sems.at[index],
            self.recv_sems.at[index],
            self.here.mate,
        )

    def to_far(self):
        return remote(
            self.pair, self.far_got, self.send_sems.at[2], self.recv_sems.at[2], self.here.far
        )

    def columns(self, body):
        step = self.step

        @pl.loop(0, self.pair.shape[1] // step)
        def _(index):
            body(pl.ds(pl.multiple_of(index * step, step), step))

    def send(self):
        here = self.here
        for index, chip in enumerate((1 - here.chip, here.chip)):
            seq = chip * 2 + 1 - here.core

            def fill(column, index=index, seq=seq):
                self.give[index, :, column] = self.piece(seq, column).astype(BF)

            self.columns(fill)
            self.to_mate(index).start()

    def pass_on(self):
        self.to_mate(0).wait_recv()

        def fill(column):
            term = self.piece(self.here.far_seq, column) + self.got[0, :, column].astype(F32)
            self.pair[:, column] = term.astype(BF)

        self.columns(fill)
        self.to_far().start()

    def add_near(self):
        self.to_mate(1).wait_recv()

        def fill(column):
            term = self.piece(self.here.seq, column) + self.got[1, :, column].astype(F32)
            self.base[:, column] += term

        self.columns(fill)

    def add_far(self):
        self.to_far().wait_recv()

        def fill(column):
            self.base[:, column] += self.far_got[:, column].astype(F32)

        self.columns(fill)
        for copy in (self.to_mate(0), self.to_mate(1), self.to_far()):
            copy.wait_send()


def identity(size):
    rows = lax.broadcasted_iota(jnp.int32, (size, size), 0)
    columns = lax.broadcasted_iota(jnp.int32, (size, size), 1)
    return jnp.where(rows == columns, 1.0, 0.0).astype(BF)


FORWARD_PLAN = (
    (("down", "send"),),
    (("out", "send"),),
    (("down", 0),),
    (),
    (),
    (("down", 1), ("down", 2), ("out", 0),),
    (),
    (),
    (("first", "send"),),
    (),
    (("second", "send"),),
    (),
    (),
    (("first", 0),),
    (),
    (),
    (("third", "send"),),
    (("first", 1),),
    (),
    (("second", "twin"), ("second", 0), ("first", 2),),
    (("third", 0),),
    (("second", 1),),
    (),
    (),
    (("third", 1),),
    (),
    (("second", 2), ("third", 2),),
    (),
    (),
)


def forward_kernel(
    size,
    hidden_hbm,
    dy_hbm,
    w_query,
    w_key,
    w_value,
    w_out,
    w_gate,
    w_up,
    w_down,
    attn_gain_ref,
    mlp_gain_ref,
    query_gain_ref,
    key_gain_ref,
    inverse_ref,
    segment_ref,
    qkv_full,
    out_full,
    first_full,
    second_full,
    down_full,
    n1_full,
    dy_full,
    n2_full,
    n1_turned,
    dy_turned,
    n2_turned,
    act_out,
    first_pair,
    second_pair,
    proj_out,
    heads_out,
    mixed_out,
    lse_out,
    middle_out,
    cos_out,
    sin_out,
    start_out,
    lhs,
    dy_all,
    turned,
    qkv_w,
    out_w,
    qkv_own,
    out_own,
    down_own,
    dy_own,
    wide_own,
    first_own,
    second_own,
    own_rows,
    give,
    got,
    pair,
    far_got,
    us,
    ur,
    ds,
    dr,
    ys,
    yr,
    row_local,
    ts,
    tr,
    token_local,
    load_sem,
    ss,
    sr,
    start_ref,
    turned_ids,
    eye,
    hidden_ref,
    proj_ref,
    heads_ref,
    mixed_ref,
    lse_ref,
    middle_ref,
    cos_ref,
    sin_ref,
    start_row,
    store_sems,
):
    here = Place(size)
    last = here.outer - 1
    length, width = lhs.shape
    lse_ref[...] = jnp.zeros_like(lse_ref)
    rows = length // 4
    units = act_out.shape[1]
    chunk = units // 2
    tail = 256
    heads = mixed_ref.shape[1] // HEAD_DIM
    kv_heads = heads // 2
    ff_part = units // size

    def sems(index):
        return tuple(kind.at[index] for kind in (us, ur, ds, dr, ys, yr, row_local))

    down_rows = pl.ds(pl.multiple_of(here.seq * ff_part, ff_part), ff_part)
    qkv = RowGather(here, qkv_own, qkv_full, sems(0))
    out = HeadGather(here, out_own, out_full, sems(1))
    down = RowGather(
        here,
        down_own,
        down_full,
        sems(2),
        lambda shard: pl.ds(pl.multiple_of(shard * ff_part, ff_part), ff_part),
    )
    first = RowGather(here, first_own, first_full, sems(3))
    cut = 2 * (chunk - tail)
    second = TwinFirstGather(
        here, second_own.at[:, 0:cut], second_full.at[:, :, 0:cut], sems(4), sems(6)
    )
    third = RowGather(
        here, second_own.at[:, cut : 2 * chunk], second_full.at[:, :, cut : 2 * chunk], sems(5)
    )
    n1 = TokenGather(here, own_rows.at[0], n1_full, (ts.at[0], tr.at[0], token_local.at[0]))
    n2 = TokenGather(here, own_rows.at[1], n2_full, (ts.at[1], tr.at[1], token_local.at[1]))
    dy = TokenGather(here, dy_own, dy_full, (ts.at[2], tr.at[2], token_local.at[2]))

    loads = []
    stores = []

    def hand_out(*pairs):
        for source, target in pairs:
            copy = pltpu.make_async_copy(source, target, store_sems.at[len(stores)])
            copy.start()
            stores.append(copy)

    load_hidden = pltpu.make_async_copy(hidden_hbm, hidden_ref, load_sem.at[8])
    at = 0
    for index, (weight, count) in enumerate(((w_query, heads), (w_key, kv_heads), (w_value, kv_heads))):
        count = count * HEAD_DIM
        source = weight.at[:, pl.ds(pl.multiple_of(here.seq * count, count), count)]
        loads.append(
            pltpu.make_async_copy(source, qkv_own.at[:, at : at + count], load_sem.at[index])
        )
        at += count
    loads.append(pltpu.make_async_copy(w_down.at[down_rows, :], down_own, load_sem.at[3]))
    loads.append(pltpu.make_async_copy(w_out, out_own, load_sem.at[4]))
    loads.append(pltpu.make_async_copy(dy_hbm, dy_own, load_sem.at[5]))
    loads.append(pltpu.make_async_copy(w_gate, wide_own, load_sem.at[6]))
    for load in loads:
        load.start()
    load_hidden.start()
    here.greet()
    for load in loads[:3]:
        load.wait()
    qkv.send()
    loads[5].wait()
    dy.send()

    def norm_rows(source, gain_ref, target):
        @pl.loop(0, rows // 32)
        def _(index):
            part = pl.ds(pl.multiple_of(index * 32, 32), 32)
            values = source[part, :].astype(F32)
            scales = lax.rsqrt(jnp.mean(values * values, axis=-1, keepdims=True) + EPSILON)
            target[part, :] = (values * scales * gain_ref[...]).astype(BF)

    gathers = {"out": out, "down": down, "first": first, "second": second, "third": third}

    def advance(steps):
        for name, step in steps:
            gather = gathers[name]
            if step == "send":
                gather.send()
            elif step == "twin":
                gather.twin()
            elif name == "out":
                gather.step()
            else:
                for distance in range(last * step // 3, last * (step + 1) // 3):
                    gather.step(distance)

    load_hidden.wait()
    norm_rows(hidden_ref, attn_gain_ref, own_rows.at[0])
    n1.send()
    for load in loads[3:5]:
        load.wait()
    advance(FORWARD_PLAN[0])
    for load in loads[6:]:
        load.wait()

    most = chunk - tail

    def cut_units(side):
        for seq in range(4):

            @pl.when(here.seq == seq)
            def _():
                @pl.loop(0, wide_own.shape[0] // 16)
                def _(index):
                    part = pl.ds(pl.multiple_of(index * 16, 16), 16)

                    def gathered(begin):
                        pieces = [
                            wide_own[part, (block * 4 + seq) * ff_part : (block * 4 + seq + 1) * ff_part]
                            for block in range(begin, begin + size // 2)
                        ]
                        return jnp.concatenate(pieces, axis=1)

                    first_own[part, side * chunk : (side + 1) * chunk] = gathered(0)
                    rest = gathered(size // 2)
                    second_own[part, side * most : (side + 1) * most] = rest[:, 0:most]
                    at = 2 * most + side * tail
                    second_own[part, at : at + tail] = rest[:, most:]

    eye[...] = identity(256)

    def rotation():
        ids = segment_ref[...].astype(F32)
        turned_ids[...] = jnp.broadcast_to(ids, (128, length)).T
        lane = lax.broadcasted_iota(jnp.int32, (128, 128), 1)

        @pl.loop(0, length // 128)
        def _(index):
            part = pl.ds(pl.multiple_of(index * 128, 128), 128)
            own_ids = turned_ids[part, :]
            count = jnp.zeros((128, 128), F32)
            for at in range(0, length, 128):
                count = count + jnp.where(
                    segment_ref[:, at : at + 128].astype(F32) < own_ids, 1.0, 0.0
                )
            starts = jnp.sum(count, axis=-1, keepdims=True)
            start_ref[part, :] = starts.astype(jnp.int32)
            starts = jnp.broadcast_to(starts, (128, 128))
            turned_ids[part, :] = starts
            places = lax.broadcasted_iota(jnp.int32, (128, 128), 0) + index * 128
            angles = (places.astype(F32) - starts) * inverse_ref[...]
            cos_ref[part, :] = jnp.cos(angles)
            sine = jnp.sin(angles)
            sin_ref[part, :] = jnp.where(lane < HEAD_DIM // 2, -sine, sine)

        start_row[...] = turned_ids[...].T[0:1].astype(jnp.int32)

    zones = width // 512

    def turn(source, target):
        for seq_group in range(4):
            for zone in range(0, zones, 2):
                at = (seq_group * zones + zone) * 128
                both = contract_cols(eye[...], source[:, at : at + 256]).astype(BF)
                turned[zone * 4 + seq_group] = both[0:128]
                turned[zone * 4 + 4 + seq_group] = both[128:256]
        copy = pltpu.make_async_copy(turned, target, load_sem.at[4])
        copy.start()
        return copy

    cut_units(0)
    load_up = pltpu.make_async_copy(w_up, wide_own, load_sem.at[7])
    load_up.start()
    load_up.wait()
    cut_units(1)
    advance(FORWARD_PLAN[1])
    for third_part in range(3):
        for distance in range(last * third_part // 3, last * (third_part + 1) // 3):
            qkv.step(distance)
        advance(FORWARD_PLAN[2 + third_part])
        if third_part == 0:
            rotation()
            hand_out((cos_ref, cos_out), (sin_ref, sin_out), (start_row, start_out))
            dy.forward()
    dy.arrive()
    load_dy = pltpu.make_async_copy(dy_full, dy_all, load_sem.at[0])
    load_dy.start()
    load_dy.wait()
    store = turn(dy_all, dy_turned)
    n1.forward()
    advance(FORWARD_PLAN[5])
    n1.arrive()
    load_lhs = pltpu.make_async_copy(n1_full, lhs, load_sem.at[0])
    load_lhs.start()
    advance(FORWARD_PLAN[6])
    qkv.arrive()
    load_qkv = pltpu.make_async_copy(qkv_full, qkv_w, load_sem.at[1])
    load_qkv.start()
    advance(FORWARD_PLAN[7])
    load_lhs.wait()
    load_qkv.wait()

    def project(tile):
        weight = qkv_w[:, :, tile * 256 : tile * 256 + 256].reshape(width, 256)
        gain_ref = query_gain_ref if tile < heads // 2 else key_gain_ref

        @pl.loop(0, 2)
        def _(index):
            part = pl.ds(pl.multiple_of(index * 2 * rows, 2 * rows), 2 * rows)
            both = dot(lhs[part, :], weight)
            for side in range(2):
                head = tile * 2 + side
                proj = both[:, side * HEAD_DIM : (side + 1) * HEAD_DIM]
                if head >= heads + kv_heads:
                    heads_ref[head, part, :] = proj.astype(BF)
                    continue
                proj_ref[head, part, :] = proj
                scales = lax.rsqrt(jnp.mean(proj * proj, axis=-1, keepdims=True) + EPSILON)
                gained = proj * scales * gain_ref[...]
                turned = pltpu.roll(gained, HEAD_DIM // 2, 1)
                heads_ref[head, part, :] = (
                    gained * cos_ref[part, :] + turned * sin_ref[part, :]
                ).astype(BF)

    def attend(head, blocks):
        pair_head = head // 2
        for block in blocks:
            end = (block + 1) * rows
            part = pl.ds(block * rows, rows)
            scores = contract_cols(
                heads_ref[head, part, :], heads_ref[heads + pair_head, 0:end, :]
            )
            row_place = lax.broadcasted_iota(jnp.int32, (rows, end), 0) + block * rows
            col_place = lax.broadcasted_iota(jnp.int32, (rows, end), 1)
            allowed = (col_place >= start_ref[part, :]) & (col_place <= row_place)
            raised = jnp.where(allowed, jnp.exp(scores * (HEAD_DIM ** (-0.5))), 0.0)
            sums = jnp.sum(raised, axis=-1, keepdims=True)
            mixed = dot(raised.astype(BF), heads_ref[heads + kv_heads + pair_head, 0:end, :])
            mixed = mixed * (1.0 / sums)
            mixed_ref[part, head * HEAD_DIM : (head + 1) * HEAD_DIM] = mixed.astype(BF)
            lse_ref[part, head : head + 1] = jnp.log(sums)

    tiles = (heads + 2 * kv_heads) // 2
    for tile in range(tiles):
        if tile == tiles // 2:
            advance(FORWARD_PLAN[8])
        project(tile)
    hand_out((proj_ref, proj_out), (heads_ref, heads_out))
    advance(FORWARD_PLAN[9])

    for head in range(heads):
        attend(head, (0, 1, 2))
        advance(FORWARD_PLAN[10 + 2 * head])
        attend(head, (3,))
        advance(FORWARD_PLAN[11 + 2 * head])
    hand_out((mixed_ref, mixed_out), (lse_ref, lse_out))

    out.arrive()
    load_out = pltpu.make_async_copy(out_full, out_w, load_sem.at[2])
    load_out.start()
    load_out.wait()

    def out_piece(seq, column):
        part = pl.ds(pl.multiple_of(seq * rows, rows), rows)
        weight = out_w[:, :, column]
        return dot(mixed_ref[part, :], weight.reshape(-1, weight.shape[-1]))

    middle_ref[...] = hidden_ref[...].astype(F32)
    token_sum = PieceSum(
        here, out_piece, middle_ref, give, got, pair, far_got, (ss, sr), 512
    )
    token_sum.send()
    advance(FORWARD_PLAN[18])
    token_sum.pass_on()
    token_sum.add_near()
    advance(FORWARD_PLAN[19])
    token_sum.add_far()
    hand_out((middle_ref, middle_out))
    norm_rows(middle_ref, mlp_gain_ref, own_rows.at[1])
    n2.send()
    advance(FORWARD_PLAN[20])
    store.wait()
    store = turn(lhs, n1_turned)
    advance(FORWARD_PLAN[21])
    n2.forward()
    advance(FORWARD_PLAN[22])
    n2.arrive()
    load_lhs = pltpu.make_async_copy(n2_full, lhs, load_sem.at[3])
    load_lhs.start()
    down.arrive()
    first.arrive()
    load_lhs.wait()

    def feed(gather, begin, count, between=()):
        tiles = count // 256
        spot = begin // 256

        def body(gate_w, up_w, down_w, act_ref, gate_grad, up_grad):
            gate_tile = gate_w[...].reshape(width, 256)
            up_tile = up_w[...].reshape(width, 256)
            down_tile = down_w[...]
            for index, steps in enumerate(between):
                if steps:
                    pl.when(pl.program_id(0) == index + 1)(lambda steps=steps: advance(steps))

            @pl.loop(0, 2)
            def _(index):
                part = pl.ds(pl.multiple_of(index * 2 * rows, 2 * rows), 2 * rows)
                gate = dot(lhs[part, :], gate_tile)
                up = dot(lhs[part, :], up_tile)
                act_grad = contract_cols(dy_all[part, :], down_tile)
                sigmoid = jax.nn.sigmoid(gate)
                silu = gate * sigmoid
                act_ref[part, :] = (silu * up).astype(BF)
                gate_grad[part, :] = (
                    act_grad * up * sigmoid * (1.0 + gate * (1.0 - sigmoid))
                ).astype(BF)
                up_grad[part, :] = (act_grad * silu).astype(BF)

        block = gather.whole.shape[:-1] + (256,)
        grads = first_pair if begin < chunk else second_pair
        first_spot = 0 if begin < chunk + 1 else 2 * (begin - chunk) // 256
        pltpu.emit_pipeline(
            body,
            grid=(tiles,),
            in_specs=[
                pl.BlockSpec(block, lambda t: (0, 0, t)),
                pl.BlockSpec(block, lambda t: (0, 0, t + tiles)),
                pl.BlockSpec((256, width), lambda t: (t + spot, 0)),
            ],
            out_specs=[
                pl.BlockSpec((length, 256), lambda t: (0, t + spot)),
                pl.BlockSpec((length, 256), lambda t: (0, t + first_spot)),
                pl.BlockSpec((length, 256), lambda t: (0, t + first_spot + tiles)),
            ],
        )(gather.whole, gather.whole, down_full, act_out, grads, grads)

    feed(first, 0, chunk, (FORWARD_PLAN[23], FORWARD_PLAN[24]))
    advance(FORWARD_PLAN[25])
    store.wait()
    store = turn(lhs, n2_turned)
    advance(FORWARD_PLAN[26])
    second.arrive()
    feed(second, chunk, chunk - tail, (FORWARD_PLAN[27],))
    advance(FORWARD_PLAN[28])
    third.arrive()
    feed(third, 2 * chunk - tail, tail)
    store.wait()
    for copy in stores:
        copy.wait()
    for gather in (qkv, out, first, second, third, down, n1, n2, dy):
        gather.finish()


def forward(hidden, upstream, weights, gains, segment):
    size = lax.axis_size("shard")
    quarter, outer = size // 4, size // 2
    piece, width = hidden.shape
    length = piece * 4
    heads = Q_HEADS // 4
    kv_heads = KV_HEADS // 4
    w_query, _, _, w_out, w_gate, _, w_down = weights
    own = w_query.shape[0]
    qkv_width = (heads + 2 * kv_heads) * HEAD_DIM
    units = w_down.shape[0] // 4 * size

    def shape(*dims, kind=BF):
        return jax.ShapeDtypeStruct(dims, kind)

    results = [
        shape(size, own, qkv_width),
        shape(quarter, *w_out.shape),
        shape(size, own, units),
        shape(size, own, units),
        shape(units, width),
        shape(length, width),
        shape(length, width),
        shape(length, width),
        shape(width // 128, 128, length),
        shape(width // 128, 128, length),
        shape(width // 128, 128, length),
        shape(length, units),
        shape(length, units),
        shape(length, units),
        shape(heads + kv_heads, length, HEAD_DIM, kind=F32),
        shape(heads + 2 * kv_heads, length, HEAD_DIM),
        shape(length, heads * HEAD_DIM),
        shape(length, 128, kind=F32),
        shape(piece, width, kind=F32),
        shape(length, HEAD_DIM, kind=F32),
        shape(length, HEAD_DIM, kind=F32),
        shape(1, length, kind=jnp.int32),
    ]
    powers = np.arange(HEAD_DIM // 2, dtype=np.float32) * np.float32(2.0) / np.float32(HEAD_DIM)
    inverse = np.float32(ROPE_BASE) ** -powers
    dma = pltpu.SemaphoreType.DMA
    return pl.pallas_call(
        functools.partial(forward_kernel, size),
        out_shape=results,
        in_specs=[ANY] * 9 + [VMEM] * 6,
        out_specs=[ANY] * 22,
        scratch_shapes=[
            pltpu.VMEM((length, width), BF),
            pltpu.VMEM((length, width), BF),
            pltpu.VMEM((width // 128, 128, length), BF),
            pltpu.VMEM((size, own, qkv_width), BF),
            pltpu.VMEM((quarter,) + w_out.shape, BF),
            pltpu.VMEM((own, qkv_width), BF),
            pltpu.VMEM(w_out.shape, BF),
            pltpu.VMEM((w_down.shape[0] // 4, width), BF),
            pltpu.VMEM((piece, width), BF),
            pltpu.VMEM(w_gate.shape, BF),
            pltpu.VMEM((own, units), BF),
            pltpu.VMEM((own, units), BF),
            pltpu.VMEM((2, piece, width), BF),
            pltpu.VMEM((2, piece, width), BF),
            pltpu.VMEM((2, piece, width), BF),
            pltpu.VMEM((piece, width), BF),
            pltpu.VMEM((piece, width), BF),
            dma((7, outer)),
            dma((7, outer)),
            dma((7, outer)),
            dma((7, outer)),
            dma((7, outer)),
            dma((7, outer)),
            dma((7,)),
            dma((3, 3)),
            dma((3, 3)),
            dma((3,)),
            dma((9,)),
            dma((3,)),
            dma((3,)),
            pltpu.VMEM((length, 1), jnp.int32),
            pltpu.VMEM((length, 128), F32),
            pltpu.VMEM((256, 256), BF),
            pltpu.VMEM((piece, width), BF),
            pltpu.VMEM((heads + kv_heads, length, HEAD_DIM), F32),
            pltpu.VMEM((heads + 2 * kv_heads, length, HEAD_DIM), BF),
            pltpu.VMEM((length, heads * HEAD_DIM), BF),
            pltpu.VMEM((length, 128), F32),
            pltpu.VMEM((piece, width), F32),
            pltpu.VMEM((length, HEAD_DIM), F32),
            pltpu.VMEM((length, HEAD_DIM), F32),
            pltpu.VMEM((1, length), jnp.int32),
            dma((8,)),
        ],
        compiler_params=pltpu.CompilerParams(
            collective_id=0, has_side_effects=True, vmem_limit_bytes=VMEM_BYTES
        ),
        name="forward_gather",
    )(
        hidden,
        upstream,
        *weights,
        *gains,
        jnp.asarray(np.concatenate([inverse, inverse])[None], F32),
        segment[None],
    )


def add_rows(target, sources, step=16):
    groups, rows, _ = target.shape

    @pl.loop(0, rows // step)
    def _(index):
        part = pl.ds(pl.multiple_of(index * step, step), step)
        for group in range(groups):
            total = sources[0][group, part, :].astype(target.dtype)
            for source in sources[1:]:
                total = total + source[group, part, :].astype(target.dtype)
            target[group, part, :] = total


class RowSum:
    def __init__(self, here, give, keep, near, rising, falling, stage, total, sems):
        self.here, self.give, self.keep = here, give, keep
        self.near, self.rising, self.falling = near, rising, falling
        self.stage, self.total = stage, total
        self.ys, self.yr, self.us, self.ur, self.ds, self.dr, self.load = sems
        self.last = here.outer - 1

    def across(self, place):
        return remote(
            self.give.at[place],
            self.near.at[place],
            self.ys.at[place],
            self.yr.at[place],
            self.here.twin,
        )

    def up(self, place):
        peer = self.here.outer_peer(self.here.place + 1)
        return remote(
            self.keep.at[place], self.rising.at[place], self.us.at[place], self.ur.at[place], peer
        )

    def down(self, place):
        peer = self.here.outer_peer(self.here.place - 1)
        return remote(
            self.keep.at[place], self.falling.at[place], self.ds.at[place], self.dr.at[place], peer
        )

    def arrived(self, slot, send, receive):
        remote(slot, slot, send, receive, self.here.twin).wait_recv()

    def fold(self, distance):
        here = self.here
        above = here.place + distance
        below = here.place - distance

        def merge(place, line, receive, first):
            near = pltpu.make_async_copy(self.near.at[place], self.stage.at[0], self.load.at[0])
            self.arrived(self.near.at[place], self.ys.at[place], self.yr.at[place])
            near.start()

            @pl.when(first)
            def _():
                near.wait()
                add_rows(self.keep.at[place], [self.keep.at[place], self.stage.at[0]])

            @pl.when(jnp.logical_not(first))
            def _():
                self.arrived(line.at[place], self.us.at[0], receive.at[place])
                far = pltpu.make_async_copy(line.at[place], self.stage.at[1], self.load.at[1])
                far.start()
                near.wait()
                far.wait()
                add_rows(
                    self.keep.at[place], [self.keep.at[place], self.stage.at[0], self.stage.at[1]]
                )

        @pl.when(above <= self.last)
        def _():
            merge(above, self.rising, self.ur, here.place == 0)
            self.up(above).start()

        @pl.when(below >= 0)
        def _():
            merge(below, self.falling, self.dr, here.place == self.last)
            self.down(below).start()

    def finish(self):
        here = self.here
        place = here.place
        self.arrived(self.near.at[place], self.ys.at[place], self.yr.at[place])
        keep = self.keep.at[place]
        near = pltpu.make_async_copy(self.near.at[place], self.stage.at[0], self.load.at[0])
        low = pltpu.make_async_copy(self.rising.at[place], self.stage.at[1], self.load.at[1])
        high = pltpu.make_async_copy(self.falling.at[place], self.stage.at[1], self.load.at[1])
        near.start()

        @pl.when(place > 0)
        def _():
            self.arrived(self.rising.at[place], self.us.at[0], self.ur.at[place])
            low.start()
            low.wait()

        @pl.when(place == 0)
        def _():
            self.arrived(self.falling.at[place], self.ds.at[0], self.dr.at[place])
            high.start()
            high.wait()

        near.wait()

        @pl.when((place > 0) & (place < self.last))
        def _():
            add_rows(keep, [keep, self.stage.at[0], self.stage.at[1]])
            self.arrived(self.falling.at[place], self.ds.at[0], self.dr.at[place])
            high.start()
            high.wait()
            add_rows(self.total, [keep, self.stage.at[1]])

        @pl.when((place == 0) | (place == self.last))
        def _():
            add_rows(self.total, [keep, self.stage.at[0], self.stage.at[1]])

    def sent(self):
        for place in range(self.here.outer):
            self.across(place).wait_send()

    def settle(self):
        here = self.here
        for place in range(here.outer):

            @pl.when(place > here.place)
            def _():
                self.up(place).wait_send()

            @pl.when(place < here.place)
            def _():
                self.down(place).wait_send()


def compute_terms(here, give, keep, left, right, tiles, orders, senders):
    own = give.shape[2]
    per = 128 // (2 * own)
    step = 768 if give.shape[3] % 768 == 0 else 512
    for group, done in orders:
        spots = tiles(group)

        @pl.loop(0, give.shape[3] // step)
        def _(index):
            lane = pl.ds(pl.multiple_of(index * step, step), step)
            terms = dot(left(group), right(lane)).astype(BF)
            for spot, (zone, seq_group) in enumerate(spots):
                for sub in range(per):
                    at = spot * 128 + sub * 2 * own
                    even, odd = terms[at : at + own], terms[at + own : at + 2 * own]
                    place = zone * per + sub
                    keep[place, seq_group, :, lane] = jnp.where(here.half == 0, even, odd)
                    give[place, seq_group, :, lane] = jnp.where(here.half == 0, odd, even)

        for zone in done:
            for sub in range(per):
                for sender in senders:
                    sender.across(zone * per + sub).start()


class LineSum:
    def __init__(self, here, terms, rising, falling, stage, sems):
        self.here, self.terms, self.stage = here, terms, stage
        self.rising, self.falling = rising, falling
        self.us, self.ur, self.ds, self.dr, self.load = sems
        self.last = here.outer - 1

    def up(self, place):
        peer = self.here.outer_peer(self.here.place + 1)
        return remote(
            self.terms.at[place], self.rising.at[place], self.us.at[place], self.ur.at[place], peer
        )

    def down(self, place):
        peer = self.here.outer_peer(self.here.place - 1)
        return remote(
            self.terms.at[place], self.falling.at[place], self.ds.at[place], self.dr.at[place], peer
        )

    def merge(self, place, line, receive):
        slot = line.at[place]
        remote(slot, slot, self.us.at[0], receive.at[place], self.here.twin).wait_recv()
        copy = pltpu.make_async_copy(slot, self.stage.at[0], self.load.at[0])
        copy.start()
        copy.wait()
        add_rows(self.terms.at[place], [self.terms.at[place], self.stage.at[0]])

    def fold(self, distance):
        here = self.here
        above = here.place + distance
        below = here.place - distance

        @pl.when(above <= self.last)
        def _():
            @pl.when(here.place > 0)
            def _():
                self.merge(above, self.rising, self.ur)

            self.up(above).start()

        @pl.when(below >= 0)
        def _():
            @pl.when(here.place < self.last)
            def _():
                self.merge(below, self.falling, self.dr)

            self.down(below).start()

    def gather(self):
        place = self.here.place

        @pl.when(place > 0)
        def _():
            self.merge(place, self.rising, self.ur)

        @pl.when(place < self.last)
        def _():
            self.merge(place, self.falling, self.dr)

    def settle(self):
        here = self.here
        for place in range(here.outer):

            @pl.when(place > here.place)
            def _():
                self.up(place).wait_send()

            @pl.when(place < here.place)
            def _():
                self.down(place).wait_send()


class LineFirstSum(RowSum):
    def __init__(self, here, give, keep, near, lines, stage, total, sems, twin_sems):
        self.here, self.give, self.keep = here, give, keep
        self.near, self.stage, self.total = near, stage, total
        self.ys, self.yr, self.load = sems[0], sems[1], sems[6]
        self.lines = [
            LineSum(here, terms, rising, falling, stage, kinds[2:])
            for terms, (rising, falling), kinds in (
                (give, lines[0], twin_sems),
                (keep, lines[1], sems),
            )
        ]

    def fold(self, distance):
        for line in self.lines:
            line.fold(distance)

    def pass_on(self):
        self.lines[0].gather()
        self.across(self.here.place).start()
        self.lines[1].gather()

    def finish(self):
        place = self.here.place
        self.arrived(self.near.at[place], self.ys.at[place], self.yr.at[place])
        near = pltpu.make_async_copy(self.near.at[place], self.stage.at[0], self.load.at[0])
        near.start()
        near.wait()
        add_rows(self.total, [self.keep.at[place], self.stage.at[0]])

    def sent(self):
        self.across(self.here.place).wait_send()

    def settle(self):
        for line in self.lines:
            line.settle()


class RowSpread:
    def __init__(self, here, rows, whole, sems):
        self.here, self.rows, self.whole = here, rows, whole
        self.send_sems, self.recv_sems, self.local = sems

    def copy(self, amount):
        seq = lax.rem(self.here.seq + amount, 4)
        return remote(
            self.rows.at[seq],
            self.whole.at[self.here.seq],
            self.send_sems.at[amount - 1],
            self.recv_sems.at[amount - 1],
            {"seq": seq},
        )

    def keep(self):
        seq = self.here.seq
        return pltpu.make_async_copy(self.rows.at[seq], self.whole.at[seq], self.local)

    def send(self):
        for amount in (2, 3, 1):
            self.copy(amount).start()
        self.keep().start()

    def arrive(self):
        for amount in (1, 2, 3):
            self.copy(amount).wait_recv()
        self.keep().wait()

    def finish(self):
        for amount in (1, 2, 3):
            self.copy(amount).wait_send()


class TokenSum:
    def __init__(self, here, part, got, pair, far_got, base, sems):
        self.here, self.part, self.got, self.pair = here, part, got, pair
        self.far_got, self.base = far_got, base
        self.send_sems, self.recv_sems = sems
        self.rows = part.shape[0] // 4

    def piece(self, seq):
        return pl.ds(pl.multiple_of(seq * self.rows, self.rows), self.rows)

    def to_mate(self, index):
        here = self.here
        chip = here.chip if index else 1 - here.chip
        seq = chip * 2 + 1 - here.core
        return remote(
            self.part.at[self.piece(seq), :],
            self.got.at[index],
            self.send_sems.at[index],
            self.recv_sems.at[index],
            here.mate,
        )

    def to_far(self, half):
        count = self.rows // 2
        part = slice(half * count, (half + 1) * count)
        return remote(
            self.pair.at[part, :],
            self.far_got.at[part, :],
            self.send_sems.at[2 + half],
            self.recv_sems.at[2 + half],
            self.here.far,
        )

    def send(self):
        self.to_mate(0).start()
        self.to_mate(1).start()

    def loop(self, body, begin=0, count=None):
        @pl.loop(0, (count or self.rows) // 32)
        def _(index):
            body(begin + index * 32)

    def pass_on(self):
        self.to_mate(0).wait_recv()
        first = self.here.far_seq * self.rows

        def body(at):
            part = pl.ds(pl.multiple_of(at, 32), 32)
            source = pl.ds(pl.multiple_of(first + at, 32), 32)
            total = self.part[source, :].astype(F32) + self.got[0, part, :].astype(F32)
            self.pair[part, :] = total.astype(BF)

        for half in range(2):
            self.loop(body, half * (self.rows // 2), self.rows // 2)
            self.to_far(half).start()

    def add_near(self):
        self.to_mate(1).wait_recv()
        first = self.here.seq * self.rows

        def body(at):
            part = pl.ds(pl.multiple_of(at, 32), 32)
            source = pl.ds(pl.multiple_of(first + at, 32), 32)
            self.base[part, :] += self.part[source, :].astype(F32) + self.got[1, part, :].astype(F32)

        self.loop(body)
        self.to_mate(0).wait_send()
        self.to_mate(1).wait_send()

    def add_far(self, half):
        self.to_far(half).wait_recv()

        def body(at):
            part = pl.ds(pl.multiple_of(at, 32), 32)
            self.base[part, :] += self.far_got[part, :].astype(F32)

        self.loop(body, half * (self.rows // 2), self.rows // 2)
        self.to_far(half).wait_send()


class GainSum:
    def __init__(self, here, own, seq_got, middle, shard_got, sems):
        self.here, self.own, self.middle = here, own, middle
        self.seq_got, self.shard_got = seq_got, shard_got
        self.seq_send, self.seq_recv, self.shard_send, self.shard_recv = sems

    def over_seq(self, amount):
        here = self.here
        return remote(
            self.own,
            self.seq_got.at[here.seq],
            self.seq_send.at[amount - 1],
            self.seq_recv.at[amount - 1],
            {"seq": lax.rem(here.seq + amount, 4)},
        )

    def over_shard(self, amount):
        here = self.here
        return remote(
            self.middle,
            self.shard_got.at[here.shard],
            self.shard_send.at[amount - 1],
            self.shard_recv.at[amount - 1],
            {"shard": lax.rem(here.shard + amount, here.size)},
        )

    def start(self):
        for amount in range(1, 4):
            self.over_seq(amount).start()
        self.seq_got[self.here.seq] = self.own[...]

    def turn(self):
        for amount in range(1, 4):
            self.over_seq(amount).wait()
        total = self.seq_got[0]
        for index in range(1, 4):
            total = total + self.seq_got[index]
        self.middle[...] = total
        for amount in range(1, self.here.size):
            self.over_shard(amount).start()
        self.shard_got[self.here.shard] = total

    def finish(self):
        for amount in range(1, self.here.size):
            self.over_shard(amount).wait()
        total = self.shard_got[0]
        for index in range(1, self.here.size):
            total = total + self.shard_got[index]
        return total


PLAN = (
    (("down_a", 3), ("down_b", 3),),
    (),
    (("down_a", 2), ("first", 3), ("down_b", 2),),
    (),
    (("down_a", 1),),
    (("first", 2), ("down_b", 1),),
    (("second", 3), ("down_a", "pass"),),
    (),
    (),
    (),
    (("second", 2), ("down_b", "finish"),),
    (("first", 1),),
    (("out", 3),),
    (("second", 1),),
    (("query", 3), ("down_a", "finish"), ("key", 3), ("out", 2), ("first", "finish"), ("second", "finish"),),
    (("query", 2), ("key", 2),),
    (("query", 1), ("key", 1), ("out", 1), ("query", "finish"), ("key", "finish"), ("out", "finish"),),
)


def backward_kernel(
    size,
    n1_hbm,
    dy_hbm,
    n2_hbm,
    act_hbm,
    first_hbm,
    second_hbm,
    proj_hbm,
    heads_hbm,
    mixed_hbm,
    lse_hbm,
    middle_hbm,
    hidden_hbm,
    dy_own,
    qkv_full,
    out_full,
    first_full,
    second_full,
    down_full,
    attn_gain_ref,
    mlp_gain_ref,
    query_gain_ref,
    key_gain_ref,
    cos_hbm,
    sin_hbm,
    start_hbm,
    grad_in_out,
    gains_out,
    grad_out_out,
    hidden_out,
    down_rows,
    first_rows,
    second_rows,
    qkv_rows,
    da_hbm,
    near_mlp,
    rising_mlp,
    falling_mlp,
    rising_twin,
    falling_twin,
    near_qkv,
    rising_qkv,
    falling_qkv,
    near_out,
    rising_out,
    falling_out,
    lhs,
    turned,
    first_r,
    second_r,
    give,
    keep,
    give_out,
    keep_out,
    stage,
    stage_out,
    dout_ref,
    da_own,
    got,
    far_got,
    pair,
    middle_grad,
    proj_buf,
    eye,
    keys_turned,
    lse_t,
    delta,
    delta_t,
    dk_sum,
    dv_sum,
    gain_row,
    gain_seq,
    gain_middle,
    gain_shard,
    ys,
    yr,
    us,
    ur,
    ds,
    dr,
    fold_load,
    spread_s,
    spread_r,
    spread_l,
    sum_s,
    sum_r,
    ts,
    tr,
    token_local,
    gss,
    gsr,
    gts,
    gtr,
    load_sem,
    credit,
    grad_in,
    grad_out,
    heads_ref,
    mixed_ref,
    lse_ref,
    cos_ref,
    sin_ref,
    start_ref,
    store_sems,
):
    here = Place(size)
    length, width = lhs.shape
    rows = length // 4
    units = first_r.shape[1]
    chunk = units // 2
    ff_part = units // size
    heads = mixed_ref.shape[1] // HEAD_DIM
    kv_heads = heads // 2
    qkv_width = qkv_full.shape[2]
    last = here.outer - 1
    scale = HEAD_DIM ** (-0.5)

    def load(source, target, index):
        copy = pltpu.make_async_copy(source, target, load_sem.at[index])
        copy.start()
        return copy

    def sems(index):
        return tuple(kind.at[index] for kind in (ys, yr, us, ur, ds, dr, fold_load))

    thin = qkv_width // 2
    cut = units * 2 // 3
    lanes = {
        "down_a": slice(0, cut),
        "down_b": slice(cut, units),
        "query": slice(0, thin),
        "key": slice(thin, 2 * thin),
    }

    def part(ref, name):
        return ref.at[:, :, :, lanes[name]]

    def row_sum(index, give_ref, keep_ref, near, rising, falling, stage_ref, total):
        return RowSum(
            here, give_ref, keep_ref, near, rising, falling, stage_ref, total, sems(index)
        )

    jobs = {
        "down_a": LineFirstSum(
            here,
            part(give.at[2], "down_a"),
            part(keep.at[0], "down_a"),
            part(near_mlp.at[0], "down_a"),
            (
                (rising_twin, falling_twin),
                (part(rising_mlp.at[0], "down_a"), part(falling_mlp.at[0], "down_a")),
            ),
            part(stage, "down_a"),
            keep.at[0, here.place, :, :, lanes["down_a"]],
            sems(0),
            sems(5),
        ),
        "down_b": row_sum(
            6,
            part(give.at[2], "down_b"),
            part(keep.at[0], "down_b"),
            part(near_mlp.at[0], "down_b"),
            part(rising_mlp.at[0], "down_b"),
            part(falling_mlp.at[0], "down_b"),
            part(stage, "down_b"),
            keep.at[0, here.place, :, :, lanes["down_b"]],
        ),
        "out": row_sum(
            4, give_out, keep_out, near_out, rising_out, falling_out, stage_out, grad_out
        ),
    }
    for index, name in ((1, "first"), (2, "second")):
        jobs[name] = row_sum(
            index,
            give.at[2 - index],
            keep.at[index],
            near_mlp.at[index],
            rising_mlp.at[index],
            falling_mlp.at[index],
            stage,
            keep.at[index, here.place],
        )
    for index, name in ((3, "query"), (7, "key")):
        jobs[name] = row_sum(
            index,
            part(give.at[1], name),
            part(second_r, name),
            part(near_qkv, name),
            part(rising_qkv, name),
            part(falling_qkv, name),
            part(stage, name),
            second_r.at[here.place, :, :, lanes[name]],
        )
    zones = width // 512

    def zone_at(index):
        zone = here.place // (here.outer // zones)
        return (
            3 * (1 - zone // 2),
            lax.rem(2 + 3 * zone, 5),
            1 + lax.rem(zone, 2),
            zone,
        )[index]

    zone_order = [zone_at(index) for index in range(zones)]
    by_zone = [(zone, (zone,)) for zone in zone_order]

    spreads = {}
    for index, (name, whole) in enumerate(
        (
            ("down_a", down_rows.at[:, :, lanes["down_a"]]),
            ("down_b", down_rows.at[:, :, lanes["down_b"]]),
            ("first", first_rows),
            ("second", second_rows),
            ("query", qkv_rows.at[:, :, lanes["query"]]),
            ("key", qkv_rows.at[:, :, lanes["key"]]),
        )
    ):
        kinds = (spread_s.at[index], spread_r.at[index], spread_l.at[index])
        spreads[name] = RowSpread(here, jobs[name].total, whole, kinds)

    def token_sum(index, base):
        return TokenSum(
            here, lhs, got, pair, far_got, base, (sum_s.at[index], sum_r.at[index])
        )

    sum_mlp = token_sum(0, middle_grad)
    sum_hidden = token_sum(1, grad_in)
    sum_attn = token_sum(2, grad_in)
    da = TokenGather(here, da_own, da_hbm, (ts, tr, token_local.at[0]), parts=2)

    def model_tiles(group):
        return [(group, seq_group) for seq_group in range(4)]

    def first_columns(lane):
        return first_r[:, lane]

    def model_left(group):
        return turned[pl.ds(group * 4, 4)].reshape(512, length)

    def advance(steps):
        for name, step in steps:
            job = jobs[name]
            if step == "pass":
                job.pass_on()
            elif step == "finish":
                job.finish()
                if name in spreads:
                    spreads[name].send()
            else:
                for distance in range(last * step // 3, last * (step - 1) // 3, -1):
                    job.fold(distance)

    load_turned = load(dy_hbm, turned, 0)
    load_act = load(act_hbm, lhs.at[:, 0:units], 1)
    eye[...] = identity(HEAD_DIM)
    here.greet(wide=True)
    load_turned.wait()
    load_act.wait()
    load_first = load(first_hbm, first_r, 1)
    load_second = load(second_hbm, second_r, 3)
    load_middle = load(middle_hbm, grad_in, 2)
    load_dy = load(dy_own, da_own, 4)
    late_loads = [
        load(source, target, 5 + index)
        for index, (source, target) in enumerate(
            (
                (mixed_hbm, mixed_ref),
                (lse_hbm, lse_ref),
                (heads_hbm, heads_ref),
                (cos_hbm, cos_ref),
                (sin_hbm, sin_ref),
                (start_hbm, start_ref),
            )
        )
    ]
    def model_terms(give_ref, keep_ref, right, senders):
        compute_terms(
            here, give_ref, keep_ref, model_left, right, model_tiles, by_zone, senders
        )

    model_terms(give.at[2], keep.at[0], lambda lane: lhs[:, lane], [jobs["down_b"]])
    load_turned = load(n2_hbm, turned, 0)
    load_first.wait()
    load_turned.wait()
    model_terms(give.at[1], keep.at[1], first_columns, [jobs["first"]])
    advance(PLAN[0])
    load_second.wait()

    own = width // size
    slabs = 256 // own

    def dn2_body(first_w, second_w):
        lane = pl.ds(pl.multiple_of(pl.program_id(0) * 256, 256), 256)
        first_tile = first_w[...].reshape(256, units)
        second_tile = second_w[...].reshape(256, units)

        @pl.loop(0, 2)
        def _(index):
            part = pl.ds(pl.multiple_of(index * 2 * rows, 2 * rows), 2 * rows)
            total = contract_cols(first_r[part, :], first_tile)
            blocks = pl.ds(index * (here.outer // 2), here.outer // 2)
            second_rows = second_r[blocks].reshape(2 * rows, units)
            total = total + contract_cols(second_rows, second_tile)
            lhs[part, lane] = total.astype(BF)

    slab = pl.BlockSpec((slabs, own, units), lambda t: (t, 0, 0))
    pltpu.emit_pipeline(dn2_body, grid=(width // 256,), in_specs=[slab, slab])(
        first_full, second_full
    )
    sum_mlp.send()
    middle_grad[...] = jnp.zeros_like(middle_grad)
    advance(PLAN[1])
    sum_mlp.pass_on()
    sum_mlp.add_near()
    load_act = load(act_hbm, first_r, 1)
    advance(PLAN[2])

    load_middle.wait()
    load_dy.wait()
    gain_row[...] = jnp.zeros_like(gain_row)
    mlp_lane = slice(2 * HEAD_DIM, 2 * HEAD_DIM + width)
    attn_lane = slice(2 * HEAD_DIM + width, 2 * HEAD_DIM + 2 * width)
    narrow = 16

    for half in range(2):
        sum_mlp.add_far(half)

        @pl.loop(0, rows // 2 // narrow)
        def _(index):
            at = half * (rows // 2) + index * narrow
            part = pl.ds(pl.multiple_of(at, narrow), narrow)
            values = grad_in[part, :]
            scales = lax.rsqrt(jnp.mean(values * values, axis=-1, keepdims=True) + EPSILON)
            normed = values * scales
            update = middle_grad[part, :]
            gain_row[:, mlp_lane] += jnp.sum(update * normed, axis=0, keepdims=True)
            upper = update * mlp_gain_ref[...]
            inner = jnp.mean(upper * normed, axis=-1, keepdims=True)
            grad = da_own[part, :].astype(F32) + scales * (upper - normed * inner)
            middle_grad[part, :] = grad
            da_own[part, :] = grad.astype(BF)

        da.send(half)

    advance(PLAN[3])
    model_terms(
        give.at[0],
        keep.at[2],
        lambda lane: second_r[:, :, :, lane].reshape(length, -1),
        [jobs["second"]],
    )
    advance(PLAN[4])

    def hidden_body(weight):
        lane = pl.ds(pl.multiple_of(pl.program_id(0) * 256, 256), 256)
        tile = weight[...]

        @pl.loop(0, 2)
        def _(index):
            part = pl.ds(pl.multiple_of(index * 2 * rows, 2 * rows), 2 * rows)
            lhs[part, lane] = dot(first_r[part, :], tile).astype(BF)

    load_act.wait()
    pltpu.emit_pipeline(
        hidden_body,
        grid=(width // 256,),
        in_specs=[pl.BlockSpec((units, 256), lambda t: (0, t))],
    )(down_full)
    da.mate_arrived()
    sum_hidden.send()
    da.forward()
    advance(PLAN[5])
    sum_hidden.pass_on()
    sum_hidden.add_near()
    advance(PLAN[6])
    da.rest_arrived()
    da.finish()
    load_lhs = load(da_hbm, lhs, 0)
    load_own = load(hidden_hbm, da_own, 2)
    load_lhs.wait()

    def dout_body(weight):
        lane = pl.ds(pl.multiple_of(pl.program_id(0) * 256, 256), 256)
        tile = weight[...].reshape(256, width)

        @pl.loop(0, 2)
        def _(index):
            part = pl.ds(pl.multiple_of(index * 2 * rows, 2 * rows), 2 * rows)
            dout_ref[part, lane] = contract_cols(lhs[part, :], tile).astype(BF)

    out_blocks, out_rows = out_full.shape[:2]
    pltpu.emit_pipeline(
        dout_body,
        grid=(out_blocks * out_rows // 256,),
        in_specs=[pl.BlockSpec((256 // out_rows, out_rows, width), lambda t: (t, 0, 0))],
    )(out_full)

    for late in late_loads:
        late.wait()
    for head in range(heads):
        lane = slice(head * HEAD_DIM, (head + 1) * HEAD_DIM)
        turned[head] = contract_cols(eye[...], mixed_ref[:, lane]).astype(BF)
    compute_terms(
        here,
        give_out,
        keep_out,
        lambda group: turned[0:heads].reshape(heads * HEAD_DIM, length),
        lambda lane: lhs[:, lane],
        lambda group: [(zone, 0) for zone in range(heads)],
        [(0, zone_order)],
        [jobs["out"]],
    )
    load_turned = load(n1_hbm, turned, 0)
    sum_hidden.add_far(0)
    sum_hidden.add_far(1)
    for index, peer in enumerate((here.mate, here.far)):
        pl.semaphore_signal(credit.at[index], inc=1, device_id=peer, device_id_type=MESH)

    @pl.loop(0, rows // 32)
    def _(index):
        part = pl.ds(pl.multiple_of(index * 32, 32), 32)
        pair[part, :] = grad_in[part, :].astype(BF)

    store_hidden = load(pair, hidden_out, 1)
    advance(PLAN[7])

    lse_t[...] = lse_ref[...].T[0:8]
    delta[...] = jnp.zeros_like(delta)
    for head in range(heads):
        lane = slice(head * HEAD_DIM, (head + 1) * HEAD_DIM)
        terms = dout_ref[:, lane].astype(F32) * mixed_ref[:, lane].astype(F32)
        delta[:, head : head + 1] = jnp.sum(terms, axis=-1, keepdims=True)
    delta_t[...] = delta[...].T[0:8]
    def through_norm(grad, head, part, gain_ref, which):
        proj = proj_buf[part, :]
        scales = lax.rsqrt(jnp.mean(proj * proj, axis=-1, keepdims=True) + EPSILON)
        normed = proj * scales
        grad = grad.astype(F32)
        upper = grad * cos_ref[part, :] - pltpu.roll(grad, HEAD_DIM // 2, 1) * sin_ref[part, :]
        gain_row[:, which * HEAD_DIM : (which + 1) * HEAD_DIM] += jnp.sum(
            upper * normed, axis=0, keepdims=True
        )
        upper = upper * gain_ref[...]
        inner = jnp.mean(upper * normed, axis=-1, keepdims=True)
        result = (scales * (upper - normed * inner)).astype(BF)
        first_r[part, head * HEAD_DIM : (head + 1) * HEAD_DIM] = result

    for head in range(heads):
        pair_head = head // 2
        load_proj = load(proj_hbm.at[head], proj_buf, 4)
        if head % 2 == 0:
            dk_sum[...] = jnp.zeros_like(dk_sum)
            dv_sum[...] = jnp.zeros_like(dv_sum)
            keys_turned[...] = contract_cols(eye[...], heads_ref[heads + pair_head]).astype(BF)
        for block in range(4):
            end = (block + 1) * rows
            part = pl.ds(block * rows, rows)
            queries = heads_ref[head, part, :]
            keys = heads_ref[heads + pair_head, 0:end, :]
            values = heads_ref[heads + kv_heads + pair_head, 0:end, :]
            out_grad = dout_ref[part, head * HEAD_DIM : (head + 1) * HEAD_DIM]
            scores = contract_cols(keys, queries)
            key_place = lax.broadcasted_iota(jnp.int32, (end, rows), 0)
            query_place = lax.broadcasted_iota(jnp.int32, (end, rows), 1) + block * rows
            allowed = (key_place >= start_ref[:, part]) & (key_place <= query_place)
            weights = jnp.exp(scores * scale - lse_t[head : head + 1, part])
            weights = jnp.where(allowed, weights, 0.0)
            weight_grad = contract_cols(values, out_grad)
            inner = delta_t[head : head + 1, part]
            score_grad = (weights * (weight_grad - inner)).astype(BF)
            dk_sum[0:end, :] += dot(score_grad, queries) * scale
            dv_sum[0:end, :] += dot(weights.astype(BF), out_grad)
            query_grad = dot(keys_turned[:, 0:end], score_grad).T
            query_grad = (query_grad * scale).astype(BF)
            if block == 0:
                load_proj.wait()
            through_norm(query_grad, head, part, query_gain_ref, 0)
        if head % 2:
            key = heads + pair_head
            value_at = (heads + kv_heads + pair_head) * HEAD_DIM
            load(proj_hbm.at[key], proj_buf, 4).wait()

            @pl.loop(0, 4)
            def _(index):
                part = pl.ds(pl.multiple_of(index * rows, rows), rows)
                through_norm(dk_sum[part, :].astype(BF), key, part, key_gain_ref, 1)
                first_r[part, value_at : value_at + HEAD_DIM] = dv_sum[part, :].astype(BF)

        advance(PLAN[8 + head])

    load_turned.wait()
    jobs["first"].sent()
    store_hidden.wait()
    proj_grads = first_r.at[:, 0:qkv_width]
    model_terms(
        give.at[1, :, :, :, 0:qkv_width],
        second_r.at[:, :, :, 0:qkv_width],
        first_columns,
        [jobs["query"], jobs["key"]],
    )
    advance(PLAN[12])

    def dn1_body(weight):
        lane = pl.ds(pl.multiple_of(pl.program_id(0) * 256, 256), 256)
        tile = weight[...].reshape(256, qkv_width)

        @pl.loop(0, 2)
        def _(index):
            part = pl.ds(pl.multiple_of(index * 2 * rows, 2 * rows), 2 * rows)
            lhs[part, lane] = contract_cols(proj_grads[part, :], tile).astype(BF)

    pltpu.emit_pipeline(
        dn1_body,
        grid=(width // 256,),
        in_specs=[pl.BlockSpec((slabs, own, qkv_width), lambda t: (t, 0, 0))],
    )(qkv_full)
    grad_in[...] = jnp.zeros_like(grad_in)
    pl.semaphore_wait(credit.at[0], 1)
    pl.semaphore_wait(credit.at[1], 1)
    sum_attn.send()
    advance(PLAN[13])
    sum_attn.pass_on()
    sum_attn.add_near()
    advance(PLAN[14])
    sum_attn.add_far(0)
    sum_attn.add_far(1)
    load_own.wait()

    @pl.loop(0, rows // narrow)
    def _(index):
        part = pl.ds(pl.multiple_of(index * narrow, narrow), narrow)
        values = da_own[part, :].astype(F32)
        scales = lax.rsqrt(jnp.mean(values * values, axis=-1, keepdims=True) + EPSILON)
        normed = values * scales
        update = grad_in[part, :]
        gain_row[:, attn_lane] += jnp.sum(update * normed, axis=0, keepdims=True)
        upper = update * attn_gain_ref[...]
        inner = jnp.mean(upper * normed, axis=-1, keepdims=True)
        grad_in[part, :] = middle_grad[part, :] + scales * (upper - normed * inner)

    store_in = pltpu.make_async_copy(grad_in, grad_in_out, store_sems.at[0])
    store_in.start()
    gain_sum = GainSum(here, gain_row, gain_seq, gain_middle, gain_shard, (gss, gsr, gts, gtr))
    gain_sum.start()
    advance(PLAN[15])
    gain_sum.turn()
    advance(PLAN[16])
    gains_out[...] = gain_sum.finish()
    store_out = pltpu.make_async_copy(grad_out, grad_out_out, store_sems.at[1])
    store_out.start()
    for spread_rows in spreads.values():
        spread_rows.arrive()
    store_in.wait()
    store_out.wait()
    for name, job in jobs.items():
        if name != "first":
            job.sent()
    for job in jobs.values():
        job.settle()
    for job in spreads.values():
        job.finish()


def backward(saved, weights, own, gains, tables, starts):
    size = lax.axis_size("shard")
    outer = size // 2
    (n1, dy, n2, act, first, second, proj, heads_all, mixed, lse, middle) = saved
    length, width = heads_all.shape[1], middle.shape[1]
    piece = length // 4
    units = act.shape[1]
    qkv_width = weights[0].shape[2]
    rows = width // (4 * size)
    q_width = mixed.shape[1]

    def shape(*dims, kind=BF):
        return jax.ShapeDtypeStruct(dims, kind)

    results = [
        shape(piece, width, kind=F32),
        shape(1, 2 * width + 2 * HEAD_DIM, kind=F32),
        shape(1, rows, width, kind=F32),
        shape(piece, width),
        shape(4, rows, units),
        shape(4, rows, units),
        shape(4, rows, units),
        shape(4, rows, qkv_width),
        shape(length, width),
    ]
    results += [shape(3, outer, 4, rows, units)] * 3
    results += [shape(outer, 4, rows, units * 2 // 3)] * 2
    results += [shape(outer, 4, rows, qkv_width)] * 3
    results += [shape(outer, 1, rows, width)] * 3
    dma = pltpu.SemaphoreType.DMA
    vmem = pltpu.VMEM
    return pl.pallas_call(
        functools.partial(backward_kernel, size),
        out_shape=results,
        in_specs=[ANY] * 18 + [VMEM] * 4 + [ANY] * 3,
        out_specs=[ANY, VMEM] + [ANY] * (len(results) - 2),
        scratch_shapes=[
            vmem((length, width), BF),
            vmem((width // 128, 128, length), BF),
            vmem((length, units), BF),
            vmem((outer, 4, rows, units), BF),
            vmem((3, outer, 4, rows, units), BF),
            vmem((3, outer, 4, rows, units), BF),
            vmem((outer, 1, rows, width), BF),
            vmem((outer, 1, rows, width), BF),
            vmem((2, 4, rows, units), BF),
            vmem((2, 1, rows, width), BF),
            vmem((length, q_width), BF),
            vmem((piece, width), BF),
            vmem((2, piece, width), BF),
            vmem((piece, width), BF),
            vmem((piece, width), BF),
            vmem((piece, width), F32),
            vmem((length, HEAD_DIM), F32),
            vmem((HEAD_DIM, HEAD_DIM), BF),
            vmem((HEAD_DIM, length), BF),
            vmem((8, length), F32),
            vmem((length, 128), F32),
            vmem((8, length), F32),
            vmem((length, HEAD_DIM), F32),
            vmem((length, HEAD_DIM), F32),
            vmem((1, 2 * width + 2 * HEAD_DIM), F32),
            vmem((4, 1, 2 * width + 2 * HEAD_DIM), F32),
            vmem((1, 2 * width + 2 * HEAD_DIM), F32),
            vmem((size, 1, 2 * width + 2 * HEAD_DIM), F32),
            dma((8, outer)),
            dma((8, outer)),
            dma((8, outer)),
            dma((8, outer)),
            dma((8, outer)),
            dma((8, outer)),
            dma((8, 3)),
            dma((6, 3)),
            dma((6, 3)),
            dma((6,)),
            dma((3, 4)),
            dma((3, 4)),
            dma((6,)),
            dma((6,)),
            dma((1,)),
            dma((3,)),
            dma((3,)),
            dma((size - 1,)),
            dma((size - 1,)),
            dma((11,)),
            pltpu.SemaphoreType.REGULAR((2,)),
            vmem((piece, width), F32),
            vmem((1, rows, width), F32),
            vmem(heads_all.shape, BF),
            vmem(mixed.shape, BF),
            vmem(lse.shape, F32),
            vmem((length, HEAD_DIM), F32),
            vmem((length, HEAD_DIM), F32),
            vmem((1, length), jnp.int32),
            dma((2,)),
        ],
        compiler_params=pltpu.CompilerParams(
            collective_id=1, has_side_effects=True, vmem_limit_bytes=VMEM_BYTES
        ),
        name="backward_sums",
    )(
        n1,
        dy,
        n2,
        act,
        first,
        second.reshape(outer, 4, rows, units),
        proj,
        heads_all,
        mixed,
        lse,
        middle,
        *own,
        *weights,
        *gains,
        *tables,
        starts,
    )


def finish_kernel(
    size,
    grad_in,
    gains,
    grad_out,
    hidden_out,
    down_rows,
    first_rows,
    second_rows,
    qkv_rows,
    grad_in_out,
    grad_out_out,
    hidden_out_out,
    grad_query,
    grad_key,
    grad_value,
    grad_gate,
    grad_up,
    grad_down,
    attn_gain,
    mlp_gain,
    query_gain,
    key_gain,
    grad_in_buf,
    grad_out_buf,
    hidden_buf,
    down_buf,
    first_buf,
    second_buf,
    qkv_buf,
    query_buf,
    key_buf,
    value_buf,
    gate_buf,
    up_buf,
    wide_buf,
    load_sems,
    store_sems,
):
    units = down_buf.shape[2]
    chunk = units // 2
    ff_part = units // size
    most, tail = chunk - 256, 256
    stores = []

    def load(source, target, index):
        copy = pltpu.make_async_copy(source, target, load_sems.at[index])
        copy.start()
        return copy

    def store(source, target):
        copy = pltpu.make_async_copy(source, target, store_sems.at[len(stores)])
        copy.start()
        stores.append(copy)

    loads = [
        load(source, target, index)
        for index, (source, target) in enumerate(
            (
                (down_rows, down_buf),
                (first_rows, first_buf),
                (second_rows, second_buf),
                (qkv_rows, qkv_buf),
                (grad_in, grad_in_buf),
                (hidden_out, hidden_buf),
                (grad_out, grad_out_buf),
            )
        )
    ]

    def place(read, target):
        @pl.loop(0, target.shape[0] // 16)
        def _(index):
            part = pl.ds(pl.multiple_of(index * 16, 16), 16)
            values = [read(seq, part).astype(F32) for seq in range(4)]
            for begin in range(0, size, size // 8):
                pieces = [
                    values[seq][:, block * ff_part : (block + 1) * ff_part]
                    for block in range(begin, begin + size // 8)
                    for seq in range(4)
                ]
                lane = slice(begin * 4 * ff_part, (begin + size // 8) * 4 * ff_part)
                target[part, lane] = jnp.concatenate(pieces, axis=1)

    def side(index):
        at = 2 * most + index * tail

        def read(seq, part):
            return jnp.concatenate(
                [
                    first_buf[seq, part, index * chunk : (index + 1) * chunk],
                    second_buf[seq, part, index * most : (index + 1) * most],
                    second_buf[seq, part, at : at + tail],
                ],
                axis=1,
            )

        return read

    loads[0].wait()
    place(lambda seq, part: down_buf[seq, part, :], wide_buf)
    store(wide_buf, grad_down)
    loads[1].wait()
    loads[2].wait()
    place(side(0), gate_buf)
    store(gate_buf, grad_gate)
    place(side(1), up_buf)
    store(up_buf, grad_up)
    loads[4].wait()
    store(grad_in_buf, grad_in_out)
    loads[5].wait()
    store(hidden_buf, hidden_out_out)
    loads[6].wait()
    store(grad_out_buf, grad_out_out)
    loads[3].wait()
    at = 0
    for buf, target in ((query_buf, grad_query), (key_buf, grad_key), (value_buf, grad_value)):
        count = buf.shape[1] // 4
        for seq in range(4):
            buf[:, seq * count : (seq + 1) * count] = qkv_buf[seq, :, at : at + count].astype(F32)
        at += count
        store(buf, target)
    at = 0
    for target in (query_gain, key_gain, mlp_gain, attn_gain):
        target[...] = gains[:, at : at + target.shape[1]]
        at += target.shape[1]
    for copy in stores:
        copy.wait()


def finish(grad_in, gains, grad_out, hidden_out, down_rows, first_rows, second_rows, qkv_rows):
    size = lax.axis_size("shard")
    piece, width = grad_in.shape
    rows, units = down_rows.shape[1:]
    qkv_width = qkv_rows.shape[2]

    def shape(*dims, kind=F32):
        return jax.ShapeDtypeStruct(dims, kind)

    results = [
        shape(piece, width),
        shape(1, rows, width),
        shape(piece, width, kind=BF),
        shape(rows, 2 * qkv_width),
        shape(rows, qkv_width),
        shape(rows, qkv_width),
        shape(rows, 4 * units),
        shape(rows, 4 * units),
        shape(rows, 4 * units),
        shape(1, width),
        shape(1, width),
        shape(1, HEAD_DIM),
        shape(1, HEAD_DIM),
    ]
    return pl.pallas_call(
        functools.partial(finish_kernel, size),
        out_shape=results,
        in_specs=[ANY, VMEM] + [ANY] * 6,
        out_specs=[ANY] * 9 + [VMEM] * 4,
        scratch_shapes=[
            pltpu.VMEM((piece, width), F32),
            pltpu.VMEM((1, rows, width), F32),
            pltpu.VMEM((piece, width), BF),
            pltpu.VMEM((4, rows, units), BF),
            pltpu.VMEM((4, rows, units), BF),
            pltpu.VMEM((4, rows, units), BF),
            pltpu.VMEM((4, rows, qkv_width), BF),
            pltpu.VMEM((rows, 2 * qkv_width), F32),
            pltpu.VMEM((rows, qkv_width), F32),
            pltpu.VMEM((rows, qkv_width), F32),
            pltpu.VMEM((rows, 4 * units), F32),
            pltpu.VMEM((rows, 4 * units), F32),
            pltpu.VMEM((rows, 4 * units), F32),
            pltpu.SemaphoreType.DMA((7,)),
            pltpu.SemaphoreType.DMA((9,)),
        ],
        compiler_params=pltpu.CompilerParams(vmem_limit_bytes=VMEM_BYTES),
        name="finish",
    )(grad_in, gains, grad_out, hidden_out, down_rows, first_rows, second_rows, qkv_rows)


def local(
    hidden_in,
    segment_ids,
    norm_attn_gain,
    w_query,
    w_key,
    w_value,
    query_gain,
    key_gain,
    w_out,
    norm_mlp_gain,
    w_gate,
    w_up,
    w_down,
    out_cotangent,
):
    segment = segment_ids[0]
    gains = (norm_attn_gain[None], norm_mlp_gain[None], query_gain[None], key_gain[None])
    results = forward(
        hidden_in[0],
        out_cotangent[0],
        (w_query, w_key, w_value, w_out, w_gate, w_up, w_down),
        gains,
        segment,
    )
    (
        grad_in,
        grad_out,
        hidden_out,
        grad_query,
        grad_key,
        grad_value,
        grad_gate,
        grad_up,
        grad_down,
        attn_gain,
        mlp_gain,
        query_grad,
        key_grad,
    ) = finish(
        *backward(
            results[8:19],
            results[:5],
            (hidden_in[0], out_cotangent[0]),
            gains,
            results[19:21],
            results[21],
        )[:8]
    )
    return (
        hidden_out[None],
        grad_in[None],
        attn_gain[0],
        grad_query,
        grad_key,
        grad_value,
        query_grad[0],
        key_grad[0],
        grad_out[0],
        mlp_gain[0],
        grad_gate,
        grad_up,
        grad_down.T,
    )


def solution(mesh):
    return jax.shard_map(
        local,
        mesh=mesh,
        in_specs=(
            P("shard", "seq", None),
            P("shard", None),
            P(),
            P("shard", None),
            P("shard", None),
            P("shard", None),
            P(),
            P(),
            P("shard", None),
            P(),
            P("shard", None),
            P("shard", None),
            P("shard", None),
            P("shard", "seq", None),
        ),
        out_specs=(
            P("shard", "seq", None),
            P("shard", "seq", None),
            P(),
            P(("seq", "shard"), None),
            P(("seq", "shard"), None),
            P(("seq", "shard"), None),
            P(),
            P(),
            P(("seq", "shard"), None),
            P(),
            P(("seq", "shard"), None),
            P(("seq", "shard"), None),
            P(None, ("seq", "shard")),
        ),
        check_vma=False,
    )
```
